32 devices in a mesh: item: 4 (over z), lat: 2 (over x), lon: 4 (over y, core).
Axes of the slice: x: 2, y: 2, z: 4, core: 2. Of those that a mesh axis runs over, the one named last changes fastest.
Arguments:
- fields: bfloat16 [4, 8, 128, 384], P('item', 'lat', 'lon'), may hold values from -6 to 6
- lead_index: int32 [4], P('item'), may hold values from 0 to 27
- rollout: int32 [4], P('item'), may hold values from 1 to 2, as said below
- w_qkv: bfloat16 [2, 384, 1152], replicated, may hold values from -0.3125 to 0.3125
- w_out: bfloat16 [2, 384, 384], replicated, may hold values from -2.5 to 2.5
- w_up: bfloat16 [2, 384, 1536], replicated, may hold values from -0.3125 to 0.3125
- w_down: bfloat16 [2, 1536, 384], replicated, may hold values from -0.15625 to 0.15625
- w_ada: bfloat16 [2, 384, 2304], replicated, may hold values from -0.3125 to 0.3125
- b_ada: float32 [2, 2304], replicated, may hold values from -3 to 3
- cotangent: bfloat16 [4, 8, 128, 384], P('item', 'lat', 'lon'), may hold values from -6 to 6
Outputs:
- final_field: float32 [4, 8, 128, 384], P('item', 'lat', 'lon')
- field_grad: float32 [4, 8, 128, 384], P('item', 'lat', 'lon')
- qkv_grad: float32 [2, 384, 1152], P(None, ('lat', 'lon'))
- out_grad: float32 [2, 384, 384], P(None, ('lat', 'lon'))
- up_grad: float32 [2, 384, 1536], P(None, ('lat', 'lon'))
- down_grad: float32 [2, 1536, 384], P(None, ('lat', 'lon'))
- ada_grad: float32 [2, 384, 2304], P(None, ('lat', 'lon'))
- bias_grad: float32 [2, 2304], P(None, ('lat', 'lon'))
- shift_grad: float32 [2, 384], P(None, ('lat', 'lon'))
The draws below stay inside these ranges and needn't reach their ends.
Inputs may be any that keep to these rules, and one draw needn't show every extreme that they name: `rollout`: rollout steps of each item; at least one item takes 2.
All inputs are finite; a program needn't handle non-finite values.
Results may differ from the reference program's by a relative error of at most 0.04.
Values may be sent and summed in bfloat16 or wider, within the bound.
No kernel may reach another device: no remote copies, remote signals or barrier semaphores. Data moves between devices by JAX's collectives and lax.ppermute only.
A program may use at most 320 MiB of HBM per device.

```python
import math
import jax
import jax.numpy as jnp
from jax import lax

D = 384
HEADS = 6
HEAD_DIM = 64
FF = 1536
MOD = 2304
LAYERS = 2
STEPS = 2
LEADS = 28
LAT = 8
LON = 128
ITEMS = 4


def draw_rollout(key, part):
    key = jax.random.fold_in(key, 7)
    first_key, second_key = jax.random.split(key)
    counts = jax.random.randint(first_key, (ITEMS,), 1, STEPS + 1)
    longest = jax.random.randint(second_key, (), 0, ITEMS)
    return jnp.where(jnp.arange(ITEMS) == longest, STEPS, counts).astype(jnp.int32)


def touch_ends(result, rng, low, largest):
    longest = result.shape.index(max(result.shape))
    spots = []
    for shift in (0, 1):
        where = [jax.random.randint(jax.random.fold_in(rng, axis), (), 0, length) for axis, length in enumerate(result.shape)]
        where[longest] = (where[longest] + shift) % result.shape[longest]
        spots.append(tuple(where))
    return result.at[spots[0]].set(low).at[spots[1]].set(largest)


def steps_of(rng, extent, pieces, low, largest):
    def one(position, blocks):
        draws = jax.random.uniform(jax.random.fold_in(jax.random.fold_in(rng, 6), position), (blocks,), jnp.float32, low / len(pieces), largest / len(pieces))
        return jnp.repeat(jnp.exp(draws), extent[position] // blocks).reshape((-1,) + (1,) * (len(extent) - position - 1))

    factor_of = one(*pieces[0])
    for cut in pieces[1:]:
        factor_of = factor_of * one(*cut)
    return factor_of


def bell_draw(key, dims, width, limit, shards=(), kind=jnp.bfloat16):
    gain = steps_of(key, dims, shards, -0.22, 0.18) if shards else 1.0
    drawn = jax.random.normal(key, dims, jnp.float32) * width * gain
    return jnp.minimum(jnp.maximum(drawn, -limit), limit).astype(kind)


def setup_inputs(seed: int = 0) -> dict:
    splits = jax.random.split(jax.random.key(seed), 11)
    fields = bell_draw(splits[0], (ITEMS, LAT, LON, D), 1.0, 6.0, ((0, 4), (1, 2), (2, 4)))
    lead_index = touch_ends(jax.random.randint(splits[1], (ITEMS,), 0, LEADS), jax.random.fold_in(splits[1], 1), 0, LEADS - 1).astype(jnp.int32)
    rollout = draw_rollout(jax.random.fold_in(splits[10], 71), 0)
    w_qkv = bell_draw(splits[3], (LAYERS, D, 3 * D), D ** -0.5, 0.3125)
    w_out = bell_draw(splits[4], (LAYERS, D, D), (D // 64) ** -0.5, 2.5)
    w_up = bell_draw(splits[5], (LAYERS, D, FF), D ** -0.5, 0.3125)
    w_down = bell_draw(splits[6], (LAYERS, FF, D), FF ** -0.5, 0.15625)
    w_ada = bell_draw(splits[7], (LAYERS, D, MOD), D ** -0.5, 0.3125)
    b_ada = bell_draw(splits[8], (LAYERS, MOD), 0.5, 3.0, (), jnp.float32)
    cotangent = bell_draw(splits[9], (ITEMS, LAT, LON, D), 1.0, 6.0, ((0, 4), (1, 2), (2, 4)))
    return dict(fields=fields, lead_index=lead_index, rollout=rollout, w_qkv=w_qkv, w_out=w_out, w_up=w_up, w_down=w_down, w_ada=w_ada, b_ada=b_ada, cotangent=cotangent)


@jax.custom_vjp
def low(v):
    return lax.optimization_barrier(v.astype(jnp.bfloat16)).astype(jnp.float32)

@jax.custom_vjp
def low_back(v):
    return v

def low_keep(v):
    return (low(v), None)

def low_pass(kept, grad):
    return (grad,)

def back_keep(v):
    return (v, None)

def back_low(kept, grad):
    return (low(grad),)
low.defvjp(low_keep, low_pass)
low_back.defvjp(back_keep, back_low)
highest = lax.Precision.HIGHEST

def matmul(left, right):
    return jnp.dot(left, right, precision=highest, preferred_element_type=jnp.float32)

def embedding(lead):
    half_width = D // 2
    lead_hours = 6.0 * (lead.astype(jnp.float32) + 1.0)
    frequencies = jnp.exp(-math.log(10000.0) * jnp.arange(half_width, dtype=jnp.float32) / half_width)
    angles = lead_hours * frequencies
    return jnp.concatenate([jnp.sin(angles), jnp.cos(angles)])

def pre_norm(values, shift_part, scale_part):
    centred = values - lax.optimization_barrier(jnp.mean(values, axis=-1, keepdims=True))
    variance = lax.optimization_barrier(jnp.mean(centred * centred, axis=-1, keepdims=True))
    return centred * lax.rsqrt(variance + 1e-06) * (1.0 + scale_part) + shift_part

def attend(queries, key_heads, value_heads):
    total_rows = queries.shape[0]
    block_rows = math.gcd(total_rows, 512)
    factor = HEAD_DIM ** (-0.5)

    def one_block(query_block):
        scores = low_back(jnp.einsum('thd,nhd->htn', query_block, key_heads, precision=highest, preferred_element_type=jnp.float32) * factor)
        probabilities = low(jax.nn.softmax(scores, axis=-1))
        return jnp.einsum('htn,nhd->thd', probabilities, value_heads, precision=highest, preferred_element_type=jnp.float32)
    blocks = queries.reshape(total_rows // block_rows, block_rows, HEADS, HEAD_DIM)
    return lax.map(jax.checkpoint(one_block), blocks).reshape(total_rows, D)

def apply_layer(current, modulation, weight_qkv, weight_out, weight_up, weight_down):
    shift_attn, scale_attn, gate_attn, shift_mlp, scale_mlp, gate_mlp = modulation
    total_rows = current.shape[0]
    normed = low(pre_norm(current, shift_attn, scale_attn))
    projected = low(low_back(matmul(normed, weight_qkv)))
    queries = projected[:, :D].reshape(total_rows, HEADS, HEAD_DIM)
    key_heads = projected[:, D:2 * D].reshape(total_rows, HEADS, HEAD_DIM)
    value_heads = projected[:, 2 * D:].reshape(total_rows, HEADS, HEAD_DIM)
    mixed = low(low_back(attend(queries, key_heads, value_heads)))
    attended = low_back(matmul(mixed, weight_out))
    middle = current + gate_attn * attended
    hidden_in = low(pre_norm(middle, shift_mlp, scale_mlp))
    hidden = low(jax.nn.gelu(low_back(matmul(hidden_in, weight_up))))
    return middle + gate_mlp * low_back(matmul(hidden, weight_down))

def reference(fields, lead_index, rollout, w_qkv, w_out, w_up, w_down, w_ada, b_ada, cotangent):
    params = tuple((weight.astype(jnp.float32) for weight in (w_qkv, w_out, w_up, w_down, w_ada, b_ada)))
    total_rows = LAT * LON

    def forward(initial, weight_qkv, weight_out, weight_up, weight_down, weight_ada, bias_ada):
        results = []
        for item_index in range(ITEMS):
            context = low(jax.nn.silu(embedding(lead_index[item_index])))
            modulations = [(matmul(context[None, :], weight_ada[layer_index])[0] + bias_ada[layer_index]).reshape(6, D) for layer_index in range(LAYERS)]
            current = initial[item_index].reshape(total_rows, D)
            for rollout_step in range(STEPS):
                updated = current
                for layer_index in range(LAYERS):
                    updated = apply_layer(updated, modulations[layer_index], weight_qkv[layer_index], weight_out[layer_index], weight_up[layer_index], weight_down[layer_index])
                current = jnp.where(rollout_step < rollout[item_index], updated, current)
            results.append(current.reshape(LAT, LON, D))
        return jnp.stack(results)
    final_field, pullback = jax.vjp(forward, fields.astype(jnp.float32), *params)
    gradients = pullback(cotangent.astype(jnp.float32))
    shift_grad = gradients[6][:, 3 * D:4 * D]
    return (final_field, gradients[0], gradients[1], gradients[2], gradients[3], gradients[4], gradients[5], gradients[6], shift_grad)
```

```python
import functools
import math

import jax
import jax.numpy as jnp
from jax import lax
from jax.experimental import pallas as pl
from jax.experimental.pallas import tpu as pltpu
from jax.sharding import PartitionSpec as P

D = 384
HEADS = 6
HEAD_DIM = 64
STEPS = 2


def shortened(shard):
    return jax.tree.map(lambda a: a.astype(jnp.bfloat16) if a.dtype == jnp.float32 else a, shard)


def embedding(lead):
    half_width = D // 2
    lead_hours = 6.0 * (lead.astype(jnp.float32) + 1.0)
    frequencies = jnp.exp(
        -math.log(10000.0) * jnp.arange(half_width, dtype=jnp.float32) / half_width
    )
    angles = lead_hours * frequencies
    return jnp.concatenate([jnp.sin(angles), jnp.cos(angles)])


def pre_norm(values, shift_part, scale_part):
    centred = values - jnp.mean(values, axis=-1, keepdims=True)
    variance = jnp.mean(centred * centred, axis=-1, keepdims=True)
    return centred * lax.rsqrt(variance + 1e-06) * (1.0 + scale_part) + shift_part


def gather_keys(keys_values):
    band_rows = lax.all_gather(keys_values, "lon", axis=0, tiled=True)
    return lax.all_gather(band_rows, "lat", axis=0, tiled=True)


def spread_keys(key_value_grads):
    band_grads = lax.psum_scatter(
        key_value_grads.astype(jnp.bfloat16), "lat", scatter_dimension=0, tiled=True
    )
    return lax.psum_scatter(band_grads, "lon", scatter_dimension=0, tiled=True).astype(jnp.float32)


def forward_layer(current, modulation, weight_qkv, weight_out, weight_up, weight_down):
    local_rows, width = current.shape
    shift_attn, scale_attn, gate_attn, shift_mlp, scale_mlp, gate_mlp = modulation
    normed = pre_norm(current, shift_attn, scale_attn).astype(jnp.bfloat16)
    projected = jnp.dot(normed, weight_qkv, preferred_element_type=jnp.float32).astype(jnp.bfloat16)
    queries = projected[:, :width].reshape(local_rows, HEADS, HEAD_DIM)
    own_keys = projected[:, width:]
    gathered = gather_keys(own_keys)
    total_rows = gathered.shape[0]
    key_heads = gathered[:, :width].reshape(total_rows, HEADS, HEAD_DIM)
    value_heads = gathered[:, width:].reshape(total_rows, HEADS, HEAD_DIM)
    scores = jnp.einsum(
        "thd,nhd->htn", queries, key_heads, preferred_element_type=jnp.float32
    ) * HEAD_DIM ** (-0.5)
    log_total = jax.nn.logsumexp(scores, axis=-1, keepdims=True)
    probabilities = jnp.exp(scores - log_total).astype(jnp.bfloat16)
    mixed = jnp.einsum(
        "htn,nhd->thd", probabilities, value_heads, preferred_element_type=jnp.float32
    )
    mixed = mixed.reshape(local_rows, width).astype(jnp.bfloat16)
    attended = jnp.dot(mixed, weight_out, preferred_element_type=jnp.float32)
    middle = current + gate_attn * attended
    hidden_in = pre_norm(middle, shift_mlp, scale_mlp).astype(jnp.bfloat16)
    pre_act = jnp.dot(hidden_in, weight_up, preferred_element_type=jnp.float32)
    hidden = jax.nn.gelu(pre_act).astype(jnp.bfloat16)
    branch = jnp.dot(hidden, weight_down, preferred_element_type=jnp.float32)
    output = middle + gate_mlp * branch
    kept = (
        current,
        normed,
        queries,
        gathered,
        own_keys,
        log_total,
        mixed,
        attended,
        middle,
        hidden_in,
        pre_act,
        hidden,
        branch,
    )
    return (output, kept)


def backward_layer(grad_out, kept, modulation, weight_qkv, weight_out, weight_up, weight_down):
    (
        current,
        normed,
        queries,
        gathered,
        own_keys,
        log_total,
        mixed,
        attended,
        middle,
        hidden_in,
        pre_act,
        hidden,
        branch,
    ) = kept
    local_rows, width = current.shape
    total_rows = gathered.shape[0]
    shift_attn, scale_attn, gate_attn, shift_mlp, scale_mlp, gate_mlp = modulation
    factor = HEAD_DIM ** (-0.5)
    branch_grad = (gate_mlp * grad_out).astype(jnp.bfloat16)
    gate_mlp_grad = jnp.sum(grad_out * branch, axis=0)
    hidden_grad = jnp.dot(branch_grad, weight_down.T, preferred_element_type=jnp.float32)
    down_grad = jnp.dot(hidden.T, branch_grad, preferred_element_type=jnp.float32)
    _, gelu_back = jax.vjp(jax.nn.gelu, pre_act)
    pre_grad = gelu_back(hidden_grad)[0].astype(jnp.bfloat16)
    hidden_in_grad = jnp.dot(pre_grad, weight_up.T, preferred_element_type=jnp.float32)
    up_grad = jnp.dot(hidden_in.T, pre_grad, preferred_element_type=jnp.float32)
    _, second_back = jax.vjp(pre_norm, middle, shift_mlp, scale_mlp)
    middle_part, shift_mlp_grad, scale_mlp_grad = second_back(hidden_in_grad)
    middle_grad = grad_out + middle_part
    attended_grad = (gate_attn * middle_grad).astype(jnp.bfloat16)
    gate_attn_grad = jnp.sum(middle_grad * attended, axis=0)
    mixed_grad = jnp.dot(attended_grad, weight_out.T, preferred_element_type=jnp.float32).astype(
        jnp.bfloat16
    )
    out_grad = jnp.dot(mixed.T, attended_grad, preferred_element_type=jnp.float32)
    mixed_heads = mixed_grad.reshape(local_rows, HEADS, HEAD_DIM)
    key_heads = gathered[:, :width].reshape(total_rows, HEADS, HEAD_DIM)
    value_heads = gathered[:, width:].reshape(total_rows, HEADS, HEAD_DIM)
    scores = (
        jnp.einsum("thd,nhd->htn", queries, key_heads, preferred_element_type=jnp.float32) * factor
    )
    probabilities = jnp.exp(scores - log_total)
    prob_grads = jnp.einsum(
        "thd,nhd->htn", mixed_heads, value_heads, preferred_element_type=jnp.float32
    )
    centre = jnp.sum(prob_grads * probabilities, axis=-1, keepdims=True)
    score_grads = (probabilities * (prob_grads - centre)).astype(jnp.bfloat16)
    query_grads = (
        jnp.einsum("htn,nhd->thd", score_grads, key_heads, preferred_element_type=jnp.float32)
        * factor
    )
    value_grads = jnp.einsum(
        "htn,thd->nhd",
        probabilities.astype(jnp.bfloat16),
        mixed_heads,
        preferred_element_type=jnp.float32,
    )
    key_grads = (
        jnp.einsum("htn,thd->nhd", score_grads, queries, preferred_element_type=jnp.float32)
        * factor
    )
    key_value_grads = jnp.concatenate(
        [key_grads.reshape(total_rows, width), value_grads.reshape(total_rows, width)], axis=1
    )
    local_grads = spread_keys(key_value_grads)
    projected_grad = jnp.concatenate(
        [query_grads.reshape(local_rows, width), local_grads], axis=1
    ).astype(jnp.bfloat16)
    normed_grad = jnp.dot(projected_grad, weight_qkv.T, preferred_element_type=jnp.float32)
    qkv_grad = jnp.dot(normed.T, projected_grad, preferred_element_type=jnp.float32)
    _, first_back = jax.vjp(pre_norm, current, shift_attn, scale_attn)
    current_part, shift_attn_grad, scale_attn_grad = first_back(normed_grad)
    input_grad = middle_grad + current_part
    modulation_grad = jnp.concatenate(
        [
            shift_attn_grad,
            scale_attn_grad,
            gate_attn_grad,
            shift_mlp_grad,
            scale_mlp_grad,
            gate_mlp_grad,
        ]
    )
    return (input_grad, (qkv_grad, out_grad, up_grad, down_grad, modulation_grad))


def shards(fields, lead_index, rollout, w_qkv, w_out, w_up, w_down, w_ada, b_ada, cotangent):
    _, rows_dev, cols_dev, width = fields.shape
    local_rows = rows_dev * cols_dev
    layer_count = w_qkv.shape[0]
    context = jax.nn.silu(embedding(lead_index[0])).astype(jnp.bfloat16)
    context_wide = context.astype(jnp.float32)
    modulations = [
        (
            jnp.dot(context[None, :], w_ada[index], preferred_element_type=jnp.float32)[0]
            + b_ada[index]
        ).reshape(6, width)
        for index in range(layer_count)
    ]
    weight_sets = [
        (w_qkv[index], w_out[index], w_up[index], w_down[index]) for index in range(layer_count)
    ]
    count = rollout[0]
    current = fields.reshape(local_rows, width).astype(jnp.float32)
    saved = []
    for rollout_step in range(STEPS):
        updated = current
        kept_layers = []
        for index in range(layer_count):
            updated, kept = forward_layer(updated, modulations[index], *weight_sets[index])
            kept_layers.append(kept)
        current = jnp.where(rollout_step < count, updated, current)
        saved.append(kept_layers)
    gradient = cotangent.reshape(local_rows, width).astype(jnp.float32)
    summed = None
    shares = None
    for rollout_step in reversed(range(STEPS)):
        active = (rollout_step < count).astype(jnp.float32)
        inner = gradient * active
        layer_terms = [None] * layer_count
        for index in reversed(range(layer_count)):
            inner, layer_terms[index] = backward_layer(
                inner, saved[rollout_step][index], modulations[index], *weight_sets[index]
            )
        gradient = inner + (1.0 - active) * gradient
        modulation_grads = jnp.stack([terms[4] for terms in layer_terms])
        step_terms = (
            jnp.stack([terms[0] for terms in layer_terms]),
            jnp.stack([terms[1] for terms in layer_terms]),
            jnp.stack([terms[2] for terms in layer_terms]),
            jnp.stack([terms[3] for terms in layer_terms]),
            context_wide[None, :, None] * modulation_grads[:, None, :],
            modulation_grads,
            modulation_grads[:, 3 * width : 4 * width],
        )
        summed = step_terms if summed is None else jax.tree.map(jnp.add, summed, step_terms)
    shares = lax.psum_scatter(summed, ("lat", "lon"), scatter_dimension=1, tiled=True)
    totals = jax.tree.map(
        lambda part: part.astype(jnp.float32), lax.psum(shortened(shares), "item")
    )
    return (
        current.reshape(1, rows_dev, cols_dev, width),
        gradient.reshape(1, rows_dev, cols_dev, width),
        totals[0],
        totals[1],
        totals[2],
        totals[3],
        totals[4],
        totals[5],
        totals[6],
    )


F32 = jnp.float32
BF16 = jnp.bfloat16
GELU_A = math.sqrt(2.0 / math.pi)
GELU_B = 0.044715
LANES = 128
BLOCK = 256


def nn(left, right):
    return lax.dot_general(left, right, (((1,), (0,)), ((), ())), preferred_element_type=F32)


def nt(left, right):
    return lax.dot_general(left, right, (((1,), (1,)), ((), ())), preferred_element_type=F32)


def wide(column_tile, lanes):
    return jnp.concatenate([column_tile] * (lanes // LANES), axis=1)


def folded(values):
    pieces = [values[:, at : at + LANES] for at in range(0, values.shape[1], LANES)]
    return sum(pieces[1:], pieces[0])


def standardise(values):
    rows = values.shape[0]
    centred = values - jnp.sum(values, axis=0, keepdims=True) * (1.0 / rows)
    variance = jnp.sum(centred * centred, axis=0, keepdims=True) * (1.0 / rows)
    scale = lax.rsqrt(variance + 1e-06)
    return centred * scale, scale


def pre_norm_back(standard, scale, grad, gain):
    rows = standard.shape[0]
    inner = grad * gain
    first = jnp.sum(inner, axis=0, keepdims=True) * (1.0 / rows)
    second = jnp.sum(inner * standard, axis=0, keepdims=True) * (1.0 / rows)
    return scale * (inner - first - standard * second)


def part(mod_ref, index, lanes):
    return wide(mod_ref[index * D : (index + 1) * D, :], lanes)


def project(x, mod_ref, w_qkv_t, w_kv, outs, at):
    q_out, kn_out, vn_out, kt_out, vt_out, normed_out = outs
    lanes = x.shape[1]
    standard, _ = standardise(x)
    normed = standard * (1.0 + part(mod_ref, 1, lanes)) + part(mod_ref, 0, lanes)
    normed_b = normed.astype(BF16)
    normed_out[:, at] = normed_b
    projected = nn(w_qkv_t[...], normed_b)
    q_out[:, at] = (projected[:D] * HEAD_DIM ** (-0.5)).astype(BF16)
    kt_out[:, at] = projected[D : 2 * D].astype(BF16)
    vt_out[:, at] = projected[2 * D :].astype(BF16)
    natural = normed.T.astype(BF16)
    plain = nn(natural, w_kv[...])
    kn_out[at, :] = plain[:, :D].astype(BF16)
    vn_out[at, :] = plain[:, D:].astype(BF16)


def blocks_of(count, body):
    def step(index, _):
        body(pl.ds(pl.multiple_of(index * BLOCK, BLOCK), BLOCK))
        return 0

    lax.fori_loop(0, count // BLOCK, step, 0)


def first_kernel(own, flip_x, flip_y, flip_xy, mod, w_qkv_t, w_kv, *outs):
    x_out = outs[0]
    for index, ref in enumerate((own, flip_x, flip_y, flip_xy)):
        rows = ref.shape[0]
        x_out[:, index * rows : (index + 1) * rows] = ref[...].astype(F32).T
    blocks_of(x_out.shape[1], lambda at: project(x_out[:, at], mod, w_qkv_t, w_kv, outs[1:], at))


def head_rows(pair_ref, pair, head):
    return pair_ref[pl.ds(pl.multiple_of(pair * 2 * HEAD_DIM + head * HEAD_DIM, HEAD_DIM), HEAD_DIM), :]


def padded(rows, head):
    zeros = jnp.zeros_like(rows)
    return jnp.concatenate([rows, zeros] if head == 0 else [zeros, rows], axis=0)


def forward_kernel(last, x, q, kn_own, kn_far, vt_own, vt_far, mod, w_out_t, w_up_t, w_down_t, *rest):
    if last:
        lse, mixed, attended, middle, pre_act, branch, x_next = rest
    else:
        mod_next, w_qkv_t, w_kv = rest[:3]
        lse, mixed, attended, middle, pre_act, branch, x_next = rest[3:10]
        next_outs = rest[10:]
    patches = x.shape[1]

    def heads(pair, _):
        columns = pl.ds(pl.multiple_of(pair * 2 * HEAD_DIM, 2 * HEAD_DIM), 2 * HEAD_DIM)
        for head in range(2):
            query = padded(head_rows(q, pair, head), head)
            scores_own = nn(kn_own[:, columns], query)
            scores_far = nn(kn_far[:, columns], query)
            top = jnp.maximum(
                jnp.max(scores_own, axis=0, keepdims=True), jnp.max(scores_far, axis=0, keepdims=True)
            )
            ones = jnp.ones((16, patches), BF16)
            value_own = jnp.concatenate([head_rows(vt_own, pair, head), ones], axis=0)
            value_far = jnp.concatenate([head_rows(vt_far, pair, head), ones], axis=0)
            total = nn(value_own, jnp.exp(scores_own - top).astype(BF16)) + nn(
                value_far, jnp.exp(scores_far - top).astype(BF16)
            )
            weight = total[HEAD_DIM : HEAD_DIM + 1]
            mixed[pl.ds(pl.multiple_of(pair * 2 * HEAD_DIM + head * HEAD_DIM, HEAD_DIM), HEAD_DIM), :] = (
                total[:HEAD_DIM] * (1.0 / weight)
            ).astype(BF16)
            lse[pair, head : head + 1, :] = top + jnp.log(weight)
        return 0

    lax.fori_loop(0, HEADS // 2, heads, 0)

    def dense(at):
        att = nn(w_out_t[...], mixed[:, at])
        attended[:, at] = att.astype(BF16)
        mid = x[:, at] + part(mod, 2, BLOCK) * att
        middle[:, at] = mid
        standard, _ = standardise(mid)
        hidden_in = (standard * (1.0 + part(mod, 4, BLOCK)) + part(mod, 3, BLOCK)).astype(BF16)
        act = nn(w_up_t[...], hidden_in)
        pre_act[:, at] = act.astype(BF16)
        hidden = (0.5 * act * (1.0 + jnp.tanh(GELU_A * (act + GELU_B * act * act * act)))).astype(BF16)
        down = nn(w_down_t[...], hidden)
        branch[:, at] = down.astype(BF16)
        out = mid + part(mod, 5, BLOCK) * down
        x_next[:, at] = out
        if not last:
            project(out, mod_next, w_qkv_t, w_kv, next_outs, at)

    blocks_of(patches, dense)


def close_part(at, d_own, d_got, dq, d_mid, x, normed, mod, w_qkv, store, shift_sum, scale_sum):
    grads = jnp.concatenate(
        [dq[:, at], (d_own[:, at] + d_got[:, at].astype(F32)).astype(BF16)], axis=0
    )
    store[:, at] = grads
    back = nn(w_qkv[...], grads)
    standard, scale = standardise(x[:, at])
    shift_sum[...] += folded(back)
    scale_sum[...] += folded(back * standard)
    return d_mid[:, at] + pre_norm_back(standard, scale, back, 1.0 + part(mod, 1, BLOCK))


def own_rows(ref, where, count):
    mine = ref[pl.ds(pl.multiple_of(where[0] * count, 16), count), :]
    other = ref[pl.ds(pl.multiple_of(where[1] * count, 16), count), :]
    return jnp.concatenate([mine, other], axis=0)


def put_grads(left_ref, right, where, count, at, mine, other, before):
    rows = own_rows(left_ref, where, count)
    product = nt(rows, right)
    for column in range(0, product.shape[1], D):
        piece = product[:, column : column + D]
        low, high = piece[:count], piece[count:]
        if before is not None:
            low = low + before[0][at : at + count, :]
            high = high + before[1][at : at + count, :]
        mine[at : at + count, :] = low.astype(mine.dtype)
        other[at : at + count, :] = high.astype(other.dtype)
        at += count


def backward_kernel(has_close, has_open, has_before, start, *refs):
    refs = list(refs)

    def take(count):
        taken = refs[:count]
        del refs[:count]
        return taken

    where, active = take(2)
    if has_close:
        close_in = take(8)
        close_before = take(2) if has_before[0] else None
        close_mod_before = take(1) if has_before[0] else None
    if start == "first":
        cots = take(4)
    elif start == "cross":
        cots = take(1)
    if has_open:
        (lse, mixed, attended, middle, pre_act, branch, q, kn_own, kn_far, vn_own, vn_far, kt_own, kt_far) = take(13)
        mod, w_out, w_up, w_down = take(4)
        open_before = take(2) if has_before[1] else None
        open_mod_before = take(1) if has_before[1] else None
    if has_close:
        close_mine, close_other, close_mods = take(3)
        if not has_open:
            (g_out,) = take(1)
    if start == "first":
        (cot_out,) = take(1)
    if has_open:
        open_mine, open_other, open_mods, d_own, d_far, dq_out, d_mid_out = take(7)
    if has_close:
        (grads_scr,) = take(1)
    if has_open:
        bg_scr, hid_scr, pg_scr, hin_scr, ag_scr, do_scr, cen_scr, dq_scr = take(8)

    patches = middle.shape[1] if has_open else close_in[0].shape[1]

    if has_close:
        if close_mod_before is None:
            close_mods[...] = jnp.zeros_like(close_mods)
        else:
            close_mods[...] = close_mod_before[0][...]
    if has_open:
        if open_mod_before is None:
            open_mods[...] = jnp.zeros_like(open_mods)
        else:
            open_mods[...] = open_mod_before[0][...]
    if start == "first":
        for index, ref in enumerate(cots):
            rows = ref.shape[0]
            cot_out[:, index * rows : (index + 1) * rows] = ref[...].astype(F32).T

    def dense(at):
        if has_close:
            d_own_in, d_got, dq_in, d_mid_in, x_in, normed_in, mod_in, w_qkv = close_in
            g = close_part(
                at, d_own_in, d_got, dq_in, d_mid_in, x_in, normed_in, mod_in, w_qkv, grads_scr,
                close_mods.at[0:D, :], close_mods.at[D : 2 * D, :],
            )
            if start == "cross":
                g = g + (1.0 - active[0]) * cots[0][:, at]
            if not has_open:
                g_out[:, at] = g
                return
        else:
            g = cot_out[:, at] * active[0]
        branch_grad = (part(mod, 5, BLOCK) * g).astype(BF16)
        bg_scr[:, at] = branch_grad
        open_mods[3 * D : 4 * D, :] += folded(g * branch[:, at].astype(F32))
        hidden_grad = nn(w_down[...], branch_grad)
        act = pre_act[:, at].astype(F32)
        square = act * act
        bent = jnp.tanh(GELU_A * act * (1.0 + GELU_B * square))
        half = 0.5 * (1.0 + bent)
        hid_scr[:, at] = (act * half).astype(BF16)
        slope = half + (0.5 * GELU_A) * act * (1.0 - bent * bent) * (1.0 + (3.0 * GELU_B) * square)
        pre_grad = (slope * hidden_grad).astype(BF16)
        pg_scr[:, at] = pre_grad
        back = nn(w_up[...], pre_grad)
        standard, scale = standardise(middle[:, at])
        gain = 1.0 + part(mod, 4, BLOCK)
        hin_scr[:, at] = (standard * gain + part(mod, 3, BLOCK)).astype(BF16)
        open_mods[D : 2 * D, :] += folded(back)
        open_mods[2 * D : 3 * D, :] += folded(back * standard)
        d_mid = g + pre_norm_back(standard, scale, back, gain)
        d_mid_out[:, at] = d_mid
        open_mods[0:D, :] += folded(d_mid * attended[:, at].astype(F32))
        att_grad = (part(mod, 2, BLOCK) * d_mid).astype(BF16)
        ag_scr[:, at] = att_grad
        mixed_grad = nn(w_out[...], att_grad).astype(BF16)
        do_scr[:, at] = mixed_grad
        product = mixed_grad.astype(F32) * mixed[:, at].astype(F32)
        for head in range(HEADS):
            cen_scr[head // 2, head % 2 : head % 2 + 1, at] = jnp.sum(
                product[head * HEAD_DIM : (head + 1) * HEAD_DIM], axis=0, keepdims=True
            )

    blocks_of(patches, dense)

    if has_close:
        put_grads(close_in[5], grads_scr[...], where, D // 8, 0, close_mine, close_other, close_before)
    if not has_open:
        return
    put_grads(hid_scr, bg_scr[...], where, w_down.shape[0] // 8, 0, open_mine, open_other, open_before)
    at = w_down.shape[0] // 8
    put_grads(hin_scr, pg_scr[...], where, D // 8, at, open_mine, open_other, open_before)
    at += (w_up.shape[1] // D) * (D // 8)
    put_grads(mixed, ag_scr[...], where, D // 8, at, open_mine, open_other, open_before)

    def heads(pair, _):
        columns = pl.ds(pl.multiple_of(pair * 2 * HEAD_DIM, 2 * HEAD_DIM), 2 * HEAD_DIM)
        for head in range(2):
            rows = pl.ds(pl.multiple_of(pair * 2 * HEAD_DIM + head * HEAD_DIM, HEAD_DIM), HEAD_DIM)
            value_rows = pl.ds(pl.multiple_of(D + pair * 2 * HEAD_DIM + head * HEAD_DIM, HEAD_DIM), HEAD_DIM)
            query = q[rows, :]
            out_grad = do_scr[rows, :]
            total = lse[pair, head : head + 1, :]
            centre = cen_scr[pair, head : head + 1, :]
            dq = None
            for kn, vn, kt, out in ((kn_far, vn_far, kt_far, d_far), (kn_own, vn_own, kt_own, d_own)):
                scores = nn(kn[:, columns], padded(query, head))
                probs = jnp.exp(scores - total)
                prob_grads = nn(vn[:, columns], padded(out_grad, head))
                score_grads = (probs * (prob_grads - centre)).astype(BF16)
                out[value_rows, :] = nt(out_grad, probs.astype(BF16)).astype(out.dtype)
                out[rows, :] = nt(query, score_grads).astype(out.dtype)
                term = nn(kt[rows, :], score_grads)
                dq = term if dq is None else dq + term
            dq_out[rows, :] = (dq * HEAD_DIM ** (-0.5)).astype(BF16)
        return 0

    lax.fori_loop(0, HEADS // 2, heads, 0)


VMEM = pl.BlockSpec(memory_space=pltpu.VMEM)
SMEM = pl.BlockSpec(memory_space=pltpu.SMEM)


def call(body, args, outs, scratch=(), scalars=0, flops=0, name=None):
    return pl.pallas_call(
        body,
        out_shape=[jax.ShapeDtypeStruct(shape, kind) for shape, kind in outs],
        in_specs=[SMEM] * scalars + [VMEM] * (len(args) - scalars),
        out_specs=[VMEM] * len(outs),
        scratch_shapes=[pltpu.VMEM(shape, kind) for shape, kind in scratch],
        compiler_params=pltpu.CompilerParams(vmem_limit_bytes=VMEM_LIMIT),
        cost_estimate=pl.CostEstimate(flops=flops, bytes_accessed=0, transcendentals=0),
        name=name,
    )(*args)


VMEM_LIMIT = 48 * 1024 * 1024


def fast_shards(lat_count, lon_count, item_count, fields, lead_index, rollout, w_qkv, w_out, w_up, w_down, w_ada, b_ada, cotangent):
    _, rows_dev, cols_dev, width = fields.shape
    local = rows_dev * cols_dev
    layers = w_qkv.shape[0]
    ff = w_up.shape[2]
    patches = 4 * local
    lat = lax.axis_index("lat")
    lon = lax.axis_index("lon")
    item = lax.axis_index("item")
    device = lat * lon_count + lon
    where = jnp.stack([device, device ^ 1]).astype(jnp.int32)
    count = rollout[0]
    active = (1 < count).astype(F32)[None]

    def plane_flip(value, flip_lat, flip_y):
        pairs = [
            (a * lon_count + b, (a ^ flip_lat) * lon_count + (b ^ (2 * flip_y)))
            for a in range(lat_count)
            for b in range(lon_count)
        ]
        return lax.ppermute(value, ("lat", "lon"), pairs)

    def swap(value):
        return lax.ppermute(value, "lon", [(index, index ^ 1) for index in range(lon_count)])

    def along_items(value):
        got = [value]
        for shift in range(1, item_count):
            pairs = [(source, (source + shift) % item_count) for source in range(item_count)]
            got.append(lax.ppermute(value, "item", pairs))
        order = (item - jnp.arange(item_count)) % item_count
        return jnp.take(jnp.stack(got), order, axis=0)

    own = fields.reshape(local, width)
    field_parts = [own, plane_flip(own, 1, 0), plane_flip(own, 0, 1), plane_flip(own, 1, 1)]
    cot_own = cotangent.reshape(local, width)
    cot_parts = [cot_own, plane_flip(cot_own, 1, 0), plane_flip(cot_own, 0, 1), plane_flip(cot_own, 1, 1)]
    leads = along_items(lead_index)[:, 0]

    contexts = jax.nn.silu(jax.vmap(embedding)(leads)).astype(BF16)
    context = lax.dynamic_slice_in_dim(contexts, item, 1, 0)
    mods = []
    for index in range(layers):
        values = jnp.dot(context, w_ada[index], preferred_element_type=F32)[0] + b_ada[index]
        mods.append(jnp.broadcast_to(values[:, None], (values.shape[0], LANES)))
    w_qkv_t = [w_qkv[index].T for index in range(layers)]
    w_kv = [w_qkv[index][:, width:] for index in range(layers)]
    w_out_t = [w_out[index].T for index in range(layers)]
    w_up_t = [w_up[index].T for index in range(layers)]
    w_down_t = [w_down[index].T for index in range(layers)]

    square = (width, patches)
    natural = (patches, width)
    project_outs = [(square, BF16), (natural, BF16), (natural, BF16), (square, BF16), (square, BF16), (square, BF16)]
    dense_flops = 2 * patches * (width * 3 * width + width * width + 2 * width * ff)
    score_flops = 2 * patches * 2 * patches * width * 4
    x, *projected = call(
        first_kernel,
        [*field_parts, mods[0], w_qkv_t[0], w_kv[0]],
        [(square, F32)] + project_outs,
        flops=2 * patches * width * 5 * width,
        name="first",
    )
    saved = []
    for step in range(STEPS):
        for index in range(layers):
            q, kn, vn, kt, vt, normed = projected
            kn_far, vt_far = swap(kn), swap(vt)
            vn_far, kt_far = swap(vn), swap(kt)
            last = step == STEPS - 1 and index == layers - 1
            following = (index + 1) % layers
            extra = [] if last else [mods[following], w_qkv_t[following], w_kv[following]]
            lse, mixed, attended, middle, pre_act, branch, x_next, *projected = call(
                functools.partial(forward_kernel, last),
                [x, q, kn, kn_far, vt, vt_far, mods[index], w_out_t[index], w_up_t[index], w_down_t[index], *extra],
                [
                    ((HEADS // 2, 2, patches), F32),
                    (square, BF16),
                    (square, BF16),
                    (square, F32),
                    ((ff, patches), BF16),
                    (square, BF16),
                    (square, F32),
                ]
                + ([] if last else project_outs),
                flops=dense_flops + 2 * score_flops,
                name="forward",
            )
            saved.append(
                dict(
                    x=x,
                    normed=normed,
                    kept=[lse, mixed, attended, middle, pre_act, branch, q, kn, kn_far, vn, vn_far, kt, kt_far],
                )
            )
            if index == 0 and step > 0:
                step_input = x
            x = x_next
    final = jnp.where(active[0] > 0, x[:, :local], step_input[:, :local]).T

    slice_rows = width // 8
    open_rows = slice_rows * (2 * (ff // width) + 1)
    close_rows = slice_rows * 3
    part_sums = (4 * width, LANES)
    input_sums = (2 * width, LANES)
    order = [(step, index) for step in reversed(range(STEPS)) for index in reversed(range(layers))]
    open_done = [None] * layers
    close_done = [None] * layers
    pending = None
    cot_t = None
    for place in range(len(order) + 1):
        has_close = pending is not None
        has_open = place < len(order)
        args = [where, active]
        outs = []
        scratch = []
        has_before = [False, False]
        start = ""
        if has_close:
            close_index = order[place - 1][1]
            args += pending
            if close_done[close_index] is not None:
                has_before[0] = True
                args += close_done[close_index]
            outs += [((close_rows, width), F32)]
            outs += [((close_rows, width), BF16 if has_before[0] else F32), (input_sums, F32)]
            scratch += [((3 * width, patches), BF16)]
            if not has_open:
                outs += [(square, F32)]
        if place == 0:
            start = "first"
            args += cot_parts
            outs += [(square, F32)]
        elif has_open and order[place][0] != order[place - 1][0]:
            start = "cross"
            args += [cot_t]
        if has_open:
            step, index = order[place]
            kept = saved[step * layers + index]
            args += kept["kept"] + [mods[index], w_out[index], w_up[index], w_down[index]]
            if open_done[index] is not None:
                has_before[1] = True
                args += open_done[index]
            outs += [
                ((open_rows, width), F32),
                ((open_rows, width), BF16 if has_before[1] else F32),
                (part_sums, F32),
                ((2 * width, patches), F32),
                ((2 * width, patches), BF16),
                (square, BF16),
                (square, F32),
            ]
            scratch += [
                (square, BF16),
                ((ff, patches), BF16),
                ((ff, patches), BF16),
                (square, BF16),
                (square, BF16),
                (square, BF16),
                ((HEADS // 2, 2, patches), F32),
                ((8, LANES), F32),
            ]
        results = call(
            functools.partial(backward_kernel, has_close, has_open, has_before, start),
            args,
            outs,
            scratch,
            scalars=2,
            flops=(dense_flops + 5 * score_flops) if has_open else dense_flops // 4,
            name="backward",
        )
        results = list(results)
        if has_close:
            close_done[close_index] = results[:3]
            del results[:3]
            if not has_open:
                gradient = results[0]
        if start == "first":
            cot_t = results.pop(0)
        if has_open:
            open_done[index] = results[:3]
            d_own, d_far, dq, d_mid = results[3:]
            pending = [d_own, swap(d_far), dq, d_mid, kept["x"], kept["normed"], mods[index], w_qkv[index]]
    gradient = gradient[:, :local].T

    def over_items(mine, other):
        total = mine + swap(other).astype(F32)
        rows = total.shape[0] // item_count
        sent = total.astype(BF16)
        share = lax.dynamic_slice_in_dim(total, item * rows, rows, 0)
        for shift in range(1, item_count):
            pairs = [(source, (source + shift) % item_count) for source in range(item_count)]
            piece = lax.dynamic_slice_in_dim(sent, (item + shift) % item_count * rows, rows, 0)
            share = share + lax.ppermute(piece, "item", pairs).astype(F32)
        return along_items(share.astype(BF16)).reshape(total.shape).astype(F32)

    def unpack(rows, blocks, height):
        return rows.reshape(blocks, height, width).transpose(1, 0, 2).reshape(height, blocks * width)

    opened = [over_items(open_done[index][0], open_done[index][1]) for index in range(layers)]
    closed = [over_items(close_done[index][0], close_done[index][1]) for index in range(layers)]
    down_rows = ff // 8
    up_blocks = ff // width
    up_end = down_rows + up_blocks * slice_rows
    down_grad = jnp.stack([rows[:down_rows] for rows in opened])
    up_grad = jnp.stack([unpack(rows[down_rows:up_end], up_blocks, slice_rows) for rows in opened])
    out_grad = jnp.stack([rows[up_end:] for rows in opened])
    qkv_grad = jnp.stack([unpack(rows, 3, slice_rows) for rows in closed])

    sums = jnp.stack(
        [
            jnp.sum(jnp.concatenate([close_done[index][2], open_done[index][2]], axis=0), axis=1)
            for index in range(layers)
        ]
    )
    sums = along_items(sums + swap(sums))
    rows = lax.dynamic_slice_in_dim(contexts, device * slice_rows, slice_rows, 1).astype(F32)
    ada_grad = jnp.sum(rows[:, None, :, None] * sums[:, :, None, :], axis=0)
    bias = jnp.sum(sums, axis=0)
    bias_rows = bias.shape[1] // 8
    bias_grad = lax.dynamic_slice_in_dim(bias, device * bias_rows, bias_rows, 1)
    shift_grad = lax.dynamic_slice_in_dim(bias, 3 * width + device * slice_rows, slice_rows, 1)
    field_shape = (1, rows_dev, cols_dev, width)
    return (
        final.reshape(field_shape),
        gradient.reshape(field_shape),
        qkv_grad,
        out_grad,
        up_grad,
        down_grad,
        ada_grad,
        bias_grad,
        shift_grad,
    )


def solution(mesh):
    lat_count, lon_count, item_count = mesh.shape["lat"], mesh.shape["lon"], mesh.shape["item"]
    if lat_count == 2 and lon_count == 4:
        body = functools.partial(fast_shards, lat_count, lon_count, item_count)
    else:
        body = shards
    return jax.shard_map(
        body,
        mesh=mesh,
        in_specs=(
            P("item", "lat", "lon", None),
            P("item"),
            P("item"),
            P(),
            P(),
            P(),
            P(),
            P(),
            P(),
            P("item", "lat", "lon", None),
        ),
        out_specs=(
            P("item", "lat", "lon", None),
            P("item", "lat", "lon", None),
            P(None, ("lat", "lon"), None),
            P(None, ("lat", "lon"), None),
            P(None, ("lat", "lon"), None),
            P(None, ("lat", "lon"), None),
            P(None, ("lat", "lon"), None),
            P(None, ("lat", "lon")),
            P(None, ("lat", "lon")),
        ),
        check_vma=False,
    )
```

```python
import functools
import math

import jax
import jax.numpy as jnp
from jax import lax
from jax.experimental import pallas as pl
from jax.experimental.pallas import tpu as pltpu
from jax.sharding import PartitionSpec as P

D = 384
HEADS = 6
HEAD_DIM = 64
STEPS = 2


def shortened(shard):
    return jax.tree.map(lambda a: a.astype(jnp.bfloat16) if a.dtype == jnp.float32 else a, shard)


def embedding(lead):
    half_width = D // 2
    lead_hours = 6.0 * (lead.astype(jnp.float32) + 1.0)
    frequencies = jnp.exp(
        -math.log(10000.0) * jnp.arange(half_width, dtype=jnp.float32) / half_width
    )
    angles = lead_hours * frequencies
    return jnp.concatenate([jnp.sin(angles), jnp.cos(angles)])


def pre_norm(values, shift_part, scale_part):
    centred = values - jnp.mean(values, axis=-1, keepdims=True)
    variance = jnp.mean(centred * centred, axis=-1, keepdims=True)
    return centred * lax.rsqrt(variance + 1e-06) * (1.0 + scale_part) + shift_part


def gather_keys(keys_values):
    band_rows = lax.all_gather(keys_values, "lon", axis=0, tiled=True)
    return lax.all_gather(band_rows, "lat", axis=0, tiled=True)


def spread_keys(key_value_grads):
    band_grads = lax.psum_scatter(
        key_value_grads.astype(jnp.bfloat16), "lat", scatter_dimension=0, tiled=True
    )
    return lax.psum_scatter(band_grads, "lon", scatter_dimension=0, tiled=True).astype(jnp.float32)


def forward_layer(current, modulation, weight_qkv, weight_out, weight_up, weight_down):
    local_rows, width = current.shape
    shift_attn, scale_attn, gate_attn, shift_mlp, scale_mlp, gate_mlp = modulation
    normed = pre_norm(current, shift_attn, scale_attn).astype(jnp.bfloat16)
    projected = jnp.dot(normed, weight_qkv, preferred_element_type=jnp.float32).astype(jnp.bfloat16)
    queries = projected[:, :width].reshape(local_rows, HEADS, HEAD_DIM)
    own_keys = projected[:, width:]
    gathered = gather_keys(own_keys)
    total_rows = gathered.shape[0]
    key_heads = gathered[:, :width].reshape(total_rows, HEADS, HEAD_DIM)
    value_heads = gathered[:, width:].reshape(total_rows, HEADS, HEAD_DIM)
    scores = jnp.einsum(
        "thd,nhd->htn", queries, key_heads, preferred_element_type=jnp.float32
    ) * HEAD_DIM ** (-0.5)
    log_total = jax.nn.logsumexp(scores, axis=-1, keepdims=True)
    probabilities = jnp.exp(scores - log_total).astype(jnp.bfloat16)
    mixed = jnp.einsum(
        "htn,nhd->thd", probabilities, value_heads, preferred_element_type=jnp.float32
    )
    mixed = mixed.reshape(local_rows, width).astype(jnp.bfloat16)
    attended = jnp.dot(mixed, weight_out, preferred_element_type=jnp.float32)
    middle = current + gate_attn * attended
    hidden_in = pre_norm(middle, shift_mlp, scale_mlp).astype(jnp.bfloat16)
    pre_act = jnp.dot(hidden_in, weight_up, preferred_element_type=jnp.float32)
    hidden = jax.nn.gelu(pre_act).astype(jnp.bfloat16)
    branch = jnp.dot(hidden, weight_down, preferred_element_type=jnp.float32)
    output = middle + gate_mlp * branch
    kept = (
        current,
        normed,
        queries,
        gathered,
        own_keys,
        log_total,
        mixed,
        attended,
        middle,
        hidden_in,
        pre_act,
        hidden,
        branch,
    )
    return (output, kept)


def backward_layer(grad_out, kept, modulation, weight_qkv, weight_out, weight_up, weight_down):
    (
        current,
        normed,
        queries,
        gathered,
        own_keys,
        log_total,
        mixed,
        attended,
        middle,
        hidden_in,
        pre_act,
        hidden,
        branch,
    ) = kept
    local_rows, width = current.shape
    total_rows = gathered.shape[0]
    shift_attn, scale_attn, gate_attn, shift_mlp, scale_mlp, gate_mlp = modulation
    factor = HEAD_DIM ** (-0.5)
    branch_grad = (gate_mlp * grad_out).astype(jnp.bfloat16)
    gate_mlp_grad = jnp.sum(grad_out * branch, axis=0)
    hidden_grad = jnp.dot(branch_grad, weight_down.T, preferred_element_type=jnp.float32)
    down_grad = jnp.dot(hidden.T, branch_grad, preferred_element_type=jnp.float32)
    _, gelu_back = jax.vjp(jax.nn.gelu, pre_act)
    pre_grad = gelu_back(hidden_grad)[0].astype(jnp.bfloat16)
    hidden_in_grad = jnp.dot(pre_grad, weight_up.T, preferred_element_type=jnp.float32)
    up_grad = jnp.dot(hidden_in.T, pre_grad, preferred_element_type=jnp.float32)
    _, second_back = jax.vjp(pre_norm, middle, shift_mlp, scale_mlp)
    middle_part, shift_mlp_grad, scale_mlp_grad = second_back(hidden_in_grad)
    middle_grad = grad_out + middle_part
    attended_grad = (gate_attn * middle_grad).astype(jnp.bfloat16)
    gate_attn_grad = jnp.sum(middle_grad * attended, axis=0)
    mixed_grad = jnp.dot(attended_grad, weight_out.T, preferred_element_type=jnp.float32).astype(
        jnp.bfloat16
    )
    out_grad = jnp.dot(mixed.T, attended_grad, preferred_element_type=jnp.float32)
    mixed_heads = mixed_grad.reshape(local_rows, HEADS, HEAD_DIM)
    key_heads = gathered[:, :width].reshape(total_rows, HEADS, HEAD_DIM)
    value_heads = gathered[:, width:].reshape(total_rows, HEADS, HEAD_DIM)
    scores = (
        jnp.einsum("thd,nhd->htn", queries, key_heads, preferred_element_type=jnp.float32) * factor
    )
    probabilities = jnp.exp(scores - log_total)
    prob_grads = jnp.einsum(
        "thd,nhd->htn", mixed_heads, value_heads, preferred_element_type=jnp.float32
    )
    centre = jnp.sum(prob_grads * probabilities, axis=-1, keepdims=True)
    score_grads = (probabilities * (prob_grads - centre)).astype(jnp.bfloat16)
    query_grads = (
        jnp.einsum("htn,nhd->thd", score_grads, key_heads, preferred_element_type=jnp.float32)
        * factor
    )
    value_grads = jnp.einsum(
        "htn,thd->nhd",
        probabilities.astype(jnp.bfloat16),
        mixed_heads,
        preferred_element_type=jnp.float32,
    )
    key_grads = (
        jnp.einsum("htn,thd->nhd", score_grads, queries, preferred_element_type=jnp.float32)
        * factor
    )
    key_value_grads = jnp.concatenate(
        [key_grads.reshape(total_rows, width), value_grads.reshape(total_rows, width)], axis=1
    )
    local_grads = spread_keys(key_value_grads)
    projected_grad = jnp.concatenate(
        [query_grads.reshape(local_rows, width), local_grads], axis=1
    ).astype(jnp.bfloat16)
    normed_grad = jnp.dot(projected_grad, weight_qkv.T, preferred_element_type=jnp.float32)
    qkv_grad = jnp.dot(normed.T, projected_grad, preferred_element_type=jnp.float32)
    _, first_back = jax.vjp(pre_norm, current, shift_attn, scale_attn)
    current_part, shift_attn_grad, scale_attn_grad = first_back(normed_grad)
    input_grad = middle_grad + current_part
    modulation_grad = jnp.concatenate(
        [
            shift_attn_grad,
            scale_attn_grad,
            gate_attn_grad,
            shift_mlp_grad,
            scale_mlp_grad,
            gate_mlp_grad,
        ]
    )
    return (input_grad, (qkv_grad, out_grad, up_grad, down_grad, modulation_grad))


def shards(fields, lead_index, rollout, w_qkv, w_out, w_up, w_down, w_ada, b_ada, cotangent):
    _, rows_dev, cols_dev, width = fields.shape
    local_rows = rows_dev * cols_dev
    layer_count = w_qkv.shape[0]
    context = jax.nn.silu(embedding(lead_index[0])).astype(jnp.bfloat16)
    context_wide = context.astype(jnp.float32)
    modulations = [
        (
            jnp.dot(context[None, :], w_ada[index], preferred_element_type=jnp.float32)[0]
            + b_ada[index]
        ).reshape(6, width)
        for index in range(layer_count)
    ]
    weight_sets = [
        (w_qkv[index], w_out[index], w_up[index], w_down[index]) for index in range(layer_count)
    ]
    count = rollout[0]
    current = fields.reshape(local_rows, width).astype(jnp.float32)
    saved = []
    for rollout_step in range(STEPS):
        updated = current
        kept_layers = []
        for index in range(layer_count):
            updated, kept = forward_layer(updated, modulations[index], *weight_sets[index])
            kept_layers.append(kept)
        current = jnp.where(rollout_step < count, updated, current)
        saved.append(kept_layers)
    gradient = cotangent.reshape(local_rows, width).astype(jnp.float32)
    summed = None
    shares = None
    for rollout_step in reversed(range(STEPS)):
        active = (rollout_step < count).astype(jnp.float32)
        inner = gradient * active
        layer_terms = [None] * layer_count
        for index in reversed(range(layer_count)):
            inner, layer_terms[index] = backward_layer(
                inner, saved[rollout_step][index], modulations[index], *weight_sets[index]
            )
        gradient = inner + (1.0 - active) * gradient
        modulation_grads = jnp.stack([terms[4] for terms in layer_terms])
        step_terms = (
            jnp.stack([terms[0] for terms in layer_terms]),
            jnp.stack([terms[1] for terms in layer_terms]),
            jnp.stack([terms[2] for terms in layer_terms]),
            jnp.stack([terms[3] for terms in layer_terms]),
            context_wide[None, :, None] * modulation_grads[:, None, :],
            modulation_grads,
            modulation_grads[:, 3 * width : 4 * width],
        )
        summed = step_terms if summed is None else jax.tree.map(jnp.add, summed, step_terms)
    shares = lax.psum_scatter(summed, ("lat", "lon"), scatter_dimension=1, tiled=True)
    totals = jax.tree.map(
        lambda part: part.astype(jnp.float32), lax.psum(shortened(shares), "item")
    )
    return (
        current.reshape(1, rows_dev, cols_dev, width),
        gradient.reshape(1, rows_dev, cols_dev, width),
        totals[0],
        totals[1],
        totals[2],
        totals[3],
        totals[4],
        totals[5],
        totals[6],
    )


F32 = jnp.float32
BF16 = jnp.bfloat16
GELU_A = math.sqrt(2.0 / math.pi)
GELU_B = 0.044715
LANES = 128
BLOCK = 256
PAIR = 2 * HEAD_DIM
SUM_ROWS = 40


def nn(left, right, precision=None):
    return lax.dot_general(
        left, right, (((1,), (0,)), ((), ())), preferred_element_type=F32, precision=precision
    )


def nt(left, right, precision=None):
    return lax.dot_general(
        left, right, (((1,), (1,)), ((), ())), preferred_element_type=F32, precision=precision
    )


def identity(size):
    rows = lax.broadcasted_iota(jnp.int32, (size, size), 0)
    columns = lax.broadcasted_iota(jnp.int32, (size, size), 1)
    return jnp.where(rows == columns, 1.0, 0.0).astype(BF16)


def turned(values):
    return nt(identity(values.shape[1]), values).astype(BF16)


def wide(column_tile, lanes):
    return jnp.concatenate([column_tile] * (lanes // LANES), axis=1)


def folded(values):
    pieces = [values[:, at : at + LANES] for at in range(0, values.shape[1], LANES)]
    return sum(pieces[1:], pieces[0])


def standardise(values):
    rows = values.shape[0]
    centred = values - jnp.sum(values, axis=0, keepdims=True) * (1.0 / rows)
    variance = jnp.sum(centred * centred, axis=0, keepdims=True) * (1.0 / rows)
    scale = lax.rsqrt(variance + 1e-06)
    return centred * scale, scale


def pre_norm_back(standard, scale, grad, gain):
    rows = standard.shape[0]
    inner = grad * gain
    first = jnp.sum(inner, axis=0, keepdims=True) * (1.0 / rows)
    second = jnp.sum(inner * standard, axis=0, keepdims=True) * (1.0 / rows)
    return scale * (inner - first - standard * second)


def part(mod_ref, index, lanes):
    return wide(mod_ref[index * D : (index + 1) * D, :], lanes)


def turn_into(source, out, at=0):
    for column in range(0, out.shape[0], BLOCK):
        width = min(BLOCK, out.shape[0] - column)
        out[column : column + width, :] = turned(source[:, at + column : at + column + width])


def prepare_kernel(context, w_ada, b_ada, w_qkv, w_out, w_up, w_down, mod, w_q_t, w_v_t, w_k, w_out_t, w_up_t, w_down_t):
    values = nn(context[...], w_ada[...])[0:1] + b_ada[...]
    for column in range(0, values.shape[1], LANES):
        tile = jnp.broadcast_to(values[:, column : column + LANES], (LANES, LANES))
        mod[column : column + LANES, :] = tile.T
    w_k[...] = w_qkv[:, D : 2 * D]
    turn_into(w_qkv, w_q_t)
    turn_into(w_qkv, w_v_t, 2 * D)
    turn_into(w_out, w_out_t)
    turn_into(w_up, w_up_t)
    turn_into(w_down, w_down_t)


def project(x, mod_ref, w_q_t, w_v_t, w_k, outs, at):
    q_out, kn_out, vt_out = outs
    lanes = x.shape[1]
    standard, _ = standardise(x)
    normed = (standard * (1.0 + part(mod_ref, 1, lanes)) + part(mod_ref, 0, lanes)).astype(BF16)
    kn_out[at, :] = nn(turned(normed), w_k[...]).astype(BF16)
    vt_out[:, at] = nn(w_v_t[...], normed).astype(BF16)
    q_out[:, at] = (nn(w_q_t[...], normed) * HEAD_DIM ** (-0.5)).astype(BF16)


def blocks_of(count, body):
    def step(index, _):
        body(pl.ds(pl.multiple_of(index * BLOCK, BLOCK), BLOCK))
        return 0

    lax.fori_loop(0, count // BLOCK, step, 0)


def first_kernel(own, flip_x, flip_y, flip_xy, mod, w_q_t, w_v_t, w_k, x_out, xb_out, *outs):
    for index, ref in enumerate((own, flip_x, flip_y, flip_xy)):
        rows = ref.shape[0]
        flat = turned(ref[...])
        xb_out[:, index * rows : (index + 1) * rows] = flat
        x_out[:, index * rows : (index + 1) * rows] = flat.astype(F32)
    blocks_of(x_out.shape[1], lambda at: project(x_out[:, at], mod, w_q_t, w_v_t, w_k, outs, at))


def head_at(pair, head):
    return pl.ds(pl.multiple_of(pair * PAIR + head * HEAD_DIM, HEAD_DIM), HEAD_DIM)


def padded(rows, head):
    zeros = jnp.zeros_like(rows)
    return jnp.concatenate([rows, zeros] if head == 0 else [zeros, rows], axis=0)


def forward_kernel(last, *refs):
    if last:
        active, x, x_step, *refs = refs
    else:
        x, *refs = refs
    q, kn_own, kn_far, vt_own, vt_far, mod, w_out_t, w_up_t, w_down_t, *refs = refs
    if not last:
        mod_next, w_q_t, w_v_t, w_k, *refs = refs
    lse, mixed, attended, middle, pre_act, branch, *refs = refs
    if last:
        final, x_next = refs
    else:
        x_next, xb_next, *next_outs = refs
    patches = x.shape[1]

    def heads(pair, _):
        columns = pl.ds(pl.multiple_of(pair * PAIR, PAIR), PAIR)
        for head in range(2):
            rows = head_at(pair, head)
            query = padded(q[rows, :], head)
            scores_own = nn(kn_own[:, columns], query)
            scores_far = nn(kn_far[:, columns], query)
            top = jnp.maximum(
                jnp.max(scores_own, axis=0, keepdims=True), jnp.max(scores_far, axis=0, keepdims=True)
            )
            ones = jnp.ones((16, patches), BF16)
            value_own = jnp.concatenate([vt_own[rows, :], ones], axis=0)
            value_far = jnp.concatenate([vt_far[rows, :], ones], axis=0)
            total = nn(value_own, jnp.exp(scores_own - top).astype(BF16)) + nn(
                value_far, jnp.exp(scores_far - top).astype(BF16)
            )
            weight = total[HEAD_DIM : HEAD_DIM + 1]
            mixed[rows, :] = (total[:HEAD_DIM] * (1.0 / weight)).astype(BF16)
            lse[pair, head : head + 1, :] = top + jnp.log(weight)
        return 0

    lax.fori_loop(0, HEADS // 2, heads, 0)

    def dense(at):
        att = nn(w_out_t[...], mixed[:, at])
        attended[:, at] = att.astype(BF16)
        mid = x[:, at] + part(mod, 2, BLOCK) * att
        middle[:, at] = mid.astype(BF16)
        standard, _ = standardise(mid)
        hidden_in = (standard * (1.0 + part(mod, 4, BLOCK)) + part(mod, 3, BLOCK)).astype(BF16)
        act = nn(w_up_t[...], hidden_in)
        pre_act[:, at] = act.astype(BF16)
        hidden = (0.5 * act * (1.0 + jnp.tanh(GELU_A * (act + GELU_B * act * act * act)))).astype(BF16)
        down = nn(w_down_t[...], hidden)
        branch[:, at] = down.astype(BF16)
        out = mid + part(mod, 5, BLOCK) * down
        x_next[:, at] = out
        if not last:
            xb_next[:, at] = out.astype(BF16)
            project(out, mod_next, w_q_t, w_v_t, w_k, next_outs, at)

    blocks_of(patches, dense)
    if last:
        own = final.shape[0]
        final[...] = jnp.where(active[0] > 0.0, x_next[:, :own], x_step[:, :own]).T


def put_grads(left_ref, right, where, count, at, mine, other, before):
    rows = [left_ref[pl.ds(pl.multiple_of(where[place] * count, 16), count), :] for place in range(2)]
    product = nt(jnp.concatenate(rows, axis=0), right)
    for column in range(0, product.shape[1], LANES):
        low = product[:count, column : column + LANES]
        high = product[count:, column : column + LANES]
        if before is not None:
            low = low + before[0][at : at + count, :]
            high = high + before[1][at : at + count, :]
        mine[at : at + count, :] = low.astype(mine.dtype)
        other[at : at + count, :] = high.astype(other.dtype)
        at += count


def dense_back_kernel(has_close, has_open, has_before, start, layers, layer_sums, waits, *refs):
    refs = list(refs)

    def take(count):
        taken = refs[:count]
        del refs[:count]
        return taken

    take(waits)
    where, active = take(2)
    close_before = open_before = None
    if has_close:
        d_own, d_got, dq, d_mid_in, x_in, mod_in, w_qkv_all = take(7)
        if has_before[0]:
            close_before = take(3)
    if start == "first":
        cots = take(4)
    elif start == "cross":
        cots = take(1)
    if has_open:
        mixed, attended, middle, pre_act, branch, mod, w_out_all, w_up_all, w_down_all = take(9)
        if has_before[1]:
            open_before = take(3)
    else:
        (context,) = take(1)
        all_sums = take(layer_sums)
    if has_close:
        close_mine, close_other, close_mods = take(3)
    if start == "first":
        (cot_out,) = take(1)
    if has_open:
        open_mine, open_other, open_mods, d_mid_out, do_out, cen_out = take(6)
    else:
        g_out, sums_out = take(2)
    sems = take(1)[0]
    copies = {}
    if has_close:
        grads_scr, normed_scr, w_qkv = take(3)
        copies["qkv"] = pltpu.make_async_copy(w_qkv_all.at[layers[0]], w_qkv, sems.at[0])
    if has_open:
        bg_scr, hid_scr, pg_scr, hin_scr, ag_scr, w_out, w_up, w_down = take(8)
        copies["down"] = pltpu.make_async_copy(w_down_all.at[layers[1]], w_down, sems.at[1])
        copies["up"] = pltpu.make_async_copy(w_up_all.at[layers[1]], w_up, sems.at[2])
        copies["out"] = pltpu.make_async_copy(w_out_all.at[layers[1]], w_out, sems.at[3])
    else:
        (g_scr,) = take(1)
    for copy in copies.values():
        copy.start()

    patches = middle.shape[1] if has_open else x_in.shape[1]
    if has_close:
        close_mods[...] = close_before[2][...] if close_before else jnp.zeros_like(close_mods)
    if has_open:
        open_mods[...] = open_before[2][...] if open_before else jnp.zeros_like(open_mods)
    if start == "first":
        for index, ref in enumerate(cots):
            rows = ref.shape[0]
            cot_out[:, index * rows : (index + 1) * rows] = turned(ref[...])
    if has_close:
        copies["qkv"].wait()
    if has_open and not has_close:
        for name in ("down", "up", "out"):
            copies[name].wait()

    def close(at):
        grads = jnp.concatenate(
            [dq[:, at], (d_own[:, at] + d_got[:, at].astype(F32)).astype(BF16)], axis=0
        )
        grads_scr[:, at] = grads
        back = nn(w_qkv[...], grads)
        standard, scale = standardise(x_in[:, at].astype(F32))
        gain = 1.0 + part(mod_in, 1, BLOCK)
        normed_scr[:, at] = (standard * gain + part(mod_in, 0, BLOCK)).astype(BF16)
        close_mods[0:D, :] += folded(back)
        close_mods[D : 2 * D, :] += folded(back * standard)
        g = d_mid_in[:, at] + pre_norm_back(standard, scale, back, gain)
        if start == "cross":
            g = g + (1.0 - active[0]) * cots[0][:, at].astype(F32)
        return g

    def dense(at, g):
        branch_grad = (part(mod, 5, BLOCK) * g).astype(BF16)
        bg_scr[:, at] = branch_grad
        open_mods[3 * D : 4 * D, :] += folded(g * branch[:, at].astype(F32))
        hidden_grad = nn(w_down[...], branch_grad)
        act = pre_act[:, at].astype(F32)
        square = act * act
        bent = jnp.tanh(GELU_A * act * (1.0 + GELU_B * square))
        half = 0.5 * (1.0 + bent)
        hid_scr[:, at] = (act * half).astype(BF16)
        slope = half + (0.5 * GELU_A) * act * (1.0 - bent * bent) * (1.0 + (3.0 * GELU_B) * square)
        pre_grad = (slope * hidden_grad).astype(BF16)
        pg_scr[:, at] = pre_grad
        back = nn(w_up[...], pre_grad)
        standard, scale = standardise(middle[:, at].astype(F32))
        gain = 1.0 + part(mod, 4, BLOCK)
        hin_scr[:, at] = (standard * gain + part(mod, 3, BLOCK)).astype(BF16)
        open_mods[D : 2 * D, :] += folded(back)
        open_mods[2 * D : 3 * D, :] += folded(back * standard)
        d_mid = g + pre_norm_back(standard, scale, back, gain)
        d_mid_out[:, at] = d_mid
        open_mods[0:D, :] += folded(d_mid * attended[:, at].astype(F32))
        att_grad = (part(mod, 2, BLOCK) * d_mid).astype(BF16)
        ag_scr[:, at] = att_grad
        mixed_grad = nn(w_out[...], att_grad).astype(BF16)
        do_out[:, at] = mixed_grad
        product = mixed_grad.astype(F32) * mixed[:, at].astype(F32)
        for head in range(HEADS):
            cen_out[head // 2, head % 2 : head % 2 + 1, at] = jnp.sum(
                product[head * HEAD_DIM : (head + 1) * HEAD_DIM], axis=0, keepdims=True
            )

    if has_close and has_open:

        def both(at):
            d_mid_out[:, at] = close(at)

        blocks_of(patches, both)
        for name in ("down", "up", "out"):
            copies[name].wait()
        blocks_of(patches, lambda at: dense(at, d_mid_out[:, at]))
    elif has_open:
        blocks_of(patches, lambda at: dense(at, cot_out[:, at].astype(F32) * active[0]))
    else:

        def alone(at):
            g_scr[:, at] = close(at)

        blocks_of(patches, alone)
        g_out[...] = g_scr[:, : g_out.shape[0]].T

    if has_close:
        put_grads(normed_scr, grads_scr[...], where, D // 8, 0, close_mine, close_other, close_before)
    if has_open:
        count = w_down.shape[0] // 8
        put_grads(hid_scr, bg_scr[...], where, count, 0, open_mine, open_other, open_before)
        at = count * (D // LANES)
        put_grads(hin_scr, pg_scr[...], where, D // 8, at, open_mine, open_other, open_before)
        at += (w_up.shape[1] // LANES) * (D // 8)
        put_grads(mixed, ag_scr[...], where, D // 8, at, open_mine, open_other, open_before)
    else:
        ones = jnp.ones((8, LANES), F32)
        sums_out[...] = jnp.zeros_like(sums_out)
        row = 0
        for ref in [close_mods] + all_sums:
            line = nt(ones, ref[...], precision=lax.Precision.HIGHEST)[0:1]
            for column in range(0, line.shape[1], LANES):
                sums_out[row : row + 1, :] = line[:, column : column + LANES]
                row += 1
        for column in range(0, D, LANES):
            sums_out[row : row + 1, :] = context[0:1, column : column + LANES].astype(F32)
            row += 1


def attend_back_kernel(has_before, waits, q, kn, vt, lse, d_out, centre, *refs):
    if has_before:
        before, *refs = refs
    d_kv, dq_out, kt_scr, vn_scr = refs[waits:]
    for column in range(0, D, LANES):
        kt_scr[column : column + LANES, :] = turned(kn[:, column : column + LANES])
    for column in range(0, vt.shape[1], BLOCK):
        vn_scr[column : column + BLOCK, :] = turned(vt[:, column : column + BLOCK])

    def heads(pair, _):
        columns = pl.ds(pl.multiple_of(pair * PAIR, PAIR), PAIR)
        for head in range(2):
            rows = head_at(pair, head)
            value_rows = pl.ds(pl.multiple_of(D + pair * PAIR + head * HEAD_DIM, HEAD_DIM), HEAD_DIM)
            query = q[rows, :]
            out_grad = d_out[rows, :]
            scores = nn(kn[:, columns], padded(query, head))
            probs = jnp.exp(scores - lse[pair, head : head + 1, :])
            prob_grads = nn(vn_scr[:, columns], padded(out_grad, head))
            score_grads = (probs * (prob_grads - centre[pair, head : head + 1, :])).astype(BF16)
            d_kv[value_rows, :] = nt(out_grad, probs.astype(BF16)).astype(d_kv.dtype)
            d_kv[rows, :] = nt(query, score_grads).astype(d_kv.dtype)
            term = nn(kt_scr[rows, :], score_grads)
            if has_before:
                term = (before[rows, :] + term) * HEAD_DIM ** (-0.5)
            dq_out[rows, :] = term.astype(dq_out.dtype)
        return 0

    lax.fori_loop(0, HEADS // 2, heads, 0)


def split_kernel(item_count, place, *refs):
    *halves, own = refs[: -item_count - 1] + refs[-item_count - 1 : -item_count]
    sent, total_scr = refs[-item_count:-1], refs[-1]
    item = place[0]
    share = own.shape[0]
    at = 0
    for mine, other in zip(halves[::2], halves[1::2]):
        rows = mine.shape[0]
        total_scr[at : at + rows, :] = mine[...] + other[...].astype(F32)
        at += rows
    if at < total_scr.shape[0]:
        total_scr[at:, :] = jnp.zeros((total_scr.shape[0] - at, LANES), F32)

    def rows_of(shift):
        place = lax.rem(item + shift, item_count)
        return pl.ds(pl.multiple_of(place * share, 16), share)

    own[...] = total_scr[rows_of(0), :]
    for shift, out in enumerate(sent):
        out[...] = total_scr[rows_of(shift + 1), :].astype(BF16)


def gather_kernel(item_count, place, *refs):
    layers = 2
    last_parts, shares, shares_1, lines = (refs[at * item_count : (at + 1) * item_count] for at in range(4))
    qkv_out, out_out, up_out, down_out, ada_out, bias_out, *scratch = refs[4 * item_count :]
    part_scr, share_scr, open_scr, open_1_scr, sum_scr = scratch
    item, device = place[0], place[1]
    for shift in range(item_count):
        source = lax.rem(item - shift + item_count, item_count)
        part_scr[source] = last_parts[shift][...]
        share_scr[source] = shares[shift][...]
        rows = shares_1[shift].shape[0]
        open_1_scr[pl.ds(pl.multiple_of(source * rows, 16), rows), :] = shares_1[shift][...]
        sum_scr[source] = lines[shift][...]
    share = share_scr.shape[1]
    for index in range(item_count - 1):
        open_scr[index * share : (index + 1) * share, :] = share_scr[index + 1]
    opened = (open_scr, open_1_scr)
    closed_1 = share_scr.at[0]
    slice_rows = qkv_out.shape[1]
    down_rows = down_out.shape[1]
    for index in range(layers):
        at = 0
        ref = opened[index]
        for column in range(0, D, LANES):
            down_out[index, :, column : column + LANES] = ref[at : at + down_rows, :].astype(F32)
            at += down_rows
        for column in range(0, up_out.shape[2], LANES):
            up_out[index, :, column : column + LANES] = ref[at : at + slice_rows, :].astype(F32)
            at += slice_rows
        for column in range(0, D, LANES):
            out_out[index, :, column : column + LANES] = ref[at : at + slice_rows, :].astype(F32)
            at += slice_rows
        for tile in range(3 * D // LANES):
            rows = slice(tile * slice_rows, (tile + 1) * slice_rows)
            if index == 1:
                total = closed_1[rows, :].astype(F32)
            else:
                total = part_scr[0, rows, :].astype(F32)
                for other in range(1, item_count):
                    total = total + part_scr[other, rows, :].astype(F32)
            qkv_out[index, :, tile * LANES : (tile + 1) * LANES] = total
    tiles = 6 * D // LANES
    contexts = []
    for other in range(item_count):
        line = jnp.concatenate([sum_scr[other, layers * tiles + c : layers * tiles + c + 1, :] for c in range(3)], axis=1)
        contexts.append(line)
    square = jnp.concatenate(contexts + [jnp.zeros((8 - item_count, D), F32)], axis=0)
    spot = lax.broadcasted_iota(jnp.int32, (slice_rows, D), 1)
    want = lax.broadcasted_iota(jnp.int32, (slice_rows, D), 0) + device * slice_rows
    pick = jnp.where(spot == want, 1.0, 0.0).astype(BF16)
    columns = nt(pick, square.astype(BF16))
    for index in range(layers):
        for tile in range(tiles):
            row = index * tiles + tile
            total = None
            flat = None
            for other in range(item_count):
                line = sum_scr[other, row : row + 1, :]
                term = columns[:, other : other + 1] * line
                total = term if total is None else total + term
                flat = line if flat is None else flat + line
            ada_out[index, :, tile * LANES : (tile + 1) * LANES] = total
            bias_out[index : index + 1, tile * LANES : (tile + 1) * LANES] = flat


VMEM = pl.BlockSpec(memory_space=pltpu.VMEM)
SMEM = pl.BlockSpec(memory_space=pltpu.SMEM)
HBM = pl.BlockSpec(memory_space=pl.ANY)


def layer_block(array, index):
    return pl.BlockSpec((None,) + array.shape[1:], lambda step: (index,) + (0,) * (array.ndim - 1))


def call(body, args, outs, scratch=(), flops=0, name=None, grid=()):
    arrays = [arg[0] if isinstance(arg, tuple) else arg for arg in args]
    specs = [arg[1] if isinstance(arg, tuple) else VMEM for arg in args]
    return pl.pallas_call(
        body,
        out_shape=[jax.ShapeDtypeStruct(shape, kind) for shape, kind in outs],
        grid=grid,
        in_specs=specs,
        out_specs=[VMEM] * len(outs),
        scratch_shapes=[one if not isinstance(one, tuple) else pltpu.VMEM(*one) for one in scratch],
        compiler_params=pltpu.CompilerParams(vmem_limit_bytes=VMEM_LIMIT),
        cost_estimate=pl.CostEstimate(flops=flops, bytes_accessed=0, transcendentals=0),
        name=name,
    )(*arrays)


VMEM_LIMIT = 22 * 1024 * 1024


def fast_shards(
    lat_count, lon_count, item_count,
    fields, lead_index, rollout, w_qkv, w_out, w_up, w_down, w_ada, b_ada, cotangent,
):
    _, rows_dev, cols_dev, width = fields.shape
    local = rows_dev * cols_dev
    layers = w_qkv.shape[0]
    ff = w_up.shape[2]
    patches = 4 * local
    device = lax.axis_index("lat") * lon_count + lax.axis_index("lon")
    item = lax.axis_index("item")
    where = jnp.stack([device, device ^ 1]).astype(jnp.int32)
    spot = jnp.stack([item, device]).astype(jnp.int32)
    active = (1 < rollout[0]).astype(F32)[None]

    def plane_flip(value, flip_lat, flip_y):
        pairs = [
            (a * lon_count + b, (a ^ flip_lat) * lon_count + (b ^ (2 * flip_y)))
            for a in range(lat_count)
            for b in range(lon_count)
        ]
        return lax.ppermute(value, ("lat", "lon"), pairs)

    def swap(value):
        return lax.ppermute(value, "lon", [(index, index ^ 1) for index in range(lon_count)])

    def around(shift):
        return [(source, (source + shift) % item_count) for source in range(item_count)]

    def from_items(value):
        return [value] + [lax.ppermute(value, "item", around(shift)) for shift in range(1, item_count)]

    own = fields.reshape(local, width)
    field_parts = [own, plane_flip(own, 1, 0), plane_flip(own, 0, 1), plane_flip(own, 1, 1)]
    cot_own = cotangent.reshape(local, width)
    cot_parts = [cot_own, plane_flip(cot_own, 1, 0), plane_flip(cot_own, 0, 1), plane_flip(cot_own, 1, 1)]

    context = jax.nn.silu(embedding(lead_index[0])).astype(BF16)
    context = jnp.broadcast_to(context[None, :], (16, width))
    square = (width, patches)
    natural = (patches, width)
    prepared = []
    for index in range(layers):
        prepared.append(
            call(
                prepare_kernel,
                [context]
                + [
                    (array, layer_block(array, index))
                    for array in (w_ada, b_ada.reshape(layers, 1, 6 * width), w_qkv, w_out, w_up, w_down)
                ],
                [
                    ((6 * width, LANES), F32),
                    ((width, width), BF16),
                    ((width, width), BF16),
                    ((width, width), BF16),
                    ((width, width), BF16),
                    ((ff, width), BF16),
                    ((width, ff), BF16),
                ],
                flops=2 * 256 * (5 * width * width + 2 * width * ff),
                name="prepare",
                grid=(1,),
            )
        )
    mods = [one[0] for one in prepared]

    project_outs = [(square, F32), (square, BF16), (square, BF16), (natural, BF16), (square, BF16)]
    dense_flops = 2 * patches * (width * 3 * width + width * width + 2 * width * ff)
    score_flops = 2 * patches * 2 * patches * width * 4
    x, xb, *projected = call(
        first_kernel,
        [*field_parts, *prepared[0][:4]],
        project_outs,
        flops=2 * patches * width * 4 * width,
        name="first",
    )
    saved = []
    for step in range(STEPS):
        for index in range(layers):
            q, kn, vt = projected
            kn_far, vt_far = swap(kn), swap(vt)
            last = step == STEPS - 1 and index == layers - 1
            if index == 0 and step > 0:
                x_step = x
            following = prepared[(index + 1) % layers]
            lse, mixed, attended, middle, pre_act, branch, *results = call(
                functools.partial(forward_kernel, last),
                ([(active, SMEM), x, x_step] if last else [x])
                + [q, kn, kn_far, vt, vt_far, mods[index], *prepared[index][4:]]
                + ([] if last else list(following[:4])),
                [
                    ((HEADS // 2, 2, patches), F32),
                    (square, BF16),
                    (square, BF16),
                    (square, BF16),
                    ((ff, patches), BF16),
                    (square, BF16),
                ]
                + ([((local, width), F32)] if last else project_outs),
                [(square, F32)] if last else [],
                flops=dense_flops + 2 * score_flops,
                name="forward",
            )
            saved.append((xb, [mixed, attended, middle, pre_act, branch], (q, kn, kn_far, vt, vt_far, lse)))
            if last:
                final = results[0]
            else:
                x, xb, *projected = results

    slice_rows = width // 8
    open_rows = 2 * (ff // 8) * (width // LANES) + slice_rows * (width // LANES)
    close_rows = slice_rows * (3 * width // LANES)
    order = [(step, index) for step in reversed(range(STEPS)) for index in reversed(range(layers))]
    open_done = [None] * layers
    close_done = [None] * layers
    shares = [None] * layers
    pending = None
    for place in range(len(order) + 1):
        has_close = pending is not None
        has_open = place < len(order)
        use = [order[place - 1][1], order[place][1] if has_open else 0]
        waits = [shares[use[0]][0]] if has_close and shares[use[0]] else []
        args = [(value, HBM) for value in waits] + [(where, SMEM), (active, SMEM)]
        outs = []
        scratch = [pltpu.SemaphoreType.DMA((4,))]
        has_before = [False, False]
        start = ""
        if has_close:
            args += pending
            if close_done[use[0]] is not None:
                has_before[0] = True
                args += close_done[use[0]]
            outs += [((close_rows, LANES), F32)]
            outs += [((close_rows, LANES), BF16 if has_before[0] else F32), ((2 * width, LANES), F32)]
            scratch += [((3 * width, patches), BF16), (square, BF16), ((width, 3 * width), BF16)]
        if place == 0:
            start = "first"
            args += cot_parts
            outs += [(square, BF16)]
        elif has_open and order[place][0] != order[place - 1][0]:
            start = "cross"
            args += [cot_t]
        if has_open:
            step, index = order[place]
            xb, kept, heads = saved[step * layers + index]
            args += kept + [mods[index], (w_out, HBM), (w_up, HBM), (w_down, HBM)]
            if open_done[index] is not None:
                has_before[1] = True
                args += open_done[index]
            outs += [
                ((open_rows, LANES), F32),
                ((open_rows, LANES), BF16 if has_before[1] else F32),
                ((4 * width, LANES), F32),
                (square, F32),
                (square, BF16),
                ((HEADS // 2, 2, patches), F32),
            ]
            scratch += [
                (square, BF16),
                ((ff, patches), BF16),
                ((ff, patches), BF16),
                (square, BF16),
                (square, BF16),
                ((width, width), BF16),
                ((width, ff), BF16),
                ((ff, width), BF16),
            ]
            sums = []
        else:
            sums = [open_done[0][2], close_done[1][2], open_done[1][2]]
            args += [context] + sums
            outs += [((local, width), F32), ((SUM_ROWS, LANES), F32)]
            scratch += [(square, F32)]
        results = list(
            call(
                functools.partial(dense_back_kernel, has_close, has_open, has_before, start, use, len(sums), len(waits)),
                args,
                outs,
                scratch,
                flops=2 * dense_flops if has_open else dense_flops // 20,
                name="dense_back" if has_open else "close_back",
            )
        )
        if has_close:
            close_done[use[0]] = results[:3]
            del results[:3]
        if start == "first":
            cot_t = results.pop(0)
        if not has_open:
            gradient, line = results
            break
        open_done[index] = results[:3]
        d_mid, d_out, centre = results[3:]
        q, kn, kn_far, vt, vt_far, lse = heads
        d_far, dq = call(
            functools.partial(attend_back_kernel, False, 0),
            [q, kn_far, vt_far, lse, d_out, centre],
            [((2 * width, patches), BF16), (square, F32)],
            [(square, BF16), (natural, BF16)],
            flops=5 * score_flops // 2,
            name="attend_far",
        )
        d_got = swap(d_far)
        waits = []
        if has_before[1]:
            halves = [open_done[index][0], swap(open_done[index][1])]
            if index == 0:
                halves = [close_done[1][0], swap(close_done[1][1])] + halves
            share_rows = -(-sum(half.shape[0] for half in halves[::2]) // (16 * item_count)) * 16
            share, *sent = call(
                functools.partial(split_kernel, item_count),
                [(spot, SMEM)] + halves,
                [((share_rows, LANES), F32)] + [((share_rows, LANES), BF16)] * (item_count - 1),
                [((item_count * share_rows, LANES), F32)],
                name="split",
            )
            waits = [share]
            if index == 0:
                waits += shares[1][1:]
            for shift, value in enumerate(sent):
                share = share + lax.ppermute(value, "item", around(shift + 1)).astype(F32)
            shares[index] = from_items(share.astype(BF16))
        d_own, dq = call(
            functools.partial(attend_back_kernel, True, len(waits)),
            [q, kn, vt, lse, d_out, centre, dq] + [(value, HBM) for value in waits],
            [((2 * width, patches), F32), (square, BF16)],
            [(square, BF16), (natural, BF16)],
            flops=5 * score_flops // 20,
            name="attend_own",
        )
        pending = [d_own, d_got, dq, d_mid, xb, mods[index], (w_qkv, HBM)]

    closed = (close_done[0][0] + swap(close_done[0][1]).astype(F32)).astype(BF16)
    tiles = 6 * width // LANES
    swapped = swap(line)
    keep = jnp.arange(SUM_ROWS)[:, None] < layers * tiles
    line = jnp.where(keep, line + swapped, line)
    qkv_grad, out_grad, up_grad, down_grad, ada_grad, bias = call(
        functools.partial(gather_kernel, item_count),
        [(spot, SMEM), *from_items(closed), *shares[0], *shares[1], *from_items(line)],
        [
            ((layers, slice_rows, 3 * width), F32),
            ((layers, slice_rows, width), F32),
            ((layers, slice_rows, ff), F32),
            ((layers, ff // 8, width), F32),
            ((layers, slice_rows, 6 * width), F32),
            ((layers, 6 * width), F32),
        ],
        [
            ((item_count, close_rows, LANES), BF16),
            ((item_count, close_rows, LANES), BF16),
            ((open_rows, LANES), BF16),
            ((item_count * shares[1][0].shape[0], LANES), BF16),
            ((item_count, SUM_ROWS, LANES), F32),
        ],
        name="gather",
    )
    bias_rows = bias.shape[1] // 8
    bias_grad = lax.dynamic_slice_in_dim(bias, device * bias_rows, bias_rows, 1)
    shift_grad = lax.dynamic_slice_in_dim(bias, 3 * width + device * slice_rows, slice_rows, 1)
    field_shape = (1, rows_dev, cols_dev, width)
    return (
        final.reshape(field_shape),
        gradient.reshape(field_shape),
        qkv_grad,
        out_grad,
        up_grad,
        down_grad,
        ada_grad,
        bias_grad,
        shift_grad,
    )


def solution(mesh):
    lat_count, lon_count, item_count = mesh.shape["lat"], mesh.shape["lon"], mesh.shape["item"]
    if lat_count == 2 and lon_count == 4:
        body = functools.partial(fast_shards, lat_count, lon_count, item_count)
    else:
        body = shards
    return jax.shard_map(
        body,
        mesh=mesh,
        in_specs=(
            P("item", "lat", "lon", None),
            P("item"),
            P("item"),
            P(),
            P(),
            P(),
            P(),
            P(),
            P(),
            P("item", "lat", "lon", None),
        ),
        out_specs=(
            P("item", "lat", "lon", None),
            P("item", "lat", "lon", None),
            P(None, ("lat", "lon"), None),
            P(None, ("lat", "lon"), None),
            P(None, ("lat", "lon"), None),
            P(None, ("lat", "lon"), None),
            P(None, ("lat", "lon"), None),
            P(None, ("lat", "lon")),
            P(None, ("lat", "lon")),
        ),
        check_vma=False,
    )
```

```python
import functools
import math

import jax
import jax.numpy as jnp
from jax import lax
from jax.experimental import pallas as pl
from jax.experimental.pallas import tpu as pltpu
from jax.sharding import PartitionSpec as P

D = 384
HEADS = 6
HEAD_DIM = 64
STEPS = 2


def shortened(shard):
    return jax.tree.map(lambda a: a.astype(jnp.bfloat16) if a.dtype == jnp.float32 else a, shard)


def embedding(lead):
    half_width = D // 2
    lead_hours = 6.0 * (lead.astype(jnp.float32) + 1.0)
    frequencies = jnp.exp(
        -math.log(10000.0) * jnp.arange(half_width, dtype=jnp.float32) / half_width
    )
    angles = lead_hours * frequencies
    return jnp.concatenate([jnp.sin(angles), jnp.cos(angles)])


def pre_norm(values, shift_part, scale_part):
    centred = values - jnp.mean(values, axis=-1, keepdims=True)
    variance = jnp.mean(centred * centred, axis=-1, keepdims=True)
    return centred * lax.rsqrt(variance + 1e-06) * (1.0 + scale_part) + shift_part


def gather_keys(keys_values):
    band_rows = lax.all_gather(keys_values, "lon", axis=0, tiled=True)
    return lax.all_gather(band_rows, "lat", axis=0, tiled=True)


def spread_keys(key_value_grads):
    band_grads = lax.psum_scatter(
        key_value_grads.astype(jnp.bfloat16), "lat", scatter_dimension=0, tiled=True
    )
    return lax.psum_scatter(band_grads, "lon", scatter_dimension=0, tiled=True).astype(jnp.float32)


def forward_layer(current, modulation, weight_qkv, weight_out, weight_up, weight_down):
    local_rows, width = current.shape
    shift_attn, scale_attn, gate_attn, shift_mlp, scale_mlp, gate_mlp = modulation
    normed = pre_norm(current, shift_attn, scale_attn).astype(jnp.bfloat16)
    projected = jnp.dot(normed, weight_qkv, preferred_element_type=jnp.float32).astype(jnp.bfloat16)
    queries = projected[:, :width].reshape(local_rows, HEADS, HEAD_DIM)
    own_keys = projected[:, width:]
    gathered = gather_keys(own_keys)
    total_rows = gathered.shape[0]
    key_heads = gathered[:, :width].reshape(total_rows, HEADS, HEAD_DIM)
    value_heads = gathered[:, width:].reshape(total_rows, HEADS, HEAD_DIM)
    scores = jnp.einsum(
        "thd,nhd->htn", queries, key_heads, preferred_element_type=jnp.float32
    ) * HEAD_DIM ** (-0.5)
    log_total = jax.nn.logsumexp(scores, axis=-1, keepdims=True)
    probabilities = jnp.exp(scores - log_total).astype(jnp.bfloat16)
    mixed = jnp.einsum(
        "htn,nhd->thd", probabilities, value_heads, preferred_element_type=jnp.float32
    )
    mixed = mixed.reshape(local_rows, width).astype(jnp.bfloat16)
    attended = jnp.dot(mixed, weight_out, preferred_element_type=jnp.float32)
    middle = current + gate_attn * attended
    hidden_in = pre_norm(middle, shift_mlp, scale_mlp).astype(jnp.bfloat16)
    pre_act = jnp.dot(hidden_in, weight_up, preferred_element_type=jnp.float32)
    hidden = jax.nn.gelu(pre_act).astype(jnp.bfloat16)
    branch = jnp.dot(hidden, weight_down, preferred_element_type=jnp.float32)
    output = middle + gate_mlp * branch
    kept = (
        current,
        normed,
        queries,
        gathered,
        own_keys,
        log_total,
        mixed,
        attended,
        middle,
        hidden_in,
        pre_act,
        hidden,
        branch,
    )
    return (output, kept)


def backward_layer(grad_out, kept, modulation, weight_qkv, weight_out, weight_up, weight_down):
    (
        current,
        normed,
        queries,
        gathered,
        own_keys,
        log_total,
        mixed,
        attended,
        middle,
        hidden_in,
        pre_act,
        hidden,
        branch,
    ) = kept
    local_rows, width = current.shape
    total_rows = gathered.shape[0]
    shift_attn, scale_attn, gate_attn, shift_mlp, scale_mlp, gate_mlp = modulation
    factor = HEAD_DIM ** (-0.5)
    branch_grad = (gate_mlp * grad_out).astype(jnp.bfloat16)
    gate_mlp_grad = jnp.sum(grad_out * branch, axis=0)
    hidden_grad = jnp.dot(branch_grad, weight_down.T, preferred_element_type=jnp.float32)
    down_grad = jnp.dot(hidden.T, branch_grad, preferred_element_type=jnp.float32)
    _, gelu_back = jax.vjp(jax.nn.gelu, pre_act)
    pre_grad = gelu_back(hidden_grad)[0].astype(jnp.bfloat16)
    hidden_in_grad = jnp.dot(pre_grad, weight_up.T, preferred_element_type=jnp.float32)
    up_grad = jnp.dot(hidden_in.T, pre_grad, preferred_element_type=jnp.float32)
    _, second_back = jax.vjp(pre_norm, middle, shift_mlp, scale_mlp)
    middle_part, shift_mlp_grad, scale_mlp_grad = second_back(hidden_in_grad)
    middle_grad = grad_out + middle_part
    attended_grad = (gate_attn * middle_grad).astype(jnp.bfloat16)
    gate_attn_grad = jnp.sum(middle_grad * attended, axis=0)
    mixed_grad = jnp.dot(attended_grad, weight_out.T, preferred_element_type=jnp.float32).astype(
        jnp.bfloat16
    )
    out_grad = jnp.dot(mixed.T, attended_grad, preferred_element_type=jnp.float32)
    mixed_heads = mixed_grad.reshape(local_rows, HEADS, HEAD_DIM)
    key_heads = gathered[:, :width].reshape(total_rows, HEADS, HEAD_DIM)
    value_heads = gathered[:, width:].reshape(total_rows, HEADS, HEAD_DIM)
    scores = (
        jnp.einsum("thd,nhd->htn", queries, key_heads, preferred_element_type=jnp.float32) * factor
    )
    probabilities = jnp.exp(scores - log_total)
    prob_grads = jnp.einsum(
        "thd,nhd->htn", mixed_heads, value_heads, preferred_element_type=jnp.float32
    )
    centre = jnp.sum(prob_grads * probabilities, axis=-1, keepdims=True)
    score_grads = (probabilities * (prob_grads - centre)).astype(jnp.bfloat16)
    query_grads = (
        jnp.einsum("htn,nhd->thd", score_grads, key_heads, preferred_element_type=jnp.float32)
        * factor
    )
    value_grads = jnp.einsum(
        "htn,thd->nhd",
        probabilities.astype(jnp.bfloat16),
        mixed_heads,
        preferred_element_type=jnp.float32,
    )
    key_grads = (
        jnp.einsum("htn,thd->nhd", score_grads, queries, preferred_element_type=jnp.float32)
        * factor
    )
    key_value_grads = jnp.concatenate(
        [key_grads.reshape(total_rows, width), value_grads.reshape(total_rows, width)], axis=1
    )
    local_grads = spread_keys(key_value_grads)
    projected_grad = jnp.concatenate(
        [query_grads.reshape(local_rows, width), local_grads], axis=1
    ).astype(jnp.bfloat16)
    normed_grad = jnp.dot(projected_grad, weight_qkv.T, preferred_element_type=jnp.float32)
    qkv_grad = jnp.dot(normed.T, projected_grad, preferred_element_type=jnp.float32)
    _, first_back = jax.vjp(pre_norm, current, shift_attn, scale_attn)
    current_part, shift_attn_grad, scale_attn_grad = first_back(normed_grad)
    input_grad = middle_grad + current_part
    modulation_grad = jnp.concatenate(
        [
            shift_attn_grad,
            scale_attn_grad,
            gate_attn_grad,
            shift_mlp_grad,
            scale_mlp_grad,
            gate_mlp_grad,
        ]
    )
    return (input_grad, (qkv_grad, out_grad, up_grad, down_grad, modulation_grad))


def shards(fields, lead_index, rollout, w_qkv, w_out, w_up, w_down, w_ada, b_ada, cotangent):
    _, rows_dev, cols_dev, width = fields.shape
    local_rows = rows_dev * cols_dev
    layer_count = w_qkv.shape[0]
    context = jax.nn.silu(embedding(lead_index[0])).astype(jnp.bfloat16)
    context_wide = context.astype(jnp.float32)
    modulations = [
        (
            jnp.dot(context[None, :], w_ada[index], preferred_element_type=jnp.float32)[0]
            + b_ada[index]
        ).reshape(6, width)
        for index in range(layer_count)
    ]
    weight_sets = [
        (w_qkv[index], w_out[index], w_up[index], w_down[index]) for index in range(layer_count)
    ]
    count = rollout[0]
    current = fields.reshape(local_rows, width).astype(jnp.float32)
    saved = []
    for rollout_step in range(STEPS):
        updated = current
        kept_layers = []
        for index in range(layer_count):
            updated, kept = forward_layer(updated, modulations[index], *weight_sets[index])
            kept_layers.append(kept)
        current = jnp.where(rollout_step < count, updated, current)
        saved.append(kept_layers)
    gradient = cotangent.reshape(local_rows, width).astype(jnp.float32)
    summed = None
    shares = None
    for rollout_step in reversed(range(STEPS)):
        active = (rollout_step < count).astype(jnp.float32)
        inner = gradient * active
        layer_terms = [None] * layer_count
        for index in reversed(range(layer_count)):
            inner, layer_terms[index] = backward_layer(
                inner, saved[rollout_step][index], modulations[index], *weight_sets[index]
            )
        gradient = inner + (1.0 - active) * gradient
        modulation_grads = jnp.stack([terms[4] for terms in layer_terms])
        step_terms = (
            jnp.stack([terms[0] for terms in layer_terms]),
            jnp.stack([terms[1] for terms in layer_terms]),
            jnp.stack([terms[2] for terms in layer_terms]),
            jnp.stack([terms[3] for terms in layer_terms]),
            context_wide[None, :, None] * modulation_grads[:, None, :],
            modulation_grads,
            modulation_grads[:, 3 * width : 4 * width],
        )
        summed = step_terms if summed is None else jax.tree.map(jnp.add, summed, step_terms)
    shares = lax.psum_scatter(summed, ("lat", "lon"), scatter_dimension=1, tiled=True)
    totals = jax.tree.map(
        lambda part: part.astype(jnp.float32), lax.psum(shortened(shares), "item")
    )
    return (
        current.reshape(1, rows_dev, cols_dev, width),
        gradient.reshape(1, rows_dev, cols_dev, width),
        totals[0],
        totals[1],
        totals[2],
        totals[3],
        totals[4],
        totals[5],
        totals[6],
    )


F32 = jnp.float32
BF16 = jnp.bfloat16
GELU_A = math.sqrt(2.0 / math.pi)
GELU_B = 0.044715
LANES = 128
BLOCK = 256
PAIR = 2 * HEAD_DIM
SUM_ROWS = 40


def nn(left, right, precision=None):
    return lax.dot_general(
        left, right, (((1,), (0,)), ((), ())), preferred_element_type=F32, precision=precision
    )


def nt(left, right, precision=None):
    return lax.dot_general(
        left, right, (((1,), (1,)), ((), ())), preferred_element_type=F32, precision=precision
    )


def identity(size):
    rows = lax.broadcasted_iota(jnp.int32, (size, size), 0)
    columns = lax.broadcasted_iota(jnp.int32, (size, size), 1)
    return jnp.where(rows == columns, 1.0, 0.0).astype(BF16)


def turned(values):
    return nt(identity(values.shape[1]), values).astype(BF16)


def wide(column_tile, lanes):
    return jnp.concatenate([column_tile] * (lanes // LANES), axis=1)


def folded(values):
    pieces = [values[:, at : at + LANES] for at in range(0, values.shape[1], LANES)]
    return sum(pieces[1:], pieces[0])


def standardise(values):
    rows = values.shape[0]
    centred = values - jnp.sum(values, axis=0, keepdims=True) * (1.0 / rows)
    variance = jnp.sum(centred * centred, axis=0, keepdims=True) * (1.0 / rows)
    scale = lax.rsqrt(variance + 1e-06)
    return centred * scale, scale


def pre_norm_back(standard, scale, grad, gain):
    rows = standard.shape[0]
    inner = grad * gain
    first = jnp.sum(inner, axis=0, keepdims=True) * (1.0 / rows)
    second = jnp.sum(inner * standard, axis=0, keepdims=True) * (1.0 / rows)
    return scale * (inner - first - standard * second)


def part(mod_ref, index, lanes):
    return wide(mod_ref[index * D : (index + 1) * D, :], lanes)


def turn_into(source, out, at=0):
    for column in range(0, out.shape[0], BLOCK):
        width = min(BLOCK, out.shape[0] - column)
        out[column : column + width, :] = turned(source[:, at + column : at + column + width])


def prepare_first_kernel(index, waits, context, w_ada, b_ada, w_qkv, *refs):
    mod, w_q_t, w_v_t, w_k = refs[waits:]
    values = nn(context[...], w_ada[index])[0:1] + b_ada[index : index + 1, :]
    for column in range(0, values.shape[1], LANES):
        tile = jnp.broadcast_to(values[:, column : column + LANES], (LANES, LANES))
        mod[column : column + LANES, :] = tile.T
    w_k[...] = w_qkv[index, :, D : 2 * D]
    turn_into(w_qkv.at[index], w_q_t)
    turn_into(w_qkv.at[index], w_v_t, 2 * D)


def prepare_rest_kernel(index, w_out, w_up, w_down, w_out_t, w_up_t, w_down_t):
    turn_into(w_out.at[index], w_out_t)
    turn_into(w_up.at[index], w_up_t)
    turn_into(w_down.at[index], w_down_t)


def project(x, mod_ref, w_q_t, w_v_t, w_k, outs, at):
    q_out, kn_out, vt_out = outs
    lanes = x.shape[1]
    standard, _ = standardise(x)
    normed = (standard * (1.0 + part(mod_ref, 1, lanes)) + part(mod_ref, 0, lanes)).astype(BF16)
    kn_out[at, :] = nn(turned(normed), w_k[...]).astype(BF16)
    vt_out[:, at] = nn(w_v_t[...], normed).astype(BF16)
    q_out[:, at] = (nn(w_q_t[...], normed) * HEAD_DIM ** (-0.5)).astype(BF16)


def blocks_of(count, body):
    def step(index, _):
        body(pl.ds(pl.multiple_of(index * BLOCK, BLOCK), BLOCK))
        return 0

    lax.fori_loop(0, count // BLOCK, step, 0)


def first_kernel(own, flip_x, flip_y, flip_xy, mod, w_q_t, w_v_t, w_k, x_out, xb_out, *outs):
    for index, ref in enumerate((own, flip_x, flip_y, flip_xy)):
        rows = ref.shape[0]
        flat = turned(ref[...])
        xb_out[:, index * rows : (index + 1) * rows] = flat
        x_out[:, index * rows : (index + 1) * rows] = flat.astype(F32)
    blocks_of(x_out.shape[1], lambda at: project(x_out[:, at], mod, w_q_t, w_v_t, w_k, outs, at))


def head_at(pair, head):
    return pl.ds(pl.multiple_of(pair * PAIR + head * HEAD_DIM, HEAD_DIM), HEAD_DIM)


def padded(rows, head):
    zeros = jnp.zeros_like(rows)
    return jnp.concatenate([rows, zeros] if head == 0 else [zeros, rows], axis=0)


def forward_kernel(last, *refs):
    if last:
        active, x, x_step, *refs = refs
    else:
        x, *refs = refs
    q, kn_own, kn_far, vt_own, vt_far, mod, w_out_t, w_up_t, w_down_t, *refs = refs
    if not last:
        mod_next, w_q_t, w_v_t, w_k, *refs = refs
    lse, mixed, attended, middle, pre_act, branch, *refs = refs
    if last:
        final, x_next = refs
    else:
        x_next, xb_next, *next_outs = refs
    patches = x.shape[1]

    def heads(pair, _):
        columns = pl.ds(pl.multiple_of(pair * PAIR, PAIR), PAIR)
        for head in range(2):
            rows = head_at(pair, head)
            query = padded(q[rows, :], head)
            scores_own = nn(kn_own[:, columns], query)
            scores_far = nn(kn_far[:, columns], query)
            top = jnp.maximum(
                jnp.max(scores_own, axis=0, keepdims=True), jnp.max(scores_far, axis=0, keepdims=True)
            )
            ones = jnp.ones((16, patches), BF16)
            value_own = jnp.concatenate([vt_own[rows, :], ones], axis=0)
            value_far = jnp.concatenate([vt_far[rows, :], ones], axis=0)
            total = nn(value_own, jnp.exp(scores_own - top).astype(BF16)) + nn(
                value_far, jnp.exp(scores_far - top).astype(BF16)
            )
            weight = total[HEAD_DIM : HEAD_DIM + 1]
            mixed[rows, :] = (total[:HEAD_DIM] * (1.0 / weight)).astype(BF16)
            lse[pair, head : head + 1, :] = top + jnp.log(weight)
        return 0

    lax.fori_loop(0, HEADS // 2, heads, 0)

    def dense(at):
        att = nn(w_out_t[...], mixed[:, at])
        attended[:, at] = att.astype(BF16)
        mid = x[:, at] + part(mod, 2, BLOCK) * att
        middle[:, at] = mid.astype(BF16)
        standard, _ = standardise(mid)
        hidden_in = (standard * (1.0 + part(mod, 4, BLOCK)) + part(mod, 3, BLOCK)).astype(BF16)
        act = nn(w_up_t[...], hidden_in)
        pre_act[:, at] = act.astype(BF16)
        hidden = (0.5 * act * (1.0 + jnp.tanh(GELU_A * (act + GELU_B * act * act * act)))).astype(BF16)
        down = nn(w_down_t[...], hidden)
        branch[:, at] = down.astype(BF16)
        out = mid + part(mod, 5, BLOCK) * down
        x_next[:, at] = out
        if not last:
            xb_next[:, at] = out.astype(BF16)
            project(out, mod_next, w_q_t, w_v_t, w_k, next_outs, at)

    blocks_of(patches, dense)
    if last:
        own = final.shape[0]
        final[...] = jnp.where(active[0] > 0.0, x_next[:, :own], x_step[:, :own]).T


def put_grads(left_ref, right, where, count, at, mine, other, before):
    rows = [left_ref[pl.ds(pl.multiple_of(where[place] * count, 16), count), :] for place in range(2)]
    product = nt(jnp.concatenate(rows, axis=0), right)
    for column in range(0, product.shape[1], LANES):
        low = product[:count, column : column + LANES]
        high = product[count:, column : column + LANES]
        if before is not None:
            low = low + before[0][at : at + count, :]
            high = high + before[1][at : at + count, :]
        mine[at : at + count, :] = low.astype(mine.dtype)
        other[at : at + count, :] = high.astype(other.dtype)
        at += count


def dense_back_kernel(has_close, has_open, has_before, start, layers, layer_sums, waits, *refs):
    refs = list(refs)

    def take(count):
        taken = refs[:count]
        del refs[:count]
        return taken

    take(waits)
    where, active = take(2)
    close_before = open_before = None
    if has_close:
        d_own, d_got, dq, d_mid_in, x_in, mod_in, w_qkv_all = take(7)
        if has_before[0]:
            close_before = take(3)
    if start == "first":
        cots = take(4)
    elif start == "cross":
        cots = take(1)
    if has_open:
        mixed, attended, middle, pre_act, branch, mod, w_out_all, w_up_all, w_down_all = take(9)
        if has_before[1]:
            open_before = take(3)
    else:
        (context,) = take(1)
        all_sums = take(layer_sums)
    if has_close:
        close_mine, close_other, close_mods = take(3)
    if start == "first":
        (cot_out,) = take(1)
    if has_open:
        open_mine, open_other, open_mods, d_mid_out, do_out, cen_out = take(6)
    else:
        g_out, sums_out = take(2)
        sums_at = close_before[1].shape[0]
    sems = take(1)[0]
    copies = {}
    if has_close:
        grads_scr, normed_scr, w_qkv = take(3)
        copies["qkv"] = pltpu.make_async_copy(w_qkv_all.at[layers[0]], w_qkv, sems.at[0])
    if has_open:
        bg_scr, hid_scr, pg_scr, hin_scr, ag_scr, w_out, w_up, w_down = take(8)
        copies["down"] = pltpu.make_async_copy(w_down_all.at[layers[1]], w_down, sems.at[1])
        copies["up"] = pltpu.make_async_copy(w_up_all.at[layers[1]], w_up, sems.at[2])
        copies["out"] = pltpu.make_async_copy(w_out_all.at[layers[1]], w_out, sems.at[3])
    else:
        (g_scr,) = take(1)
    for copy in copies.values():
        copy.start()

    patches = middle.shape[1] if has_open else x_in.shape[1]
    if has_close:
        close_mods[...] = close_before[2][...] if close_before else jnp.zeros_like(close_mods)
    if has_open:
        open_mods[...] = open_before[2][...] if open_before else jnp.zeros_like(open_mods)
    if start == "first":
        for index, ref in enumerate(cots):
            rows = ref.shape[0]
            cot_out[:, index * rows : (index + 1) * rows] = turned(ref[...])
    if has_close:
        copies["qkv"].wait()
    if has_open and not has_close:
        for name in ("down", "up", "out"):
            copies[name].wait()

    def close(at):
        grads = jnp.concatenate(
            [dq[:, at], (d_own[:, at] + d_got[:, at].astype(F32)).astype(BF16)], axis=0
        )
        grads_scr[:, at] = grads
        back = nn(w_qkv[...], grads)
        standard, scale = standardise(x_in[:, at].astype(F32))
        gain = 1.0 + part(mod_in, 1, BLOCK)
        normed_scr[:, at] = (standard * gain + part(mod_in, 0, BLOCK)).astype(BF16)
        close_mods[0:D, :] += folded(back)
        close_mods[D : 2 * D, :] += folded(back * standard)
        g = d_mid_in[:, at] + pre_norm_back(standard, scale, back, gain)
        if start == "cross":
            g = g + (1.0 - active[0]) * cots[0][:, at].astype(F32)
        return g

    def dense(at, g):
        branch_grad = (part(mod, 5, BLOCK) * g).astype(BF16)
        bg_scr[:, at] = branch_grad
        open_mods[3 * D : 4 * D, :] += folded(g * branch[:, at].astype(F32))
        hidden_grad = nn(w_down[...], branch_grad)
        act = pre_act[:, at].astype(F32)
        square = act * act
        bent = jnp.tanh(GELU_A * act * (1.0 + GELU_B * square))
        half = 0.5 * (1.0 + bent)
        hid_scr[:, at] = (act * half).astype(BF16)
        slope = half + (0.5 * GELU_A) * act * (1.0 - bent * bent) * (1.0 + (3.0 * GELU_B) * square)
        pre_grad = (slope * hidden_grad).astype(BF16)
        pg_scr[:, at] = pre_grad
        back = nn(w_up[...], pre_grad)
        standard, scale = standardise(middle[:, at].astype(F32))
        gain = 1.0 + part(mod, 4, BLOCK)
        hin_scr[:, at] = (standard * gain + part(mod, 3, BLOCK)).astype(BF16)
        open_mods[D : 2 * D, :] += folded(back)
        open_mods[2 * D : 3 * D, :] += folded(back * standard)
        d_mid = g + pre_norm_back(standard, scale, back, gain)
        d_mid_out[:, at] = d_mid
        open_mods[0:D, :] += folded(d_mid * attended[:, at].astype(F32))
        att_grad = (part(mod, 2, BLOCK) * d_mid).astype(BF16)
        ag_scr[:, at] = att_grad
        mixed_grad = nn(w_out[...], att_grad).astype(BF16)
        do_out[:, at] = mixed_grad
        product = mixed_grad.astype(F32) * mixed[:, at].astype(F32)
        for head in range(HEADS):
            cen_out[head // 2, head % 2 : head % 2 + 1, at] = jnp.sum(
                product[head * HEAD_DIM : (head + 1) * HEAD_DIM], axis=0, keepdims=True
            )

    if has_close and has_open:

        def both(at):
            d_mid_out[:, at] = close(at)

        blocks_of(patches, both)
        for name in ("down", "up", "out"):
            copies[name].wait()
        blocks_of(patches, lambda at: dense(at, d_mid_out[:, at]))
    elif has_open:
        blocks_of(patches, lambda at: dense(at, cot_out[:, at].astype(F32) * active[0]))
    else:

        def alone(at):
            g_scr[:, at] = close(at)

        blocks_of(patches, alone)
        g_out[...] = g_scr[:, : g_out.shape[0]].T

    if has_close:
        put_grads(normed_scr, grads_scr[...], where, D // 8, 0, close_mine, close_other, close_before)
    if has_open:
        count = w_down.shape[0] // 8
        put_grads(hid_scr, bg_scr[...], where, count, 0, open_mine, open_other, open_before)
        at = count * (D // LANES)
        put_grads(hin_scr, pg_scr[...], where, D // 8, at, open_mine, open_other, open_before)
        at += (w_up.shape[1] // LANES) * (D // 8)
        put_grads(mixed, ag_scr[...], where, D // 8, at, open_mine, open_other, open_before)
    else:
        ones = jnp.ones((8, LANES), F32)
        sums_out[...] = jnp.zeros_like(sums_out)
        row = 0
        for ref in [close_mods] + all_sums:
            line = nt(ones, ref[...], precision=lax.Precision.HIGHEST)[0:1]
            for column in range(0, line.shape[1], LANES):
                sums_out[row : row + 1, :] = line[:, column : column + LANES]
                row += 1
        for column in range(0, D, LANES):
            sums_out[row : row + 1, :] = context[0:1, column : column + LANES].astype(F32)
            row += 1
        put_pair(close_other, sums_at, sums_out[...])


def attend_back_kernel(has_before, waits, q, kn, vt, lse, d_out, centre, *refs):
    if has_before:
        before, *refs = refs
    d_kv, dq_out, kt_scr, vn_scr = refs[waits:]
    for column in range(0, D, LANES):
        kt_scr[column : column + LANES, :] = turned(kn[:, column : column + LANES])
    for column in range(0, vt.shape[1], BLOCK):
        vn_scr[column : column + BLOCK, :] = turned(vt[:, column : column + BLOCK])

    def heads(pair, _):
        columns = pl.ds(pl.multiple_of(pair * PAIR, PAIR), PAIR)
        for head in range(2):
            rows = head_at(pair, head)
            value_rows = pl.ds(pl.multiple_of(D + pair * PAIR + head * HEAD_DIM, HEAD_DIM), HEAD_DIM)
            query = q[rows, :]
            out_grad = d_out[rows, :]
            scores = nn(kn[:, columns], padded(query, head))
            probs = jnp.exp(scores - lse[pair, head : head + 1, :])
            prob_grads = nn(vn_scr[:, columns], padded(out_grad, head))
            score_grads = (probs * (prob_grads - centre[pair, head : head + 1, :])).astype(BF16)
            d_kv[value_rows, :] = nt(out_grad, probs.astype(BF16)).astype(d_kv.dtype)
            d_kv[rows, :] = nt(query, score_grads).astype(d_kv.dtype)
            term = nn(kt_scr[rows, :], score_grads)
            if has_before:
                term = (before[rows, :] + term) * HEAD_DIM ** (-0.5)
            dq_out[rows, :] = term.astype(dq_out.dtype)
        return 0

    lax.fori_loop(0, HEADS // 2, heads, 0)


def split_kernel(where, *refs):
    *halves, keep, sent, total_scr = refs
    rows_half = keep.shape[0]
    at = 0
    for mine, other in zip(halves[::2], halves[1::2]):
        rows = mine.shape[0]
        total_scr[at : at + rows, :] = mine[...] + other[...].astype(F32)
        at += rows
    if at < total_scr.shape[0]:
        total_scr[at:, :] = jnp.zeros((total_scr.shape[0] - at, LANES), F32)
    odd = where[3]
    keep[...] = total_scr[pl.ds(pl.multiple_of(odd * rows_half, 16), rows_half), :]
    sent[...] = total_scr[pl.ds(pl.multiple_of((1 - odd) * rows_half, 16), rows_half), :].astype(BF16)


def pair_sum_kernel(keep, got, late, out):
    out[...] = (keep[...] + got[...].astype(F32)).astype(BF16)


def put_pair(out, at, values):
    rows = values.shape[0]
    high = values.astype(BF16)
    out[at : at + rows, :] = high
    out[at + rows : at + 2 * rows, :] = (values - high.astype(F32)).astype(BF16)


def get_pair(ref, at, rows):
    return ref[at : at + rows, :].astype(F32) + ref[at + rows : at + 2 * rows, :].astype(F32)


def join_kernel(sum_count, mine, sums, got, out):
    rows = mine.shape[0]
    out[:rows, :] = (mine[...] + got[:rows, :].astype(F32)).astype(BF16)
    other = get_pair(got, rows, SUM_ROWS)
    summed = lax.broadcasted_iota(jnp.int32, (SUM_ROWS, LANES), 0) < sum_count
    put_pair(out, rows, sums[...] + jnp.where(summed, other, 0.0))


def pair_kernel(rows, where, own, got, out):
    out[:rows, :] = (own[:rows, :].astype(F32) + got[:rows, :].astype(F32)).astype(BF16)
    odd = where[3]
    size = 2 * SUM_ROWS
    out[pl.ds(pl.multiple_of(rows + odd * size, 16), size), :] = own[rows:, :]
    out[pl.ds(pl.multiple_of(rows + (1 - odd) * size, 16), size), :] = got[rows:, :]


def gather_kernel(item_count, where, *refs):
    layers = 2
    own, got, *halves = refs[:6]
    qkv_out, out_out, up_out, down_out, ada_out, bias_out, shift_out, *scratch = refs[6:]
    total_scr, sum_scr = scratch[:2], scratch[2]
    device, odd, high = where[0], where[3], where[4]
    for index in range(layers):
        kept, other = halves[2 * index], halves[2 * index + 1]
        rows = kept.shape[0]
        total_scr[index][pl.ds(pl.multiple_of(odd * rows, 16), rows), :] = kept[...]
        total_scr[index][pl.ds(pl.multiple_of((1 - odd) * rows, 16), rows), :] = other[...]
    slice_rows = qkv_out.shape[1]
    down_rows = down_out.shape[1]
    close_rows = slice_rows * (3 * D // LANES)
    for other in range(2):
        at = close_rows + other * 2 * SUM_ROWS
        sum_scr[2 * high + other] = get_pair(own, at, SUM_ROWS)
        sum_scr[2 * (1 - high) + other] = get_pair(got, at, SUM_ROWS)
    for index in range(layers):
        ref = total_scr[index]
        at = close_rows if index == 0 else 0
        for column in range(0, D, LANES):
            down_out[index, :, column : column + LANES] = ref[at : at + down_rows, :].astype(F32)
            at += down_rows
        for column in range(0, up_out.shape[2], LANES):
            up_out[index, :, column : column + LANES] = ref[at : at + slice_rows, :].astype(F32)
            at += slice_rows
        for column in range(0, D, LANES):
            out_out[index, :, column : column + LANES] = ref[at : at + slice_rows, :].astype(F32)
            at += slice_rows
        for tile in range(3 * D // LANES):
            rows = slice(tile * slice_rows, (tile + 1) * slice_rows)
            if index == 1:
                total = total_scr[0][rows, :].astype(F32)
            else:
                total = own[rows, :].astype(F32) + got[rows, :].astype(F32)
            qkv_out[index, :, tile * LANES : (tile + 1) * LANES] = total
    tiles = 6 * D // LANES
    contexts = []
    for other in range(item_count):
        line = jnp.concatenate([sum_scr[other, layers * tiles + c : layers * tiles + c + 1, :] for c in range(3)], axis=1)
        contexts.append(line)
    square = jnp.concatenate(contexts + [jnp.zeros((8 - item_count, D), F32)], axis=0)
    spot = lax.broadcasted_iota(jnp.int32, (slice_rows, D), 1)
    want = lax.broadcasted_iota(jnp.int32, (slice_rows, D), 0) + device * slice_rows
    pick = jnp.where(spot == want, 1.0, 0.0).astype(BF16)
    columns = nt(pick, square.astype(BF16))
    bias_scr, shift_scr = scratch[3:]
    bias_rows = bias_out.shape[1]
    for index in range(layers):
        flats = []
        for tile in range(tiles):
            row = index * tiles + tile
            total = None
            flat = None
            for other in range(item_count):
                line = sum_scr[other, row : row + 1, :]
                term = columns[:, other : other + 1] * line
                total = term if total is None else total + term
                flat = line if flat is None else flat + line
            ada_out[index, :, tile * LANES : (tile + 1) * LANES] = total
            flats.append(flat)
        flat = jnp.concatenate(flats, axis=1)
        for place in range(flat.shape[1] // bias_rows):
            bias_scr[place, index : index + 1, :] = flat[:, place * bias_rows : (place + 1) * bias_rows]
            at = 3 * D + place * slice_rows
            shift_scr[place, index : index + 1, :] = flat[:, at : at + slice_rows]
    bias_out[...] = bias_scr[device]
    shift_out[...] = shift_scr[device]


VMEM = pl.BlockSpec(memory_space=pltpu.VMEM)
SMEM = pl.BlockSpec(memory_space=pltpu.SMEM)
HBM = pl.BlockSpec(memory_space=pl.ANY)


def layer_block(array, index):
    return pl.BlockSpec((None,) + array.shape[1:], lambda step: (index,) + (0,) * (array.ndim - 1))


def call(body, args, outs, scratch=(), flops=0, name=None, grid=()):
    arrays = [arg[0] if isinstance(arg, tuple) else arg for arg in args]
    specs = [arg[1] if isinstance(arg, tuple) else VMEM for arg in args]
    return pl.pallas_call(
        body,
        out_shape=[jax.ShapeDtypeStruct(shape, kind) for shape, kind in outs],
        grid=grid,
        in_specs=specs,
        out_specs=[VMEM] * len(outs),
        scratch_shapes=[one if not isinstance(one, tuple) else pltpu.VMEM(*one) for one in scratch],
        compiler_params=pltpu.CompilerParams(vmem_limit_bytes=VMEM_LIMIT),
        cost_estimate=pl.CostEstimate(flops=flops, bytes_accessed=0, transcendentals=0),
        name=name,
    )(*arrays)


VMEM_LIMIT = 16 * 1024 * 1024


def fast_shards(
    lat_count, lon_count, item_count,
    fields, lead_index, rollout, w_qkv, w_out, w_up, w_down, w_ada, b_ada, cotangent,
):
    _, rows_dev, cols_dev, width = fields.shape
    local = rows_dev * cols_dev
    layers = w_qkv.shape[0]
    ff = w_up.shape[2]
    patches = 4 * local
    device = lax.axis_index("lat") * lon_count + lax.axis_index("lon")
    item = lax.axis_index("item")
    where = jnp.stack([device, device ^ 1, item, item & 1, item >> 1]).astype(jnp.int32)
    active = (1 < rollout[0]).astype(F32)[None]

    def plane_flip(value, flip_lat, flip_y):
        pairs = [
            (a * lon_count + b, (a ^ flip_lat) * lon_count + (b ^ (2 * flip_y)))
            for a in range(lat_count)
            for b in range(lon_count)
        ]
        return lax.ppermute(value, ("lat", "lon"), pairs)

    def swap(value):
        return lax.ppermute(value, "lon", [(index, index ^ 1) for index in range(lon_count)])

    def with_item(value, flip):
        return lax.ppermute(value, "item", [(index, index ^ flip) for index in range(item_count)])

    own = fields.reshape(local, width)
    field_parts = [own, plane_flip(own, 1, 0), plane_flip(own, 0, 1), plane_flip(own, 1, 1)]
    cot_own = cotangent.reshape(local, width)
    cot_parts = [cot_own, plane_flip(cot_own, 1, 0), plane_flip(cot_own, 0, 1), plane_flip(cot_own, 1, 1)]

    context = jax.nn.silu(embedding(lead_index[0])).astype(BF16)
    context = jnp.broadcast_to(context[None, :], (16, width))
    square = (width, patches)
    natural = (patches, width)
    first_parts = []
    rest_parts = []
    for index in range(layers):
        waits = [(where, SMEM), (active, SMEM)] if index == 0 else []
        first_parts.append(
            call(
                functools.partial(prepare_first_kernel, index, len(waits)),
                [context, w_ada, b_ada, w_qkv] + waits,
                [((6 * width, LANES), F32)] + [((width, width), BF16)] * 3,
                name="prepare_first",
            )
        )
        rest_parts.append(
            call(
                functools.partial(prepare_rest_kernel, index),
                [w_out, w_up, w_down],
                [((width, width), BF16), ((ff, width), BF16), ((width, ff), BF16)],
                name="prepare_rest",
            )
        )
    mods = [one[0] for one in first_parts]

    project_outs = [(square, F32), (square, BF16), (square, BF16), (natural, BF16), (square, BF16)]
    dense_flops = 2 * patches * (width * 3 * width + width * width + 2 * width * ff)
    score_flops = 2 * patches * 2 * patches * width * 4
    x, xb, *projected = call(
        first_kernel,
        [*field_parts, *first_parts[0]],
        project_outs,
        flops=2 * patches * width * 4 * width,
        name="first",
    )
    saved = []
    for step in range(STEPS):
        for index in range(layers):
            q, kn, vt = projected
            kn_far, vt_far = swap(kn), swap(vt)
            last = step == STEPS - 1 and index == layers - 1
            if index == 0 and step > 0:
                x_step = x
            following = list(first_parts[(index + 1) % layers])
            lse, mixed, attended, middle, pre_act, branch, *results = call(
                functools.partial(forward_kernel, last),
                ([(active, SMEM), x, x_step] if last else [x])
                + [q, kn, kn_far, vt, vt_far, mods[index], *rest_parts[index]]
                + ([] if last else following),
                [
                    ((HEADS // 2, 2, patches), F32),
                    (square, BF16),
                    (square, BF16),
                    (square, BF16),
                    ((ff, patches), BF16),
                    (square, BF16),
                ]
                + ([((local, width), F32)] if last else project_outs),
                [(square, F32)] if last else [],
                flops=dense_flops + 2 * score_flops,
                name="forward",
            )
            saved.append((xb, [mixed, attended, middle, pre_act, branch], (q, kn, kn_far, vt, vt_far, lse)))
            if last:
                final = results[0]
            else:
                x, xb, *projected = results

    slice_rows = width // 8
    open_rows = 2 * (ff // 8) * (width // LANES) + slice_rows * (width // LANES)
    close_rows = slice_rows * (3 * width // LANES)
    order = [(step, index) for step in reversed(range(STEPS)) for index in reversed(range(layers))]
    open_done = [None] * layers
    close_done = [None] * layers
    reduced = [None] * layers
    pending = None
    for place in range(len(order) + 1):
        has_close = pending is not None
        has_open = place < len(order)
        use = [order[place - 1][1], order[place][1] if has_open else 0]
        waits = [reduced[use[0]][0]] if has_close and reduced[use[0]] else []
        if not has_open:
            waits.append(reduced[1][2])
        args = [(value, HBM) for value in waits] + [(where, SMEM), (active, SMEM)]
        outs = []
        scratch = [pltpu.SemaphoreType.DMA((4,))]
        has_before = [False, False]
        start = ""
        if has_close:
            args += pending
            if close_done[use[0]] is not None:
                has_before[0] = True
                args += close_done[use[0]]
            outs += [((close_rows, LANES), F32)]
            sent_rows = close_rows + (0 if has_open else 2 * SUM_ROWS)
            outs += [((sent_rows, LANES), BF16 if has_before[0] else F32), ((2 * width, LANES), F32)]
            scratch += [((3 * width, patches), BF16), (square, BF16), ((width, 3 * width), BF16)]
        if place == 0:
            start = "first"
            args += cot_parts
            outs += [(square, BF16)]
        elif has_open and order[place][0] != order[place - 1][0]:
            start = "cross"
            args += [cot_t]
        if has_open:
            step, index = order[place]
            xb, kept, heads = saved[step * layers + index]
            args += kept + [mods[index], (w_out, HBM), (w_up, HBM), (w_down, HBM)]
            if open_done[index] is not None:
                has_before[1] = True
                args += open_done[index]
            outs += [
                ((open_rows, LANES), F32),
                ((open_rows, LANES), BF16 if has_before[1] else F32),
                ((4 * width, LANES), F32),
                (square, F32),
                (square, BF16),
                ((HEADS // 2, 2, patches), F32),
            ]
            scratch += [
                (square, BF16),
                ((ff, patches), BF16),
                ((ff, patches), BF16),
                (square, BF16),
                (square, BF16),
                ((width, width), BF16),
                ((width, ff), BF16),
                ((ff, width), BF16),
            ]
            sums = []
        else:
            sums = [open_done[0][2], close_done[1][2], open_done[1][2]]
            args += [context] + sums
            outs += [((local, width), F32), ((SUM_ROWS, LANES), F32)]
            scratch += [(square, F32)]
        results = list(
            call(
                functools.partial(dense_back_kernel, has_close, has_open, has_before, start, use, len(sums), len(waits)),
                args,
                outs,
                scratch,
                flops=2 * dense_flops if has_open else 0,
                name="dense_back" if has_open else "close_back",
            )
        )
        if has_close:
            close_done[use[0]] = results[:3]
            del results[:3]
        if start == "first":
            cot_t = results.pop(0)
        if not has_open:
            gradient, line = results
            break
        open_done[index] = results[:3]
        d_mid, d_out, centre = results[3:]
        q, kn, kn_far, vt, vt_far, lse = heads
        d_far, dq = call(
            functools.partial(attend_back_kernel, False, 0),
            [q, kn_far, vt_far, lse, d_out, centre],
            [((2 * width, patches), BF16), (square, F32)],
            [(square, BF16), (natural, BF16)],
            flops=5 * score_flops // 2,
            name="attend_far",
        )
        d_got = swap(d_far)
        waits = []
        summing = []
        if has_before[1]:
            halves = [open_done[index][0], swap(open_done[index][1])]
            if index == 0:
                halves = [close_done[1][0], swap(close_done[1][1])] + halves
            half_rows = -(-sum(half.shape[0] for half in halves[::2]) // 32) * 16
            keep, sent = call(
                split_kernel,
                [(where, SMEM)] + halves,
                [((half_rows, LANES), F32), ((half_rows, LANES), BF16)],
                [((2 * half_rows, LANES), F32)],
                name="split",
            )
            waits = [keep]
            summing.append((index, keep, with_item(sent, 1)))
            if index == 0:
                waits.append(reduced[1][1])
        d_own, dq = call(
            functools.partial(attend_back_kernel, True, len(waits)),
            [q, kn, vt, lse, d_out, centre, dq] + [(value, HBM) for value in waits],
            [((2 * width, patches), F32), (square, BF16)],
            [(square, BF16), (natural, BF16)],
            flops=5 * score_flops // 2,
            name="attend_own",
        )
        for index, keep, got in summing:
            pair_sum = call(
                pair_sum_kernel, [keep, got, (dq, HBM)], [(keep.shape, BF16)], name="pair_sum"
            )[0]
            item_sum = (pair_sum.astype(F32) + with_item(pair_sum, 2).astype(F32)).astype(BF16)
            reduced[index] = [pair_sum, item_sum, with_item(item_sum, 1)]
        pending = [d_own, d_got, dq, d_mid, xb, mods[index], (w_qkv, HBM)]

    message = call(
        functools.partial(join_kernel, layers * 6 * width // LANES),
        [close_done[0][0], line, swap(close_done[0][1])],
        [((close_rows + 2 * SUM_ROWS, LANES), BF16)],
        name="join",
    )[0]
    message = call(
        functools.partial(pair_kernel, close_rows),
        [(where, SMEM), message, with_item(message, 1)],
        [((close_rows + 4 * SUM_ROWS, LANES), BF16)],
        name="pair",
    )[0]
    halves = [value for index in range(layers) for value in reduced[index][1:]]
    bias_rows = 6 * width // 8
    qkv_grad, out_grad, up_grad, down_grad, ada_grad, bias_grad, shift_grad = call(
        functools.partial(gather_kernel, item_count),
        [(where, SMEM), message, with_item(message, 2), *halves],
        [
            ((layers, slice_rows, 3 * width), F32),
            ((layers, slice_rows, width), F32),
            ((layers, slice_rows, ff), F32),
            ((layers, ff // 8, width), F32),
            ((layers, slice_rows, 6 * width), F32),
            ((layers, bias_rows), F32),
            ((layers, slice_rows), F32),
        ],
        [((2 * halves[2 * index].shape[0], LANES), BF16) for index in range(layers)]
        + [
            ((item_count, SUM_ROWS, LANES), F32),
            ((8, layers, bias_rows), F32),
            ((8, layers, slice_rows), F32),
        ],
        name="gather",
    )
    field_shape = (1, rows_dev, cols_dev, width)
    return (
        final.reshape(field_shape),
        gradient.reshape(field_shape),
        qkv_grad,
        out_grad,
        up_grad,
        down_grad,
        ada_grad,
        bias_grad,
        shift_grad,
    )


def solution(mesh):
    lat_count, lon_count, item_count = mesh.shape["lat"], mesh.shape["lon"], mesh.shape["item"]
    if lat_count == 2 and lon_count == 4:
        body = functools.partial(fast_shards, lat_count, lon_count, item_count)
    else:
        body = shards
    return jax.shard_map(
        body,
        mesh=mesh,
        in_specs=(
            P("item", "lat", "lon", None),
            P("item"),
            P("item"),
            P(),
            P(),
            P(),
            P(),
            P(),
            P(),
            P("item", "lat", "lon", None),
        ),
        out_specs=(
            P("item", "lat", "lon", None),
            P("item", "lat", "lon", None),
            P(None, ("lat", "lon"), None),
            P(None, ("lat", "lon"), None),
            P(None, ("lat", "lon"), None),
            P(None, ("lat", "lon"), None),
            P(None, ("lat", "lon"), None),
            P(None, ("lat", "lon")),
            P(None, ("lat", "lon")),
        ),
        check_vma=False,
    )
```

```python
import functools
import math

import jax
import jax.numpy as jnp
from jax import lax
from jax.experimental import pallas as pl
from jax.experimental.pallas import tpu as pltpu
from jax.sharding import PartitionSpec as P

D = 384
HEADS = 6
HEAD_DIM = 64
STEPS = 2


def shortened(shard):
    return jax.tree.map(lambda a: a.astype(jnp.bfloat16) if a.dtype == jnp.float32 else a, shard)


def embedding(lead):
    half_width = D // 2
    lead_hours = 6.0 * (lead.astype(jnp.float32) + 1.0)
    frequencies = jnp.exp(
        -math.log(10000.0) * jnp.arange(half_width, dtype=jnp.float32) / half_width
    )
    angles = lead_hours * frequencies
    return jnp.concatenate([jnp.sin(angles), jnp.cos(angles)])


def pre_norm(values, shift_part, scale_part):
    centred = values - jnp.mean(values, axis=-1, keepdims=True)
    variance = jnp.mean(centred * centred, axis=-1, keepdims=True)
    return centred * lax.rsqrt(variance + 1e-06) * (1.0 + scale_part) + shift_part


def gather_keys(keys_values):
    band_rows = lax.all_gather(keys_values, "lon", axis=0, tiled=True)
    return lax.all_gather(band_rows, "lat", axis=0, tiled=True)


def spread_keys(key_value_grads):
    band_grads = lax.psum_scatter(
        key_value_grads.astype(jnp.bfloat16), "lat", scatter_dimension=0, tiled=True
    )
    return lax.psum_scatter(band_grads, "lon", scatter_dimension=0, tiled=True).astype(jnp.float32)


def forward_layer(current, modulation, weight_qkv, weight_out, weight_up, weight_down):
    local_rows, width = current.shape
    shift_attn, scale_attn, gate_attn, shift_mlp, scale_mlp, gate_mlp = modulation
    normed = pre_norm(current, shift_attn, scale_attn).astype(jnp.bfloat16)
    projected = jnp.dot(normed, weight_qkv, preferred_element_type=jnp.float32).astype(jnp.bfloat16)
    queries = projected[:, :width].reshape(local_rows, HEADS, HEAD_DIM)
    own_keys = projected[:, width:]
    gathered = gather_keys(own_keys)
    total_rows = gathered.shape[0]
    key_heads = gathered[:, :width].reshape(total_rows, HEADS, HEAD_DIM)
    value_heads = gathered[:, width:].reshape(total_rows, HEADS, HEAD_DIM)
    scores = jnp.einsum(
        "thd,nhd->htn", queries, key_heads, preferred_element_type=jnp.float32
    ) * HEAD_DIM ** (-0.5)
    log_total = jax.nn.logsumexp(scores, axis=-1, keepdims=True)
    probabilities = jnp.exp(scores - log_total).astype(jnp.bfloat16)
    mixed = jnp.einsum(
        "htn,nhd->thd", probabilities, value_heads, preferred_element_type=jnp.float32
    )
    mixed = mixed.reshape(local_rows, width).astype(jnp.bfloat16)
    attended = jnp.dot(mixed, weight_out, preferred_element_type=jnp.float32)
    middle = current + gate_attn * attended
    hidden_in = pre_norm(middle, shift_mlp, scale_mlp).astype(jnp.bfloat16)
    pre_act = jnp.dot(hidden_in, weight_up, preferred_element_type=jnp.float32)
    hidden = jax.nn.gelu(pre_act).astype(jnp.bfloat16)
    branch = jnp.dot(hidden, weight_down, preferred_element_type=jnp.float32)
    output = middle + gate_mlp * branch
    kept = (
        current,
        normed,
        queries,
        gathered,
        own_keys,
        log_total,
        mixed,
        attended,
        middle,
        hidden_in,
        pre_act,
        hidden,
        branch,
    )
    return (output, kept)


def backward_layer(grad_out, kept, modulation, weight_qkv, weight_out, weight_up, weight_down):
    (
        current,
        normed,
        queries,
        gathered,
        own_keys,
        log_total,
        mixed,
        attended,
        middle,
        hidden_in,
        pre_act,
        hidden,
        branch,
    ) = kept
    local_rows, width = current.shape
    total_rows = gathered.shape[0]
    shift_attn, scale_attn, gate_attn, shift_mlp, scale_mlp, gate_mlp = modulation
    factor = HEAD_DIM ** (-0.5)
    branch_grad = (gate_mlp * grad_out).astype(jnp.bfloat16)
    gate_mlp_grad = jnp.sum(grad_out * branch, axis=0)
    hidden_grad = jnp.dot(branch_grad, weight_down.T, preferred_element_type=jnp.float32)
    down_grad = jnp.dot(hidden.T, branch_grad, preferred_element_type=jnp.float32)
    _, gelu_back = jax.vjp(jax.nn.gelu, pre_act)
    pre_grad = gelu_back(hidden_grad)[0].astype(jnp.bfloat16)
    hidden_in_grad = jnp.dot(pre_grad, weight_up.T, preferred_element_type=jnp.float32)
    up_grad = jnp.dot(hidden_in.T, pre_grad, preferred_element_type=jnp.float32)
    _, second_back = jax.vjp(pre_norm, middle, shift_mlp, scale_mlp)
    middle_part, shift_mlp_grad, scale_mlp_grad = second_back(hidden_in_grad)
    middle_grad = grad_out + middle_part
    attended_grad = (gate_attn * middle_grad).astype(jnp.bfloat16)
    gate_attn_grad = jnp.sum(middle_grad * attended, axis=0)
    mixed_grad = jnp.dot(attended_grad, weight_out.T, preferred_element_type=jnp.float32).astype(
        jnp.bfloat16
    )
    out_grad = jnp.dot(mixed.T, attended_grad, preferred_element_type=jnp.float32)
    mixed_heads = mixed_grad.reshape(local_rows, HEADS, HEAD_DIM)
    key_heads = gathered[:, :width].reshape(total_rows, HEADS, HEAD_DIM)
    value_heads = gathered[:, width:].reshape(total_rows, HEADS, HEAD_DIM)
    scores = (
        jnp.einsum("thd,nhd->htn", queries, key_heads, preferred_element_type=jnp.float32) * factor
    )
    probabilities = jnp.exp(scores - log_total)
    prob_grads = jnp.einsum(
        "thd,nhd->htn", mixed_heads, value_heads, preferred_element_type=jnp.float32
    )
    centre = jnp.sum(prob_grads * probabilities, axis=-1, keepdims=True)
    score_grads = (probabilities * (prob_grads - centre)).astype(jnp.bfloat16)
    query_grads = (
        jnp.einsum("htn,nhd->thd", score_grads, key_heads, preferred_element_type=jnp.float32)
        * factor
    )
    value_grads = jnp.einsum(
        "htn,thd->nhd",
        probabilities.astype(jnp.bfloat16),
        mixed_heads,
        preferred_element_type=jnp.float32,
    )
    key_grads = (
        jnp.einsum("htn,thd->nhd", score_grads, queries, preferred_element_type=jnp.float32)
        * factor
    )
    key_value_grads = jnp.concatenate(
        [key_grads.reshape(total_rows, width), value_grads.reshape(total_rows, width)], axis=1
    )
    local_grads = spread_keys(key_value_grads)
    projected_grad = jnp.concatenate(
        [query_grads.reshape(local_rows, width), local_grads], axis=1
    ).astype(jnp.bfloat16)
    normed_grad = jnp.dot(projected_grad, weight_qkv.T, preferred_element_type=jnp.float32)
    qkv_grad = jnp.dot(normed.T, projected_grad, preferred_element_type=jnp.float32)
    _, first_back = jax.vjp(pre_norm, current, shift_attn, scale_attn)
    current_part, shift_attn_grad, scale_attn_grad = first_back(normed_grad)
    input_grad = middle_grad + current_part
    modulation_grad = jnp.concatenate(
        [
            shift_attn_grad,
            scale_attn_grad,
            gate_attn_grad,
            shift_mlp_grad,
            scale_mlp_grad,
            gate_mlp_grad,
        ]
    )
    return (input_grad, (qkv_grad, out_grad, up_grad, down_grad, modulation_grad))


def shards(fields, lead_index, rollout, w_qkv, w_out, w_up, w_down, w_ada, b_ada, cotangent):
    _, rows_dev, cols_dev, width = fields.shape
    local_rows = rows_dev * cols_dev
    layer_count = w_qkv.shape[0]
    context = jax.nn.silu(embedding(lead_index[0])).astype(jnp.bfloat16)
    context_wide = context.astype(jnp.float32)
    modulations = [
        (
            jnp.dot(context[None, :], w_ada[index], preferred_element_type=jnp.float32)[0]
            + b_ada[index]
        ).reshape(6, width)
        for index in range(layer_count)
    ]
    weight_sets = [
        (w_qkv[index], w_out[index], w_up[index], w_down[index]) for index in range(layer_count)
    ]
    count = rollout[0]
    current = fields.reshape(local_rows, width).astype(jnp.float32)
    saved = []
    for rollout_step in range(STEPS):
        updated = current
        kept_layers = []
        for index in range(layer_count):
            updated, kept = forward_layer(updated, modulations[index], *weight_sets[index])
            kept_layers.append(kept)
        current = jnp.where(rollout_step < count, updated, current)
        saved.append(kept_layers)
    gradient = cotangent.reshape(local_rows, width).astype(jnp.float32)
    summed = None
    shares = None
    for rollout_step in reversed(range(STEPS)):
        active = (rollout_step < count).astype(jnp.float32)
        inner = gradient * active
        layer_terms = [None] * layer_count
        for index in reversed(range(layer_count)):
            inner, layer_terms[index] = backward_layer(
                inner, saved[rollout_step][index], modulations[index], *weight_sets[index]
            )
        gradient = inner + (1.0 - active) * gradient
        modulation_grads = jnp.stack([terms[4] for terms in layer_terms])
        step_terms = (
            jnp.stack([terms[0] for terms in layer_terms]),
            jnp.stack([terms[1] for terms in layer_terms]),
            jnp.stack([terms[2] for terms in layer_terms]),
            jnp.stack([terms[3] for terms in layer_terms]),
            context_wide[None, :, None] * modulation_grads[:, None, :],
            modulation_grads,
            modulation_grads[:, 3 * width : 4 * width],
        )
        summed = step_terms if summed is None else jax.tree.map(jnp.add, summed, step_terms)
    shares = lax.psum_scatter(summed, ("lat", "lon"), scatter_dimension=1, tiled=True)
    totals = jax.tree.map(
        lambda part: part.astype(jnp.float32), lax.psum(shortened(shares), "item")
    )
    return (
        current.reshape(1, rows_dev, cols_dev, width),
        gradient.reshape(1, rows_dev, cols_dev, width),
        totals[0],
        totals[1],
        totals[2],
        totals[3],
        totals[4],
        totals[5],
        totals[6],
    )


F32 = jnp.float32
BF16 = jnp.bfloat16
GELU_A = math.sqrt(2.0 / math.pi)
GELU_B = 0.044715
LANES = 128
BLOCK = 256
PAIR = 2 * HEAD_DIM
SUM_ROWS = 40


def nn(left, right, precision=None):
    return lax.dot_general(
        left, right, (((1,), (0,)), ((), ())), preferred_element_type=F32, precision=precision
    )


def nt(left, right, precision=None):
    return lax.dot_general(
        left, right, (((1,), (1,)), ((), ())), preferred_element_type=F32, precision=precision
    )


def identity(size):
    rows = lax.broadcasted_iota(jnp.int32, (size, size), 0)
    columns = lax.broadcasted_iota(jnp.int32, (size, size), 1)
    return jnp.where(rows == columns, 1.0, 0.0).astype(BF16)


def turned(values):
    return nt(identity(values.shape[1]), values).astype(BF16)


def wide(column_tile, lanes):
    return jnp.concatenate([column_tile] * (lanes // LANES), axis=1)


def folded(values):
    pieces = [values[:, at : at + LANES] for at in range(0, values.shape[1], LANES)]
    return sum(pieces[1:], pieces[0])


def standardise(values):
    rows = values.shape[0]
    centred = values - jnp.sum(values, axis=0, keepdims=True) * (1.0 / rows)
    variance = jnp.sum(centred * centred, axis=0, keepdims=True) * (1.0 / rows)
    scale = lax.rsqrt(variance + 1e-06)
    return centred * scale, scale


def pre_norm_back(standard, scale, grad, gain):
    rows = standard.shape[0]
    inner = grad * gain
    first = jnp.sum(inner, axis=0, keepdims=True) * (1.0 / rows)
    second = jnp.sum(inner * standard, axis=0, keepdims=True) * (1.0 / rows)
    return scale * (inner - first - standard * second)


def part(mod_ref, index, lanes):
    return wide(mod_ref[index * D : (index + 1) * D, :], lanes)


def turn_into(source, out, at=0):
    for column in range(0, out.shape[0], BLOCK):
        width = min(BLOCK, out.shape[0] - column)
        out[column : column + width, :] = turned(source[:, at + column : at + column + width])


def prepare_first_kernel(index, waits, context, w_ada, b_ada, w_qkv, *refs):
    mod, w_q_t, w_v_t, w_k = refs[waits:]
    values = nn(context[...], w_ada[index])[0:1] + b_ada[index : index + 1, :]
    for column in range(0, values.shape[1], LANES):
        tile = jnp.broadcast_to(values[:, column : column + LANES], (LANES, LANES))
        mod[column : column + LANES, :] = tile.T
    w_k[...] = w_qkv[index, :, D : 2 * D]
    turn_into(w_qkv.at[index], w_q_t)
    turn_into(w_qkv.at[index], w_v_t, 2 * D)


def prepare_rest_kernel(index, w_out, w_up, w_down, w_out_t, w_up_t, w_down_t):
    turn_into(w_out.at[index], w_out_t)
    turn_into(w_up.at[index], w_up_t)
    turn_into(w_down.at[index], w_down_t)


def project(x, mod_ref, w_q_t, w_v_t, w_k, outs):
    q_out, kn_out, vt_out = outs
    lanes = x.shape[1]
    standard, _ = standardise(x)
    normed = (standard * (1.0 + part(mod_ref, 1, lanes)) + part(mod_ref, 0, lanes)).astype(BF16)
    vt_out[...] = nn(w_v_t[...], normed).astype(BF16)
    q_out[...] = (nn(w_q_t[...], normed) * HEAD_DIM ** (-0.5)).astype(BF16)
    for at in range(0, lanes, BLOCK):
        kn_out[at : at + BLOCK, :] = nn(turned(normed[:, at : at + BLOCK]), w_k[...]).astype(BF16)


def first_kernel(own, flip_x, flip_y, flip_xy, mod, w_q_t, w_v_t, w_k, x_out, xb_out, *outs):
    for index, ref in enumerate((own, flip_x, flip_y, flip_xy)):
        rows = ref.shape[0]
        flat = turned(ref[...])
        xb_out[:, index * rows : (index + 1) * rows] = flat
        x_out[:, index * rows : (index + 1) * rows] = flat.astype(F32)
    project(x_out[...], mod, w_q_t, w_v_t, w_k, outs)


def head_rows(head):
    return slice(head * HEAD_DIM, (head + 1) * HEAD_DIM)


def pair_columns(head):
    return slice(head // 2 * PAIR, (head // 2 + 1) * PAIR)


def padded(rows, head):
    zeros = jnp.zeros_like(rows)
    return jnp.concatenate([rows, zeros] if head % 2 == 0 else [zeros, rows], axis=0)


def forward_kernel(last, *refs):
    if last:
        active, x, x_step, *refs = refs
    else:
        x, *refs = refs
    q, kn_own, kn_far, vt_own, vt_far, mod, w_out_t, w_up_t, w_down_t, *refs = refs
    if not last:
        mod_next, w_q_t, w_v_t, w_k, *refs = refs
    lse, mixed, attended, middle, hidden, slope, branch, *refs = refs
    if last:
        (final,) = refs
    else:
        x_next, xb_next, *next_outs = refs
    patches = x.shape[1]

    def score(head):
        columns = pair_columns(head)
        query = padded(q[head_rows(head), :], head)
        return nn(kn_own[:, columns], query), nn(kn_far[:, columns], query)

    ones = jnp.ones((16, patches), BF16)
    following = score(0)
    for head in range(HEADS):
        scores_own, scores_far = following
        if head + 1 < HEADS:
            following = score(head + 1)
        rows = head_rows(head)
        top = jnp.maximum(
            jnp.max(scores_own, axis=0, keepdims=True), jnp.max(scores_far, axis=0, keepdims=True)
        )
        total = None
        for scores, values in ((scores_own, vt_own), (scores_far, vt_far)):
            for key in range(0, patches, BLOCK):
                probs = jnp.exp(scores[key : key + BLOCK] - top).astype(BF16)
                value = jnp.concatenate([values[rows, key : key + BLOCK], ones[:, :BLOCK]], axis=0)
                term = nn(value, probs)
                total = term if total is None else total + term
        weight = total[HEAD_DIM : HEAD_DIM + 1]
        mixed[rows, :] = (total[:HEAD_DIM] * (1.0 / weight)).astype(BF16)
        lse[head : head + 1, :] = top + jnp.log(weight)

    att = nn(w_out_t[...], mixed[...])
    attended[...] = att.astype(BF16)
    mid = x[...] + part(mod, 2, patches) * att
    middle[...] = mid.astype(BF16)
    standard, _ = standardise(mid)
    hidden_in = (standard * (1.0 + part(mod, 4, patches)) + part(mod, 3, patches)).astype(BF16)
    chunks = w_up_t.shape[0] // D

    def up(chunk):
        return nn(w_up_t[chunk * D : (chunk + 1) * D, :], hidden_in)

    following = up(0)
    down = None
    for chunk in range(chunks):
        act = following
        if chunk + 1 < chunks:
            following = up(chunk + 1)
        rows = slice(chunk * D, (chunk + 1) * D)
        squared = act * act
        bent = jnp.tanh(act * (GELU_A + (GELU_A * GELU_B) * squared))
        half = 0.5 + 0.5 * bent
        kept = (act * half).astype(BF16)
        hidden[rows, :] = kept
        curve = (1.0 - bent * bent) * (0.5 * GELU_A + (1.5 * GELU_A * GELU_B) * squared)
        slope[rows, :] = (half + act * curve).astype(BF16)
        term = nn(w_down_t[:, chunk * D : (chunk + 1) * D], kept)
        down = term if down is None else down + term
    branch[...] = down.astype(BF16)
    out = mid + part(mod, 5, patches) * down
    if last:
        own = final.shape[0]
        final[...] = jnp.where(active[0] > 0.0, out[:, :own], x_step[:, :own]).T
    else:
        x_next[...] = out
        xb_next[...] = out.astype(BF16)
        project(out, mod_next, w_q_t, w_v_t, w_k, next_outs)


def put_grads(left_ref, right, where, count, at, mine, other, before):
    rows = [left_ref[pl.ds(pl.multiple_of(where[place] * count, 16), count), :] for place in range(2)]
    product = nt(jnp.concatenate(rows, axis=0), right)
    for column in range(0, product.shape[1], LANES):
        low = product[:count, column : column + LANES]
        high = product[count:, column : column + LANES]
        if before is not None:
            low = low + before[0][at : at + count, :]
            high = high + before[1][at : at + count, :]
        mine[at : at + count, :] = low.astype(mine.dtype)
        other[at : at + count, :] = high.astype(other.dtype)
        at += count


def dense_back_kernel(has_close, has_open, has_before, start, layers, layer_sums, waits, *refs):
    refs = list(refs)

    def take(count):
        taken = refs[:count]
        del refs[:count]
        return taken

    take(waits)
    where, active = take(2)
    close_before = open_before = None
    if has_close:
        d_own, d_got, dq, d_mid_in, x_in, mod_in, w_qkv = take(7)
        w_qkv = w_qkv.at[layers[0]]
        if has_before[0]:
            close_before = take(3)
    if start == "first":
        cots = take(4)
    elif start == "cross":
        cots = take(1)
    if has_open:
        mixed, attended, middle, hidden, slope, branch, mod, w_out, w_up, w_down = take(10)
        w_out, w_up, w_down = (ref.at[layers[1]] for ref in (w_out, w_up, w_down))
        if has_before[1]:
            open_before = take(3)
    else:
        (context,) = take(1)
        all_sums = take(layer_sums)
    if has_close:
        close_mine, close_other, close_mods = take(3)
    if start == "first":
        (cot_out,) = take(1)
    if has_open:
        open_mine, open_other, open_mods, d_mid_out, do_out, cen_out = take(6)
    else:
        g_out, sums_out = take(2)
        sums_at = close_before[1].shape[0]
    if has_close:
        grads_scr, normed_scr = take(2)
    if has_open:
        bg_scr, pg_scr, hin_scr, ag_scr = take(4)

    patches = middle.shape[1] if has_open else x_in.shape[1]

    def add_sums(out, before, at, values):
        total = folded(values)
        out[at * D : (at + 1) * D, :] = total + before[2][at * D : (at + 1) * D, :] if before else total

    if start == "first":
        pieces = [turned(ref[...]) for ref in cots]
        for index, piece in enumerate(pieces):
            rows = piece.shape[1]
            cot_out[:, index * rows : (index + 1) * rows] = piece
        g = cot_out[...].astype(F32) * active[0]
    if has_open:
        standard_mid, scale_mid = standardise(middle[...].astype(F32))
        gain_mid = 1.0 + part(mod, 4, patches)
        hin_scr[...] = (standard_mid * gain_mid + part(mod, 3, patches)).astype(BF16)
    if has_close:
        back = None
        standard, scale = standardise(x_in[...].astype(F32))
        gain = 1.0 + part(mod_in, 1, patches)
        normed_scr[...] = (standard * gain + part(mod_in, 0, patches)).astype(BF16)
        for third in range(3):
            if third == 0:
                piece = dq[...]
            else:
                rows = slice((third - 1) * D, third * D)
                piece = (d_own[rows, :] + d_got[rows, :].astype(F32)).astype(BF16)
            grads_scr[third * D : (third + 1) * D, :] = piece
            term = nn(w_qkv[:, third * D : (third + 1) * D], piece)
            back = term if back is None else back + term
        put_grads(normed_scr, grads_scr[...], where, D // 8, 0, close_mine, close_other, close_before)
        add_sums(close_mods, close_before, 0, back)
        add_sums(close_mods, close_before, 1, back * standard)
        g = d_mid_in[...] + pre_norm_back(standard, scale, back, gain)
        if start == "cross":
            g = g + (1.0 - active[0]) * cots[0][...].astype(F32)
    if has_open:
        branch_grad = (part(mod, 5, patches) * g).astype(BF16)
        bg_scr[...] = branch_grad
        add_sums(open_mods, open_before, 3, g * branch[...].astype(F32))
        chunks = w_down.shape[0] // D

        def down(chunk):
            return nn(w_down[chunk * D : (chunk + 1) * D, :], branch_grad)

        following = down(0)
        back = None
        for chunk in range(chunks):
            hidden_grad = following
            if chunk + 1 < chunks:
                following = down(chunk + 1)
            rows = slice(chunk * D, (chunk + 1) * D)
            pre_grad = (slope[rows, :].astype(F32) * hidden_grad).astype(BF16)
            pg_scr[rows, :] = pre_grad
            term = nn(w_up[:, chunk * D : (chunk + 1) * D], pre_grad)
            back = term if back is None else back + term
        count = w_down.shape[0] // 8
        put_grads(hidden, branch_grad, where, count, 0, open_mine, open_other, open_before)
        at = count * (D // LANES)
        add_sums(open_mods, open_before, 1, back)
        add_sums(open_mods, open_before, 2, back * standard_mid)
        d_mid = g + pre_norm_back(standard_mid, scale_mid, back, gain_mid)
        put_grads(hin_scr, pg_scr[...], where, D // 8, at, open_mine, open_other, open_before)
        at += (w_up.shape[1] // LANES) * (D // 8)
        d_mid_out[...] = d_mid
        att_grad = (part(mod, 2, patches) * d_mid).astype(BF16)
        ag_scr[...] = att_grad
        mixed_grad = nn(w_out[...], att_grad).astype(BF16)
        do_out[...] = mixed_grad
        add_sums(open_mods, open_before, 0, d_mid * attended[...].astype(F32))
        put_grads(mixed, att_grad, where, D // 8, at, open_mine, open_other, open_before)
        product = mixed_grad.astype(F32) * mixed[...].astype(F32)
        for head in range(HEADS):
            cen_out[head : head + 1, :] = jnp.sum(product[head_rows(head)], axis=0, keepdims=True)
    else:
        g_out[...] = g[:, : g_out.shape[0]].T
        ones = jnp.ones((8, LANES), F32)
        sums_out[...] = jnp.zeros_like(sums_out)
        row = 0
        for ref in [close_mods] + all_sums:
            line = nt(ones, ref[...], precision=lax.Precision.HIGHEST)[0:1]
            for column in range(0, line.shape[1], LANES):
                sums_out[row : row + 1, :] = line[:, column : column + LANES]
                row += 1
        for column in range(0, D, LANES):
            sums_out[row : row + 1, :] = context[0:1, column : column + LANES].astype(F32)
            row += 1
        put_pair(close_other, sums_at, sums_out[...])


def attend_back_kernel(has_before, waits, q, kn, vt, lse, d_out, centre, *refs):
    if has_before:
        before, *refs = refs
    d_kv, dq_out, kt_scr, vn_scr = refs[waits:]
    for column in range(0, D, LANES):
        kt_scr[column : column + LANES, :] = turned(kn[:, column : column + LANES])
    for column in range(0, vt.shape[1], BLOCK):
        vn_scr[column : column + BLOCK, :] = turned(vt[:, column : column + BLOCK])

    def score(head):
        columns = pair_columns(head)
        rows = head_rows(head)
        return nn(kn[:, columns], padded(q[rows, :], head)), nn(vn_scr[:, columns], padded(d_out[rows, :], head))

    following = score(0)
    for head in range(HEADS):
        scores, prob_grads = following
        if head + 1 < HEADS:
            following = score(head + 1)
        rows = head_rows(head)
        value_rows = slice(D + rows.start, D + rows.stop)
        probs = jnp.exp(scores - lse[head : head + 1, :])
        score_grads = (probs * (prob_grads - centre[head : head + 1, :])).astype(BF16)
        d_kv[value_rows, :] = nt(d_out[rows, :], probs.astype(BF16)).astype(d_kv.dtype)
        d_kv[rows, :] = nt(q[rows, :], score_grads).astype(d_kv.dtype)
        term = nn(kt_scr[rows, :], score_grads)
        if has_before:
            term = (before[rows, :] + term) * HEAD_DIM ** (-0.5)
        dq_out[rows, :] = term.astype(dq_out.dtype)


def split_kernel(where, *refs):
    *halves, keep, sent, total_scr = refs
    rows_half = keep.shape[0]
    at = 0
    for mine, other in zip(halves[::2], halves[1::2]):
        rows = mine.shape[0]
        total_scr[at : at + rows, :] = mine[...] + other[...].astype(F32)
        at += rows
    if at < total_scr.shape[0]:
        total_scr[at:, :] = jnp.zeros((total_scr.shape[0] - at, LANES), F32)
    odd = where[3]
    keep[...] = total_scr[pl.ds(pl.multiple_of(odd * rows_half, 16), rows_half), :]
    sent[...] = total_scr[pl.ds(pl.multiple_of((1 - odd) * rows_half, 16), rows_half), :].astype(BF16)


def pair_sum_kernel(keep, got, late, out):
    out[...] = (keep[...] + got[...].astype(F32)).astype(BF16)


def put_pair(out, at, values):
    rows = values.shape[0]
    high = values.astype(BF16)
    out[at : at + rows, :] = high
    out[at + rows : at + 2 * rows, :] = (values - high.astype(F32)).astype(BF16)


def get_pair(ref, at, rows):
    return ref[at : at + rows, :].astype(F32) + ref[at + rows : at + 2 * rows, :].astype(F32)


def join_kernel(sum_count, mine, sums, got, out):
    rows = mine.shape[0]
    out[:rows, :] = (mine[...] + got[:rows, :].astype(F32)).astype(BF16)
    other = get_pair(got, rows, SUM_ROWS)
    summed = lax.broadcasted_iota(jnp.int32, (SUM_ROWS, LANES), 0) < sum_count
    put_pair(out, rows, sums[...] + jnp.where(summed, other, 0.0))


def pair_kernel(rows, where, own, got, out):
    out[:rows, :] = (own[:rows, :].astype(F32) + got[:rows, :].astype(F32)).astype(BF16)
    odd = where[3]
    size = 2 * SUM_ROWS
    out[pl.ds(pl.multiple_of(rows + odd * size, 16), size), :] = own[rows:, :]
    out[pl.ds(pl.multiple_of(rows + (1 - odd) * size, 16), size), :] = got[rows:, :]


def gather_kernel(item_count, where, *refs):
    layers = 2
    own, got, *halves = refs[:6]
    qkv_out, out_out, up_out, down_out, ada_out, bias_out, shift_out, *scratch = refs[6:]
    total_scr, sum_scr = scratch[:2], scratch[2]
    device, odd, high = where[0], where[3], where[4]
    for index in range(layers):
        kept, other = halves[2 * index], halves[2 * index + 1]
        rows = kept.shape[0]
        total_scr[index][pl.ds(pl.multiple_of(odd * rows, 16), rows), :] = kept[...]
        total_scr[index][pl.ds(pl.multiple_of((1 - odd) * rows, 16), rows), :] = other[...]
    slice_rows = qkv_out.shape[1]
    down_rows = down_out.shape[1]
    close_rows = slice_rows * (3 * D // LANES)
    for other in range(2):
        at = close_rows + other * 2 * SUM_ROWS
        sum_scr[2 * high + other] = get_pair(own, at, SUM_ROWS)
        sum_scr[2 * (1 - high) + other] = get_pair(got, at, SUM_ROWS)
    for index in range(layers):
        ref = total_scr[index]
        at = close_rows if index == 0 else 0
        for column in range(0, D, LANES):
            down_out[index, :, column : column + LANES] = ref[at : at + down_rows, :].astype(F32)
            at += down_rows
        for column in range(0, up_out.shape[2], LANES):
            up_out[index, :, column : column + LANES] = ref[at : at + slice_rows, :].astype(F32)
            at += slice_rows
        for column in range(0, D, LANES):
            out_out[index, :, column : column + LANES] = ref[at : at + slice_rows, :].astype(F32)
            at += slice_rows
        for tile in range(3 * D // LANES):
            rows = slice(tile * slice_rows, (tile + 1) * slice_rows)
            if index == 1:
                total = total_scr[0][rows, :].astype(F32)
            else:
                total = own[rows, :].astype(F32) + got[rows, :].astype(F32)
            qkv_out[index, :, tile * LANES : (tile + 1) * LANES] = total
    tiles = 6 * D // LANES
    contexts = []
    for other in range(item_count):
        line = jnp.concatenate([sum_scr[other, layers * tiles + c : layers * tiles + c + 1, :] for c in range(3)], axis=1)
        contexts.append(line)
    square = jnp.concatenate(contexts + [jnp.zeros((8 - item_count, D), F32)], axis=0)
    spot = lax.broadcasted_iota(jnp.int32, (slice_rows, D), 1)
    want = lax.broadcasted_iota(jnp.int32, (slice_rows, D), 0) + device * slice_rows
    pick = jnp.where(spot == want, 1.0, 0.0).astype(BF16)
    columns = nt(pick, square.astype(BF16))
    bias_scr, shift_scr = scratch[3:]
    bias_rows = bias_out.shape[1]
    for index in range(layers):
        flats = []
        for tile in range(tiles):
            row = index * tiles + tile
            total = None
            flat = None
            for other in range(item_count):
                line = sum_scr[other, row : row + 1, :]
                term = columns[:, other : other + 1] * line
                total = term if total is None else total + term
                flat = line if flat is None else flat + line
            ada_out[index, :, tile * LANES : (tile + 1) * LANES] = total
            flats.append(flat)
        flat = jnp.concatenate(flats, axis=1)
        for place in range(flat.shape[1] // bias_rows):
            bias_scr[place, index : index + 1, :] = flat[:, place * bias_rows : (place + 1) * bias_rows]
            at = 3 * D + place * slice_rows
            shift_scr[place, index : index + 1, :] = flat[:, at : at + slice_rows]
    bias_out[...] = bias_scr[device]
    shift_out[...] = shift_scr[device]


VMEM = pl.BlockSpec(memory_space=pltpu.VMEM)
SMEM = pl.BlockSpec(memory_space=pltpu.SMEM)
HBM = pl.BlockSpec(memory_space=pl.ANY)


def layer_block(array, index):
    return pl.BlockSpec((None,) + array.shape[1:], lambda step: (index,) + (0,) * (array.ndim - 1))


def call(body, args, outs, scratch=(), flops=0, name=None, grid=()):
    arrays = [arg[0] if isinstance(arg, tuple) else arg for arg in args]
    specs = [arg[1] if isinstance(arg, tuple) else VMEM for arg in args]
    return pl.pallas_call(
        body,
        out_shape=[jax.ShapeDtypeStruct(shape, kind) for shape, kind in outs],
        grid=grid,
        in_specs=specs,
        out_specs=[VMEM] * len(outs),
        scratch_shapes=[one if not isinstance(one, tuple) else pltpu.VMEM(*one) for one in scratch],
        compiler_params=pltpu.CompilerParams(vmem_limit_bytes=VMEM_LIMIT),
        cost_estimate=pl.CostEstimate(flops=flops, bytes_accessed=0, transcendentals=0),
        name=name,
    )(*arrays)


VMEM_LIMIT = 16 * 1024 * 1024


def fast_shards(
    lat_count, lon_count, item_count,
    fields, lead_index, rollout, w_qkv, w_out, w_up, w_down, w_ada, b_ada, cotangent,
):
    _, rows_dev, cols_dev, width = fields.shape
    local = rows_dev * cols_dev
    layers = w_qkv.shape[0]
    ff = w_up.shape[2]
    patches = 4 * local
    device = lax.axis_index("lat") * lon_count + lax.axis_index("lon")
    item = lax.axis_index("item")
    where = jnp.stack([device, device ^ 1, item, item & 1, item >> 1]).astype(jnp.int32)
    active = (1 < rollout[0]).astype(F32)[None]

    def plane_flip(value, flip_lat, flip_y):
        pairs = [
            (a * lon_count + b, (a ^ flip_lat) * lon_count + (b ^ (2 * flip_y)))
            for a in range(lat_count)
            for b in range(lon_count)
        ]
        return lax.ppermute(value, ("lat", "lon"), pairs)

    def swap(value):
        return lax.ppermute(value, "lon", [(index, index ^ 1) for index in range(lon_count)])

    def with_item(value, flip):
        return lax.ppermute(value, "item", [(index, index ^ flip) for index in range(item_count)])

    own = fields.reshape(local, width)
    field_parts = [own, plane_flip(own, 1, 0), plane_flip(own, 0, 1), plane_flip(own, 1, 1)]
    cot_own = cotangent.reshape(local, width)
    cot_parts = [cot_own, plane_flip(cot_own, 1, 0), plane_flip(cot_own, 0, 1), plane_flip(cot_own, 1, 1)]

    context = jax.nn.silu(embedding(lead_index[0])).astype(BF16)
    context = jnp.broadcast_to(context[None, :], (16, width))
    square = (width, patches)
    natural = (patches, width)
    first_parts = []
    rest_parts = []
    for index in range(layers):
        waits = [(where, SMEM), (active, SMEM)] if index == 0 else []
        first_parts.append(
            call(
                functools.partial(prepare_first_kernel, index, len(waits)),
                [context, w_ada, b_ada, w_qkv] + waits,
                [((6 * width, LANES), F32)] + [((width, width), BF16)] * 3,
                name="prepare_first",
            )
        )
        rest_parts.append(
            call(
                functools.partial(prepare_rest_kernel, index),
                [w_out, w_up, w_down],
                [((width, width), BF16), ((ff, width), BF16), ((width, ff), BF16)],
                name="prepare_rest",
            )
        )
    mods = [one[0] for one in first_parts]

    project_outs = [(square, F32), (square, BF16), (square, BF16), (natural, BF16), (square, BF16)]
    dense_flops = 2 * patches * (width * 3 * width + width * width + 2 * width * ff)
    score_flops = 2 * patches * 2 * patches * width * 4
    x, xb, *projected = call(
        first_kernel,
        [*field_parts, *first_parts[0]],
        project_outs,
        flops=2 * patches * width * 4 * width,
        name="first",
    )
    saved = []
    for step in range(STEPS):
        for index in range(layers):
            q, kn, vt = projected
            kn_far, vt_far = swap(kn), swap(vt)
            last = step == STEPS - 1 and index == layers - 1
            if index == 0 and step > 0:
                x_step = x
            following = list(first_parts[(index + 1) % layers])
            lse, mixed, attended, middle, hidden, slope, branch, *results = call(
                functools.partial(forward_kernel, last),
                ([(active, SMEM), x, x_step] if last else [x])
                + [q, kn, kn_far, vt, vt_far, mods[index], *rest_parts[index]]
                + ([] if last else following),
                [
                    ((HEADS, patches), F32),
                    (square, BF16),
                    (square, BF16),
                    (square, BF16),
                    ((ff, patches), BF16),
                    ((ff, patches), BF16),
                    (square, BF16),
                ]
                + ([((local, width), F32)] if last else project_outs),
                flops=dense_flops + 2 * score_flops,
                name="forward",
            )
            saved.append((xb, [mixed, attended, middle, hidden, slope, branch], (q, kn, kn_far, vt, vt_far, lse)))
            if last:
                final = results[0]
            else:
                x, xb, *projected = results

    slice_rows = width // 8
    open_rows = 2 * (ff // 8) * (width // LANES) + slice_rows * (width // LANES)
    close_rows = slice_rows * (3 * width // LANES)
    order = [(step, index) for step in reversed(range(STEPS)) for index in reversed(range(layers))]
    open_done = [None] * layers
    close_done = [None] * layers
    reduced = [None] * layers
    pending = None
    for place in range(len(order) + 1):
        has_close = pending is not None
        has_open = place < len(order)
        use = [order[place - 1][1], order[place][1] if has_open else 0]
        waits = [reduced[use[0]][0]] if has_close and reduced[use[0]] else []
        if not has_open:
            waits.append(reduced[1][2])
        args = [(value, HBM) for value in waits] + [(where, SMEM), (active, SMEM)]
        outs = []
        scratch = []
        has_before = [False, False]
        start = ""
        if has_close:
            args += pending
            if close_done[use[0]] is not None:
                has_before[0] = True
                args += close_done[use[0]]
            outs += [((close_rows, LANES), F32)]
            sent_rows = close_rows + (0 if has_open else 2 * SUM_ROWS)
            outs += [((sent_rows, LANES), BF16 if has_before[0] else F32), ((2 * width, LANES), F32)]
            scratch += [((3 * width, patches), BF16), (square, BF16)]
        if place == 0:
            start = "first"
            args += cot_parts
            outs += [(square, BF16)]
        elif has_open and order[place][0] != order[place - 1][0]:
            start = "cross"
            args += [cot_t]
        if has_open:
            step, index = order[place]
            xb, kept, heads = saved[step * layers + index]
            args += kept + [mods[index], w_out, w_up, w_down]
            if open_done[index] is not None:
                has_before[1] = True
                args += open_done[index]
            outs += [
                ((open_rows, LANES), F32),
                ((open_rows, LANES), BF16 if has_before[1] else F32),
                ((4 * width, LANES), F32),
                (square, F32),
                (square, BF16),
                ((HEADS, patches), F32),
            ]
            scratch += [(square, BF16), ((ff, patches), BF16), (square, BF16), (square, BF16)]
            sums = []
        else:
            sums = [open_done[0][2], close_done[1][2], open_done[1][2]]
            args += [context] + sums
            outs += [((local, width), F32), ((SUM_ROWS, LANES), F32)]
        results = list(
            call(
                functools.partial(dense_back_kernel, has_close, has_open, has_before, start, use, len(sums), len(waits)),
                args,
                outs,
                scratch,
                flops=2 * dense_flops if has_open else 0,
                name="dense_back" if has_open else "close_back",
            )
        )
        if has_close:
            close_done[use[0]] = results[:3]
            del results[:3]
        if start == "first":
            cot_t = results.pop(0)
        if not has_open:
            gradient, line = results
            break
        open_done[index] = results[:3]
        d_mid, d_out, centre = results[3:]
        q, kn, kn_far, vt, vt_far, lse = heads
        d_far, dq = call(
            functools.partial(attend_back_kernel, False, 0),
            [q, kn_far, vt_far, lse, d_out, centre],
            [((2 * width, patches), BF16), (square, F32)],
            [(square, BF16), (natural, BF16)],
            flops=5 * score_flops // 2,
            name="attend_far",
        )
        d_got = swap(d_far)
        waits = []
        summing = []
        if has_before[1]:
            halves = [open_done[index][0], swap(open_done[index][1])]
            if index == 0:
                halves = [close_done[1][0], swap(close_done[1][1])] + halves
            half_rows = -(-sum(half.shape[0] for half in halves[::2]) // 32) * 16
            keep, sent = call(
                split_kernel,
                [(where, SMEM)] + halves,
                [((half_rows, LANES), F32), ((half_rows, LANES), BF16)],
                [((2 * half_rows, LANES), F32)],
                name="split",
            )
            waits = [keep]
            summing.append((index, keep, with_item(sent, 1)))
            if index == 0:
                waits.append(reduced[1][1])
        d_own, dq = call(
            functools.partial(attend_back_kernel, True, len(waits)),
            [q, kn, vt, lse, d_out, centre, dq] + [(value, HBM) for value in waits],
            [((2 * width, patches), F32), (square, BF16)],
            [(square, BF16), (natural, BF16)],
            flops=5 * score_flops // 2,
            name="attend_own",
        )
        for index, keep, got in summing:
            pair_sum = call(
                pair_sum_kernel, [keep, got, (dq, HBM)], [(keep.shape, BF16)], name="pair_sum"
            )[0]
            item_sum = (pair_sum.astype(F32) + with_item(pair_sum, 2).astype(F32)).astype(BF16)
            reduced[index] = [pair_sum, item_sum, with_item(item_sum, 1)]
        pending = [d_own, d_got, dq, d_mid, xb, mods[index], w_qkv]

    message = call(
        functools.partial(join_kernel, layers * 6 * width // LANES),
        [close_done[0][0], line, swap(close_done[0][1])],
        [((close_rows + 2 * SUM_ROWS, LANES), BF16)],
        name="join",
    )[0]
    message = call(
        functools.partial(pair_kernel, close_rows),
        [(where, SMEM), message, with_item(message, 1)],
        [((close_rows + 4 * SUM_ROWS, LANES), BF16)],
        name="pair",
    )[0]
    halves = [value for index in range(layers) for value in reduced[index][1:]]
    bias_rows = 6 * width // 8
    qkv_grad, out_grad, up_grad, down_grad, ada_grad, bias_grad, shift_grad = call(
        functools.partial(gather_kernel, item_count),
        [(where, SMEM), message, with_item(message, 2), *halves],
        [
            ((layers, slice_rows, 3 * width), F32),
            ((layers, slice_rows, width), F32),
            ((layers, slice_rows, ff), F32),
            ((layers, ff // 8, width), F32),
            ((layers, slice_rows, 6 * width), F32),
            ((layers, bias_rows), F32),
            ((layers, slice_rows), F32),
        ],
        [((2 * halves[2 * index].shape[0], LANES), BF16) for index in range(layers)]
        + [
            ((item_count, SUM_ROWS, LANES), F32),
            ((8, layers, bias_rows), F32),
            ((8, layers, slice_rows), F32),
        ],
        name="gather",
    )
    field_shape = (1, rows_dev, cols_dev, width)
    return (
        final.reshape(field_shape),
        gradient.reshape(field_shape),
        qkv_grad,
        out_grad,
        up_grad,
        down_grad,
        ada_grad,
        bias_grad,
        shift_grad,
    )


def solution(mesh):
    lat_count, lon_count, item_count = mesh.shape["lat"], mesh.shape["lon"], mesh.shape["item"]
    if lat_count == 2 and lon_count == 4:
        body = functools.partial(fast_shards, lat_count, lon_count, item_count)
    else:
        body = shards
    return jax.shard_map(
        body,
        mesh=mesh,
        in_specs=(
            P("item", "lat", "lon", None),
            P("item"),
            P("item"),
            P(),
            P(),
            P(),
            P(),
            P(),
            P(),
            P("item", "lat", "lon", None),
        ),
        out_specs=(
            P("item", "lat", "lon", None),
            P("item", "lat", "lon", None),
            P(None, ("lat", "lon"), None),
            P(None, ("lat", "lon"), None),
            P(None, ("lat", "lon"), None),
            P(None, ("lat", "lon"), None),
            P(None, ("lat", "lon"), None),
            P(None, ("lat", "lon")),
            P(None, ("lat", "lon")),
        ),
        check_vma=False,
    )
```

```python
import functools
import math

import jax
import jax.numpy as jnp
from jax import lax
from jax.experimental import pallas as pl
from jax.experimental.pallas import tpu as pltpu
from jax.sharding import PartitionSpec as P

D = 384
HEADS = 6
HEAD_DIM = 64
STEPS = 2


def shortened(shard):
    return jax.tree.map(lambda a: a.astype(jnp.bfloat16) if a.dtype == jnp.float32 else a, shard)


def embedding(lead):
    half_width = D // 2
    lead_hours = 6.0 * (lead.astype(jnp.float32) + 1.0)
    frequencies = jnp.exp(
        -math.log(10000.0) * jnp.arange(half_width, dtype=jnp.float32) / half_width
    )
    angles = lead_hours * frequencies
    return jnp.concatenate([jnp.sin(angles), jnp.cos(angles)])


def pre_norm(values, shift_part, scale_part):
    centred = values - jnp.mean(values, axis=-1, keepdims=True)
    variance = jnp.mean(centred * centred, axis=-1, keepdims=True)
    return centred * lax.rsqrt(variance + 1e-06) * (1.0 + scale_part) + shift_part


def gather_keys(keys_values):
    band_rows = lax.all_gather(keys_values, "lon", axis=0, tiled=True)
    return lax.all_gather(band_rows, "lat", axis=0, tiled=True)


def spread_keys(key_value_grads):
    band_grads = lax.psum_scatter(
        key_value_grads.astype(jnp.bfloat16), "lat", scatter_dimension=0, tiled=True
    )
    return lax.psum_scatter(band_grads, "lon", scatter_dimension=0, tiled=True).astype(jnp.float32)


def forward_layer(current, modulation, weight_qkv, weight_out, weight_up, weight_down):
    local_rows, width = current.shape
    shift_attn, scale_attn, gate_attn, shift_mlp, scale_mlp, gate_mlp = modulation
    normed = pre_norm(current, shift_attn, scale_attn).astype(jnp.bfloat16)
    projected = jnp.dot(normed, weight_qkv, preferred_element_type=jnp.float32).astype(jnp.bfloat16)
    queries = projected[:, :width].reshape(local_rows, HEADS, HEAD_DIM)
    own_keys = projected[:, width:]
    gathered = gather_keys(own_keys)
    total_rows = gathered.shape[0]
    key_heads = gathered[:, :width].reshape(total_rows, HEADS, HEAD_DIM)
    value_heads = gathered[:, width:].reshape(total_rows, HEADS, HEAD_DIM)
    scores = jnp.einsum(
        "thd,nhd->htn", queries, key_heads, preferred_element_type=jnp.float32
    ) * HEAD_DIM ** (-0.5)
    log_total = jax.nn.logsumexp(scores, axis=-1, keepdims=True)
    probabilities = jnp.exp(scores - log_total).astype(jnp.bfloat16)
    mixed = jnp.einsum(
        "htn,nhd->thd", probabilities, value_heads, preferred_element_type=jnp.float32
    )
    mixed = mixed.reshape(local_rows, width).astype(jnp.bfloat16)
    attended = jnp.dot(mixed, weight_out, preferred_element_type=jnp.float32)
    middle = current + gate_attn * attended
    hidden_in = pre_norm(middle, shift_mlp, scale_mlp).astype(jnp.bfloat16)
    pre_act = jnp.dot(hidden_in, weight_up, preferred_element_type=jnp.float32)
    hidden = jax.nn.gelu(pre_act).astype(jnp.bfloat16)
    branch = jnp.dot(hidden, weight_down, preferred_element_type=jnp.float32)
    output = middle + gate_mlp * branch
    kept = (
        current,
        normed,
        queries,
        gathered,
        own_keys,
        log_total,
        mixed,
        attended,
        middle,
        hidden_in,
        pre_act,
        hidden,
        branch,
    )
    return (output, kept)


def backward_layer(grad_out, kept, modulation, weight_qkv, weight_out, weight_up, weight_down):
    (
        current,
        normed,
        queries,
        gathered,
        own_keys,
        log_total,
        mixed,
        attended,
        middle,
        hidden_in,
        pre_act,
        hidden,
        branch,
    ) = kept
    local_rows, width = current.shape
    total_rows = gathered.shape[0]
    shift_attn, scale_attn, gate_attn, shift_mlp, scale_mlp, gate_mlp = modulation
    factor = HEAD_DIM ** (-0.5)
    branch_grad = (gate_mlp * grad_out).astype(jnp.bfloat16)
    gate_mlp_grad = jnp.sum(grad_out * branch, axis=0)
    hidden_grad = jnp.dot(branch_grad, weight_down.T, preferred_element_type=jnp.float32)
    down_grad = jnp.dot(hidden.T, branch_grad, preferred_element_type=jnp.float32)
    _, gelu_back = jax.vjp(jax.nn.gelu, pre_act)
    pre_grad = gelu_back(hidden_grad)[0].astype(jnp.bfloat16)
    hidden_in_grad = jnp.dot(pre_grad, weight_up.T, preferred_element_type=jnp.float32)
    up_grad = jnp.dot(hidden_in.T, pre_grad, preferred_element_type=jnp.float32)
    _, second_back = jax.vjp(pre_norm, middle, shift_mlp, scale_mlp)
    middle_part, shift_mlp_grad, scale_mlp_grad = second_back(hidden_in_grad)
    middle_grad = grad_out + middle_part
    attended_grad = (gate_attn * middle_grad).astype(jnp.bfloat16)
    gate_attn_grad = jnp.sum(middle_grad * attended, axis=0)
    mixed_grad = jnp.dot(attended_grad, weight_out.T, preferred_element_type=jnp.float32).astype(
        jnp.bfloat16
    )
    out_grad = jnp.dot(mixed.T, attended_grad, preferred_element_type=jnp.float32)
    mixed_heads = mixed_grad.reshape(local_rows, HEADS, HEAD_DIM)
    key_heads = gathered[:, :width].reshape(total_rows, HEADS, HEAD_DIM)
    value_heads = gathered[:, width:].reshape(total_rows, HEADS, HEAD_DIM)
    scores = (
        jnp.einsum("thd,nhd->htn", queries, key_heads, preferred_element_type=jnp.float32) * factor
    )
    probabilities = jnp.exp(scores - log_total)
    prob_grads = jnp.einsum(
        "thd,nhd->htn", mixed_heads, value_heads, preferred_element_type=jnp.float32
    )
    centre = jnp.sum(prob_grads * probabilities, axis=-1, keepdims=True)
    score_grads = (probabilities * (prob_grads - centre)).astype(jnp.bfloat16)
    query_grads = (
        jnp.einsum("htn,nhd->thd", score_grads, key_heads, preferred_element_type=jnp.float32)
        * factor
    )
    value_grads = jnp.einsum(
        "htn,thd->nhd",
        probabilities.astype(jnp.bfloat16),
        mixed_heads,
        preferred_element_type=jnp.float32,
    )
    key_grads = (
        jnp.einsum("htn,thd->nhd", score_grads, queries, preferred_element_type=jnp.float32)
        * factor
    )
    key_value_grads = jnp.concatenate(
        [key_grads.reshape(total_rows, width), value_grads.reshape(total_rows, width)], axis=1
    )
    local_grads = spread_keys(key_value_grads)
    projected_grad = jnp.concatenate(
        [query_grads.reshape(local_rows, width), local_grads], axis=1
    ).astype(jnp.bfloat16)
    normed_grad = jnp.dot(projected_grad, weight_qkv.T, preferred_element_type=jnp.float32)
    qkv_grad = jnp.dot(normed.T, projected_grad, preferred_element_type=jnp.float32)
    _, first_back = jax.vjp(pre_norm, current, shift_attn, scale_attn)
    current_part, shift_attn_grad, scale_attn_grad = first_back(normed_grad)
    input_grad = middle_grad + current_part
    modulation_grad = jnp.concatenate(
        [
            shift_attn_grad,
            scale_attn_grad,
            gate_attn_grad,
            shift_mlp_grad,
            scale_mlp_grad,
            gate_mlp_grad,
        ]
    )
    return (input_grad, (qkv_grad, out_grad, up_grad, down_grad, modulation_grad))


def shards(fields, lead_index, rollout, w_qkv, w_out, w_up, w_down, w_ada, b_ada, cotangent):
    _, rows_dev, cols_dev, width = fields.shape
    local_rows = rows_dev * cols_dev
    layer_count = w_qkv.shape[0]
    context = jax.nn.silu(embedding(lead_index[0])).astype(jnp.bfloat16)
    context_wide = context.astype(jnp.float32)
    modulations = [
        (
            jnp.dot(context[None, :], w_ada[index], preferred_element_type=jnp.float32)[0]
            + b_ada[index]
        ).reshape(6, width)
        for index in range(layer_count)
    ]
    weight_sets = [
        (w_qkv[index], w_out[index], w_up[index], w_down[index]) for index in range(layer_count)
    ]
    count = rollout[0]
    current = fields.reshape(local_rows, width).astype(jnp.float32)
    saved = []
    for rollout_step in range(STEPS):
        updated = current
        kept_layers = []
        for index in range(layer_count):
            updated, kept = forward_layer(updated, modulations[index], *weight_sets[index])
            kept_layers.append(kept)
        current = jnp.where(rollout_step < count, updated, current)
        saved.append(kept_layers)
    gradient = cotangent.reshape(local_rows, width).astype(jnp.float32)
    summed = None
    shares = None
    for rollout_step in reversed(range(STEPS)):
        active = (rollout_step < count).astype(jnp.float32)
        inner = gradient * active
        layer_terms = [None] * layer_count
        for index in reversed(range(layer_count)):
            inner, layer_terms[index] = backward_layer(
                inner, saved[rollout_step][index], modulations[index], *weight_sets[index]
            )
        gradient = inner + (1.0 - active) * gradient
        modulation_grads = jnp.stack([terms[4] for terms in layer_terms])
        step_terms = (
            jnp.stack([terms[0] for terms in layer_terms]),
            jnp.stack([terms[1] for terms in layer_terms]),
            jnp.stack([terms[2] for terms in layer_terms]),
            jnp.stack([terms[3] for terms in layer_terms]),
            context_wide[None, :, None] * modulation_grads[:, None, :],
            modulation_grads,
            modulation_grads[:, 3 * width : 4 * width],
        )
        summed = step_terms if summed is None else jax.tree.map(jnp.add, summed, step_terms)
    shares = lax.psum_scatter(summed, ("lat", "lon"), scatter_dimension=1, tiled=True)
    totals = jax.tree.map(
        lambda part: part.astype(jnp.float32), lax.psum(shortened(shares), "item")
    )
    return (
        current.reshape(1, rows_dev, cols_dev, width),
        gradient.reshape(1, rows_dev, cols_dev, width),
        totals[0],
        totals[1],
        totals[2],
        totals[3],
        totals[4],
        totals[5],
        totals[6],
    )


F32 = jnp.float32
BF16 = jnp.bfloat16
GELU_A = math.sqrt(2.0 / math.pi)
GELU_B = 0.044715
LANES = 128
BLOCK = 256
PAIR = 2 * HEAD_DIM
SUM_ROWS = 40


def nn(left, right, precision=None):
    return lax.dot_general(
        left, right, (((1,), (0,)), ((), ())), preferred_element_type=F32, precision=precision
    )


def nt(left, right, precision=None):
    return lax.dot_general(
        left, right, (((1,), (1,)), ((), ())), preferred_element_type=F32, precision=precision
    )


def identity(size):
    rows = lax.broadcasted_iota(jnp.int32, (size, size), 0)
    columns = lax.broadcasted_iota(jnp.int32, (size, size), 1)
    return jnp.where(rows == columns, 1.0, 0.0).astype(BF16)


def turned(values):
    return nt(identity(values.shape[1]), values).astype(BF16)


def wide(column_tile, lanes):
    return jnp.concatenate([column_tile] * (lanes // LANES), axis=1)


def folded(values):
    pieces = [values[:, at : at + LANES] for at in range(0, values.shape[1], LANES)]
    return sum(pieces[1:], pieces[0])


def standardise(values):
    rows = values.shape[0]
    centred = values - jnp.sum(values, axis=0, keepdims=True) * (1.0 / rows)
    variance = jnp.sum(centred * centred, axis=0, keepdims=True) * (1.0 / rows)
    scale = lax.rsqrt(variance + 1e-06)
    return centred * scale, scale


def pre_norm_back(standard, scale, grad, gain):
    rows = standard.shape[0]
    inner = grad * gain
    first = jnp.sum(inner, axis=0, keepdims=True) * (1.0 / rows)
    second = jnp.sum(inner * standard, axis=0, keepdims=True) * (1.0 / rows)
    return scale * (inner - first - standard * second)


def part(mod_ref, index, lanes):
    return wide(mod_ref[index * D : (index + 1) * D, :], lanes)


def turn_into(source, out, at=0):
    for column in range(0, out.shape[0], BLOCK):
        width = min(BLOCK, out.shape[0] - column)
        out[column : column + width, :] = turned(source[:, at + column : at + column + width])


def prepare_first_kernel(index, between, waits, context, w_ada, b_ada, w_qkv, *refs):
    mod, w_q_t, w_v_t, w_k, *scratch, sems = refs[waits:]
    copies = [
        pltpu.make_async_copy(source, target, sems.at[place])
        for place, (source, target) in enumerate(zip((w_qkv.at[index], w_ada.at[index], b_ada), scratch))
    ]
    for copy in copies:
        copy.start()
    if between:
        between()
    w_qkv, w_ada, b_ada = scratch
    copies[0].wait()
    w_k[...] = w_qkv[:, D : 2 * D]
    turn_into(w_qkv, w_q_t)
    turn_into(w_qkv, w_v_t, 2 * D)
    copies[1].wait()
    copies[2].wait()
    values = nn(context[...], w_ada[...])[0:1] + b_ada[index : index + 1, :]
    for column in range(0, values.shape[1], LANES):
        tile = jnp.broadcast_to(values[:, column : column + LANES], (LANES, LANES))
        mod[column : column + LANES, :] = tile.T


def prepare_rest_kernel(index, w_out, w_up, w_down, *outs):
    for weight, out in zip((w_out, w_up, w_down), outs):
        turn_into(weight.at[index], out)


def prepare_both_kernel(context, w_ada, b_ada, w_qkv, w_out, w_up, w_down, *refs):
    between = functools.partial(prepare_rest_kernel, 0, w_out, w_up, w_down, *refs[4:7])
    prepare_first_kernel(1, between, 0, context, w_ada, b_ada, w_qkv, *refs[:4], *refs[7:])


def project(x, mod_ref, w_q_t, w_v_t, w_k, outs):
    q_out, kn_out, vt_out = outs
    lanes = x.shape[1]
    standard, _ = standardise(x)
    normed = (standard * (1.0 + part(mod_ref, 1, lanes)) + part(mod_ref, 0, lanes)).astype(BF16)
    vt_out[...] = nn(w_v_t[...], normed).astype(BF16)
    q_out[...] = (nn(w_q_t[...], normed) * HEAD_DIM ** (-0.5)).astype(BF16)
    for at in range(0, lanes, BLOCK):
        kn_out[at : at + BLOCK, :] = nn(turned(normed[:, at : at + BLOCK]), w_k[...]).astype(BF16)


def first_kernel(own, flip_x, flip_y, flip_xy, mod, w_q_t, w_v_t, w_k, x_out, xb_out, *outs):
    for index, ref in enumerate((own, flip_x, flip_y, flip_xy)):
        rows = ref.shape[0] // 2
        flat = turned(ref[:rows, :])
        xb_out[:, index * rows : (index + 1) * rows] = flat
        x_out[:, index * rows : (index + 1) * rows] = flat.astype(F32)
    project(x_out[...], mod, w_q_t, w_v_t, w_k, outs)


def head_rows(head):
    return slice(head * HEAD_DIM, (head + 1) * HEAD_DIM)


def pair_columns(head):
    return slice(head // 2 * PAIR, (head // 2 + 1) * PAIR)


def padded(rows, head):
    zeros = jnp.zeros_like(rows)
    return jnp.concatenate([rows, zeros] if head % 2 == 0 else [zeros, rows], axis=0)


def forward_kernel(last, *refs):
    if last:
        active, x, x_step, *refs = refs
    else:
        x, *refs = refs
    q, kn_own, kn_far, vt_own, vt_far, mod, w_out_t, w_up_t, w_down_t, *refs = refs
    if not last:
        mod_next, w_q_t, w_v_t, w_k, *refs = refs
    lse, mixed, attended, middle, hidden, slope, branch, *refs = refs
    if last:
        (final,) = refs
    else:
        x_next, xb_next, *next_outs = refs
    patches = x.shape[1]

    def score(head):
        columns = pair_columns(head)
        query = padded(q[head_rows(head), :], head)
        return nn(kn_own[:, columns], query), nn(kn_far[:, columns], query)

    ones = jnp.ones((16, patches), BF16)
    following = score(0)
    for head in range(HEADS):
        scores_own, scores_far = following
        if head + 1 < HEADS:
            following = score(head + 1)
        rows = head_rows(head)
        top = jnp.maximum(
            jnp.max(scores_own, axis=0, keepdims=True), jnp.max(scores_far, axis=0, keepdims=True)
        )
        total = None
        for scores, values in ((scores_own, vt_own), (scores_far, vt_far)):
            for key in range(0, patches, BLOCK):
                probs = jnp.exp(scores[key : key + BLOCK] - top).astype(BF16)
                value = jnp.concatenate([values[rows, key : key + BLOCK], ones[:, :BLOCK]], axis=0)
                term = nn(value, probs)
                total = term if total is None else total + term
        weight = total[HEAD_DIM : HEAD_DIM + 1]
        mixed[rows, :] = (total[:HEAD_DIM] * (1.0 / weight)).astype(BF16)
        lse[head : head + 1, :] = top + jnp.log(weight)

    att = nn(w_out_t[...], mixed[...])
    attended[...] = att.astype(BF16)
    mid = x[...] + part(mod, 2, patches) * att
    middle[...] = mid.astype(BF16)
    standard, _ = standardise(mid)
    hidden_in = (standard * (1.0 + part(mod, 4, patches)) + part(mod, 3, patches)).astype(BF16)
    chunks = w_up_t.shape[0] // D

    def up(chunk):
        return nn(w_up_t[chunk * D : (chunk + 1) * D, :], hidden_in)

    following = up(0)
    down = None
    for chunk in range(chunks):
        act = following
        if chunk + 1 < chunks:
            following = up(chunk + 1)
        rows = slice(chunk * D, (chunk + 1) * D)
        squared = act * act
        bent = jnp.tanh(act * (GELU_A + (GELU_A * GELU_B) * squared))
        half = 0.5 + 0.5 * bent
        kept = (act * half).astype(BF16)
        hidden[rows, :] = kept
        curve = (1.0 - bent * bent) * (0.5 * GELU_A + (1.5 * GELU_A * GELU_B) * squared)
        slope[rows, :] = (half + act * curve).astype(BF16)
        term = nn(w_down_t[:, chunk * D : (chunk + 1) * D], kept)
        down = term if down is None else down + term
    branch[...] = down.astype(BF16)
    out = mid + part(mod, 5, patches) * down
    if last:
        own = final.shape[0]
        final[...] = jnp.where(active[0] > 0.0, out[:, :own], x_step[:, :own]).T
    else:
        x_next[...] = out
        xb_next[...] = out.astype(BF16)
        project(out, mod_next, w_q_t, w_v_t, w_k, next_outs)


def put_grads(left_ref, right, where, count, at, mine, other, before):
    rows = [left_ref[pl.ds(pl.multiple_of(where[place] * count, 16), count), :] for place in range(2)]
    product = nt(jnp.concatenate(rows, axis=0), right)
    for column in range(0, product.shape[1], LANES):
        low = product[:count, column : column + LANES]
        high = product[count:, column : column + LANES]
        if before is not None:
            low = low + before[0][at : at + count, :]
            high = high + before[1][at : at + count, :]
        mine[at : at + count, :] = low.astype(mine.dtype)
        other[at : at + count, :] = high.astype(other.dtype)
        at += count


def dense_back_kernel(has_close, has_open, has_before, start, layers, waits, *refs):
    refs = list(refs)

    def take(count):
        taken = refs[:count]
        del refs[:count]
        return taken

    take(waits)
    where, active = take(2)
    close_before = open_before = None
    if has_close:
        d_own, d_got, dq, d_mid_in, x_in, mod_in, w_qkv = take(7)
        w_qkv = w_qkv.at[layers[0]]
        if has_before[0]:
            close_before = take(3)
    if start == "first":
        cots = take(4)
    elif start == "cross":
        cots = take(1)
    if has_open:
        mixed, attended, middle, hidden, slope, branch, mod, w_out, w_up, w_down = take(10)
        w_out, w_up, w_down = (ref.at[layers[1]] for ref in (w_out, w_up, w_down))
        if has_before[1]:
            open_before = take(3)
    else:
        (lines,) = take(1)
    if has_close:
        close_mine, close_other, close_mods = take(3)
    if start == "first":
        (cot_out,) = take(1)
    if has_open:
        open_mine, open_other, open_mods, d_mid_out, do_out, cen_out = take(6)
    else:
        g_out, sums_out = take(2)
        sums_at = close_before[1].shape[0]
    if has_close:
        grads_scr, normed_scr = take(2)
    if has_open:
        bg_scr, pg_scr, hin_scr, ag_scr = take(4)

    patches = middle.shape[1] if has_open else x_in.shape[1]

    def add_sums(out, before, at, values):
        total = folded(values)
        out[at * D : (at + 1) * D, :] = total + before[2][at * D : (at + 1) * D, :] if before else total

    if start == "first":
        pieces = [turned(ref[ref.shape[0] // 2 :, :]) for ref in cots]
        for index, piece in enumerate(pieces):
            rows = piece.shape[1]
            cot_out[:, index * rows : (index + 1) * rows] = piece
        g = cot_out[...].astype(F32) * active[0]
    if has_open:
        standard_mid, scale_mid = standardise(middle[...].astype(F32))
        gain_mid = 1.0 + part(mod, 4, patches)
        hin_scr[...] = (standard_mid * gain_mid + part(mod, 3, patches)).astype(BF16)
    if has_close:
        back = None
        standard, scale = standardise(x_in[...].astype(F32))
        gain = 1.0 + part(mod_in, 1, patches)
        normed_scr[...] = (standard * gain + part(mod_in, 0, patches)).astype(BF16)
        for third in range(3):
            if third == 0:
                piece = dq[...]
            else:
                rows = slice((third - 1) * D, third * D)
                piece = (d_own[rows, :] + d_got[rows, :].astype(F32)).astype(BF16)
            grads_scr[third * D : (third + 1) * D, :] = piece
            term = nn(w_qkv[:, third * D : (third + 1) * D], piece)
            back = term if back is None else back + term
        put_grads(normed_scr, grads_scr[...], where, D // 8, 0, close_mine, close_other, close_before)
        add_sums(close_mods, close_before, 0, back)
        add_sums(close_mods, close_before, 1, back * standard)
        g = d_mid_in[...] + pre_norm_back(standard, scale, back, gain)
        if start == "cross":
            g = g + (1.0 - active[0]) * cots[0][...].astype(F32)
    if has_open:
        branch_grad = (part(mod, 5, patches) * g).astype(BF16)
        bg_scr[...] = branch_grad
        add_sums(open_mods, open_before, 3, g * branch[...].astype(F32))
        chunks = w_down.shape[0] // D

        def down(chunk):
            return nn(w_down[chunk * D : (chunk + 1) * D, :], branch_grad)

        following = down(0)
        back = None
        for chunk in range(chunks):
            hidden_grad = following
            if chunk + 1 < chunks:
                following = down(chunk + 1)
            rows = slice(chunk * D, (chunk + 1) * D)
            pre_grad = (slope[rows, :].astype(F32) * hidden_grad).astype(BF16)
            pg_scr[rows, :] = pre_grad
            term = nn(w_up[:, chunk * D : (chunk + 1) * D], pre_grad)
            back = term if back is None else back + term
        count = w_down.shape[0] // 8
        put_grads(hidden, branch_grad, where, count, 0, open_mine, open_other, open_before)
        at = count * (D // LANES)
        add_sums(open_mods, open_before, 1, back)
        add_sums(open_mods, open_before, 2, back * standard_mid)
        d_mid = g + pre_norm_back(standard_mid, scale_mid, back, gain_mid)
        put_grads(hin_scr, pg_scr[...], where, D // 8, at, open_mine, open_other, open_before)
        at += (w_up.shape[1] // LANES) * (D // 8)
        d_mid_out[...] = d_mid
        att_grad = (part(mod, 2, patches) * d_mid).astype(BF16)
        ag_scr[...] = att_grad
        mixed_grad = nn(w_out[...], att_grad).astype(BF16)
        do_out[...] = mixed_grad
        add_sums(open_mods, open_before, 0, d_mid * attended[...].astype(F32))
        put_grads(mixed, att_grad, where, D // 8, at, open_mine, open_other, open_before)
        product = mixed_grad.astype(F32) * mixed[...].astype(F32)
        for head in range(HEADS):
            cen_out[head : head + 1, :] = jnp.sum(product[head_rows(head)], axis=0, keepdims=True)
    else:
        g_out[...] = g[:, : g_out.shape[0]].T
        sums_out[...] = lines[...]
        put_lines(sums_out, 0, close_mods[...])
        put_pair(close_other, sums_at, sums_out[...])


def attend_back_kernel(has_before, waits, q, kn, vt, lse, d_out, centre, *refs):
    if has_before:
        before, *refs = refs
    d_kv, dq_out, kt_scr, vn_scr = refs[waits:]
    for column in range(0, D, LANES):
        kt_scr[column : column + LANES, :] = turned(kn[:, column : column + LANES])
    for column in range(0, vt.shape[1], BLOCK):
        vn_scr[column : column + BLOCK, :] = turned(vt[:, column : column + BLOCK])

    def score(head):
        columns = pair_columns(head)
        rows = head_rows(head)
        return nn(kn[:, columns], padded(q[rows, :], head)), nn(vn_scr[:, columns], padded(d_out[rows, :], head))

    following = score(0)
    for head in range(HEADS):
        scores, prob_grads = following
        if head + 1 < HEADS:
            following = score(head + 1)
        rows = head_rows(head)
        value_rows = slice(D + rows.start, D + rows.stop)
        probs = jnp.exp(scores - lse[head : head + 1, :])
        score_grads = (probs * (prob_grads - centre[head : head + 1, :])).astype(BF16)
        d_kv[value_rows, :] = nt(d_out[rows, :], probs.astype(BF16)).astype(d_kv.dtype)
        d_kv[rows, :] = nt(q[rows, :], score_grads).astype(d_kv.dtype)
        term = nn(kt_scr[rows, :], score_grads)
        if has_before:
            term = (before[rows, :] + term) * HEAD_DIM ** (-0.5)
        dq_out[rows, :] = term.astype(dq_out.dtype)


def split_kernel(waits, has_last, where, *refs):
    refs = refs[waits:]
    if has_last:
        last_own, last_got, *refs = refs
    *halves, keep, sent, total_scr = refs
    rows_half = keep.shape[0]
    if has_last:
        sent[rows_half:, :] = (last_own[...].astype(F32) + last_got[...].astype(F32)).astype(BF16)
    at = 0
    for mine, other in zip(halves[::2], halves[1::2]):
        rows = mine.shape[0]
        total_scr[at : at + rows, :] = mine[...] + other[...].astype(F32)
        at += rows
    if at < total_scr.shape[0]:
        total_scr[at:, :] = jnp.zeros((total_scr.shape[0] - at, LANES), F32)
    odd = where[3]
    keep[...] = total_scr[pl.ds(pl.multiple_of(odd * rows_half, 16), rows_half), :]
    sent[:rows_half, :] = total_scr[pl.ds(pl.multiple_of((1 - odd) * rows_half, 16), rows_half), :].astype(BF16)


def pair_sum_kernel(keep, got, late, out):
    out[...] = (keep[...].astype(F32) + got[: keep.shape[0], :].astype(F32)).astype(BF16)


def put_lines(out, row, values):
    ones = jnp.ones((16, LANES), BF16)
    high = values.astype(BF16)
    low = (values - high.astype(F32)).astype(BF16)
    line = (nt(ones, high) + nt(ones, low))[0:1]
    for column in range(0, line.shape[1], LANES):
        out[row : row + 1, :] = line[:, column : column + LANES]
        row += 1
    return row


def lines_kernel(early, context, *refs):
    *sums, out = refs
    out[...] = jnp.zeros_like(out)
    row = 2 * D // LANES
    for ref in sums:
        row = put_lines(out, row, ref[...])
    for column in range(0, D, LANES):
        out[row : row + 1, :] = context[0:1, column : column + LANES].astype(F32)
        row += 1


def put_pair(out, at, values):
    rows = values.shape[0]
    high = values.astype(BF16)
    out[at : at + rows, :] = high
    out[at + rows : at + 2 * rows, :] = (values - high.astype(F32)).astype(BF16)


def get_pair(ref, at, rows):
    return ref[at : at + rows, :].astype(F32) + ref[at + rows : at + 2 * rows, :].astype(F32)


def join_kernel(sum_count, mine, sums, got, out):
    rows = mine.shape[0]
    out[:rows, :] = (mine[...] + got[:rows, :].astype(F32)).astype(BF16)
    other = get_pair(got, rows, SUM_ROWS)
    summed = lax.broadcasted_iota(jnp.int32, (SUM_ROWS, LANES), 0) < sum_count
    put_pair(out, rows, sums[...] + jnp.where(summed, other, 0.0))


def pair_kernel(rows, where, own, got, out):
    out[:rows, :] = (own[:rows, :].astype(F32) + got[:rows, :].astype(F32)).astype(BF16)
    odd = where[3]
    size = 2 * SUM_ROWS
    out[pl.ds(pl.multiple_of(rows + odd * size, 16), size), :] = own[rows:, :]
    out[pl.ds(pl.multiple_of(rows + (1 - odd) * size, 16), size), :] = got[rows:, :]


def gather_kernel(where, sent_0, got_0, last_0, last_got_0, out_out, up_out, down_out, qkv_out, scr_0, scr_1):
    odd = where[3]
    rows = last_0.shape[0]
    scr_0[pl.ds(pl.multiple_of(odd * rows, 16), rows), :] = last_0[...]
    scr_0[pl.ds(pl.multiple_of((1 - odd) * rows, 16), rows), :] = last_got_0[...]
    rows_1 = scr_1.shape[0] // 2
    scr_1[pl.ds(pl.multiple_of(odd * rows_1, 16), rows_1), :] = sent_0[rows:, :]
    scr_1[pl.ds(pl.multiple_of((1 - odd) * rows_1, 16), rows_1), :] = got_0[rows:, :]
    slice_rows = out_out.shape[1]
    for index, ref in enumerate((scr_0, scr_1)):
        at = 0
        for out in (down_out, up_out, out_out):
            rows = out.shape[1]
            for column in range(0, out.shape[2], LANES):
                out[index, :, column : column + LANES] = ref[at : at + rows, :].astype(F32)
                at += rows
        if index == 0:
            for column in range(0, qkv_out.shape[1], LANES):
                qkv_out[:, column : column + LANES] = ref[at : at + slice_rows, :].astype(F32)
                at += slice_rows


def finish_kernel(item_count, where, own, got, qkv_1, qkv_out, ada_out, bias_out, shift_out, sum_scr, bias_scr, shift_scr):
    layers = 2
    device, high = where[0], where[4]
    slice_rows = qkv_out.shape[1]
    close_rows = slice_rows * (3 * D // LANES)
    for other in range(2):
        at = close_rows + other * 2 * SUM_ROWS
        sum_scr[2 * high + other] = get_pair(own, at, SUM_ROWS)
        sum_scr[2 * (1 - high) + other] = get_pair(got, at, SUM_ROWS)
    qkv_out[1] = qkv_1[...]
    for tile in range(3 * D // LANES):
        rows = slice(tile * slice_rows, (tile + 1) * slice_rows)
        total = own[rows, :].astype(F32) + got[rows, :].astype(F32)
        qkv_out[0, :, tile * LANES : (tile + 1) * LANES] = total
    tiles = 6 * D // LANES
    contexts = []
    for other in range(item_count):
        line = jnp.concatenate([sum_scr[other, layers * tiles + c : layers * tiles + c + 1, :] for c in range(3)], axis=1)
        contexts.append(line)
    square = jnp.concatenate(contexts + [jnp.zeros((8 - item_count, D), F32)], axis=0)
    spot = lax.broadcasted_iota(jnp.int32, (slice_rows, D), 1)
    want = lax.broadcasted_iota(jnp.int32, (slice_rows, D), 0) + device * slice_rows
    pick = jnp.where(spot == want, 1.0, 0.0).astype(BF16)
    columns = nt(pick, square.astype(BF16))
    bias_rows = bias_out.shape[1]
    for index in range(layers):
        flats = []
        for tile in range(tiles):
            row = index * tiles + tile
            total = None
            flat = None
            for other in range(item_count):
                line = sum_scr[other, row : row + 1, :]
                term = columns[:, other : other + 1] * line
                total = term if total is None else total + term
                flat = line if flat is None else flat + line
            ada_out[index, :, tile * LANES : (tile + 1) * LANES] = total
            flats.append(flat)
        flat = jnp.concatenate(flats, axis=1)
        for place in range(flat.shape[1] // bias_rows):
            bias_scr[place, index : index + 1, :] = flat[:, place * bias_rows : (place + 1) * bias_rows]
            at = 3 * D + place * slice_rows
            shift_scr[place, index : index + 1, :] = flat[:, at : at + slice_rows]
    bias_out[...] = bias_scr[device]
    shift_out[...] = shift_scr[device]


VMEM = pl.BlockSpec(memory_space=pltpu.VMEM)
SMEM = pl.BlockSpec(memory_space=pltpu.SMEM)
ANY = pl.BlockSpec(memory_space=pl.ANY)
HBM = pl.BlockSpec(memory_space=pltpu.HBM)


def layer_block(array, index):
    return pl.BlockSpec((None,) + array.shape[1:], lambda step: (index,) + (0,) * (array.ndim - 1))


def call(body, args, outs, scratch=(), flops=0, name=None):
    arrays = [arg[0] if isinstance(arg, tuple) else arg for arg in args]
    specs = [arg[1] if isinstance(arg, tuple) else VMEM for arg in args]
    return pl.pallas_call(
        body,
        out_shape=[jax.ShapeDtypeStruct(shape, kind) for shape, kind in outs],
        in_specs=specs,
        out_specs=[VMEM] * len(outs),
        scratch_shapes=[one if not isinstance(one, tuple) else pltpu.VMEM(*one) for one in scratch],
        compiler_params=pltpu.CompilerParams(vmem_limit_bytes=VMEM_LIMIT),
        cost_estimate=pl.CostEstimate(flops=flops, bytes_accessed=0, transcendentals=0),
        name=name,
    )(*arrays)


VMEM_LIMIT = 12 * 1024 * 1024


def fast_shards(
    lat_count, lon_count, item_count,
    fields, lead_index, rollout, w_qkv, w_out, w_up, w_down, w_ada, b_ada, cotangent,
):
    _, rows_dev, cols_dev, width = fields.shape
    local = rows_dev * cols_dev
    layers = w_qkv.shape[0]
    ff = w_up.shape[2]
    patches = 4 * local
    device = lax.axis_index("lat") * lon_count + lax.axis_index("lon")
    item = lax.axis_index("item")
    where = jnp.stack([device, device ^ 1, item, item & 1, item >> 1]).astype(jnp.int32)
    active = (1 < rollout[0]).astype(F32)[None]

    def plane_flip(value, flip_lat, flip_y):
        pairs = [
            (a * lon_count + b, (a ^ flip_lat) * lon_count + (b ^ (2 * flip_y)))
            for a in range(lat_count)
            for b in range(lon_count)
        ]
        return lax.ppermute(value, ("lat", "lon"), pairs)

    def swap(value):
        return lax.ppermute(value, "lon", [(index, index ^ 1) for index in range(lon_count)])

    def with_item(value, flip):
        return lax.ppermute(value, "item", [(index, index ^ flip) for index in range(item_count)])

    own = jnp.concatenate([fields.reshape(local, width), cotangent.reshape(local, width)], axis=0)
    parts = [own, plane_flip(own, 1, 0), plane_flip(own, 0, 1), plane_flip(own, 1, 1)]

    context = jax.nn.silu(embedding(lead_index[0])).astype(BF16)
    context = jnp.broadcast_to(context[None, :], (16, width))
    square = (width, patches)
    natural = (patches, width)
    fetched = [(pltpu.with_memory_space_constraint(value, pltpu.HBM), HBM) for value in (w_ada, b_ada, w_qkv)]
    fetch_scratch = [((width, 3 * width), BF16), ((width, 6 * width), BF16), (b_ada.shape, F32)]
    fetch_scratch.append(pltpu.SemaphoreType.DMA((3,)))
    first_outs = [((6 * width, LANES), F32)] + [((width, width), BF16)] * 3
    rest_outs = [((width, width), BF16), ((ff, width), BF16), ((width, ff), BF16)]
    first_0 = call(
        functools.partial(prepare_first_kernel, 0, None, 2),
        [context, *fetched, (where, SMEM), (active, SMEM)],
        first_outs,
        fetch_scratch,
        name="prepare_first",
    )
    both = call(
        prepare_both_kernel,
        [context, *fetched, w_out, w_up, w_down],
        first_outs + rest_outs,
        fetch_scratch,
        name="prepare_both",
    )
    rest_1 = call(
        functools.partial(prepare_rest_kernel, 1), [w_out, w_up, w_down], rest_outs, name="prepare_rest"
    )
    first_parts = [first_0, both[:4]]
    rest_parts = [both[4:], rest_1]
    mods = [one[0] for one in first_parts]

    project_outs = [(square, F32), (square, BF16), (square, BF16), (natural, BF16), (square, BF16)]
    dense_flops = 2 * patches * (width * 3 * width + width * width + 2 * width * ff)
    score_flops = 2 * patches * 2 * patches * width * 4
    x, xb, *projected = call(
        first_kernel,
        [*parts, *first_parts[0]],
        project_outs,
        flops=2 * patches * width * 4 * width,
        name="first",
    )
    saved = []
    for step in range(STEPS):
        for index in range(layers):
            q, kn, vt = projected
            kn_far, vt_far = swap(kn), swap(vt)
            last = step == STEPS - 1 and index == layers - 1
            if index == 0 and step > 0:
                x_step = x
            following = list(first_parts[(index + 1) % layers])
            lse, mixed, attended, middle, hidden, slope, branch, *results = call(
                functools.partial(forward_kernel, last),
                ([(active, SMEM), x, x_step] if last else [x])
                + [q, kn, kn_far, vt, vt_far, mods[index], *rest_parts[index]]
                + ([] if last else following),
                [
                    ((HEADS, patches), F32),
                    (square, BF16),
                    (square, BF16),
                    (square, BF16),
                    ((ff, patches), BF16),
                    ((ff, patches), BF16),
                    (square, BF16),
                ]
                + ([((local, width), F32)] if last else project_outs),
                flops=dense_flops + 2 * score_flops,
                name="forward",
            )
            saved.append((xb, [mixed, attended, middle, hidden, slope, branch], (q, kn, kn_far, vt, vt_far, lse)))
            if last:
                final = results[0]
            else:
                x, xb, *projected = results

    slice_rows = width // 8
    open_rows = 2 * (ff // 8) * (width // LANES) + slice_rows * (width // LANES)
    close_rows = slice_rows * (3 * width // LANES)
    order = [(step, index) for step in reversed(range(STEPS)) for index in reversed(range(layers))]
    open_done = [None] * layers
    close_done = [None] * layers
    pending = None
    for place in range(len(order) + 1):
        has_close = pending is not None
        has_open = place < len(order)
        use = [order[place - 1][1], order[place][1] if has_open else 0]
        waits = [pair_1] if has_close and has_open and close_done[use[0]] else []
        args = [(value, ANY) for value in waits] + [(where, SMEM), (active, SMEM)]
        outs = []
        scratch = []
        has_before = [False, False]
        start = ""
        if has_close:
            args += pending
            if close_done[use[0]] is not None:
                has_before[0] = True
                args += close_done[use[0]]
            outs += [((close_rows, LANES), F32)]
            sent_rows = close_rows + (0 if has_open else 2 * SUM_ROWS)
            outs += [((sent_rows, LANES), BF16 if has_before[0] else F32), ((2 * width, LANES), F32)]
            scratch += [((3 * width, patches), BF16), (square, BF16)]
        if place == 0:
            start = "first"
            args += parts
            outs += [(square, BF16)]
        elif has_open and order[place][0] != order[place - 1][0]:
            start = "cross"
            args += [cot_t]
        if has_open:
            step, index = order[place]
            xb, kept, heads = saved[step * layers + index]
            args += kept + [mods[index], w_out, w_up, w_down]
            if open_done[index] is not None:
                has_before[1] = True
                args += open_done[index]
            outs += [
                ((open_rows, LANES), F32),
                ((open_rows, LANES), BF16 if has_before[1] else F32),
                ((4 * width, LANES), F32),
                (square, F32),
                (square, BF16),
                ((HEADS, patches), F32),
            ]
            scratch += [(square, BF16), ((ff, patches), BF16), (square, BF16), (square, BF16)]
        else:
            args += [lines]
            outs += [((local, width), F32), ((SUM_ROWS, LANES), F32)]
        results = list(
            call(
                functools.partial(dense_back_kernel, has_close, has_open, has_before, start, use, len(waits)),
                args,
                outs,
                scratch,
                flops=2 * dense_flops if has_open else 0,
                name="dense_back" if has_open else "close_back",
            )
        )
        if has_close:
            close_done[use[0]] = results[:3]
            del results[:3]
        if start == "first":
            cot_t = results.pop(0)
        if not has_open:
            gradient, line = results
            break
        open_done[index] = results[:3]
        d_mid, d_out, centre = results[3:]
        q, kn, kn_far, vt, vt_far, lse = heads
        halves = [open_done[index][0], open_done[index][1]]
        if index == 0:
            halves += [close_done[1][0], close_done[1][1]]
        half_rows = -(-sum(half.shape[0] for half in halves[::2]) // 32) * 16

        def split(waits, last):
            pieces = [half if place % 2 == 0 else swap(half) for place, half in enumerate(halves)]
            sent_rows = half_rows + (last[0].shape[0] if last else 0)
            return call(
                functools.partial(split_kernel, len(waits), bool(last)),
                [(where, SMEM), *waits, *last, *pieces],
                [((half_rows, LANES), F32), ((sent_rows, LANES), BF16)],
                [((2 * half_rows, LANES), F32)],
                name="split",
            )

        def pair_sum(keep, got, late):
            return call(pair_sum_kernel, [keep, got, (late, ANY)], [(keep.shape, BF16)], name="pair_sum")[0]

        waits = []
        if has_before[1] and index == 0:
            pair_got_1 = with_item(pair_1, 2)
            lines = call(
                lines_kernel,
                [(pair_got_1, ANY), context, open_done[0][2], close_done[1][2], open_done[1][2]],
                [((SUM_ROWS, LANES), F32)],
                flops=10 * score_flops,
                name="lines",
            )[0]
            keep, sent = split([(lines, ANY)], [pair_1, pair_got_1])
            got_0 = with_item(sent, 1)
            waits = [keep]
        d_far, dq = call(
            functools.partial(attend_back_kernel, False, len(waits)),
            [q, kn_far, vt_far, lse, d_out, centre] + [(value, ANY) for value in waits],
            [((2 * width, patches), BF16), (square, F32)],
            [(square, BF16), (natural, BF16)],
            flops=10 * score_flops,
            name="attend_far",
        )
        d_got = swap(d_far)
        waits = []
        if has_before[1]:
            if index == 1:
                keep, sent = split([(d_far, ANY)], [])
                got_1 = with_item(sent, 1)
                waits = [keep]
            else:
                pair_0 = pair_sum(keep, got_0, d_far)
                pair_got_0 = with_item(pair_0, 2)
                waits = [pair_0]
        d_own, dq = call(
            functools.partial(attend_back_kernel, True, len(waits)),
            [q, kn, vt, lse, d_out, centre, dq] + [(value, ANY) for value in waits],
            [((2 * width, patches), F32), (square, BF16)],
            [(square, BF16), (natural, BF16)],
            flops=10 * score_flops,
            name="attend_own",
        )
        if has_before[1] and index == 1:
            pair_1 = pair_sum(keep, got_1, dq)
        pending = [d_own, d_got, dq, d_mid, xb, mods[index], w_qkv]

    message = call(
        functools.partial(join_kernel, layers * 6 * width // LANES),
        [close_done[0][0], line, swap(close_done[0][1])],
        [((close_rows + 2 * SUM_ROWS, LANES), BF16)],
        name="join",
    )[0]
    message = call(
        functools.partial(pair_kernel, close_rows),
        [(where, SMEM), message, with_item(message, 1)],
        [((close_rows + 4 * SUM_ROWS, LANES), BF16)],
        name="pair",
    )[0]
    message_got = with_item(message, 2)
    item_0 = pair_sum(pair_0, pair_got_0, gradient)
    out_grad, up_grad, down_grad, qkv_1 = call(
        gather_kernel,
        [(where, SMEM), sent, got_0, item_0, with_item(item_0, 1)],
        [
            ((layers, slice_rows, width), F32),
            ((layers, slice_rows, ff), F32),
            ((layers, ff // 8, width), F32),
            ((slice_rows, 3 * width), F32),
        ],
        [((2 * item_0.shape[0], LANES), BF16), ((2 * pair_1.shape[0], LANES), BF16)],
        name="gather",
    )
    bias_rows = 6 * width // 8
    qkv_grad, ada_grad, bias_grad, shift_grad = call(
        functools.partial(finish_kernel, item_count),
        [(where, SMEM), message, message_got, qkv_1],
        [
            ((layers, slice_rows, 3 * width), F32),
            ((layers, slice_rows, 6 * width), F32),
            ((layers, bias_rows), F32),
            ((layers, slice_rows), F32),
        ],
        [
            ((item_count, SUM_ROWS, LANES), F32),
            ((8, layers, bias_rows), F32),
            ((8, layers, slice_rows), F32),
        ],
        name="finish",
    )
    field_shape = (1, rows_dev, cols_dev, width)
    return (
        final.reshape(field_shape),
        gradient.reshape(field_shape),
        qkv_grad,
        out_grad,
        up_grad,
        down_grad,
        ada_grad,
        bias_grad,
        shift_grad,
    )


def solution(mesh):
    lat_count, lon_count, item_count = mesh.shape["lat"], mesh.shape["lon"], mesh.shape["item"]
    if lat_count == 2 and lon_count == 4:
        body = functools.partial(fast_shards, lat_count, lon_count, item_count)
    else:
        body = shards
    return jax.shard_map(
        body,
        mesh=mesh,
        in_specs=(
            P("item", "lat", "lon", None),
            P("item"),
            P("item"),
            P(),
            P(),
            P(),
            P(),
            P(),
            P(),
            P("item", "lat", "lon", None),
        ),
        out_specs=(
            P("item", "lat", "lon", None),
            P("item", "lat", "lon", None),
            P(None, ("lat", "lon"), None),
            P(None, ("lat", "lon"), None),
            P(None, ("lat", "lon"), None),
            P(None, ("lat", "lon"), None),
            P(None, ("lat", "lon"), None),
            P(None, ("lat", "lon")),
            P(None, ("lat", "lon")),
        ),
        check_vma=False,
    )
```

```python
import functools
import math

import jax
import jax.numpy as jnp
from jax import lax
from jax.experimental import pallas as pl
from jax.experimental.pallas import tpu as pltpu
from jax.sharding import PartitionSpec as P

D = 384
HEADS = 6
HEAD_DIM = 64
STEPS = 2


def shortened(shard):
    return jax.tree.map(lambda a: a.astype(jnp.bfloat16) if a.dtype == jnp.float32 else a, shard)


def embedding(lead):
    half_width = D // 2
    lead_hours = 6.0 * (lead.astype(jnp.float32) + 1.0)
    frequencies = jnp.exp(
        -math.log(10000.0) * jnp.arange(half_width, dtype=jnp.float32) / half_width
    )
    angles = lead_hours * frequencies
    return jnp.concatenate([jnp.sin(angles), jnp.cos(angles)])


def pre_norm(values, shift_part, scale_part):
    centred = values - jnp.mean(values, axis=-1, keepdims=True)
    variance = jnp.mean(centred * centred, axis=-1, keepdims=True)
    return centred * lax.rsqrt(variance + 1e-06) * (1.0 + scale_part) + shift_part


def gather_keys(keys_values):
    band_rows = lax.all_gather(keys_values, "lon", axis=0, tiled=True)
    return lax.all_gather(band_rows, "lat", axis=0, tiled=True)


def spread_keys(key_value_grads):
    band_grads = lax.psum_scatter(
        key_value_grads.astype(jnp.bfloat16), "lat", scatter_dimension=0, tiled=True
    )
    return lax.psum_scatter(band_grads, "lon", scatter_dimension=0, tiled=True).astype(jnp.float32)


def forward_layer(current, modulation, weight_qkv, weight_out, weight_up, weight_down):
    local_rows, width = current.shape
    shift_attn, scale_attn, gate_attn, shift_mlp, scale_mlp, gate_mlp = modulation
    normed = pre_norm(current, shift_attn, scale_attn).astype(jnp.bfloat16)
    projected = jnp.dot(normed, weight_qkv, preferred_element_type=jnp.float32).astype(jnp.bfloat16)
    queries = projected[:, :width].reshape(local_rows, HEADS, HEAD_DIM)
    own_keys = projected[:, width:]
    gathered = gather_keys(own_keys)
    total_rows = gathered.shape[0]
    key_heads = gathered[:, :width].reshape(total_rows, HEADS, HEAD_DIM)
    value_heads = gathered[:, width:].reshape(total_rows, HEADS, HEAD_DIM)
    scores = jnp.einsum(
        "thd,nhd->htn", queries, key_heads, preferred_element_type=jnp.float32
    ) * HEAD_DIM ** (-0.5)
    log_total = jax.nn.logsumexp(scores, axis=-1, keepdims=True)
    probabilities = jnp.exp(scores - log_total).astype(jnp.bfloat16)
    mixed = jnp.einsum(
        "htn,nhd->thd", probabilities, value_heads, preferred_element_type=jnp.float32
    )
    mixed = mixed.reshape(local_rows, width).astype(jnp.bfloat16)
    attended = jnp.dot(mixed, weight_out, preferred_element_type=jnp.float32)
    middle = current + gate_attn * attended
    hidden_in = pre_norm(middle, shift_mlp, scale_mlp).astype(jnp.bfloat16)
    pre_act = jnp.dot(hidden_in, weight_up, preferred_element_type=jnp.float32)
    hidden = jax.nn.gelu(pre_act).astype(jnp.bfloat16)
    branch = jnp.dot(hidden, weight_down, preferred_element_type=jnp.float32)
    output = middle + gate_mlp * branch
    kept = (
        current,
        normed,
        queries,
        gathered,
        own_keys,
        log_total,
        mixed,
        attended,
        middle,
        hidden_in,
        pre_act,
        hidden,
        branch,
    )
    return (output, kept)


def backward_layer(grad_out, kept, modulation, weight_qkv, weight_out, weight_up, weight_down):
    (
        current,
        normed,
        queries,
        gathered,
        own_keys,
        log_total,
        mixed,
        attended,
        middle,
        hidden_in,
        pre_act,
        hidden,
        branch,
    ) = kept
    local_rows, width = current.shape
    total_rows = gathered.shape[0]
    shift_attn, scale_attn, gate_attn, shift_mlp, scale_mlp, gate_mlp = modulation
    factor = HEAD_DIM ** (-0.5)
    branch_grad = (gate_mlp * grad_out).astype(jnp.bfloat16)
    gate_mlp_grad = jnp.sum(grad_out * branch, axis=0)
    hidden_grad = jnp.dot(branch_grad, weight_down.T, preferred_element_type=jnp.float32)
    down_grad = jnp.dot(hidden.T, branch_grad, preferred_element_type=jnp.float32)
    _, gelu_back = jax.vjp(jax.nn.gelu, pre_act)
    pre_grad = gelu_back(hidden_grad)[0].astype(jnp.bfloat16)
    hidden_in_grad = jnp.dot(pre_grad, weight_up.T, preferred_element_type=jnp.float32)
    up_grad = jnp.dot(hidden_in.T, pre_grad, preferred_element_type=jnp.float32)
    _, second_back = jax.vjp(pre_norm, middle, shift_mlp, scale_mlp)
    middle_part, shift_mlp_grad, scale_mlp_grad = second_back(hidden_in_grad)
    middle_grad = grad_out + middle_part
    attended_grad = (gate_attn * middle_grad).astype(jnp.bfloat16)
    gate_attn_grad = jnp.sum(middle_grad * attended, axis=0)
    mixed_grad = jnp.dot(attended_grad, weight_out.T, preferred_element_type=jnp.float32).astype(
        jnp.bfloat16
    )
    out_grad = jnp.dot(mixed.T, attended_grad, preferred_element_type=jnp.float32)
    mixed_heads = mixed_grad.reshape(local_rows, HEADS, HEAD_DIM)
    key_heads = gathered[:, :width].reshape(total_rows, HEADS, HEAD_DIM)
    value_heads = gathered[:, width:].reshape(total_rows, HEADS, HEAD_DIM)
    scores = (
        jnp.einsum("thd,nhd->htn", queries, key_heads, preferred_element_type=jnp.float32) * factor
    )
    probabilities = jnp.exp(scores - log_total)
    prob_grads = jnp.einsum(
        "thd,nhd->htn", mixed_heads, value_heads, preferred_element_type=jnp.float32
    )
    centre = jnp.sum(prob_grads * probabilities, axis=-1, keepdims=True)
    score_grads = (probabilities * (prob_grads - centre)).astype(jnp.bfloat16)
    query_grads = (
        jnp.einsum("htn,nhd->thd", score_grads, key_heads, preferred_element_type=jnp.float32)
        * factor
    )
    value_grads = jnp.einsum(
        "htn,thd->nhd",
        probabilities.astype(jnp.bfloat16),
        mixed_heads,
        preferred_element_type=jnp.float32,
    )
    key_grads = (
        jnp.einsum("htn,thd->nhd", score_grads, queries, preferred_element_type=jnp.float32)
        * factor
    )
    key_value_grads = jnp.concatenate(
        [key_grads.reshape(total_rows, width), value_grads.reshape(total_rows, width)], axis=1
    )
    local_grads = spread_keys(key_value_grads)
    projected_grad = jnp.concatenate(
        [query_grads.reshape(local_rows, width), local_grads], axis=1
    ).astype(jnp.bfloat16)
    normed_grad = jnp.dot(projected_grad, weight_qkv.T, preferred_element_type=jnp.float32)
    qkv_grad = jnp.dot(normed.T, projected_grad, preferred_element_type=jnp.float32)
    _, first_back = jax.vjp(pre_norm, current, shift_attn, scale_attn)
    current_part, shift_attn_grad, scale_attn_grad = first_back(normed_grad)
    input_grad = middle_grad + current_part
    modulation_grad = jnp.concatenate(
        [
            shift_attn_grad,
            scale_attn_grad,
            gate_attn_grad,
            shift_mlp_grad,
            scale_mlp_grad,
            gate_mlp_grad,
        ]
    )
    return (input_grad, (qkv_grad, out_grad, up_grad, down_grad, modulation_grad))


def shards(fields, lead_index, rollout, w_qkv, w_out, w_up, w_down, w_ada, b_ada, cotangent):
    _, rows_dev, cols_dev, width = fields.shape
    local_rows = rows_dev * cols_dev
    layer_count = w_qkv.shape[0]
    context = jax.nn.silu(embedding(lead_index[0])).astype(jnp.bfloat16)
    context_wide = context.astype(jnp.float32)
    modulations = [
        (
            jnp.dot(context[None, :], w_ada[index], preferred_element_type=jnp.float32)[0]
            + b_ada[index]
        ).reshape(6, width)
        for index in range(layer_count)
    ]
    weight_sets = [
        (w_qkv[index], w_out[index], w_up[index], w_down[index]) for index in range(layer_count)
    ]
    count = rollout[0]
    current = fields.reshape(local_rows, width).astype(jnp.float32)
    saved = []
    for rollout_step in range(STEPS):
        updated = current
        kept_layers = []
        for index in range(layer_count):
            updated, kept = forward_layer(updated, modulations[index], *weight_sets[index])
            kept_layers.append(kept)
        current = jnp.where(rollout_step < count, updated, current)
        saved.append(kept_layers)
    gradient = cotangent.reshape(local_rows, width).astype(jnp.float32)
    summed = None
    shares = None
    for rollout_step in reversed(range(STEPS)):
        active = (rollout_step < count).astype(jnp.float32)
        inner = gradient * active
        layer_terms = [None] * layer_count
        for index in reversed(range(layer_count)):
            inner, layer_terms[index] = backward_layer(
                inner, saved[rollout_step][index], modulations[index], *weight_sets[index]
            )
        gradient = inner + (1.0 - active) * gradient
        modulation_grads = jnp.stack([terms[4] for terms in layer_terms])
        step_terms = (
            jnp.stack([terms[0] for terms in layer_terms]),
            jnp.stack([terms[1] for terms in layer_terms]),
            jnp.stack([terms[2] for terms in layer_terms]),
            jnp.stack([terms[3] for terms in layer_terms]),
            context_wide[None, :, None] * modulation_grads[:, None, :],
            modulation_grads,
            modulation_grads[:, 3 * width : 4 * width],
        )
        summed = step_terms if summed is None else jax.tree.map(jnp.add, summed, step_terms)
    shares = lax.psum_scatter(summed, ("lat", "lon"), scatter_dimension=1, tiled=True)
    totals = jax.tree.map(
        lambda part: part.astype(jnp.float32), lax.psum(shortened(shares), "item")
    )
    return (
        current.reshape(1, rows_dev, cols_dev, width),
        gradient.reshape(1, rows_dev, cols_dev, width),
        totals[0],
        totals[1],
        totals[2],
        totals[3],
        totals[4],
        totals[5],
        totals[6],
    )


F32 = jnp.float32
BF16 = jnp.bfloat16
GELU_A = math.sqrt(2.0 / math.pi)
GELU_B = 0.044715
LANES = 128
BLOCK = 256
PAIR = 2 * HEAD_DIM
SUM_ROWS = 40


def nn(left, right, precision=None):
    return lax.dot_general(
        left, right, (((1,), (0,)), ((), ())), preferred_element_type=F32, precision=precision
    )


def nt(left, right, precision=None):
    return lax.dot_general(
        left, right, (((1,), (1,)), ((), ())), preferred_element_type=F32, precision=precision
    )


def identity(size):
    rows = lax.broadcasted_iota(jnp.int32, (size, size), 0)
    columns = lax.broadcasted_iota(jnp.int32, (size, size), 1)
    return jnp.where(rows == columns, 1.0, 0.0).astype(BF16)


def turned(values):
    return nt(identity(values.shape[1]), values).astype(BF16)


def wide(column_tile, lanes):
    return jnp.concatenate([column_tile] * (lanes // LANES), axis=1)


def folded(values):
    pieces = [values[:, at : at + LANES] for at in range(0, values.shape[1], LANES)]
    return sum(pieces[1:], pieces[0])


def standardise(values):
    rows = values.shape[0]
    centred = values - jnp.sum(values, axis=0, keepdims=True) * (1.0 / rows)
    variance = jnp.sum(centred * centred, axis=0, keepdims=True) * (1.0 / rows)
    scale = lax.rsqrt(variance + 1e-06)
    return centred * scale, scale


def pre_norm_back(standard, scale, grad, gain):
    rows = standard.shape[0]
    inner = grad * gain
    first = jnp.sum(inner, axis=0, keepdims=True) * (1.0 / rows)
    second = jnp.sum(inner * standard, axis=0, keepdims=True) * (1.0 / rows)
    return scale * (inner - first - standard * second)


def part(mod_ref, index, lanes):
    return wide(mod_ref[index * D : (index + 1) * D, :], lanes)


def turn_into(source, out, at=0):
    for column in range(0, out.shape[0], BLOCK):
        width = min(BLOCK, out.shape[0] - column)
        out[column : column + width, :] = turned(source[:, at + column : at + column + width])


def prepare_first_kernel(index, between, waits, context, w_ada, b_ada, w_qkv, *refs):
    mod, w_q_t, w_v_t, w_k, *scratch, sems = refs[waits:]
    copies = [
        pltpu.make_async_copy(source, target, sems.at[place])
        for place, (source, target) in enumerate(zip((w_qkv.at[index], w_ada.at[index], b_ada), scratch))
    ]
    for copy in copies:
        copy.start()
    if between:
        between()
    w_qkv, w_ada, b_ada = scratch
    copies[0].wait()
    w_k[...] = w_qkv[:, D : 2 * D]
    turn_into(w_qkv, w_q_t)
    turn_into(w_qkv, w_v_t, 2 * D)
    copies[1].wait()
    copies[2].wait()
    values = nn(context[...], w_ada[...])[0:1] + b_ada[index : index + 1, :]
    for column in range(0, values.shape[1], LANES):
        tile = jnp.broadcast_to(values[:, column : column + LANES], (LANES, LANES))
        mod[column : column + LANES, :] = tile.T


def prepare_rest_kernel(index, w_out, w_up, w_down, *outs):
    for weight, out in zip((w_out, w_up, w_down), outs):
        turn_into(weight.at[index], out)


def prepare_both_kernel(context, w_ada, b_ada, w_qkv, w_out, w_up, w_down, *refs):
    between = functools.partial(prepare_rest_kernel, 0, w_out, w_up, w_down, *refs[4:7])
    prepare_first_kernel(1, between, 0, context, w_ada, b_ada, w_qkv, *refs[:4], *refs[7:])


def project(x, mod_ref, w_q_t, w_v_t, w_k, outs, at):
    q_out, kn_out, vt_out = outs
    lanes = x.shape[1]
    standard, _ = standardise(x)
    normed = (standard * (1.0 + part(mod_ref, 1, lanes)) + part(mod_ref, 0, lanes)).astype(BF16)
    kn_out[at, :] = nn(turned(normed), w_k[...]).astype(BF16)
    vt_out[:, at] = nn(w_v_t[...], normed).astype(BF16)
    q_out[:, at] = (nn(w_q_t[...], normed) * HEAD_DIM ** (-0.5)).astype(BF16)


def blocks_of(count):
    return [slice(at, at + BLOCK) for at in range(0, count, BLOCK)]


def first_kernel(own, flip_x, flip_y, flip_xy, mod, w_q_t, w_v_t, w_k, x_out, xb_out, *outs):
    for index, ref in enumerate((own, flip_x, flip_y, flip_xy)):
        rows = ref.shape[0]
        flat = turned(ref[...])
        xb_out[:, index * rows : (index + 1) * rows] = flat
        x_out[:, index * rows : (index + 1) * rows] = flat.astype(F32)
    for at in blocks_of(x_out.shape[1]):
        project(x_out[:, at], mod, w_q_t, w_v_t, w_k, outs, at)


def head_rows(head):
    return slice(head * HEAD_DIM, (head + 1) * HEAD_DIM)


def pair_columns(head):
    return slice(head // 2 * PAIR, (head // 2 + 1) * PAIR)


def padded(rows, head):
    zeros = jnp.zeros_like(rows)
    return jnp.concatenate([rows, zeros] if head % 2 == 0 else [zeros, rows], axis=0)


def forward_kernel(last, *refs):
    if last:
        active, x, x_step, *refs = refs
    else:
        x, *refs = refs
    q, kn_own, kn_far, vt_own, vt_far, mod, w_out_t, w_up_t, w_down_t, *refs = refs
    if not last:
        mod_next, w_q_t, w_v_t, w_k, *refs = refs
    lse, mixed, attended, middle, hidden, slope, branch, *refs = refs
    if last:
        (final,) = refs
    else:
        x_next, xb_next, *next_outs = refs
    patches = x.shape[1]

    chunks = w_up_t.shape[0] // D
    ones = jnp.ones((16, BLOCK), BF16)

    def attend(at):
        def score(head):
            columns = pair_columns(head)
            query = padded(q[head_rows(head), at], head)
            return nn(kn_own[:, columns], query), nn(kn_far[:, columns], query)

        following = score(0)
        for head in range(HEADS):
            scores_own, scores_far = following
            if head + 1 < HEADS:
                following = score(head + 1)
            rows = head_rows(head)
            top = jnp.maximum(
                jnp.max(scores_own, axis=0, keepdims=True), jnp.max(scores_far, axis=0, keepdims=True)
            )
            total = None
            for scores, values in ((scores_own, vt_own), (scores_far, vt_far)):
                for key in range(0, patches, BLOCK):
                    probs = jnp.exp(scores[key : key + BLOCK] - top).astype(BF16)
                    value = jnp.concatenate([values[rows, key : key + BLOCK], ones], axis=0)
                    term = nn(value, probs)
                    total = term if total is None else total + term
            weight = total[HEAD_DIM : HEAD_DIM + 1]
            mixed[rows, at] = (total[:HEAD_DIM] * (1.0 / weight)).astype(BF16)
            lse[head : head + 1, at] = top + jnp.log(weight)

    def dense(at):
        att = nn(w_out_t[...], mixed[:, at])
        attended[:, at] = att.astype(BF16)
        mid = x[:, at] + part(mod, 2, BLOCK) * att
        middle[:, at] = mid.astype(BF16)
        standard, _ = standardise(mid)
        hidden_in = (standard * (1.0 + part(mod, 4, BLOCK)) + part(mod, 3, BLOCK)).astype(BF16)

        def up(chunk):
            return nn(w_up_t[chunk * D : (chunk + 1) * D, :], hidden_in)

        following = up(0)
        down = None
        for chunk in range(chunks):
            act = following
            if chunk + 1 < chunks:
                following = up(chunk + 1)
            rows = slice(chunk * D, (chunk + 1) * D)
            squared = act * act
            bent = jnp.tanh(act * (GELU_A + (GELU_A * GELU_B) * squared))
            half = 0.5 + 0.5 * bent
            kept = (act * half).astype(BF16)
            hidden[rows, at] = kept
            curve = (1.0 - bent * bent) * (0.5 * GELU_A + (1.5 * GELU_A * GELU_B) * squared)
            slope[rows, at] = (half + act * curve).astype(BF16)
            term = nn(w_down_t[:, chunk * D : (chunk + 1) * D], kept)
            down = term if down is None else down + term
        branch[:, at] = down.astype(BF16)
        out = mid + part(mod, 5, BLOCK) * down
        if last:
            own = final.shape[0]
            if at.start == 0:
                final[...] = jnp.where(active[0] > 0.0, out[:, :own], x_step[:, :own]).T
        else:
            x_next[:, at] = out
            xb_next[:, at] = out.astype(BF16)
            project(out, mod_next, w_q_t, w_v_t, w_k, next_outs, at)

    for at in blocks_of(patches):
        attend(at)
        dense(at)


def put_grads(left_ref, right, where, count, at, mine, other, before):
    rows = [left_ref[pl.ds(pl.multiple_of(where[place] * count, 16), count), :] for place in range(2)]
    product = nt(jnp.concatenate(rows, axis=0), right)
    for column in range(0, product.shape[1], LANES):
        low = product[:count, column : column + LANES]
        high = product[count:, column : column + LANES]
        if before is not None:
            low = low + before[0][at : at + count, :]
            high = high + before[1][at : at + count, :]
        mine[at : at + count, :] = low.astype(mine.dtype)
        other[at : at + count, :] = high.astype(other.dtype)
        at += count


def dense_back_kernel(has_close, has_open, has_before, start, layers, waits, *refs):
    refs = list(refs)

    def take(count):
        taken = refs[:count]
        del refs[:count]
        return taken

    take(waits)
    where, active = take(2)
    close_before = open_before = None
    if has_close:
        d_own, d_got, dq, d_mid_in, x_in, mod_in, w_qkv = take(7)
        w_qkv = w_qkv.at[layers[0]]
        if has_before[0]:
            close_before = take(3)
    if start == "first":
        cots = take(4)
    elif start == "cross":
        cots = take(1)
    if has_open:
        mixed, attended, middle, hidden, slope, branch, mod, w_out, w_up, w_down = take(10)
        w_out, w_up, w_down = (ref.at[layers[1]] for ref in (w_out, w_up, w_down))
        if has_before[1]:
            open_before = take(3)
    else:
        (lines,) = take(1)
    if has_close:
        close_mine, close_other, close_mods = take(3)
    if start == "first":
        (cot_out,) = take(1)
    if has_open:
        open_mine, open_other, open_mods, d_mid_out, do_out, cen_out = take(6)
    else:
        g_out, sums_out = take(2)
        sums_at = close_before[1].shape[0]
    if has_close:
        grads_scr, normed_scr = take(2)
    if has_open:
        bg_scr, pg_scr, hin_scr, ag_scr = take(4)

    patches = middle.shape[1] if has_open else x_in.shape[1]
    totals = {}

    def add_sums(name, values):
        totals[name] = totals[name] + folded(values) if name in totals else folded(values)

    def put_sums(out, before, names):
        for place, name in enumerate(names):
            rows = slice(place * D, (place + 1) * D)
            out[rows, :] = totals[name] + before[2][rows, :] if before else totals[name]

    if start == "first":
        for index, ref in enumerate(cots):
            rows = ref.shape[0]
            cot_out[:, index * rows : (index + 1) * rows] = turned(ref[...])

    def close(at):
        back = None
        standard, scale = standardise(x_in[:, at].astype(F32))
        gain = 1.0 + part(mod_in, 1, BLOCK)
        normed_scr[:, at] = (standard * gain + part(mod_in, 0, BLOCK)).astype(BF16)
        for third in range(3):
            if third == 0:
                piece = dq[:, at]
            else:
                rows = slice((third - 1) * D, third * D)
                piece = (d_own[rows, at] + d_got[rows, at].astype(F32)).astype(BF16)
            grads_scr[third * D : (third + 1) * D, at] = piece
            term = nn(w_qkv[:, third * D : (third + 1) * D], piece)
            back = term if back is None else back + term
        add_sums("shift_a", back)
        add_sums("scale_a", back * standard)
        g = d_mid_in[:, at] + pre_norm_back(standard, scale, back, gain)
        if start == "cross":
            g = g + (1.0 - active[0]) * cots[0][:, at].astype(F32)
        return g

    def dense(at, g):
        standard, scale = standardise(middle[:, at].astype(F32))
        gain = 1.0 + part(mod, 4, BLOCK)
        hin_scr[:, at] = (standard * gain + part(mod, 3, BLOCK)).astype(BF16)
        branch_grad = (part(mod, 5, BLOCK) * g).astype(BF16)
        bg_scr[:, at] = branch_grad
        add_sums("gate_m", g * branch[:, at].astype(F32))
        chunks = w_down.shape[0] // D

        def down(chunk):
            return nn(w_down[chunk * D : (chunk + 1) * D, :], branch_grad)

        following = down(0)
        back = None
        for chunk in range(chunks):
            hidden_grad = following
            if chunk + 1 < chunks:
                following = down(chunk + 1)
            rows = slice(chunk * D, (chunk + 1) * D)
            pre_grad = (slope[rows, at].astype(F32) * hidden_grad).astype(BF16)
            pg_scr[rows, at] = pre_grad
            term = nn(w_up[:, chunk * D : (chunk + 1) * D], pre_grad)
            back = term if back is None else back + term
        add_sums("shift_m", back)
        add_sums("scale_m", back * standard)
        d_mid = g + pre_norm_back(standard, scale, back, gain)
        d_mid_out[:, at] = d_mid
        att_grad = (part(mod, 2, BLOCK) * d_mid).astype(BF16)
        ag_scr[:, at] = att_grad
        mixed_grad = nn(w_out[...], att_grad).astype(BF16)
        do_out[:, at] = mixed_grad
        add_sums("gate_a", d_mid * attended[:, at].astype(F32))
        product = mixed_grad.astype(F32) * mixed[:, at].astype(F32)
        for head in range(HEADS):
            cen_out[head : head + 1, at] = jnp.sum(product[head_rows(head)], axis=0, keepdims=True)

    for at in blocks_of(patches):
        g = close(at) if has_close else cot_out[:, at].astype(F32) * active[0]
        if has_open:
            dense(at, g)
        elif at.start == 0:
            g_out[...] = g[:, : g_out.shape[0]].T
    if has_close:
        put_sums(close_mods, close_before, ("shift_a", "scale_a"))
        put_grads(normed_scr, grads_scr[...], where, D // 8, 0, close_mine, close_other, close_before)
    if has_open:
        put_sums(open_mods, open_before, ("gate_a", "shift_m", "scale_m", "gate_m"))
        count = w_down.shape[0] // 8
        put_grads(hidden, bg_scr[...], where, count, 0, open_mine, open_other, open_before)
        at = count * (D // LANES)
        put_grads(hin_scr, pg_scr[...], where, D // 8, at, open_mine, open_other, open_before)
        at += (w_up.shape[1] // LANES) * (D // 8)
        put_grads(mixed, ag_scr[...], where, D // 8, at, open_mine, open_other, open_before)
    else:
        sums_out[...] = lines[...]
        put_lines(sums_out, 0, close_mods[...])
        put_pair(close_other, sums_at, sums_out[...])


def attend_back_kernel(has_before, waits, q, kn, vt, lse, d_out, centre, *refs):
    if has_before:
        before, *refs = refs
    d_kv, dq_out, kt_scr, vn_scr = refs[waits:]
    for column in range(0, D, LANES):
        kt_scr[column : column + LANES, :] = turned(kn[:, column : column + LANES])
    for column in range(0, vt.shape[1], BLOCK):
        vn_scr[column : column + BLOCK, :] = turned(vt[:, column : column + BLOCK])

    def score(head):
        columns = pair_columns(head)
        rows = head_rows(head)
        return nn(kn[:, columns], padded(q[rows, :], head)), nn(vn_scr[:, columns], padded(d_out[rows, :], head))

    following = score(0)
    for head in range(HEADS):
        scores, prob_grads = following
        if head + 1 < HEADS:
            following = score(head + 1)
        rows = head_rows(head)
        value_rows = slice(D + rows.start, D + rows.stop)
        probs = jnp.exp(scores - lse[head : head + 1, :])
        score_grads = (probs * (prob_grads - centre[head : head + 1, :])).astype(BF16)
        d_kv[value_rows, :] = nt(d_out[rows, :], probs.astype(BF16)).astype(d_kv.dtype)
        d_kv[rows, :] = nt(q[rows, :], score_grads).astype(d_kv.dtype)
        term = nn(kt_scr[rows, :], score_grads)
        if has_before:
            term = (before[rows, :] + term) * HEAD_DIM ** (-0.5)
        dq_out[rows, :] = term.astype(dq_out.dtype)


def split_kernel(waits, where, *refs):
    *halves, keep, sent, total_scr = refs[waits:]
    rows_half = keep.shape[0]
    at = 0
    for mine, other in zip(halves[::2], halves[1::2]):
        rows = mine.shape[0]
        total_scr[at : at + rows, :] = mine[...] + other[...].astype(F32)
        at += rows
    if at < total_scr.shape[0]:
        total_scr[at:, :] = jnp.zeros((total_scr.shape[0] - at, LANES), F32)
    odd = where[3]
    keep[...] = total_scr[pl.ds(pl.multiple_of(odd * rows_half, 16), rows_half), :]
    sent[...] = total_scr[pl.ds(pl.multiple_of((1 - odd) * rows_half, 16), rows_half), :].astype(BF16)


def pair_sum_kernel(late, *refs):
    *pairs, out = refs
    at = 0
    for keep, got in zip(pairs[::2], pairs[1::2]):
        rows = keep.shape[0]
        out[at : at + rows, :] = (keep[...].astype(F32) + got[...].astype(F32)).astype(BF16)
        at += rows


def put_lines(out, row, values):
    ones = jnp.ones((16, LANES), BF16)
    high = values.astype(BF16)
    low = (values - high.astype(F32)).astype(BF16)
    line = (nt(ones, high) + nt(ones, low))[0:1]
    for column in range(0, line.shape[1], LANES):
        out[row : row + 1, :] = line[:, column : column + LANES]
        row += 1
    return row


def lines_kernel(early, context, *refs):
    *sums, out = refs
    out[...] = jnp.zeros_like(out)
    row = 2 * D // LANES
    for ref in sums:
        row = put_lines(out, row, ref[...])
    for column in range(0, D, LANES):
        out[row : row + 1, :] = context[0:1, column : column + LANES].astype(F32)
        row += 1


def put_pair(out, at, values):
    rows = values.shape[0]
    high = values.astype(BF16)
    out[at : at + rows, :] = high
    out[at + rows : at + 2 * rows, :] = (values - high.astype(F32)).astype(BF16)


def get_pair(ref, at, rows):
    return ref[at : at + rows, :].astype(F32) + ref[at + rows : at + 2 * rows, :].astype(F32)


def join_kernel(sum_count, mine, sums, got, out):
    rows = mine.shape[0]
    out[:rows, :] = (mine[...] + got[:rows, :].astype(F32)).astype(BF16)
    other = get_pair(got, rows, SUM_ROWS)
    summed = lax.broadcasted_iota(jnp.int32, (SUM_ROWS, LANES), 0) < sum_count
    put_pair(out, rows, sums[...] + jnp.where(summed, other, 0.0))


def pair_kernel(rows, where, own, got, out):
    out[:rows, :] = (own[:rows, :].astype(F32) + got[:rows, :].astype(F32)).astype(BF16)
    odd = where[3]
    size = 2 * SUM_ROWS
    out[pl.ds(pl.multiple_of(rows + odd * size, 16), size), :] = own[rows:, :]
    out[pl.ds(pl.multiple_of(rows + (1 - odd) * size, 16), size), :] = got[rows:, :]


def gather_kernel(where, own, got, out_out, up_out, down_out, qkv_out, *scratch):
    odd = where[3]
    at = 0
    for ref in scratch:
        rows = ref.shape[0] // 2
        ref[pl.ds(pl.multiple_of(odd * rows, 16), rows), :] = own[at : at + rows, :]
        ref[pl.ds(pl.multiple_of((1 - odd) * rows, 16), rows), :] = got[at : at + rows, :]
        at += rows
    slice_rows = out_out.shape[1]
    for index, ref in enumerate(scratch):
        at = 0
        for out in (down_out, up_out, out_out):
            rows = out.shape[1]
            for column in range(0, out.shape[2], LANES):
                out[index, :, column : column + LANES] = ref[at : at + rows, :].astype(F32)
                at += rows
        if index == 0:
            for column in range(0, qkv_out.shape[1], LANES):
                qkv_out[:, column : column + LANES] = ref[at : at + slice_rows, :].astype(F32)
                at += slice_rows


def finish_kernel(item_count, where, own, got, qkv_1, qkv_out, ada_out, bias_out, shift_out, sum_scr, bias_scr, shift_scr):
    layers = 2
    device, high = where[0], where[4]
    slice_rows = qkv_out.shape[1]
    close_rows = slice_rows * (3 * D // LANES)
    for other in range(2):
        at = close_rows + other * 2 * SUM_ROWS
        sum_scr[2 * high + other] = get_pair(own, at, SUM_ROWS)
        sum_scr[2 * (1 - high) + other] = get_pair(got, at, SUM_ROWS)
    qkv_out[1] = qkv_1[...]
    for tile in range(3 * D // LANES):
        rows = slice(tile * slice_rows, (tile + 1) * slice_rows)
        total = own[rows, :].astype(F32) + got[rows, :].astype(F32)
        qkv_out[0, :, tile * LANES : (tile + 1) * LANES] = total
    tiles = 6 * D // LANES
    contexts = []
    for other in range(item_count):
        line = jnp.concatenate([sum_scr[other, layers * tiles + c : layers * tiles + c + 1, :] for c in range(3)], axis=1)
        contexts.append(line)
    square = jnp.concatenate(contexts + [jnp.zeros((8 - item_count, D), F32)], axis=0)
    spot = lax.broadcasted_iota(jnp.int32, (slice_rows, D), 1)
    want = lax.broadcasted_iota(jnp.int32, (slice_rows, D), 0) + device * slice_rows
    pick = jnp.where(spot == want, 1.0, 0.0).astype(BF16)
    columns = nt(pick, square.astype(BF16))
    bias_rows = bias_out.shape[1]
    for index in range(layers):
        flats = []
        for tile in range(tiles):
            row = index * tiles + tile
            total = None
            flat = None
            for other in range(item_count):
                line = sum_scr[other, row : row + 1, :]
                term = columns[:, other : other + 1] * line
                total = term if total is None else total + term
                flat = line if flat is None else flat + line
            ada_out[index, :, tile * LANES : (tile + 1) * LANES] = total
            flats.append(flat)
        flat = jnp.concatenate(flats, axis=1)
        for place in range(flat.shape[1] // bias_rows):
            bias_scr[place, index : index + 1, :] = flat[:, place * bias_rows : (place + 1) * bias_rows]
            at = 3 * D + place * slice_rows
            shift_scr[place, index : index + 1, :] = flat[:, at : at + slice_rows]
    bias_out[...] = bias_scr[device]
    shift_out[...] = shift_scr[device]


VMEM = pl.BlockSpec(memory_space=pltpu.VMEM)
SMEM = pl.BlockSpec(memory_space=pltpu.SMEM)
ANY = pl.BlockSpec(memory_space=pl.ANY)
HBM = pl.BlockSpec(memory_space=pltpu.HBM)


def layer_block(array, index):
    return pl.BlockSpec((None,) + array.shape[1:], lambda step: (index,) + (0,) * (array.ndim - 1))


def call(body, args, outs, scratch=(), flops=0, name=None):
    arrays = [arg[0] if isinstance(arg, tuple) else arg for arg in args]
    specs = [arg[1] if isinstance(arg, tuple) else VMEM for arg in args]
    return pl.pallas_call(
        body,
        out_shape=[jax.ShapeDtypeStruct(shape, kind) for shape, kind in outs],
        in_specs=specs,
        out_specs=[VMEM] * len(outs),
        scratch_shapes=[one if not isinstance(one, tuple) else pltpu.VMEM(*one) for one in scratch],
        compiler_params=pltpu.CompilerParams(vmem_limit_bytes=VMEM_LIMIT),
        cost_estimate=pl.CostEstimate(flops=flops, bytes_accessed=0, transcendentals=0),
        name=name,
    )(*arrays)


VMEM_LIMIT = 12 * 1024 * 1024


def fast_shards(
    lat_count, lon_count, item_count,
    fields, lead_index, rollout, w_qkv, w_out, w_up, w_down, w_ada, b_ada, cotangent,
):
    _, rows_dev, cols_dev, width = fields.shape
    local = rows_dev * cols_dev
    layers = w_qkv.shape[0]
    ff = w_up.shape[2]
    patches = 4 * local
    device = lax.axis_index("lat") * lon_count + lax.axis_index("lon")
    item = lax.axis_index("item")
    where = jnp.stack([device, device ^ 1, item, item & 1, item >> 1]).astype(jnp.int32)
    active = (1 < rollout[0]).astype(F32)[None]

    def plane_flip(value, flip_lat, flip_y):
        pairs = [
            (a * lon_count + b, (a ^ flip_lat) * lon_count + (b ^ (2 * flip_y)))
            for a in range(lat_count)
            for b in range(lon_count)
        ]
        return lax.ppermute(value, ("lat", "lon"), pairs)

    def swap(value):
        return lax.ppermute(value, "lon", [(index, index ^ 1) for index in range(lon_count)])

    def with_item(value, flip):
        return lax.ppermute(value, "item", [(index, index ^ flip) for index in range(item_count)])

    def plane_parts(value):
        return [value, plane_flip(value, 1, 0), plane_flip(value, 0, 1), plane_flip(value, 1, 1)]

    field_parts = plane_parts(fields.reshape(local, width))
    cot_parts = plane_parts(cotangent.reshape(local, width))

    context = jax.nn.silu(embedding(lead_index[0])).astype(BF16)
    context = jnp.broadcast_to(context[None, :], (16, width))
    square = (width, patches)
    natural = (patches, width)
    fetched = [(pltpu.with_memory_space_constraint(value, pltpu.HBM), HBM) for value in (w_ada, b_ada, w_qkv)]
    fetch_scratch = [((width, 3 * width), BF16), ((width, 6 * width), BF16), (b_ada.shape, F32)]
    fetch_scratch.append(pltpu.SemaphoreType.DMA((3,)))
    first_outs = [((6 * width, LANES), F32)] + [((width, width), BF16)] * 3
    rest_outs = [((width, width), BF16), ((ff, width), BF16), ((width, ff), BF16)]
    first_0 = call(
        functools.partial(prepare_first_kernel, 0, None, 2),
        [context, *fetched, (where, SMEM), (active, SMEM)],
        first_outs,
        fetch_scratch,
        name="prepare_first",
    )
    both = call(
        prepare_both_kernel,
        [context, *fetched, w_out, w_up, w_down],
        first_outs + rest_outs,
        fetch_scratch,
        name="prepare_both",
    )
    rest_1 = call(
        functools.partial(prepare_rest_kernel, 1), [w_out, w_up, w_down], rest_outs, name="prepare_rest"
    )
    first_parts = [first_0, both[:4]]
    rest_parts = [both[4:], rest_1]
    mods = [one[0] for one in first_parts]

    project_outs = [(square, F32), (square, BF16), (square, BF16), (natural, BF16), (square, BF16)]
    dense_flops = 2 * patches * (width * 3 * width + width * width + 2 * width * ff)
    score_flops = 2 * patches * 2 * patches * width * 4
    x, xb, *projected = call(
        first_kernel,
        [*field_parts, *first_parts[0]],
        project_outs,
        flops=2 * patches * width * 4 * width,
        name="first",
    )
    saved = []
    for step in range(STEPS):
        for index in range(layers):
            q, kn, vt = projected
            kn_far, vt_far = swap(kn), swap(vt)
            last = step == STEPS - 1 and index == layers - 1
            if index == 0 and step > 0:
                x_step = x
            following = list(first_parts[(index + 1) % layers])
            lse, mixed, attended, middle, hidden, slope, branch, *results = call(
                functools.partial(forward_kernel, last),
                ([(active, SMEM), x, x_step] if last else [x])
                + [q, kn, kn_far, vt, vt_far, mods[index], *rest_parts[index]]
                + ([] if last else following),
                [
                    ((HEADS, patches), F32),
                    (square, BF16),
                    (square, BF16),
                    (square, BF16),
                    ((ff, patches), BF16),
                    ((ff, patches), BF16),
                    (square, BF16),
                ]
                + ([((local, width), F32)] if last else project_outs),
                flops=dense_flops + 2 * score_flops,
                name="forward",
            )
            saved.append((xb, [mixed, attended, middle, hidden, slope, branch], (q, kn, kn_far, vt, vt_far, lse)))
            if last:
                final = results[0]
            else:
                x, xb, *projected = results

    slice_rows = width // 8
    open_rows = 2 * (ff // 8) * (width // LANES) + slice_rows * (width // LANES)
    close_rows = slice_rows * (3 * width // LANES)
    order = [(step, index) for step in reversed(range(STEPS)) for index in reversed(range(layers))]
    open_done = [None] * layers
    close_done = [None] * layers
    pending = None
    for place in range(len(order) + 1):
        has_close = pending is not None
        has_open = place < len(order)
        use = [order[place - 1][1], order[place][1] if has_open else 0]
        waits = [pair_1] if has_close and has_open and close_done[use[0]] else []
        args = [(value, ANY) for value in waits] + [(where, SMEM), (active, SMEM)]
        outs = []
        scratch = []
        has_before = [False, False]
        start = ""
        if has_close:
            args += pending
            if close_done[use[0]] is not None:
                has_before[0] = True
                args += close_done[use[0]]
            outs += [((close_rows, LANES), F32)]
            sent_rows = close_rows + (0 if has_open else 2 * SUM_ROWS)
            outs += [((sent_rows, LANES), BF16 if has_before[0] else F32), ((2 * width, LANES), F32)]
            scratch += [((3 * width, patches), BF16), (square, BF16)]
        if place == 0:
            start = "first"
            args += cot_parts
            outs += [(square, BF16)]
        elif has_open and order[place][0] != order[place - 1][0]:
            start = "cross"
            args += [cot_t]
        if has_open:
            step, index = order[place]
            xb, kept, heads = saved[step * layers + index]
            args += kept + [mods[index], w_out, w_up, w_down]
            if open_done[index] is not None:
                has_before[1] = True
                args += open_done[index]
            outs += [
                ((open_rows, LANES), F32),
                ((open_rows, LANES), BF16 if has_before[1] else F32),
                ((4 * width, LANES), F32),
                (square, F32),
                (square, BF16),
                ((HEADS, patches), F32),
            ]
            scratch += [(square, BF16), ((ff, patches), BF16), (square, BF16), (square, BF16)]
        else:
            args += [lines]
            outs += [((local, width), F32), ((SUM_ROWS, LANES), F32)]
        results = list(
            call(
                functools.partial(dense_back_kernel, has_close, has_open, has_before, start, use, len(waits)),
                args,
                outs,
                scratch,
                flops=2 * dense_flops if has_open else 0,
                name="dense_back" if has_open else "close_back",
            )
        )
        if has_close:
            close_done[use[0]] = results[:3]
            del results[:3]
        if start == "first":
            cot_t = results.pop(0)
        if not has_open:
            gradient, line = results
            break
        open_done[index] = results[:3]
        d_mid, d_out, centre = results[3:]
        q, kn, kn_far, vt, vt_far, lse = heads
        halves = [open_done[index][0], open_done[index][1]]
        if index == 0:
            halves += [close_done[1][0], close_done[1][1]]
        half_rows = -(-sum(half.shape[0] for half in halves[::2]) // 32) * 16

        def split(waits):
            pieces = [half if place % 2 == 0 else swap(half) for place, half in enumerate(halves)]
            return call(
                functools.partial(split_kernel, len(waits)),
                [(where, SMEM), *waits, *pieces],
                [((half_rows, LANES), F32), ((half_rows, LANES), BF16)],
                [((2 * half_rows, LANES), F32)],
                name="split",
            )

        def pair_sum(late, *pairs):
            rows = sum(keep.shape[0] for keep in pairs[::2])
            return call(pair_sum_kernel, [(late, ANY), *pairs], [((rows, LANES), BF16)], name="pair_sum")[0]

        waits = []
        if has_before[1] and index == 0:
            pair_got_1 = with_item(pair_1, 2)
            lines = call(
                lines_kernel,
                [(pair_got_1, ANY), context, open_done[0][2], close_done[1][2], open_done[1][2]],
                [((SUM_ROWS, LANES), F32)],
                flops=10 * score_flops,
                name="lines",
            )[0]
            keep, sent = split([(lines, ANY)])
            got_0 = with_item(sent, 1)
            waits = [keep]
        d_far, dq = call(
            functools.partial(attend_back_kernel, False, len(waits)),
            [q, kn_far, vt_far, lse, d_out, centre] + [(value, ANY) for value in waits],
            [((2 * width, patches), BF16), (square, F32)],
            [(square, BF16), (natural, BF16)],
            flops=10 * score_flops,
            name="attend_far",
        )
        d_got = swap(d_far)
        waits = []
        if has_before[1]:
            if index == 1:
                keep, sent = split([(d_far, ANY)])
                got_1 = with_item(sent, 1)
                waits = [keep]
            else:
                pair_0 = pair_sum(d_far, keep, got_0)
                pair_got_0 = with_item(pair_0, 2)
                waits = [pair_0]
        d_own, dq = call(
            functools.partial(attend_back_kernel, True, len(waits)),
            [q, kn, vt, lse, d_out, centre, dq] + [(value, ANY) for value in waits],
            [((2 * width, patches), F32), (square, BF16)],
            [(square, BF16), (natural, BF16)],
            flops=10 * score_flops,
            name="attend_own",
        )
        if has_before[1] and index == 1:
            pair_1 = pair_sum(dq, keep, got_1)
        pending = [d_own, d_got, dq, d_mid, xb, mods[index], w_qkv]

    message = call(
        functools.partial(join_kernel, layers * 6 * width // LANES),
        [close_done[0][0], line, swap(close_done[0][1])],
        [((close_rows + 2 * SUM_ROWS, LANES), BF16)],
        name="join",
    )[0]
    done = pair_sum(message, pair_0, pair_got_0, pair_1, pair_got_1)
    message = call(
        functools.partial(pair_kernel, close_rows),
        [(where, SMEM), message, with_item(message, 1)],
        [((close_rows + 4 * SUM_ROWS, LANES), BF16)],
        name="pair",
    )[0]
    out_grad, up_grad, down_grad, qkv_1 = call(
        gather_kernel,
        [(where, SMEM), done, with_item(done, 1)],
        [
            ((layers, slice_rows, width), F32),
            ((layers, slice_rows, ff), F32),
            ((layers, ff // 8, width), F32),
            ((slice_rows, 3 * width), F32),
        ],
        [((2 * pair.shape[0], LANES), BF16) for pair in (pair_0, pair_1)],
        name="gather",
    )
    bias_rows = 6 * width // 8
    qkv_grad, ada_grad, bias_grad, shift_grad = call(
        functools.partial(finish_kernel, item_count),
        [(where, SMEM), message, with_item(message, 2), qkv_1],
        [
            ((layers, slice_rows, 3 * width), F32),
            ((layers, slice_rows, 6 * width), F32),
            ((layers, bias_rows), F32),
            ((layers, slice_rows), F32),
        ],
        [
            ((item_count, SUM_ROWS, LANES), F32),
            ((8, layers, bias_rows), F32),
            ((8, layers, slice_rows), F32),
        ],
        name="finish",
    )
    field_shape = (1, rows_dev, cols_dev, width)
    return (
        final.reshape(field_shape),
        gradient.reshape(field_shape),
        qkv_grad,
        out_grad,
        up_grad,
        down_grad,
        ada_grad,
        bias_grad,
        shift_grad,
    )


def solution(mesh):
    lat_count, lon_count, item_count = mesh.shape["lat"], mesh.shape["lon"], mesh.shape["item"]
    if lat_count == 2 and lon_count == 4:
        body = functools.partial(fast_shards, lat_count, lon_count, item_count)
    else:
        body = shards
    return jax.shard_map(
        body,
        mesh=mesh,
        in_specs=(
            P("item", "lat", "lon", None),
            P("item"),
            P("item"),
            P(),
            P(),
            P(),
            P(),
            P(),
            P(),
            P("item", "lat", "lon", None),
        ),
        out_specs=(
            P("item", "lat", "lon", None),
            P("item", "lat", "lon", None),
            P(None, ("lat", "lon"), None),
            P(None, ("lat", "lon"), None),
            P(None, ("lat", "lon"), None),
            P(None, ("lat", "lon"), None),
            P(None, ("lat", "lon"), None),
            P(None, ("lat", "lon")),
            P(None, ("lat", "lon")),
        ),
        check_vma=False,
    )
```

```python
import functools
import math

import jax
import jax.numpy as jnp
from jax import lax
from jax.experimental import pallas as pl
from jax.experimental.pallas import tpu as pltpu
from jax.sharding import PartitionSpec as P

D = 384
HEADS = 6
HEAD_DIM = 64
STEPS = 2


def shortened(shard):
    return jax.tree.map(lambda a: a.astype(jnp.bfloat16) if a.dtype == jnp.float32 else a, shard)


def embedding(lead):
    half_width = D // 2
    lead_hours = 6.0 * (lead.astype(jnp.float32) + 1.0)
    frequencies = jnp.exp(
        -math.log(10000.0) * jnp.arange(half_width, dtype=jnp.float32) / half_width
    )
    angles = lead_hours * frequencies
    return jnp.concatenate([jnp.sin(angles), jnp.cos(angles)])


def pre_norm(values, shift_part, scale_part):
    centred = values - jnp.mean(values, axis=-1, keepdims=True)
    variance = jnp.mean(centred * centred, axis=-1, keepdims=True)
    return centred * lax.rsqrt(variance + 1e-06) * (1.0 + scale_part) + shift_part


def gather_keys(keys_values):
    band_rows = lax.all_gather(keys_values, "lon", axis=0, tiled=True)
    return lax.all_gather(band_rows, "lat", axis=0, tiled=True)


def spread_keys(key_value_grads):
    band_grads = lax.psum_scatter(
        key_value_grads.astype(jnp.bfloat16), "lat", scatter_dimension=0, tiled=True
    )
    return lax.psum_scatter(band_grads, "lon", scatter_dimension=0, tiled=True).astype(jnp.float32)


def forward_layer(current, modulation, weight_qkv, weight_out, weight_up, weight_down):
    local_rows, width = current.shape
    shift_attn, scale_attn, gate_attn, shift_mlp, scale_mlp, gate_mlp = modulation
    normed = pre_norm(current, shift_attn, scale_attn).astype(jnp.bfloat16)
    projected = jnp.dot(normed, weight_qkv, preferred_element_type=jnp.float32).astype(jnp.bfloat16)
    queries = projected[:, :width].reshape(local_rows, HEADS, HEAD_DIM)
    own_keys = projected[:, width:]
    gathered = gather_keys(own_keys)
    total_rows = gathered.shape[0]
    key_heads = gathered[:, :width].reshape(total_rows, HEADS, HEAD_DIM)
    value_heads = gathered[:, width:].reshape(total_rows, HEADS, HEAD_DIM)
    scores = jnp.einsum(
        "thd,nhd->htn", queries, key_heads, preferred_element_type=jnp.float32
    ) * HEAD_DIM ** (-0.5)
    log_total = jax.nn.logsumexp(scores, axis=-1, keepdims=True)
    probabilities = jnp.exp(scores - log_total).astype(jnp.bfloat16)
    mixed = jnp.einsum(
        "htn,nhd->thd", probabilities, value_heads, preferred_element_type=jnp.float32
    )
    mixed = mixed.reshape(local_rows, width).astype(jnp.bfloat16)
    attended = jnp.dot(mixed, weight_out, preferred_element_type=jnp.float32)
    middle = current + gate_attn * attended
    hidden_in = pre_norm(middle, shift_mlp, scale_mlp).astype(jnp.bfloat16)
    pre_act = jnp.dot(hidden_in, weight_up, preferred_element_type=jnp.float32)
    hidden = jax.nn.gelu(pre_act).astype(jnp.bfloat16)
    branch = jnp.dot(hidden, weight_down, preferred_element_type=jnp.float32)
    output = middle + gate_mlp * branch
    kept = (
        current,
        normed,
        queries,
        gathered,
        own_keys,
        log_total,
        mixed,
        attended,
        middle,
        hidden_in,
        pre_act,
        hidden,
        branch,
    )
    return (output, kept)


def backward_layer(grad_out, kept, modulation, weight_qkv, weight_out, weight_up, weight_down):
    (
        current,
        normed,
        queries,
        gathered,
        own_keys,
        log_total,
        mixed,
        attended,
        middle,
        hidden_in,
        pre_act,
        hidden,
        branch,
    ) = kept
    local_rows, width = current.shape
    total_rows = gathered.shape[0]
    shift_attn, scale_attn, gate_attn, shift_mlp, scale_mlp, gate_mlp = modulation
    factor = HEAD_DIM ** (-0.5)
    branch_grad = (gate_mlp * grad_out).astype(jnp.bfloat16)
    gate_mlp_grad = jnp.sum(grad_out * branch, axis=0)
    hidden_grad = jnp.dot(branch_grad, weight_down.T, preferred_element_type=jnp.float32)
    down_grad = jnp.dot(hidden.T, branch_grad, preferred_element_type=jnp.float32)
    _, gelu_back = jax.vjp(jax.nn.gelu, pre_act)
    pre_grad = gelu_back(hidden_grad)[0].astype(jnp.bfloat16)
    hidden_in_grad = jnp.dot(pre_grad, weight_up.T, preferred_element_type=jnp.float32)
    up_grad = jnp.dot(hidden_in.T, pre_grad, preferred_element_type=jnp.float32)
    _, second_back = jax.vjp(pre_norm, middle, shift_mlp, scale_mlp)
    middle_part, shift_mlp_grad, scale_mlp_grad = second_back(hidden_in_grad)
    middle_grad = grad_out + middle_part
    attended_grad = (gate_attn * middle_grad).astype(jnp.bfloat16)
    gate_attn_grad = jnp.sum(middle_grad * attended, axis=0)
    mixed_grad = jnp.dot(attended_grad, weight_out.T, preferred_element_type=jnp.float32).astype(
        jnp.bfloat16
    )
    out_grad = jnp.dot(mixed.T, attended_grad, preferred_element_type=jnp.float32)
    mixed_heads = mixed_grad.reshape(local_rows, HEADS, HEAD_DIM)
    key_heads = gathered[:, :width].reshape(total_rows, HEADS, HEAD_DIM)
    value_heads = gathered[:, width:].reshape(total_rows, HEADS, HEAD_DIM)
    scores = (
        jnp.einsum("thd,nhd->htn", queries, key_heads, preferred_element_type=jnp.float32) * factor
    )
    probabilities = jnp.exp(scores - log_total)
    prob_grads = jnp.einsum(
        "thd,nhd->htn", mixed_heads, value_heads, preferred_element_type=jnp.float32
    )
    centre = jnp.sum(prob_grads * probabilities, axis=-1, keepdims=True)
    score_grads = (probabilities * (prob_grads - centre)).astype(jnp.bfloat16)
    query_grads = (
        jnp.einsum("htn,nhd->thd", score_grads, key_heads, preferred_element_type=jnp.float32)
        * factor
    )
    value_grads = jnp.einsum(
        "htn,thd->nhd",
        probabilities.astype(jnp.bfloat16),
        mixed_heads,
        preferred_element_type=jnp.float32,
    )
    key_grads = (
        jnp.einsum("htn,thd->nhd", score_grads, queries, preferred_element_type=jnp.float32)
        * factor
    )
    key_value_grads = jnp.concatenate(
        [key_grads.reshape(total_rows, width), value_grads.reshape(total_rows, width)], axis=1
    )
    local_grads = spread_keys(key_value_grads)
    projected_grad = jnp.concatenate(
        [query_grads.reshape(local_rows, width), local_grads], axis=1
    ).astype(jnp.bfloat16)
    normed_grad = jnp.dot(projected_grad, weight_qkv.T, preferred_element_type=jnp.float32)
    qkv_grad = jnp.dot(normed.T, projected_grad, preferred_element_type=jnp.float32)
    _, first_back = jax.vjp(pre_norm, current, shift_attn, scale_attn)
    current_part, shift_attn_grad, scale_attn_grad = first_back(normed_grad)
    input_grad = middle_grad + current_part
    modulation_grad = jnp.concatenate(
        [
            shift_attn_grad,
            scale_attn_grad,
            gate_attn_grad,
            shift_mlp_grad,
            scale_mlp_grad,
            gate_mlp_grad,
        ]
    )
    return (input_grad, (qkv_grad, out_grad, up_grad, down_grad, modulation_grad))


def shards(fields, lead_index, rollout, w_qkv, w_out, w_up, w_down, w_ada, b_ada, cotangent):
    _, rows_dev, cols_dev, width = fields.shape
    local_rows = rows_dev * cols_dev
    layer_count = w_qkv.shape[0]
    context = jax.nn.silu(embedding(lead_index[0])).astype(jnp.bfloat16)
    context_wide = context.astype(jnp.float32)
    modulations = [
        (
            jnp.dot(context[None, :], w_ada[index], preferred_element_type=jnp.float32)[0]
            + b_ada[index]
        ).reshape(6, width)
        for index in range(layer_count)
    ]
    weight_sets = [
        (w_qkv[index], w_out[index], w_up[index], w_down[index]) for index in range(layer_count)
    ]
    count = rollout[0]
    current = fields.reshape(local_rows, width).astype(jnp.float32)
    saved = []
    for rollout_step in range(STEPS):
        updated = current
        kept_layers = []
        for index in range(layer_count):
            updated, kept = forward_layer(updated, modulations[index], *weight_sets[index])
            kept_layers.append(kept)
        current = jnp.where(rollout_step < count, updated, current)
        saved.append(kept_layers)
    gradient = cotangent.reshape(local_rows, width).astype(jnp.float32)
    summed = None
    shares = None
    for rollout_step in reversed(range(STEPS)):
        active = (rollout_step < count).astype(jnp.float32)
        inner = gradient * active
        layer_terms = [None] * layer_count
        for index in reversed(range(layer_count)):
            inner, layer_terms[index] = backward_layer(
                inner, saved[rollout_step][index], modulations[index], *weight_sets[index]
            )
        gradient = inner + (1.0 - active) * gradient
        modulation_grads = jnp.stack([terms[4] for terms in layer_terms])
        step_terms = (
            jnp.stack([terms[0] for terms in layer_terms]),
            jnp.stack([terms[1] for terms in layer_terms]),
            jnp.stack([terms[2] for terms in layer_terms]),
            jnp.stack([terms[3] for terms in layer_terms]),
            context_wide[None, :, None] * modulation_grads[:, None, :],
            modulation_grads,
            modulation_grads[:, 3 * width : 4 * width],
        )
        summed = step_terms if summed is None else jax.tree.map(jnp.add, summed, step_terms)
    shares = lax.psum_scatter(summed, ("lat", "lon"), scatter_dimension=1, tiled=True)
    totals = jax.tree.map(
        lambda part: part.astype(jnp.float32), lax.psum(shortened(shares), "item")
    )
    return (
        current.reshape(1, rows_dev, cols_dev, width),
        gradient.reshape(1, rows_dev, cols_dev, width),
        totals[0],
        totals[1],
        totals[2],
        totals[3],
        totals[4],
        totals[5],
        totals[6],
    )


F32 = jnp.float32
BF16 = jnp.bfloat16
GELU_A = math.sqrt(2.0 / math.pi)
GELU_B = 0.044715
LANES = 128
BLOCK = 256
PAIR = 2 * HEAD_DIM
SUM_ROWS = 48


def nn(left, right, precision=None):
    return lax.dot_general(
        left, right, (((1,), (0,)), ((), ())), preferred_element_type=F32, precision=precision
    )


def nt(left, right, precision=None):
    return lax.dot_general(
        left, right, (((1,), (1,)), ((), ())), preferred_element_type=F32, precision=precision
    )


def identity(size):
    rows = lax.broadcasted_iota(jnp.int32, (size, size), 0)
    columns = lax.broadcasted_iota(jnp.int32, (size, size), 1)
    return jnp.where(rows == columns, 1.0, 0.0).astype(BF16)


def turned(values):
    return nt(identity(values.shape[1]), values).astype(BF16)


def wide(column_tile, lanes):
    return jnp.concatenate([column_tile] * (lanes // LANES), axis=1)


def folded(values):
    pieces = [values[:, at : at + LANES] for at in range(0, values.shape[1], LANES)]
    return sum(pieces[1:], pieces[0])


def standardise(values):
    rows = values.shape[0]
    centred = values - jnp.sum(values, axis=0, keepdims=True) * (1.0 / rows)
    variance = jnp.sum(centred * centred, axis=0, keepdims=True) * (1.0 / rows)
    scale = lax.rsqrt(variance + 1e-06)
    return centred * scale, scale


def pre_norm_back(standard, scale, grad, gain):
    rows = standard.shape[0]
    inner = grad * gain
    first = jnp.sum(inner, axis=0, keepdims=True) * (1.0 / rows)
    second = jnp.sum(inner * standard, axis=0, keepdims=True) * (1.0 / rows)
    return scale * (inner - first - standard * second)


def part(mod_ref, index, lanes):
    return wide(mod_ref[index * D : (index + 1) * D, :], lanes)


def turn_into(source, out, at=0):
    for column in range(0, out.shape[0], BLOCK):
        width = min(BLOCK, out.shape[0] - column)
        out[column : column + width, :] = turned(source[:, at + column : at + column + width])


def prepare_first_kernel(index, between, waits, context, w_ada, b_ada, w_qkv, *refs):
    mod, w_q_t, w_v_t, w_k, *scratch, sems = refs[waits:]
    copies = [
        pltpu.make_async_copy(source, target, sems.at[place])
        for place, (source, target) in enumerate(zip((w_qkv.at[index], w_ada.at[index], b_ada), scratch))
    ]
    for copy in copies:
        copy.start()
    if between:
        between()
    w_qkv, w_ada, b_ada = scratch
    copies[0].wait()
    w_k[...] = w_qkv[:, D : 2 * D]
    turn_into(w_qkv, w_q_t)
    turn_into(w_qkv, w_v_t, 2 * D)
    copies[1].wait()
    copies[2].wait()
    values = nn(context[...], w_ada[...])[0:1] + b_ada[index : index + 1, :]
    for column in range(0, values.shape[1], LANES):
        tile = jnp.broadcast_to(values[:, column : column + LANES], (LANES, LANES))
        mod[column : column + LANES, :] = tile.T


def prepare_rest_kernel(index, w_out, w_up, w_down, *outs):
    for weight, out in zip((w_out, w_up, w_down), outs):
        turn_into(weight.at[index], out)


def prepare_both_kernel(context, w_ada, b_ada, w_qkv, w_out, w_up, w_down, *refs):
    between = functools.partial(prepare_rest_kernel, 0, w_out, w_up, w_down, *refs[4:7])
    prepare_first_kernel(1, between, 0, context, w_ada, b_ada, w_qkv, *refs[:4], *refs[7:])


def project(x, mod_ref, w_q_t, w_v_t, w_k, outs):
    q_out, kn_out, vt_out = outs
    lanes = x.shape[1]
    standard, _ = standardise(x)
    normed = (standard * (1.0 + part(mod_ref, 1, lanes)) + part(mod_ref, 0, lanes)).astype(BF16)
    vt_out[...] = nn(w_v_t[...], normed).astype(BF16)
    q_out[...] = (nn(w_q_t[...], normed) * HEAD_DIM ** (-0.5)).astype(BF16)
    for at in range(0, lanes, BLOCK):
        kn_out[at : at + BLOCK, :] = nn(turned(normed[:, at : at + BLOCK]), w_k[...]).astype(BF16)


def first_kernel(own, flip_x, flip_y, flip_xy, mod, w_q_t, w_v_t, w_k, x_out, xb_out, *outs):
    for index, ref in enumerate((own, flip_x, flip_y, flip_xy)):
        rows = ref.shape[0]
        flat = turned(ref[...])
        xb_out[:, index * rows : (index + 1) * rows] = flat
        x_out[:, index * rows : (index + 1) * rows] = flat.astype(F32)
    project(x_out[...], mod, w_q_t, w_v_t, w_k, outs)


def head_rows(head):
    return slice(head * HEAD_DIM, (head + 1) * HEAD_DIM)


def side_by_side(rows):
    first, second = rows[:HEAD_DIM], rows[HEAD_DIM:]
    zeros = jnp.zeros_like(first)
    upper = jnp.concatenate([first, zeros], axis=1)
    return jnp.concatenate([upper, jnp.concatenate([zeros, second], axis=1)], axis=0)


def forward_kernel(last, *refs):
    if last:
        active, x, x_step, *refs = refs
    else:
        x, *refs = refs
    q, kn_own, kn_far, vt_own, vt_far, mod, w_out_t, w_up_t, w_down_t, *refs = refs
    if not last:
        mod_next, w_q_t, w_v_t, w_k, *refs = refs
    lse, mixed, attended, middle, hidden, slope, branch, *refs = refs
    if last:
        (final,) = refs
    else:
        x_next, xb_next, *next_outs = refs
    patches = x.shape[1]

    def score(pair):
        columns = slice(pair * PAIR, (pair + 1) * PAIR)
        query = side_by_side(q[columns, :])
        return nn(kn_own[:, columns], query), nn(kn_far[:, columns], query)

    ones = jnp.ones((16, BLOCK), BF16)
    following = score(0)
    for pair in range(HEADS // 2):
        both_own, both_far = following
        if pair + 1 < HEADS // 2:
            following = score(pair + 1)
        for side in range(2):
            head = 2 * pair + side
            rows = head_rows(head)
            at = slice(side * patches, (side + 1) * patches)
            scores_own, scores_far = both_own[:, at], both_far[:, at]
            top = jnp.maximum(
                jnp.max(scores_own, axis=0, keepdims=True), jnp.max(scores_far, axis=0, keepdims=True)
            )
            total = None
            for scores, values in ((scores_own, vt_own), (scores_far, vt_far)):
                for key in range(0, patches, BLOCK):
                    probs = jnp.exp(scores[key : key + BLOCK] - top).astype(BF16)
                    value = jnp.concatenate([values[rows, key : key + BLOCK], ones], axis=0)
                    term = nn(value, probs)
                    total = term if total is None else total + term
            weight = total[HEAD_DIM : HEAD_DIM + 1]
            mixed[rows, :] = (total[:HEAD_DIM] * (1.0 / weight)).astype(BF16)
            lse[head : head + 1, :] = top + jnp.log(weight)

    att = nn(w_out_t[...], mixed[...])
    attended[...] = att.astype(BF16)
    mid = x[...] + part(mod, 2, patches) * att
    middle[...] = mid.astype(BF16)
    standard, _ = standardise(mid)
    hidden_in = (standard * (1.0 + part(mod, 4, patches)) + part(mod, 3, patches)).astype(BF16)
    chunks = w_up_t.shape[0] // D

    def up(chunk):
        return nn(w_up_t[chunk * D : (chunk + 1) * D, :], hidden_in)

    following = up(0)
    down = None
    for chunk in range(chunks):
        act = following
        if chunk + 1 < chunks:
            following = up(chunk + 1)
        rows = slice(chunk * D, (chunk + 1) * D)
        squared = act * act
        bent = jnp.tanh(act * (GELU_A + (GELU_A * GELU_B) * squared))
        half = 0.5 + 0.5 * bent
        kept = (act * half).astype(BF16)
        hidden[rows, :] = kept
        curve = (1.0 - bent * bent) * (0.5 * GELU_A + (1.5 * GELU_A * GELU_B) * squared)
        slope[rows, :] = (half + act * curve).astype(BF16)
        term = nn(w_down_t[:, chunk * D : (chunk + 1) * D], kept)
        down = term if down is None else down + term
    branch[...] = down.astype(BF16)
    out = mid + part(mod, 5, patches) * down
    if last:
        own = final.shape[0]
        final[...] = jnp.where(active[0] > 0.0, out[:, :own], x_step[:, :own]).T
    else:
        x_next[...] = out
        xb_next[...] = out.astype(BF16)
        project(out, mod_next, w_q_t, w_v_t, w_k, next_outs)


def put_grads(left_ref, right, where, count, at, mine, other, before):
    rows = [left_ref[pl.ds(pl.multiple_of(where[place] * count, 16), count), :] for place in range(2)]
    product = nt(jnp.concatenate(rows, axis=0), right)
    for column in range(0, product.shape[1], LANES):
        low = product[:count, column : column + LANES]
        high = product[count:, column : column + LANES]
        if before is not None:
            low = low + before[0][at : at + count, :]
            high = high + before[1][at : at + count, :]
        mine[at : at + count, :] = low.astype(mine.dtype)
        other[at : at + count, :] = high.astype(other.dtype)
        at += count


def dense_back_kernel(has_close, has_open, has_before, start, layers, waits, *refs):
    refs = list(refs)

    def take(count):
        taken = refs[:count]
        del refs[:count]
        return taken

    take(waits)
    where, active = take(2)
    close_before = open_before = None
    if has_close:
        d_own, d_got, dq, d_mid_in, x_in, mod_in, w_qkv = take(7)
        w_qkv = w_qkv.at[layers[0]]
        if has_before[0]:
            close_before = take(3)
    if start == "first":
        cots = take(4)
    elif start == "cross":
        cots = take(1)
    if has_open:
        mixed, attended, middle, hidden, slope, branch, mod, w_out, w_up, w_down = take(10)
        w_out, w_up, w_down = (ref.at[layers[1]] for ref in (w_out, w_up, w_down))
        if has_before[1]:
            open_before = take(3)
    else:
        (lines,) = take(1)
    if has_close:
        close_mine, close_other, close_mods = take(3)
    if start == "first":
        (cot_out,) = take(1)
    if has_open:
        open_mine, open_other, open_mods, d_mid_out, do_out, cen_out = take(6)
    else:
        g_out, sums_out = take(2)
        sums_at = close_before[1].shape[0]
    if has_close:
        grads_scr, normed_scr = take(2)
    if has_open:
        bg_scr, pg_scr, hin_scr, ag_scr = take(4)

    patches = middle.shape[1] if has_open else x_in.shape[1]
    totals = {}

    def add_sums(name, values):
        totals[name] = totals[name] + folded(values) if name in totals else folded(values)

    def put_sums(out, before, names):
        for place, name in enumerate(names):
            rows = slice(place * D, (place + 1) * D)
            out[rows, :] = totals[name] + before[2][rows, :] if before else totals[name]

    if start == "first":
        for index, ref in enumerate(cots):
            rows = ref.shape[0]
            cot_out[:, index * rows : (index + 1) * rows] = turned(ref[...])

    def close(at):
        back = None
        standard, scale = standardise(x_in[:, at].astype(F32))
        gain = 1.0 + part(mod_in, 1, patches)
        normed_scr[:, at] = (standard * gain + part(mod_in, 0, patches)).astype(BF16)
        for third in range(3):
            if third == 0:
                piece = dq[:, at]
            else:
                rows = slice((third - 1) * D, third * D)
                piece = (d_own[rows, at] + d_got[rows, at].astype(F32)).astype(BF16)
            grads_scr[third * D : (third + 1) * D, at] = piece
            term = nn(w_qkv[:, third * D : (third + 1) * D], piece)
            back = term if back is None else back + term
        add_sums("shift_a", back)
        add_sums("scale_a", back * standard)
        g = d_mid_in[:, at] + pre_norm_back(standard, scale, back, gain)
        if start == "cross":
            g = g + (1.0 - active[0]) * cots[0][:, at].astype(F32)
        return g

    def dense(at, g):
        standard, scale = standardise(middle[:, at].astype(F32))
        gain = 1.0 + part(mod, 4, patches)
        hin_scr[:, at] = (standard * gain + part(mod, 3, patches)).astype(BF16)
        branch_grad = (part(mod, 5, patches) * g).astype(BF16)
        bg_scr[:, at] = branch_grad
        add_sums("gate_m", g * branch[:, at].astype(F32))
        chunks = w_down.shape[0] // D

        def down(chunk):
            return nn(w_down[chunk * D : (chunk + 1) * D, :], branch_grad)

        following = down(0)
        back = None
        for chunk in range(chunks):
            hidden_grad = following
            if chunk + 1 < chunks:
                following = down(chunk + 1)
            rows = slice(chunk * D, (chunk + 1) * D)
            pre_grad = (slope[rows, at].astype(F32) * hidden_grad).astype(BF16)
            pg_scr[rows, at] = pre_grad
            term = nn(w_up[:, chunk * D : (chunk + 1) * D], pre_grad)
            back = term if back is None else back + term
        add_sums("shift_m", back)
        add_sums("scale_m", back * standard)
        d_mid = g + pre_norm_back(standard, scale, back, gain)
        d_mid_out[:, at] = d_mid
        att_grad = (part(mod, 2, patches) * d_mid).astype(BF16)
        ag_scr[:, at] = att_grad
        mixed_grad = nn(w_out[...], att_grad).astype(BF16)
        do_out[:, at] = mixed_grad
        add_sums("gate_a", d_mid * attended[:, at].astype(F32))
        product = mixed_grad.astype(F32) * mixed[:, at].astype(F32)
        for head in range(HEADS):
            cen_out[head : head + 1, at] = jnp.sum(product[head_rows(head)], axis=0, keepdims=True)

    at = slice(0, patches)
    g = close(at) if has_close else cot_out[:, at].astype(F32) * active[0]
    if has_open:
        dense(at, g)
    else:
        g_out[...] = g[:, : g_out.shape[0]].T
    if has_close:
        put_sums(close_mods, close_before, ("shift_a", "scale_a"))
        put_grads(normed_scr, grads_scr[...], where, D // 8, 0, close_mine, close_other, close_before)
    if has_open:
        put_sums(open_mods, open_before, ("gate_a", "shift_m", "scale_m", "gate_m"))
        count = w_down.shape[0] // 8
        put_grads(hidden, bg_scr[...], where, count, 0, open_mine, open_other, open_before)
        at = count * (D // LANES)
        put_grads(hin_scr, pg_scr[...], where, D // 8, at, open_mine, open_other, open_before)
        at += (w_up.shape[1] // LANES) * (D // 8)
        put_grads(mixed, ag_scr[...], where, D // 8, at, open_mine, open_other, open_before)
    else:
        sums_out[...] = lines[...]
        put_lines(sums_out, 0, close_mods[...])
        close_other[sums_at:, :] = sums_out[...].astype(BF16)


def attend_back_kernel(has_before, waits, q, kn, vt, lse, d_out, centre, *refs):
    if has_before:
        before, *refs = refs
    d_kv, dq_out, kt_scr, vn_scr = refs[waits:]
    for column in range(0, D, LANES):
        kt_scr[column : column + LANES, :] = turned(kn[:, column : column + LANES])
    for column in range(0, vt.shape[1], BLOCK):
        vn_scr[column : column + BLOCK, :] = turned(vt[:, column : column + BLOCK])

    def score(pair):
        columns = slice(pair * PAIR, (pair + 1) * PAIR)
        return nn(kn[:, columns], side_by_side(q[columns, :])), nn(vn_scr[:, columns], side_by_side(d_out[columns, :]))

    queries = q.shape[1]
    following = score(0)
    for pair in range(HEADS // 2):
        both_scores, both_grads = following
        if pair + 1 < HEADS // 2:
            following = score(pair + 1)
        for side in range(2):
            head = 2 * pair + side
            rows = head_rows(head)
            value_rows = slice(D + rows.start, D + rows.stop)
            at = slice(side * queries, (side + 1) * queries)
            probs = jnp.exp(both_scores[:, at] - lse[head : head + 1, :])
            score_grads = (probs * (both_grads[:, at] - centre[head : head + 1, :])).astype(BF16)
            d_kv[value_rows, :] = nt(d_out[rows, :], probs.astype(BF16)).astype(d_kv.dtype)
            d_kv[rows, :] = nt(q[rows, :], score_grads).astype(d_kv.dtype)
            term = nn(kt_scr[rows, :], score_grads)
            if has_before:
                term = (before[rows, :] + term) * HEAD_DIM ** (-0.5)
            dq_out[rows, :] = term.astype(dq_out.dtype)


def split_kernel(waits, where, *refs):
    *halves, keep, sent, total_scr = refs[waits:]
    rows_half = keep.shape[0]
    at = 0
    for mine, other in zip(halves[::2], halves[1::2]):
        rows = mine.shape[0]
        total_scr[at : at + rows, :] = mine[...] + other[...].astype(F32)
        at += rows
    if at < total_scr.shape[0]:
        total_scr[at:, :] = jnp.zeros((total_scr.shape[0] - at, LANES), F32)
    odd = where[3]
    keep[...] = total_scr[pl.ds(pl.multiple_of(odd * rows_half, 16), rows_half), :]
    sent[...] = total_scr[pl.ds(pl.multiple_of((1 - odd) * rows_half, 16), rows_half), :].astype(BF16)


def pair_sum_kernel(late, *refs):
    count = len(refs) // 3
    for keep, got, out in zip(refs[:count], refs[count : 2 * count], refs[2 * count :]):
        out[...] = (keep[...].astype(F32) + got[...].astype(F32)).astype(BF16)


def put_lines(out, row, values):
    ones = jnp.ones((16, LANES), BF16)
    high = values.astype(BF16)
    low = (values - high.astype(F32)).astype(BF16)
    line = (nt(ones, high) + nt(ones, low))[0:1]
    for column in range(0, line.shape[1], LANES):
        out[row : row + 1, :] = line[:, column : column + LANES]
        row += 1
    return row


def lines_kernel(early, context, *refs):
    *sums, out = refs
    out[...] = jnp.zeros_like(out)
    row = 2 * D // LANES
    for ref in sums:
        row = put_lines(out, row, ref[...])
    for column in range(0, D, LANES):
        out[row : row + 1, :] = context[0:1, column : column + LANES].astype(F32)
        row += 1


def join_kernel(sum_count, early, mine, sums, got, out):
    rows = mine.shape[0]
    out[:rows, :] = (mine[...] + got[:rows, :].astype(F32)).astype(BF16)
    other = got[rows:, :].astype(F32)
    summed = lax.broadcasted_iota(jnp.int32, (SUM_ROWS, LANES), 0) < sum_count
    out[rows:, :] = (sums[...] + jnp.where(summed, other, 0.0)).astype(BF16)


def pair_kernel(rows, where, own, got, out):
    out[:rows, :] = (own[:rows, :].astype(F32) + got[:rows, :].astype(F32)).astype(BF16)
    odd = where[3]
    size = SUM_ROWS
    out[pl.ds(pl.multiple_of(rows + odd * size, 16), size), :] = own[rows:, :]
    out[pl.ds(pl.multiple_of(rows + (1 - odd) * size, 16), size), :] = got[rows:, :]


def gather_kernel(where, *refs):
    halves, (out_out, up_out, down_out, qkv_out), scratch = refs[:4], refs[4:8], refs[8:]
    odd = where[3]
    for ref, own, got in zip(scratch, halves[::2], halves[1::2]):
        rows = own.shape[0]
        ref[pl.ds(pl.multiple_of(odd * rows, 16), rows), :] = own[...]
        ref[pl.ds(pl.multiple_of((1 - odd) * rows, 16), rows), :] = got[...]
    slice_rows = out_out.shape[1]
    for index, ref in enumerate(scratch):
        at = 0
        for out in (down_out, up_out, out_out):
            rows = out.shape[1]
            for column in range(0, out.shape[2], LANES):
                out[index, :, column : column + LANES] = ref[at : at + rows, :].astype(F32)
                at += rows
        if index == 0:
            for column in range(0, qkv_out.shape[1], LANES):
                qkv_out[:, column : column + LANES] = ref[at : at + slice_rows, :].astype(F32)
                at += slice_rows


def finish_kernel(item_count, where, own, got, qkv_1, qkv_out, ada_out, bias_out, shift_out, sum_scr, bias_scr, shift_scr):
    layers = 2
    device, high = where[0], where[4]
    slice_rows = qkv_out.shape[1]
    close_rows = slice_rows * (3 * D // LANES)
    for other in range(2):
        rows = slice(close_rows + other * SUM_ROWS, close_rows + (other + 1) * SUM_ROWS)
        sum_scr[2 * high + other] = own[rows, :].astype(F32)
        sum_scr[2 * (1 - high) + other] = got[rows, :].astype(F32)
    qkv_out[1] = qkv_1[...]
    for tile in range(3 * D // LANES):
        rows = slice(tile * slice_rows, (tile + 1) * slice_rows)
        total = own[rows, :].astype(F32) + got[rows, :].astype(F32)
        qkv_out[0, :, tile * LANES : (tile + 1) * LANES] = total
    tiles = 6 * D // LANES
    contexts = []
    for other in range(item_count):
        line = jnp.concatenate([sum_scr[other, layers * tiles + c : layers * tiles + c + 1, :] for c in range(3)], axis=1)
        contexts.append(line)
    square = jnp.concatenate(contexts + [jnp.zeros((8 - item_count, D), F32)], axis=0)
    spot = lax.broadcasted_iota(jnp.int32, (slice_rows, D), 1)
    want = lax.broadcasted_iota(jnp.int32, (slice_rows, D), 0) + device * slice_rows
    pick = jnp.where(spot == want, 1.0, 0.0).astype(BF16)
    columns = nt(pick, square.astype(BF16))
    bias_rows = bias_out.shape[1]
    for index in range(layers):
        flats = []
        for tile in range(tiles):
            row = index * tiles + tile
            total = None
            flat = None
            for other in range(item_count):
                line = sum_scr[other, row : row + 1, :]
                term = columns[:, other : other + 1] * line
                total = term if total is None else total + term
                flat = line if flat is None else flat + line
            ada_out[index, :, tile * LANES : (tile + 1) * LANES] = total
            flats.append(flat)
        flat = jnp.concatenate(flats, axis=1)
        for place in range(flat.shape[1] // bias_rows):
            bias_scr[place, index : index + 1, :] = flat[:, place * bias_rows : (place + 1) * bias_rows]
            at = 3 * D + place * slice_rows
            shift_scr[place, index : index + 1, :] = flat[:, at : at + slice_rows]
    bias_out[...] = bias_scr[device]
    shift_out[...] = shift_scr[device]


VMEM = pl.BlockSpec(memory_space=pltpu.VMEM)
SMEM = pl.BlockSpec(memory_space=pltpu.SMEM)
ANY = pl.BlockSpec(memory_space=pl.ANY)
HBM = pl.BlockSpec(memory_space=pltpu.HBM)


def layer_block(array, index):
    return pl.BlockSpec((None,) + array.shape[1:], lambda step: (index,) + (0,) * (array.ndim - 1))


def call(body, args, outs, scratch=(), flops=0, name=None):
    arrays = [arg[0] if isinstance(arg, tuple) else arg for arg in args]
    specs = [arg[1] if isinstance(arg, tuple) else VMEM for arg in args]
    return pl.pallas_call(
        body,
        out_shape=[jax.ShapeDtypeStruct(shape, kind) for shape, kind in outs],
        in_specs=specs,
        out_specs=[VMEM] * len(outs),
        scratch_shapes=[one if not isinstance(one, tuple) else pltpu.VMEM(*one) for one in scratch],
        compiler_params=pltpu.CompilerParams(vmem_limit_bytes=VMEM_LIMIT),
        cost_estimate=pl.CostEstimate(flops=flops, bytes_accessed=0, transcendentals=0),
        name=name,
    )(*arrays)


VMEM_LIMIT = 16 * 1024 * 1024


def fast_shards(
    lat_count, lon_count, item_count,
    fields, lead_index, rollout, w_qkv, w_out, w_up, w_down, w_ada, b_ada, cotangent,
):
    _, rows_dev, cols_dev, width = fields.shape
    local = rows_dev * cols_dev
    layers = w_qkv.shape[0]
    ff = w_up.shape[2]
    patches = 4 * local
    device = lax.axis_index("lat") * lon_count + lax.axis_index("lon")
    item = lax.axis_index("item")
    where = jnp.stack([device, device ^ 1, item, item & 1, item >> 1]).astype(jnp.int32)
    active = (1 < rollout[0]).astype(F32)[None]

    def plane_flip(value, flip_lat, flip_y):
        pairs = [
            (a * lon_count + b, (a ^ flip_lat) * lon_count + (b ^ (2 * flip_y)))
            for a in range(lat_count)
            for b in range(lon_count)
        ]
        return lax.ppermute(value, ("lat", "lon"), pairs)

    def swap(value):
        return lax.ppermute(value, "lon", [(index, index ^ 1) for index in range(lon_count)])

    def with_item(value, flip):
        return lax.ppermute(value, "item", [(index, index ^ flip) for index in range(item_count)])

    def plane_parts(value):
        return [value, plane_flip(value, 1, 0), plane_flip(value, 0, 1), plane_flip(value, 1, 1)]

    field_parts = plane_parts(fields.reshape(local, width))
    cot_parts = plane_parts(cotangent.reshape(local, width))

    context = jax.nn.silu(embedding(lead_index[0])).astype(BF16)
    context = jnp.broadcast_to(context[None, :], (16, width))
    square = (width, patches)
    natural = (patches, width)
    fetched = [(pltpu.with_memory_space_constraint(value, pltpu.HBM), HBM) for value in (w_ada, b_ada, w_qkv)]
    fetch_scratch = [((width, 3 * width), BF16), ((width, 6 * width), BF16), (b_ada.shape, F32)]
    fetch_scratch.append(pltpu.SemaphoreType.DMA((3,)))
    first_outs = [((6 * width, LANES), F32)] + [((width, width), BF16)] * 3
    rest_outs = [((width, width), BF16), ((ff, width), BF16), ((width, ff), BF16)]
    first_0 = call(
        functools.partial(prepare_first_kernel, 0, None, 2),
        [context, *fetched, (where, SMEM), (active, SMEM)],
        first_outs,
        fetch_scratch,
        name="prepare_first",
    )
    both = call(
        prepare_both_kernel,
        [context, *fetched, w_out, w_up, w_down],
        first_outs + rest_outs,
        fetch_scratch,
        name="prepare_both",
    )
    rest_1 = call(
        functools.partial(prepare_rest_kernel, 1), [w_out, w_up, w_down], rest_outs, name="prepare_rest"
    )
    first_parts = [first_0, both[:4]]
    rest_parts = [both[4:], rest_1]
    mods = [one[0] for one in first_parts]

    project_outs = [(square, F32), (square, BF16), (square, BF16), (natural, BF16), (square, BF16)]
    dense_flops = 2 * patches * (width * 3 * width + width * width + 2 * width * ff)
    score_flops = 2 * patches * 2 * patches * width * 4
    x, xb, *projected = call(
        first_kernel,
        [*field_parts, *first_parts[0]],
        project_outs,
        flops=2 * patches * width * 4 * width,
        name="first",
    )
    saved = []
    for step in range(STEPS):
        for index in range(layers):
            q, kn, vt = projected
            kn_far, vt_far = swap(kn), swap(vt)
            last = step == STEPS - 1 and index == layers - 1
            if index == 0 and step > 0:
                x_step = x
            following = list(first_parts[(index + 1) % layers])
            lse, mixed, attended, middle, hidden, slope, branch, *results = call(
                functools.partial(forward_kernel, last),
                ([(active, SMEM), x, x_step] if last else [x])
                + [q, kn, kn_far, vt, vt_far, mods[index], *rest_parts[index]]
                + ([] if last else following),
                [
                    ((HEADS, patches), F32),
                    (square, BF16),
                    (square, BF16),
                    (square, BF16),
                    ((ff, patches), BF16),
                    ((ff, patches), BF16),
                    (square, BF16),
                ]
                + ([((local, width), F32)] if last else project_outs),
                flops=dense_flops + 2 * score_flops,
                name="forward",
            )
            saved.append((xb, [mixed, attended, middle, hidden, slope, branch], (q, kn, kn_far, vt, vt_far, lse)))
            if last:
                final = results[0]
            else:
                x, xb, *projected = results

    slice_rows = width // 8
    open_rows = 2 * (ff // 8) * (width // LANES) + slice_rows * (width // LANES)
    close_rows = slice_rows * (3 * width // LANES)
    order = [(step, index) for step in reversed(range(STEPS)) for index in reversed(range(layers))]
    open_done = [None] * layers
    close_done = [None] * layers
    pending = None
    for place in range(len(order) + 1):
        has_close = pending is not None
        has_open = place < len(order)
        use = [order[place - 1][1], order[place][1] if has_open else 0]
        waits = []
        if has_close and close_done[use[0]]:
            waits = [pair_1] if has_open else [item_got_1]
        args = [(value, ANY) for value in waits] + [(where, SMEM), (active, SMEM)]
        outs = []
        scratch = []
        has_before = [False, False]
        start = ""
        if has_close:
            args += pending
            if close_done[use[0]] is not None:
                has_before[0] = True
                args += close_done[use[0]]
            outs += [((close_rows, LANES), F32)]
            sent_rows = close_rows + (0 if has_open else SUM_ROWS)
            outs += [((sent_rows, LANES), BF16 if has_before[0] else F32), ((2 * width, LANES), F32)]
            scratch += [((3 * width, patches), BF16), (square, BF16)]
        if place == 0:
            start = "first"
            args += cot_parts
            outs += [(square, BF16)]
        elif has_open and order[place][0] != order[place - 1][0]:
            start = "cross"
            args += [cot_t]
        if has_open:
            step, index = order[place]
            xb, kept, heads = saved[step * layers + index]
            args += kept + [mods[index], w_out, w_up, w_down]
            if open_done[index] is not None:
                has_before[1] = True
                args += open_done[index]
            outs += [
                ((open_rows, LANES), F32),
                ((open_rows, LANES), BF16 if has_before[1] else F32),
                ((4 * width, LANES), F32),
                (square, F32),
                (square, BF16),
                ((HEADS, patches), F32),
            ]
            scratch += [(square, BF16), ((ff, patches), BF16), (square, BF16), (square, BF16)]
        else:
            args += [lines]
            outs += [((local, width), F32), ((SUM_ROWS, LANES), F32)]
        results = list(
            call(
                functools.partial(dense_back_kernel, has_close, has_open, has_before, start, use, len(waits)),
                args,
                outs,
                scratch,
                flops=2 * dense_flops if has_open else 0,
                name="dense_back" if has_open else "close_back",
            )
        )
        if has_close:
            close_done[use[0]] = results[:3]
            del results[:3]
        if start == "first":
            cot_t = results.pop(0)
        if not has_open:
            gradient, line = results
            break
        open_done[index] = results[:3]
        d_mid, d_out, centre = results[3:]
        q, kn, kn_far, vt, vt_far, lse = heads
        halves = [open_done[index][0], open_done[index][1]]
        if index == 0:
            halves += [close_done[1][0], close_done[1][1]]
        half_rows = -(-sum(half.shape[0] for half in halves[::2]) // 32) * 16

        def split(waits):
            pieces = [half if place % 2 == 0 else swap(half) for place, half in enumerate(halves)]
            return call(
                functools.partial(split_kernel, len(waits)),
                [(where, SMEM), *waits, *pieces],
                [((half_rows, LANES), F32), ((half_rows, LANES), BF16)],
                [((2 * half_rows, LANES), F32)],
                name="split",
            )

        def pair_sum(late, keeps, gots):
            outs = [(keep.shape, BF16) for keep in keeps]
            return call(pair_sum_kernel, [(late, ANY), *keeps, *gots], outs, name="pair_sum")

        waits = []
        if has_before[1] and index == 0:
            pair_got_1 = with_item(pair_1, 2)
            lines = call(
                lines_kernel,
                [(pair_got_1, ANY), context, open_done[0][2], close_done[1][2], open_done[1][2]],
                [((SUM_ROWS, LANES), F32)],
                flops=10 * score_flops,
                name="lines",
            )[0]
            keep, sent = split([(lines, ANY)])
            got_0 = with_item(sent, 1)
            waits = [keep]
        d_far, dq = call(
            functools.partial(attend_back_kernel, False, len(waits)),
            [q, kn_far, vt_far, lse, d_out, centre] + [(value, ANY) for value in waits],
            [((2 * width, patches), BF16), (square, F32)],
            [(square, BF16), (natural, BF16)],
            flops=10 * score_flops,
            name="attend_far",
        )
        d_got = swap(d_far)
        waits = []
        if has_before[1]:
            if index == 1:
                keep, sent = split([(d_far, ANY)])
                got_1 = with_item(sent, 1)
                waits = [keep]
            else:
                pair_0, item_1 = pair_sum(d_far, [keep, pair_1], [got_0, pair_got_1])
                item_got_1 = with_item(item_1, 1)
                pair_got_0 = with_item(pair_0, 2)
                waits = [pair_0]
        d_own, dq = call(
            functools.partial(attend_back_kernel, True, len(waits)),
            [q, kn, vt, lse, d_out, centre, dq] + [(value, ANY) for value in waits],
            [((2 * width, patches), F32), (square, BF16)],
            [(square, BF16), (natural, BF16)],
            flops=10 * score_flops,
            name="attend_own",
        )
        if has_before[1] and index == 1:
            (pair_1,) = pair_sum(dq, [keep], [got_1])
        pending = [d_own, d_got, dq, d_mid, xb, mods[index], w_qkv]

    message = call(
        functools.partial(join_kernel, layers * 6 * width // LANES),
        [(pair_got_0, ANY), close_done[0][0], line, swap(close_done[0][1])],
        [((close_rows + SUM_ROWS, LANES), BF16)],
        name="join",
    )[0]
    message_got = with_item(message, 1)
    (item_0,) = pair_sum(message_got, [pair_0], [pair_got_0])
    message = call(
        functools.partial(pair_kernel, close_rows),
        [(where, SMEM), message, message_got],
        [((close_rows + 2 * SUM_ROWS, LANES), BF16)],
        name="pair",
    )[0]
    out_grad, up_grad, down_grad, qkv_1 = call(
        gather_kernel,
        [(where, SMEM), item_0, with_item(item_0, 1), item_1, item_got_1],
        [
            ((layers, slice_rows, width), F32),
            ((layers, slice_rows, ff), F32),
            ((layers, ff // 8, width), F32),
            ((slice_rows, 3 * width), F32),
        ],
        [((2 * pair.shape[0], LANES), BF16) for pair in (pair_0, pair_1)],
        name="gather",
    )
    bias_rows = 6 * width // 8
    qkv_grad, ada_grad, bias_grad, shift_grad = call(
        functools.partial(finish_kernel, item_count),
        [(where, SMEM), message, with_item(message, 2), qkv_1],
        [
            ((layers, slice_rows, 3 * width), F32),
            ((layers, slice_rows, 6 * width), F32),
            ((layers, bias_rows), F32),
            ((layers, slice_rows), F32),
        ],
        [
            ((item_count, SUM_ROWS, LANES), F32),
            ((8, layers, bias_rows), F32),
            ((8, layers, slice_rows), F32),
        ],
        name="finish",
    )
    field_shape = (1, rows_dev, cols_dev, width)
    return (
        final.reshape(field_shape),
        gradient.reshape(field_shape),
        qkv_grad,
        out_grad,
        up_grad,
        down_grad,
        ada_grad,
        bias_grad,
        shift_grad,
    )


def solution(mesh):
    lat_count, lon_count, item_count = mesh.shape["lat"], mesh.shape["lon"], mesh.shape["item"]
    if lat_count == 2 and lon_count == 4:
        body = functools.partial(fast_shards, lat_count, lon_count, item_count)
    else:
        body = shards
    return jax.shard_map(
        body,
        mesh=mesh,
        in_specs=(
            P("item", "lat", "lon", None),
            P("item"),
            P("item"),
            P(),
            P(),
            P(),
            P(),
            P(),
            P(),
            P("item", "lat", "lon", None),
        ),
        out_specs=(
            P("item", "lat", "lon", None),
            P("item", "lat", "lon", None),
            P(None, ("lat", "lon"), None),
            P(None, ("lat", "lon"), None),
            P(None, ("lat", "lon"), None),
            P(None, ("lat", "lon"), None),
            P(None, ("lat", "lon"), None),
            P(None, ("lat", "lon")),
            P(None, ("lat", "lon")),
        ),
        check_vma=False,
    )
```

```python
import functools
import math

import jax
import jax.numpy as jnp
from jax import lax
from jax.experimental import pallas as pl
from jax.experimental.pallas import tpu as pltpu
from jax.sharding import PartitionSpec as P

D = 384
HEADS = 6
HEAD_DIM = 64
STEPS = 2


def shortened(shard):
    return jax.tree.map(lambda a: a.astype(jnp.bfloat16) if a.dtype == jnp.float32 else a, shard)


def embedding(lead):
    half_width = D // 2
    lead_hours = 6.0 * (lead.astype(jnp.float32) + 1.0)
    frequencies = jnp.exp(
        -math.log(10000.0) * jnp.arange(half_width, dtype=jnp.float32) / half_width
    )
    angles = lead_hours * frequencies
    return jnp.concatenate([jnp.sin(angles), jnp.cos(angles)])


def pre_norm(values, shift_part, scale_part):
    centred = values - jnp.mean(values, axis=-1, keepdims=True)
    variance = jnp.mean(centred * centred, axis=-1, keepdims=True)
    return centred * lax.rsqrt(variance + 1e-06) * (1.0 + scale_part) + shift_part


def gather_keys(keys_values):
    band_rows = lax.all_gather(keys_values, "lon", axis=0, tiled=True)
    return lax.all_gather(band_rows, "lat", axis=0, tiled=True)


def spread_keys(key_value_grads):
    band_grads = lax.psum_scatter(
        key_value_grads.astype(jnp.bfloat16), "lat", scatter_dimension=0, tiled=True
    )
    return lax.psum_scatter(band_grads, "lon", scatter_dimension=0, tiled=True).astype(jnp.float32)


def forward_layer(current, modulation, weight_qkv, weight_out, weight_up, weight_down):
    local_rows, width = current.shape
    shift_attn, scale_attn, gate_attn, shift_mlp, scale_mlp, gate_mlp = modulation
    normed = pre_norm(current, shift_attn, scale_attn).astype(jnp.bfloat16)
    projected = jnp.dot(normed, weight_qkv, preferred_element_type=jnp.float32).astype(jnp.bfloat16)
    queries = projected[:, :width].reshape(local_rows, HEADS, HEAD_DIM)
    own_keys = projected[:, width:]
    gathered = gather_keys(own_keys)
    total_rows = gathered.shape[0]
    key_heads = gathered[:, :width].reshape(total_rows, HEADS, HEAD_DIM)
    value_heads = gathered[:, width:].reshape(total_rows, HEADS, HEAD_DIM)
    scores = jnp.einsum(
        "thd,nhd->htn", queries, key_heads, preferred_element_type=jnp.float32
    ) * HEAD_DIM ** (-0.5)
    log_total = jax.nn.logsumexp(scores, axis=-1, keepdims=True)
    probabilities = jnp.exp(scores - log_total).astype(jnp.bfloat16)
    mixed = jnp.einsum(
        "htn,nhd->thd", probabilities, value_heads, preferred_element_type=jnp.float32
    )
    mixed = mixed.reshape(local_rows, width).astype(jnp.bfloat16)
    attended = jnp.dot(mixed, weight_out, preferred_element_type=jnp.float32)
    middle = current + gate_attn * attended
    hidden_in = pre_norm(middle, shift_mlp, scale_mlp).astype(jnp.bfloat16)
    pre_act = jnp.dot(hidden_in, weight_up, preferred_element_type=jnp.float32)
    hidden = jax.nn.gelu(pre_act).astype(jnp.bfloat16)
    branch = jnp.dot(hidden, weight_down, preferred_element_type=jnp.float32)
    output = middle + gate_mlp * branch
    kept = (
        current,
        normed,
        queries,
        gathered,
        own_keys,
        log_total,
        mixed,
        attended,
        middle,
        hidden_in,
        pre_act,
        hidden,
        branch,
    )
    return (output, kept)


def backward_layer(grad_out, kept, modulation, weight_qkv, weight_out, weight_up, weight_down):
    (
        current,
        normed,
        queries,
        gathered,
        own_keys,
        log_total,
        mixed,
        attended,
        middle,
        hidden_in,
        pre_act,
        hidden,
        branch,
    ) = kept
    local_rows, width = current.shape
    total_rows = gathered.shape[0]
    shift_attn, scale_attn, gate_attn, shift_mlp, scale_mlp, gate_mlp = modulation
    factor = HEAD_DIM ** (-0.5)
    branch_grad = (gate_mlp * grad_out).astype(jnp.bfloat16)
    gate_mlp_grad = jnp.sum(grad_out * branch, axis=0)
    hidden_grad = jnp.dot(branch_grad, weight_down.T, preferred_element_type=jnp.float32)
    down_grad = jnp.dot(hidden.T, branch_grad, preferred_element_type=jnp.float32)
    _, gelu_back = jax.vjp(jax.nn.gelu, pre_act)
    pre_grad = gelu_back(hidden_grad)[0].astype(jnp.bfloat16)
    hidden_in_grad = jnp.dot(pre_grad, weight_up.T, preferred_element_type=jnp.float32)
    up_grad = jnp.dot(hidden_in.T, pre_grad, preferred_element_type=jnp.float32)
    _, second_back = jax.vjp(pre_norm, middle, shift_mlp, scale_mlp)
    middle_part, shift_mlp_grad, scale_mlp_grad = second_back(hidden_in_grad)
    middle_grad = grad_out + middle_part
    attended_grad = (gate_attn * middle_grad).astype(jnp.bfloat16)
    gate_attn_grad = jnp.sum(middle_grad * attended, axis=0)
    mixed_grad = jnp.dot(attended_grad, weight_out.T, preferred_element_type=jnp.float32).astype(
        jnp.bfloat16
    )
    out_grad = jnp.dot(mixed.T, attended_grad, preferred_element_type=jnp.float32)
    mixed_heads = mixed_grad.reshape(local_rows, HEADS, HEAD_DIM)
    key_heads = gathered[:, :width].reshape(total_rows, HEADS, HEAD_DIM)
    value_heads = gathered[:, width:].reshape(total_rows, HEADS, HEAD_DIM)
    scores = (
        jnp.einsum("thd,nhd->htn", queries, key_heads, preferred_element_type=jnp.float32) * factor
    )
    probabilities = jnp.exp(scores - log_total)
    prob_grads = jnp.einsum(
        "thd,nhd->htn", mixed_heads, value_heads, preferred_element_type=jnp.float32
    )
    centre = jnp.sum(prob_grads * probabilities, axis=-1, keepdims=True)
    score_grads = (probabilities * (prob_grads - centre)).astype(jnp.bfloat16)
    query_grads = (
        jnp.einsum("htn,nhd->thd", score_grads, key_heads, preferred_element_type=jnp.float32)
        * factor
    )
    value_grads = jnp.einsum(
        "htn,thd->nhd",
        probabilities.astype(jnp.bfloat16),
        mixed_heads,
        preferred_element_type=jnp.float32,
    )
    key_grads = (
        jnp.einsum("htn,thd->nhd", score_grads, queries, preferred_element_type=jnp.float32)
        * factor
    )
    key_value_grads = jnp.concatenate(
        [key_grads.reshape(total_rows, width), value_grads.reshape(total_rows, width)], axis=1
    )
    local_grads = spread_keys(key_value_grads)
    projected_grad = jnp.concatenate(
        [query_grads.reshape(local_rows, width), local_grads], axis=1
    ).astype(jnp.bfloat16)
    normed_grad = jnp.dot(projected_grad, weight_qkv.T, preferred_element_type=jnp.float32)
    qkv_grad = jnp.dot(normed.T, projected_grad, preferred_element_type=jnp.float32)
    _, first_back = jax.vjp(pre_norm, current, shift_attn, scale_attn)
    current_part, shift_attn_grad, scale_attn_grad = first_back(normed_grad)
    input_grad = middle_grad + current_part
    modulation_grad = jnp.concatenate(
        [
            shift_attn_grad,
            scale_attn_grad,
            gate_attn_grad,
            shift_mlp_grad,
            scale_mlp_grad,
            gate_mlp_grad,
        ]
    )
    return (input_grad, (qkv_grad, out_grad, up_grad, down_grad, modulation_grad))


def shards(fields, lead_index, rollout, w_qkv, w_out, w_up, w_down, w_ada, b_ada, cotangent):
    _, rows_dev, cols_dev, width = fields.shape
    local_rows = rows_dev * cols_dev
    layer_count = w_qkv.shape[0]
    context = jax.nn.silu(embedding(lead_index[0])).astype(jnp.bfloat16)
    context_wide = context.astype(jnp.float32)
    modulations = [
        (
            jnp.dot(context[None, :], w_ada[index], preferred_element_type=jnp.float32)[0]
            + b_ada[index]
        ).reshape(6, width)
        for index in range(layer_count)
    ]
    weight_sets = [
        (w_qkv[index], w_out[index], w_up[index], w_down[index]) for index in range(layer_count)
    ]
    count = rollout[0]
    current = fields.reshape(local_rows, width).astype(jnp.float32)
    saved = []
    for rollout_step in range(STEPS):
        updated = current
        kept_layers = []
        for index in range(layer_count):
            updated, kept = forward_layer(updated, modulations[index], *weight_sets[index])
            kept_layers.append(kept)
        current = jnp.where(rollout_step < count, updated, current)
        saved.append(kept_layers)
    gradient = cotangent.reshape(local_rows, width).astype(jnp.float32)
    summed = None
    shares = None
    for rollout_step in reversed(range(STEPS)):
        active = (rollout_step < count).astype(jnp.float32)
        inner = gradient * active
        layer_terms = [None] * layer_count
        for index in reversed(range(layer_count)):
            inner, layer_terms[index] = backward_layer(
                inner, saved[rollout_step][index], modulations[index], *weight_sets[index]
            )
        gradient = inner + (1.0 - active) * gradient
        modulation_grads = jnp.stack([terms[4] for terms in layer_terms])
        step_terms = (
            jnp.stack([terms[0] for terms in layer_terms]),
            jnp.stack([terms[1] for terms in layer_terms]),
            jnp.stack([terms[2] for terms in layer_terms]),
            jnp.stack([terms[3] for terms in layer_terms]),
            context_wide[None, :, None] * modulation_grads[:, None, :],
            modulation_grads,
            modulation_grads[:, 3 * width : 4 * width],
        )
        summed = step_terms if summed is None else jax.tree.map(jnp.add, summed, step_terms)
    shares = lax.psum_scatter(summed, ("lat", "lon"), scatter_dimension=1, tiled=True)
    totals = jax.tree.map(
        lambda part: part.astype(jnp.float32), lax.psum(shortened(shares), "item")
    )
    return (
        current.reshape(1, rows_dev, cols_dev, width),
        gradient.reshape(1, rows_dev, cols_dev, width),
        totals[0],
        totals[1],
        totals[2],
        totals[3],
        totals[4],
        totals[5],
        totals[6],
    )


F32 = jnp.float32
BF16 = jnp.bfloat16
GELU_A = math.sqrt(2.0 / math.pi)
GELU_B = 0.044715
LANES = 128
BLOCK = 256
PAIR = 2 * HEAD_DIM
SUM_ROWS = 48


def nn(left, right, precision=None):
    return lax.dot_general(
        left, right, (((1,), (0,)), ((), ())), preferred_element_type=F32, precision=precision
    )


def nt(left, right, precision=None):
    return lax.dot_general(
        left, right, (((1,), (1,)), ((), ())), preferred_element_type=F32, precision=precision
    )


def identity(size):
    rows = lax.broadcasted_iota(jnp.int32, (size, size), 0)
    columns = lax.broadcasted_iota(jnp.int32, (size, size), 1)
    return jnp.where(rows == columns, 1.0, 0.0).astype(BF16)


def turned(values):
    return nt(identity(values.shape[1]), values).astype(BF16)


def wide(column_tile, lanes):
    return jnp.concatenate([column_tile] * (lanes // LANES), axis=1)


def folded(values):
    pieces = [values[:, at : at + LANES] for at in range(0, values.shape[1], LANES)]
    return sum(pieces[1:], pieces[0])


def standardise(values):
    rows = values.shape[0]
    centred = values - jnp.sum(values, axis=0, keepdims=True) * (1.0 / rows)
    variance = jnp.sum(centred * centred, axis=0, keepdims=True) * (1.0 / rows)
    scale = lax.rsqrt(variance + 1e-06)
    return centred * scale, scale


def pre_norm_back(standard, scale, grad, gain):
    rows = standard.shape[0]
    inner = grad * gain
    first = jnp.sum(inner, axis=0, keepdims=True) * (1.0 / rows)
    second = jnp.sum(inner * standard, axis=0, keepdims=True) * (1.0 / rows)
    return scale * (inner - first - standard * second)


def part(mod_ref, index, lanes):
    return wide(mod_ref[index * D : (index + 1) * D, :], lanes)


def turn_into(source, out, at=0):
    for column in range(0, out.shape[0], BLOCK):
        width = min(BLOCK, out.shape[0] - column)
        out[column : column + width, :] = turned(source[:, at + column : at + column + width])


def prepare_first_kernel(index, between, waits, context, w_ada, b_ada, w_qkv, *refs):
    mod, w_q_t, w_v_t, w_k, *scratch, sems = refs[waits:]
    copies = [
        pltpu.make_async_copy(source, target, sems.at[place])
        for place, (source, target) in enumerate(zip((w_qkv.at[index], w_ada.at[index], b_ada), scratch))
    ]
    for copy in copies:
        copy.start()
    if between:
        between()
    w_qkv, w_ada, b_ada = scratch
    copies[0].wait()
    w_k[...] = w_qkv[:, D : 2 * D]
    turn_into(w_qkv, w_q_t)
    turn_into(w_qkv, w_v_t, 2 * D)
    copies[1].wait()
    copies[2].wait()
    values = nn(context[...], w_ada[...])[0:1] + b_ada[index : index + 1, :]
    for column in range(0, values.shape[1], LANES):
        tile = jnp.broadcast_to(values[:, column : column + LANES], (LANES, LANES))
        mod[column : column + LANES, :] = tile.T


def prepare_rest_kernel(index, w_out, w_up, w_down, *outs):
    for weight, out in zip((w_out, w_up, w_down), outs):
        turn_into(weight.at[index], out)


def prepare_both_kernel(context, w_ada, b_ada, w_qkv, w_out, w_up, w_down, *refs):
    between = functools.partial(prepare_rest_kernel, 0, w_out, w_up, w_down, *refs[4:7])
    prepare_first_kernel(1, between, 0, context, w_ada, b_ada, w_qkv, *refs[:4], *refs[7:])


def project(x, mod_ref, w_q_t, w_v_t, w_k, outs):
    q_out, kn_out, vt_out = outs
    lanes = x.shape[1]
    standard, _ = standardise(x)
    normed = (standard * (1.0 + part(mod_ref, 1, lanes)) + part(mod_ref, 0, lanes)).astype(BF16)
    vt_out[...] = nn(w_v_t[...], normed).astype(BF16)
    q_out[...] = (nn(w_q_t[...], normed) * HEAD_DIM ** (-0.5)).astype(BF16)
    for at in range(0, lanes, BLOCK):
        kn_out[at : at + BLOCK, :] = nn(turned(normed[:, at : at + BLOCK]), w_k[...]).astype(BF16)


def first_kernel(own, flip_x, flip_y, flip_xy, mod, w_q_t, w_v_t, w_k, x_out, xb_out, *outs):
    for index, ref in enumerate((own, flip_x, flip_y, flip_xy)):
        rows = ref.shape[0]
        flat = turned(ref[...])
        xb_out[:, index * rows : (index + 1) * rows] = flat
        x_out[:, index * rows : (index + 1) * rows] = flat.astype(F32)
    project(x_out[...], mod, w_q_t, w_v_t, w_k, outs)


def head_rows(head):
    return slice(head * HEAD_DIM, (head + 1) * HEAD_DIM)


def pair_columns(head):
    return slice(head // 2 * PAIR, (head // 2 + 1) * PAIR)


def padded(rows, head):
    zeros = jnp.zeros_like(rows)
    return jnp.concatenate([rows, zeros] if head % 2 == 0 else [zeros, rows], axis=0)


def forward_kernel(last, *refs):
    if last:
        active, x, x_step, *refs = refs
    else:
        x, *refs = refs
    q, kn_own, kn_far, vt_own, vt_far, mod, w_out_t, w_up_t, w_down_t, *refs = refs
    if not last:
        mod_next, w_q_t, w_v_t, w_k, *refs = refs
    lse, mixed, attended, middle, hidden, slope, branch, *refs = refs
    if last:
        (final,) = refs
    else:
        x_next, xb_next, *next_outs = refs
    patches = x.shape[1]

    keys = [(kn, vt, slice(at, at + BLOCK)) for kn, vt in ((kn_own, vt_own), (kn_far, vt_far)) for at in range(0, patches, BLOCK)]
    ones = jnp.ones((16, BLOCK), BF16)
    queries = [padded(q[head_rows(head), :], head) for head in range(HEADS)]

    def score(head, step):
        kn, _, at = keys[step]
        scores = nn(kn[at, pair_columns(head)], queries[head])
        return scores, jnp.max(scores, axis=0, keepdims=True)

    def value(head, step, probs):
        _, vt, at = keys[step]
        return nn(jnp.concatenate([vt[head_rows(head), at], ones], axis=0), probs)

    current = [score(0, step) for step in range(len(keys))]
    for head in range(HEADS):
        top = functools.reduce(jnp.maximum, [highest for _, highest in current])
        following = []
        total = None
        waiting = None
        for step in range(len(keys)):
            if head + 1 < HEADS:
                following.append(score(head + 1, step))
            probs = jnp.exp(current[step][0] - top).astype(BF16)
            if waiting is not None:
                term = value(head, step - 1, waiting)
                total = term if total is None else total + term
            waiting = probs
        total = total + value(head, len(keys) - 1, waiting)
        weight = total[HEAD_DIM : HEAD_DIM + 1]
        mixed[head_rows(head), :] = (total[:HEAD_DIM] * (1.0 / weight)).astype(BF16)
        lse[head : head + 1, :] = top + jnp.log(weight)
        current = following

    att = nn(w_out_t[...], mixed[...])
    attended[...] = att.astype(BF16)
    mid = x[...] + part(mod, 2, patches) * att
    middle[...] = mid.astype(BF16)
    standard, _ = standardise(mid)
    hidden_in = (standard * (1.0 + part(mod, 4, patches)) + part(mod, 3, patches)).astype(BF16)
    chunks = [slice(at, at + BLOCK) for at in range(0, w_up_t.shape[0], BLOCK)]
    down = None
    waiting = None
    following = nn(w_up_t[chunks[0], :], hidden_in)
    for place, rows in enumerate(chunks):
        act = following
        if place + 1 < len(chunks):
            following = nn(w_up_t[chunks[place + 1], :], hidden_in)
        if place > 0:
            term = nn(w_down_t[:, chunks[place - 1]], waiting)
            down = term if down is None else down + term
        squared = act * act
        bent = jnp.tanh(act * (GELU_A + (GELU_A * GELU_B) * squared))
        half = 0.5 + 0.5 * bent
        waiting = (act * half).astype(BF16)
        hidden[rows, :] = waiting
        curve = (1.0 - bent * bent) * (0.5 * GELU_A + (1.5 * GELU_A * GELU_B) * squared)
        slope[rows, :] = (half + act * curve).astype(BF16)
    down = down + nn(w_down_t[:, chunks[-1]], waiting)
    branch[...] = down.astype(BF16)
    out = mid + part(mod, 5, patches) * down
    if last:
        own = final.shape[0]
        final[...] = jnp.where(active[0] > 0.0, out[:, :own], x_step[:, :own]).T
    else:
        x_next[...] = out
        xb_next[...] = out.astype(BF16)
        project(out, mod_next, w_q_t, w_v_t, w_k, next_outs)


def put_grads(left_ref, right, where, count, at, mine, other, before):
    rows = [left_ref[pl.ds(pl.multiple_of(where[place] * count, 16), count), :] for place in range(2)]
    product = nt(jnp.concatenate(rows, axis=0), right)
    for column in range(0, product.shape[1], LANES):
        low = product[:count, column : column + LANES]
        high = product[count:, column : column + LANES]
        if before is not None:
            low = low + before[0][at : at + count, :]
            high = high + before[1][at : at + count, :]
        mine[at : at + count, :] = low.astype(mine.dtype)
        other[at : at + count, :] = high.astype(other.dtype)
        at += count


def dense_back_kernel(has_close, has_open, has_before, start, layers, waits, *refs):
    refs = list(refs)

    def take(count):
        taken = refs[:count]
        del refs[:count]
        return taken

    take(waits)
    where, active = take(2)
    close_before = open_before = None
    if has_close:
        d_own, d_got, dq, d_mid_in, x_in, mod_in, w_qkv = take(7)
        w_qkv = w_qkv.at[layers[0]]
        if has_before[0]:
            close_before = take(3)
    if start == "first":
        cots = take(4)
    elif start == "cross":
        cots = take(1)
    if has_open:
        mixed, attended, middle, hidden, slope, branch, mod, w_out, w_up, w_down = take(10)
        w_out, w_up, w_down = (ref.at[layers[1]] for ref in (w_out, w_up, w_down))
        if has_before[1]:
            open_before = take(3)
    else:
        (lines,) = take(1)
    if has_close:
        close_mine, close_other, close_mods = take(3)
    if start == "first":
        (cot_out,) = take(1)
    if has_open:
        open_mine, open_other, open_mods, d_mid_out, do_out, cen_out = take(6)
    else:
        g_out, sums_out = take(2)
        sums_at = close_before[1].shape[0]
    if has_close:
        grads_scr, normed_scr = take(2)
    if has_open:
        bg_scr, pg_scr, hin_scr, ag_scr = take(4)

    patches = middle.shape[1] if has_open else x_in.shape[1]
    totals = {}

    def add_sums(name, values):
        totals[name] = totals[name] + folded(values) if name in totals else folded(values)

    def put_sums(out, before, names):
        for place, name in enumerate(names):
            rows = slice(place * D, (place + 1) * D)
            out[rows, :] = totals[name] + before[2][rows, :] if before else totals[name]

    if start == "first":
        for index, ref in enumerate(cots):
            rows = ref.shape[0]
            cot_out[:, index * rows : (index + 1) * rows] = turned(ref[...])

    def close(at):
        standard, scale = standardise(x_in[:, at].astype(F32))
        gain = 1.0 + part(mod_in, 1, patches)
        normed_scr[:, at] = (standard * gain + part(mod_in, 0, patches)).astype(BF16)
        for third in range(3):
            if third == 0:
                piece = dq[:, at]
            else:
                rows = slice((third - 1) * D, third * D)
                piece = (d_own[rows, at] + d_got[rows, at].astype(F32)).astype(BF16)
            grads_scr[third * D : (third + 1) * D, at] = piece
        back = nn(w_qkv[...], grads_scr[:, at])
        add_sums("shift_a", back)
        add_sums("scale_a", back * standard)
        g = d_mid_in[:, at] + pre_norm_back(standard, scale, back, gain)
        if start == "cross":
            g = g + (1.0 - active[0]) * cots[0][:, at].astype(F32)
        return g

    def dense(at, g):
        standard, scale = standardise(middle[:, at].astype(F32))
        gain = 1.0 + part(mod, 4, patches)
        hin_scr[:, at] = (standard * gain + part(mod, 3, patches)).astype(BF16)
        branch_grad = (part(mod, 5, patches) * g).astype(BF16)
        bg_scr[:, at] = branch_grad
        add_sums("gate_m", g * branch[:, at].astype(F32))
        chunks = [slice(start, start + BLOCK) for start in range(0, w_down.shape[0], BLOCK)]
        back = None
        waiting = None
        following = nn(w_down[chunks[0], :], branch_grad)
        for place, rows in enumerate(chunks):
            hidden_grad = following
            if place + 1 < len(chunks):
                following = nn(w_down[chunks[place + 1], :], branch_grad)
            if place > 0:
                term = nn(w_up[:, chunks[place - 1]], waiting)
                back = term if back is None else back + term
            waiting = (slope[rows, at].astype(F32) * hidden_grad).astype(BF16)
            pg_scr[rows, at] = waiting
        back = back + nn(w_up[:, chunks[-1]], waiting)
        add_sums("shift_m", back)
        add_sums("scale_m", back * standard)
        d_mid = g + pre_norm_back(standard, scale, back, gain)
        d_mid_out[:, at] = d_mid
        att_grad = (part(mod, 2, patches) * d_mid).astype(BF16)
        ag_scr[:, at] = att_grad
        mixed_grad = nn(w_out[...], att_grad).astype(BF16)
        do_out[:, at] = mixed_grad
        add_sums("gate_a", d_mid * attended[:, at].astype(F32))
        product = mixed_grad.astype(F32) * mixed[:, at].astype(F32)
        for head in range(HEADS):
            cen_out[head : head + 1, at] = jnp.sum(product[head_rows(head)], axis=0, keepdims=True)

    at = slice(0, patches)
    g = close(at) if has_close else cot_out[:, at].astype(F32) * active[0]
    if has_open:
        dense(at, g)
    else:
        g_out[...] = g[:, : g_out.shape[0]].T
    if has_close:
        put_sums(close_mods, close_before, ("shift_a", "scale_a"))
        put_grads(normed_scr, grads_scr[...], where, D // 8, 0, close_mine, close_other, close_before)
    if has_open:
        put_sums(open_mods, open_before, ("gate_a", "shift_m", "scale_m", "gate_m"))
        count = w_down.shape[0] // 8
        put_grads(hidden, bg_scr[...], where, count, 0, open_mine, open_other, open_before)
        at = count * (D // LANES)
        put_grads(hin_scr, pg_scr[...], where, D // 8, at, open_mine, open_other, open_before)
        at += (w_up.shape[1] // LANES) * (D // 8)
        put_grads(mixed, ag_scr[...], where, D // 8, at, open_mine, open_other, open_before)
    else:
        sums_out[...] = lines[...]
        put_lines(sums_out, 0, close_mods[...])
        close_other[sums_at:, :] = sums_out[...].astype(BF16)


def attend_back_kernel(has_before, waits, q, kn, vt, lse, d_out, centre, *refs):
    if has_before:
        before, *refs = refs
    d_kv, dq_out, kt_scr, vn_scr = refs[waits:]
    for column in range(0, D, LANES):
        kt_scr[column : column + LANES, :] = turned(kn[:, column : column + LANES])
    for column in range(0, vt.shape[1], BLOCK):
        vn_scr[column : column + BLOCK, :] = turned(vt[:, column : column + BLOCK])

    steps = [(head, slice(at, at + BLOCK)) for head in range(HEADS) for at in range(0, kn.shape[0], BLOCK)]

    def score(head, at):
        columns = pair_columns(head)
        rows = head_rows(head)
        return nn(kn[at, columns], padded(q[rows, :], head)), nn(vn_scr[at, columns], padded(d_out[rows, :], head))

    totals = {}

    def finish(head, at, probs, score_grads):
        rows = head_rows(head)
        d_kv[D + rows.start : D + rows.stop, at] = nt(d_out[rows, :], probs).astype(d_kv.dtype)
        d_kv[rows, at] = nt(q[rows, :], score_grads).astype(d_kv.dtype)
        term = nn(kt_scr[rows, at], score_grads)
        if head not in totals:
            totals[head] = before[rows, :] + term if has_before else term
            return
        term = totals[head] + term
        if has_before:
            term = term * HEAD_DIM ** (-0.5)
        dq_out[rows, :] = term.astype(dq_out.dtype)

    waiting = None
    following = score(*steps[0])
    for place, (head, at) in enumerate(steps):
        scores, prob_grads = following
        if place + 1 < len(steps):
            following = score(*steps[place + 1])
        if waiting is not None:
            finish(*waiting)
        probs = jnp.exp(scores - lse[head : head + 1, :])
        score_grads = (probs * (prob_grads - centre[head : head + 1, :])).astype(BF16)
        waiting = (head, at, probs.astype(BF16), score_grads)
    finish(*waiting)


def split_kernel(waits, where, *refs):
    *halves, keep, sent, total_scr = refs[waits:]
    rows_half = keep.shape[0]
    at = 0
    for mine, other in zip(halves[::2], halves[1::2]):
        rows = mine.shape[0]
        total_scr[at : at + rows, :] = mine[...] + other[...].astype(F32)
        at += rows
    if at < total_scr.shape[0]:
        total_scr[at:, :] = jnp.zeros((total_scr.shape[0] - at, LANES), F32)
    odd = where[3]
    keep[...] = total_scr[pl.ds(pl.multiple_of(odd * rows_half, 16), rows_half), :]
    sent[...] = total_scr[pl.ds(pl.multiple_of((1 - odd) * rows_half, 16), rows_half), :].astype(BF16)


def pair_sum_kernel(late, *refs):
    count = len(refs) // 3
    for keep, got, out in zip(refs[:count], refs[count : 2 * count], refs[2 * count :]):
        out[...] = (keep[...].astype(F32) + got[...].astype(F32)).astype(BF16)


def put_lines(out, row, values):
    ones = jnp.ones((16, LANES), BF16)
    high = values.astype(BF16)
    low = (values - high.astype(F32)).astype(BF16)
    line = (nt(ones, high) + nt(ones, low))[0:1]
    for column in range(0, line.shape[1], LANES):
        out[row : row + 1, :] = line[:, column : column + LANES]
        row += 1
    return row


def lines_kernel(early, context, *refs):
    *sums, out = refs
    out[...] = jnp.zeros_like(out)
    row = 2 * D // LANES
    for ref in sums:
        row = put_lines(out, row, ref[...])
    for column in range(0, D, LANES):
        out[row : row + 1, :] = context[0:1, column : column + LANES].astype(F32)
        row += 1


def join_kernel(sum_count, early, mine, sums, got, out):
    rows = mine.shape[0]
    out[:rows, :] = (mine[...] + got[:rows, :].astype(F32)).astype(BF16)
    other = got[rows:, :].astype(F32)
    summed = lax.broadcasted_iota(jnp.int32, (SUM_ROWS, LANES), 0) < sum_count
    out[rows:, :] = (sums[...] + jnp.where(summed, other, 0.0)).astype(BF16)


def pair_kernel(rows, where, own, got, out):
    out[:rows, :] = (own[:rows, :].astype(F32) + got[:rows, :].astype(F32)).astype(BF16)
    odd = where[3]
    size = SUM_ROWS
    out[pl.ds(pl.multiple_of(rows + odd * size, 16), size), :] = own[rows:, :]
    out[pl.ds(pl.multiple_of(rows + (1 - odd) * size, 16), size), :] = got[rows:, :]


def gather_kernel(where, *refs):
    halves, (out_out, up_out, down_out, qkv_out), scratch = refs[:4], refs[4:8], refs[8:]
    odd = where[3]
    for ref, own, got in zip(scratch, halves[::2], halves[1::2]):
        rows = own.shape[0]
        ref[pl.ds(pl.multiple_of(odd * rows, 16), rows), :] = own[...]
        ref[pl.ds(pl.multiple_of((1 - odd) * rows, 16), rows), :] = got[...]
    slice_rows = out_out.shape[1]
    for index, ref in enumerate(scratch):
        at = 0
        for out in (down_out, up_out, out_out):
            rows = out.shape[1]
            for column in range(0, out.shape[2], LANES):
                out[index, :, column : column + LANES] = ref[at : at + rows, :].astype(F32)
                at += rows
        if index == 0:
            for column in range(0, qkv_out.shape[1], LANES):
                qkv_out[:, column : column + LANES] = ref[at : at + slice_rows, :].astype(F32)
                at += slice_rows


def finish_kernel(item_count, where, own, got, qkv_1, qkv_out, ada_out, bias_out, shift_out, sum_scr, bias_scr, shift_scr):
    layers = 2
    device, high = where[0], where[4]
    slice_rows = qkv_out.shape[1]
    close_rows = slice_rows * (3 * D // LANES)
    for other in range(2):
        rows = slice(close_rows + other * SUM_ROWS, close_rows + (other + 1) * SUM_ROWS)
        sum_scr[2 * high + other] = own[rows, :].astype(F32)
        sum_scr[2 * (1 - high) + other] = got[rows, :].astype(F32)
    qkv_out[1] = qkv_1[...]
    for tile in range(3 * D // LANES):
        rows = slice(tile * slice_rows, (tile + 1) * slice_rows)
        total = own[rows, :].astype(F32) + got[rows, :].astype(F32)
        qkv_out[0, :, tile * LANES : (tile + 1) * LANES] = total
    tiles = 6 * D // LANES
    contexts = []
    for other in range(item_count):
        line = jnp.concatenate([sum_scr[other, layers * tiles + c : layers * tiles + c + 1, :] for c in range(3)], axis=1)
        contexts.append(line)
    square = jnp.concatenate(contexts + [jnp.zeros((8 - item_count, D), F32)], axis=0)
    spot = lax.broadcasted_iota(jnp.int32, (slice_rows, D), 1)
    want = lax.broadcasted_iota(jnp.int32, (slice_rows, D), 0) + device * slice_rows
    pick = jnp.where(spot == want, 1.0, 0.0).astype(BF16)
    columns = nt(pick, square.astype(BF16))
    bias_rows = bias_out.shape[1]
    for index in range(layers):
        flats = []
        for tile in range(tiles):
            row = index * tiles + tile
            total = None
            flat = None
            for other in range(item_count):
                line = sum_scr[other, row : row + 1, :]
                term = columns[:, other : other + 1] * line
                total = term if total is None else total + term
                flat = line if flat is None else flat + line
            ada_out[index, :, tile * LANES : (tile + 1) * LANES] = total
            flats.append(flat)
        flat = jnp.concatenate(flats, axis=1)
        for place in range(flat.shape[1] // bias_rows):
            bias_scr[place, index : index + 1, :] = flat[:, place * bias_rows : (place + 1) * bias_rows]
            at = 3 * D + place * slice_rows
            shift_scr[place, index : index + 1, :] = flat[:, at : at + slice_rows]
    bias_out[...] = bias_scr[device]
    shift_out[...] = shift_scr[device]


VMEM = pl.BlockSpec(memory_space=pltpu.VMEM)
SMEM = pl.BlockSpec(memory_space=pltpu.SMEM)
ANY = pl.BlockSpec(memory_space=pl.ANY)
HBM = pl.BlockSpec(memory_space=pltpu.HBM)


def layer_block(array, index):
    return pl.BlockSpec((None,) + array.shape[1:], lambda step: (index,) + (0,) * (array.ndim - 1))


def call(body, args, outs, scratch=(), flops=0, name=None):
    arrays = [arg[0] if isinstance(arg, tuple) else arg for arg in args]
    specs = [arg[1] if isinstance(arg, tuple) else VMEM for arg in args]
    return pl.pallas_call(
        body,
        out_shape=[jax.ShapeDtypeStruct(shape, kind) for shape, kind in outs],
        in_specs=specs,
        out_specs=[VMEM] * len(outs),
        scratch_shapes=[one if not isinstance(one, tuple) else pltpu.VMEM(*one) for one in scratch],
        compiler_params=pltpu.CompilerParams(vmem_limit_bytes=VMEM_LIMIT),
        cost_estimate=pl.CostEstimate(flops=flops, bytes_accessed=0, transcendentals=0),
        name=name,
    )(*arrays)


VMEM_LIMIT = 16 * 1024 * 1024


def fast_shards(
    lat_count, lon_count, item_count,
    fields, lead_index, rollout, w_qkv, w_out, w_up, w_down, w_ada, b_ada, cotangent,
):
    _, rows_dev, cols_dev, width = fields.shape
    local = rows_dev * cols_dev
    layers = w_qkv.shape[0]
    ff = w_up.shape[2]
    patches = 4 * local
    device = lax.axis_index("lat") * lon_count + lax.axis_index("lon")
    item = lax.axis_index("item")
    where = jnp.stack([device, device ^ 1, item, item & 1, item >> 1]).astype(jnp.int32)
    active = (1 < rollout[0]).astype(F32)[None]

    def plane_flip(value, flip_lat, flip_y):
        pairs = [
            (a * lon_count + b, (a ^ flip_lat) * lon_count + (b ^ (2 * flip_y)))
            for a in range(lat_count)
            for b in range(lon_count)
        ]
        return lax.ppermute(value, ("lat", "lon"), pairs)

    def swap(value):
        return lax.ppermute(value, "lon", [(index, index ^ 1) for index in range(lon_count)])

    def with_item(value, flip):
        return lax.ppermute(value, "item", [(index, index ^ flip) for index in range(item_count)])

    def plane_parts(value):
        return [value, plane_flip(value, 1, 0), plane_flip(value, 0, 1), plane_flip(value, 1, 1)]

    field_parts = plane_parts(fields.reshape(local, width))
    cot_parts = plane_parts(cotangent.reshape(local, width))

    context = jax.nn.silu(embedding(lead_index[0])).astype(BF16)
    context = jnp.broadcast_to(context[None, :], (16, width))
    square = (width, patches)
    natural = (patches, width)
    fetched = [(pltpu.with_memory_space_constraint(value, pltpu.HBM), HBM) for value in (w_ada, b_ada, w_qkv)]
    fetch_scratch = [((width, 3 * width), BF16), ((width, 6 * width), BF16), (b_ada.shape, F32)]
    fetch_scratch.append(pltpu.SemaphoreType.DMA((3,)))
    first_outs = [((6 * width, LANES), F32)] + [((width, width), BF16)] * 3
    rest_outs = [((width, width), BF16), ((ff, width), BF16), ((width, ff), BF16)]
    first_0 = call(
        functools.partial(prepare_first_kernel, 0, None, 2),
        [context, *fetched, (where, SMEM), (active, SMEM)],
        first_outs,
        fetch_scratch,
        name="prepare_first",
    )
    both = call(
        prepare_both_kernel,
        [context, *fetched, w_out, w_up, w_down],
        first_outs + rest_outs,
        fetch_scratch,
        name="prepare_both",
    )
    rest_1 = call(
        functools.partial(prepare_rest_kernel, 1), [w_out, w_up, w_down], rest_outs, name="prepare_rest"
    )
    first_parts = [first_0, both[:4]]
    rest_parts = [both[4:], rest_1]
    mods = [one[0] for one in first_parts]

    project_outs = [(square, F32), (square, BF16), (square, BF16), (natural, BF16), (square, BF16)]
    dense_flops = 2 * patches * (width * 3 * width + width * width + 2 * width * ff)
    score_flops = 2 * patches * 2 * patches * width * 4
    x, xb, *projected = call(
        first_kernel,
        [*field_parts, *first_parts[0]],
        project_outs,
        flops=2 * patches * width * 4 * width,
        name="first",
    )
    saved = []
    for step in range(STEPS):
        for index in range(layers):
            q, kn, vt = projected
            kn_far, vt_far = swap(kn), swap(vt)
            last = step == STEPS - 1 and index == layers - 1
            if index == 0 and step > 0:
                x_step = x
            following = list(first_parts[(index + 1) % layers])
            lse, mixed, attended, middle, hidden, slope, branch, *results = call(
                functools.partial(forward_kernel, last),
                ([(active, SMEM), x, x_step] if last else [x])
                + [q, kn, kn_far, vt, vt_far, mods[index], *rest_parts[index]]
                + ([] if last else following),
                [
                    ((HEADS, patches), F32),
                    (square, BF16),
                    (square, BF16),
                    (square, BF16),
                    ((ff, patches), BF16),
                    ((ff, patches), BF16),
                    (square, BF16),
                ]
                + ([((local, width), F32)] if last else project_outs),
                flops=dense_flops + 2 * score_flops,
                name="forward",
            )
            saved.append((xb, [mixed, attended, middle, hidden, slope, branch], (q, kn, kn_far, vt, vt_far, lse)))
            if last:
                final = results[0]
            else:
                x, xb, *projected = results

    slice_rows = width // 8
    open_rows = 2 * (ff // 8) * (width // LANES) + slice_rows * (width // LANES)
    close_rows = slice_rows * (3 * width // LANES)
    order = [(step, index) for step in reversed(range(STEPS)) for index in reversed(range(layers))]
    open_done = [None] * layers
    close_done = [None] * layers
    pending = None
    for place in range(len(order) + 1):
        has_close = pending is not None
        has_open = place < len(order)
        use = [order[place - 1][1], order[place][1] if has_open else 0]
        waits = []
        if has_close and close_done[use[0]]:
            waits = [pair_1] if has_open else [item_got_1]
        args = [(value, ANY) for value in waits] + [(where, SMEM), (active, SMEM)]
        outs = []
        scratch = []
        has_before = [False, False]
        start = ""
        if has_close:
            args += pending
            if close_done[use[0]] is not None:
                has_before[0] = True
                args += close_done[use[0]]
            outs += [((close_rows, LANES), F32)]
            sent_rows = close_rows + (0 if has_open else SUM_ROWS)
            outs += [((sent_rows, LANES), BF16 if has_before[0] else F32), ((2 * width, LANES), F32)]
            scratch += [((3 * width, patches), BF16), (square, BF16)]
        if place == 0:
            start = "first"
            args += cot_parts
            outs += [(square, BF16)]
        elif has_open and order[place][0] != order[place - 1][0]:
            start = "cross"
            args += [cot_t]
        if has_open:
            step, index = order[place]
            xb, kept, heads = saved[step * layers + index]
            args += kept + [mods[index], w_out, w_up, w_down]
            if open_done[index] is not None:
                has_before[1] = True
                args += open_done[index]
            outs += [
                ((open_rows, LANES), F32),
                ((open_rows, LANES), BF16 if has_before[1] else F32),
                ((4 * width, LANES), F32),
                (square, F32),
                (square, BF16),
                ((HEADS, patches), F32),
            ]
            scratch += [(square, BF16), ((ff, patches), BF16), (square, BF16), (square, BF16)]
        else:
            args += [lines]
            outs += [((local, width), F32), ((SUM_ROWS, LANES), F32)]
        results = list(
            call(
                functools.partial(dense_back_kernel, has_close, has_open, has_before, start, use, len(waits)),
                args,
                outs,
                scratch,
                flops=2 * dense_flops if has_open else 0,
                name="dense_back" if has_open else "close_back",
            )
        )
        if has_close:
            close_done[use[0]] = results[:3]
            del results[:3]
        if start == "first":
            cot_t = results.pop(0)
        if not has_open:
            gradient, line = results
            break
        open_done[index] = results[:3]
        d_mid, d_out, centre = results[3:]
        q, kn, kn_far, vt, vt_far, lse = heads
        halves = [open_done[index][0], open_done[index][1]]
        if index == 0:
            halves += [close_done[1][0], close_done[1][1]]
        half_rows = -(-sum(half.shape[0] for half in halves[::2]) // 32) * 16

        def split(waits):
            pieces = [half if place % 2 == 0 else swap(half) for place, half in enumerate(halves)]
            return call(
                functools.partial(split_kernel, len(waits)),
                [(where, SMEM), *waits, *pieces],
                [((half_rows, LANES), F32), ((half_rows, LANES), BF16)],
                [((2 * half_rows, LANES), F32)],
                name="split",
            )

        def pair_sum(late, keeps, gots):
            outs = [(keep.shape, BF16) for keep in keeps]
            return call(pair_sum_kernel, [(late, ANY), *keeps, *gots], outs, name="pair_sum")

        waits = []
        if has_before[1] and index == 0:
            pair_got_1 = with_item(pair_1, 2)
            lines = call(
                lines_kernel,
                [(pair_got_1, ANY), context, open_done[0][2], close_done[1][2], open_done[1][2]],
                [((SUM_ROWS, LANES), F32)],
                flops=10 * score_flops,
                name="lines",
            )[0]
            keep, sent = split([(lines, ANY)])
            got_0 = with_item(sent, 1)
            waits = [keep]
        d_far, dq = call(
            functools.partial(attend_back_kernel, False, len(waits)),
            [q, kn_far, vt_far, lse, d_out, centre] + [(value, ANY) for value in waits],
            [((2 * width, patches), BF16), (square, F32)],
            [(square, BF16), (natural, BF16)],
            flops=10 * score_flops,
            name="attend_far",
        )
        d_got = swap(d_far)
        waits = []
        if has_before[1]:
            if index == 1:
                keep, sent = split([(d_far, ANY)])
                got_1 = with_item(sent, 1)
                waits = [keep]
            else:
                pair_0, item_1 = pair_sum(d_far, [keep, pair_1], [got_0, pair_got_1])
                item_got_1 = with_item(item_1, 1)
                pair_got_0 = with_item(pair_0, 2)
                waits = [pair_0]
        d_own, dq = call(
            functools.partial(attend_back_kernel, True, len(waits)),
            [q, kn, vt, lse, d_out, centre, dq] + [(value, ANY) for value in waits],
            [((2 * width, patches), F32), (square, BF16)],
            [(square, BF16), (natural, BF16)],
            flops=10 * score_flops,
            name="attend_own",
        )
        if has_before[1] and index == 1:
            (pair_1,) = pair_sum(dq, [keep], [got_1])
        pending = [d_own, d_got, dq, d_mid, xb, mods[index], w_qkv]

    message = call(
        functools.partial(join_kernel, layers * 6 * width // LANES),
        [(pair_got_0, ANY), close_done[0][0], line, swap(close_done[0][1])],
        [((close_rows + SUM_ROWS, LANES), BF16)],
        name="join",
    )[0]
    message_got = with_item(message, 1)
    (item_0,) = pair_sum(message_got, [pair_0], [pair_got_0])
    message = call(
        functools.partial(pair_kernel, close_rows),
        [(where, SMEM), message, message_got],
        [((close_rows + 2 * SUM_ROWS, LANES), BF16)],
        name="pair",
    )[0]
    out_grad, up_grad, down_grad, qkv_1 = call(
        gather_kernel,
        [(where, SMEM), item_0, with_item(item_0, 1), item_1, item_got_1],
        [
            ((layers, slice_rows, width), F32),
            ((layers, slice_rows, ff), F32),
            ((layers, ff // 8, width), F32),
            ((slice_rows, 3 * width), F32),
        ],
        [((2 * pair.shape[0], LANES), BF16) for pair in (pair_0, pair_1)],
        name="gather",
    )
    bias_rows = 6 * width // 8
    qkv_grad, ada_grad, bias_grad, shift_grad = call(
        functools.partial(finish_kernel, item_count),
        [(where, SMEM), message, with_item(message, 2), qkv_1],
        [
            ((layers, slice_rows, 3 * width), F32),
            ((layers, slice_rows, 6 * width), F32),
            ((layers, bias_rows), F32),
            ((layers, slice_rows), F32),
        ],
        [
            ((item_count, SUM_ROWS, LANES), F32),
            ((8, layers, bias_rows), F32),
            ((8, layers, slice_rows), F32),
        ],
        name="finish",
    )
    field_shape = (1, rows_dev, cols_dev, width)
    return (
        final.reshape(field_shape),
        gradient.reshape(field_shape),
        qkv_grad,
        out_grad,
        up_grad,
        down_grad,
        ada_grad,
        bias_grad,
        shift_grad,
    )


def solution(mesh):
    lat_count, lon_count, item_count = mesh.shape["lat"], mesh.shape["lon"], mesh.shape["item"]
    if lat_count == 2 and lon_count == 4:
        body = functools.partial(fast_shards, lat_count, lon_count, item_count)
    else:
        body = shards
    return jax.shard_map(
        body,
        mesh=mesh,
        in_specs=(
            P("item", "lat", "lon", None),
            P("item"),
            P("item"),
            P(),
            P(),
            P(),
            P(),
            P(),
            P(),
            P("item", "lat", "lon", None),
        ),
        out_specs=(
            P("item", "lat", "lon", None),
            P("item", "lat", "lon", None),
            P(None, ("lat", "lon"), None),
            P(None, ("lat", "lon"), None),
            P(None, ("lat", "lon"), None),
            P(None, ("lat", "lon"), None),
            P(None, ("lat", "lon"), None),
            P(None, ("lat", "lon")),
            P(None, ("lat", "lon")),
        ),
        check_vma=False,
    )
```

```python
import functools
import math

import jax
import jax.numpy as jnp
from jax import lax
from jax.experimental import pallas as pl
from jax.experimental.pallas import tpu as pltpu
from jax.sharding import PartitionSpec as P

D = 384
HEADS = 6
HEAD_DIM = 64
STEPS = 2


def shortened(shard):
    return jax.tree.map(lambda a: a.astype(jnp.bfloat16) if a.dtype == jnp.float32 else a, shard)


def embedding(lead):
    half_width = D // 2
    lead_hours = 6.0 * (lead.astype(jnp.float32) + 1.0)
    frequencies = jnp.exp(
        -math.log(10000.0) * jnp.arange(half_width, dtype=jnp.float32) / half_width
    )
    angles = lead_hours * frequencies
    return jnp.concatenate([jnp.sin(angles), jnp.cos(angles)])


def pre_norm(values, shift_part, scale_part):
    centred = values - jnp.mean(values, axis=-1, keepdims=True)
    variance = jnp.mean(centred * centred, axis=-1, keepdims=True)
    return centred * lax.rsqrt(variance + 1e-06) * (1.0 + scale_part) + shift_part


def gather_keys(keys_values):
    band_rows = lax.all_gather(keys_values, "lon", axis=0, tiled=True)
    return lax.all_gather(band_rows, "lat", axis=0, tiled=True)


def spread_keys(key_value_grads):
    band_grads = lax.psum_scatter(
        key_value_grads.astype(jnp.bfloat16), "lat", scatter_dimension=0, tiled=True
    )
    return lax.psum_scatter(band_grads, "lon", scatter_dimension=0, tiled=True).astype(jnp.float32)


def forward_layer(current, modulation, weight_qkv, weight_out, weight_up, weight_down):
    local_rows, width = current.shape
    shift_attn, scale_attn, gate_attn, shift_mlp, scale_mlp, gate_mlp = modulation
    normed = pre_norm(current, shift_attn, scale_attn).astype(jnp.bfloat16)
    projected = jnp.dot(normed, weight_qkv, preferred_element_type=jnp.float32).astype(jnp.bfloat16)
    queries = projected[:, :width].reshape(local_rows, HEADS, HEAD_DIM)
    own_keys = projected[:, width:]
    gathered = gather_keys(own_keys)
    total_rows = gathered.shape[0]
    key_heads = gathered[:, :width].reshape(total_rows, HEADS, HEAD_DIM)
    value_heads = gathered[:, width:].reshape(total_rows, HEADS, HEAD_DIM)
    scores = jnp.einsum(
        "thd,nhd->htn", queries, key_heads, preferred_element_type=jnp.float32
    ) * HEAD_DIM ** (-0.5)
    log_total = jax.nn.logsumexp(scores, axis=-1, keepdims=True)
    probabilities = jnp.exp(scores - log_total).astype(jnp.bfloat16)
    mixed = jnp.einsum(
        "htn,nhd->thd", probabilities, value_heads, preferred_element_type=jnp.float32
    )
    mixed = mixed.reshape(local_rows, width).astype(jnp.bfloat16)
    attended = jnp.dot(mixed, weight_out, preferred_element_type=jnp.float32)
    middle = current + gate_attn * attended
    hidden_in = pre_norm(middle, shift_mlp, scale_mlp).astype(jnp.bfloat16)
    pre_act = jnp.dot(hidden_in, weight_up, preferred_element_type=jnp.float32)
    hidden = jax.nn.gelu(pre_act).astype(jnp.bfloat16)
    branch = jnp.dot(hidden, weight_down, preferred_element_type=jnp.float32)
    output = middle + gate_mlp * branch
    kept = (
        current,
        normed,
        queries,
        gathered,
        own_keys,
        log_total,
        mixed,
        attended,
        middle,
        hidden_in,
        pre_act,
        hidden,
        branch,
    )
    return (output, kept)


def backward_layer(grad_out, kept, modulation, weight_qkv, weight_out, weight_up, weight_down):
    (
        current,
        normed,
        queries,
        gathered,
        own_keys,
        log_total,
        mixed,
        attended,
        middle,
        hidden_in,
        pre_act,
        hidden,
        branch,
    ) = kept
    local_rows, width = current.shape
    total_rows = gathered.shape[0]
    shift_attn, scale_attn, gate_attn, shift_mlp, scale_mlp, gate_mlp = modulation
    factor = HEAD_DIM ** (-0.5)
    branch_grad = (gate_mlp * grad_out).astype(jnp.bfloat16)
    gate_mlp_grad = jnp.sum(grad_out * branch, axis=0)
    hidden_grad = jnp.dot(branch_grad, weight_down.T, preferred_element_type=jnp.float32)
    down_grad = jnp.dot(hidden.T, branch_grad, preferred_element_type=jnp.float32)
    _, gelu_back = jax.vjp(jax.nn.gelu, pre_act)
    pre_grad = gelu_back(hidden_grad)[0].astype(jnp.bfloat16)
    hidden_in_grad = jnp.dot(pre_grad, weight_up.T, preferred_element_type=jnp.float32)
    up_grad = jnp.dot(hidden_in.T, pre_grad, preferred_element_type=jnp.float32)
    _, second_back = jax.vjp(pre_norm, middle, shift_mlp, scale_mlp)
    middle_part, shift_mlp_grad, scale_mlp_grad = second_back(hidden_in_grad)
    middle_grad = grad_out + middle_part
    attended_grad = (gate_attn * middle_grad).astype(jnp.bfloat16)
    gate_attn_grad = jnp.sum(middle_grad * attended, axis=0)
    mixed_grad = jnp.dot(attended_grad, weight_out.T, preferred_element_type=jnp.float32).astype(
        jnp.bfloat16
    )
    out_grad = jnp.dot(mixed.T, attended_grad, preferred_element_type=jnp.float32)
    mixed_heads = mixed_grad.reshape(local_rows, HEADS, HEAD_DIM)
    key_heads = gathered[:, :width].reshape(total_rows, HEADS, HEAD_DIM)
    value_heads = gathered[:, width:].reshape(total_rows, HEADS, HEAD_DIM)
    scores = (
        jnp.einsum("thd,nhd->htn", queries, key_heads, preferred_element_type=jnp.float32) * factor
    )
    probabilities = jnp.exp(scores - log_total)
    prob_grads = jnp.einsum(
        "thd,nhd->htn", mixed_heads, value_heads, preferred_element_type=jnp.float32
    )
    centre = jnp.sum(prob_grads * probabilities, axis=-1, keepdims=True)
    score_grads = (probabilities * (prob_grads - centre)).astype(jnp.bfloat16)
    query_grads = (
        jnp.einsum("htn,nhd->thd", score_grads, key_heads, preferred_element_type=jnp.float32)
        * factor
    )
    value_grads = jnp.einsum(
        "htn,thd->nhd",
        probabilities.astype(jnp.bfloat16),
        mixed_heads,
        preferred_element_type=jnp.float32,
    )
    key_grads = (
        jnp.einsum("htn,thd->nhd", score_grads, queries, preferred_element_type=jnp.float32)
        * factor
    )
    key_value_grads = jnp.concatenate(
        [key_grads.reshape(total_rows, width), value_grads.reshape(total_rows, width)], axis=1
    )
    local_grads = spread_keys(key_value_grads)
    projected_grad = jnp.concatenate(
        [query_grads.reshape(local_rows, width), local_grads], axis=1
    ).astype(jnp.bfloat16)
    normed_grad = jnp.dot(projected_grad, weight_qkv.T, preferred_element_type=jnp.float32)
    qkv_grad = jnp.dot(normed.T, projected_grad, preferred_element_type=jnp.float32)
    _, first_back = jax.vjp(pre_norm, current, shift_attn, scale_attn)
    current_part, shift_attn_grad, scale_attn_grad = first_back(normed_grad)
    input_grad = middle_grad + current_part
    modulation_grad = jnp.concatenate(
        [
            shift_attn_grad,
            scale_attn_grad,
            gate_attn_grad,
            shift_mlp_grad,
            scale_mlp_grad,
            gate_mlp_grad,
        ]
    )
    return (input_grad, (qkv_grad, out_grad, up_grad, down_grad, modulation_grad))


def shards(fields, lead_index, rollout, w_qkv, w_out, w_up, w_down, w_ada, b_ada, cotangent):
    _, rows_dev, cols_dev, width = fields.shape
    local_rows = rows_dev * cols_dev
    layer_count = w_qkv.shape[0]
    context = jax.nn.silu(embedding(lead_index[0])).astype(jnp.bfloat16)
    context_wide = context.astype(jnp.float32)
    modulations = [
        (
            jnp.dot(context[None, :], w_ada[index], preferred_element_type=jnp.float32)[0]
            + b_ada[index]
        ).reshape(6, width)
        for index in range(layer_count)
    ]
    weight_sets = [
        (w_qkv[index], w_out[index], w_up[index], w_down[index]) for index in range(layer_count)
    ]
    count = rollout[0]
    current = fields.reshape(local_rows, width).astype(jnp.float32)
    saved = []
    for rollout_step in range(STEPS):
        updated = current
        kept_layers = []
        for index in range(layer_count):
            updated, kept = forward_layer(updated, modulations[index], *weight_sets[index])
            kept_layers.append(kept)
        current = jnp.where(rollout_step < count, updated, current)
        saved.append(kept_layers)
    gradient = cotangent.reshape(local_rows, width).astype(jnp.float32)
    summed = None
    shares = None
    for rollout_step in reversed(range(STEPS)):
        active = (rollout_step < count).astype(jnp.float32)
        inner = gradient * active
        layer_terms = [None] * layer_count
        for index in reversed(range(layer_count)):
            inner, layer_terms[index] = backward_layer(
                inner, saved[rollout_step][index], modulations[index], *weight_sets[index]
            )
        gradient = inner + (1.0 - active) * gradient
        modulation_grads = jnp.stack([terms[4] for terms in layer_terms])
        step_terms = (
            jnp.stack([terms[0] for terms in layer_terms]),
            jnp.stack([terms[1] for terms in layer_terms]),
            jnp.stack([terms[2] for terms in layer_terms]),
            jnp.stack([terms[3] for terms in layer_terms]),
            context_wide[None, :, None] * modulation_grads[:, None, :],
            modulation_grads,
            modulation_grads[:, 3 * width : 4 * width],
        )
        summed = step_terms if summed is None else jax.tree.map(jnp.add, summed, step_terms)
    shares = lax.psum_scatter(summed, ("lat", "lon"), scatter_dimension=1, tiled=True)
    totals = jax.tree.map(
        lambda part: part.astype(jnp.float32), lax.psum(shortened(shares), "item")
    )
    return (
        current.reshape(1, rows_dev, cols_dev, width),
        gradient.reshape(1, rows_dev, cols_dev, width),
        totals[0],
        totals[1],
        totals[2],
        totals[3],
        totals[4],
        totals[5],
        totals[6],
    )


F32 = jnp.float32
BF16 = jnp.bfloat16
GELU_A = math.sqrt(2.0 / math.pi)
GELU_B = 0.044715
LANES = 128
BLOCK = 256
PAIR = 2 * HEAD_DIM
SUM_ROWS = 48


def nn(left, right, precision=None):
    return lax.dot_general(
        left, right, (((1,), (0,)), ((), ())), preferred_element_type=F32, precision=precision
    )


def nt(left, right, precision=None):
    return lax.dot_general(
        left, right, (((1,), (1,)), ((), ())), preferred_element_type=F32, precision=precision
    )


def identity(size):
    rows = lax.broadcasted_iota(jnp.int32, (size, size), 0)
    columns = lax.broadcasted_iota(jnp.int32, (size, size), 1)
    return jnp.where(rows == columns, 1.0, 0.0).astype(BF16)


def turned(values):
    return nt(identity(values.shape[1]), values).astype(BF16)


def wide(column_tile, lanes):
    return jnp.concatenate([column_tile] * (lanes // LANES), axis=1)


def folded(values):
    pieces = [values[:, at : at + LANES] for at in range(0, values.shape[1], LANES)]
    return sum(pieces[1:], pieces[0])


def standardise(values):
    rows = values.shape[0]
    centred = values - jnp.sum(values, axis=0, keepdims=True) * (1.0 / rows)
    variance = jnp.sum(centred * centred, axis=0, keepdims=True) * (1.0 / rows)
    scale = lax.rsqrt(variance + 1e-06)
    return centred * scale, scale


def pre_norm_back(standard, scale, grad, gain):
    rows = standard.shape[0]
    inner = grad * gain
    first = jnp.sum(inner, axis=0, keepdims=True) * (1.0 / rows)
    second = jnp.sum(inner * standard, axis=0, keepdims=True) * (1.0 / rows)
    return scale * (inner - first - standard * second)


def part(mod_ref, index, lanes):
    return wide(mod_ref[index * D : (index + 1) * D, :], lanes)


def turn_into(source, out, at=0):
    for column in range(0, out.shape[0], BLOCK):
        width = min(BLOCK, out.shape[0] - column)
        out[column : column + width, :] = turned(source[:, at + column : at + column + width])


def prepare_kernel(first, rest, waits, context, *refs):
    hbm, refs = refs[:6], refs[6 + waits :]
    outs = refs[: (4 if first is not None else 0) + (3 if rest is not None else 0)]
    scratch, sems = refs[len(outs) : -1], refs[-1]
    sources = []
    if rest is not None:
        sources += [ref.at[rest] for ref in hbm[3:]]
    if first is not None:
        sources += [hbm[0].at[first], hbm[1].at[first], hbm[2]]
    copies = [
        pltpu.make_async_copy(source, target, sems.at[place])
        for place, (source, target) in enumerate(zip(sources, scratch))
    ]
    for copy in copies:
        copy.start()
    if rest is not None:
        for copy, source, out in zip(copies, scratch, outs[-3:]):
            copy.wait()
            turn_into(source, out)
    if first is not None:
        mod, w_q_t, w_v_t, w_k = outs[:4]
        w_qkv, w_ada, b_ada = scratch[-3:]
        copies[-3].wait()
        w_k[...] = w_qkv[:, D : 2 * D]
        turn_into(w_qkv, w_q_t)
        turn_into(w_qkv, w_v_t, 2 * D)
        copies[-2].wait()
        copies[-1].wait()
        values = nn(context[...], w_ada[...])[0:1] + b_ada[first : first + 1, :]
        for column in range(0, values.shape[1], LANES):
            tile = jnp.broadcast_to(values[:, column : column + LANES], (LANES, LANES))
            mod[column : column + LANES, :] = tile.T


def prepare_start_kernel(context, *refs):
    weights, fields = refs[:6], refs[6]
    outs, out, scratch, sem = refs[9:13], refs[13], refs[14:-1], refs[-1]
    copy = pltpu.make_async_copy(fields, out, sem)
    copy.start()
    prepare_kernel(0, None, 0, context, *weights, *outs, *scratch)
    copy.wait()


def project(x, mod_ref, w_q_t, w_v_t, w_k, outs):
    q_out, kn_out, vt_out = outs
    lanes = x.shape[1]
    standard, _ = standardise(x)
    normed = (standard * (1.0 + part(mod_ref, 1, lanes)) + part(mod_ref, 0, lanes)).astype(BF16)
    vt_out[...] = nn(w_v_t[...], normed).astype(BF16)
    q_out[...] = (nn(w_q_t[...], normed) * HEAD_DIM ** (-0.5)).astype(BF16)
    for at in range(0, lanes, BLOCK):
        kn_out[at : at + BLOCK, :] = nn(turned(normed[:, at : at + BLOCK]), w_k[...]).astype(BF16)


def first_kernel(early, own, flip_x, flip_y, flip_xy, mod, w_q_t, w_v_t, w_k, x_out, xb_out, *outs):
    for index, ref in enumerate((own, flip_x, flip_y, flip_xy)):
        rows = ref.shape[0]
        flat = turned(ref[...])
        xb_out[:, index * rows : (index + 1) * rows] = flat
        x_out[:, index * rows : (index + 1) * rows] = flat.astype(F32)
    project(x_out[...], mod, w_q_t, w_v_t, w_k, outs)


def head_rows(head):
    return slice(head * HEAD_DIM, (head + 1) * HEAD_DIM)


def pair_columns(head):
    return slice(head // 2 * PAIR, (head // 2 + 1) * PAIR)


def padded(rows, head):
    zeros = jnp.zeros_like(rows)
    return jnp.concatenate([rows, zeros] if head % 2 == 0 else [zeros, rows], axis=0)


def forward_kernel(last, *refs):
    if last:
        active, x, x_step, *refs = refs
    else:
        x, *refs = refs
    q, kn_own, kn_far, vt_own, vt_far, mod, w_out_t, w_up_t, w_down_t, *refs = refs
    if not last:
        mod_next, w_q_t, w_v_t, w_k, *refs = refs
    lse, mixed, attended, middle, hidden, slope, branch, *refs = refs
    if last:
        (final,) = refs
    else:
        x_next, xb_next, *next_outs = refs
    patches = x.shape[1]

    keys = [(kn, vt, slice(at, at + BLOCK)) for kn, vt in ((kn_own, vt_own), (kn_far, vt_far)) for at in range(0, patches, BLOCK)]
    ones = jnp.ones((16, BLOCK), BF16)
    queries = [padded(q[head_rows(head), :], head) for head in range(HEADS)]

    def score(head, step):
        kn, _, at = keys[step]
        scores = nn(kn[at, pair_columns(head)], queries[head])
        return scores, jnp.max(scores, axis=0, keepdims=True)

    def value(head, step, probs):
        _, vt, at = keys[step]
        return nn(jnp.concatenate([vt[head_rows(head), at], ones], axis=0), probs)

    current = [score(0, step) for step in range(len(keys))]
    for head in range(HEADS):
        top = functools.reduce(jnp.maximum, [highest for _, highest in current])
        following = []
        total = None
        waiting = None
        for step in range(len(keys)):
            if head + 1 < HEADS:
                following.append(score(head + 1, step))
            probs = jnp.exp(current[step][0] - top).astype(BF16)
            if waiting is not None:
                term = value(head, step - 1, waiting)
                total = term if total is None else total + term
            waiting = probs
        total = total + value(head, len(keys) - 1, waiting)
        weight = total[HEAD_DIM : HEAD_DIM + 1]
        mixed[head_rows(head), :] = (total[:HEAD_DIM] * (1.0 / weight)).astype(BF16)
        lse[head : head + 1, :] = top + jnp.log(weight)
        current = following

    att = nn(w_out_t[...], mixed[...])
    attended[...] = att.astype(BF16)
    mid = x[...] + part(mod, 2, patches) * att
    middle[...] = mid.astype(BF16)
    standard, _ = standardise(mid)
    hidden_in = (standard * (1.0 + part(mod, 4, patches)) + part(mod, 3, patches)).astype(BF16)
    chunks = [slice(at, at + BLOCK) for at in range(0, w_up_t.shape[0], BLOCK)]
    down = None
    waiting = None
    following = nn(w_up_t[chunks[0], :], hidden_in)
    for place, rows in enumerate(chunks):
        act = following
        if place + 1 < len(chunks):
            following = nn(w_up_t[chunks[place + 1], :], hidden_in)
        if place > 0:
            term = nn(w_down_t[:, chunks[place - 1]], waiting)
            down = term if down is None else down + term
        squared = act * act
        bent = jnp.tanh(act * (GELU_A + (GELU_A * GELU_B) * squared))
        half = 0.5 + 0.5 * bent
        waiting = (act * half).astype(BF16)
        hidden[rows, :] = waiting
        curve = (1.0 - bent * bent) * (0.5 * GELU_A + (1.5 * GELU_A * GELU_B) * squared)
        slope[rows, :] = (half + act * curve).astype(BF16)
    down = down + nn(w_down_t[:, chunks[-1]], waiting)
    branch[...] = down.astype(BF16)
    out = mid + part(mod, 5, patches) * down
    if last:
        own = final.shape[0]
        final[...] = jnp.where(active[0] > 0.0, out[:, :own], x_step[:, :own]).T
    else:
        x_next[...] = out
        xb_next[...] = out.astype(BF16)
        project(out, mod_next, w_q_t, w_v_t, w_k, next_outs)


def put_grads(left_ref, right, where, count, at, mine, other, before):
    rows = [left_ref[pl.ds(pl.multiple_of(where[place] * count, 16), count), :] for place in range(2)]
    product = nt(jnp.concatenate(rows, axis=0), right)
    for column in range(0, product.shape[1], LANES):
        low = product[:count, column : column + LANES]
        high = product[count:, column : column + LANES]
        if before is not None:
            low = low + before[0][at : at + count, :]
            high = high + before[1][at : at + count, :]
        mine[at : at + count, :] = low.astype(mine.dtype)
        other[at : at + count, :] = high.astype(other.dtype)
        at += count


def dense_back_kernel(has_close, has_open, has_before, start, layers, waits, *refs):
    refs = list(refs)

    def take(count):
        taken = refs[:count]
        del refs[:count]
        return taken

    take(waits)
    where, active = take(2)
    close_before = open_before = None
    if has_close:
        d_own, d_got, dq, d_mid_in, x_in, mod_in, w_qkv = take(7)
        w_qkv = w_qkv.at[layers[0]]
        if has_before[0]:
            close_before = take(3)
    if start == "first":
        cots = take(4)
    elif start == "cross":
        cots = take(1)
    if has_open:
        mixed, attended, middle, hidden, slope, branch, mod, w_out, w_up, w_down = take(10)
        w_out, w_up, w_down = (ref.at[layers[1]] for ref in (w_out, w_up, w_down))
        if has_before[1]:
            open_before = take(3)
    else:
        (lines,) = take(1)
    if has_close:
        close_mine, close_other, close_mods = take(3)
    if start == "first":
        (cot_out,) = take(1)
    if has_open:
        open_mine, open_other, open_mods, d_mid_out, do_out, cen_out = take(6)
    else:
        g_out, sums_out = take(2)
        sums_at = close_before[1].shape[0]
    if has_close:
        grads_scr, normed_scr = take(2)
    if has_open:
        bg_scr, pg_scr, hin_scr, ag_scr = take(4)

    patches = middle.shape[1] if has_open else x_in.shape[1]
    totals = {}

    def add_sums(name, values):
        totals[name] = totals[name] + folded(values) if name in totals else folded(values)

    def put_sums(out, before, names):
        for place, name in enumerate(names):
            rows = slice(place * D, (place + 1) * D)
            out[rows, :] = totals[name] + before[2][rows, :] if before else totals[name]

    if start == "first":
        for index, ref in enumerate(cots):
            rows = ref.shape[0]
            cot_out[:, index * rows : (index + 1) * rows] = turned(ref[...])

    def close(at):
        standard, scale = standardise(x_in[:, at].astype(F32))
        gain = 1.0 + part(mod_in, 1, patches)
        normed_scr[:, at] = (standard * gain + part(mod_in, 0, patches)).astype(BF16)
        for third in range(3):
            if third == 0:
                piece = dq[:, at]
            else:
                rows = slice((third - 1) * D, third * D)
                piece = (d_own[rows, at] + d_got[rows, at].astype(F32)).astype(BF16)
            grads_scr[third * D : (third + 1) * D, at] = piece
        back = nn(w_qkv[...], grads_scr[:, at])
        add_sums("shift_a", back)
        add_sums("scale_a", back * standard)
        g = d_mid_in[:, at] + pre_norm_back(standard, scale, back, gain)
        if start == "cross":
            g = g + (1.0 - active[0]) * cots[0][:, at].astype(F32)
        return g

    def dense(at, g):
        standard, scale = standardise(middle[:, at].astype(F32))
        gain = 1.0 + part(mod, 4, patches)
        hin_scr[:, at] = (standard * gain + part(mod, 3, patches)).astype(BF16)
        branch_grad = (part(mod, 5, patches) * g).astype(BF16)
        bg_scr[:, at] = branch_grad
        add_sums("gate_m", g * branch[:, at].astype(F32))
        chunks = [slice(start, start + BLOCK) for start in range(0, w_down.shape[0], BLOCK)]
        back = None
        waiting = None
        following = nn(w_down[chunks[0], :], branch_grad)
        for place, rows in enumerate(chunks):
            hidden_grad = following
            if place + 1 < len(chunks):
                following = nn(w_down[chunks[place + 1], :], branch_grad)
            if place > 0:
                term = nn(w_up[:, chunks[place - 1]], waiting)
                back = term if back is None else back + term
            waiting = (slope[rows, at].astype(F32) * hidden_grad).astype(BF16)
            pg_scr[rows, at] = waiting
        back = back + nn(w_up[:, chunks[-1]], waiting)
        add_sums("shift_m", back)
        add_sums("scale_m", back * standard)
        d_mid = g + pre_norm_back(standard, scale, back, gain)
        d_mid_out[:, at] = d_mid
        att_grad = (part(mod, 2, patches) * d_mid).astype(BF16)
        ag_scr[:, at] = att_grad
        mixed_grad = nn(w_out[...], att_grad).astype(BF16)
        do_out[:, at] = mixed_grad
        add_sums("gate_a", d_mid * attended[:, at].astype(F32))
        product = mixed_grad.astype(F32) * mixed[:, at].astype(F32)
        for head in range(HEADS):
            cen_out[head : head + 1, at] = jnp.sum(product[head_rows(head)], axis=0, keepdims=True)

    at = slice(0, patches)
    g = close(at) if has_close else cot_out[:, at].astype(F32) * active[0]
    if has_open:
        dense(at, g)
    else:
        g_out[...] = g[:, : g_out.shape[0]].T
    if has_close:
        put_sums(close_mods, close_before, ("shift_a", "scale_a"))
        put_grads(normed_scr, grads_scr[...], where, D // 8, 0, close_mine, close_other, close_before)
    if has_open:
        put_sums(open_mods, open_before, ("gate_a", "shift_m", "scale_m", "gate_m"))
        count = w_down.shape[0] // 8
        put_grads(hidden, bg_scr[...], where, count, 0, open_mine, open_other, open_before)
        at = count * (D // LANES)
        put_grads(hin_scr, pg_scr[...], where, D // 8, at, open_mine, open_other, open_before)
        at += (w_up.shape[1] // LANES) * (D // 8)
        put_grads(mixed, ag_scr[...], where, D // 8, at, open_mine, open_other, open_before)
    else:
        sums_out[...] = lines[...]
        put_lines(sums_out, 0, close_mods[...])
        close_other[sums_at:, :] = sums_out[...].astype(BF16)


def attend_back_kernel(has_before, waits, q, kn, vt, lse, d_out, centre, *refs):
    if has_before:
        before, *refs = refs
    d_kv, dq_out, kt_scr, vn_scr = refs[waits:]
    for column in range(0, D, LANES):
        kt_scr[column : column + LANES, :] = turned(kn[:, column : column + LANES])
    for column in range(0, vt.shape[1], BLOCK):
        vn_scr[column : column + BLOCK, :] = turned(vt[:, column : column + BLOCK])

    steps = [(head, slice(at, at + BLOCK)) for head in range(HEADS) for at in range(0, kn.shape[0], BLOCK)]

    def score(head, at):
        columns = pair_columns(head)
        rows = head_rows(head)
        return nn(kn[at, columns], padded(q[rows, :], head)), nn(vn_scr[at, columns], padded(d_out[rows, :], head))

    totals = {}

    def finish(head, at, probs, score_grads):
        rows = head_rows(head)
        d_kv[D + rows.start : D + rows.stop, at] = nt(d_out[rows, :], probs).astype(d_kv.dtype)
        d_kv[rows, at] = nt(q[rows, :], score_grads).astype(d_kv.dtype)
        term = nn(kt_scr[rows, at], score_grads)
        if head not in totals:
            totals[head] = before[rows, :] + term if has_before else term
            return
        term = totals[head] + term
        if has_before:
            term = term * HEAD_DIM ** (-0.5)
        dq_out[rows, :] = term.astype(dq_out.dtype)

    waiting = None
    following = score(*steps[0])
    for place, (head, at) in enumerate(steps):
        scores, prob_grads = following
        if place + 1 < len(steps):
            following = score(*steps[place + 1])
        if waiting is not None:
            finish(*waiting)
        probs = jnp.exp(scores - lse[head : head + 1, :])
        score_grads = (probs * (prob_grads - centre[head : head + 1, :])).astype(BF16)
        waiting = (head, at, probs.astype(BF16), score_grads)
    finish(*waiting)


def split_kernel(waits, where, *refs):
    *halves, keep, sent, total_scr = refs[waits:]
    rows_half = keep.shape[0]
    at = 0
    for mine, other in zip(halves[::2], halves[1::2]):
        rows = mine.shape[0]
        total_scr[at : at + rows, :] = mine[...] + other[...].astype(F32)
        at += rows
    if at < total_scr.shape[0]:
        total_scr[at:, :] = jnp.zeros((total_scr.shape[0] - at, LANES), F32)
    odd = where[3]
    keep[...] = total_scr[pl.ds(pl.multiple_of(odd * rows_half, 16), rows_half), :]
    sent[...] = total_scr[pl.ds(pl.multiple_of((1 - odd) * rows_half, 16), rows_half), :].astype(BF16)


def pair_sum_kernel(late, *refs):
    count = len(refs) // 3
    for keep, got, out in zip(refs[:count], refs[count : 2 * count], refs[2 * count :]):
        out[...] = (keep[...].astype(F32) + got[...].astype(F32)).astype(BF16)


def put_lines(out, row, values):
    ones = jnp.ones((16, LANES), BF16)
    high = values.astype(BF16)
    low = (values - high.astype(F32)).astype(BF16)
    line = (nt(ones, high) + nt(ones, low))[0:1]
    for column in range(0, line.shape[1], LANES):
        out[row : row + 1, :] = line[:, column : column + LANES]
        row += 1
    return row


def lines_kernel(early, context, *refs):
    *sums, out = refs
    out[...] = jnp.zeros_like(out)
    row = 2 * D // LANES
    for ref in sums:
        row = put_lines(out, row, ref[...])
    for column in range(0, D, LANES):
        out[row : row + 1, :] = context[0:1, column : column + LANES].astype(F32)
        row += 1


def join_kernel(sum_count, early, mine, sums, got, out):
    rows = mine.shape[0]
    out[:rows, :] = (mine[...] + got[:rows, :].astype(F32)).astype(BF16)
    other = got[rows:, :].astype(F32)
    summed = lax.broadcasted_iota(jnp.int32, (SUM_ROWS, LANES), 0) < sum_count
    out[rows:, :] = (sums[...] + jnp.where(summed, other, 0.0)).astype(BF16)


def pair_kernel(rows, where, own, got, out):
    out[:rows, :] = (own[:rows, :].astype(F32) + got[:rows, :].astype(F32)).astype(BF16)
    odd = where[3]
    size = SUM_ROWS
    out[pl.ds(pl.multiple_of(rows + odd * size, 16), size), :] = own[rows:, :]
    out[pl.ds(pl.multiple_of(rows + (1 - odd) * size, 16), size), :] = got[rows:, :]


def gather_kernel(where, *refs):
    halves, (out_out, up_out, down_out, qkv_out), scratch = refs[:4], refs[4:8], refs[8:]
    odd = where[3]
    for ref, own, got in zip(scratch, halves[::2], halves[1::2]):
        rows = own.shape[0]
        ref[pl.ds(pl.multiple_of(odd * rows, 16), rows), :] = own[...]
        ref[pl.ds(pl.multiple_of((1 - odd) * rows, 16), rows), :] = got[...]
    slice_rows = out_out.shape[1]
    for index, ref in enumerate(scratch):
        at = 0
        for out in (down_out, up_out, out_out):
            rows = out.shape[1]
            for column in range(0, out.shape[2], LANES):
                out[index, :, column : column + LANES] = ref[at : at + rows, :].astype(F32)
                at += rows
        if index == 0:
            for column in range(0, qkv_out.shape[1], LANES):
                qkv_out[:, column : column + LANES] = ref[at : at + slice_rows, :].astype(F32)
                at += slice_rows


def finish_kernel(item_count, where, own, got, qkv_1, qkv_out, ada_out, bias_out, shift_out, sum_scr, bias_scr, shift_scr):
    layers = 2
    device, first_weight, second_weight = where[0], where[5], where[6]
    slice_rows = qkv_out.shape[1]
    close_rows = slice_rows * (3 * D // LANES)
    for other in range(2):
        rows = slice(close_rows + other * SUM_ROWS, close_rows + (other + 1) * SUM_ROWS)
        sum_scr[first_weight * other + second_weight * where[4]] = own[rows, :].astype(F32)
        sum_scr[first_weight * other + second_weight * (1 - where[4])] = got[rows, :].astype(F32)
    qkv_out[1] = qkv_1[...]
    for tile in range(3 * D // LANES):
        rows = slice(tile * slice_rows, (tile + 1) * slice_rows)
        total = own[rows, :].astype(F32) + got[rows, :].astype(F32)
        qkv_out[0, :, tile * LANES : (tile + 1) * LANES] = total
    tiles = 6 * D // LANES
    contexts = []
    for other in range(item_count):
        line = jnp.concatenate([sum_scr[other, layers * tiles + c : layers * tiles + c + 1, :] for c in range(3)], axis=1)
        contexts.append(line)
    square = jnp.concatenate(contexts + [jnp.zeros((8 - item_count, D), F32)], axis=0)
    spot = lax.broadcasted_iota(jnp.int32, (slice_rows, D), 1)
    want = lax.broadcasted_iota(jnp.int32, (slice_rows, D), 0) + device * slice_rows
    pick = jnp.where(spot == want, 1.0, 0.0).astype(BF16)
    columns = nt(pick, square.astype(BF16))
    bias_rows = bias_out.shape[1]
    for index in range(layers):
        flats = []
        for tile in range(tiles):
            row = index * tiles + tile
            total = None
            flat = None
            for other in range(item_count):
                line = sum_scr[other, row : row + 1, :]
                term = columns[:, other : other + 1] * line
                total = term if total is None else total + term
                flat = line if flat is None else flat + line
            ada_out[index, :, tile * LANES : (tile + 1) * LANES] = total
            flats.append(flat)
        flat = jnp.concatenate(flats, axis=1)
        for place in range(flat.shape[1] // bias_rows):
            bias_scr[place, index : index + 1, :] = flat[:, place * bias_rows : (place + 1) * bias_rows]
            at = 3 * D + place * slice_rows
            shift_scr[place, index : index + 1, :] = flat[:, at : at + slice_rows]
    bias_out[...] = bias_scr[device]
    shift_out[...] = shift_scr[device]


VMEM = pl.BlockSpec(memory_space=pltpu.VMEM)
SMEM = pl.BlockSpec(memory_space=pltpu.SMEM)
ANY = pl.BlockSpec(memory_space=pl.ANY)
HBM = pl.BlockSpec(memory_space=pltpu.HBM)


def layer_block(array, index):
    return pl.BlockSpec((None,) + array.shape[1:], lambda step: (index,) + (0,) * (array.ndim - 1))


def call(body, args, outs, scratch=(), flops=0, name=None):
    arrays = [arg[0] if isinstance(arg, tuple) else arg for arg in args]
    specs = [arg[1] if isinstance(arg, tuple) else VMEM for arg in args]
    return pl.pallas_call(
        body,
        out_shape=[jax.ShapeDtypeStruct(shape, kind) for shape, kind in outs],
        in_specs=specs,
        out_specs=[VMEM] * len(outs),
        scratch_shapes=[one if not isinstance(one, tuple) else pltpu.VMEM(*one) for one in scratch],
        compiler_params=pltpu.CompilerParams(vmem_limit_bytes=VMEM_LIMIT),
        cost_estimate=pl.CostEstimate(flops=flops, bytes_accessed=0, transcendentals=0),
        name=name,
    )(*arrays)


VMEM_LIMIT = 16 * 1024 * 1024


def fast_shards(
    lat_count, lon_count, item_count,
    fields, lead_index, rollout, w_qkv, w_out, w_up, w_down, w_ada, b_ada, cotangent,
):
    _, rows_dev, cols_dev, width = fields.shape
    local = rows_dev * cols_dev
    layers = w_qkv.shape[0]
    ff = w_up.shape[2]
    patches = 4 * local
    device = lax.axis_index("lat") * lon_count + lax.axis_index("lon")
    item = lax.axis_index("item")
    core = device & 1
    bits = [jnp.where(core == 0, item & 1, item >> 1), jnp.where(core == 0, item >> 1, item & 1)]
    where = jnp.stack([device, device ^ 1, item, *bits, 1 + core, 2 - core]).astype(jnp.int32)
    active = (1 < rollout[0]).astype(F32)[None]

    def plane_flip(value, flip_lat, flip_y):
        pairs = [
            (a * lon_count + b, (a ^ flip_lat) * lon_count + (b ^ (2 * flip_y)))
            for a in range(lat_count)
            for b in range(lon_count)
        ]
        return lax.ppermute(value, ("lat", "lon"), pairs)

    def swap(value):
        return lax.ppermute(value, "lon", [(index, index ^ 1) for index in range(lon_count)])

    def with_item(value, phase):
        pairs = []
        for index in range(item_count):
            for lon in range(lon_count):
                flip = 1 if lon % 2 == phase % 2 else 2
                pairs.append((index * lon_count + lon, (index ^ flip) * lon_count + lon))
        return lax.ppermute(value, ("item", "lon"), pairs)

    def plane_parts(value):
        return [value, plane_flip(value, 1, 0), plane_flip(value, 0, 1), plane_flip(value, 1, 1)]

    cot_parts = plane_parts(cotangent.reshape(local, width))

    context = jax.nn.silu(embedding(lead_index[0])).astype(BF16)
    context = jnp.broadcast_to(context[None, :], (16, width))
    square = (width, patches)
    natural = (patches, width)
    weights = (w_qkv, w_ada, b_ada, w_out, w_up, w_down)
    weights = [(pltpu.with_memory_space_constraint(value, pltpu.HBM), HBM) for value in weights]
    first_fetch = [((width, 3 * width), BF16), ((width, 6 * width), BF16), (b_ada.shape, F32)]
    rest_fetch = [((width, width), BF16), ((width, ff), BF16), ((ff, width), BF16)]
    first_outs = [((6 * width, LANES), F32)] + [((width, width), BF16)] * 3
    rest_outs = [((width, width), BF16), ((ff, width), BF16), ((width, ff), BF16)]
    own = pltpu.with_memory_space_constraint(fields.reshape(local, width), pltpu.HBM)
    *first_0, own = call(
        prepare_start_kernel,
        [context, *weights, (own, HBM), (where, SMEM), (active, SMEM)],
        first_outs + [((local, width), BF16)],
        first_fetch + [pltpu.SemaphoreType.DMA((3,)), pltpu.SemaphoreType.DMA],
        name="prepare_start",
    )
    field_parts = plane_parts(own)
    both = call(
        functools.partial(prepare_kernel, 1, 0, 1),
        [context, *weights, (own, ANY)],
        first_outs + rest_outs,
        rest_fetch + first_fetch + [pltpu.SemaphoreType.DMA((6,))],
        name="prepare_both",
    )
    first_parts = [first_0, both[:4]]
    mods = [one[0] for one in first_parts]

    project_outs = [(square, F32), (square, BF16), (square, BF16), (natural, BF16), (square, BF16)]
    dense_flops = 2 * patches * (width * 3 * width + width * width + 2 * width * ff)
    score_flops = 2 * patches * 2 * patches * width * 4
    x, xb, *projected = call(
        first_kernel,
        [(both[0], ANY), *field_parts, *first_parts[0]],
        project_outs,
        flops=2 * patches * width * 4 * width,
        name="first",
    )
    rest_1 = call(
        functools.partial(prepare_kernel, None, 1, 1),
        [context, *weights, (x, ANY)],
        rest_outs,
        rest_fetch + [pltpu.SemaphoreType.DMA((3,))],
        name="prepare_rest",
    )
    rest_parts = [both[4:], rest_1]
    saved = []
    for step in range(STEPS):
        for index in range(layers):
            q, kn, vt = projected
            kn_far, vt_far = swap(kn), swap(vt)
            last = step == STEPS - 1 and index == layers - 1
            if index == 0 and step > 0:
                x_step = x
            following = list(first_parts[(index + 1) % layers])
            lse, mixed, attended, middle, hidden, slope, branch, *results = call(
                functools.partial(forward_kernel, last),
                ([(active, SMEM), x, x_step] if last else [x])
                + [q, kn, kn_far, vt, vt_far, mods[index], *rest_parts[index]]
                + ([] if last else following),
                [
                    ((HEADS, patches), F32),
                    (square, BF16),
                    (square, BF16),
                    (square, BF16),
                    ((ff, patches), BF16),
                    ((ff, patches), BF16),
                    (square, BF16),
                ]
                + ([((local, width), F32)] if last else project_outs),
                flops=dense_flops + 2 * score_flops,
                name="forward",
            )
            saved.append((xb, [mixed, attended, middle, hidden, slope, branch], (q, kn, kn_far, vt, vt_far, lse)))
            if last:
                final = results[0]
            else:
                x, xb, *projected = results

    slice_rows = width // 8
    open_rows = 2 * (ff // 8) * (width // LANES) + slice_rows * (width // LANES)
    close_rows = slice_rows * (3 * width // LANES)
    order = [(step, index) for step in reversed(range(STEPS)) for index in reversed(range(layers))]
    open_done = [None] * layers
    close_done = [None] * layers
    pending = None
    for place in range(len(order) + 1):
        has_close = pending is not None
        has_open = place < len(order)
        use = [order[place - 1][1], order[place][1] if has_open else 0]
        waits = []
        if has_close and close_done[use[0]]:
            waits = [pair_1] if has_open else [item_got_1]
        args = [(value, ANY) for value in waits] + [(where, SMEM), (active, SMEM)]
        outs = []
        scratch = []
        has_before = [False, False]
        start = ""
        if has_close:
            args += pending
            if close_done[use[0]] is not None:
                has_before[0] = True
                args += close_done[use[0]]
            outs += [((close_rows, LANES), F32)]
            sent_rows = close_rows + (0 if has_open else SUM_ROWS)
            outs += [((sent_rows, LANES), BF16 if has_before[0] else F32), ((2 * width, LANES), F32)]
            scratch += [((3 * width, patches), BF16), (square, BF16)]
        if place == 0:
            start = "first"
            args += cot_parts
            outs += [(square, BF16)]
        elif has_open and order[place][0] != order[place - 1][0]:
            start = "cross"
            args += [cot_t]
        if has_open:
            step, index = order[place]
            xb, kept, heads = saved[step * layers + index]
            args += kept + [mods[index], w_out, w_up, w_down]
            if open_done[index] is not None:
                has_before[1] = True
                args += open_done[index]
            outs += [
                ((open_rows, LANES), F32),
                ((open_rows, LANES), BF16 if has_before[1] else F32),
                ((4 * width, LANES), F32),
                (square, F32),
                (square, BF16),
                ((HEADS, patches), F32),
            ]
            scratch += [(square, BF16), ((ff, patches), BF16), (square, BF16), (square, BF16)]
        else:
            args += [lines]
            outs += [((local, width), F32), ((SUM_ROWS, LANES), F32)]
        results = list(
            call(
                functools.partial(dense_back_kernel, has_close, has_open, has_before, start, use, len(waits)),
                args,
                outs,
                scratch,
                flops=2 * dense_flops if has_open else 0,
                name="dense_back" if has_open else "close_back",
            )
        )
        if has_close:
            close_done[use[0]] = results[:3]
            del results[:3]
        if start == "first":
            cot_t = results.pop(0)
        if not has_open:
            gradient, line = results
            break
        open_done[index] = results[:3]
        d_mid, d_out, centre = results[3:]
        q, kn, kn_far, vt, vt_far, lse = heads
        halves = [open_done[index][0], open_done[index][1]]
        if index == 0:
            halves += [close_done[1][0], close_done[1][1]]
        half_rows = -(-sum(half.shape[0] for half in halves[::2]) // 32) * 16

        def split(waits):
            pieces = [half if place % 2 == 0 else swap(half) for place, half in enumerate(halves)]
            return call(
                functools.partial(split_kernel, len(waits)),
                [(where, SMEM), *waits, *pieces],
                [((half_rows, LANES), F32), ((half_rows, LANES), BF16)],
                [((2 * half_rows, LANES), F32)],
                name="split",
            )

        def pair_sum(late, keeps, gots):
            outs = [(keep.shape, BF16) for keep in keeps]
            return call(pair_sum_kernel, [(late, ANY), *keeps, *gots], outs, name="pair_sum")

        waits = []
        if has_before[1] and index == 0:
            pair_got_1 = with_item(pair_1, 1)
            lines = call(
                lines_kernel,
                [(pair_got_1, ANY), context, open_done[0][2], close_done[1][2], open_done[1][2]],
                [((SUM_ROWS, LANES), F32)],
                flops=10 * score_flops,
                name="lines",
            )[0]
            keep, sent = split([(lines, ANY)])
            got_0 = with_item(sent, 0)
            waits = [keep]
        d_far, dq = call(
            functools.partial(attend_back_kernel, False, len(waits)),
            [q, kn_far, vt_far, lse, d_out, centre] + [(value, ANY) for value in waits],
            [((2 * width, patches), BF16), (square, F32)],
            [(square, BF16), (natural, BF16)],
            flops=10 * score_flops,
            name="attend_far",
        )
        d_got = swap(d_far)
        waits = []
        if has_before[1]:
            if index == 1:
                keep, sent = split([(d_far, ANY)])
                got_1 = with_item(sent, 0)
                waits = [keep]
            else:
                pair_0, item_1 = pair_sum(d_far, [keep, pair_1], [got_0, pair_got_1])
                item_got_1 = with_item(item_1, 0)
                pair_got_0 = with_item(pair_0, 1)
                waits = [pair_0]
        d_own, dq = call(
            functools.partial(attend_back_kernel, True, len(waits)),
            [q, kn, vt, lse, d_out, centre, dq] + [(value, ANY) for value in waits],
            [((2 * width, patches), F32), (square, BF16)],
            [(square, BF16), (natural, BF16)],
            flops=10 * score_flops,
            name="attend_own",
        )
        if has_before[1] and index == 1:
            (pair_1,) = pair_sum(dq, [keep], [got_1])
        pending = [d_own, d_got, dq, d_mid, xb, mods[index], w_qkv]

    message = call(
        functools.partial(join_kernel, layers * 6 * width // LANES),
        [(pair_got_0, ANY), close_done[0][0], line, swap(close_done[0][1])],
        [((close_rows + SUM_ROWS, LANES), BF16)],
        name="join",
    )[0]
    message_got = with_item(message, 0)
    (item_0,) = pair_sum(message_got, [pair_0], [pair_got_0])
    message = call(
        functools.partial(pair_kernel, close_rows),
        [(where, SMEM), message, message_got],
        [((close_rows + 2 * SUM_ROWS, LANES), BF16)],
        name="pair",
    )[0]
    out_grad, up_grad, down_grad, qkv_1 = call(
        gather_kernel,
        [(where, SMEM), item_0, with_item(item_0, 0), item_1, item_got_1],
        [
            ((layers, slice_rows, width), F32),
            ((layers, slice_rows, ff), F32),
            ((layers, ff // 8, width), F32),
            ((slice_rows, 3 * width), F32),
        ],
        [((2 * pair.shape[0], LANES), BF16) for pair in (pair_0, pair_1)],
        name="gather",
    )
    bias_rows = 6 * width // 8
    qkv_grad, ada_grad, bias_grad, shift_grad = call(
        functools.partial(finish_kernel, item_count),
        [(where, SMEM), message, with_item(message, 1), qkv_1],
        [
            ((layers, slice_rows, 3 * width), F32),
            ((layers, slice_rows, 6 * width), F32),
            ((layers, bias_rows), F32),
            ((layers, slice_rows), F32),
        ],
        [
            ((item_count, SUM_ROWS, LANES), F32),
            ((8, layers, bias_rows), F32),
            ((8, layers, slice_rows), F32),
        ],
        name="finish",
    )
    field_shape = (1, rows_dev, cols_dev, width)
    return (
        final.reshape(field_shape),
        gradient.reshape(field_shape),
        qkv_grad,
        out_grad,
        up_grad,
        down_grad,
        ada_grad,
        bias_grad,
        shift_grad,
    )


def solution(mesh):
    lat_count, lon_count, item_count = mesh.shape["lat"], mesh.shape["lon"], mesh.shape["item"]
    if lat_count == 2 and lon_count == 4:
        body = functools.partial(fast_shards, lat_count, lon_count, item_count)
    else:
        body = shards
    return jax.shard_map(
        body,
        mesh=mesh,
        in_specs=(
            P("item", "lat", "lon", None),
            P("item"),
            P("item"),
            P(),
            P(),
            P(),
            P(),
            P(),
            P(),
            P("item", "lat", "lon", None),
        ),
        out_specs=(
            P("item", "lat", "lon", None),
            P("item", "lat", "lon", None),
            P(None, ("lat", "lon"), None),
            P(None, ("lat", "lon"), None),
            P(None, ("lat", "lon"), None),
            P(None, ("lat", "lon"), None),
            P(None, ("lat", "lon"), None),
            P(None, ("lat", "lon")),
            P(None, ("lat", "lon")),
        ),
        check_vma=False,
    )
```

```python
import functools
import math

import jax
import jax.numpy as jnp
from jax import lax
from jax.experimental import pallas as pl
from jax.experimental.pallas import tpu as pltpu
from jax.sharding import PartitionSpec as P

D = 384
HEADS = 6
HEAD_DIM = 64
STEPS = 2


def shortened(shard):
    return jax.tree.map(lambda a: a.astype(jnp.bfloat16) if a.dtype == jnp.float32 else a, shard)


def embedding(lead):
    half_width = D // 2
    lead_hours = 6.0 * (lead.astype(jnp.float32) + 1.0)
    frequencies = jnp.exp(
        -math.log(10000.0) * jnp.arange(half_width, dtype=jnp.float32) / half_width
    )
    angles = lead_hours * frequencies
    return jnp.concatenate([jnp.sin(angles), jnp.cos(angles)])


def pre_norm(values, shift_part, scale_part):
    centred = values - jnp.mean(values, axis=-1, keepdims=True)
    variance = jnp.mean(centred * centred, axis=-1, keepdims=True)
    return centred * lax.rsqrt(variance + 1e-06) * (1.0 + scale_part) + shift_part


def gather_keys(keys_values):
    band_rows = lax.all_gather(keys_values, "lon", axis=0, tiled=True)
    return lax.all_gather(band_rows, "lat", axis=0, tiled=True)


def spread_keys(key_value_grads):
    band_grads = lax.psum_scatter(
        key_value_grads.astype(jnp.bfloat16), "lat", scatter_dimension=0, tiled=True
    )
    return lax.psum_scatter(band_grads, "lon", scatter_dimension=0, tiled=True).astype(jnp.float32)


def forward_layer(current, modulation, weight_qkv, weight_out, weight_up, weight_down):
    local_rows, width = current.shape
    shift_attn, scale_attn, gate_attn, shift_mlp, scale_mlp, gate_mlp = modulation
    normed = pre_norm(current, shift_attn, scale_attn).astype(jnp.bfloat16)
    projected = jnp.dot(normed, weight_qkv, preferred_element_type=jnp.float32).astype(jnp.bfloat16)
    queries = projected[:, :width].reshape(local_rows, HEADS, HEAD_DIM)
    own_keys = projected[:, width:]
    gathered = gather_keys(own_keys)
    total_rows = gathered.shape[0]
    key_heads = gathered[:, :width].reshape(total_rows, HEADS, HEAD_DIM)
    value_heads = gathered[:, width:].reshape(total_rows, HEADS, HEAD_DIM)
    scores = jnp.einsum(
        "thd,nhd->htn", queries, key_heads, preferred_element_type=jnp.float32
    ) * HEAD_DIM ** (-0.5)
    log_total = jax.nn.logsumexp(scores, axis=-1, keepdims=True)
    probabilities = jnp.exp(scores - log_total).astype(jnp.bfloat16)
    mixed = jnp.einsum(
        "htn,nhd->thd", probabilities, value_heads, preferred_element_type=jnp.float32
    )
    mixed = mixed.reshape(local_rows, width).astype(jnp.bfloat16)
    attended = jnp.dot(mixed, weight_out, preferred_element_type=jnp.float32)
    middle = current + gate_attn * attended
    hidden_in = pre_norm(middle, shift_mlp, scale_mlp).astype(jnp.bfloat16)
    pre_act = jnp.dot(hidden_in, weight_up, preferred_element_type=jnp.float32)
    hidden = jax.nn.gelu(pre_act).astype(jnp.bfloat16)
    branch = jnp.dot(hidden, weight_down, preferred_element_type=jnp.float32)
    output = middle + gate_mlp * branch
    kept = (
        current,
        normed,
        queries,
        gathered,
        own_keys,
        log_total,
        mixed,
        attended,
        middle,
        hidden_in,
        pre_act,
        hidden,
        branch,
    )
    return (output, kept)


def backward_layer(grad_out, kept, modulation, weight_qkv, weight_out, weight_up, weight_down):
    (
        current,
        normed,
        queries,
        gathered,
        own_keys,
        log_total,
        mixed,
        attended,
        middle,
        hidden_in,
        pre_act,
        hidden,
        branch,
    ) = kept
    local_rows, width = current.shape
    total_rows = gathered.shape[0]
    shift_attn, scale_attn, gate_attn, shift_mlp, scale_mlp, gate_mlp = modulation
    factor = HEAD_DIM ** (-0.5)
    branch_grad = (gate_mlp * grad_out).astype(jnp.bfloat16)
    gate_mlp_grad = jnp.sum(grad_out * branch, axis=0)
    hidden_grad = jnp.dot(branch_grad, weight_down.T, preferred_element_type=jnp.float32)
    down_grad = jnp.dot(hidden.T, branch_grad, preferred_element_type=jnp.float32)
    _, gelu_back = jax.vjp(jax.nn.gelu, pre_act)
    pre_grad = gelu_back(hidden_grad)[0].astype(jnp.bfloat16)
    hidden_in_grad = jnp.dot(pre_grad, weight_up.T, preferred_element_type=jnp.float32)
    up_grad = jnp.dot(hidden_in.T, pre_grad, preferred_element_type=jnp.float32)
    _, second_back = jax.vjp(pre_norm, middle, shift_mlp, scale_mlp)
    middle_part, shift_mlp_grad, scale_mlp_grad = second_back(hidden_in_grad)
    middle_grad = grad_out + middle_part
    attended_grad = (gate_attn * middle_grad).astype(jnp.bfloat16)
    gate_attn_grad = jnp.sum(middle_grad * attended, axis=0)
    mixed_grad = jnp.dot(attended_grad, weight_out.T, preferred_element_type=jnp.float32).astype(
        jnp.bfloat16
    )
    out_grad = jnp.dot(mixed.T, attended_grad, preferred_element_type=jnp.float32)
    mixed_heads = mixed_grad.reshape(local_rows, HEADS, HEAD_DIM)
    key_heads = gathered[:, :width].reshape(total_rows, HEADS, HEAD_DIM)
    value_heads = gathered[:, width:].reshape(total_rows, HEADS, HEAD_DIM)
    scores = (
        jnp.einsum("thd,nhd->htn", queries, key_heads, preferred_element_type=jnp.float32) * factor
    )
    probabilities = jnp.exp(scores - log_total)
    prob_grads = jnp.einsum(
        "thd,nhd->htn", mixed_heads, value_heads, preferred_element_type=jnp.float32
    )
    centre = jnp.sum(prob_grads * probabilities, axis=-1, keepdims=True)
    score_grads = (probabilities * (prob_grads - centre)).astype(jnp.bfloat16)
    query_grads = (
        jnp.einsum("htn,nhd->thd", score_grads, key_heads, preferred_element_type=jnp.float32)
        * factor
    )
    value_grads = jnp.einsum(
        "htn,thd->nhd",
        probabilities.astype(jnp.bfloat16),
        mixed_heads,
        preferred_element_type=jnp.float32,
    )
    key_grads = (
        jnp.einsum("htn,thd->nhd", score_grads, queries, preferred_element_type=jnp.float32)
        * factor
    )
    key_value_grads = jnp.concatenate(
        [key_grads.reshape(total_rows, width), value_grads.reshape(total_rows, width)], axis=1
    )
    local_grads = spread_keys(key_value_grads)
    projected_grad = jnp.concatenate(
        [query_grads.reshape(local_rows, width), local_grads], axis=1
    ).astype(jnp.bfloat16)
    normed_grad = jnp.dot(projected_grad, weight_qkv.T, preferred_element_type=jnp.float32)
    qkv_grad = jnp.dot(normed.T, projected_grad, preferred_element_type=jnp.float32)
    _, first_back = jax.vjp(pre_norm, current, shift_attn, scale_attn)
    current_part, shift_attn_grad, scale_attn_grad = first_back(normed_grad)
    input_grad = middle_grad + current_part
    modulation_grad = jnp.concatenate(
        [
            shift_attn_grad,
            scale_attn_grad,
            gate_attn_grad,
            shift_mlp_grad,
            scale_mlp_grad,
            gate_mlp_grad,
        ]
    )
    return (input_grad, (qkv_grad, out_grad, up_grad, down_grad, modulation_grad))


def shards(fields, lead_index, rollout, w_qkv, w_out, w_up, w_down, w_ada, b_ada, cotangent):
    _, rows_dev, cols_dev, width = fields.shape
    local_rows = rows_dev * cols_dev
    layer_count = w_qkv.shape[0]
    context = jax.nn.silu(embedding(lead_index[0])).astype(jnp.bfloat16)
    context_wide = context.astype(jnp.float32)
    modulations = [
        (
            jnp.dot(context[None, :], w_ada[index], preferred_element_type=jnp.float32)[0]
            + b_ada[index]
        ).reshape(6, width)
        for index in range(layer_count)
    ]
    weight_sets = [
        (w_qkv[index], w_out[index], w_up[index], w_down[index]) for index in range(layer_count)
    ]
    count = rollout[0]
    current = fields.reshape(local_rows, width).astype(jnp.float32)
    saved = []
    for rollout_step in range(STEPS):
        updated = current
        kept_layers = []
        for index in range(layer_count):
            updated, kept = forward_layer(updated, modulations[index], *weight_sets[index])
            kept_layers.append(kept)
        current = jnp.where(rollout_step < count, updated, current)
        saved.append(kept_layers)
    gradient = cotangent.reshape(local_rows, width).astype(jnp.float32)
    summed = None
    shares = None
    for rollout_step in reversed(range(STEPS)):
        active = (rollout_step < count).astype(jnp.float32)
        inner = gradient * active
        layer_terms = [None] * layer_count
        for index in reversed(range(layer_count)):
            inner, layer_terms[index] = backward_layer(
                inner, saved[rollout_step][index], modulations[index], *weight_sets[index]
            )
        gradient = inner + (1.0 - active) * gradient
        modulation_grads = jnp.stack([terms[4] for terms in layer_terms])
        step_terms = (
            jnp.stack([terms[0] for terms in layer_terms]),
            jnp.stack([terms[1] for terms in layer_terms]),
            jnp.stack([terms[2] for terms in layer_terms]),
            jnp.stack([terms[3] for terms in layer_terms]),
            context_wide[None, :, None] * modulation_grads[:, None, :],
            modulation_grads,
            modulation_grads[:, 3 * width : 4 * width],
        )
        summed = step_terms if summed is None else jax.tree.map(jnp.add, summed, step_terms)
    shares = lax.psum_scatter(summed, ("lat", "lon"), scatter_dimension=1, tiled=True)
    totals = jax.tree.map(
        lambda part: part.astype(jnp.float32), lax.psum(shortened(shares), "item")
    )
    return (
        current.reshape(1, rows_dev, cols_dev, width),
        gradient.reshape(1, rows_dev, cols_dev, width),
        totals[0],
        totals[1],
        totals[2],
        totals[3],
        totals[4],
        totals[5],
        totals[6],
    )


F32 = jnp.float32
BF16 = jnp.bfloat16
GELU_A = math.sqrt(2.0 / math.pi)
GELU_B = 0.044715
LANES = 128
BLOCK = 256
PAIR = 2 * HEAD_DIM
SUM_ROWS = 48
ONES = 16
SAFE_SCORE = 60.0


def nn(left, right, precision=None):
    return lax.dot_general(
        left, right, (((1,), (0,)), ((), ())), preferred_element_type=F32, precision=precision
    )


def nt(left, right, precision=None):
    return lax.dot_general(
        left, right, (((1,), (1,)), ((), ())), preferred_element_type=F32, precision=precision
    )


def identity(size):
    rows = lax.broadcasted_iota(jnp.int32, (size, size), 0)
    columns = lax.broadcasted_iota(jnp.int32, (size, size), 1)
    return jnp.where(rows == columns, 1.0, 0.0).astype(BF16)


def turned(values):
    return nt(identity(values.shape[1]), values).astype(BF16)


def wide(column_tile, lanes):
    return jnp.concatenate([column_tile] * (lanes // LANES), axis=1)


def folded(values):
    pieces = [values[:, at : at + LANES] for at in range(0, values.shape[1], LANES)]
    return sum(pieces[1:], pieces[0])


def standardise(values):
    rows = values.shape[0]
    centred = values - jnp.sum(values, axis=0, keepdims=True) * (1.0 / rows)
    variance = jnp.sum(centred * centred, axis=0, keepdims=True) * (1.0 / rows)
    scale = lax.rsqrt(variance + 1e-06)
    return centred * scale, scale


def pre_norm_back(standard, scale, grad, gain):
    rows = standard.shape[0]
    inner = grad * gain
    first = jnp.sum(inner, axis=0, keepdims=True) * (1.0 / rows)
    second = jnp.sum(inner * standard, axis=0, keepdims=True) * (1.0 / rows)
    return scale * (inner - first - standard * second)


def part(mod_ref, index, lanes):
    return wide(mod_ref[index * D : (index + 1) * D, :], lanes)


def turn_into(source, out, at=0):
    for column in range(0, out.shape[0], BLOCK):
        width = min(BLOCK, out.shape[0] - column)
        out[column : column + width, :] = turned(source[:, at + column : at + column + width])


def prepare_first_kernel(index, between, waits, context, w_ada, b_ada, w_qkv, *refs):
    mod, w_q_t, w_v_t, w_k, *scratch, sems = refs[waits:]
    copies = [
        pltpu.make_async_copy(source, target, sems.at[place])
        for place, (source, target) in enumerate(zip((w_qkv.at[index], w_ada.at[index], b_ada), scratch))
    ]
    for copy in copies:
        copy.start()
    if between:
        between()
    w_qkv, w_ada, b_ada = scratch
    copies[0].wait()
    w_k[...] = w_qkv[:, D : 2 * D]
    turn_into(w_qkv, w_q_t)
    turn_into(w_qkv, w_v_t, 2 * D)
    copies[1].wait()
    copies[2].wait()
    values = nn(context[...], w_ada[...])[0:1] + b_ada[index : index + 1, :]
    for column in range(0, values.shape[1], LANES):
        tile = jnp.broadcast_to(values[:, column : column + LANES], (LANES, LANES))
        mod[column : column + LANES, :] = tile.T


def prepare_rest_kernel(index, early, w_out, w_up, w_down, *outs):
    for weight, out in zip((w_out, w_up, w_down), outs):
        turn_into(weight.at[index], out)


def prepare_both_kernel(early, context, w_ada, b_ada, w_qkv, w_out, w_up, w_down, *refs):
    between = functools.partial(prepare_rest_kernel, 0, early, w_out, w_up, w_down, *refs[4:7])
    prepare_first_kernel(1, between, 0, context, w_ada, b_ada, w_qkv, *refs[:4], *refs[7:])


def project(x, mod_ref, w_q_t, w_v_t, w_k, outs):
    q_out, kn_out, vt_out = outs
    lanes = x.shape[1]
    standard, _ = standardise(x)
    normed = (standard * (1.0 + part(mod_ref, 1, lanes)) + part(mod_ref, 0, lanes)).astype(BF16)
    vt_out[...] = nn(w_v_t[...], normed).astype(BF16)
    q_out[...] = (nn(w_q_t[...], normed) * HEAD_DIM ** (-0.5)).astype(BF16)
    for at in range(0, lanes, BLOCK):
        kn_out[at : at + BLOCK, :] = nn(turned(normed[:, at : at + BLOCK]), w_k[...]).astype(BF16)


def first_kernel(own, flip_x, flip_y, flip_xy, mod, w_q_t, w_v_t, w_k, x_out, xb_out, *outs):
    for index, ref in enumerate((own, flip_x, flip_y, flip_xy)):
        rows = ref.shape[0]
        flat = turned(ref[...])
        xb_out[:, index * rows : (index + 1) * rows] = flat
        x_out[:, index * rows : (index + 1) * rows] = flat.astype(F32)
    project(x_out[...], mod, w_q_t, w_v_t, w_k, outs)


def head_rows(head):
    return slice(head * HEAD_DIM, (head + 1) * HEAD_DIM)


def pair_columns(head):
    return slice(head // 2 * PAIR, (head // 2 + 1) * PAIR)


def padded(rows, head):
    zeros = jnp.zeros_like(rows)
    return jnp.concatenate([rows, zeros] if head % 2 == 0 else [zeros, rows], axis=0)


def score_bound(q, *kns):
    tops = [jnp.max(jnp.abs(kn[...].astype(F32)), axis=0, keepdims=True) for kn in kns]
    top = functools.reduce(jnp.maximum, tops) * 1.01
    first = lax.broadcasted_iota(jnp.int32, (16, D), 0) * HEAD_DIM
    column = lax.broadcasted_iota(jnp.int32, (16, D), 1)
    weights = jnp.where((column >= first) & (column < first + HEAD_DIM), top, 0.0).astype(BF16)
    return jnp.max(nn(weights, jnp.abs(q[...].astype(F32)).astype(BF16)))


def value_rows(vt, rows, at):
    values = vt[rows, at]
    return jnp.concatenate([values, jnp.ones((ONES, values.shape[1]), BF16)], axis=0)


def attend_plain(q, kn, vt, put):
    steps = [(head, slice(at, at + BLOCK)) for head in range(HEADS) for at in range(0, kn.shape[0], BLOCK)]
    last_at = steps[-1][1]

    def score(head, at):
        return nn(kn[at, pair_columns(head)], padded(q[head_rows(head), :], head))

    totals = {}

    def finish(head, at, probs):
        term = nn(value_rows(vt, head_rows(head), at), probs)
        totals[head] = totals[head] + term if head in totals else term
        if at == last_at:
            put(head, totals[head])

    waiting = None
    following = score(*steps[0])
    for place, (head, at) in enumerate(steps):
        scores = following
        if place + 1 < len(steps):
            following = score(*steps[place + 1])
        if waiting is not None:
            finish(*waiting)
        waiting = (head, at, jnp.exp(scores).astype(BF16))
    finish(*waiting)


def attend_own_kernel(q, kn, vt, *refs):
    passing, (sums, *passed) = refs[: len(refs) // 2], refs[len(refs) // 2 :]
    for source, out in zip(passing, passed):
        out[...] = source[...]

    def put(head, total):
        sums[head] = total

    @pl.when(score_bound(q, kn) < SAFE_SCORE)
    def _():
        attend_plain(q, kn, vt, put)


def forward_kernel(last, *refs):
    if last:
        active, x, x_step, *refs = refs
    else:
        x, *refs = refs
    q, kn_own, kn_far, vt_own, vt_far, sums, mod, w_out_t, w_up_t, w_down_t, *refs = refs
    if not last:
        mod_next, w_q_t, w_v_t, w_k, *refs = refs
    lse, mixed, attended, middle, hidden, slope, branch, *refs = refs
    if last:
        (final,) = refs
    else:
        x_next, xb_next, *next_outs = refs
    patches = x.shape[1]
    safe = score_bound(q, kn_own, kn_far) < SAFE_SCORE

    def put(head, total):
        total = sums[head] + total
        weight = total[HEAD_DIM : HEAD_DIM + 1]
        mixed[head_rows(head), :] = (total[:HEAD_DIM] * (1.0 / weight)).astype(BF16)
        lse[head : head + 1, :] = jnp.log(weight)

    @pl.when(safe)
    def _():
        attend_plain(q, kn_far, vt_far, put)

    @pl.when(jnp.logical_not(safe))
    def _():
        def pair_heads(pair, _):
            columns = pl.ds(pl.multiple_of(pair * PAIR, PAIR), PAIR)
            for head in range(2):
                rows = pl.ds(pl.multiple_of(pair * PAIR + head * HEAD_DIM, HEAD_DIM), HEAD_DIM)
                query = padded(q[rows, :], head)
                scores = [nn(kn[:, columns], query) for kn in (kn_own, kn_far)]
                tops = [jnp.max(score, axis=0, keepdims=True) for score in scores]
                top = jnp.maximum(*tops)
                total = None
                for score, vt in zip(scores, (vt_own, vt_far)):
                    term = nn(value_rows(vt, rows, slice(None)), jnp.exp(score - top).astype(BF16))
                    total = term if total is None else total + term
                weight = total[HEAD_DIM : HEAD_DIM + 1]
                mixed[rows, :] = (total[:HEAD_DIM] * (1.0 / weight)).astype(BF16)
                lse[pl.ds(pair * 2 + head, 1), :] = top + jnp.log(weight)
            return 0

        lax.fori_loop(0, HEADS // 2, pair_heads, 0)

    att = nn(w_out_t[...], mixed[...])
    attended[...] = att.astype(BF16)
    mid = x[...] + part(mod, 2, patches) * att
    middle[...] = mid.astype(BF16)
    standard, _ = standardise(mid)
    hidden_in = (standard * (1.0 + part(mod, 4, patches)) + part(mod, 3, patches)).astype(BF16)
    chunks = [slice(at, at + BLOCK) for at in range(0, w_up_t.shape[0], BLOCK)]
    down = None
    waiting = None
    following = nn(w_up_t[chunks[0], :], hidden_in)
    for place, rows in enumerate(chunks):
        act = following
        if place + 1 < len(chunks):
            following = nn(w_up_t[chunks[place + 1], :], hidden_in)
        if place > 0:
            term = nn(w_down_t[:, chunks[place - 1]], waiting)
            down = term if down is None else down + term
        squared = act * act
        bent = jnp.tanh(act * (GELU_A + (GELU_A * GELU_B) * squared))
        half = 0.5 + 0.5 * bent
        waiting = (act * half).astype(BF16)
        hidden[rows, :] = waiting
        curve = (1.0 - bent * bent) * (0.5 * GELU_A + (1.5 * GELU_A * GELU_B) * squared)
        slope[rows, :] = (half + act * curve).astype(BF16)
    down = down + nn(w_down_t[:, chunks[-1]], waiting)
    branch[...] = down.astype(BF16)
    out = mid + part(mod, 5, patches) * down
    if last:
        own = final.shape[0]
        final[...] = jnp.where(active[0] > 0.0, out[:, :own], x_step[:, :own]).T
    else:
        x_next[...] = out
        xb_next[...] = out.astype(BF16)
        project(out, mod_next, w_q_t, w_v_t, w_k, next_outs)


def put_grads(left_ref, right, where, count, at, mine, other, before):
    rows = [left_ref[pl.ds(pl.multiple_of(where[place] * count, 16), count), :] for place in range(2)]
    product = nt(jnp.concatenate(rows, axis=0), right)
    for column in range(0, product.shape[1], LANES):
        low = product[:count, column : column + LANES]
        high = product[count:, column : column + LANES]
        if before is not None:
            low = low + before[0][at : at + count, :]
            high = high + before[1][at : at + count, :]
        mine[at : at + count, :] = low.astype(mine.dtype)
        other[at : at + count, :] = high.astype(other.dtype)
        at += count


def dense_back_kernel(has_close, has_open, has_before, start, layers, waits, *refs):
    refs = list(refs)

    def take(count):
        taken = refs[:count]
        del refs[:count]
        return taken

    take(waits)
    where, active = take(2)
    close_before = open_before = None
    if has_close:
        d_own, d_got, dq, d_mid_in, x_in, mod_in, w_qkv = take(7)
        w_qkv = w_qkv.at[layers[0]]
        if has_before[0]:
            close_before = take(3)
    if start == "first":
        cots = take(4)
    elif start == "cross":
        cots = take(1)
    if has_open:
        mixed, attended, middle, hidden, slope, branch, mod, w_out, w_up, w_down = take(10)
        w_out, w_up, w_down = (ref.at[layers[1]] for ref in (w_out, w_up, w_down))
        if has_before[1]:
            open_before = take(3)
    else:
        (lines,) = take(1)
    if has_close:
        close_mine, close_other, close_mods = take(3)
    if start == "first":
        (cot_out,) = take(1)
    if has_open:
        open_mine, open_other, open_mods, d_mid_out, do_out, cen_out = take(6)
    else:
        g_out, sums_out = take(2)
        sums_at = close_before[1].shape[0]
    if has_close:
        grads_scr, normed_scr = take(2)
    if has_open:
        bg_scr, pg_scr, hin_scr, ag_scr = take(4)

    patches = middle.shape[1] if has_open else x_in.shape[1]
    totals = {}

    def add_sums(name, values):
        totals[name] = totals[name] + folded(values) if name in totals else folded(values)

    def put_sums(out, before, names):
        for place, name in enumerate(names):
            rows = slice(place * D, (place + 1) * D)
            out[rows, :] = totals[name] + before[2][rows, :] if before else totals[name]

    if start == "first":
        for index, ref in enumerate(cots):
            rows = ref.shape[0]
            cot_out[:, index * rows : (index + 1) * rows] = turned(ref[...])

    def close(at):
        standard, scale = standardise(x_in[:, at].astype(F32))
        gain = 1.0 + part(mod_in, 1, patches)
        normed_scr[:, at] = (standard * gain + part(mod_in, 0, patches)).astype(BF16)
        for third in range(3):
            if third == 0:
                piece = dq[:, at]
            else:
                rows = slice((third - 1) * D, third * D)
                piece = (d_own[rows, at] + d_got[rows, at].astype(F32)).astype(BF16)
            grads_scr[third * D : (third + 1) * D, at] = piece
        back = nn(w_qkv[...], grads_scr[:, at])
        add_sums("shift_a", back)
        add_sums("scale_a", back * standard)
        g = d_mid_in[:, at] + pre_norm_back(standard, scale, back, gain)
        if start == "cross":
            g = g + (1.0 - active[0]) * cots[0][:, at].astype(F32)
        return g

    def dense(at, g):
        standard, scale = standardise(middle[:, at].astype(F32))
        gain = 1.0 + part(mod, 4, patches)
        hin_scr[:, at] = (standard * gain + part(mod, 3, patches)).astype(BF16)
        branch_grad = (part(mod, 5, patches) * g).astype(BF16)
        bg_scr[:, at] = branch_grad
        add_sums("gate_m", g * branch[:, at].astype(F32))
        chunks = [slice(start, start + BLOCK) for start in range(0, w_down.shape[0], BLOCK)]
        back = None
        waiting = None
        following = nn(w_down[chunks[0], :], branch_grad)
        for place, rows in enumerate(chunks):
            hidden_grad = following
            if place + 1 < len(chunks):
                following = nn(w_down[chunks[place + 1], :], branch_grad)
            if place > 0:
                term = nn(w_up[:, chunks[place - 1]], waiting)
                back = term if back is None else back + term
            waiting = (slope[rows, at].astype(F32) * hidden_grad).astype(BF16)
            pg_scr[rows, at] = waiting
        back = back + nn(w_up[:, chunks[-1]], waiting)
        add_sums("shift_m", back)
        add_sums("scale_m", back * standard)
        d_mid = g + pre_norm_back(standard, scale, back, gain)
        d_mid_out[:, at] = d_mid
        att_grad = (part(mod, 2, patches) * d_mid).astype(BF16)
        ag_scr[:, at] = att_grad
        mixed_grad = nn(w_out[...], att_grad).astype(BF16)
        do_out[:, at] = mixed_grad
        add_sums("gate_a", d_mid * attended[:, at].astype(F32))
        product = mixed_grad.astype(F32) * mixed[:, at].astype(F32)
        for head in range(HEADS):
            cen_out[head : head + 1, at] = jnp.sum(product[head_rows(head)], axis=0, keepdims=True)

    at = slice(0, patches)
    g = close(at) if has_close else cot_out[:, at].astype(F32) * active[0]
    if has_open:
        dense(at, g)
    else:
        g_out[...] = g[:, : g_out.shape[0]].T
    if has_close:
        put_sums(close_mods, close_before, ("shift_a", "scale_a"))
        put_grads(normed_scr, grads_scr[...], where, D // 8, 0, close_mine, close_other, close_before)
    if has_open:
        put_sums(open_mods, open_before, ("gate_a", "shift_m", "scale_m", "gate_m"))
        count = w_down.shape[0] // 8
        put_grads(hidden, bg_scr[...], where, count, 0, open_mine, open_other, open_before)
        at = count * (D // LANES)
        put_grads(hin_scr, pg_scr[...], where, D // 8, at, open_mine, open_other, open_before)
        at += (w_up.shape[1] // LANES) * (D // 8)
        put_grads(mixed, ag_scr[...], where, D // 8, at, open_mine, open_other, open_before)
    else:
        sums_out[...] = lines[...]
        put_lines(sums_out, 0, close_mods[...])
        close_other[sums_at:, :] = sums_out[...].astype(BF16)


def attend_back_kernel(has_before, waits, q, kn, vt, lse, d_out, centre, *refs):
    if has_before:
        before, *refs = refs
    d_kv, dq_out, kt_scr, vn_scr = refs[waits:]
    for column in range(0, D, LANES):
        kt_scr[column : column + LANES, :] = turned(kn[:, column : column + LANES])
    for column in range(0, vt.shape[1], BLOCK):
        vn_scr[column : column + BLOCK, :] = turned(vt[:, column : column + BLOCK])

    steps = [(head, slice(at, at + BLOCK)) for head in range(HEADS) for at in range(0, kn.shape[0], BLOCK)]

    def score(head, at):
        columns = pair_columns(head)
        rows = head_rows(head)
        return nn(kn[at, columns], padded(q[rows, :], head)), nn(vn_scr[at, columns], padded(d_out[rows, :], head))

    totals = {}

    def finish(head, at, probs, score_grads):
        rows = head_rows(head)
        d_kv[D + rows.start : D + rows.stop, at] = nt(d_out[rows, :], probs).astype(d_kv.dtype)
        d_kv[rows, at] = nt(q[rows, :], score_grads).astype(d_kv.dtype)
        term = nn(kt_scr[rows, at], score_grads)
        if head not in totals:
            totals[head] = before[rows, :] + term if has_before else term
            return
        term = totals[head] + term
        if has_before:
            term = term * HEAD_DIM ** (-0.5)
        dq_out[rows, :] = term.astype(dq_out.dtype)

    waiting = None
    following = score(*steps[0])
    for place, (head, at) in enumerate(steps):
        scores, prob_grads = following
        if place + 1 < len(steps):
            following = score(*steps[place + 1])
        if waiting is not None:
            finish(*waiting)
        probs = jnp.exp(scores - lse[head : head + 1, :])
        score_grads = (probs * (prob_grads - centre[head : head + 1, :])).astype(BF16)
        waiting = (head, at, probs.astype(BF16), score_grads)
    finish(*waiting)


def split_kernel(waits, where, *refs):
    *halves, keep, sent, total_scr = refs[waits:]
    rows_half = keep.shape[0]
    at = 0
    for mine, other in zip(halves[::2], halves[1::2]):
        rows = mine.shape[0]
        total_scr[at : at + rows, :] = mine[...] + other[...].astype(F32)
        at += rows
    if at < total_scr.shape[0]:
        total_scr[at:, :] = jnp.zeros((total_scr.shape[0] - at, LANES), F32)
    odd = where[3]
    keep[...] = total_scr[pl.ds(pl.multiple_of(odd * rows_half, 16), rows_half), :]
    sent[...] = total_scr[pl.ds(pl.multiple_of((1 - odd) * rows_half, 16), rows_half), :].astype(BF16)


def pair_sum_kernel(late, *refs):
    count = len(refs) // 3
    for keep, got, out in zip(refs[:count], refs[count : 2 * count], refs[2 * count :]):
        out[...] = (keep[...].astype(F32) + got[...].astype(F32)).astype(BF16)


def put_lines(out, row, values):
    ones = jnp.ones((16, LANES), BF16)
    high = values.astype(BF16)
    low = (values - high.astype(F32)).astype(BF16)
    line = (nt(ones, high) + nt(ones, low))[0:1]
    for column in range(0, line.shape[1], LANES):
        out[row : row + 1, :] = line[:, column : column + LANES]
        row += 1
    return row


def lines_kernel(early, context, *refs):
    *sums, out = refs
    out[...] = jnp.zeros_like(out)
    row = 2 * D // LANES
    for ref in sums:
        row = put_lines(out, row, ref[...])
    for column in range(0, D, LANES):
        out[row : row + 1, :] = context[0:1, column : column + LANES].astype(F32)
        row += 1


def join_kernel(sum_count, early, mine, sums, got, out):
    rows = mine.shape[0]
    out[:rows, :] = (mine[...] + got[:rows, :].astype(F32)).astype(BF16)
    other = got[rows:, :].astype(F32)
    summed = lax.broadcasted_iota(jnp.int32, (SUM_ROWS, LANES), 0) < sum_count
    out[rows:, :] = (sums[...] + jnp.where(summed, other, 0.0)).astype(BF16)


def pair_kernel(rows, where, own, got, out):
    out[:rows, :] = (own[:rows, :].astype(F32) + got[:rows, :].astype(F32)).astype(BF16)
    odd = where[3]
    size = SUM_ROWS
    out[pl.ds(pl.multiple_of(rows + odd * size, 16), size), :] = own[rows:, :]
    out[pl.ds(pl.multiple_of(rows + (1 - odd) * size, 16), size), :] = got[rows:, :]


def gather_kernel(where, *refs):
    halves, (out_out, up_out, down_out, qkv_out), scratch = refs[:4], refs[4:8], refs[8:]
    odd = where[3]
    for ref, own, got in zip(scratch, halves[::2], halves[1::2]):
        rows = own.shape[0]
        ref[pl.ds(pl.multiple_of(odd * rows, 16), rows), :] = own[...]
        ref[pl.ds(pl.multiple_of((1 - odd) * rows, 16), rows), :] = got[...]
    slice_rows = out_out.shape[1]
    for index, ref in enumerate(scratch):
        at = 0
        for out in (down_out, up_out, out_out):
            rows = out.shape[1]
            for column in range(0, out.shape[2], LANES):
                out[index, :, column : column + LANES] = ref[at : at + rows, :].astype(F32)
                at += rows
        if index == 0:
            for column in range(0, qkv_out.shape[1], LANES):
                qkv_out[:, column : column + LANES] = ref[at : at + slice_rows, :].astype(F32)
                at += slice_rows


def finish_kernel(item_count, where, own, got, qkv_1, qkv_out, ada_out, bias_out, shift_out, sum_scr, bias_scr, shift_scr):
    layers = 2
    device, high = where[0], where[4]
    slice_rows = qkv_out.shape[1]
    close_rows = slice_rows * (3 * D // LANES)
    for other in range(2):
        rows = slice(close_rows + other * SUM_ROWS, close_rows + (other + 1) * SUM_ROWS)
        sum_scr[2 * high + other] = own[rows, :].astype(F32)
        sum_scr[2 * (1 - high) + other] = got[rows, :].astype(F32)
    qkv_out[1] = qkv_1[...]
    for tile in range(3 * D // LANES):
        rows = slice(tile * slice_rows, (tile + 1) * slice_rows)
        total = own[rows, :].astype(F32) + got[rows, :].astype(F32)
        qkv_out[0, :, tile * LANES : (tile + 1) * LANES] = total
    tiles = 6 * D // LANES
    contexts = []
    for other in range(item_count):
        line = jnp.concatenate([sum_scr[other, layers * tiles + c : layers * tiles + c + 1, :] for c in range(3)], axis=1)
        contexts.append(line)
    square = jnp.concatenate(contexts + [jnp.zeros((8 - item_count, D), F32)], axis=0)
    spot = lax.broadcasted_iota(jnp.int32, (slice_rows, D), 1)
    want = lax.broadcasted_iota(jnp.int32, (slice_rows, D), 0) + device * slice_rows
    pick = jnp.where(spot == want, 1.0, 0.0).astype(BF16)
    columns = nt(pick, square.astype(BF16))
    bias_rows = bias_out.shape[1]
    for index in range(layers):
        flats = []
        for tile in range(tiles):
            row = index * tiles + tile
            total = None
            flat = None
            for other in range(item_count):
                line = sum_scr[other, row : row + 1, :]
                term = columns[:, other : other + 1] * line
                total = term if total is None else total + term
                flat = line if flat is None else flat + line
            ada_out[index, :, tile * LANES : (tile + 1) * LANES] = total
            flats.append(flat)
        flat = jnp.concatenate(flats, axis=1)
        for place in range(flat.shape[1] // bias_rows):
            bias_scr[place, index : index + 1, :] = flat[:, place * bias_rows : (place + 1) * bias_rows]
            at = 3 * D + place * slice_rows
            shift_scr[place, index : index + 1, :] = flat[:, at : at + slice_rows]
    bias_out[...] = bias_scr[device]
    shift_out[...] = shift_scr[device]


VMEM = pl.BlockSpec(memory_space=pltpu.VMEM)
SMEM = pl.BlockSpec(memory_space=pltpu.SMEM)
ANY = pl.BlockSpec(memory_space=pl.ANY)
HBM = pl.BlockSpec(memory_space=pltpu.HBM)


def layer_block(array, index):
    return pl.BlockSpec((None,) + array.shape[1:], lambda step: (index,) + (0,) * (array.ndim - 1))


def call(body, args, outs, scratch=(), flops=0, name=None):
    arrays = [arg[0] if isinstance(arg, tuple) else arg for arg in args]
    specs = [arg[1] if isinstance(arg, tuple) else VMEM for arg in args]
    return pl.pallas_call(
        body,
        out_shape=[jax.ShapeDtypeStruct(shape, kind) for shape, kind in outs],
        in_specs=specs,
        out_specs=[VMEM] * len(outs),
        scratch_shapes=[one if not isinstance(one, tuple) else pltpu.VMEM(*one) for one in scratch],
        compiler_params=pltpu.CompilerParams(vmem_limit_bytes=VMEM_LIMIT),
        cost_estimate=pl.CostEstimate(flops=flops, bytes_accessed=0, transcendentals=0),
        name=name,
    )(*arrays)


VMEM_LIMIT = 14 * 1024 * 1024


def fast_shards(
    lat_count, lon_count, item_count,
    fields, lead_index, rollout, w_qkv, w_out, w_up, w_down, w_ada, b_ada, cotangent,
):
    _, rows_dev, cols_dev, width = fields.shape
    local = rows_dev * cols_dev
    layers = w_qkv.shape[0]
    ff = w_up.shape[2]
    patches = 4 * local
    device = lax.axis_index("lat") * lon_count + lax.axis_index("lon")
    item = lax.axis_index("item")
    where = jnp.stack([device, device ^ 1, item, item & 1, item >> 1]).astype(jnp.int32)
    active = (1 < rollout[0]).astype(F32)[None]

    def plane_flip(value, flip_lat, flip_y):
        pairs = [
            (a * lon_count + b, (a ^ flip_lat) * lon_count + (b ^ (2 * flip_y)))
            for a in range(lat_count)
            for b in range(lon_count)
        ]
        return lax.ppermute(value, ("lat", "lon"), pairs)

    def swap(value):
        return lax.ppermute(value, "lon", [(index, index ^ 1) for index in range(lon_count)])

    def with_item(value, flip):
        return lax.ppermute(value, "item", [(index, index ^ flip) for index in range(item_count)])

    def plane_parts(value):
        return [value, plane_flip(value, 1, 0), plane_flip(value, 0, 1), plane_flip(value, 1, 1)]

    field_parts = plane_parts(fields.reshape(local, width))

    context = jax.nn.silu(embedding(lead_index[0])).astype(BF16)
    context = jnp.broadcast_to(context[None, :], (16, width))
    square = (width, patches)
    natural = (patches, width)
    fetched = [(pltpu.with_memory_space_constraint(value, pltpu.HBM), HBM) for value in (w_ada, b_ada, w_qkv)]
    fetch_scratch = [((width, 3 * width), BF16), ((width, 6 * width), BF16), (b_ada.shape, F32)]
    fetch_scratch.append(pltpu.SemaphoreType.DMA((3,)))
    first_outs = [((6 * width, LANES), F32)] + [((width, width), BF16)] * 3
    rest_outs = [((width, width), BF16), ((ff, width), BF16), ((width, ff), BF16)]
    first_0 = call(
        functools.partial(prepare_first_kernel, 0, None, 2),
        [context, *fetched, (where, SMEM), (active, SMEM)],
        first_outs,
        fetch_scratch,
        name="prepare_first",
    )
    project_outs = [(square, F32), (square, BF16), (square, BF16), (natural, BF16), (square, BF16)]
    dense_flops = 2 * patches * (width * 3 * width + width * width + 2 * width * ff)
    score_flops = 2 * patches * 2 * patches * width * 4
    x, xb, *projected = call(
        first_kernel,
        [*field_parts, *first_0],
        project_outs,
        flops=2 * patches * width * 4 * width,
        name="first",
    )
    both = call(
        prepare_both_kernel,
        [(x, ANY), context, *fetched, w_out, w_up, w_down],
        first_outs + rest_outs,
        fetch_scratch,
        name="prepare_both",
    )
    first_parts = [first_0, both[:4]]
    rest_parts = [both[4:]]
    mods = [one[0] for one in first_parts]
    saved = []
    for step in range(STEPS):
        for index in range(layers):
            q, kn, vt = projected
            if len(rest_parts) == index:
                rest_parts.append(
                    call(
                        functools.partial(prepare_rest_kernel, index),
                        [(kn, ANY), w_out, w_up, w_down],
                        rest_outs,
                        name="prepare_rest",
                    )
                )
            kn_far, vt_far = swap(kn), swap(vt)
            passing = [cotangent.reshape(local, width)] if step == STEPS - 1 and index == 0 else []
            sums, *passed = call(
                attend_own_kernel,
                [q, kn, vt] + passing,
                [((HEADS, HEAD_DIM + ONES, patches), F32)] + [((local, width), BF16)] * len(passing),
                flops=10 * score_flops,
                name="forward_own",
            )
            if passed:
                cot_parts = plane_parts(passed[0])
            last = step == STEPS - 1 and index == layers - 1
            if index == 0 and step > 0:
                x_step = x
            following = list(first_parts[(index + 1) % layers])
            lse, mixed, attended, middle, hidden, slope, branch, *results = call(
                functools.partial(forward_kernel, last),
                ([(active, SMEM), x, x_step] if last else [x])
                + [q, kn, kn_far, vt, vt_far, sums, mods[index], *rest_parts[index]]
                + ([] if last else following),
                [
                    ((HEADS, patches), F32),
                    (square, BF16),
                    (square, BF16),
                    (square, BF16),
                    ((ff, patches), BF16),
                    ((ff, patches), BF16),
                    (square, BF16),
                ]
                + ([((local, width), F32)] if last else project_outs),
                flops=dense_flops + 2 * score_flops,
                name="forward",
            )
            saved.append((xb, [mixed, attended, middle, hidden, slope, branch], (q, kn, kn_far, vt, vt_far, lse)))
            if last:
                final = results[0]
            else:
                x, xb, *projected = results

    slice_rows = width // 8
    open_rows = 2 * (ff // 8) * (width // LANES) + slice_rows * (width // LANES)
    close_rows = slice_rows * (3 * width // LANES)
    order = [(step, index) for step in reversed(range(STEPS)) for index in reversed(range(layers))]
    open_done = [None] * layers
    close_done = [None] * layers
    pending = None
    for place in range(len(order) + 1):
        has_close = pending is not None
        has_open = place < len(order)
        use = [order[place - 1][1], order[place][1] if has_open else 0]
        waits = []
        if has_close and close_done[use[0]]:
            waits = [pair_1] if has_open else [item_got_1]
        args = [(value, ANY) for value in waits] + [(where, SMEM), (active, SMEM)]
        outs = []
        scratch = []
        has_before = [False, False]
        start = ""
        if has_close:
            args += pending
            if close_done[use[0]] is not None:
                has_before[0] = True
                args += close_done[use[0]]
            outs += [((close_rows, LANES), F32)]
            sent_rows = close_rows + (0 if has_open else SUM_ROWS)
            outs += [((sent_rows, LANES), BF16 if has_before[0] else F32), ((2 * width, LANES), F32)]
            scratch += [((3 * width, patches), BF16), (square, BF16)]
        if place == 0:
            start = "first"
            args += cot_parts
            outs += [(square, BF16)]
        elif has_open and order[place][0] != order[place - 1][0]:
            start = "cross"
            args += [cot_t]
        if has_open:
            step, index = order[place]
            xb, kept, heads = saved[step * layers + index]
            args += kept + [mods[index], w_out, w_up, w_down]
            if open_done[index] is not None:
                has_before[1] = True
                args += open_done[index]
            outs += [
                ((open_rows, LANES), F32),
                ((open_rows, LANES), BF16 if has_before[1] else F32),
                ((4 * width, LANES), F32),
                (square, F32),
                (square, BF16),
                ((HEADS, patches), F32),
            ]
            scratch += [(square, BF16), ((ff, patches), BF16), (square, BF16), (square, BF16)]
        else:
            args += [lines]
            outs += [((local, width), F32), ((SUM_ROWS, LANES), F32)]
        results = list(
            call(
                functools.partial(dense_back_kernel, has_close, has_open, has_before, start, use, len(waits)),
                args,
                outs,
                scratch,
                flops=2 * dense_flops if has_open else 0,
                name="dense_back" if has_open else "close_back",
            )
        )
        if has_close:
            close_done[use[0]] = results[:3]
            del results[:3]
        if start == "first":
            cot_t = results.pop(0)
        if not has_open:
            gradient, line = results
            break
        open_done[index] = results[:3]
        d_mid, d_out, centre = results[3:]
        q, kn, kn_far, vt, vt_far, lse = heads
        halves = [open_done[index][0], open_done[index][1]]
        if index == 0:
            halves += [close_done[1][0], close_done[1][1]]
        half_rows = -(-sum(half.shape[0] for half in halves[::2]) // 32) * 16

        def split(waits):
            pieces = [half if place % 2 == 0 else swap(half) for place, half in enumerate(halves)]
            return call(
                functools.partial(split_kernel, len(waits)),
                [(where, SMEM), *waits, *pieces],
                [((half_rows, LANES), F32), ((half_rows, LANES), BF16)],
                [((2 * half_rows, LANES), F32)],
                name="split",
            )

        def pair_sum(late, keeps, gots):
            outs = [(keep.shape, BF16) for keep in keeps]
            return call(pair_sum_kernel, [(late, ANY), *keeps, *gots], outs, name="pair_sum")

        waits = []
        if has_before[1] and index == 0:
            pair_got_1 = with_item(pair_1, 2)
            lines = call(
                lines_kernel,
                [(pair_got_1, ANY), context, open_done[0][2], close_done[1][2], open_done[1][2]],
                [((SUM_ROWS, LANES), F32)],
                flops=10 * score_flops,
                name="lines",
            )[0]
            keep, sent = split([(lines, ANY)])
            got_0 = with_item(sent, 1)
            waits = [keep]
        d_far, dq = call(
            functools.partial(attend_back_kernel, False, len(waits)),
            [q, kn_far, vt_far, lse, d_out, centre] + [(value, ANY) for value in waits],
            [((2 * width, patches), BF16), (square, F32)],
            [(square, BF16), (natural, BF16)],
            flops=10 * score_flops,
            name="attend_far",
        )
        d_got = swap(d_far)
        waits = []
        if has_before[1]:
            if index == 1:
                keep, sent = split([(d_far, ANY)])
                got_1 = with_item(sent, 1)
                waits = [keep]
            else:
                pair_0, item_1 = pair_sum(d_far, [keep, pair_1], [got_0, pair_got_1])
                item_got_1 = with_item(item_1, 1)
                pair_got_0 = with_item(pair_0, 2)
                waits = [pair_0]
        d_own, dq = call(
            functools.partial(attend_back_kernel, True, len(waits)),
            [q, kn, vt, lse, d_out, centre, dq] + [(value, ANY) for value in waits],
            [((2 * width, patches), F32), (square, BF16)],
            [(square, BF16), (natural, BF16)],
            flops=10 * score_flops,
            name="attend_own",
        )
        if has_before[1] and index == 1:
            (pair_1,) = pair_sum(dq, [keep], [got_1])
        pending = [d_own, d_got, dq, d_mid, xb, mods[index], w_qkv]

    message = call(
        functools.partial(join_kernel, layers * 6 * width // LANES),
        [(pair_got_0, ANY), close_done[0][0], line, swap(close_done[0][1])],
        [((close_rows + SUM_ROWS, LANES), BF16)],
        name="join",
    )[0]
    message_got = with_item(message, 1)
    (item_0,) = pair_sum(message_got, [pair_0], [pair_got_0])
    message = call(
        functools.partial(pair_kernel, close_rows),
        [(where, SMEM), message, message_got],
        [((close_rows + 2 * SUM_ROWS, LANES), BF16)],
        name="pair",
    )[0]
    out_grad, up_grad, down_grad, qkv_1 = call(
        gather_kernel,
        [(where, SMEM), item_0, with_item(item_0, 1), item_1, item_got_1],
        [
            ((layers, slice_rows, width), F32),
            ((layers, slice_rows, ff), F32),
            ((layers, ff // 8, width), F32),
            ((slice_rows, 3 * width), F32),
        ],
        [((2 * pair.shape[0], LANES), BF16) for pair in (pair_0, pair_1)],
        name="gather",
    )
    bias_rows = 6 * width // 8
    qkv_grad, ada_grad, bias_grad, shift_grad = call(
        functools.partial(finish_kernel, item_count),
        [(where, SMEM), message, with_item(message, 2), qkv_1],
        [
            ((layers, slice_rows, 3 * width), F32),
            ((layers, slice_rows, 6 * width), F32),
            ((layers, bias_rows), F32),
            ((layers, slice_rows), F32),
        ],
        [
            ((item_count, SUM_ROWS, LANES), F32),
            ((8, layers, bias_rows), F32),
            ((8, layers, slice_rows), F32),
        ],
        name="finish",
    )
    field_shape = (1, rows_dev, cols_dev, width)
    return (
        final.reshape(field_shape),
        gradient.reshape(field_shape),
        qkv_grad,
        out_grad,
        up_grad,
        down_grad,
        ada_grad,
        bias_grad,
        shift_grad,
    )


def solution(mesh):
    lat_count, lon_count, item_count = mesh.shape["lat"], mesh.shape["lon"], mesh.shape["item"]
    if lat_count == 2 and lon_count == 4:
        body = functools.partial(fast_shards, lat_count, lon_count, item_count)
    else:
        body = shards
    return jax.shard_map(
        body,
        mesh=mesh,
        in_specs=(
            P("item", "lat", "lon", None),
            P("item"),
            P("item"),
            P(),
            P(),
            P(),
            P(),
            P(),
            P(),
            P("item", "lat", "lon", None),
        ),
        out_specs=(
            P("item", "lat", "lon", None),
            P("item", "lat", "lon", None),
            P(None, ("lat", "lon"), None),
            P(None, ("lat", "lon"), None),
            P(None, ("lat", "lon"), None),
            P(None, ("lat", "lon"), None),
            P(None, ("lat", "lon"), None),
            P(None, ("lat", "lon")),
            P(None, ("lat", "lon")),
        ),
        check_vma=False,
    )
```

```python
import functools
import math

import jax
import jax.numpy as jnp
from jax import lax
from jax.experimental import pallas as pl
from jax.experimental.pallas import tpu as pltpu
from jax.sharding import PartitionSpec as P

D = 384
HEADS = 6
HEAD_DIM = 64
STEPS = 2


def shortened(shard):
    return jax.tree.map(lambda a: a.astype(jnp.bfloat16) if a.dtype == jnp.float32 else a, shard)


def embedding(lead):
    half_width = D // 2
    lead_hours = 6.0 * (lead.astype(jnp.float32) + 1.0)
    frequencies = jnp.exp(
        -math.log(10000.0) * jnp.arange(half_width, dtype=jnp.float32) / half_width
    )
    angles = lead_hours * frequencies
    return jnp.concatenate([jnp.sin(angles), jnp.cos(angles)])


def pre_norm(values, shift_part, scale_part):
    centred = values - jnp.mean(values, axis=-1, keepdims=True)
    variance = jnp.mean(centred * centred, axis=-1, keepdims=True)
    return centred * lax.rsqrt(variance + 1e-06) * (1.0 + scale_part) + shift_part


def gather_keys(keys_values):
    band_rows = lax.all_gather(keys_values, "lon", axis=0, tiled=True)
    return lax.all_gather(band_rows, "lat", axis=0, tiled=True)


def spread_keys(key_value_grads):
    band_grads = lax.psum_scatter(
        key_value_grads.astype(jnp.bfloat16), "lat", scatter_dimension=0, tiled=True
    )
    return lax.psum_scatter(band_grads, "lon", scatter_dimension=0, tiled=True).astype(jnp.float32)


def forward_layer(current, modulation, weight_qkv, weight_out, weight_up, weight_down):
    local_rows, width = current.shape
    shift_attn, scale_attn, gate_attn, shift_mlp, scale_mlp, gate_mlp = modulation
    normed = pre_norm(current, shift_attn, scale_attn).astype(jnp.bfloat16)
    projected = jnp.dot(normed, weight_qkv, preferred_element_type=jnp.float32).astype(jnp.bfloat16)
    queries = projected[:, :width].reshape(local_rows, HEADS, HEAD_DIM)
    own_keys = projected[:, width:]
    gathered = gather_keys(own_keys)
    total_rows = gathered.shape[0]
    key_heads = gathered[:, :width].reshape(total_rows, HEADS, HEAD_DIM)
    value_heads = gathered[:, width:].reshape(total_rows, HEADS, HEAD_DIM)
    scores = jnp.einsum(
        "thd,nhd->htn", queries, key_heads, preferred_element_type=jnp.float32
    ) * HEAD_DIM ** (-0.5)
    log_total = jax.nn.logsumexp(scores, axis=-1, keepdims=True)
    probabilities = jnp.exp(scores - log_total).astype(jnp.bfloat16)
    mixed = jnp.einsum(
        "htn,nhd->thd", probabilities, value_heads, preferred_element_type=jnp.float32
    )
    mixed = mixed.reshape(local_rows, width).astype(jnp.bfloat16)
    attended = jnp.dot(mixed, weight_out, preferred_element_type=jnp.float32)
    middle = current + gate_attn * attended
    hidden_in = pre_norm(middle, shift_mlp, scale_mlp).astype(jnp.bfloat16)
    pre_act = jnp.dot(hidden_in, weight_up, preferred_element_type=jnp.float32)
    hidden = jax.nn.gelu(pre_act).astype(jnp.bfloat16)
    branch = jnp.dot(hidden, weight_down, preferred_element_type=jnp.float32)
    output = middle + gate_mlp * branch
    kept = (
        current,
        normed,
        queries,
        gathered,
        own_keys,
        log_total,
        mixed,
        attended,
        middle,
        hidden_in,
        pre_act,
        hidden,
        branch,
    )
    return (output, kept)


def backward_layer(grad_out, kept, modulation, weight_qkv, weight_out, weight_up, weight_down):
    (
        current,
        normed,
        queries,
        gathered,
        own_keys,
        log_total,
        mixed,
        attended,
        middle,
        hidden_in,
        pre_act,
        hidden,
        branch,
    ) = kept
    local_rows, width = current.shape
    total_rows = gathered.shape[0]
    shift_attn, scale_attn, gate_attn, shift_mlp, scale_mlp, gate_mlp = modulation
    factor = HEAD_DIM ** (-0.5)
    branch_grad = (gate_mlp * grad_out).astype(jnp.bfloat16)
    gate_mlp_grad = jnp.sum(grad_out * branch, axis=0)
    hidden_grad = jnp.dot(branch_grad, weight_down.T, preferred_element_type=jnp.float32)
    down_grad = jnp.dot(hidden.T, branch_grad, preferred_element_type=jnp.float32)
    _, gelu_back = jax.vjp(jax.nn.gelu, pre_act)
    pre_grad = gelu_back(hidden_grad)[0].astype(jnp.bfloat16)
    hidden_in_grad = jnp.dot(pre_grad, weight_up.T, preferred_element_type=jnp.float32)
    up_grad = jnp.dot(hidden_in.T, pre_grad, preferred_element_type=jnp.float32)
    _, second_back = jax.vjp(pre_norm, middle, shift_mlp, scale_mlp)
    middle_part, shift_mlp_grad, scale_mlp_grad = second_back(hidden_in_grad)
    middle_grad = grad_out + middle_part
    attended_grad = (gate_attn * middle_grad).astype(jnp.bfloat16)
    gate_attn_grad = jnp.sum(middle_grad * attended, axis=0)
    mixed_grad = jnp.dot(attended_grad, weight_out.T, preferred_element_type=jnp.float32).astype(
        jnp.bfloat16
    )
    out_grad = jnp.dot(mixed.T, attended_grad, preferred_element_type=jnp.float32)
    mixed_heads = mixed_grad.reshape(local_rows, HEADS, HEAD_DIM)
    key_heads = gathered[:, :width].reshape(total_rows, HEADS, HEAD_DIM)
    value_heads = gathered[:, width:].reshape(total_rows, HEADS, HEAD_DIM)
    scores = (
        jnp.einsum("thd,nhd->htn", queries, key_heads, preferred_element_type=jnp.float32) * factor
    )
    probabilities = jnp.exp(scores - log_total)
    prob_grads = jnp.einsum(
        "thd,nhd->htn", mixed_heads, value_heads, preferred_element_type=jnp.float32
    )
    centre = jnp.sum(prob_grads * probabilities, axis=-1, keepdims=True)
    score_grads = (probabilities * (prob_grads - centre)).astype(jnp.bfloat16)
    query_grads = (
        jnp.einsum("htn,nhd->thd", score_grads, key_heads, preferred_element_type=jnp.float32)
        * factor
    )
    value_grads = jnp.einsum(
        "htn,thd->nhd",
        probabilities.astype(jnp.bfloat16),
        mixed_heads,
        preferred_element_type=jnp.float32,
    )
    key_grads = (
        jnp.einsum("htn,thd->nhd", score_grads, queries, preferred_element_type=jnp.float32)
        * factor
    )
    key_value_grads = jnp.concatenate(
        [key_grads.reshape(total_rows, width), value_grads.reshape(total_rows, width)], axis=1
    )
    local_grads = spread_keys(key_value_grads)
    projected_grad = jnp.concatenate(
        [query_grads.reshape(local_rows, width), local_grads], axis=1
    ).astype(jnp.bfloat16)
    normed_grad = jnp.dot(projected_grad, weight_qkv.T, preferred_element_type=jnp.float32)
    qkv_grad = jnp.dot(normed.T, projected_grad, preferred_element_type=jnp.float32)
    _, first_back = jax.vjp(pre_norm, current, shift_attn, scale_attn)
    current_part, shift_attn_grad, scale_attn_grad = first_back(normed_grad)
    input_grad = middle_grad + current_part
    modulation_grad = jnp.concatenate(
        [
            shift_attn_grad,
            scale_attn_grad,
            gate_attn_grad,
            shift_mlp_grad,
            scale_mlp_grad,
            gate_mlp_grad,
        ]
    )
    return (input_grad, (qkv_grad, out_grad, up_grad, down_grad, modulation_grad))


def shards(fields, lead_index, rollout, w_qkv, w_out, w_up, w_down, w_ada, b_ada, cotangent):
    _, rows_dev, cols_dev, width = fields.shape
    local_rows = rows_dev * cols_dev
    layer_count = w_qkv.shape[0]
    context = jax.nn.silu(embedding(lead_index[0])).astype(jnp.bfloat16)
    context_wide = context.astype(jnp.float32)
    modulations = [
        (
            jnp.dot(context[None, :], w_ada[index], preferred_element_type=jnp.float32)[0]
            + b_ada[index]
        ).reshape(6, width)
        for index in range(layer_count)
    ]
    weight_sets = [
        (w_qkv[index], w_out[index], w_up[index], w_down[index]) for index in range(layer_count)
    ]
    count = rollout[0]
    current = fields.reshape(local_rows, width).astype(jnp.float32)
    saved = []
    for rollout_step in range(STEPS):
        updated = current
        kept_layers = []
        for index in range(layer_count):
            updated, kept = forward_layer(updated, modulations[index], *weight_sets[index])
            kept_layers.append(kept)
        current = jnp.where(rollout_step < count, updated, current)
        saved.append(kept_layers)
    gradient = cotangent.reshape(local_rows, width).astype(jnp.float32)
    summed = None
    shares = None
    for rollout_step in reversed(range(STEPS)):
        active = (rollout_step < count).astype(jnp.float32)
        inner = gradient * active
        layer_terms = [None] * layer_count
        for index in reversed(range(layer_count)):
            inner, layer_terms[index] = backward_layer(
                inner, saved[rollout_step][index], modulations[index], *weight_sets[index]
            )
        gradient = inner + (1.0 - active) * gradient
        modulation_grads = jnp.stack([terms[4] for terms in layer_terms])
        step_terms = (
            jnp.stack([terms[0] for terms in layer_terms]),
            jnp.stack([terms[1] for terms in layer_terms]),
            jnp.stack([terms[2] for terms in layer_terms]),
            jnp.stack([terms[3] for terms in layer_terms]),
            context_wide[None, :, None] * modulation_grads[:, None, :],
            modulation_grads,
            modulation_grads[:, 3 * width : 4 * width],
        )
        summed = step_terms if summed is None else jax.tree.map(jnp.add, summed, step_terms)
    shares = lax.psum_scatter(summed, ("lat", "lon"), scatter_dimension=1, tiled=True)
    totals = jax.tree.map(
        lambda part: part.astype(jnp.float32), lax.psum(shortened(shares), "item")
    )
    return (
        current.reshape(1, rows_dev, cols_dev, width),
        gradient.reshape(1, rows_dev, cols_dev, width),
        totals[0],
        totals[1],
        totals[2],
        totals[3],
        totals[4],
        totals[5],
        totals[6],
    )


F32 = jnp.float32
BF16 = jnp.bfloat16
GELU_A = math.sqrt(2.0 / math.pi)
GELU_B = 0.044715
LANES = 128
BLOCK = 256
PAIR = 2 * HEAD_DIM
SUM_ROWS = 48
ONES = 16
SAFE_SCORE = 60.0


def nn(left, right, precision=None):
    return lax.dot_general(
        left, right, (((1,), (0,)), ((), ())), preferred_element_type=F32, precision=precision
    )


def nt(left, right, precision=None):
    return lax.dot_general(
        left, right, (((1,), (1,)), ((), ())), preferred_element_type=F32, precision=precision
    )


def identity(size):
    rows = lax.broadcasted_iota(jnp.int32, (size, size), 0)
    columns = lax.broadcasted_iota(jnp.int32, (size, size), 1)
    return jnp.where(rows == columns, 1.0, 0.0).astype(BF16)


def turned(values):
    return nt(identity(values.shape[1]), values).astype(BF16)


def wide(column_tile, lanes):
    return jnp.concatenate([column_tile] * (lanes // LANES), axis=1)


def folded(values):
    pieces = [values[:, at : at + LANES] for at in range(0, values.shape[1], LANES)]
    return sum(pieces[1:], pieces[0])


def standardise(values):
    rows = values.shape[0]
    centred = values - jnp.sum(values, axis=0, keepdims=True) * (1.0 / rows)
    variance = jnp.sum(centred * centred, axis=0, keepdims=True) * (1.0 / rows)
    scale = lax.rsqrt(variance + 1e-06)
    return centred * scale, scale


def pre_norm_back(standard, scale, grad, gain):
    rows = standard.shape[0]
    inner = grad * gain
    first = jnp.sum(inner, axis=0, keepdims=True) * (1.0 / rows)
    second = jnp.sum(inner * standard, axis=0, keepdims=True) * (1.0 / rows)
    return scale * (inner - first - standard * second)


def part(mod_ref, index, lanes):
    return wide(mod_ref[index * D : (index + 1) * D, :], lanes)


def turn_into(source, out, at=0):
    for column in range(0, out.shape[0], BLOCK):
        width = min(BLOCK, out.shape[0] - column)
        out[column : column + width, :] = turned(source[:, at + column : at + column + width])


def prepare_first_kernel(index, between, waits, context, w_ada, b_ada, w_qkv, *refs):
    mod, w_q_t, w_v_t, w_k, *scratch, sems = refs[waits:]
    copies = [
        pltpu.make_async_copy(source, target, sems.at[place])
        for place, (source, target) in enumerate(zip((w_qkv.at[index], w_ada.at[index], b_ada), scratch))
    ]
    for copy in copies:
        copy.start()
    if between:
        between()
    w_qkv, w_ada, b_ada = scratch
    copies[0].wait()
    w_k[...] = w_qkv[:, D : 2 * D]
    turn_into(w_qkv, w_q_t)
    turn_into(w_qkv, w_v_t, 2 * D)
    copies[1].wait()
    copies[2].wait()
    values = nn(context[...], w_ada[...])[0:1] + b_ada[index : index + 1, :]
    for column in range(0, values.shape[1], LANES):
        tile = jnp.broadcast_to(values[:, column : column + LANES], (LANES, LANES))
        mod[column : column + LANES, :] = tile.T


def prepare_rest_kernel(index, early, w_out, w_up, w_down, *outs):
    for weight, out in zip((w_out, w_up, w_down), outs):
        turn_into(weight.at[index], out)


def prepare_both_kernel(early, context, w_ada, b_ada, w_qkv, w_out, w_up, w_down, *refs):
    between = functools.partial(prepare_rest_kernel, 0, early, w_out, w_up, w_down, *refs[4:7])
    prepare_first_kernel(1, between, 0, context, w_ada, b_ada, w_qkv, *refs[:4], *refs[7:])


def project(x, mod_ref, w_q_t, w_v_t, w_k, outs):
    q_out, kn_out, vt_out = outs
    lanes = x.shape[1]
    standard, _ = standardise(x)
    normed = (standard * (1.0 + part(mod_ref, 1, lanes)) + part(mod_ref, 0, lanes)).astype(BF16)
    vt_out[...] = nn(w_v_t[...], normed).astype(BF16)
    q_out[...] = (nn(w_q_t[...], normed) * HEAD_DIM ** (-0.5)).astype(BF16)
    for at in range(0, lanes, BLOCK):
        kn_out[at : at + BLOCK, :] = nn(turned(normed[:, at : at + BLOCK]), w_k[...]).astype(BF16)


def first_kernel(own, flip_x, flip_y, flip_xy, mod, w_q_t, w_v_t, w_k, x_out, xb_out, *outs):
    for index, ref in enumerate((own, flip_x, flip_y, flip_xy)):
        rows = ref.shape[0]
        flat = turned(ref[...])
        xb_out[:, index * rows : (index + 1) * rows] = flat
        x_out[:, index * rows : (index + 1) * rows] = flat.astype(F32)
    project(x_out[...], mod, w_q_t, w_v_t, w_k, outs)


def head_rows(head):
    return slice(head * HEAD_DIM, (head + 1) * HEAD_DIM)


def pair_columns(head):
    return slice(head // 2 * PAIR, (head // 2 + 1) * PAIR)


def padded(rows, head):
    zeros = jnp.zeros_like(rows)
    return jnp.concatenate([rows, zeros] if head % 2 == 0 else [zeros, rows], axis=0)


def query_top(q):
    square = q[...].astype(F32)
    square = square * square
    norms = [jnp.sum(square[head_rows(head)], axis=0, keepdims=True) for head in range(HEADS)]
    return jnp.max(functools.reduce(jnp.maximum, norms), axis=1, keepdims=True)


def key_top(kn):
    first = lax.broadcasted_iota(jnp.int32, (D, LANES), 1) * HEAD_DIM
    row = lax.broadcasted_iota(jnp.int32, (D, LANES), 0)
    pick = jnp.where((row >= first) & (row < first + HEAD_DIM), 1.0, 0.0).astype(BF16)
    square = kn[...].astype(F32)
    norms = nn((square * square).astype(BF16), pick)
    return jnp.max(jnp.max(norms, axis=0, keepdims=True), axis=1, keepdims=True) * 1.02


def value_rows(vt, rows, at):
    values = vt[rows, at]
    return jnp.concatenate([values, jnp.ones((ONES, values.shape[1]), BF16)], axis=0)


def attend_plain(q, kn, vt, put):
    steps = [(head, slice(at, at + BLOCK)) for head in range(HEADS) for at in range(0, kn.shape[0], BLOCK)]
    last_at = steps[-1][1]

    def score(head, at):
        return nn(kn[at, pair_columns(head)], padded(q[head_rows(head), :], head))

    totals = {}

    def finish(head, at, probs):
        term = nn(value_rows(vt, head_rows(head), at), probs)
        totals[head] = totals[head] + term if head in totals else term
        if at == last_at:
            put(head, totals[head])

    waiting = None
    following = score(*steps[0])
    for place, (head, at) in enumerate(steps):
        scores = following
        if place + 1 < len(steps):
            following = score(*steps[place + 1])
        if waiting is not None:
            finish(*waiting)
        waiting = (head, at, jnp.exp(scores).astype(BF16))
    finish(*waiting)


def attend_own_kernel(q, kn, vt, *refs):
    half = len(refs) // 2 - 1
    passing, (sums, tops, *passed) = refs[:half], refs[half:]
    for source, out in zip(passing, passed):
        out[...] = source[...]

    def put(head, total):
        sums[head] = total

    query, key = query_top(q), key_top(kn)
    tops[0:8, :] = jnp.broadcast_to(query, (8, LANES))
    tops[8:16, :] = jnp.broadcast_to(key, (8, LANES))

    @pl.when(jnp.max(query * key) < SAFE_SCORE**2)
    def _():
        attend_plain(q, kn, vt, put)


def forward_kernel(last, *refs):
    if last:
        active, x, x_step, *refs = refs
    else:
        x, *refs = refs
    q, kn_own, kn_far, vt_own, vt_far, sums, tops, mod, w_out_t, w_up_t, w_down_t, *refs = refs
    if not last:
        mod_next, w_q_t, w_v_t, w_k, *refs = refs
    lse, mixed, attended, middle, hidden, slope, branch, *refs = refs
    if last:
        (final,) = refs
    else:
        x_next, xb_next, *next_outs = refs
    patches = x.shape[1]
    bound = tops[0:1, 0:1] * jnp.maximum(tops[8:9, 0:1], key_top(kn_far))
    safe = jnp.max(bound) < SAFE_SCORE**2

    def put(head, total):
        total = sums[head] + total
        weight = total[HEAD_DIM : HEAD_DIM + 1]
        mixed[head_rows(head), :] = (total[:HEAD_DIM] * (1.0 / weight)).astype(BF16)
        lse[head : head + 1, :] = jnp.log(weight)

    @pl.when(safe)
    def _():
        attend_plain(q, kn_far, vt_far, put)

    @pl.when(jnp.logical_not(safe))
    def _():
        def pair_heads(pair, _):
            columns = pl.ds(pl.multiple_of(pair * PAIR, PAIR), PAIR)
            for head in range(2):
                rows = pl.ds(pl.multiple_of(pair * PAIR + head * HEAD_DIM, HEAD_DIM), HEAD_DIM)
                query = padded(q[rows, :], head)
                scores = [nn(kn[:, columns], query) for kn in (kn_own, kn_far)]
                tops = [jnp.max(score, axis=0, keepdims=True) for score in scores]
                top = jnp.maximum(*tops)
                total = None
                for score, vt in zip(scores, (vt_own, vt_far)):
                    term = nn(value_rows(vt, rows, slice(None)), jnp.exp(score - top).astype(BF16))
                    total = term if total is None else total + term
                weight = total[HEAD_DIM : HEAD_DIM + 1]
                mixed[rows, :] = (total[:HEAD_DIM] * (1.0 / weight)).astype(BF16)
                lse[pl.ds(pair * 2 + head, 1), :] = top + jnp.log(weight)
            return 0

        lax.fori_loop(0, HEADS // 2, pair_heads, 0)

    att = nn(w_out_t[...], mixed[...])
    attended[...] = att.astype(BF16)
    mid = x[...] + part(mod, 2, patches) * att
    middle[...] = mid.astype(BF16)
    standard, _ = standardise(mid)
    hidden_in = (standard * (1.0 + part(mod, 4, patches)) + part(mod, 3, patches)).astype(BF16)
    chunks = [slice(at, at + BLOCK) for at in range(0, w_up_t.shape[0], BLOCK)]
    down = None
    waiting = None
    following = nn(w_up_t[chunks[0], :], hidden_in)
    for place, rows in enumerate(chunks):
        act = following
        if place + 1 < len(chunks):
            following = nn(w_up_t[chunks[place + 1], :], hidden_in)
        if place > 0:
            term = nn(w_down_t[:, chunks[place - 1]], waiting)
            down = term if down is None else down + term
        inner = GELU_A + (GELU_A * GELU_B) * (act * act)
        half = 0.5 + 0.5 * jnp.tanh(act * inner)
        gelu = act * half
        waiting = gelu.astype(BF16)
        hidden[rows, :] = waiting
        slope[rows, :] = (half + (gelu - gelu * half) * (6.0 * inner - 4.0 * GELU_A)).astype(BF16)
    down = down + nn(w_down_t[:, chunks[-1]], waiting)
    branch[...] = down.astype(BF16)
    out = mid + part(mod, 5, patches) * down
    if last:
        own = final.shape[0]
        final[...] = jnp.where(active[0] > 0.0, out[:, :own], x_step[:, :own]).T
    else:
        x_next[...] = out
        xb_next[...] = out.astype(BF16)
        project(out, mod_next, w_q_t, w_v_t, w_k, next_outs)


def put_grads(left_ref, right, where, count, at, mine, other, before):
    rows = [left_ref[pl.ds(pl.multiple_of(where[place] * count, 16), count), :] for place in range(2)]
    product = nt(jnp.concatenate(rows, axis=0), right)
    for column in range(0, product.shape[1], LANES):
        low = product[:count, column : column + LANES]
        high = product[count:, column : column + LANES]
        if before is not None:
            low = low + before[0][at : at + count, :]
            high = high + before[1][at : at + count, :]
        mine[at : at + count, :] = low.astype(mine.dtype)
        other[at : at + count, :] = high.astype(other.dtype)
        at += count


def dense_back_kernel(has_close, has_open, has_before, start, layers, waits, *refs):
    refs = list(refs)

    def take(count):
        taken = refs[:count]
        del refs[:count]
        return taken

    take(waits)
    where, active = take(2)
    close_before = open_before = None
    if has_close:
        d_own, d_got, dq, d_mid_in, x_in, mod_in, w_qkv = take(7)
        w_qkv = w_qkv.at[layers[0]]
        if has_before[0]:
            close_before = take(3)
    if start == "first":
        cots = take(4)
    elif start == "cross":
        cots = take(1)
    if has_open:
        mixed, attended, middle, hidden, slope, branch, mod, w_out, w_up, w_down = take(10)
        w_out, w_up, w_down = (ref.at[layers[1]] for ref in (w_out, w_up, w_down))
        if has_before[1]:
            open_before = take(3)
    else:
        (lines,) = take(1)
    if has_close:
        close_mine, close_other, close_mods = take(3)
    if start == "first":
        (cot_out,) = take(1)
    if has_open:
        open_mine, open_other, open_mods, d_mid_out, do_out, cen_out = take(6)
    else:
        g_out, sums_out = take(2)
        sums_at = close_before[1].shape[0]
    if has_close:
        grads_scr, normed_scr = take(2)
    if has_open:
        bg_scr, pg_scr, hin_scr, ag_scr = take(4)

    patches = middle.shape[1] if has_open else x_in.shape[1]
    totals = {}

    def add_sums(name, values):
        totals[name] = totals[name] + folded(values) if name in totals else folded(values)

    def put_sums(out, before, names):
        for place, name in enumerate(names):
            rows = slice(place * D, (place + 1) * D)
            out[rows, :] = totals[name] + before[2][rows, :] if before else totals[name]

    if start == "first":
        for index, ref in enumerate(cots):
            rows = ref.shape[0]
            cot_out[:, index * rows : (index + 1) * rows] = turned(ref[...])

    def close(at):
        standard, scale = standardise(x_in[:, at].astype(F32))
        gain = 1.0 + part(mod_in, 1, patches)
        normed_scr[:, at] = (standard * gain + part(mod_in, 0, patches)).astype(BF16)
        for third in range(3):
            if third == 0:
                piece = dq[:, at]
            else:
                rows = slice((third - 1) * D, third * D)
                piece = (d_own[rows, at] + d_got[rows, at].astype(F32)).astype(BF16)
            grads_scr[third * D : (third + 1) * D, at] = piece
        back = nn(w_qkv[...], grads_scr[:, at])
        add_sums("shift_a", back)
        add_sums("scale_a", back * standard)
        g = d_mid_in[:, at] + pre_norm_back(standard, scale, back, gain)
        if start == "cross":
            g = g + (1.0 - active[0]) * cots[0][:, at].astype(F32)
        return g

    def dense(at, g):
        standard, scale = standardise(middle[:, at].astype(F32))
        gain = 1.0 + part(mod, 4, patches)
        hin_scr[:, at] = (standard * gain + part(mod, 3, patches)).astype(BF16)
        branch_grad = (part(mod, 5, patches) * g).astype(BF16)
        bg_scr[:, at] = branch_grad
        add_sums("gate_m", g * branch[:, at].astype(F32))
        chunks = [slice(start, start + BLOCK) for start in range(0, w_down.shape[0], BLOCK)]
        back = None
        waiting = None
        following = nn(w_down[chunks[0], :], branch_grad)
        for place, rows in enumerate(chunks):
            hidden_grad = following
            if place + 1 < len(chunks):
                following = nn(w_down[chunks[place + 1], :], branch_grad)
            if place > 0:
                term = nn(w_up[:, chunks[place - 1]], waiting)
                back = term if back is None else back + term
            waiting = (slope[rows, at].astype(F32) * hidden_grad).astype(BF16)
            pg_scr[rows, at] = waiting
        back = back + nn(w_up[:, chunks[-1]], waiting)
        add_sums("shift_m", back)
        add_sums("scale_m", back * standard)
        d_mid = g + pre_norm_back(standard, scale, back, gain)
        d_mid_out[:, at] = d_mid
        att_grad = (part(mod, 2, patches) * d_mid).astype(BF16)
        ag_scr[:, at] = att_grad
        mixed_grad = nn(w_out[...], att_grad).astype(BF16)
        do_out[:, at] = mixed_grad
        add_sums("gate_a", d_mid * attended[:, at].astype(F32))
        product = mixed_grad.astype(F32) * mixed[:, at].astype(F32)
        for head in range(HEADS):
            cen_out[head : head + 1, at] = jnp.sum(product[head_rows(head)], axis=0, keepdims=True)

    at = slice(0, patches)
    g = close(at) if has_close else cot_out[:, at].astype(F32) * active[0]
    if has_open:
        dense(at, g)
    else:
        g_out[...] = g[:, : g_out.shape[0]].T
    if has_close:
        put_sums(close_mods, close_before, ("shift_a", "scale_a"))
        put_grads(normed_scr, grads_scr[...], where, D // 8, 0, close_mine, close_other, close_before)
    if has_open:
        put_sums(open_mods, open_before, ("gate_a", "shift_m", "scale_m", "gate_m"))
        count = w_down.shape[0] // 8
        put_grads(hidden, bg_scr[...], where, count, 0, open_mine, open_other, open_before)
        at = count * (D // LANES)
        put_grads(hin_scr, pg_scr[...], where, D // 8, at, open_mine, open_other, open_before)
        at += (w_up.shape[1] // LANES) * (D // 8)
        put_grads(mixed, ag_scr[...], where, D // 8, at, open_mine, open_other, open_before)
    else:
        sums_out[...] = lines[...]
        put_lines(sums_out, 0, close_mods[...])
        close_other[sums_at:, :] = sums_out[...].astype(BF16)


def attend_back_kernel(has_before, waits, q, kn, vt, lse, d_out, centre, *refs):
    if has_before:
        before, *refs = refs
    d_kv, dq_out, kt_scr, vn_scr = refs[waits:]
    for column in range(0, D, LANES):
        kt_scr[column : column + LANES, :] = turned(kn[:, column : column + LANES])
    for column in range(0, vt.shape[1], BLOCK):
        vn_scr[column : column + BLOCK, :] = turned(vt[:, column : column + BLOCK])

    steps = [(head, slice(at, at + BLOCK)) for head in range(HEADS) for at in range(0, kn.shape[0], BLOCK)]

    def score(head, at):
        columns = pair_columns(head)
        rows = head_rows(head)
        return nn(kn[at, columns], padded(q[rows, :], head)), nn(vn_scr[at, columns], padded(d_out[rows, :], head))

    totals = {}

    def finish(head, at, probs, score_grads):
        rows = head_rows(head)
        d_kv[D + rows.start : D + rows.stop, at] = nt(d_out[rows, :], probs).astype(d_kv.dtype)
        d_kv[rows, at] = nt(q[rows, :], score_grads).astype(d_kv.dtype)
        term = nn(kt_scr[rows, at], score_grads)
        if head not in totals:
            totals[head] = before[rows, :] + term if has_before else term
            return
        term = totals[head] + term
        if has_before:
            term = term * HEAD_DIM ** (-0.5)
        dq_out[rows, :] = term.astype(dq_out.dtype)

    waiting = None
    following = score(*steps[0])
    for place, (head, at) in enumerate(steps):
        scores, prob_grads = following
        if place + 1 < len(steps):
            following = score(*steps[place + 1])
        if waiting is not None:
            finish(*waiting)
        probs = jnp.exp(scores - lse[head : head + 1, :])
        score_grads = (probs * (prob_grads - centre[head : head + 1, :])).astype(BF16)
        waiting = (head, at, probs.astype(BF16), score_grads)
    finish(*waiting)


def split_kernel(waits, where, *refs):
    *halves, keep, sent, total_scr = refs[waits:]
    rows_half = keep.shape[0]
    at = 0
    for mine, other in zip(halves[::2], halves[1::2]):
        rows = mine.shape[0]
        total_scr[at : at + rows, :] = mine[...] + other[...].astype(F32)
        at += rows
    if at < total_scr.shape[0]:
        total_scr[at:, :] = jnp.zeros((total_scr.shape[0] - at, LANES), F32)
    odd = where[3]
    keep[...] = total_scr[pl.ds(pl.multiple_of(odd * rows_half, 16), rows_half), :]
    sent[...] = total_scr[pl.ds(pl.multiple_of((1 - odd) * rows_half, 16), rows_half), :].astype(BF16)


def pair_sum_kernel(late, *refs):
    count = len(refs) // 3
    for keep, got, out in zip(refs[:count], refs[count : 2 * count], refs[2 * count :]):
        out[...] = (keep[...].astype(F32) + got[...].astype(F32)).astype(BF16)


def put_lines(out, row, values):
    ones = jnp.ones((16, LANES), BF16)
    high = values.astype(BF16)
    low = (values - high.astype(F32)).astype(BF16)
    line = (nt(ones, high) + nt(ones, low))[0:1]
    for column in range(0, line.shape[1], LANES):
        out[row : row + 1, :] = line[:, column : column + LANES]
        row += 1
    return row


def lines_kernel(early, context, *refs):
    *sums, out = refs
    out[...] = jnp.zeros_like(out)
    row = 2 * D // LANES
    for ref in sums:
        row = put_lines(out, row, ref[...])
    for column in range(0, D, LANES):
        out[row : row + 1, :] = context[0:1, column : column + LANES].astype(F32)
        row += 1


def join_kernel(sum_count, early, mine, sums, got, out):
    rows = mine.shape[0]
    out[:rows, :] = (mine[...] + got[:rows, :].astype(F32)).astype(BF16)
    other = got[rows:, :].astype(F32)
    summed = lax.broadcasted_iota(jnp.int32, (SUM_ROWS, LANES), 0) < sum_count
    out[rows:, :] = (sums[...] + jnp.where(summed, other, 0.0)).astype(BF16)


def pair_kernel(rows, where, own, got, out):
    out[:rows, :] = (own[:rows, :].astype(F32) + got[:rows, :].astype(F32)).astype(BF16)
    odd = where[3]
    size = SUM_ROWS
    out[pl.ds(pl.multiple_of(rows + odd * size, 16), size), :] = own[rows:, :]
    out[pl.ds(pl.multiple_of(rows + (1 - odd) * size, 16), size), :] = got[rows:, :]


def gather_kernel(where, *refs):
    halves, (out_out, up_out, down_out, qkv_out), scratch = refs[:4], refs[4:8], refs[8:]
    odd = where[3]
    for ref, own, got in zip(scratch, halves[::2], halves[1::2]):
        rows = own.shape[0]
        ref[pl.ds(pl.multiple_of(odd * rows, 16), rows), :] = own[...]
        ref[pl.ds(pl.multiple_of((1 - odd) * rows, 16), rows), :] = got[...]
    slice_rows = out_out.shape[1]
    for index, ref in enumerate(scratch):
        at = 0
        for out in (down_out, up_out, out_out):
            rows = out.shape[1]
            for column in range(0, out.shape[2], LANES):
                out[index, :, column : column + LANES] = ref[at : at + rows, :].astype(F32)
                at += rows
        if index == 0:
            for column in range(0, qkv_out.shape[1], LANES):
                qkv_out[:, column : column + LANES] = ref[at : at + slice_rows, :].astype(F32)
                at += slice_rows


def finish_kernel(item_count, where, own, got, qkv_1, qkv_out, ada_out, bias_out, shift_out, sum_scr, bias_scr, shift_scr):
    layers = 2
    device, high = where[0], where[4]
    slice_rows = qkv_out.shape[1]
    close_rows = slice_rows * (3 * D // LANES)
    for other in range(2):
        rows = slice(close_rows + other * SUM_ROWS, close_rows + (other + 1) * SUM_ROWS)
        sum_scr[2 * high + other] = own[rows, :].astype(F32)
        sum_scr[2 * (1 - high) + other] = got[rows, :].astype(F32)
    qkv_out[1] = qkv_1[...]
    for tile in range(3 * D // LANES):
        rows = slice(tile * slice_rows, (tile + 1) * slice_rows)
        total = own[rows, :].astype(F32) + got[rows, :].astype(F32)
        qkv_out[0, :, tile * LANES : (tile + 1) * LANES] = total
    tiles = 6 * D // LANES
    contexts = []
    for other in range(item_count):
        line = jnp.concatenate([sum_scr[other, layers * tiles + c : layers * tiles + c + 1, :] for c in range(3)], axis=1)
        contexts.append(line)
    square = jnp.concatenate(contexts + [jnp.zeros((8 - item_count, D), F32)], axis=0)
    spot = lax.broadcasted_iota(jnp.int32, (slice_rows, D), 1)
    want = lax.broadcasted_iota(jnp.int32, (slice_rows, D), 0) + device * slice_rows
    pick = jnp.where(spot == want, 1.0, 0.0).astype(BF16)
    columns = nt(pick, square.astype(BF16))
    bias_rows = bias_out.shape[1]
    for index in range(layers):
        flats = []
        for tile in range(tiles):
            row = index * tiles + tile
            total = None
            flat = None
            for other in range(item_count):
                line = sum_scr[other, row : row + 1, :]
                term = columns[:, other : other + 1] * line
                total = term if total is None else total + term
                flat = line if flat is None else flat + line
            ada_out[index, :, tile * LANES : (tile + 1) * LANES] = total
            flats.append(flat)
        flat = jnp.concatenate(flats, axis=1)
        for place in range(flat.shape[1] // bias_rows):
            bias_scr[place, index : index + 1, :] = flat[:, place * bias_rows : (place + 1) * bias_rows]
            at = 3 * D + place * slice_rows
            shift_scr[place, index : index + 1, :] = flat[:, at : at + slice_rows]
    bias_out[...] = bias_scr[device]
    shift_out[...] = shift_scr[device]


VMEM = pl.BlockSpec(memory_space=pltpu.VMEM)
SMEM = pl.BlockSpec(memory_space=pltpu.SMEM)
ANY = pl.BlockSpec(memory_space=pl.ANY)
HBM = pl.BlockSpec(memory_space=pltpu.HBM)


def layer_block(array, index):
    return pl.BlockSpec((None,) + array.shape[1:], lambda step: (index,) + (0,) * (array.ndim - 1))


def call(body, args, outs, scratch=(), flops=0, name=None):
    arrays = [arg[0] if isinstance(arg, tuple) else arg for arg in args]
    specs = [arg[1] if isinstance(arg, tuple) else VMEM for arg in args]
    return pl.pallas_call(
        body,
        out_shape=[jax.ShapeDtypeStruct(shape, kind) for shape, kind in outs],
        in_specs=specs,
        out_specs=[VMEM] * len(outs),
        scratch_shapes=[one if not isinstance(one, tuple) else pltpu.VMEM(*one) for one in scratch],
        compiler_params=pltpu.CompilerParams(vmem_limit_bytes=VMEM_LIMIT),
        cost_estimate=pl.CostEstimate(flops=flops, bytes_accessed=0, transcendentals=0),
        name=name,
    )(*arrays)


VMEM_LIMIT = 14 * 1024 * 1024


def fast_shards(
    lat_count, lon_count, item_count,
    fields, lead_index, rollout, w_qkv, w_out, w_up, w_down, w_ada, b_ada, cotangent,
):
    _, rows_dev, cols_dev, width = fields.shape
    local = rows_dev * cols_dev
    layers = w_qkv.shape[0]
    ff = w_up.shape[2]
    patches = 4 * local
    device = lax.axis_index("lat") * lon_count + lax.axis_index("lon")
    item = lax.axis_index("item")
    where = jnp.stack([device, device ^ 1, item, item & 1, item >> 1]).astype(jnp.int32)
    active = (1 < rollout[0]).astype(F32)[None]

    def plane_flip(value, flip_lat, flip_y):
        pairs = [
            (a * lon_count + b, (a ^ flip_lat) * lon_count + (b ^ (2 * flip_y)))
            for a in range(lat_count)
            for b in range(lon_count)
        ]
        return lax.ppermute(value, ("lat", "lon"), pairs)

    def swap(value):
        return lax.ppermute(value, "lon", [(index, index ^ 1) for index in range(lon_count)])

    def with_item(value, flip):
        return lax.ppermute(value, "item", [(index, index ^ flip) for index in range(item_count)])

    def plane_parts(value):
        return [value, plane_flip(value, 1, 0), plane_flip(value, 0, 1), plane_flip(value, 1, 1)]

    field_parts = plane_parts(fields.reshape(local, width))

    context = jax.nn.silu(embedding(lead_index[0])).astype(BF16)
    context = jnp.broadcast_to(context[None, :], (16, width))
    square = (width, patches)
    natural = (patches, width)
    fetched = [(pltpu.with_memory_space_constraint(value, pltpu.HBM), HBM) for value in (w_ada, b_ada, w_qkv)]
    fetch_scratch = [((width, 3 * width), BF16), ((width, 6 * width), BF16), (b_ada.shape, F32)]
    fetch_scratch.append(pltpu.SemaphoreType.DMA((3,)))
    first_outs = [((6 * width, LANES), F32)] + [((width, width), BF16)] * 3
    rest_outs = [((width, width), BF16), ((ff, width), BF16), ((width, ff), BF16)]
    first_0 = call(
        functools.partial(prepare_first_kernel, 0, None, 2),
        [context, *fetched, (where, SMEM), (active, SMEM)],
        first_outs,
        fetch_scratch,
        name="prepare_first",
    )
    project_outs = [(square, F32), (square, BF16), (square, BF16), (natural, BF16), (square, BF16)]
    dense_flops = 2 * patches * (width * 3 * width + width * width + 2 * width * ff)
    score_flops = 2 * patches * 2 * patches * width * 4
    x, xb, *projected = call(
        first_kernel,
        [*field_parts, *first_0],
        project_outs,
        flops=2 * patches * width * 4 * width,
        name="first",
    )
    both = call(
        prepare_both_kernel,
        [(x, ANY), context, *fetched, w_out, w_up, w_down],
        first_outs + rest_outs,
        fetch_scratch,
        name="prepare_both",
    )
    first_parts = [first_0, both[:4]]
    rest_parts = [both[4:]]
    mods = [one[0] for one in first_parts]
    saved = []
    for step in range(STEPS):
        for index in range(layers):
            q, kn, vt = projected
            if len(rest_parts) == index:
                rest_parts.append(
                    call(
                        functools.partial(prepare_rest_kernel, index),
                        [(kn, ANY), w_out, w_up, w_down],
                        rest_outs,
                        name="prepare_rest",
                    )
                )
            kn_far, vt_far = swap(kn), swap(vt)
            passing = [cotangent.reshape(local, width)] if step == STEPS - 1 and index == 0 else []
            sums, tops, *passed = call(
                attend_own_kernel,
                [q, kn, vt] + passing,
                [((HEADS, HEAD_DIM + ONES, patches), F32), ((16, LANES), F32)] + [((local, width), BF16)] * len(passing),
                flops=10 * score_flops,
                name="forward_own",
            )
            if passed:
                cot_parts = plane_parts(passed[0])
            last = step == STEPS - 1 and index == layers - 1
            if index == 0 and step > 0:
                x_step = x
            following = list(first_parts[(index + 1) % layers])
            lse, mixed, attended, middle, hidden, slope, branch, *results = call(
                functools.partial(forward_kernel, last),
                ([(active, SMEM), x, x_step] if last else [x])
                + [q, kn, kn_far, vt, vt_far, sums, tops, mods[index], *rest_parts[index]]
                + ([] if last else following),
                [
                    ((HEADS, patches), F32),
                    (square, BF16),
                    (square, BF16),
                    (square, BF16),
                    ((ff, patches), BF16),
                    ((ff, patches), BF16),
                    (square, BF16),
                ]
                + ([((local, width), F32)] if last else project_outs),
                flops=dense_flops + 2 * score_flops,
                name="forward",
            )
            saved.append((xb, [mixed, attended, middle, hidden, slope, branch], (q, kn, kn_far, vt, vt_far, lse)))
            if last:
                final = results[0]
            else:
                x, xb, *projected = results

    slice_rows = width // 8
    open_rows = 2 * (ff // 8) * (width // LANES) + slice_rows * (width // LANES)
    close_rows = slice_rows * (3 * width // LANES)
    order = [(step, index) for step in reversed(range(STEPS)) for index in reversed(range(layers))]
    open_done = [None] * layers
    close_done = [None] * layers
    pending = None
    for place in range(len(order) + 1):
        has_close = pending is not None
        has_open = place < len(order)
        use = [order[place - 1][1], order[place][1] if has_open else 0]
        waits = []
        if has_close and close_done[use[0]]:
            waits = [pair_1] if has_open else [item_got_1]
        args = [(value, ANY) for value in waits] + [(where, SMEM), (active, SMEM)]
        outs = []
        scratch = []
        has_before = [False, False]
        start = ""
        if has_close:
            args += pending
            if close_done[use[0]] is not None:
                has_before[0] = True
                args += close_done[use[0]]
            outs += [((close_rows, LANES), F32)]
            sent_rows = close_rows + (0 if has_open else SUM_ROWS)
            outs += [((sent_rows, LANES), BF16 if has_before[0] else F32), ((2 * width, LANES), F32)]
            scratch += [((3 * width, patches), BF16), (square, BF16)]
        if place == 0:
            start = "first"
            args += cot_parts
            outs += [(square, BF16)]
        elif has_open and order[place][0] != order[place - 1][0]:
            start = "cross"
            args += [cot_t]
        if has_open:
            step, index = order[place]
            xb, kept, heads = saved[step * layers + index]
            args += kept + [mods[index], w_out, w_up, w_down]
            if open_done[index] is not None:
                has_before[1] = True
                args += open_done[index]
            outs += [
                ((open_rows, LANES), F32),
                ((open_rows, LANES), BF16 if has_before[1] else F32),
                ((4 * width, LANES), F32),
                (square, F32),
                (square, BF16),
                ((HEADS, patches), F32),
            ]
            scratch += [(square, BF16), ((ff, patches), BF16), (square, BF16), (square, BF16)]
        else:
            args += [lines]
            outs += [((local, width), F32), ((SUM_ROWS, LANES), F32)]
        results = list(
            call(
                functools.partial(dense_back_kernel, has_close, has_open, has_before, start, use, len(waits)),
                args,
                outs,
                scratch,
                flops=2 * dense_flops if has_open else 0,
                name="dense_back" if has_open else "close_back",
            )
        )
        if has_close:
            close_done[use[0]] = results[:3]
            del results[:3]
        if start == "first":
            cot_t = results.pop(0)
        if not has_open:
            gradient, line = results
            break
        open_done[index] = results[:3]
        d_mid, d_out, centre = results[3:]
        q, kn, kn_far, vt, vt_far, lse = heads
        halves = [open_done[index][0], open_done[index][1]]
        if index == 0:
            halves += [close_done[1][0], close_done[1][1]]
        half_rows = -(-sum(half.shape[0] for half in halves[::2]) // 32) * 16

        def split(waits):
            pieces = [half if place % 2 == 0 else swap(half) for place, half in enumerate(halves)]
            return call(
                functools.partial(split_kernel, len(waits)),
                [(where, SMEM), *waits, *pieces],
                [((half_rows, LANES), F32), ((half_rows, LANES), BF16)],
                [((2 * half_rows, LANES), F32)],
                name="split",
            )

        def pair_sum(late, keeps, gots):
            outs = [(keep.shape, BF16) for keep in keeps]
            return call(pair_sum_kernel, [(late, ANY), *keeps, *gots], outs, name="pair_sum")

        waits = []
        if has_before[1] and index == 0:
            pair_got_1 = with_item(pair_1, 2)
            lines = call(
                lines_kernel,
                [(pair_got_1, ANY), context, open_done[0][2], close_done[1][2], open_done[1][2]],
                [((SUM_ROWS, LANES), F32)],
                flops=10 * score_flops,
                name="lines",
            )[0]
            keep, sent = split([(lines, ANY)])
            got_0 = with_item(sent, 1)
            waits = [keep]
        d_far, dq = call(
            functools.partial(attend_back_kernel, False, len(waits)),
            [q, kn_far, vt_far, lse, d_out, centre] + [(value, ANY) for value in waits],
            [((2 * width, patches), BF16), (square, F32)],
            [(square, BF16), (natural, BF16)],
            flops=10 * score_flops,
            name="attend_far",
        )
        d_got = swap(d_far)
        waits = []
        if has_before[1]:
            if index == 1:
                keep, sent = split([(d_far, ANY)])
                got_1 = with_item(sent, 1)
                waits = [keep]
            else:
                pair_0, item_1 = pair_sum(d_far, [keep, pair_1], [got_0, pair_got_1])
                item_got_1 = with_item(item_1, 1)
                pair_got_0 = with_item(pair_0, 2)
                waits = [pair_0]
        d_own, dq = call(
            functools.partial(attend_back_kernel, True, len(waits)),
            [q, kn, vt, lse, d_out, centre, dq] + [(value, ANY) for value in waits],
            [((2 * width, patches), F32), (square, BF16)],
            [(square, BF16), (natural, BF16)],
            flops=10 * score_flops,
            name="attend_own",
        )
        if has_before[1] and index == 1:
            (pair_1,) = pair_sum(dq, [keep], [got_1])
        pending = [d_own, d_got, dq, d_mid, xb, mods[index], w_qkv]

    message = call(
        functools.partial(join_kernel, layers * 6 * width // LANES),
        [(pair_got_0, ANY), close_done[0][0], line, swap(close_done[0][1])],
        [((close_rows + SUM_ROWS, LANES), BF16)],
        name="join",
    )[0]
    message_got = with_item(message, 1)
    (item_0,) = pair_sum(message_got, [pair_0], [pair_got_0])
    message = call(
        functools.partial(pair_kernel, close_rows),
        [(where, SMEM), message, message_got],
        [((close_rows + 2 * SUM_ROWS, LANES), BF16)],
        name="pair",
    )[0]
    out_grad, up_grad, down_grad, qkv_1 = call(
        gather_kernel,
        [(where, SMEM), item_0, with_item(item_0, 1), item_1, item_got_1],
        [
            ((layers, slice_rows, width), F32),
            ((layers, slice_rows, ff), F32),
            ((layers, ff // 8, width), F32),
            ((slice_rows, 3 * width), F32),
        ],
        [((2 * pair.shape[0], LANES), BF16) for pair in (pair_0, pair_1)],
        name="gather",
    )
    bias_rows = 6 * width // 8
    qkv_grad, ada_grad, bias_grad, shift_grad = call(
        functools.partial(finish_kernel, item_count),
        [(where, SMEM), message, with_item(message, 2), qkv_1],
        [
            ((layers, slice_rows, 3 * width), F32),
            ((layers, slice_rows, 6 * width), F32),
            ((layers, bias_rows), F32),
            ((layers, slice_rows), F32),
        ],
        [
            ((item_count, SUM_ROWS, LANES), F32),
            ((8, layers, bias_rows), F32),
            ((8, layers, slice_rows), F32),
        ],
        name="finish",
    )
    field_shape = (1, rows_dev, cols_dev, width)
    return (
        final.reshape(field_shape),
        gradient.reshape(field_shape),
        qkv_grad,
        out_grad,
        up_grad,
        down_grad,
        ada_grad,
        bias_grad,
        shift_grad,
    )


def solution(mesh):
    lat_count, lon_count, item_count = mesh.shape["lat"], mesh.shape["lon"], mesh.shape["item"]
    if lat_count == 2 and lon_count == 4:
        body = functools.partial(fast_shards, lat_count, lon_count, item_count)
    else:
        body = shards
    return jax.shard_map(
        body,
        mesh=mesh,
        in_specs=(
            P("item", "lat", "lon", None),
            P("item"),
            P("item"),
            P(),
            P(),
            P(),
            P(),
            P(),
            P(),
            P("item", "lat", "lon", None),
        ),
        out_specs=(
            P("item", "lat", "lon", None),
            P("item", "lat", "lon", None),
            P(None, ("lat", "lon"), None),
            P(None, ("lat", "lon"), None),
            P(None, ("lat", "lon"), None),
            P(None, ("lat", "lon"), None),
            P(None, ("lat", "lon"), None),
            P(None, ("lat", "lon")),
            P(None, ("lat", "lon")),
        ),
        check_vma=False,
    )
```

```python
import functools
import math

import jax
import jax.numpy as jnp
from jax import lax
from jax.experimental import pallas as pl
from jax.experimental.pallas import tpu as pltpu
from jax.sharding import PartitionSpec as P

D = 384
HEADS = 6
HEAD_DIM = 64
STEPS = 2


def shortened(shard):
    return jax.tree.map(lambda a: a.astype(jnp.bfloat16) if a.dtype == jnp.float32 else a, shard)


def embedding(lead):
    half_width = D // 2
    lead_hours = 6.0 * (lead.astype(jnp.float32) + 1.0)
    frequencies = jnp.exp(
        -math.log(10000.0) * jnp.arange(half_width, dtype=jnp.float32) / half_width
    )
    angles = lead_hours * frequencies
    return jnp.concatenate([jnp.sin(angles), jnp.cos(angles)])


def pre_norm(values, shift_part, scale_part):
    centred = values - jnp.mean(values, axis=-1, keepdims=True)
    variance = jnp.mean(centred * centred, axis=-1, keepdims=True)
    return centred * lax.rsqrt(variance + 1e-06) * (1.0 + scale_part) + shift_part


def gather_keys(keys_values):
    band_rows = lax.all_gather(keys_values, "lon", axis=0, tiled=True)
    return lax.all_gather(band_rows, "lat", axis=0, tiled=True)


def spread_keys(key_value_grads):
    band_grads = lax.psum_scatter(
        key_value_grads.astype(jnp.bfloat16), "lat", scatter_dimension=0, tiled=True
    )
    return lax.psum_scatter(band_grads, "lon", scatter_dimension=0, tiled=True).astype(jnp.float32)


def forward_layer(current, modulation, weight_qkv, weight_out, weight_up, weight_down):
    local_rows, width = current.shape
    shift_attn, scale_attn, gate_attn, shift_mlp, scale_mlp, gate_mlp = modulation
    normed = pre_norm(current, shift_attn, scale_attn).astype(jnp.bfloat16)
    projected = jnp.dot(normed, weight_qkv, preferred_element_type=jnp.float32).astype(jnp.bfloat16)
    queries = projected[:, :width].reshape(local_rows, HEADS, HEAD_DIM)
    own_keys = projected[:, width:]
    gathered = gather_keys(own_keys)
    total_rows = gathered.shape[0]
    key_heads = gathered[:, :width].reshape(total_rows, HEADS, HEAD_DIM)
    value_heads = gathered[:, width:].reshape(total_rows, HEADS, HEAD_DIM)
    scores = jnp.einsum(
        "thd,nhd->htn", queries, key_heads, preferred_element_type=jnp.float32
    ) * HEAD_DIM ** (-0.5)
    log_total = jax.nn.logsumexp(scores, axis=-1, keepdims=True)
    probabilities = jnp.exp(scores - log_total).astype(jnp.bfloat16)
    mixed = jnp.einsum(
        "htn,nhd->thd", probabilities, value_heads, preferred_element_type=jnp.float32
    )
    mixed = mixed.reshape(local_rows, width).astype(jnp.bfloat16)
    attended = jnp.dot(mixed, weight_out, preferred_element_type=jnp.float32)
    middle = current + gate_attn * attended
    hidden_in = pre_norm(middle, shift_mlp, scale_mlp).astype(jnp.bfloat16)
    pre_act = jnp.dot(hidden_in, weight_up, preferred_element_type=jnp.float32)
    hidden = jax.nn.gelu(pre_act).astype(jnp.bfloat16)
    branch = jnp.dot(hidden, weight_down, preferred_element_type=jnp.float32)
    output = middle + gate_mlp * branch
    kept = (
        current,
        normed,
        queries,
        gathered,
        own_keys,
        log_total,
        mixed,
        attended,
        middle,
        hidden_in,
        pre_act,
        hidden,
        branch,
    )
    return (output, kept)


def backward_layer(grad_out, kept, modulation, weight_qkv, weight_out, weight_up, weight_down):
    (
        current,
        normed,
        queries,
        gathered,
        own_keys,
        log_total,
        mixed,
        attended,
        middle,
        hidden_in,
        pre_act,
        hidden,
        branch,
    ) = kept
    local_rows, width = current.shape
    total_rows = gathered.shape[0]
    shift_attn, scale_attn, gate_attn, shift_mlp, scale_mlp, gate_mlp = modulation
    factor = HEAD_DIM ** (-0.5)
    branch_grad = (gate_mlp * grad_out).astype(jnp.bfloat16)
    gate_mlp_grad = jnp.sum(grad_out * branch, axis=0)
    hidden_grad = jnp.dot(branch_grad, weight_down.T, preferred_element_type=jnp.float32)
    down_grad = jnp.dot(hidden.T, branch_grad, preferred_element_type=jnp.float32)
    _, gelu_back = jax.vjp(jax.nn.gelu, pre_act)
    pre_grad = gelu_back(hidden_grad)[0].astype(jnp.bfloat16)
    hidden_in_grad = jnp.dot(pre_grad, weight_up.T, preferred_element_type=jnp.float32)
    up_grad = jnp.dot(hidden_in.T, pre_grad, preferred_element_type=jnp.float32)
    _, second_back = jax.vjp(pre_norm, middle, shift_mlp, scale_mlp)
    middle_part, shift_mlp_grad, scale_mlp_grad = second_back(hidden_in_grad)
    middle_grad = grad_out + middle_part
    attended_grad = (gate_attn * middle_grad).astype(jnp.bfloat16)
    gate_attn_grad = jnp.sum(middle_grad * attended, axis=0)
    mixed_grad = jnp.dot(attended_grad, weight_out.T, preferred_element_type=jnp.float32).astype(
        jnp.bfloat16
    )
    out_grad = jnp.dot(mixed.T, attended_grad, preferred_element_type=jnp.float32)
    mixed_heads = mixed_grad.reshape(local_rows, HEADS, HEAD_DIM)
    key_heads = gathered[:, :width].reshape(total_rows, HEADS, HEAD_DIM)
    value_heads = gathered[:, width:].reshape(total_rows, HEADS, HEAD_DIM)
    scores = (
        jnp.einsum("thd,nhd->htn", queries, key_heads, preferred_element_type=jnp.float32) * factor
    )
    probabilities = jnp.exp(scores - log_total)
    prob_grads = jnp.einsum(
        "thd,nhd->htn", mixed_heads, value_heads, preferred_element_type=jnp.float32
    )
    centre = jnp.sum(prob_grads * probabilities, axis=-1, keepdims=True)
    score_grads = (probabilities * (prob_grads - centre)).astype(jnp.bfloat16)
    query_grads = (
        jnp.einsum("htn,nhd->thd", score_grads, key_heads, preferred_element_type=jnp.float32)
        * factor
    )
    value_grads = jnp.einsum(
        "htn,thd->nhd",
        probabilities.astype(jnp.bfloat16),
        mixed_heads,
        preferred_element_type=jnp.float32,
    )
    key_grads = (
        jnp.einsum("htn,thd->nhd", score_grads, queries, preferred_element_type=jnp.float32)
        * factor
    )
    key_value_grads = jnp.concatenate(
        [key_grads.reshape(total_rows, width), value_grads.reshape(total_rows, width)], axis=1
    )
    local_grads = spread_keys(key_value_grads)
    projected_grad = jnp.concatenate(
        [query_grads.reshape(local_rows, width), local_grads], axis=1
    ).astype(jnp.bfloat16)
    normed_grad = jnp.dot(projected_grad, weight_qkv.T, preferred_element_type=jnp.float32)
    qkv_grad = jnp.dot(normed.T, projected_grad, preferred_element_type=jnp.float32)
    _, first_back = jax.vjp(pre_norm, current, shift_attn, scale_attn)
    current_part, shift_attn_grad, scale_attn_grad = first_back(normed_grad)
    input_grad = middle_grad + current_part
    modulation_grad = jnp.concatenate(
        [
            shift_attn_grad,
            scale_attn_grad,
            gate_attn_grad,
            shift_mlp_grad,
            scale_mlp_grad,
            gate_mlp_grad,
        ]
    )
    return (input_grad, (qkv_grad, out_grad, up_grad, down_grad, modulation_grad))


def shards(fields, lead_index, rollout, w_qkv, w_out, w_up, w_down, w_ada, b_ada, cotangent):
    _, rows_dev, cols_dev, width = fields.shape
    local_rows = rows_dev * cols_dev
    layer_count = w_qkv.shape[0]
    context = jax.nn.silu(embedding(lead_index[0])).astype(jnp.bfloat16)
    context_wide = context.astype(jnp.float32)
    modulations = [
        (
            jnp.dot(context[None, :], w_ada[index], preferred_element_type=jnp.float32)[0]
            + b_ada[index]
        ).reshape(6, width)
        for index in range(layer_count)
    ]
    weight_sets = [
        (w_qkv[index], w_out[index], w_up[index], w_down[index]) for index in range(layer_count)
    ]
    count = rollout[0]
    current = fields.reshape(local_rows, width).astype(jnp.float32)
    saved = []
    for rollout_step in range(STEPS):
        updated = current
        kept_layers = []
        for index in range(layer_count):
            updated, kept = forward_layer(updated, modulations[index], *weight_sets[index])
            kept_layers.append(kept)
        current = jnp.where(rollout_step < count, updated, current)
        saved.append(kept_layers)
    gradient = cotangent.reshape(local_rows, width).astype(jnp.float32)
    summed = None
    shares = None
    for rollout_step in reversed(range(STEPS)):
        active = (rollout_step < count).astype(jnp.float32)
        inner = gradient * active
        layer_terms = [None] * layer_count
        for index in reversed(range(layer_count)):
            inner, layer_terms[index] = backward_layer(
                inner, saved[rollout_step][index], modulations[index], *weight_sets[index]
            )
        gradient = inner + (1.0 - active) * gradient
        modulation_grads = jnp.stack([terms[4] for terms in layer_terms])
        step_terms = (
            jnp.stack([terms[0] for terms in layer_terms]),
            jnp.stack([terms[1] for terms in layer_terms]),
            jnp.stack([terms[2] for terms in layer_terms]),
            jnp.stack([terms[3] for terms in layer_terms]),
            context_wide[None, :, None] * modulation_grads[:, None, :],
            modulation_grads,
            modulation_grads[:, 3 * width : 4 * width],
        )
        summed = step_terms if summed is None else jax.tree.map(jnp.add, summed, step_terms)
    shares = lax.psum_scatter(summed, ("lat", "lon"), scatter_dimension=1, tiled=True)
    totals = jax.tree.map(
        lambda part: part.astype(jnp.float32), lax.psum(shortened(shares), "item")
    )
    return (
        current.reshape(1, rows_dev, cols_dev, width),
        gradient.reshape(1, rows_dev, cols_dev, width),
        totals[0],
        totals[1],
        totals[2],
        totals[3],
        totals[4],
        totals[5],
        totals[6],
    )


F32 = jnp.float32
BF16 = jnp.bfloat16
GELU_A = math.sqrt(2.0 / math.pi)
GELU_B = 0.044715
LANES = 128
BLOCK = 256
PAIR = 2 * HEAD_DIM
SUM_ROWS = 48
ONES = 16
SAFE_SCORE = 60.0


def nn(left, right, precision=None):
    return lax.dot_general(
        left, right, (((1,), (0,)), ((), ())), preferred_element_type=F32, precision=precision
    )


def nt(left, right, precision=None):
    return lax.dot_general(
        left, right, (((1,), (1,)), ((), ())), preferred_element_type=F32, precision=precision
    )


def identity(size):
    rows = lax.broadcasted_iota(jnp.int32, (size, size), 0)
    columns = lax.broadcasted_iota(jnp.int32, (size, size), 1)
    return jnp.where(rows == columns, 1.0, 0.0).astype(BF16)


def turned(values):
    return nt(identity(values.shape[1]), values).astype(BF16)


def wide(column_tile, lanes):
    return jnp.concatenate([column_tile] * (lanes // LANES), axis=1)


def folded(values):
    pieces = [values[:, at : at + LANES] for at in range(0, values.shape[1], LANES)]
    return sum(pieces[1:], pieces[0])


def standardise(values):
    rows = values.shape[0]
    centred = values - jnp.sum(values, axis=0, keepdims=True) * (1.0 / rows)
    variance = jnp.sum(centred * centred, axis=0, keepdims=True) * (1.0 / rows)
    scale = lax.rsqrt(variance + 1e-06)
    return centred * scale, scale


def pre_norm_back(standard, scale, grad, gain):
    rows = standard.shape[0]
    inner = grad * gain
    first = jnp.sum(inner, axis=0, keepdims=True) * (1.0 / rows)
    second = jnp.sum(inner * standard, axis=0, keepdims=True) * (1.0 / rows)
    return scale * (inner - first - standard * second)


def part(mod_ref, index, lanes):
    return wide(mod_ref[index * D : (index + 1) * D, :], lanes)


def turn_into(source, out, at=0):
    for column in range(0, out.shape[0], BLOCK):
        width = min(BLOCK, out.shape[0] - column)
        out[column : column + width, :] = turned(source[:, at + column : at + column + width])


def prepare_first(mod, w_q_t, w_v_t, w_k, w_qkv, w_ada, b_ada, context):
    w_k[...] = w_qkv[:, D : 2 * D]
    turn_into(w_qkv, w_q_t)
    turn_into(w_qkv, w_v_t, 2 * D)
    values = nn(context[...], w_ada[...])[0:1] + b_ada
    for column in range(0, values.shape[1], LANES):
        tile = jnp.broadcast_to(values[:, column : column + LANES], (LANES, LANES))
        mod[column : column + LANES, :] = tile.T


def prepare_kernel(context, *refs):
    w_qkv, w_ada, b_ada, w_out, w_up, w_down = refs[:6]
    outs, scratch, sems = refs[8:19], refs[19:-1], refs[-1]
    sources = [w_qkv.at[0], w_ada.at[0], b_ada, w_out.at[0], w_up.at[0], w_down.at[0], w_qkv.at[1], w_ada.at[1]]
    copies = [
        pltpu.make_async_copy(source, target, sems.at[place])
        for place, (source, target) in enumerate(zip(sources, scratch))
    ]
    for copy in copies:
        copy.start()
    for copy in copies[:3]:
        copy.wait()
    prepare_first(*outs[0:4], scratch[0], scratch[1], scratch[2][0:1, :], context)
    for copy, source, out in zip(copies[3:6], scratch[3:6], outs[8:11]):
        copy.wait()
        turn_into(source, out)
    for copy in copies[6:]:
        copy.wait()
    prepare_first(*outs[4:8], scratch[6], scratch[7], scratch[2][1:2, :], context)


def prepare_rest_kernel(index, early, w_out, w_up, w_down, *outs):
    for weight, out in zip((w_out, w_up, w_down), outs):
        turn_into(weight.at[index], out)


def project(x, mod_ref, w_q_t, w_v_t, w_k, outs):
    q_out, kn_out, vt_out = outs
    lanes = x.shape[1]
    standard, _ = standardise(x)
    normed = (standard * (1.0 + part(mod_ref, 1, lanes)) + part(mod_ref, 0, lanes)).astype(BF16)
    vt_out[...] = nn(w_v_t[...], normed).astype(BF16)
    q_out[...] = (nn(w_q_t[...], normed) * HEAD_DIM ** (-0.5)).astype(BF16)
    for at in range(0, lanes, BLOCK):
        kn_out[at : at + BLOCK, :] = nn(turned(normed[:, at : at + BLOCK]), w_k[...]).astype(BF16)


def first_kernel(own, flip_x, flip_y, flip_xy, mod, w_q_t, w_v_t, w_k, x_out, xb_out, *outs):
    for index, ref in enumerate((own, flip_x, flip_y, flip_xy)):
        rows = ref.shape[0]
        flat = turned(ref[...])
        xb_out[:, index * rows : (index + 1) * rows] = flat
        x_out[:, index * rows : (index + 1) * rows] = flat.astype(F32)
    project(x_out[...], mod, w_q_t, w_v_t, w_k, outs)


def head_rows(head):
    return slice(head * HEAD_DIM, (head + 1) * HEAD_DIM)


def pair_columns(head):
    return slice(head // 2 * PAIR, (head // 2 + 1) * PAIR)


def padded(rows, head):
    zeros = jnp.zeros_like(rows)
    return jnp.concatenate([rows, zeros] if head % 2 == 0 else [zeros, rows], axis=0)


def query_top(q):
    square = q[...].astype(F32)
    square = square * square
    norms = [jnp.sum(square[head_rows(head)], axis=0, keepdims=True) for head in range(HEADS)]
    return jnp.max(functools.reduce(jnp.maximum, norms), axis=1, keepdims=True)


def key_top(kn):
    first = lax.broadcasted_iota(jnp.int32, (D, LANES), 1) * HEAD_DIM
    row = lax.broadcasted_iota(jnp.int32, (D, LANES), 0)
    pick = jnp.where((row >= first) & (row < first + HEAD_DIM), 1.0, 0.0).astype(BF16)
    square = kn[...].astype(F32)
    norms = nn((square * square).astype(BF16), pick)
    return jnp.max(jnp.max(norms, axis=0, keepdims=True), axis=1, keepdims=True) * 1.02


def value_rows(vt, rows, at):
    values = vt[rows, at]
    return jnp.concatenate([values, jnp.ones((ONES, values.shape[1]), BF16)], axis=0)


def attend_plain(q, kn, vt, put):
    steps = [(head, slice(at, at + BLOCK)) for head in range(HEADS) for at in range(0, kn.shape[0], BLOCK)]
    last_at = steps[-1][1]

    def score(head, at):
        return nn(kn[at, pair_columns(head)], padded(q[head_rows(head), :], head))

    totals = {}

    def finish(head, at, probs):
        term = nn(value_rows(vt, head_rows(head), at), probs)
        totals[head] = totals[head] + term if head in totals else term
        if at == last_at:
            put(head, totals[head])

    waiting = None
    following = score(*steps[0])
    for place, (head, at) in enumerate(steps):
        scores = following
        if place + 1 < len(steps):
            following = score(*steps[place + 1])
        if waiting is not None:
            finish(*waiting)
        waiting = (head, at, jnp.exp(scores).astype(BF16))
    finish(*waiting)


def attend_own_kernel(early, *refs):
    q, kn, vt, *refs = refs[early:]
    passing = []
    if len(refs) > 2:
        *passing, sums, tops, passed = refs
    else:
        sums, tops = refs
    at = 0
    for source in passing:
        rows = source.shape[0]
        passed[at : at + rows, :] = source[...]
        at += rows

    def put(head, total):
        sums[head] = total

    query, key = query_top(q), key_top(kn)
    tops[0:8, :] = jnp.broadcast_to(query, (8, LANES))
    tops[8:16, :] = jnp.broadcast_to(key, (8, LANES))

    @pl.when(jnp.max(query * key) < SAFE_SCORE**2)
    def _():
        attend_plain(q, kn, vt, put)


def forward_kernel(last, early, *refs):
    refs = refs[early:]
    if last:
        active, x, x_step, *refs = refs
    else:
        x, *refs = refs
    q, kn_own, kn_far, vt_own, vt_far, sums, tops, mod, w_out_t, w_up_t, w_down_t, *refs = refs
    if not last:
        mod_next, w_q_t, w_v_t, w_k, *refs = refs
    lse, mixed, attended, middle, hidden, slope, branch, *refs = refs
    if last:
        (final,) = refs
    else:
        x_next, xb_next, *next_outs = refs
    patches = x.shape[1]
    bound = tops[0:1, 0:1] * jnp.maximum(tops[8:9, 0:1], key_top(kn_far))
    safe = jnp.max(bound) < SAFE_SCORE**2

    def put(head, total):
        total = sums[head] + total
        weight = total[HEAD_DIM : HEAD_DIM + 1]
        mixed[head_rows(head), :] = (total[:HEAD_DIM] * (1.0 / weight)).astype(BF16)
        lse[head : head + 1, :] = jnp.log(weight)

    @pl.when(safe)
    def _():
        attend_plain(q, kn_far, vt_far, put)

    @pl.when(jnp.logical_not(safe))
    def _():
        def pair_heads(pair, _):
            columns = pl.ds(pl.multiple_of(pair * PAIR, PAIR), PAIR)
            for head in range(2):
                rows = pl.ds(pl.multiple_of(pair * PAIR + head * HEAD_DIM, HEAD_DIM), HEAD_DIM)
                query = padded(q[rows, :], head)
                scores = [nn(kn[:, columns], query) for kn in (kn_own, kn_far)]
                tops = [jnp.max(score, axis=0, keepdims=True) for score in scores]
                top = jnp.maximum(*tops)
                total = None
                for score, vt in zip(scores, (vt_own, vt_far)):
                    term = nn(value_rows(vt, rows, slice(None)), jnp.exp(score - top).astype(BF16))
                    total = term if total is None else total + term
                weight = total[HEAD_DIM : HEAD_DIM + 1]
                mixed[rows, :] = (total[:HEAD_DIM] * (1.0 / weight)).astype(BF16)
                lse[pl.ds(pair * 2 + head, 1), :] = top + jnp.log(weight)
            return 0

        lax.fori_loop(0, HEADS // 2, pair_heads, 0)

    att = nn(w_out_t[...], mixed[...])
    attended[...] = att.astype(BF16)
    mid = x[...] + part(mod, 2, patches) * att
    middle[...] = mid.astype(BF16)
    standard, _ = standardise(mid)
    hidden_in = (standard * (1.0 + part(mod, 4, patches)) + part(mod, 3, patches)).astype(BF16)
    chunks = [slice(at, at + BLOCK) for at in range(0, w_up_t.shape[0], BLOCK)]
    down = None
    waiting = None
    following = nn(w_up_t[chunks[0], :], hidden_in)
    for place, rows in enumerate(chunks):
        act = following
        if place + 1 < len(chunks):
            following = nn(w_up_t[chunks[place + 1], :], hidden_in)
        if place > 0:
            term = nn(w_down_t[:, chunks[place - 1]], waiting)
            down = term if down is None else down + term
        act = act.astype(BF16)
        inner = GELU_A + (GELU_A * GELU_B) * (act * act)
        half = 0.5 + 0.5 * jnp.tanh(act * inner)
        waiting = gelu = act * half
        hidden[rows, :] = waiting
        slope[rows, :] = (half + (gelu - gelu * half) * (6.0 * inner - 4.0 * GELU_A))
    down = down + nn(w_down_t[:, chunks[-1]], waiting)
    branch[...] = down.astype(BF16)
    out = mid + part(mod, 5, patches) * down
    if last:
        own = final.shape[0]
        final[...] = jnp.where(active[0] > 0.0, out[:, :own], x_step[:, :own]).T
    else:
        x_next[...] = out
        xb_next[...] = out.astype(BF16)
        project(out, mod_next, w_q_t, w_v_t, w_k, next_outs)


def put_grads(left_ref, right, where, count, at, mine, other, before):
    rows = [left_ref[pl.ds(pl.multiple_of(where[place] * count, 16), count), :] for place in range(2)]
    product = nt(jnp.concatenate(rows, axis=0), right)
    for column in range(0, product.shape[1], LANES):
        low = product[:count, column : column + LANES]
        high = product[count:, column : column + LANES]
        if before is not None:
            low = low + before[0][at : at + count, :]
            high = high + before[1][at : at + count, :]
        mine[at : at + count, :] = low.astype(mine.dtype)
        other[at : at + count, :] = high.astype(other.dtype)
        at += count


def dense_back_kernel(has_close, has_open, has_before, start, layers, waits, *refs):
    refs = list(refs)

    def take(count):
        taken = refs[:count]
        del refs[:count]
        return taken

    take(waits)
    where, active = take(2)
    close_before = open_before = None
    if has_close:
        d_own, d_got, dq, d_mid_in, x_in, mod_in, w_qkv = take(7)
        w_qkv = w_qkv.at[layers[0]]
        if has_before[0]:
            close_before = take(3)
    if start == "first":
        cots = take(2)
    elif start == "cross":
        cots = take(1)
    if has_open:
        mixed, attended, middle, hidden, slope, branch, mod, w_out, w_up, w_down = take(10)
        w_out, w_up, w_down = (ref.at[layers[1]] for ref in (w_out, w_up, w_down))
        if has_before[1]:
            open_before = take(3)
    else:
        (lines,) = take(1)
    if has_close:
        close_mine, close_other, close_mods = take(3)
    if start == "first":
        (cot_out,) = take(1)
    if has_open:
        open_mine, open_other, open_mods, d_mid_out, do_out, cen_out = take(6)
    else:
        g_out, sums_out = take(2)
        sums_at = close_before[1].shape[0]
    if has_close:
        grads_scr, normed_scr = take(2)
    if has_open:
        bg_scr, pg_scr, hin_scr, ag_scr = take(4)

    patches = middle.shape[1] if has_open else x_in.shape[1]
    totals = {}

    def add_sums(name, values):
        totals[name] = totals[name] + folded(values) if name in totals else folded(values)

    def put_sums(out, before, names):
        for place, name in enumerate(names):
            rows = slice(place * D, (place + 1) * D)
            out[rows, :] = totals[name] + before[2][rows, :] if before else totals[name]

    if start == "first":
        for index, ref in enumerate(cots):
            rows = ref.shape[0]
            cot_out[:, index * rows : (index + 1) * rows] = turned(ref[...])

    def close(at):
        standard, scale = standardise(x_in[:, at].astype(F32))
        gain = 1.0 + part(mod_in, 1, patches)
        normed_scr[:, at] = (standard * gain + part(mod_in, 0, patches)).astype(BF16)
        for third in range(3):
            if third == 0:
                piece = dq[:, at]
            else:
                rows = slice((third - 1) * D, third * D)
                piece = (d_own[rows, at] + d_got[rows, at].astype(F32)).astype(BF16)
            grads_scr[third * D : (third + 1) * D, at] = piece
        back = nn(w_qkv[...], grads_scr[:, at])
        add_sums("shift_a", back)
        add_sums("scale_a", back * standard)
        g = d_mid_in[:, at] + pre_norm_back(standard, scale, back, gain)
        if start == "cross":
            g = g + (1.0 - active[0]) * cots[0][:, at].astype(F32)
        return g

    def dense(at, g):
        standard, scale = standardise(middle[:, at].astype(F32))
        gain = 1.0 + part(mod, 4, patches)
        hin_scr[:, at] = (standard * gain + part(mod, 3, patches)).astype(BF16)
        branch_grad = (part(mod, 5, patches) * g).astype(BF16)
        bg_scr[:, at] = branch_grad
        add_sums("gate_m", g * branch[:, at].astype(F32))
        chunks = [slice(start, start + BLOCK) for start in range(0, w_down.shape[0], BLOCK)]
        back = None
        waiting = None
        following = nn(w_down[chunks[0], :], branch_grad)
        for place, rows in enumerate(chunks):
            hidden_grad = following
            if place + 1 < len(chunks):
                following = nn(w_down[chunks[place + 1], :], branch_grad)
            if place > 0:
                term = nn(w_up[:, chunks[place - 1]], waiting)
                back = term if back is None else back + term
            waiting = (slope[rows, at].astype(F32) * hidden_grad).astype(BF16)
            pg_scr[rows, at] = waiting
        back = back + nn(w_up[:, chunks[-1]], waiting)
        add_sums("shift_m", back)
        add_sums("scale_m", back * standard)
        d_mid = g + pre_norm_back(standard, scale, back, gain)
        d_mid_out[:, at] = d_mid
        att_grad = (part(mod, 2, patches) * d_mid).astype(BF16)
        ag_scr[:, at] = att_grad
        mixed_grad = nn(w_out[...], att_grad).astype(BF16)
        do_out[:, at] = mixed_grad
        add_sums("gate_a", d_mid * attended[:, at].astype(F32))
        product = mixed_grad.astype(F32) * mixed[:, at].astype(F32)
        for head in range(HEADS):
            cen_out[head : head + 1, at] = jnp.sum(product[head_rows(head)], axis=0, keepdims=True)

    at = slice(0, patches)
    g = close(at) if has_close else cot_out[:, at].astype(F32) * active[0]
    if has_open:
        dense(at, g)
    else:
        g_out[...] = g[:, : g_out.shape[0]].T
    if has_close:
        put_sums(close_mods, close_before, ("shift_a", "scale_a"))
        put_grads(normed_scr, grads_scr[...], where, D // 8, 0, close_mine, close_other, close_before)
    if has_open:
        put_sums(open_mods, open_before, ("gate_a", "shift_m", "scale_m", "gate_m"))
        count = w_down.shape[0] // 8
        put_grads(hidden, bg_scr[...], where, count, 0, open_mine, open_other, open_before)
        at = count * (D // LANES)
        put_grads(hin_scr, pg_scr[...], where, D // 8, at, open_mine, open_other, open_before)
        at += (w_up.shape[1] // LANES) * (D // 8)
        put_grads(mixed, ag_scr[...], where, D // 8, at, open_mine, open_other, open_before)
    else:
        sums_out[...] = lines[...]
        put_lines(sums_out, 0, close_mods[...])
        close_other[sums_at:, :] = sums_out[...].astype(BF16)


def attend_back_kernel(has_before, waits, q, kn, vt, lse, d_out, centre, *refs):
    if has_before:
        before, *refs = refs
    d_kv, dq_out, kt_scr, vn_scr = refs[waits:]
    for column in range(0, D, LANES):
        kt_scr[column : column + LANES, :] = turned(kn[:, column : column + LANES])
    for column in range(0, vt.shape[1], BLOCK):
        vn_scr[column : column + BLOCK, :] = turned(vt[:, column : column + BLOCK])

    steps = [(head, slice(at, at + BLOCK)) for head in range(HEADS) for at in range(0, kn.shape[0], BLOCK)]

    def score(head, at):
        columns = pair_columns(head)
        rows = head_rows(head)
        return nn(kn[at, columns], padded(q[rows, :], head)), nn(vn_scr[at, columns], padded(d_out[rows, :], head))

    totals = {}

    def finish(head, at, probs, score_grads):
        rows = head_rows(head)
        d_kv[D + rows.start : D + rows.stop, at] = nt(d_out[rows, :], probs).astype(d_kv.dtype)
        d_kv[rows, at] = nt(q[rows, :], score_grads).astype(d_kv.dtype)
        term = nn(kt_scr[rows, at], score_grads)
        if head not in totals:
            totals[head] = before[rows, :] + term if has_before else term
            return
        term = totals[head] + term
        if has_before:
            term = term * HEAD_DIM ** (-0.5)
        dq_out[rows, :] = term.astype(dq_out.dtype)

    waiting = None
    following = score(*steps[0])
    for place, (head, at) in enumerate(steps):
        scores, prob_grads = following
        if place + 1 < len(steps):
            following = score(*steps[place + 1])
        if waiting is not None:
            finish(*waiting)
        probs = jnp.exp(scores - lse[head : head + 1, :])
        score_grads = (probs * (prob_grads - centre[head : head + 1, :])).astype(BF16)
        waiting = (head, at, probs.astype(BF16), score_grads)
    finish(*waiting)


def split_kernel(waits, where, *refs):
    *halves, keep, sent, total_scr = refs[waits:]
    rows_half = keep.shape[0]
    at = 0
    for mine, other in zip(halves[::2], halves[1::2]):
        rows = mine.shape[0]
        total_scr[at : at + rows, :] = mine[...] + other[...].astype(F32)
        at += rows
    if at < total_scr.shape[0]:
        total_scr[at:, :] = jnp.zeros((total_scr.shape[0] - at, LANES), F32)
    odd = where[3]
    keep[...] = total_scr[pl.ds(pl.multiple_of(odd * rows_half, 16), rows_half), :]
    sent[...] = total_scr[pl.ds(pl.multiple_of((1 - odd) * rows_half, 16), rows_half), :].astype(BF16)


def pair_sum_kernel(late, *refs):
    count = len(refs) // 3
    for keep, got, out in zip(refs[:count], refs[count : 2 * count], refs[2 * count :]):
        out[...] = (keep[...].astype(F32) + got[...].astype(F32)).astype(BF16)


def put_lines(out, row, values):
    ones = jnp.ones((16, LANES), BF16)
    high = values.astype(BF16)
    low = (values - high.astype(F32)).astype(BF16)
    line = (nt(ones, high) + nt(ones, low))[0:1]
    for column in range(0, line.shape[1], LANES):
        out[row : row + 1, :] = line[:, column : column + LANES]
        row += 1
    return row


def lines_kernel(early, context, *refs):
    *sums, out = refs
    out[...] = jnp.zeros_like(out)
    row = 2 * D // LANES
    for ref in sums:
        row = put_lines(out, row, ref[...])
    for column in range(0, D, LANES):
        out[row : row + 1, :] = context[0:1, column : column + LANES].astype(F32)
        row += 1


def join_kernel(sum_count, early, mine, sums, got, out):
    rows = mine.shape[0]
    out[:rows, :] = (mine[...] + got[:rows, :].astype(F32)).astype(BF16)
    other = got[rows:, :].astype(F32)
    summed = lax.broadcasted_iota(jnp.int32, (SUM_ROWS, LANES), 0) < sum_count
    out[rows:, :] = (sums[...] + jnp.where(summed, other, 0.0)).astype(BF16)


def pair_kernel(rows, where, own, got, out):
    out[:rows, :] = (own[:rows, :].astype(F32) + got[:rows, :].astype(F32)).astype(BF16)
    odd = where[3]
    size = SUM_ROWS
    out[pl.ds(pl.multiple_of(rows + odd * size, 16), size), :] = own[rows:, :]
    out[pl.ds(pl.multiple_of(rows + (1 - odd) * size, 16), size), :] = got[rows:, :]


def gather_kernel(where, *refs):
    halves, (out_out, up_out, down_out, qkv_out), scratch = refs[:4], refs[4:8], refs[8:]
    odd = where[3]
    for ref, own, got in zip(scratch, halves[::2], halves[1::2]):
        rows = own.shape[0]
        ref[pl.ds(pl.multiple_of(odd * rows, 16), rows), :] = own[...]
        ref[pl.ds(pl.multiple_of((1 - odd) * rows, 16), rows), :] = got[...]
    slice_rows = out_out.shape[1]
    for index, ref in enumerate(scratch):
        at = 0
        for out in (down_out, up_out, out_out):
            rows = out.shape[1]
            for column in range(0, out.shape[2], LANES):
                out[index, :, column : column + LANES] = ref[at : at + rows, :].astype(F32)
                at += rows
        if index == 0:
            for column in range(0, qkv_out.shape[1], LANES):
                qkv_out[:, column : column + LANES] = ref[at : at + slice_rows, :].astype(F32)
                at += slice_rows


def finish_kernel(item_count, where, own, got, qkv_1, qkv_out, ada_out, bias_out, shift_out, sum_scr, bias_scr, shift_scr):
    layers = 2
    device, high = where[0], where[4]
    slice_rows = qkv_out.shape[1]
    close_rows = slice_rows * (3 * D // LANES)
    for other in range(2):
        rows = slice(close_rows + other * SUM_ROWS, close_rows + (other + 1) * SUM_ROWS)
        sum_scr[2 * high + other] = own[rows, :].astype(F32)
        sum_scr[2 * (1 - high) + other] = got[rows, :].astype(F32)
    qkv_out[1] = qkv_1[...]
    for tile in range(3 * D // LANES):
        rows = slice(tile * slice_rows, (tile + 1) * slice_rows)
        total = own[rows, :].astype(F32) + got[rows, :].astype(F32)
        qkv_out[0, :, tile * LANES : (tile + 1) * LANES] = total
    tiles = 6 * D // LANES
    contexts = []
    for other in range(item_count):
        line = jnp.concatenate([sum_scr[other, layers * tiles + c : layers * tiles + c + 1, :] for c in range(3)], axis=1)
        contexts.append(line)
    square = jnp.concatenate(contexts + [jnp.zeros((8 - item_count, D), F32)], axis=0)
    spot = lax.broadcasted_iota(jnp.int32, (slice_rows, D), 1)
    want = lax.broadcasted_iota(jnp.int32, (slice_rows, D), 0) + device * slice_rows
    pick = jnp.where(spot == want, 1.0, 0.0).astype(BF16)
    columns = nt(pick, square.astype(BF16))
    bias_rows = bias_out.shape[1]
    for index in range(layers):
        flats = []
        for tile in range(tiles):
            row = index * tiles + tile
            total = None
            flat = None
            for other in range(item_count):
                line = sum_scr[other, row : row + 1, :]
                term = columns[:, other : other + 1] * line
                total = term if total is None else total + term
                flat = line if flat is None else flat + line
            ada_out[index, :, tile * LANES : (tile + 1) * LANES] = total
            flats.append(flat)
        flat = jnp.concatenate(flats, axis=1)
        for place in range(flat.shape[1] // bias_rows):
            bias_scr[place, index : index + 1, :] = flat[:, place * bias_rows : (place + 1) * bias_rows]
            at = 3 * D + place * slice_rows
            shift_scr[place, index : index + 1, :] = flat[:, at : at + slice_rows]
    bias_out[...] = bias_scr[device]
    shift_out[...] = shift_scr[device]


VMEM = pl.BlockSpec(memory_space=pltpu.VMEM)
SMEM = pl.BlockSpec(memory_space=pltpu.SMEM)
ANY = pl.BlockSpec(memory_space=pl.ANY)
HBM = pl.BlockSpec(memory_space=pltpu.HBM)


def layer_block(array, index):
    return pl.BlockSpec((None,) + array.shape[1:], lambda step: (index,) + (0,) * (array.ndim - 1))


def call(body, args, outs, scratch=(), flops=0, name=None):
    arrays = [arg[0] if isinstance(arg, tuple) else arg for arg in args]
    specs = [arg[1] if isinstance(arg, tuple) else VMEM for arg in args]
    return pl.pallas_call(
        body,
        out_shape=[jax.ShapeDtypeStruct(shape, kind) for shape, kind in outs],
        in_specs=specs,
        out_specs=[VMEM] * len(outs),
        scratch_shapes=[one if not isinstance(one, tuple) else pltpu.VMEM(*one) for one in scratch],
        compiler_params=pltpu.CompilerParams(vmem_limit_bytes=VMEM_LIMIT),
        cost_estimate=pl.CostEstimate(flops=flops, bytes_accessed=0, transcendentals=0),
        name=name,
    )(*arrays)


VMEM_LIMIT = 14 * 1024 * 1024


def fast_shards(
    lat_count, lon_count, item_count,
    fields, lead_index, rollout, w_qkv, w_out, w_up, w_down, w_ada, b_ada, cotangent,
):
    _, rows_dev, cols_dev, width = fields.shape
    local = rows_dev * cols_dev
    layers = w_qkv.shape[0]
    ff = w_up.shape[2]
    patches = 4 * local
    device = lax.axis_index("lat") * lon_count + lax.axis_index("lon")
    item = lax.axis_index("item")
    where = jnp.stack([device, device ^ 1, item, item & 1, item >> 1]).astype(jnp.int32)
    active = (1 < rollout[0]).astype(F32)[None]

    def plane_flip(value, flip_lat, flip_y):
        pairs = [
            (a * lon_count + b, (a ^ flip_lat) * lon_count + (b ^ (2 * flip_y)))
            for a in range(lat_count)
            for b in range(lon_count)
        ]
        return lax.ppermute(value, ("lat", "lon"), pairs)

    def swap(value):
        return lax.ppermute(value, "lon", [(index, index ^ 1) for index in range(lon_count)])

    def with_item(value, flip):
        return lax.ppermute(value, "item", [(index, index ^ flip) for index in range(item_count)])

    def plane_parts(value):
        return [value, plane_flip(value, 1, 0), plane_flip(value, 0, 1), plane_flip(value, 1, 1)]

    field_parts = plane_parts(fields.reshape(local, width))

    context = jax.nn.silu(embedding(lead_index[0])).astype(BF16)
    context = jnp.broadcast_to(context[None, :], (16, width))
    square = (width, patches)
    natural = (patches, width)
    weights = (w_qkv, w_ada, b_ada, w_out, w_up, w_down)
    weights = [(pltpu.with_memory_space_constraint(value, pltpu.HBM), HBM) for value in weights]
    first_outs = [((6 * width, LANES), F32)] + [((width, width), BF16)] * 3
    rest_outs = [((width, width), BF16), ((ff, width), BF16), ((width, ff), BF16)]
    first_fetch = [((width, 3 * width), BF16), ((width, 6 * width), BF16)]
    rest_fetch = [((width, width), BF16), ((width, ff), BF16), ((ff, width), BF16)]
    prepared = call(
        prepare_kernel,
        [context, *weights, (where, SMEM), (active, SMEM)],
        first_outs * 2 + rest_outs,
        first_fetch + [(b_ada.shape, F32)] + rest_fetch + first_fetch + [pltpu.SemaphoreType.DMA((8,))],
        name="prepare",
    )
    first_parts = [prepared[0:4], prepared[4:8]]
    rest_parts = [prepared[8:11]]
    mods = [one[0] for one in first_parts]

    project_outs = [(square, F32), (square, BF16), (square, BF16), (natural, BF16), (square, BF16)]
    dense_flops = 2 * patches * (width * 3 * width + width * width + 2 * width * ff)
    score_flops = 2 * patches * 2 * patches * width * 4
    x, xb, *projected = call(
        first_kernel,
        [*field_parts, *first_parts[0]],
        project_outs,
        flops=2 * patches * width * 4 * width,
        name="first",
    )
    saved = []
    for step in range(STEPS):
        for index in range(layers):
            q, kn, vt = projected
            if len(rest_parts) == index:
                rest_parts.append(
                    call(
                        functools.partial(prepare_rest_kernel, index),
                        [(kn, ANY), w_out, w_up, w_down],
                        rest_outs,
                        name="prepare_rest",
                    )
                )
            kn_far, vt_far = swap(kn), swap(vt)
            early = [w_up] if len(rest_parts) == index + 1 < layers else []
            passing = []
            if step == STEPS - 1:
                passing = [cotangent.reshape(local, width)] if index == 0 else cot_parts
            passed = [((len(passing) * local, width), BF16)] if passing else []
            sums, tops, *passed = call(
                functools.partial(attend_own_kernel, len(early)),
                early + [q, kn, vt] + passing,
                [((HEADS, HEAD_DIM + ONES, patches), F32), ((16, LANES), F32)] + passed,
                flops=10 * score_flops,
                name="forward_own",
            )
            if passed:
                cot_parts = [passed[0], plane_flip(passed[0], 1 - index, index)]
            last = step == STEPS - 1 and index == layers - 1
            if index == 0 and step > 0:
                x_step = x
            following = list(first_parts[(index + 1) % layers])
            early = [w_down] if len(rest_parts) == index + 1 < layers else []
            lse, mixed, attended, middle, hidden, slope, branch, *results = call(
                functools.partial(forward_kernel, last, len(early)),
                early
                + ([(active, SMEM), x, x_step] if last else [x])
                + [q, kn, kn_far, vt, vt_far, sums, tops, mods[index], *rest_parts[index]]
                + ([] if last else following),
                [
                    ((HEADS, patches), F32),
                    (square, BF16),
                    (square, BF16),
                    (square, BF16),
                    ((ff, patches), BF16),
                    ((ff, patches), BF16),
                    (square, BF16),
                ]
                + ([((local, width), F32)] if last else project_outs),
                flops=dense_flops + 2 * score_flops,
                name="forward",
            )
            saved.append((xb, [mixed, attended, middle, hidden, slope, branch], (q, kn, kn_far, vt, vt_far, lse)))
            if last:
                final = results[0]
            else:
                x, xb, *projected = results

    slice_rows = width // 8
    open_rows = 2 * (ff // 8) * (width // LANES) + slice_rows * (width // LANES)
    close_rows = slice_rows * (3 * width // LANES)
    order = [(step, index) for step in reversed(range(STEPS)) for index in reversed(range(layers))]
    open_done = [None] * layers
    close_done = [None] * layers
    pending = None
    for place in range(len(order) + 1):
        has_close = pending is not None
        has_open = place < len(order)
        use = [order[place - 1][1], order[place][1] if has_open else 0]
        waits = []
        if has_close and close_done[use[0]]:
            waits = [pair_1] if has_open else [item_got_1]
        args = [(value, ANY) for value in waits] + [(where, SMEM), (active, SMEM)]
        outs = []
        scratch = []
        has_before = [False, False]
        start = ""
        if has_close:
            args += pending
            if close_done[use[0]] is not None:
                has_before[0] = True
                args += close_done[use[0]]
            outs += [((close_rows, LANES), F32)]
            sent_rows = close_rows + (0 if has_open else SUM_ROWS)
            outs += [((sent_rows, LANES), BF16 if has_before[0] else F32), ((2 * width, LANES), F32)]
            scratch += [((3 * width, patches), BF16), (square, BF16)]
        if place == 0:
            start = "first"
            args += cot_parts
            outs += [(square, BF16)]
        elif has_open and order[place][0] != order[place - 1][0]:
            start = "cross"
            args += [cot_t]
        if has_open:
            step, index = order[place]
            xb, kept, heads = saved[step * layers + index]
            args += kept + [mods[index], w_out, w_up, w_down]
            if open_done[index] is not None:
                has_before[1] = True
                args += open_done[index]
            outs += [
                ((open_rows, LANES), F32),
                ((open_rows, LANES), BF16 if has_before[1] else F32),
                ((4 * width, LANES), F32),
                (square, F32),
                (square, BF16),
                ((HEADS, patches), F32),
            ]
            scratch += [(square, BF16), ((ff, patches), BF16), (square, BF16), (square, BF16)]
        else:
            args += [lines]
            outs += [((local, width), F32), ((SUM_ROWS, LANES), F32)]
        results = list(
            call(
                functools.partial(dense_back_kernel, has_close, has_open, has_before, start, use, len(waits)),
                args,
                outs,
                scratch,
                flops=2 * dense_flops if has_open else 0,
                name="dense_back" if has_open else "close_back",
            )
        )
        if has_close:
            close_done[use[0]] = results[:3]
            del results[:3]
        if start == "first":
            cot_t = results.pop(0)
        if not has_open:
            gradient, line = results
            break
        open_done[index] = results[:3]
        d_mid, d_out, centre = results[3:]
        q, kn, kn_far, vt, vt_far, lse = heads
        halves = [open_done[index][0], open_done[index][1]]
        if index == 0:
            halves += [close_done[1][0], close_done[1][1]]
        half_rows = -(-sum(half.shape[0] for half in halves[::2]) // 32) * 16

        def split(waits):
            pieces = [half if place % 2 == 0 else swap(half) for place, half in enumerate(halves)]
            return call(
                functools.partial(split_kernel, len(waits)),
                [(where, SMEM), *waits, *pieces],
                [((half_rows, LANES), F32), ((half_rows, LANES), BF16)],
                [((2 * half_rows, LANES), F32)],
                name="split",
            )

        def pair_sum(late, keeps, gots):
            outs = [(keep.shape, BF16) for keep in keeps]
            return call(pair_sum_kernel, [(late, ANY), *keeps, *gots], outs, name="pair_sum")

        waits = []
        if has_before[1] and index == 0:
            pair_got_1 = with_item(pair_1, 2)
            lines = call(
                lines_kernel,
                [(pair_got_1, ANY), context, open_done[0][2], close_done[1][2], open_done[1][2]],
                [((SUM_ROWS, LANES), F32)],
                flops=10 * score_flops,
                name="lines",
            )[0]
            keep, sent = split([(lines, ANY)])
            got_0 = with_item(sent, 1)
            waits = [keep]
        d_far, dq = call(
            functools.partial(attend_back_kernel, False, len(waits)),
            [q, kn_far, vt_far, lse, d_out, centre] + [(value, ANY) for value in waits],
            [((2 * width, patches), BF16), (square, F32)],
            [(square, BF16), (natural, BF16)],
            flops=10 * score_flops,
            name="attend_far",
        )
        d_got = swap(d_far)
        waits = []
        if has_before[1]:
            if index == 1:
                keep, sent = split([(d_far, ANY)])
                got_1 = with_item(sent, 1)
                waits = [keep]
            else:
                pair_0, item_1 = pair_sum(d_far, [keep, pair_1], [got_0, pair_got_1])
                item_got_1 = with_item(item_1, 1)
                pair_got_0 = with_item(pair_0, 2)
                waits = [pair_0]
        d_own, dq = call(
            functools.partial(attend_back_kernel, True, len(waits)),
            [q, kn, vt, lse, d_out, centre, dq] + [(value, ANY) for value in waits],
            [((2 * width, patches), F32), (square, BF16)],
            [(square, BF16), (natural, BF16)],
            flops=10 * score_flops,
            name="attend_own",
        )
        if has_before[1] and index == 1:
            (pair_1,) = pair_sum(dq, [keep], [got_1])
        pending = [d_own, d_got, dq, d_mid, xb, mods[index], w_qkv]

    message = call(
        functools.partial(join_kernel, layers * 6 * width // LANES),
        [(pair_got_0, ANY), close_done[0][0], line, swap(close_done[0][1])],
        [((close_rows + SUM_ROWS, LANES), BF16)],
        name="join",
    )[0]
    message_got = with_item(message, 1)
    (item_0,) = pair_sum(message_got, [pair_0], [pair_got_0])
    message = call(
        functools.partial(pair_kernel, close_rows),
        [(where, SMEM), message, message_got],
        [((close_rows + 2 * SUM_ROWS, LANES), BF16)],
        name="pair",
    )[0]
    out_grad, up_grad, down_grad, qkv_1 = call(
        gather_kernel,
        [(where, SMEM), item_0, with_item(item_0, 1), item_1, item_got_1],
        [
            ((layers, slice_rows, width), F32),
            ((layers, slice_rows, ff), F32),
            ((layers, ff // 8, width), F32),
            ((slice_rows, 3 * width), F32),
        ],
        [((2 * pair.shape[0], LANES), BF16) for pair in (pair_0, pair_1)],
        name="gather",
    )
    bias_rows = 6 * width // 8
    qkv_grad, ada_grad, bias_grad, shift_grad = call(
        functools.partial(finish_kernel, item_count),
        [(where, SMEM), message, with_item(message, 2), qkv_1],
        [
            ((layers, slice_rows, 3 * width), F32),
            ((layers, slice_rows, 6 * width), F32),
            ((layers, bias_rows), F32),
            ((layers, slice_rows), F32),
        ],
        [
            ((item_count, SUM_ROWS, LANES), F32),
            ((8, layers, bias_rows), F32),
            ((8, layers, slice_rows), F32),
        ],
        name="finish",
    )
    field_shape = (1, rows_dev, cols_dev, width)
    return (
        final.reshape(field_shape),
        gradient.reshape(field_shape),
        qkv_grad,
        out_grad,
        up_grad,
        down_grad,
        ada_grad,
        bias_grad,
        shift_grad,
    )


def solution(mesh):
    lat_count, lon_count, item_count = mesh.shape["lat"], mesh.shape["lon"], mesh.shape["item"]
    if lat_count == 2 and lon_count == 4:
        body = functools.partial(fast_shards, lat_count, lon_count, item_count)
    else:
        body = shards
    return jax.shard_map(
        body,
        mesh=mesh,
        in_specs=(
            P("item", "lat", "lon", None),
            P("item"),
            P("item"),
            P(),
            P(),
            P(),
            P(),
            P(),
            P(),
            P("item", "lat", "lon", None),
        ),
        out_specs=(
            P("item", "lat", "lon", None),
            P("item", "lat", "lon", None),
            P(None, ("lat", "lon"), None),
            P(None, ("lat", "lon"), None),
            P(None, ("lat", "lon"), None),
            P(None, ("lat", "lon"), None),
            P(None, ("lat", "lon"), None),
            P(None, ("lat", "lon")),
            P(None, ("lat", "lon")),
        ),
        check_vma=False,
    )
```

```python
import functools
import math

import jax
import jax.numpy as jnp
from jax import lax
from jax.experimental import pallas as pl
from jax.experimental.pallas import tpu as pltpu
from jax.sharding import PartitionSpec as P

D = 384
HEADS = 6
HEAD_DIM = 64
STEPS = 2


def shortened(shard):
    return jax.tree.map(lambda a: a.astype(jnp.bfloat16) if a.dtype == jnp.float32 else a, shard)


def embedding(lead):
    half_width = D // 2
    lead_hours = 6.0 * (lead.astype(jnp.float32) + 1.0)
    frequencies = jnp.exp(
        -math.log(10000.0) * jnp.arange(half_width, dtype=jnp.float32) / half_width
    )
    angles = lead_hours * frequencies
    return jnp.concatenate([jnp.sin(angles), jnp.cos(angles)])


def pre_norm(values, shift_part, scale_part):
    centred = values - jnp.mean(values, axis=-1, keepdims=True)
    variance = jnp.mean(centred * centred, axis=-1, keepdims=True)
    return centred * lax.rsqrt(variance + 1e-06) * (1.0 + scale_part) + shift_part


def gather_keys(keys_values):
    band_rows = lax.all_gather(keys_values, "lon", axis=0, tiled=True)
    return lax.all_gather(band_rows, "lat", axis=0, tiled=True)


def spread_keys(key_value_grads):
    band_grads = lax.psum_scatter(
        key_value_grads.astype(jnp.bfloat16), "lat", scatter_dimension=0, tiled=True
    )
    return lax.psum_scatter(band_grads, "lon", scatter_dimension=0, tiled=True).astype(jnp.float32)


def forward_layer(current, modulation, weight_qkv, weight_out, weight_up, weight_down):
    local_rows, width = current.shape
    shift_attn, scale_attn, gate_attn, shift_mlp, scale_mlp, gate_mlp = modulation
    normed = pre_norm(current, shift_attn, scale_attn).astype(jnp.bfloat16)
    projected = jnp.dot(normed, weight_qkv, preferred_element_type=jnp.float32).astype(jnp.bfloat16)
    queries = projected[:, :width].reshape(local_rows, HEADS, HEAD_DIM)
    own_keys = projected[:, width:]
    gathered = gather_keys(own_keys)
    total_rows = gathered.shape[0]
    key_heads = gathered[:, :width].reshape(total_rows, HEADS, HEAD_DIM)
    value_heads = gathered[:, width:].reshape(total_rows, HEADS, HEAD_DIM)
    scores = jnp.einsum(
        "thd,nhd->htn", queries, key_heads, preferred_element_type=jnp.float32
    ) * HEAD_DIM ** (-0.5)
    log_total = jax.nn.logsumexp(scores, axis=-1, keepdims=True)
    probabilities = jnp.exp(scores - log_total).astype(jnp.bfloat16)
    mixed = jnp.einsum(
        "htn,nhd->thd", probabilities, value_heads, preferred_element_type=jnp.float32
    )
    mixed = mixed.reshape(local_rows, width).astype(jnp.bfloat16)
    attended = jnp.dot(mixed, weight_out, preferred_element_type=jnp.float32)
    middle = current + gate_attn * attended
    hidden_in = pre_norm(middle, shift_mlp, scale_mlp).astype(jnp.bfloat16)
    pre_act = jnp.dot(hidden_in, weight_up, preferred_element_type=jnp.float32)
    hidden = jax.nn.gelu(pre_act).astype(jnp.bfloat16)
    branch = jnp.dot(hidden, weight_down, preferred_element_type=jnp.float32)
    output = middle + gate_mlp * branch
    kept = (
        current,
        normed,
        queries,
        gathered,
        own_keys,
        log_total,
        mixed,
        attended,
        middle,
        hidden_in,
        pre_act,
        hidden,
        branch,
    )
    return (output, kept)


def backward_layer(grad_out, kept, modulation, weight_qkv, weight_out, weight_up, weight_down):
    (
        current,
        normed,
        queries,
        gathered,
        own_keys,
        log_total,
        mixed,
        attended,
        middle,
        hidden_in,
        pre_act,
        hidden,
        branch,
    ) = kept
    local_rows, width = current.shape
    total_rows = gathered.shape[0]
    shift_attn, scale_attn, gate_attn, shift_mlp, scale_mlp, gate_mlp = modulation
    factor = HEAD_DIM ** (-0.5)
    branch_grad = (gate_mlp * grad_out).astype(jnp.bfloat16)
    gate_mlp_grad = jnp.sum(grad_out * branch, axis=0)
    hidden_grad = jnp.dot(branch_grad, weight_down.T, preferred_element_type=jnp.float32)
    down_grad = jnp.dot(hidden.T, branch_grad, preferred_element_type=jnp.float32)
    _, gelu_back = jax.vjp(jax.nn.gelu, pre_act)
    pre_grad = gelu_back(hidden_grad)[0].astype(jnp.bfloat16)
    hidden_in_grad = jnp.dot(pre_grad, weight_up.T, preferred_element_type=jnp.float32)
    up_grad = jnp.dot(hidden_in.T, pre_grad, preferred_element_type=jnp.float32)
    _, second_back = jax.vjp(pre_norm, middle, shift_mlp, scale_mlp)
    middle_part, shift_mlp_grad, scale_mlp_grad = second_back(hidden_in_grad)
    middle_grad = grad_out + middle_part
    attended_grad = (gate_attn * middle_grad).astype(jnp.bfloat16)
    gate_attn_grad = jnp.sum(middle_grad * attended, axis=0)
    mixed_grad = jnp.dot(attended_grad, weight_out.T, preferred_element_type=jnp.float32).astype(
        jnp.bfloat16
    )
    out_grad = jnp.dot(mixed.T, attended_grad, preferred_element_type=jnp.float32)
    mixed_heads = mixed_grad.reshape(local_rows, HEADS, HEAD_DIM)
    key_heads = gathered[:, :width].reshape(total_rows, HEADS, HEAD_DIM)
    value_heads = gathered[:, width:].reshape(total_rows, HEADS, HEAD_DIM)
    scores = (
        jnp.einsum("thd,nhd->htn", queries, key_heads, preferred_element_type=jnp.float32) * factor
    )
    probabilities = jnp.exp(scores - log_total)
    prob_grads = jnp.einsum(
        "thd,nhd->htn", mixed_heads, value_heads, preferred_element_type=jnp.float32
    )
    centre = jnp.sum(prob_grads * probabilities, axis=-1, keepdims=True)
    score_grads = (probabilities * (prob_grads - centre)).astype(jnp.bfloat16)
    query_grads = (
        jnp.einsum("htn,nhd->thd", score_grads, key_heads, preferred_element_type=jnp.float32)
        * factor
    )
    value_grads = jnp.einsum(
        "htn,thd->nhd",
        probabilities.astype(jnp.bfloat16),
        mixed_heads,
        preferred_element_type=jnp.float32,
    )
    key_grads = (
        jnp.einsum("htn,thd->nhd", score_grads, queries, preferred_element_type=jnp.float32)
        * factor
    )
    key_value_grads = jnp.concatenate(
        [key_grads.reshape(total_rows, width), value_grads.reshape(total_rows, width)], axis=1
    )
    local_grads = spread_keys(key_value_grads)
    projected_grad = jnp.concatenate(
        [query_grads.reshape(local_rows, width), local_grads], axis=1
    ).astype(jnp.bfloat16)
    normed_grad = jnp.dot(projected_grad, weight_qkv.T, preferred_element_type=jnp.float32)
    qkv_grad = jnp.dot(normed.T, projected_grad, preferred_element_type=jnp.float32)
    _, first_back = jax.vjp(pre_norm, current, shift_attn, scale_attn)
    current_part, shift_attn_grad, scale_attn_grad = first_back(normed_grad)
    input_grad = middle_grad + current_part
    modulation_grad = jnp.concatenate(
        [
            shift_attn_grad,
            scale_attn_grad,
            gate_attn_grad,
            shift_mlp_grad,
            scale_mlp_grad,
            gate_mlp_grad,
        ]
    )
    return (input_grad, (qkv_grad, out_grad, up_grad, down_grad, modulation_grad))


def shards(fields, lead_index, rollout, w_qkv, w_out, w_up, w_down, w_ada, b_ada, cotangent):
    _, rows_dev, cols_dev, width = fields.shape
    local_rows = rows_dev * cols_dev
    layer_count = w_qkv.shape[0]
    context = jax.nn.silu(embedding(lead_index[0])).astype(jnp.bfloat16)
    context_wide = context.astype(jnp.float32)
    modulations = [
        (
            jnp.dot(context[None, :], w_ada[index], preferred_element_type=jnp.float32)[0]
            + b_ada[index]
        ).reshape(6, width)
        for index in range(layer_count)
    ]
    weight_sets = [
        (w_qkv[index], w_out[index], w_up[index], w_down[index]) for index in range(layer_count)
    ]
    count = rollout[0]
    current = fields.reshape(local_rows, width).astype(jnp.float32)
    saved = []
    for rollout_step in range(STEPS):
        updated = current
        kept_layers = []
        for index in range(layer_count):
            updated, kept = forward_layer(updated, modulations[index], *weight_sets[index])
            kept_layers.append(kept)
        current = jnp.where(rollout_step < count, updated, current)
        saved.append(kept_layers)
    gradient = cotangent.reshape(local_rows, width).astype(jnp.float32)
    summed = None
    shares = None
    for rollout_step in reversed(range(STEPS)):
        active = (rollout_step < count).astype(jnp.float32)
        inner = gradient * active
        layer_terms = [None] * layer_count
        for index in reversed(range(layer_count)):
            inner, layer_terms[index] = backward_layer(
                inner, saved[rollout_step][index], modulations[index], *weight_sets[index]
            )
        gradient = inner + (1.0 - active) * gradient
        modulation_grads = jnp.stack([terms[4] for terms in layer_terms])
        step_terms = (
            jnp.stack([terms[0] for terms in layer_terms]),
            jnp.stack([terms[1] for terms in layer_terms]),
            jnp.stack([terms[2] for terms in layer_terms]),
            jnp.stack([terms[3] for terms in layer_terms]),
            context_wide[None, :, None] * modulation_grads[:, None, :],
            modulation_grads,
            modulation_grads[:, 3 * width : 4 * width],
        )
        summed = step_terms if summed is None else jax.tree.map(jnp.add, summed, step_terms)
    shares = lax.psum_scatter(summed, ("lat", "lon"), scatter_dimension=1, tiled=True)
    totals = jax.tree.map(
        lambda part: part.astype(jnp.float32), lax.psum(shortened(shares), "item")
    )
    return (
        current.reshape(1, rows_dev, cols_dev, width),
        gradient.reshape(1, rows_dev, cols_dev, width),
        totals[0],
        totals[1],
        totals[2],
        totals[3],
        totals[4],
        totals[5],
        totals[6],
    )


F32 = jnp.float32
BF16 = jnp.bfloat16
GELU_A = math.sqrt(2.0 / math.pi)
GELU_B = 0.044715
LANES = 128
BLOCK = 256
PAIR = 2 * HEAD_DIM
SUM_ROWS = 48
ONES = 16
SAFE_SCORE = 60.0


def nn(left, right, precision=None):
    return lax.dot_general(
        left, right, (((1,), (0,)), ((), ())), preferred_element_type=F32, precision=precision
    )


def nt(left, right, precision=None):
    return lax.dot_general(
        left, right, (((1,), (1,)), ((), ())), preferred_element_type=F32, precision=precision
    )


def identity(size):
    rows = lax.broadcasted_iota(jnp.int32, (size, size), 0)
    columns = lax.broadcasted_iota(jnp.int32, (size, size), 1)
    return jnp.where(rows == columns, 1.0, 0.0).astype(BF16)


def turned(values):
    return nt(identity(values.shape[1]), values).astype(BF16)


def wide(column_tile, lanes):
    return jnp.concatenate([column_tile] * (lanes // LANES), axis=1)


def folded(values):
    pieces = [values[:, at : at + LANES] for at in range(0, values.shape[1], LANES)]
    return sum(pieces[1:], pieces[0])


def standardise(values):
    rows = values.shape[0]
    centred = values - jnp.sum(values, axis=0, keepdims=True) * (1.0 / rows)
    variance = jnp.sum(centred * centred, axis=0, keepdims=True) * (1.0 / rows)
    scale = lax.rsqrt(variance + 1e-06)
    return centred * scale, scale


def pre_norm_back(standard, scale, grad, gain):
    rows = standard.shape[0]
    inner = grad * gain
    first = jnp.sum(inner, axis=0, keepdims=True) * (1.0 / rows)
    second = jnp.sum(inner * standard, axis=0, keepdims=True) * (1.0 / rows)
    return scale * (inner - first - standard * second)


def part(mod_ref, index, lanes):
    return wide(mod_ref[index * D : (index + 1) * D, :], lanes)


def turn_into(source, out, at=0):
    for column in range(0, out.shape[0], BLOCK):
        width = min(BLOCK, out.shape[0] - column)
        out[column : column + width, :] = turned(source[:, at + column : at + column + width])


def prepare_first(mod, w_q_t, w_v_t, w_k, w_qkv, w_ada, b_ada, context):
    w_k[...] = w_qkv[:, D : 2 * D]
    turn_into(w_qkv, w_q_t)
    turn_into(w_qkv, w_v_t, 2 * D)
    values = nn(context[...], w_ada[...])[0:1] + b_ada
    for column in range(0, values.shape[1], LANES):
        tile = jnp.broadcast_to(values[:, column : column + LANES], (LANES, LANES))
        mod[column : column + LANES, :] = tile.T


def prepare_kernel(context, *refs):
    w_qkv, w_ada, b_ada, w_out, w_up, w_down = refs[:6]
    outs, scratch, sems = refs[8:19], refs[19:-1], refs[-1]
    sources = [w_qkv.at[0], w_ada.at[0], b_ada, w_out.at[0], w_up.at[0], w_down.at[0], w_qkv.at[1], w_ada.at[1]]
    copies = [
        pltpu.make_async_copy(source, target, sems.at[place])
        for place, (source, target) in enumerate(zip(sources, scratch))
    ]
    for copy in copies:
        copy.start()
    for copy in copies[:3]:
        copy.wait()
    prepare_first(*outs[0:4], scratch[0], scratch[1], scratch[2][0:1, :], context)
    for copy, source, out in zip(copies[3:6], scratch[3:6], outs[8:11]):
        copy.wait()
        turn_into(source, out)
    for copy in copies[6:]:
        copy.wait()
    prepare_first(*outs[4:8], scratch[6], scratch[7], scratch[2][1:2, :], context)


def prepare_rest_kernel(index, early, w_out, w_up, w_down, *outs):
    for weight, out in zip((w_out, w_up, w_down), outs):
        turn_into(weight.at[index], out)


def project(x, mod_ref, w_q_t, w_v_t, w_k, outs):
    q_out, kn_out, vt_out = outs
    lanes = x.shape[1]
    standard, _ = standardise(x)
    normed = (standard * (1.0 + part(mod_ref, 1, lanes)) + part(mod_ref, 0, lanes)).astype(BF16)
    vt_out[...] = nn(w_v_t[...], normed).astype(BF16)
    q_out[...] = (nn(w_q_t[...], normed) * HEAD_DIM ** (-0.5)).astype(BF16)
    for at in range(0, lanes, BLOCK):
        kn_out[at : at + BLOCK, :] = nn(turned(normed[:, at : at + BLOCK]), w_k[...]).astype(BF16)


def first_kernel(own, flip_x, flip_y, flip_xy, mod, w_q_t, w_v_t, w_k, x_out, xb_out, *outs):
    for index, ref in enumerate((own, flip_x, flip_y, flip_xy)):
        rows = ref.shape[0]
        flat = turned(ref[...])
        xb_out[:, index * rows : (index + 1) * rows] = flat
        x_out[:, index * rows : (index + 1) * rows] = flat.astype(F32)
    project(x_out[...], mod, w_q_t, w_v_t, w_k, outs)


def head_rows(head):
    return slice(head * HEAD_DIM, (head + 1) * HEAD_DIM)


def pair_columns(head):
    return slice(head // 2 * PAIR, (head // 2 + 1) * PAIR)


def padded(rows, head):
    zeros = jnp.zeros_like(rows)
    return jnp.concatenate([rows, zeros] if head % 2 == 0 else [zeros, rows], axis=0)


def query_top(q):
    square = q[...].astype(F32)
    square = square * square
    norms = [jnp.sum(square[head_rows(head)], axis=0, keepdims=True) for head in range(HEADS)]
    return jnp.max(functools.reduce(jnp.maximum, norms), axis=1, keepdims=True)


def key_top(kn):
    first = lax.broadcasted_iota(jnp.int32, (D, LANES), 1) * HEAD_DIM
    row = lax.broadcasted_iota(jnp.int32, (D, LANES), 0)
    pick = jnp.where((row >= first) & (row < first + HEAD_DIM), 1.0, 0.0).astype(BF16)
    square = kn[...].astype(F32)
    norms = nn((square * square).astype(BF16), pick)
    return jnp.max(jnp.max(norms, axis=0, keepdims=True), axis=1, keepdims=True) * 1.02


def value_rows(vt, rows, at):
    values = vt[rows, at]
    return jnp.concatenate([values, jnp.ones((ONES, values.shape[1]), BF16)], axis=0)


def attend_plain(q, kn, vt, put):
    chunks = [slice(at, at + BLOCK) for at in range(0, kn.shape[0], BLOCK)]

    def score(head):
        return nn(kn[:, pair_columns(head)], padded(q[head_rows(head), :], head))

    totals = {}

    def finish(head, at, probs):
        term = nn(value_rows(vt, head_rows(head), at), probs)
        totals[head] = totals[head] + term if head in totals else term
        if at == chunks[-1]:
            put(head, totals[head])

    waiting = None
    following = score(0)
    for head in range(HEADS):
        scores = following
        for at in chunks:
            if at == chunks[0] and head + 1 < HEADS:
                following = score(head + 1)
            if waiting is not None:
                finish(*waiting)
            waiting = (head, at, jnp.exp(scores[at]).astype(BF16))
    finish(*waiting)


def attend_own_kernel(early, *refs):
    q, kn, vt, *refs = refs[early:]
    passing = []
    if len(refs) > 2:
        *passing, sums, tops, passed = refs
    else:
        sums, tops = refs
    at = 0
    for source in passing:
        rows = source.shape[0]
        passed[at : at + rows, :] = source[...]
        at += rows

    def put(head, total):
        sums[head] = total

    query, key = query_top(q), key_top(kn)
    tops[0:8, :] = jnp.broadcast_to(query, (8, LANES))
    tops[8:16, :] = jnp.broadcast_to(key, (8, LANES))

    @pl.when(jnp.max(query * key) < SAFE_SCORE**2)
    def _():
        attend_plain(q, kn, vt, put)


def forward_kernel(last, early, *refs):
    refs = refs[early:]
    if last:
        active, x, x_step, *refs = refs
    else:
        x, *refs = refs
    q, kn_own, kn_far, vt_own, vt_far, sums, tops, mod, w_out_t, w_up_t, w_down_t, *refs = refs
    if not last:
        mod_next, w_q_t, w_v_t, w_k, *refs = refs
    lse, mixed, attended, middle, hidden, slope, branch, *refs = refs
    if last:
        (final,) = refs
    else:
        x_next, xb_next, *next_outs = refs
    patches = x.shape[1]
    bound = tops[0:1, 0:1] * jnp.maximum(tops[8:9, 0:1], key_top(kn_far))
    safe = jnp.max(bound) < SAFE_SCORE**2

    def put(head, total):
        total = sums[head] + total
        weight = total[HEAD_DIM : HEAD_DIM + 1]
        mixed[head_rows(head), :] = (total[:HEAD_DIM] * (1.0 / weight)).astype(BF16)
        lse[head : head + 1, :] = jnp.log(weight)

    @pl.when(safe)
    def _():
        attend_plain(q, kn_far, vt_far, put)

    @pl.when(jnp.logical_not(safe))
    def _():
        def pair_heads(pair, _):
            columns = pl.ds(pl.multiple_of(pair * PAIR, PAIR), PAIR)
            for head in range(2):
                rows = pl.ds(pl.multiple_of(pair * PAIR + head * HEAD_DIM, HEAD_DIM), HEAD_DIM)
                query = padded(q[rows, :], head)
                scores = [nn(kn[:, columns], query) for kn in (kn_own, kn_far)]
                tops = [jnp.max(score, axis=0, keepdims=True) for score in scores]
                top = jnp.maximum(*tops)
                total = None
                for score, vt in zip(scores, (vt_own, vt_far)):
                    term = nn(value_rows(vt, rows, slice(None)), jnp.exp(score - top).astype(BF16))
                    total = term if total is None else total + term
                weight = total[HEAD_DIM : HEAD_DIM + 1]
                mixed[rows, :] = (total[:HEAD_DIM] * (1.0 / weight)).astype(BF16)
                lse[pl.ds(pair * 2 + head, 1), :] = top + jnp.log(weight)
            return 0

        lax.fori_loop(0, HEADS // 2, pair_heads, 0)

    att = nn(w_out_t[...], mixed[...])
    attended[...] = att.astype(BF16)
    mid = x[...] + part(mod, 2, patches) * att
    middle[...] = mid.astype(BF16)
    standard, _ = standardise(mid)
    hidden_in = (standard * (1.0 + part(mod, 4, patches)) + part(mod, 3, patches)).astype(BF16)
    chunks = [slice(at, at + BLOCK) for at in range(0, w_up_t.shape[0], BLOCK)]

    def up(place):
        wide_rows = slice(place * BLOCK, (place + 2) * BLOCK)
        both = nn(w_up_t[wide_rows, :], hidden_in)
        return [both[:BLOCK], both[BLOCK:]]

    down = None
    waiting = None
    acts = up(0)
    for place, rows in enumerate(chunks):
        act = acts[place]
        if place % 2 == 0 and place + 2 < len(chunks):
            acts += up(place + 2)
        if place > 0:
            term = nn(w_down_t[:, chunks[place - 1]], waiting)
            down = term if down is None else down + term
        act = act.astype(BF16)
        inner = GELU_A + (GELU_A * GELU_B) * (act * act)
        half = 0.5 + 0.5 * jnp.tanh(act * inner)
        waiting = gelu = act * half
        hidden[rows, :] = waiting
        slope[rows, :] = (half + (gelu - gelu * half) * (6.0 * inner - 4.0 * GELU_A))
    down = down + nn(w_down_t[:, chunks[-1]], waiting)
    branch[...] = down.astype(BF16)
    out = mid + part(mod, 5, patches) * down
    if last:
        own = final.shape[0]
        final[...] = jnp.where(active[0] > 0.0, out[:, :own], x_step[:, :own]).T
    else:
        x_next[...] = out
        xb_next[...] = out.astype(BF16)
        project(out, mod_next, w_q_t, w_v_t, w_k, next_outs)


def put_grads(left_ref, right, where, count, at, mine, other, before):
    rows = [left_ref[pl.ds(pl.multiple_of(where[place] * count, 16), count), :] for place in range(2)]
    product = nt(jnp.concatenate(rows, axis=0), right)
    for column in range(0, product.shape[1], LANES):
        low = product[:count, column : column + LANES]
        high = product[count:, column : column + LANES]
        if before is not None:
            low = low + before[0][at : at + count, :]
            high = high + before[1][at : at + count, :]
        mine[at : at + count, :] = low.astype(mine.dtype)
        other[at : at + count, :] = high.astype(other.dtype)
        at += count


def dense_back_kernel(has_close, has_open, has_before, start, layers, waits, *refs):
    refs = list(refs)

    def take(count):
        taken = refs[:count]
        del refs[:count]
        return taken

    take(waits)
    where, active = take(2)
    close_before = open_before = None
    if has_close:
        d_own, d_got, dq, d_mid_in, x_in, mod_in, w_qkv = take(7)
        w_qkv = w_qkv.at[layers[0]]
        if has_before[0]:
            close_before = take(3)
    if start == "first":
        cots = take(2)
    elif start == "cross":
        cots = take(1)
    if has_open:
        mixed, attended, middle, hidden, slope, branch, mod, w_out, w_up, w_down = take(10)
        w_out, w_up, w_down = (ref.at[layers[1]] for ref in (w_out, w_up, w_down))
        if has_before[1]:
            open_before = take(3)
    else:
        (lines,) = take(1)
    if has_close:
        close_mine, close_other, close_mods = take(3)
    if start == "first":
        (cot_out,) = take(1)
    if has_open:
        open_mine, open_other, open_mods, d_mid_out, do_out, cen_out = take(6)
    else:
        g_out, sums_out = take(2)
        sums_at = close_before[1].shape[0]
    if has_close:
        grads_scr, normed_scr = take(2)
    if has_open:
        bg_scr, pg_scr, hin_scr, ag_scr = take(4)

    patches = middle.shape[1] if has_open else x_in.shape[1]
    totals = {}

    def add_sums(name, values):
        totals[name] = totals[name] + folded(values) if name in totals else folded(values)

    def put_sums(out, before, names):
        for place, name in enumerate(names):
            rows = slice(place * D, (place + 1) * D)
            out[rows, :] = totals[name] + before[2][rows, :] if before else totals[name]

    if start == "first":
        for index, ref in enumerate(cots):
            rows = ref.shape[0]
            cot_out[:, index * rows : (index + 1) * rows] = turned(ref[...])

    def close(at):
        standard, scale = standardise(x_in[:, at].astype(F32))
        gain = 1.0 + part(mod_in, 1, patches)
        normed_scr[:, at] = (standard * gain + part(mod_in, 0, patches)).astype(BF16)
        for third in range(3):
            if third == 0:
                piece = dq[:, at]
            else:
                rows = slice((third - 1) * D, third * D)
                piece = (d_own[rows, at] + d_got[rows, at].astype(F32)).astype(BF16)
            grads_scr[third * D : (third + 1) * D, at] = piece
        back = nn(w_qkv[...], grads_scr[:, at])
        add_sums("shift_a", back)
        add_sums("scale_a", back * standard)
        g = d_mid_in[:, at] + pre_norm_back(standard, scale, back, gain)
        if start == "cross":
            g = g + (1.0 - active[0]) * cots[0][:, at].astype(F32)
        return g

    def dense(at, g):
        standard, scale = standardise(middle[:, at].astype(F32))
        gain = 1.0 + part(mod, 4, patches)
        hin_scr[:, at] = (standard * gain + part(mod, 3, patches)).astype(BF16)
        branch_grad = (part(mod, 5, patches) * g).astype(BF16)
        bg_scr[:, at] = branch_grad
        add_sums("gate_m", g * branch[:, at].astype(F32))
        chunks = [slice(start, start + BLOCK) for start in range(0, w_down.shape[0], BLOCK)]
        back = None
        waiting = None

        def down(place):
            wide_rows = slice(place * BLOCK, (place + 2) * BLOCK)
            both = nn(w_down[wide_rows, :], branch_grad)
            return [both[:BLOCK], both[BLOCK:]]

        hidden_grads = down(0)
        for place, rows in enumerate(chunks):
            hidden_grad = hidden_grads[place]
            if place % 2 == 0 and place + 2 < len(chunks):
                hidden_grads += down(place + 2)
            if place > 0:
                term = nn(w_up[:, chunks[place - 1]], waiting)
                back = term if back is None else back + term
            waiting = slope[rows, at] * hidden_grad.astype(BF16)
            pg_scr[rows, at] = waiting
        back = back + nn(w_up[:, chunks[-1]], waiting)
        add_sums("shift_m", back)
        add_sums("scale_m", back * standard)
        d_mid = g + pre_norm_back(standard, scale, back, gain)
        d_mid_out[:, at] = d_mid
        att_grad = (part(mod, 2, patches) * d_mid).astype(BF16)
        ag_scr[:, at] = att_grad
        mixed_grad = nn(w_out[...], att_grad).astype(BF16)
        do_out[:, at] = mixed_grad
        add_sums("gate_a", d_mid * attended[:, at].astype(F32))
        product = mixed_grad.astype(F32) * mixed[:, at].astype(F32)
        for head in range(HEADS):
            cen_out[head : head + 1, at] = jnp.sum(product[head_rows(head)], axis=0, keepdims=True)

    at = slice(0, patches)
    g = close(at) if has_close else cot_out[:, at].astype(F32) * active[0]
    if has_open:
        dense(at, g)
    else:
        g_out[...] = g[:, : g_out.shape[0]].T
    if has_close:
        put_sums(close_mods, close_before, ("shift_a", "scale_a"))
        put_grads(normed_scr, grads_scr[...], where, D // 8, 0, close_mine, close_other, close_before)
    if has_open:
        put_sums(open_mods, open_before, ("gate_a", "shift_m", "scale_m", "gate_m"))
        count = w_down.shape[0] // 8
        put_grads(hidden, bg_scr[...], where, count, 0, open_mine, open_other, open_before)
        at = count * (D // LANES)
        put_grads(hin_scr, pg_scr[...], where, D // 8, at, open_mine, open_other, open_before)
        at += (w_up.shape[1] // LANES) * (D // 8)
        put_grads(mixed, ag_scr[...], where, D // 8, at, open_mine, open_other, open_before)
    else:
        sums_out[...] = lines[...]
        put_lines(sums_out, 0, close_mods[...])
        close_other[sums_at:, :] = sums_out[...].astype(BF16)


def attend_back_kernel(has_before, waits, q, kn, vt, lse, d_out, centre, *refs):
    if has_before:
        before, *refs = refs
    d_kv, dq_out, kt_scr, vn_scr = refs[waits:]
    for column in range(0, D, LANES):
        kt_scr[column : column + LANES, :] = turned(kn[:, column : column + LANES])
    for column in range(0, vt.shape[1], BLOCK):
        vn_scr[column : column + BLOCK, :] = turned(vt[:, column : column + BLOCK])

    chunks = [slice(at, at + BLOCK) for at in range(0, kn.shape[0], BLOCK)]

    def score(head):
        columns = pair_columns(head)
        rows = head_rows(head)
        return nn(kn[:, columns], padded(q[rows, :], head)), nn(vn_scr[:, columns], padded(d_out[rows, :], head))

    totals = {}

    def finish(head, at, probs, score_grads):
        rows = head_rows(head)
        d_kv[D + rows.start : D + rows.stop, at] = nt(d_out[rows, :], probs).astype(d_kv.dtype)
        d_kv[rows, at] = nt(q[rows, :], score_grads).astype(d_kv.dtype)
        term = nn(kt_scr[rows, at], score_grads)
        if head not in totals:
            totals[head] = before[rows, :] + term if has_before else term
            return
        term = totals[head] + term
        if has_before:
            term = term * HEAD_DIM ** (-0.5)
        dq_out[rows, :] = term.astype(dq_out.dtype)

    waiting = None
    following = score(0)
    for head in range(HEADS):
        scores, prob_grads = following
        for at in chunks:
            if at == chunks[0] and head + 1 < HEADS:
                following = score(head + 1)
            if waiting is not None:
                finish(*waiting)
            probs = jnp.exp(scores[at] - lse[head : head + 1, :])
            score_grads = (probs * (prob_grads[at] - centre[head : head + 1, :])).astype(BF16)
            waiting = (head, at, probs.astype(BF16), score_grads)
    finish(*waiting)


def split_kernel(waits, where, *refs):
    *halves, keep, sent, total_scr = refs[waits:]
    rows_half = keep.shape[0]
    at = 0
    for mine, other in zip(halves[::2], halves[1::2]):
        rows = mine.shape[0]
        total_scr[at : at + rows, :] = mine[...] + other[...].astype(F32)
        at += rows
    if at < total_scr.shape[0]:
        total_scr[at:, :] = jnp.zeros((total_scr.shape[0] - at, LANES), F32)
    odd = where[3]
    keep[...] = total_scr[pl.ds(pl.multiple_of(odd * rows_half, 16), rows_half), :]
    sent[...] = total_scr[pl.ds(pl.multiple_of((1 - odd) * rows_half, 16), rows_half), :].astype(BF16)


def pair_sum_kernel(late, *refs):
    count = len(refs) // 3
    for keep, got, out in zip(refs[:count], refs[count : 2 * count], refs[2 * count :]):
        out[...] = (keep[...].astype(F32) + got[...].astype(F32)).astype(BF16)


def put_lines(out, row, values):
    ones = jnp.ones((16, LANES), BF16)
    high = values.astype(BF16)
    low = (values - high.astype(F32)).astype(BF16)
    line = (nt(ones, high) + nt(ones, low))[0:1]
    for column in range(0, line.shape[1], LANES):
        out[row : row + 1, :] = line[:, column : column + LANES]
        row += 1
    return row


def lines_kernel(early, context, *refs):
    *sums, out = refs
    out[...] = jnp.zeros_like(out)
    row = 2 * D // LANES
    for ref in sums:
        row = put_lines(out, row, ref[...])
    for column in range(0, D, LANES):
        out[row : row + 1, :] = context[0:1, column : column + LANES].astype(F32)
        row += 1


def join_kernel(sum_count, early, mine, sums, got, out):
    rows = mine.shape[0]
    out[:rows, :] = (mine[...] + got[:rows, :].astype(F32)).astype(BF16)
    other = got[rows:, :].astype(F32)
    summed = lax.broadcasted_iota(jnp.int32, (SUM_ROWS, LANES), 0) < sum_count
    out[rows:, :] = (sums[...] + jnp.where(summed, other, 0.0)).astype(BF16)


def pair_kernel(rows, where, own, got, out):
    out[:rows, :] = (own[:rows, :].astype(F32) + got[:rows, :].astype(F32)).astype(BF16)
    odd = where[3]
    size = SUM_ROWS
    out[pl.ds(pl.multiple_of(rows + odd * size, 16), size), :] = own[rows:, :]
    out[pl.ds(pl.multiple_of(rows + (1 - odd) * size, 16), size), :] = got[rows:, :]


def gather_kernel(where, *refs):
    halves, (out_out, up_out, down_out, qkv_out), scratch = refs[:4], refs[4:8], refs[8:]
    odd = where[3]
    for ref, own, got in zip(scratch, halves[::2], halves[1::2]):
        rows = own.shape[0]
        ref[pl.ds(pl.multiple_of(odd * rows, 16), rows), :] = own[...]
        ref[pl.ds(pl.multiple_of((1 - odd) * rows, 16), rows), :] = got[...]
    slice_rows = out_out.shape[1]
    for index, ref in enumerate(scratch):
        at = 0
        for out in (down_out, up_out, out_out):
            rows = out.shape[1]
            for column in range(0, out.shape[2], LANES):
                out[index, :, column : column + LANES] = ref[at : at + rows, :].astype(F32)
                at += rows
        if index == 0:
            for column in range(0, qkv_out.shape[1], LANES):
                qkv_out[:, column : column + LANES] = ref[at : at + slice_rows, :].astype(F32)
                at += slice_rows


def finish_kernel(item_count, where, own, got, qkv_1, qkv_out, ada_out, bias_out, shift_out, sum_scr, bias_scr, shift_scr):
    layers = 2
    device, high = where[0], where[4]
    slice_rows = qkv_out.shape[1]
    close_rows = slice_rows * (3 * D // LANES)
    for other in range(2):
        rows = slice(close_rows + other * SUM_ROWS, close_rows + (other + 1) * SUM_ROWS)
        sum_scr[2 * high + other] = own[rows, :].astype(F32)
        sum_scr[2 * (1 - high) + other] = got[rows, :].astype(F32)
    qkv_out[1] = qkv_1[...]
    for tile in range(3 * D // LANES):
        rows = slice(tile * slice_rows, (tile + 1) * slice_rows)
        total = own[rows, :].astype(F32) + got[rows, :].astype(F32)
        qkv_out[0, :, tile * LANES : (tile + 1) * LANES] = total
    tiles = 6 * D // LANES
    contexts = []
    for other in range(item_count):
        line = jnp.concatenate([sum_scr[other, layers * tiles + c : layers * tiles + c + 1, :] for c in range(3)], axis=1)
        contexts.append(line)
    square = jnp.concatenate(contexts + [jnp.zeros((8 - item_count, D), F32)], axis=0)
    spot = lax.broadcasted_iota(jnp.int32, (slice_rows, D), 1)
    want = lax.broadcasted_iota(jnp.int32, (slice_rows, D), 0) + device * slice_rows
    pick = jnp.where(spot == want, 1.0, 0.0).astype(BF16)
    columns = nt(pick, square.astype(BF16))
    bias_rows = bias_out.shape[1]
    for index in range(layers):
        flats = []
        for tile in range(tiles):
            row = index * tiles + tile
            total = None
            flat = None
            for other in range(item_count):
                line = sum_scr[other, row : row + 1, :]
                term = columns[:, other : other + 1] * line
                total = term if total is None else total + term
                flat = line if flat is None else flat + line
            ada_out[index, :, tile * LANES : (tile + 1) * LANES] = total
            flats.append(flat)
        flat = jnp.concatenate(flats, axis=1)
        for place in range(flat.shape[1] // bias_rows):
            bias_scr[place, index : index + 1, :] = flat[:, place * bias_rows : (place + 1) * bias_rows]
            at = 3 * D + place * slice_rows
            shift_scr[place, index : index + 1, :] = flat[:, at : at + slice_rows]
    bias_out[...] = bias_scr[device]
    shift_out[...] = shift_scr[device]


VMEM = pl.BlockSpec(memory_space=pltpu.VMEM)
SMEM = pl.BlockSpec(memory_space=pltpu.SMEM)
ANY = pl.BlockSpec(memory_space=pl.ANY)
HBM = pl.BlockSpec(memory_space=pltpu.HBM)


def layer_block(array, index):
    return pl.BlockSpec((None,) + array.shape[1:], lambda step: (index,) + (0,) * (array.ndim - 1))


def call(body, args, outs, scratch=(), flops=0, name=None):
    arrays = [arg[0] if isinstance(arg, tuple) else arg for arg in args]
    specs = [arg[1] if isinstance(arg, tuple) else VMEM for arg in args]
    return pl.pallas_call(
        body,
        out_shape=[jax.ShapeDtypeStruct(shape, kind) for shape, kind in outs],
        in_specs=specs,
        out_specs=[VMEM] * len(outs),
        scratch_shapes=[one if not isinstance(one, tuple) else pltpu.VMEM(*one) for one in scratch],
        compiler_params=pltpu.CompilerParams(vmem_limit_bytes=VMEM_LIMIT),
        cost_estimate=pl.CostEstimate(flops=flops, bytes_accessed=0, transcendentals=0),
        name=name,
    )(*arrays)


VMEM_LIMIT = 14 * 1024 * 1024


def fast_shards(
    lat_count, lon_count, item_count,
    fields, lead_index, rollout, w_qkv, w_out, w_up, w_down, w_ada, b_ada, cotangent,
):
    _, rows_dev, cols_dev, width = fields.shape
    local = rows_dev * cols_dev
    layers = w_qkv.shape[0]
    ff = w_up.shape[2]
    patches = 4 * local
    device = lax.axis_index("lat") * lon_count + lax.axis_index("lon")
    item = lax.axis_index("item")
    where = jnp.stack([device, device ^ 1, item, item & 1, item >> 1]).astype(jnp.int32)
    active = (1 < rollout[0]).astype(F32)[None]

    def plane_flip(value, flip_lat, flip_y):
        pairs = [
            (a * lon_count + b, (a ^ flip_lat) * lon_count + (b ^ (2 * flip_y)))
            for a in range(lat_count)
            for b in range(lon_count)
        ]
        return lax.ppermute(value, ("lat", "lon"), pairs)

    def swap(value):
        return lax.ppermute(value, "lon", [(index, index ^ 1) for index in range(lon_count)])

    def with_item(value, flip):
        return lax.ppermute(value, "item", [(index, index ^ flip) for index in range(item_count)])

    def plane_parts(value):
        return [value, plane_flip(value, 1, 0), plane_flip(value, 0, 1), plane_flip(value, 1, 1)]

    field_parts = plane_parts(fields.reshape(local, width))

    context = jax.nn.silu(embedding(lead_index[0])).astype(BF16)
    context = jnp.broadcast_to(context[None, :], (16, width))
    square = (width, patches)
    natural = (patches, width)
    weights = (w_qkv, w_ada, b_ada, w_out, w_up, w_down)
    weights = [(pltpu.with_memory_space_constraint(value, pltpu.HBM), HBM) for value in weights]
    first_outs = [((6 * width, LANES), F32)] + [((width, width), BF16)] * 3
    rest_outs = [((width, width), BF16), ((ff, width), BF16), ((width, ff), BF16)]
    first_fetch = [((width, 3 * width), BF16), ((width, 6 * width), BF16)]
    rest_fetch = [((width, width), BF16), ((width, ff), BF16), ((ff, width), BF16)]
    prepared = call(
        prepare_kernel,
        [context, *weights, (where, SMEM), (active, SMEM)],
        first_outs * 2 + rest_outs,
        first_fetch + [(b_ada.shape, F32)] + rest_fetch + first_fetch + [pltpu.SemaphoreType.DMA((8,))],
        name="prepare",
    )
    first_parts = [prepared[0:4], prepared[4:8]]
    rest_parts = [prepared[8:11]]
    mods = [one[0] for one in first_parts]

    project_outs = [(square, F32), (square, BF16), (square, BF16), (natural, BF16), (square, BF16)]
    dense_flops = 2 * patches * (width * 3 * width + width * width + 2 * width * ff)
    score_flops = 2 * patches * 2 * patches * width * 4
    x, xb, *projected = call(
        first_kernel,
        [*field_parts, *first_parts[0]],
        project_outs,
        flops=2 * patches * width * 4 * width,
        name="first",
    )
    saved = []
    for step in range(STEPS):
        for index in range(layers):
            q, kn, vt = projected
            if len(rest_parts) == index:
                rest_parts.append(
                    call(
                        functools.partial(prepare_rest_kernel, index),
                        [(kn, ANY), w_out, w_up, w_down],
                        rest_outs,
                        name="prepare_rest",
                    )
                )
            kn_far, vt_far = swap(kn), swap(vt)
            early = [w_up] if len(rest_parts) == index + 1 < layers else []
            passing = []
            if step == STEPS - 1:
                passing = [cotangent.reshape(local, width)] if index == 0 else cot_parts
            passed = [((len(passing) * local, width), BF16)] if passing else []
            sums, tops, *passed = call(
                functools.partial(attend_own_kernel, len(early)),
                early + [q, kn, vt] + passing,
                [((HEADS, HEAD_DIM + ONES, patches), F32), ((16, LANES), F32)] + passed,
                flops=10 * score_flops,
                name="forward_own",
            )
            if passed:
                cot_parts = [passed[0], plane_flip(passed[0], 1 - index, index)]
            last = step == STEPS - 1 and index == layers - 1
            if index == 0 and step > 0:
                x_step = x
            following = list(first_parts[(index + 1) % layers])
            early = [w_down] if len(rest_parts) == index + 1 < layers else []
            lse, mixed, attended, middle, hidden, slope, branch, *results = call(
                functools.partial(forward_kernel, last, len(early)),
                early
                + ([(active, SMEM), x, x_step] if last else [x])
                + [q, kn, kn_far, vt, vt_far, sums, tops, mods[index], *rest_parts[index]]
                + ([] if last else following),
                [
                    ((HEADS, patches), F32),
                    (square, BF16),
                    (square, BF16),
                    (square, BF16),
                    ((ff, patches), BF16),
                    ((ff, patches), BF16),
                    (square, BF16),
                ]
                + ([((local, width), F32)] if last else project_outs),
                flops=dense_flops + 2 * score_flops,
                name="forward",
            )
            saved.append((xb, [mixed, attended, middle, hidden, slope, branch], (q, kn, kn_far, vt, vt_far, lse)))
            if last:
                final = results[0]
            else:
                x, xb, *projected = results

    slice_rows = width // 8
    open_rows = 2 * (ff // 8) * (width // LANES) + slice_rows * (width // LANES)
    close_rows = slice_rows * (3 * width // LANES)
    order = [(step, index) for step in reversed(range(STEPS)) for index in reversed(range(layers))]
    open_done = [None] * layers
    close_done = [None] * layers
    pending = None
    for place in range(len(order) + 1):
        has_close = pending is not None
        has_open = place < len(order)
        use = [order[place - 1][1], order[place][1] if has_open else 0]
        waits = []
        if has_close and close_done[use[0]]:
            waits = [pair_1] if has_open else [item_got_1]
        args = [(value, ANY) for value in waits] + [(where, SMEM), (active, SMEM)]
        outs = []
        scratch = []
        has_before = [False, False]
        start = ""
        if has_close:
            args += pending
            if close_done[use[0]] is not None:
                has_before[0] = True
                args += close_done[use[0]]
            outs += [((close_rows, LANES), F32)]
            sent_rows = close_rows + (0 if has_open else SUM_ROWS)
            outs += [((sent_rows, LANES), BF16 if has_before[0] else F32), ((2 * width, LANES), F32)]
            scratch += [((3 * width, patches), BF16), (square, BF16)]
        if place == 0:
            start = "first"
            args += cot_parts
            outs += [(square, BF16)]
        elif has_open and order[place][0] != order[place - 1][0]:
            start = "cross"
            args += [cot_t]
        if has_open:
            step, index = order[place]
            xb, kept, heads = saved[step * layers + index]
            args += kept + [mods[index], w_out, w_up, w_down]
            if open_done[index] is not None:
                has_before[1] = True
                args += open_done[index]
            outs += [
                ((open_rows, LANES), F32),
                ((open_rows, LANES), BF16 if has_before[1] else F32),
                ((4 * width, LANES), F32),
                (square, F32),
                (square, BF16),
                ((HEADS, patches), F32),
            ]
            scratch += [(square, BF16), ((ff, patches), BF16), (square, BF16), (square, BF16)]
        else:
            args += [lines]
            outs += [((local, width), F32), ((SUM_ROWS, LANES), F32)]
        results = list(
            call(
                functools.partial(dense_back_kernel, has_close, has_open, has_before, start, use, len(waits)),
                args,
                outs,
                scratch,
                flops=2 * dense_flops if has_open else 0,
                name="dense_back" if has_open else "close_back",
            )
        )
        if has_close:
            close_done[use[0]] = results[:3]
            del results[:3]
        if start == "first":
            cot_t = results.pop(0)
        if not has_open:
            gradient, line = results
            break
        open_done[index] = results[:3]
        d_mid, d_out, centre = results[3:]
        q, kn, kn_far, vt, vt_far, lse = heads
        halves = [open_done[index][0], open_done[index][1]]
        if index == 0:
            halves += [close_done[1][0], close_done[1][1]]
        half_rows = -(-sum(half.shape[0] for half in halves[::2]) // 32) * 16

        def split(waits):
            pieces = [half if place % 2 == 0 else swap(half) for place, half in enumerate(halves)]
            return call(
                functools.partial(split_kernel, len(waits)),
                [(where, SMEM), *waits, *pieces],
                [((half_rows, LANES), F32), ((half_rows, LANES), BF16)],
                [((2 * half_rows, LANES), F32)],
                name="split",
            )

        def pair_sum(late, keeps, gots):
            outs = [(keep.shape, BF16) for keep in keeps]
            return call(pair_sum_kernel, [(late, ANY), *keeps, *gots], outs, name="pair_sum")

        waits = []
        if has_before[1] and index == 0:
            pair_got_1 = with_item(pair_1, 2)
            lines = call(
                lines_kernel,
                [(pair_got_1, ANY), context, open_done[0][2], close_done[1][2], open_done[1][2]],
                [((SUM_ROWS, LANES), F32)],
                flops=10 * score_flops,
                name="lines",
            )[0]
            keep, sent = split([(lines, ANY)])
            got_0 = with_item(sent, 1)
            waits = [keep]
        d_far, dq = call(
            functools.partial(attend_back_kernel, False, len(waits)),
            [q, kn_far, vt_far, lse, d_out, centre] + [(value, ANY) for value in waits],
            [((2 * width, patches), BF16), (square, F32)],
            [(square, BF16), (natural, BF16)],
            flops=10 * score_flops,
            name="attend_far",
        )
        d_got = swap(d_far)
        waits = []
        if has_before[1]:
            if index == 1:
                keep, sent = split([(d_far, ANY)])
                got_1 = with_item(sent, 1)
                waits = [keep]
            else:
                pair_0, item_1 = pair_sum(d_far, [keep, pair_1], [got_0, pair_got_1])
                item_got_1 = with_item(item_1, 1)
                pair_got_0 = with_item(pair_0, 2)
                waits = [pair_0]
        d_own, dq = call(
            functools.partial(attend_back_kernel, True, len(waits)),
            [q, kn, vt, lse, d_out, centre, dq] + [(value, ANY) for value in waits],
            [((2 * width, patches), F32), (square, BF16)],
            [(square, BF16), (natural, BF16)],
            flops=10 * score_flops,
            name="attend_own",
        )
        if has_before[1] and index == 1:
            (pair_1,) = pair_sum(dq, [keep], [got_1])
        pending = [d_own, d_got, dq, d_mid, xb, mods[index], w_qkv]

    message = call(
        functools.partial(join_kernel, layers * 6 * width // LANES),
        [(pair_got_0, ANY), close_done[0][0], line, swap(close_done[0][1])],
        [((close_rows + SUM_ROWS, LANES), BF16)],
        name="join",
    )[0]
    message_got = with_item(message, 1)
    (item_0,) = pair_sum(message_got, [pair_0], [pair_got_0])
    message = call(
        functools.partial(pair_kernel, close_rows),
        [(where, SMEM), message, message_got],
        [((close_rows + 2 * SUM_ROWS, LANES), BF16)],
        name="pair",
    )[0]
    out_grad, up_grad, down_grad, qkv_1 = call(
        gather_kernel,
        [(where, SMEM), item_0, with_item(item_0, 1), item_1, item_got_1],
        [
            ((layers, slice_rows, width), F32),
            ((layers, slice_rows, ff), F32),
            ((layers, ff // 8, width), F32),
            ((slice_rows, 3 * width), F32),
        ],
        [((2 * pair.shape[0], LANES), BF16) for pair in (pair_0, pair_1)],
        name="gather",
    )
    bias_rows = 6 * width // 8
    qkv_grad, ada_grad, bias_grad, shift_grad = call(
        functools.partial(finish_kernel, item_count),
        [(where, SMEM), message, with_item(message, 2), qkv_1],
        [
            ((layers, slice_rows, 3 * width), F32),
            ((layers, slice_rows, 6 * width), F32),
            ((layers, bias_rows), F32),
            ((layers, slice_rows), F32),
        ],
        [
            ((item_count, SUM_ROWS, LANES), F32),
            ((8, layers, bias_rows), F32),
            ((8, layers, slice_rows), F32),
        ],
        name="finish",
    )
    field_shape = (1, rows_dev, cols_dev, width)
    return (
        final.reshape(field_shape),
        gradient.reshape(field_shape),
        qkv_grad,
        out_grad,
        up_grad,
        down_grad,
        ada_grad,
        bias_grad,
        shift_grad,
    )


def solution(mesh):
    lat_count, lon_count, item_count = mesh.shape["lat"], mesh.shape["lon"], mesh.shape["item"]
    if lat_count == 2 and lon_count == 4:
        body = functools.partial(fast_shards, lat_count, lon_count, item_count)
    else:
        body = shards
    return jax.shard_map(
        body,
        mesh=mesh,
        in_specs=(
            P("item", "lat", "lon", None),
            P("item"),
            P("item"),
            P(),
            P(),
            P(),
            P(),
            P(),
            P(),
            P("item", "lat", "lon", None),
        ),
        out_specs=(
            P("item", "lat", "lon", None),
            P("item", "lat", "lon", None),
            P(None, ("lat", "lon"), None),
            P(None, ("lat", "lon"), None),
            P(None, ("lat", "lon"), None),
            P(None, ("lat", "lon"), None),
            P(None, ("lat", "lon"), None),
            P(None, ("lat", "lon")),
            P(None, ("lat", "lon")),
        ),
        check_vma=False,
    )
```

```python
import functools
import math

import jax
import jax.numpy as jnp
from jax import lax
from jax.experimental import pallas as pl
from jax.experimental.pallas import tpu as pltpu
from jax.sharding import PartitionSpec as P

D = 384
HEADS = 6
HEAD_DIM = 64
STEPS = 2


def shortened(shard):
    return jax.tree.map(lambda a: a.astype(jnp.bfloat16) if a.dtype == jnp.float32 else a, shard)


def embedding(lead):
    half_width = D // 2
    lead_hours = 6.0 * (lead.astype(jnp.float32) + 1.0)
    frequencies = jnp.exp(
        -math.log(10000.0) * jnp.arange(half_width, dtype=jnp.float32) / half_width
    )
    angles = lead_hours * frequencies
    return jnp.concatenate([jnp.sin(angles), jnp.cos(angles)])


def pre_norm(values, shift_part, scale_part):
    centred = values - jnp.mean(values, axis=-1, keepdims=True)
    variance = jnp.mean(centred * centred, axis=-1, keepdims=True)
    return centred * lax.rsqrt(variance + 1e-06) * (1.0 + scale_part) + shift_part


def gather_keys(keys_values):
    band_rows = lax.all_gather(keys_values, "lon", axis=0, tiled=True)
    return lax.all_gather(band_rows, "lat", axis=0, tiled=True)


def spread_keys(key_value_grads):
    band_grads = lax.psum_scatter(
        key_value_grads.astype(jnp.bfloat16), "lat", scatter_dimension=0, tiled=True
    )
    return lax.psum_scatter(band_grads, "lon", scatter_dimension=0, tiled=True).astype(jnp.float32)


def forward_layer(current, modulation, weight_qkv, weight_out, weight_up, weight_down):
    local_rows, width = current.shape
    shift_attn, scale_attn, gate_attn, shift_mlp, scale_mlp, gate_mlp = modulation
    normed = pre_norm(current, shift_attn, scale_attn).astype(jnp.bfloat16)
    projected = jnp.dot(normed, weight_qkv, preferred_element_type=jnp.float32).astype(jnp.bfloat16)
    queries = projected[:, :width].reshape(local_rows, HEADS, HEAD_DIM)
    own_keys = projected[:, width:]
    gathered = gather_keys(own_keys)
    total_rows = gathered.shape[0]
    key_heads = gathered[:, :width].reshape(total_rows, HEADS, HEAD_DIM)
    value_heads = gathered[:, width:].reshape(total_rows, HEADS, HEAD_DIM)
    scores = jnp.einsum(
        "thd,nhd->htn", queries, key_heads, preferred_element_type=jnp.float32
    ) * HEAD_DIM ** (-0.5)
    log_total = jax.nn.logsumexp(scores, axis=-1, keepdims=True)
    probabilities = jnp.exp(scores - log_total).astype(jnp.bfloat16)
    mixed = jnp.einsum(
        "htn,nhd->thd", probabilities, value_heads, preferred_element_type=jnp.float32
    )
    mixed = mixed.reshape(local_rows, width).astype(jnp.bfloat16)
    attended = jnp.dot(mixed, weight_out, preferred_element_type=jnp.float32)
    middle = current + gate_attn * attended
    hidden_in = pre_norm(middle, shift_mlp, scale_mlp).astype(jnp.bfloat16)
    pre_act = jnp.dot(hidden_in, weight_up, preferred_element_type=jnp.float32)
    hidden = jax.nn.gelu(pre_act).astype(jnp.bfloat16)
    branch = jnp.dot(hidden, weight_down, preferred_element_type=jnp.float32)
    output = middle + gate_mlp * branch
    kept = (
        current,
        normed,
        queries,
        gathered,
        own_keys,
        log_total,
        mixed,
        attended,
        middle,
        hidden_in,
        pre_act,
        hidden,
        branch,
    )
    return (output, kept)


def backward_layer(grad_out, kept, modulation, weight_qkv, weight_out, weight_up, weight_down):
    (
        current,
        normed,
        queries,
        gathered,
        own_keys,
        log_total,
        mixed,
        attended,
        middle,
        hidden_in,
        pre_act,
        hidden,
        branch,
    ) = kept
    local_rows, width = current.shape
    total_rows = gathered.shape[0]
    shift_attn, scale_attn, gate_attn, shift_mlp, scale_mlp, gate_mlp = modulation
    factor = HEAD_DIM ** (-0.5)
    branch_grad = (gate_mlp * grad_out).astype(jnp.bfloat16)
    gate_mlp_grad = jnp.sum(grad_out * branch, axis=0)
    hidden_grad = jnp.dot(branch_grad, weight_down.T, preferred_element_type=jnp.float32)
    down_grad = jnp.dot(hidden.T, branch_grad, preferred_element_type=jnp.float32)
    _, gelu_back = jax.vjp(jax.nn.gelu, pre_act)
    pre_grad = gelu_back(hidden_grad)[0].astype(jnp.bfloat16)
    hidden_in_grad = jnp.dot(pre_grad, weight_up.T, preferred_element_type=jnp.float32)
    up_grad = jnp.dot(hidden_in.T, pre_grad, preferred_element_type=jnp.float32)
    _, second_back = jax.vjp(pre_norm, middle, shift_mlp, scale_mlp)
    middle_part, shift_mlp_grad, scale_mlp_grad = second_back(hidden_in_grad)
    middle_grad = grad_out + middle_part
    attended_grad = (gate_attn * middle_grad).astype(jnp.bfloat16)
    gate_attn_grad = jnp.sum(middle_grad * attended, axis=0)
    mixed_grad = jnp.dot(attended_grad, weight_out.T, preferred_element_type=jnp.float32).astype(
        jnp.bfloat16
    )
    out_grad = jnp.dot(mixed.T, attended_grad, preferred_element_type=jnp.float32)
    mixed_heads = mixed_grad.reshape(local_rows, HEADS, HEAD_DIM)
    key_heads = gathered[:, :width].reshape(total_rows, HEADS, HEAD_DIM)
    value_heads = gathered[:, width:].reshape(total_rows, HEADS, HEAD_DIM)
    scores = (
        jnp.einsum("thd,nhd->htn", queries, key_heads, preferred_element_type=jnp.float32) * factor
    )
    probabilities = jnp.exp(scores - log_total)
    prob_grads = jnp.einsum(
        "thd,nhd->htn", mixed_heads, value_heads, preferred_element_type=jnp.float32
    )
    centre = jnp.sum(prob_grads * probabilities, axis=-1, keepdims=True)
    score_grads = (probabilities * (prob_grads - centre)).astype(jnp.bfloat16)
    query_grads = (
        jnp.einsum("htn,nhd->thd", score_grads, key_heads, preferred_element_type=jnp.float32)
        * factor
    )
    value_grads = jnp.einsum(
        "htn,thd->nhd",
        probabilities.astype(jnp.bfloat16),
        mixed_heads,
        preferred_element_type=jnp.float32,
    )
    key_grads = (
        jnp.einsum("htn,thd->nhd", score_grads, queries, preferred_element_type=jnp.float32)
        * factor
    )
    key_value_grads = jnp.concatenate(
        [key_grads.reshape(total_rows, width), value_grads.reshape(total_rows, width)], axis=1
    )
    local_grads = spread_keys(key_value_grads)
    projected_grad = jnp.concatenate(
        [query_grads.reshape(local_rows, width), local_grads], axis=1
    ).astype(jnp.bfloat16)
    normed_grad = jnp.dot(projected_grad, weight_qkv.T, preferred_element_type=jnp.float32)
    qkv_grad = jnp.dot(normed.T, projected_grad, preferred_element_type=jnp.float32)
    _, first_back = jax.vjp(pre_norm, current, shift_attn, scale_attn)
    current_part, shift_attn_grad, scale_attn_grad = first_back(normed_grad)
    input_grad = middle_grad + current_part
    modulation_grad = jnp.concatenate(
        [
            shift_attn_grad,
            scale_attn_grad,
            gate_attn_grad,
            shift_mlp_grad,
            scale_mlp_grad,
            gate_mlp_grad,
        ]
    )
    return (input_grad, (qkv_grad, out_grad, up_grad, down_grad, modulation_grad))


def shards(fields, lead_index, rollout, w_qkv, w_out, w_up, w_down, w_ada, b_ada, cotangent):
    _, rows_dev, cols_dev, width = fields.shape
    local_rows = rows_dev * cols_dev
    layer_count = w_qkv.shape[0]
    context = jax.nn.silu(embedding(lead_index[0])).astype(jnp.bfloat16)
    context_wide = context.astype(jnp.float32)
    modulations = [
        (
            jnp.dot(context[None, :], w_ada[index], preferred_element_type=jnp.float32)[0]
            + b_ada[index]
        ).reshape(6, width)
        for index in range(layer_count)
    ]
    weight_sets = [
        (w_qkv[index], w_out[index], w_up[index], w_down[index]) for index in range(layer_count)
    ]
    count = rollout[0]
    current = fields.reshape(local_rows, width).astype(jnp.float32)
    saved = []
    for rollout_step in range(STEPS):
        updated = current
        kept_layers = []
        for index in range(layer_count):
            updated, kept = forward_layer(updated, modulations[index], *weight_sets[index])
            kept_layers.append(kept)
        current = jnp.where(rollout_step < count, updated, current)
        saved.append(kept_layers)
    gradient = cotangent.reshape(local_rows, width).astype(jnp.float32)
    summed = None
    shares = None
    for rollout_step in reversed(range(STEPS)):
        active = (rollout_step < count).astype(jnp.float32)
        inner = gradient * active
        layer_terms = [None] * layer_count
        for index in reversed(range(layer_count)):
            inner, layer_terms[index] = backward_layer(
                inner, saved[rollout_step][index], modulations[index], *weight_sets[index]
            )
        gradient = inner + (1.0 - active) * gradient
        modulation_grads = jnp.stack([terms[4] for terms in layer_terms])
        step_terms = (
            jnp.stack([terms[0] for terms in layer_terms]),
            jnp.stack([terms[1] for terms in layer_terms]),
            jnp.stack([terms[2] for terms in layer_terms]),
            jnp.stack([terms[3] for terms in layer_terms]),
            context_wide[None, :, None] * modulation_grads[:, None, :],
            modulation_grads,
            modulation_grads[:, 3 * width : 4 * width],
        )
        summed = step_terms if summed is None else jax.tree.map(jnp.add, summed, step_terms)
    shares = lax.psum_scatter(summed, ("lat", "lon"), scatter_dimension=1, tiled=True)
    totals = jax.tree.map(
        lambda part: part.astype(jnp.float32), lax.psum(shortened(shares), "item")
    )
    return (
        current.reshape(1, rows_dev, cols_dev, width),
        gradient.reshape(1, rows_dev, cols_dev, width),
        totals[0],
        totals[1],
        totals[2],
        totals[3],
        totals[4],
        totals[5],
        totals[6],
    )


F32 = jnp.float32
BF16 = jnp.bfloat16
GELU_A = math.sqrt(2.0 / math.pi)
GELU_B = 0.044715
LANES = 128
BLOCK = 256
PAIR = 2 * HEAD_DIM
SUM_ROWS = 48
ONES = 16
SAFE_SCORE = 60.0


def nn(left, right, precision=None):
    return lax.dot_general(
        left, right, (((1,), (0,)), ((), ())), preferred_element_type=F32, precision=precision
    )


def nt(left, right, precision=None):
    return lax.dot_general(
        left, right, (((1,), (1,)), ((), ())), preferred_element_type=F32, precision=precision
    )


def identity(size):
    rows = lax.broadcasted_iota(jnp.int32, (size, size), 0)
    columns = lax.broadcasted_iota(jnp.int32, (size, size), 1)
    return jnp.where(rows == columns, 1.0, 0.0).astype(BF16)


def turned(values):
    return nt(identity(values.shape[1]), values).astype(BF16)


def wide(column_tile, lanes):
    return jnp.concatenate([column_tile] * (lanes // LANES), axis=1)


def folded(values):
    pieces = [values[:, at : at + LANES] for at in range(0, values.shape[1], LANES)]
    return sum(pieces[1:], pieces[0])


def standardise(values):
    rows = values.shape[0]
    centred = values - jnp.sum(values, axis=0, keepdims=True) * (1.0 / rows)
    variance = jnp.sum(centred * centred, axis=0, keepdims=True) * (1.0 / rows)
    scale = lax.rsqrt(variance + 1e-06)
    return centred * scale, scale


def pre_norm_back(standard, scale, grad, gain):
    rows = standard.shape[0]
    inner = grad * gain
    first = jnp.sum(inner, axis=0, keepdims=True) * (1.0 / rows)
    second = jnp.sum(inner * standard, axis=0, keepdims=True) * (1.0 / rows)
    return scale * (inner - first - standard * second)


def part(mod_ref, index, lanes):
    return wide(mod_ref[index * D : (index + 1) * D, :], lanes)


def turn_into(source, out, at=0):
    for column in range(0, out.shape[0], BLOCK):
        width = min(BLOCK, out.shape[0] - column)
        out[column : column + width, :] = turned(source[:, at + column : at + column + width])


def prepare_first(mod, w_q_t, w_v_t, w_k, w_qkv, w_ada, b_ada, context):
    w_k[...] = w_qkv[:, D : 2 * D]
    turn_into(w_qkv, w_q_t)
    turn_into(w_qkv, w_v_t, 2 * D)
    values = nn(context[...], w_ada[...])[0:1] + b_ada
    for column in range(0, values.shape[1], LANES):
        tile = jnp.broadcast_to(values[:, column : column + LANES], (LANES, LANES))
        mod[column : column + LANES, :] = tile.T


def prepare_kernel(context, *refs):
    w_qkv, w_ada, b_ada, w_out, w_up, w_down = refs[:6]
    outs, scratch, sems = refs[8:19], refs[19:-1], refs[-1]
    sources = [w_qkv.at[0], w_ada.at[0], b_ada, w_out.at[0], w_up.at[0], w_down.at[0], w_qkv.at[1], w_ada.at[1]]
    copies = [
        pltpu.make_async_copy(source, target, sems.at[place])
        for place, (source, target) in enumerate(zip(sources, scratch))
    ]
    for copy in copies:
        copy.start()
    for copy in copies[:3]:
        copy.wait()
    prepare_first(*outs[0:4], scratch[0], scratch[1], scratch[2][0:1, :], context)
    for copy, source, out in zip(copies[3:6], scratch[3:6], outs[8:11]):
        copy.wait()
        turn_into(source, out)
    for copy in copies[6:]:
        copy.wait()
    prepare_first(*outs[4:8], scratch[6], scratch[7], scratch[2][1:2, :], context)


def prepare_rest_kernel(index, early, w_out, w_up, w_down, *outs):
    for weight, out in zip((w_out, w_up, w_down), outs):
        turn_into(weight.at[index], out)


def project(x, mod_ref, w_q_t, w_v_t, w_k, outs):
    q_out, kn_out, vt_out = outs
    lanes = x.shape[1]
    standard, _ = standardise(x)
    normed = (standard * (1.0 + part(mod_ref, 1, lanes)) + part(mod_ref, 0, lanes)).astype(BF16)
    vt_out[...] = nn(w_v_t[...], normed).astype(BF16)
    q_out[...] = (nn(w_q_t[...], normed) * HEAD_DIM ** (-0.5)).astype(BF16)
    for at in range(0, lanes, BLOCK):
        kn_out[at : at + BLOCK, :] = nn(turned(normed[:, at : at + BLOCK]), w_k[...]).astype(BF16)


def first_kernel(own, flip_x, flip_y, flip_xy, mod, w_q_t, w_v_t, w_k, x_out, xb_out, *outs):
    for index, ref in enumerate((own, flip_x, flip_y, flip_xy)):
        rows = ref.shape[0]
        flat = turned(ref[...])
        xb_out[:, index * rows : (index + 1) * rows] = flat
        x_out[:, index * rows : (index + 1) * rows] = flat.astype(F32)
    project(x_out[...], mod, w_q_t, w_v_t, w_k, outs)


def head_rows(head):
    return slice(head * HEAD_DIM, (head + 1) * HEAD_DIM)


def pair_columns(head):
    return slice(head // 2 * PAIR, (head // 2 + 1) * PAIR)


def padded(rows, head):
    zeros = jnp.zeros_like(rows)
    return jnp.concatenate([rows, zeros] if head % 2 == 0 else [zeros, rows], axis=0)


def query_top(q):
    square = q[...].astype(F32)
    square = square * square
    norms = [jnp.sum(square[head_rows(head)], axis=0, keepdims=True) for head in range(HEADS)]
    return jnp.max(functools.reduce(jnp.maximum, norms), axis=1, keepdims=True)


def key_top(kn):
    first = lax.broadcasted_iota(jnp.int32, (D, LANES), 1) * HEAD_DIM
    row = lax.broadcasted_iota(jnp.int32, (D, LANES), 0)
    pick = jnp.where((row >= first) & (row < first + HEAD_DIM), 1.0, 0.0).astype(BF16)
    square = kn[...].astype(F32)
    norms = nn((square * square).astype(BF16), pick)
    return jnp.max(jnp.max(norms, axis=0, keepdims=True), axis=1, keepdims=True) * 1.02


def value_rows(vt, rows, at):
    values = vt[rows, at]
    return jnp.concatenate([values, jnp.ones((ONES, values.shape[1]), BF16)], axis=0)


def attend_plain(q, kn, vt, put):
    chunks = [slice(at, at + BLOCK) for at in range(0, kn.shape[0], BLOCK)]

    def score(head):
        return nn(kn[:, pair_columns(head)], padded(q[head_rows(head), :], head))

    totals = {}

    def finish(head, at, probs):
        term = nn(value_rows(vt, head_rows(head), at), probs)
        totals[head] = totals[head] + term if head in totals else term
        if at == chunks[-1]:
            put(head, totals[head])

    waiting = None
    following = score(0)
    for head in range(HEADS):
        scores = following
        for at in chunks:
            if at == chunks[0] and head + 1 < HEADS:
                following = score(head + 1)
            if waiting is not None:
                finish(*waiting)
            waiting = (head, at, jnp.exp(scores[at]).astype(BF16))
    finish(*waiting)


def attend_own_kernel(early, *refs):
    q, kn, vt, *refs = refs[early:]
    passing = []
    if len(refs) > 2:
        *passing, sums, tops, passed = refs
    else:
        sums, tops = refs
    at = 0
    for source in passing:
        rows = source.shape[0]
        passed[at : at + rows, :] = source[...]
        at += rows

    def put(head, total):
        sums[head] = total

    query, key = query_top(q), key_top(kn)
    tops[0:8, :] = jnp.broadcast_to(query, (8, LANES))
    tops[8:16, :] = jnp.broadcast_to(key, (8, LANES))

    @pl.when(jnp.max(query * key) < SAFE_SCORE**2)
    def _():
        attend_plain(q, kn, vt, put)


def forward_kernel(last, early, *refs):
    refs = refs[early:]
    if last:
        active, x, x_step, *refs = refs
    else:
        x, *refs = refs
    q, kn_own, kn_far, vt_own, vt_far, sums, tops, mod, w_out_t, w_up_t, w_down_t, *refs = refs
    if not last:
        mod_next, w_q_t, w_v_t, w_k, *refs = refs
    lse, mixed, attended, middle, hidden, slope, branch, *refs = refs
    if last:
        (final,) = refs
    else:
        x_next, xb_next, *next_outs = refs
    patches = x.shape[1]
    bound = tops[0:1, 0:1] * jnp.maximum(tops[8:9, 0:1], key_top(kn_far))
    safe = jnp.max(bound) < SAFE_SCORE**2

    def put(head, total):
        total = sums[head] + total
        weight = total[HEAD_DIM : HEAD_DIM + 1]
        mixed[head_rows(head), :] = (total[:HEAD_DIM] * (1.0 / weight)).astype(BF16)
        lse[head : head + 1, :] = jnp.log(weight)

    @pl.when(safe)
    def _():
        attend_plain(q, kn_far, vt_far, put)

    @pl.when(jnp.logical_not(safe))
    def _():
        def pair_heads(pair, _):
            columns = pl.ds(pl.multiple_of(pair * PAIR, PAIR), PAIR)
            for head in range(2):
                rows = pl.ds(pl.multiple_of(pair * PAIR + head * HEAD_DIM, HEAD_DIM), HEAD_DIM)
                query = padded(q[rows, :], head)
                scores = [nn(kn[:, columns], query) for kn in (kn_own, kn_far)]
                tops = [jnp.max(score, axis=0, keepdims=True) for score in scores]
                top = jnp.maximum(*tops)
                total = None
                for score, vt in zip(scores, (vt_own, vt_far)):
                    term = nn(value_rows(vt, rows, slice(None)), jnp.exp(score - top).astype(BF16))
                    total = term if total is None else total + term
                weight = total[HEAD_DIM : HEAD_DIM + 1]
                mixed[rows, :] = (total[:HEAD_DIM] * (1.0 / weight)).astype(BF16)
                lse[pl.ds(pair * 2 + head, 1), :] = top + jnp.log(weight)
            return 0

        lax.fori_loop(0, HEADS // 2, pair_heads, 0)

    att = nn(w_out_t[...], mixed[...])
    attended[...] = att.astype(BF16)
    mid = x[...] + part(mod, 2, patches) * att
    middle[...] = mid.astype(BF16)
    standard, _ = standardise(mid)
    hidden_in = (standard * (1.0 + part(mod, 4, patches)) + part(mod, 3, patches)).astype(BF16)
    chunks = [slice(at, at + BLOCK) for at in range(0, w_up_t.shape[0], BLOCK)]

    def up(place):
        wide_rows = slice(place * BLOCK, (place + 2) * BLOCK)
        both = nn(w_up_t[wide_rows, :], hidden_in)
        return [both[:BLOCK], both[BLOCK:]]

    down = None
    waiting = None
    acts = up(0)
    for place, rows in enumerate(chunks):
        act = acts[place]
        if place % 2 == 0 and place + 2 < len(chunks):
            acts += up(place + 2)
        if place > 0:
            term = nn(w_down_t[:, chunks[place - 1]], waiting)
            down = term if down is None else down + term
        act = act.astype(BF16)
        inner = GELU_A + (GELU_A * GELU_B) * (act * act)
        half = 0.5 + 0.5 * jnp.tanh(act * inner)
        waiting = gelu = act * half
        hidden[rows, :] = waiting
        slope[rows, :] = (half + (gelu - gelu * half) * (6.0 * inner - 4.0 * GELU_A))
    down = down + nn(w_down_t[:, chunks[-1]], waiting)
    branch[...] = down.astype(BF16)
    out = mid + part(mod, 5, patches) * down
    if last:
        own = final.shape[0]
        final[...] = jnp.where(active[0] > 0.0, out[:, :own], x_step[:, :own]).T
    else:
        x_next[...] = out
        xb_next[...] = out.astype(BF16)
        project(out, mod_next, w_q_t, w_v_t, w_k, next_outs)


def put_grads(left_ref, right, where, count, at, mine, other, before):
    rows = [left_ref[pl.ds(pl.multiple_of(where[place] * count, 16), count), :] for place in range(2)]
    product = nt(jnp.concatenate(rows, axis=0), right)
    for column in range(0, product.shape[1], LANES):
        low = product[:count, column : column + LANES]
        high = product[count:, column : column + LANES]
        if before is not None:
            low = low + before[0][at : at + count, :]
            high = high + before[1][at : at + count, :]
        mine[at : at + count, :] = low.astype(mine.dtype)
        other[at : at + count, :] = high.astype(other.dtype)
        at += count


def dense_back_kernel(has_close, has_open, has_before, start, layers, waits, *refs):
    refs = list(refs)

    def take(count):
        taken = refs[:count]
        del refs[:count]
        return taken

    take(waits)
    where, active = take(2)
    close_before = open_before = None
    if has_close:
        d_own, d_got, dq, d_mid_in, x_in, mod_in, w_qkv = take(7)
        w_qkv = w_qkv.at[layers[0]]
        if has_before[0]:
            close_before = take(3)
    if start == "first":
        cots = take(2)
    elif start == "cross":
        cots = take(1)
    if has_open:
        mixed, attended, middle, hidden, slope, branch, mod, w_out, w_up, w_down = take(10)
        w_out, w_up, w_down = (ref.at[layers[1]] for ref in (w_out, w_up, w_down))
        if has_before[1]:
            open_before = take(3)
    else:
        (lines,) = take(1)
    if has_close:
        close_mine, close_other, close_mods = take(3)
    if start == "first":
        (cot_out,) = take(1)
    if has_open:
        open_mine, open_other, open_mods, d_mid_out, do_out, cen_out = take(6)
    else:
        g_out, sums_out = take(2)
        sums_at = close_before[1].shape[0]
    if has_close:
        grads_scr, normed_scr = take(2)
    if has_open:
        pg_scr, hin_scr = take(2)

    patches = middle.shape[1] if has_open else x_in.shape[1]
    totals = {}

    def add_sums(name, values):
        totals[name] = totals[name] + folded(values) if name in totals else folded(values)

    def put_sums(out, before, names):
        for place, name in enumerate(names):
            rows = slice(place * D, (place + 1) * D)
            out[rows, :] = totals[name] + before[2][rows, :] if before else totals[name]

    if start == "first":
        for index, ref in enumerate(cots):
            rows = ref.shape[0]
            cot_out[:, index * rows : (index + 1) * rows] = turned(ref[...])

    def close(at):
        standard, scale = standardise(x_in[:, at].astype(F32))
        gain = 1.0 + part(mod_in, 1, patches)
        normed_scr[:, at] = (standard * gain + part(mod_in, 0, patches)).astype(BF16)
        for third in range(3):
            if third == 0:
                piece = dq[:, at]
            else:
                rows = slice((third - 1) * D, third * D)
                piece = (d_own[rows, at] + d_got[rows, at].astype(F32)).astype(BF16)
            grads_scr[third * D : (third + 1) * D, at] = piece
        back = nn(w_qkv[...], grads_scr[:, at])
        put_grads(normed_scr, grads_scr[...], where, D // 8, 0, close_mine, close_other, close_before)
        add_sums("shift_a", back)
        add_sums("scale_a", back * standard)
        g = d_mid_in[:, at] + pre_norm_back(standard, scale, back, gain)
        if start == "cross":
            g = g + (1.0 - active[0]) * cots[0][:, at].astype(F32)
        return g

    def dense(at, g):
        standard, scale = standardise(middle[:, at].astype(F32))
        gain = 1.0 + part(mod, 4, patches)
        hin_scr[:, at] = (standard * gain + part(mod, 3, patches)).astype(BF16)
        branch_grad = (part(mod, 5, patches) * g).astype(BF16)
        add_sums("gate_m", g * branch[:, at].astype(F32))
        chunks = [slice(start, start + BLOCK) for start in range(0, w_down.shape[0], BLOCK)]
        back = None
        waiting = None

        def down(place):
            wide_rows = slice(place * BLOCK, (place + 2) * BLOCK)
            both = nn(w_down[wide_rows, :], branch_grad)
            return [both[:BLOCK], both[BLOCK:]]

        hidden_grads = down(0)
        for place, rows in enumerate(chunks):
            hidden_grad = hidden_grads[place]
            if place % 2 == 0 and place + 2 < len(chunks):
                hidden_grads += down(place + 2)
            if place > 0:
                term = nn(w_up[:, chunks[place - 1]], waiting)
                back = term if back is None else back + term
            waiting = slope[rows, at] * hidden_grad.astype(BF16)
            pg_scr[rows, at] = waiting
        back = back + nn(w_up[:, chunks[-1]], waiting)
        count = w_down.shape[0] // 8
        start_at = count * (D // LANES)
        put_grads(hidden, branch_grad, where, count, 0, open_mine, open_other, open_before)
        put_grads(hin_scr, pg_scr[...], where, D // 8, start_at, open_mine, open_other, open_before)
        add_sums("shift_m", back)
        add_sums("scale_m", back * standard)
        d_mid = g + pre_norm_back(standard, scale, back, gain)
        d_mid_out[:, at] = d_mid
        att_grad = (part(mod, 2, patches) * d_mid).astype(BF16)
        mixed_grad = nn(w_out[...], att_grad).astype(BF16)
        do_out[:, at] = mixed_grad
        start_at += (w_up.shape[1] // LANES) * (D // 8)
        put_grads(mixed, att_grad, where, D // 8, start_at, open_mine, open_other, open_before)
        add_sums("gate_a", d_mid * attended[:, at].astype(F32))
        product = mixed_grad.astype(F32) * mixed[:, at].astype(F32)
        for head in range(HEADS):
            cen_out[head : head + 1, at] = jnp.sum(product[head_rows(head)], axis=0, keepdims=True)

    at = slice(0, patches)
    g = close(at) if has_close else cot_out[:, at].astype(F32) * active[0]
    if has_open:
        dense(at, g)
    else:
        g_out[...] = g[:, : g_out.shape[0]].T
    if has_close:
        put_sums(close_mods, close_before, ("shift_a", "scale_a"))
    if has_open:
        put_sums(open_mods, open_before, ("gate_a", "shift_m", "scale_m", "gate_m"))
    else:
        sums_out[...] = lines[...]
        put_lines(sums_out, 0, close_mods[...])
        close_other[sums_at:, :] = sums_out[...].astype(BF16)


def attend_back_kernel(has_before, waits, q, kn, vt, lse, d_out, centre, *refs):
    if has_before:
        before, *refs = refs
    d_kv, dq_out, kt_scr, vn_scr = refs[waits:]
    for column in range(0, D, LANES):
        kt_scr[column : column + LANES, :] = turned(kn[:, column : column + LANES])
    for column in range(0, vt.shape[1], BLOCK):
        vn_scr[column : column + BLOCK, :] = turned(vt[:, column : column + BLOCK])

    steps = [(head, slice(at, at + BLOCK)) for head in range(HEADS) for at in range(0, kn.shape[0], BLOCK)]

    def score(head, at):
        columns = pair_columns(head)
        rows = head_rows(head)
        return nn(kn[at, columns], padded(q[rows, :], head)), nn(vn_scr[at, columns], padded(d_out[rows, :], head))

    totals = {}

    def finish(head, at, probs, score_grads):
        rows = head_rows(head)
        d_kv[D + rows.start : D + rows.stop, at] = nt(d_out[rows, :], probs).astype(d_kv.dtype)
        d_kv[rows, at] = nt(q[rows, :], score_grads).astype(d_kv.dtype)
        term = nn(kt_scr[rows, at], score_grads)
        if head not in totals:
            totals[head] = before[rows, :] + term if has_before else term
            return
        term = totals[head] + term
        if has_before:
            term = term * HEAD_DIM ** (-0.5)
        dq_out[rows, :] = term.astype(dq_out.dtype)

    waiting = None
    following = score(*steps[0])
    for place, (head, at) in enumerate(steps):
        scores, prob_grads = following
        if place + 1 < len(steps):
            following = score(*steps[place + 1])
        if waiting is not None:
            finish(*waiting)
        probs = jnp.exp(scores - lse[head : head + 1, :])
        score_grads = (probs * (prob_grads - centre[head : head + 1, :])).astype(BF16)
        waiting = (head, at, probs.astype(BF16), score_grads)
    finish(*waiting)


def split_kernel(waits, where, *refs):
    *halves, keep, sent, total_scr = refs[waits:]
    rows_half = keep.shape[0]
    at = 0
    for mine, other in zip(halves[::2], halves[1::2]):
        rows = mine.shape[0]
        total_scr[at : at + rows, :] = mine[...] + other[...].astype(F32)
        at += rows
    if at < total_scr.shape[0]:
        total_scr[at:, :] = jnp.zeros((total_scr.shape[0] - at, LANES), F32)
    odd = where[3]
    keep[...] = total_scr[pl.ds(pl.multiple_of(odd * rows_half, 16), rows_half), :]
    sent[...] = total_scr[pl.ds(pl.multiple_of((1 - odd) * rows_half, 16), rows_half), :].astype(BF16)


def pair_sum_kernel(waits, *refs):
    refs = refs[waits:]
    count = len(refs) // 3
    for keep, got, out in zip(refs[:count], refs[count : 2 * count], refs[2 * count :]):
        out[...] = (keep[...].astype(F32) + got[...].astype(F32)).astype(BF16)


def put_lines(out, row, values):
    ones = jnp.ones((16, LANES), BF16)
    high = values.astype(BF16)
    low = (values - high.astype(F32)).astype(BF16)
    line = (nt(ones, high) + nt(ones, low))[0:1]
    for column in range(0, line.shape[1], LANES):
        out[row : row + 1, :] = line[:, column : column + LANES]
        row += 1
    return row


def lines_kernel(early, context, *refs):
    *sums, out = refs
    out[...] = jnp.zeros_like(out)
    row = 2 * D // LANES
    for ref in sums:
        row = put_lines(out, row, ref[...])
    for column in range(0, D, LANES):
        out[row : row + 1, :] = context[0:1, column : column + LANES].astype(F32)
        row += 1


def join_kernel(sum_count, early, other_early, mine, sums, got, out):
    rows = mine.shape[0]
    out[:rows, :] = (mine[...] + got[:rows, :].astype(F32)).astype(BF16)
    other = got[rows:, :].astype(F32)
    summed = lax.broadcasted_iota(jnp.int32, (SUM_ROWS, LANES), 0) < sum_count
    out[rows:, :] = (sums[...] + jnp.where(summed, other, 0.0)).astype(BF16)


def pair_kernel(rows, where, own, got, out):
    out[:rows, :] = (own[:rows, :].astype(F32) + got[:rows, :].astype(F32)).astype(BF16)
    odd = where[3]
    size = SUM_ROWS
    out[pl.ds(pl.multiple_of(rows + odd * size, 16), size), :] = own[rows:, :]
    out[pl.ds(pl.multiple_of(rows + (1 - odd) * size, 16), size), :] = got[rows:, :]


def gather_kernel(layer, where, own, got, *refs):
    outs, qkv_out, rows_scr, scratch, sems = refs[-9:-6], refs[-6], refs[-5], refs[-4:-1], refs[-1]
    if layer == 1:
        outs = refs[-8:-5]
    half = own.shape[0]
    rows_scr[pl.ds(pl.multiple_of(where[3] * half, 16), half), :] = own[...]
    rows_scr[pl.ds(pl.multiple_of((1 - where[3]) * half, 16), half), :] = got[...]
    at = 0
    copies = []
    for place, (out, held) in enumerate(zip(outs, scratch)):
        rows = held.shape[0]
        for column in range(0, held.shape[1], LANES):
            held[:, column : column + LANES] = rows_scr[at : at + rows, :].astype(F32)
            at += rows
        copies.append(pltpu.make_async_copy(held, out.at[layer], sems.at[place]))
        copies[-1].start()
    if layer == 0:
        rows = qkv_out.shape[0]
        for column in range(0, qkv_out.shape[1], LANES):
            qkv_out[:, column : column + LANES] = rows_scr[at : at + rows, :].astype(F32)
            at += rows
    for copy in copies:
        copy.wait()


def finish_kernel(item_count, where, own, got, qkv_1, qkv_hbm, ada_hbm, bias_out, shift_out, *scratch):
    layers = 2
    qkv_out, ada_out, sum_scr, bias_scr, shift_scr, sems = scratch
    device, high = where[0], where[4]
    slice_rows = qkv_out.shape[0]
    copies = [pltpu.make_async_copy(qkv_1, qkv_hbm.at[1], sems.at[0])]
    copies[0].start()
    close_rows = slice_rows * (3 * D // LANES)
    for other in range(2):
        rows = slice(close_rows + other * SUM_ROWS, close_rows + (other + 1) * SUM_ROWS)
        sum_scr[2 * high + other] = own[rows, :].astype(F32)
        sum_scr[2 * (1 - high) + other] = got[rows, :].astype(F32)
    for tile in range(3 * D // LANES):
        rows = slice(tile * slice_rows, (tile + 1) * slice_rows)
        total = own[rows, :].astype(F32) + got[rows, :].astype(F32)
        qkv_out[:, tile * LANES : (tile + 1) * LANES] = total
    copies.append(pltpu.make_async_copy(qkv_out, qkv_hbm.at[0], sems.at[1]))
    copies[1].start()
    tiles = 6 * D // LANES
    contexts = []
    for other in range(item_count):
        line = jnp.concatenate([sum_scr[other, layers * tiles + c : layers * tiles + c + 1, :] for c in range(3)], axis=1)
        contexts.append(line)
    square = jnp.concatenate(contexts + [jnp.zeros((8 - item_count, D), F32)], axis=0)
    spot = lax.broadcasted_iota(jnp.int32, (slice_rows, D), 1)
    want = lax.broadcasted_iota(jnp.int32, (slice_rows, D), 0) + device * slice_rows
    pick = jnp.where(spot == want, 1.0, 0.0).astype(BF16)
    columns = nt(pick, square.astype(BF16))
    bias_rows = bias_out.shape[1]
    for index in range(layers):
        flats = []
        for tile in range(tiles):
            row = index * tiles + tile
            total = None
            flat = None
            for other in range(item_count):
                line = sum_scr[other, row : row + 1, :]
                term = columns[:, other : other + 1] * line
                total = term if total is None else total + term
                flat = line if flat is None else flat + line
            ada_out[index, :, tile * LANES : (tile + 1) * LANES] = total
            flats.append(flat)
        copies.append(pltpu.make_async_copy(ada_out.at[index], ada_hbm.at[index], sems.at[2 + index]))
        copies[-1].start()
        flat = jnp.concatenate(flats, axis=1)
        for place in range(flat.shape[1] // bias_rows):
            bias_scr[place, index : index + 1, :] = flat[:, place * bias_rows : (place + 1) * bias_rows]
            at = 3 * D + place * slice_rows
            shift_scr[place, index : index + 1, :] = flat[:, at : at + slice_rows]
    bias_out[...] = bias_scr[device]
    shift_out[...] = shift_scr[device]
    for copy in copies:
        copy.wait()


VMEM = pl.BlockSpec(memory_space=pltpu.VMEM)
SMEM = pl.BlockSpec(memory_space=pltpu.SMEM)
ANY = pl.BlockSpec(memory_space=pl.ANY)
HBM = pl.BlockSpec(memory_space=pltpu.HBM)


def layer_block(array, index):
    return pl.BlockSpec((None,) + array.shape[1:], lambda step: (index,) + (0,) * (array.ndim - 1))


def call(body, args, outs, scratch=(), flops=0, name=None, direct=0, aliases=None):
    arrays = [arg[0] if isinstance(arg, tuple) else arg for arg in args]
    specs = [arg[1] if isinstance(arg, tuple) else VMEM for arg in args]
    return pl.pallas_call(
        body,
        out_shape=[jax.ShapeDtypeStruct(shape, kind) for shape, kind in outs],
        in_specs=specs,
        out_specs=[ANY] * direct + [VMEM] * (len(outs) - direct),
        input_output_aliases=aliases or {},
        scratch_shapes=[one if not isinstance(one, tuple) else pltpu.VMEM(*one) for one in scratch],
        compiler_params=pltpu.CompilerParams(vmem_limit_bytes=VMEM_LIMIT),
        cost_estimate=pl.CostEstimate(flops=flops, bytes_accessed=0, transcendentals=0),
        name=name,
    )(*arrays)


VMEM_LIMIT = 14 * 1024 * 1024


def fast_shards(
    lat_count, lon_count, item_count,
    fields, lead_index, rollout, w_qkv, w_out, w_up, w_down, w_ada, b_ada, cotangent,
):
    _, rows_dev, cols_dev, width = fields.shape
    local = rows_dev * cols_dev
    layers = w_qkv.shape[0]
    ff = w_up.shape[2]
    patches = 4 * local
    device = lax.axis_index("lat") * lon_count + lax.axis_index("lon")
    item = lax.axis_index("item")
    where = jnp.stack([device, device ^ 1, item, item & 1, item >> 1]).astype(jnp.int32)
    active = (1 < rollout[0]).astype(F32)[None]

    def plane_flip(value, flip_lat, flip_y):
        pairs = [
            (a * lon_count + b, (a ^ flip_lat) * lon_count + (b ^ (2 * flip_y)))
            for a in range(lat_count)
            for b in range(lon_count)
        ]
        return lax.ppermute(value, ("lat", "lon"), pairs)

    def swap(value):
        return lax.ppermute(value, "lon", [(index, index ^ 1) for index in range(lon_count)])

    def with_item(value, flip):
        return lax.ppermute(value, "item", [(index, index ^ flip) for index in range(item_count)])

    def plane_parts(value):
        return [value, plane_flip(value, 1, 0), plane_flip(value, 0, 1), plane_flip(value, 1, 1)]

    field_parts = plane_parts(fields.reshape(local, width))

    context = jax.nn.silu(embedding(lead_index[0])).astype(BF16)
    context = jnp.broadcast_to(context[None, :], (16, width))
    square = (width, patches)
    natural = (patches, width)
    weights = (w_qkv, w_ada, b_ada, w_out, w_up, w_down)
    weights = [(pltpu.with_memory_space_constraint(value, pltpu.HBM), HBM) for value in weights]
    first_outs = [((6 * width, LANES), F32)] + [((width, width), BF16)] * 3
    rest_outs = [((width, width), BF16), ((ff, width), BF16), ((width, ff), BF16)]
    first_fetch = [((width, 3 * width), BF16), ((width, 6 * width), BF16)]
    rest_fetch = [((width, width), BF16), ((width, ff), BF16), ((ff, width), BF16)]
    prepared = call(
        prepare_kernel,
        [context, *weights, (where, SMEM), (active, SMEM)],
        first_outs * 2 + rest_outs,
        first_fetch + [(b_ada.shape, F32)] + rest_fetch + first_fetch + [pltpu.SemaphoreType.DMA((8,))],
        name="prepare",
    )
    first_parts = [prepared[0:4], prepared[4:8]]
    rest_parts = [prepared[8:11]]
    mods = [one[0] for one in first_parts]

    project_outs = [(square, F32), (square, BF16), (square, BF16), (natural, BF16), (square, BF16)]
    dense_flops = 2 * patches * (width * 3 * width + width * width + 2 * width * ff)
    score_flops = 2 * patches * 2 * patches * width * 4
    x, xb, *projected = call(
        first_kernel,
        [*field_parts, *first_parts[0]],
        project_outs,
        flops=2 * patches * width * 4 * width,
        name="first",
    )
    saved = []
    for step in range(STEPS):
        for index in range(layers):
            q, kn, vt = projected
            if len(rest_parts) == index:
                rest_parts.append(
                    call(
                        functools.partial(prepare_rest_kernel, index),
                        [(kn, ANY), w_out, w_up, w_down],
                        rest_outs,
                        name="prepare_rest",
                    )
                )
            kn_far, vt_far = swap(kn), swap(vt)
            early = [w_up] if len(rest_parts) == index + 1 < layers else []
            passing = []
            if step == STEPS - 1:
                passing = [cotangent.reshape(local, width)] if index == 0 else cot_parts
            passed = [((len(passing) * local, width), BF16)] if passing else []
            sums, tops, *passed = call(
                functools.partial(attend_own_kernel, len(early)),
                early + [q, kn, vt] + passing,
                [((HEADS, HEAD_DIM + ONES, patches), F32), ((16, LANES), F32)] + passed,
                flops=10 * score_flops,
                name="forward_own",
            )
            if passed:
                cot_parts = [passed[0], plane_flip(passed[0], 1 - index, index)]
            last = step == STEPS - 1 and index == layers - 1
            if index == 0 and step > 0:
                x_step = x
            following = list(first_parts[(index + 1) % layers])
            early = [w_down] if len(rest_parts) == index + 1 < layers else []
            lse, mixed, attended, middle, hidden, slope, branch, *results = call(
                functools.partial(forward_kernel, last, len(early)),
                early
                + ([(active, SMEM), x, x_step] if last else [x])
                + [q, kn, kn_far, vt, vt_far, sums, tops, mods[index], *rest_parts[index]]
                + ([] if last else following),
                [
                    ((HEADS, patches), F32),
                    (square, BF16),
                    (square, BF16),
                    (square, BF16),
                    ((ff, patches), BF16),
                    ((ff, patches), BF16),
                    (square, BF16),
                ]
                + ([((local, width), F32)] if last else project_outs),
                flops=dense_flops + 2 * score_flops,
                name="forward",
            )
            saved.append((xb, [mixed, attended, middle, hidden, slope, branch], (q, kn, kn_far, vt, vt_far, lse)))
            if last:
                final = results[0]
            else:
                x, xb, *projected = results

    slice_rows = width // 8
    open_rows = 2 * (ff // 8) * (width // LANES) + slice_rows * (width // LANES)
    close_rows = slice_rows * (3 * width // LANES)
    order = [(step, index) for step in reversed(range(STEPS)) for index in reversed(range(layers))]
    open_done = [None] * layers
    close_done = [None] * layers
    pending = None
    for place in range(len(order) + 1):
        has_close = pending is not None
        has_open = place < len(order)
        use = [order[place - 1][1], order[place][1] if has_open else 0]
        waits = []
        if has_close and close_done[use[0]]:
            waits = [pair_1] if has_open else []
        args = [(value, ANY) for value in waits] + [(where, SMEM), (active, SMEM)]
        outs = []
        scratch = []
        has_before = [False, False]
        start = ""
        if has_close:
            args += pending
            if close_done[use[0]] is not None:
                has_before[0] = True
                args += close_done[use[0]]
            outs += [((close_rows, LANES), F32)]
            sent_rows = close_rows + (0 if has_open else SUM_ROWS)
            outs += [((sent_rows, LANES), BF16 if has_before[0] else F32), ((2 * width, LANES), F32)]
            scratch += [((3 * width, patches), BF16), (square, BF16)]
        if place == 0:
            start = "first"
            args += cot_parts
            outs += [(square, BF16)]
        elif has_open and order[place][0] != order[place - 1][0]:
            start = "cross"
            args += [cot_t]
        if has_open:
            step, index = order[place]
            xb, kept, heads = saved[step * layers + index]
            args += kept + [mods[index], w_out, w_up, w_down]
            if open_done[index] is not None:
                has_before[1] = True
                args += open_done[index]
            outs += [
                ((open_rows, LANES), F32),
                ((open_rows, LANES), BF16 if has_before[1] else F32),
                ((4 * width, LANES), F32),
                (square, F32),
                (square, BF16),
                ((HEADS, patches), F32),
            ]
            scratch += [((ff, patches), BF16), (square, BF16)]
        else:
            args += [lines]
            outs += [((local, width), F32), ((SUM_ROWS, LANES), F32)]
        results = list(
            call(
                functools.partial(dense_back_kernel, has_close, has_open, has_before, start, use, len(waits)),
                args,
                outs,
                scratch,
                flops=2 * dense_flops if has_open else 0,
                name="dense_back" if has_open else "close_back",
            )
        )
        if has_close:
            close_done[use[0]] = results[:3]
            del results[:3]
        if start == "first":
            cot_t = results.pop(0)
        if not has_open:
            gradient, line = results
            break
        open_done[index] = results[:3]
        d_mid, d_out, centre = results[3:]
        q, kn, kn_far, vt, vt_far, lse = heads
        halves = [open_done[index][0], open_done[index][1]]
        if index == 0:
            halves += [close_done[1][0], close_done[1][1]]
        half_rows = -(-sum(half.shape[0] for half in halves[::2]) // 32) * 16

        def split(waits):
            pieces = [half if place % 2 == 0 else swap(half) for place, half in enumerate(halves)]
            return call(
                functools.partial(split_kernel, len(waits)),
                [(where, SMEM), *waits, *pieces],
                [((half_rows, LANES), F32), ((half_rows, LANES), BF16)],
                [((2 * half_rows, LANES), F32)],
                name="split",
            )

        def pair_sum(late, keeps, gots, others=()):
            outs = [(keep.shape, BF16) for keep in keeps]
            body = functools.partial(pair_sum_kernel, 1 + len(others))
            return call(body, [(late, ANY), *others, *keeps, *gots], outs, name="pair_sum")

        waits = []
        if has_before[1] and index == 0:
            pair_got_1 = with_item(pair_1, 2)
            lines = call(
                lines_kernel,
                [(pair_got_1, ANY), context, open_done[0][2], close_done[1][2], open_done[1][2]],
                [((SUM_ROWS, LANES), F32)],
                flops=10 * score_flops,
                name="lines",
            )[0]
            keep, sent = split([(lines, ANY)])
            got_0 = with_item(sent, 1)
            waits = [keep]
        d_far, dq = call(
            functools.partial(attend_back_kernel, False, len(waits)),
            [q, kn_far, vt_far, lse, d_out, centre] + [(value, ANY) for value in waits],
            [((2 * width, patches), BF16), (square, F32)],
            [(square, BF16), (natural, BF16)],
            flops=10 * score_flops,
            name="attend_far",
        )
        d_got = swap(d_far)
        waits = []
        if has_before[1]:
            if index == 1:
                keep, sent = split([(d_far, ANY)])
                got_1 = with_item(sent, 1)
                waits = [keep]
            else:
                (pair_0,) = pair_sum(d_far, [keep], [got_0])
                pair_got_0 = with_item(pair_0, 2)
                waits = [pair_0]
        d_own, dq = call(
            functools.partial(attend_back_kernel, True, len(waits)),
            [q, kn, vt, lse, d_out, centre, dq] + [(value, ANY) for value in waits],
            [((2 * width, patches), F32), (square, BF16)],
            [(square, BF16), (natural, BF16)],
            flops=10 * score_flops,
            name="attend_own",
        )
        if has_before[1] and index == 1:
            (pair_1,) = pair_sum(dq, [keep], [got_1])
        elif has_before[1]:
            (item_1,) = pair_sum(dq, [pair_1], [pair_got_1])
            item_got_1 = with_item(item_1, 1)
        pending = [d_own, d_got, dq, d_mid, xb, mods[index], w_qkv]

    message = call(
        functools.partial(join_kernel, layers * 6 * width // LANES),
        [(pair_got_0, ANY), (item_got_1, ANY), close_done[0][0], line, swap(close_done[0][1])],
        [((close_rows + SUM_ROWS, LANES), BF16)],
        name="join",
    )[0]
    message_got = with_item(message, 1)
    stacks = [
        ((layers, ff // 8, width), F32),
        ((layers, slice_rows, ff), F32),
        ((layers, slice_rows, width), F32),
    ]
    held = [(shape[1:], kind) for shape, kind in stacks]
    sems = [pltpu.SemaphoreType.DMA((3,))]
    stacked = call(
        functools.partial(gather_kernel, 1),
        [(where, SMEM), item_1, item_got_1],
        stacks,
        [((2 * pair_1.shape[0], LANES), BF16)] + held + sems,
        name="gather",
        direct=3,
    )
    early = (pltpu.with_memory_space_constraint(stacked[2], pltpu.HBM), HBM)
    (item_0,) = pair_sum(message_got, [pair_0], [pair_got_0], [early])
    message = call(
        functools.partial(pair_kernel, close_rows),
        [(where, SMEM), message, message_got],
        [((close_rows + 2 * SUM_ROWS, LANES), BF16)],
        name="pair",
    )[0]
    down_grad, up_grad, out_grad, qkv_1 = call(
        functools.partial(gather_kernel, 0),
        [(where, SMEM), item_0, with_item(item_0, 1)] + [(value, ANY) for value in stacked],
        stacks + [((slice_rows, 3 * width), F32)],
        [((2 * pair_0.shape[0], LANES), BF16)] + held + sems,
        name="gather",
        direct=3,
        aliases={3: 0, 4: 1, 5: 2},
    )
    bias_rows = 6 * width // 8
    qkv_grad, ada_grad, bias_grad, shift_grad = call(
        functools.partial(finish_kernel, item_count),
        [(where, SMEM), message, with_item(message, 2), qkv_1],
        [
            ((layers, slice_rows, 3 * width), F32),
            ((layers, slice_rows, 6 * width), F32),
            ((layers, bias_rows), F32),
            ((layers, slice_rows), F32),
        ],
        [
            ((slice_rows, 3 * width), F32),
            ((layers, slice_rows, 6 * width), F32),
            ((item_count, SUM_ROWS, LANES), F32),
            ((8, layers, bias_rows), F32),
            ((8, layers, slice_rows), F32),
            pltpu.SemaphoreType.DMA((4,)),
        ],
        name="finish",
        direct=2,
    )
    field_shape = (1, rows_dev, cols_dev, width)
    return (
        final.reshape(field_shape),
        gradient.reshape(field_shape),
        qkv_grad,
        out_grad,
        up_grad,
        down_grad,
        ada_grad,
        bias_grad,
        shift_grad,
    )


def solution(mesh):
    lat_count, lon_count, item_count = mesh.shape["lat"], mesh.shape["lon"], mesh.shape["item"]
    if lat_count == 2 and lon_count == 4:
        body = functools.partial(fast_shards, lat_count, lon_count, item_count)
    else:
        body = shards
    return jax.shard_map(
        body,
        mesh=mesh,
        in_specs=(
            P("item", "lat", "lon", None),
            P("item"),
            P("item"),
            P(),
            P(),
            P(),
            P(),
            P(),
            P(),
            P("item", "lat", "lon", None),
        ),
        out_specs=(
            P("item", "lat", "lon", None),
            P("item", "lat", "lon", None),
            P(None, ("lat", "lon"), None),
            P(None, ("lat", "lon"), None),
            P(None, ("lat", "lon"), None),
            P(None, ("lat", "lon"), None),
            P(None, ("lat", "lon"), None),
            P(None, ("lat", "lon")),
            P(None, ("lat", "lon")),
        ),
        check_vma=False,
    )
```

```python
import functools
import math

import jax
import jax.numpy as jnp
from jax import lax
from jax.experimental import pallas as pl
from jax.experimental.pallas import tpu as pltpu
from jax.sharding import PartitionSpec as P

D = 384
HEADS = 6
HEAD_DIM = 64
STEPS = 2


def shortened(shard):
    return jax.tree.map(lambda a: a.astype(jnp.bfloat16) if a.dtype == jnp.float32 else a, shard)


def embedding(lead):
    half_width = D // 2
    lead_hours = 6.0 * (lead.astype(jnp.float32) + 1.0)
    frequencies = jnp.exp(
        -math.log(10000.0) * jnp.arange(half_width, dtype=jnp.float32) / half_width
    )
    angles = lead_hours * frequencies
    return jnp.concatenate([jnp.sin(angles), jnp.cos(angles)])


def pre_norm(values, shift_part, scale_part):
    centred = values - jnp.mean(values, axis=-1, keepdims=True)
    variance = jnp.mean(centred * centred, axis=-1, keepdims=True)
    return centred * lax.rsqrt(variance + 1e-06) * (1.0 + scale_part) + shift_part


def gather_keys(keys_values):
    band_rows = lax.all_gather(keys_values, "lon", axis=0, tiled=True)
    return lax.all_gather(band_rows, "lat", axis=0, tiled=True)


def spread_keys(key_value_grads):
    band_grads = lax.psum_scatter(
        key_value_grads.astype(jnp.bfloat16), "lat", scatter_dimension=0, tiled=True
    )
    return lax.psum_scatter(band_grads, "lon", scatter_dimension=0, tiled=True).astype(jnp.float32)


def forward_layer(current, modulation, weight_qkv, weight_out, weight_up, weight_down):
    local_rows, width = current.shape
    shift_attn, scale_attn, gate_attn, shift_mlp, scale_mlp, gate_mlp = modulation
    normed = pre_norm(current, shift_attn, scale_attn).astype(jnp.bfloat16)
    projected = jnp.dot(normed, weight_qkv, preferred_element_type=jnp.float32).astype(jnp.bfloat16)
    queries = projected[:, :width].reshape(local_rows, HEADS, HEAD_DIM)
    own_keys = projected[:, width:]
    gathered = gather_keys(own_keys)
    total_rows = gathered.shape[0]
    key_heads = gathered[:, :width].reshape(total_rows, HEADS, HEAD_DIM)
    value_heads = gathered[:, width:].reshape(total_rows, HEADS, HEAD_DIM)
    scores = jnp.einsum(
        "thd,nhd->htn", queries, key_heads, preferred_element_type=jnp.float32
    ) * HEAD_DIM ** (-0.5)
    log_total = jax.nn.logsumexp(scores, axis=-1, keepdims=True)
    probabilities = jnp.exp(scores - log_total).astype(jnp.bfloat16)
    mixed = jnp.einsum(
        "htn,nhd->thd", probabilities, value_heads, preferred_element_type=jnp.float32
    )
    mixed = mixed.reshape(local_rows, width).astype(jnp.bfloat16)
    attended = jnp.dot(mixed, weight_out, preferred_element_type=jnp.float32)
    middle = current + gate_attn * attended
    hidden_in = pre_norm(middle, shift_mlp, scale_mlp).astype(jnp.bfloat16)
    pre_act = jnp.dot(hidden_in, weight_up, preferred_element_type=jnp.float32)
    hidden = jax.nn.gelu(pre_act).astype(jnp.bfloat16)
    branch = jnp.dot(hidden, weight_down, preferred_element_type=jnp.float32)
    output = middle + gate_mlp * branch
    kept = (
        current,
        normed,
        queries,
        gathered,
        own_keys,
        log_total,
        mixed,
        attended,
        middle,
        hidden_in,
        pre_act,
        hidden,
        branch,
    )
    return (output, kept)


def backward_layer(grad_out, kept, modulation, weight_qkv, weight_out, weight_up, weight_down):
    (
        current,
        normed,
        queries,
        gathered,
        own_keys,
        log_total,
        mixed,
        attended,
        middle,
        hidden_in,
        pre_act,
        hidden,
        branch,
    ) = kept
    local_rows, width = current.shape
    total_rows = gathered.shape[0]
    shift_attn, scale_attn, gate_attn, shift_mlp, scale_mlp, gate_mlp = modulation
    factor = HEAD_DIM ** (-0.5)
    branch_grad = (gate_mlp * grad_out).astype(jnp.bfloat16)
    gate_mlp_grad = jnp.sum(grad_out * branch, axis=0)
    hidden_grad = jnp.dot(branch_grad, weight_down.T, preferred_element_type=jnp.float32)
    down_grad = jnp.dot(hidden.T, branch_grad, preferred_element_type=jnp.float32)
    _, gelu_back = jax.vjp(jax.nn.gelu, pre_act)
    pre_grad = gelu_back(hidden_grad)[0].astype(jnp.bfloat16)
    hidden_in_grad = jnp.dot(pre_grad, weight_up.T, preferred_element_type=jnp.float32)
    up_grad = jnp.dot(hidden_in.T, pre_grad, preferred_element_type=jnp.float32)
    _, second_back = jax.vjp(pre_norm, middle, shift_mlp, scale_mlp)
    middle_part, shift_mlp_grad, scale_mlp_grad = second_back(hidden_in_grad)
    middle_grad = grad_out + middle_part
    attended_grad = (gate_attn * middle_grad).astype(jnp.bfloat16)
    gate_attn_grad = jnp.sum(middle_grad * attended, axis=0)
    mixed_grad = jnp.dot(attended_grad, weight_out.T, preferred_element_type=jnp.float32).astype(
        jnp.bfloat16
    )
    out_grad = jnp.dot(mixed.T, attended_grad, preferred_element_type=jnp.float32)
    mixed_heads = mixed_grad.reshape(local_rows, HEADS, HEAD_DIM)
    key_heads = gathered[:, :width].reshape(total_rows, HEADS, HEAD_DIM)
    value_heads = gathered[:, width:].reshape(total_rows, HEADS, HEAD_DIM)
    scores = (
        jnp.einsum("thd,nhd->htn", queries, key_heads, preferred_element_type=jnp.float32) * factor
    )
    probabilities = jnp.exp(scores - log_total)
    prob_grads = jnp.einsum(
        "thd,nhd->htn", mixed_heads, value_heads, preferred_element_type=jnp.float32
    )
    centre = jnp.sum(prob_grads * probabilities, axis=-1, keepdims=True)
    score_grads = (probabilities * (prob_grads - centre)).astype(jnp.bfloat16)
    query_grads = (
        jnp.einsum("htn,nhd->thd", score_grads, key_heads, preferred_element_type=jnp.float32)
        * factor
    )
    value_grads = jnp.einsum(
        "htn,thd->nhd",
        probabilities.astype(jnp.bfloat16),
        mixed_heads,
        preferred_element_type=jnp.float32,
    )
    key_grads = (
        jnp.einsum("htn,thd->nhd", score_grads, queries, preferred_element_type=jnp.float32)
        * factor
    )
    key_value_grads = jnp.concatenate(
        [key_grads.reshape(total_rows, width), value_grads.reshape(total_rows, width)], axis=1
    )
    local_grads = spread_keys(key_value_grads)
    projected_grad = jnp.concatenate(
        [query_grads.reshape(local_rows, width), local_grads], axis=1
    ).astype(jnp.bfloat16)
    normed_grad = jnp.dot(projected_grad, weight_qkv.T, preferred_element_type=jnp.float32)
    qkv_grad = jnp.dot(normed.T, projected_grad, preferred_element_type=jnp.float32)
    _, first_back = jax.vjp(pre_norm, current, shift_attn, scale_attn)
    current_part, shift_attn_grad, scale_attn_grad = first_back(normed_grad)
    input_grad = middle_grad + current_part
    modulation_grad = jnp.concatenate(
        [
            shift_attn_grad,
            scale_attn_grad,
            gate_attn_grad,
            shift_mlp_grad,
            scale_mlp_grad,
            gate_mlp_grad,
        ]
    )
    return (input_grad, (qkv_grad, out_grad, up_grad, down_grad, modulation_grad))


def shards(fields, lead_index, rollout, w_qkv, w_out, w_up, w_down, w_ada, b_ada, cotangent):
    _, rows_dev, cols_dev, width = fields.shape
    local_rows = rows_dev * cols_dev
    layer_count = w_qkv.shape[0]
    context = jax.nn.silu(embedding(lead_index[0])).astype(jnp.bfloat16)
    context_wide = context.astype(jnp.float32)
    modulations = [
        (
            jnp.dot(context[None, :], w_ada[index], preferred_element_type=jnp.float32)[0]
            + b_ada[index]
        ).reshape(6, width)
        for index in range(layer_count)
    ]
    weight_sets = [
        (w_qkv[index], w_out[index], w_up[index], w_down[index]) for index in range(layer_count)
    ]
    count = rollout[0]
    current = fields.reshape(local_rows, width).astype(jnp.float32)
    saved = []
    for rollout_step in range(STEPS):
        updated = current
        kept_layers = []
        for index in range(layer_count):
            updated, kept = forward_layer(updated, modulations[index], *weight_sets[index])
            kept_layers.append(kept)
        current = jnp.where(rollout_step < count, updated, current)
        saved.append(kept_layers)
    gradient = cotangent.reshape(local_rows, width).astype(jnp.float32)
    summed = None
    shares = None
    for rollout_step in reversed(range(STEPS)):
        active = (rollout_step < count).astype(jnp.float32)
        inner = gradient * active
        layer_terms = [None] * layer_count
        for index in reversed(range(layer_count)):
            inner, layer_terms[index] = backward_layer(
                inner, saved[rollout_step][index], modulations[index], *weight_sets[index]
            )
        gradient = inner + (1.0 - active) * gradient
        modulation_grads = jnp.stack([terms[4] for terms in layer_terms])
        step_terms = (
            jnp.stack([terms[0] for terms in layer_terms]),
            jnp.stack([terms[1] for terms in layer_terms]),
            jnp.stack([terms[2] for terms in layer_terms]),
            jnp.stack([terms[3] for terms in layer_terms]),
            context_wide[None, :, None] * modulation_grads[:, None, :],
            modulation_grads,
            modulation_grads[:, 3 * width : 4 * width],
        )
        summed = step_terms if summed is None else jax.tree.map(jnp.add, summed, step_terms)
    shares = lax.psum_scatter(summed, ("lat", "lon"), scatter_dimension=1, tiled=True)
    totals = jax.tree.map(
        lambda part: part.astype(jnp.float32), lax.psum(shortened(shares), "item")
    )
    return (
        current.reshape(1, rows_dev, cols_dev, width),
        gradient.reshape(1, rows_dev, cols_dev, width),
        totals[0],
        totals[1],
        totals[2],
        totals[3],
        totals[4],
        totals[5],
        totals[6],
    )


F32 = jnp.float32
BF16 = jnp.bfloat16
GELU_A = math.sqrt(2.0 / math.pi)
GELU_B = 0.044715
LANES = 128
BLOCK = 256
PAIR = 2 * HEAD_DIM
SUM_ROWS = 48
ONES = 16
SAFE_SCORE = 60.0


def nn(left, right, precision=None):
    return lax.dot_general(
        left, right, (((1,), (0,)), ((), ())), preferred_element_type=F32, precision=precision
    )


def nt(left, right, precision=None):
    return lax.dot_general(
        left, right, (((1,), (1,)), ((), ())), preferred_element_type=F32, precision=precision
    )


def identity(size):
    rows = lax.broadcasted_iota(jnp.int32, (size, size), 0)
    columns = lax.broadcasted_iota(jnp.int32, (size, size), 1)
    return jnp.where(rows == columns, 1.0, 0.0).astype(BF16)


def turned(values):
    return nt(identity(values.shape[1]), values).astype(BF16)


def wide(column_tile, lanes):
    return jnp.concatenate([column_tile] * (lanes // LANES), axis=1)


def folded(values):
    pieces = [values[:, at : at + LANES] for at in range(0, values.shape[1], LANES)]
    return sum(pieces[1:], pieces[0])


def standardise(values):
    rows = values.shape[0]
    centred = values - jnp.sum(values, axis=0, keepdims=True) * (1.0 / rows)
    variance = jnp.sum(centred * centred, axis=0, keepdims=True) * (1.0 / rows)
    scale = lax.rsqrt(variance + 1e-06)
    return centred * scale, scale


def pre_norm_back(standard, scale, grad, gain):
    rows = standard.shape[0]
    inner = grad * gain
    first = jnp.sum(inner, axis=0, keepdims=True) * (1.0 / rows)
    second = jnp.sum(inner * standard, axis=0, keepdims=True) * (1.0 / rows)
    return scale * (inner - first - standard * second)


def part(mod_ref, index, lanes):
    return wide(mod_ref[index * D : (index + 1) * D, :], lanes)


def turn_into(source, out, at=0):
    for column in range(0, out.shape[0], BLOCK):
        width = min(BLOCK, out.shape[0] - column)
        out[column : column + width, :] = turned(source[:, at + column : at + column + width])


def prepare_first(mod, w_q_t, w_v_t, w_k, w_qkv, w_ada, b_ada, context):
    w_k[...] = w_qkv[:, D : 2 * D]
    turn_into(w_qkv, w_q_t)
    turn_into(w_qkv, w_v_t, 2 * D)
    values = nn(context[...], w_ada[...])[0:1] + b_ada
    for column in range(0, values.shape[1], LANES):
        tile = jnp.broadcast_to(values[:, column : column + LANES], (LANES, LANES))
        mod[column : column + LANES, :] = tile.T


def prepare_kernel(context, *refs):
    w_qkv, w_ada, b_ada, w_out, w_up, w_down = refs[:6]
    outs, scratch, sems = refs[8:19], refs[19:-1], refs[-1]
    sources = [w_qkv.at[0], w_ada.at[0], b_ada, w_out.at[0], w_up.at[0], w_down.at[0], w_qkv.at[1], w_ada.at[1]]
    copies = [
        pltpu.make_async_copy(source, target, sems.at[place])
        for place, (source, target) in enumerate(zip(sources, scratch))
    ]
    for copy in copies:
        copy.start()
    for copy in copies[:3]:
        copy.wait()
    prepare_first(*outs[0:4], scratch[0], scratch[1], scratch[2][0:1, :], context)
    for copy, source, out in zip(copies[3:6], scratch[3:6], outs[8:11]):
        copy.wait()
        turn_into(source, out)
    for copy in copies[6:]:
        copy.wait()
    prepare_first(*outs[4:8], scratch[6], scratch[7], scratch[2][1:2, :], context)


def prepare_rest_kernel(index, early, w_out, w_up, w_down, *outs):
    for weight, out in zip((w_out, w_up, w_down), outs):
        turn_into(weight.at[index], out)


def project(x, mod_ref, w_q_t, w_v_t, w_k, outs):
    q_out, kn_out, vt_out = outs
    lanes = x.shape[1]
    standard, _ = standardise(x)
    normed = (standard * (1.0 + part(mod_ref, 1, lanes)) + part(mod_ref, 0, lanes)).astype(BF16)
    vt_out[...] = nn(w_v_t[...], normed).astype(BF16)
    q_out[...] = (nn(w_q_t[...], normed) * HEAD_DIM ** (-0.5)).astype(BF16)
    for at in range(0, lanes, BLOCK):
        kn_out[at : at + BLOCK, :] = nn(turned(normed[:, at : at + BLOCK]), w_k[...]).astype(BF16)


def first_kernel(own, flip_x, flip_y, flip_xy, mod, w_q_t, w_v_t, w_k, x_out, xb_out, *outs):
    for index, ref in enumerate((own, flip_x, flip_y, flip_xy)):
        rows = ref.shape[0]
        flat = turned(ref[...])
        xb_out[:, index * rows : (index + 1) * rows] = flat
        x_out[:, index * rows : (index + 1) * rows] = flat.astype(F32)
    project(x_out[...], mod, w_q_t, w_v_t, w_k, outs)


def head_rows(head):
    return slice(head * HEAD_DIM, (head + 1) * HEAD_DIM)


def pair_columns(head):
    return slice(head // 2 * PAIR, (head // 2 + 1) * PAIR)


def padded(rows, head):
    zeros = jnp.zeros_like(rows)
    return jnp.concatenate([rows, zeros] if head % 2 == 0 else [zeros, rows], axis=0)


def query_top(q):
    square = q[...].astype(F32)
    square = square * square
    norms = [jnp.sum(square[head_rows(head)], axis=0, keepdims=True) for head in range(HEADS)]
    return jnp.max(functools.reduce(jnp.maximum, norms), axis=1, keepdims=True)


def key_top(kn):
    first = lax.broadcasted_iota(jnp.int32, (D, LANES), 1) * HEAD_DIM
    row = lax.broadcasted_iota(jnp.int32, (D, LANES), 0)
    pick = jnp.where((row >= first) & (row < first + HEAD_DIM), 1.0, 0.0).astype(BF16)
    square = kn[...].astype(F32)
    norms = nn((square * square).astype(BF16), pick)
    return jnp.max(jnp.max(norms, axis=0, keepdims=True), axis=1, keepdims=True) * 1.02


def value_rows(vt, rows, at):
    values = vt[rows, at]
    return jnp.concatenate([values, jnp.ones((ONES, values.shape[1]), BF16)], axis=0)


def attend_plain(q, kn, vt, put):
    chunks = [slice(at, at + BLOCK) for at in range(0, kn.shape[0], BLOCK)]

    def score(head):
        return nn(kn[:, pair_columns(head)], padded(q[head_rows(head), :], head))

    totals = {}

    def finish(head, at, probs):
        term = nn(value_rows(vt, head_rows(head), at), probs)
        totals[head] = totals[head] + term if head in totals else term
        if at == chunks[-1]:
            put(head, totals[head])

    waiting = None
    following = score(0)
    for head in range(HEADS):
        scores = following
        for at in chunks:
            if at == chunks[0] and head + 1 < HEADS:
                following = score(head + 1)
            if waiting is not None:
                finish(*waiting)
            waiting = (head, at, jnp.exp(scores[at]).astype(BF16))
    finish(*waiting)


def attend_own_kernel(early, *refs):
    q, kn, vt, *refs = refs[early:]
    passing = []
    if len(refs) > 2:
        *passing, sums, tops, passed = refs
    else:
        sums, tops = refs
    at = 0
    for source in passing:
        rows = source.shape[0]
        passed[at : at + rows, :] = source[...]
        at += rows

    def put(head, total):
        sums[head] = total

    query, key = query_top(q), key_top(kn)
    tops[0:8, :] = jnp.broadcast_to(query, (8, LANES))
    tops[8:16, :] = jnp.broadcast_to(key, (8, LANES))

    @pl.when(jnp.max(query * key) < SAFE_SCORE**2)
    def _():
        attend_plain(q, kn, vt, put)


def forward_kernel(last, early, *refs):
    refs = refs[early:]
    if last:
        active, x, x_step, *refs = refs
    else:
        x, *refs = refs
    q, kn_own, kn_far, vt_own, vt_far, sums, tops, mod, w_out_t, w_up_t, w_down_t, *refs = refs
    if not last:
        mod_next, w_q_t, w_v_t, w_k, *refs = refs
    lse, mixed, attended, middle, hidden, slope, branch, *refs = refs
    if last:
        (final,) = refs
    else:
        x_next, xb_next, *next_outs = refs
    patches = x.shape[1]
    bound = tops[0:1, 0:1] * jnp.maximum(tops[8:9, 0:1], key_top(kn_far))
    safe = jnp.max(bound) < SAFE_SCORE**2

    def put(head, total):
        total = sums[head] + total
        weight = total[HEAD_DIM : HEAD_DIM + 1]
        mixed[head_rows(head), :] = (total[:HEAD_DIM] * (1.0 / weight)).astype(BF16)
        lse[head : head + 1, :] = jnp.log(weight)

    @pl.when(safe)
    def _():
        attend_plain(q, kn_far, vt_far, put)

    @pl.when(jnp.logical_not(safe))
    def _():
        def pair_heads(pair, _):
            columns = pl.ds(pl.multiple_of(pair * PAIR, PAIR), PAIR)
            for head in range(2):
                rows = pl.ds(pl.multiple_of(pair * PAIR + head * HEAD_DIM, HEAD_DIM), HEAD_DIM)
                query = padded(q[rows, :], head)
                scores = [nn(kn[:, columns], query) for kn in (kn_own, kn_far)]
                tops = [jnp.max(score, axis=0, keepdims=True) for score in scores]
                top = jnp.maximum(*tops)
                total = None
                for score, vt in zip(scores, (vt_own, vt_far)):
                    term = nn(value_rows(vt, rows, slice(None)), jnp.exp(score - top).astype(BF16))
                    total = term if total is None else total + term
                weight = total[HEAD_DIM : HEAD_DIM + 1]
                mixed[rows, :] = (total[:HEAD_DIM] * (1.0 / weight)).astype(BF16)
                lse[pl.ds(pair * 2 + head, 1), :] = top + jnp.log(weight)
            return 0

        lax.fori_loop(0, HEADS // 2, pair_heads, 0)

    att = nn(w_out_t[...], mixed[...])
    attended[...] = att.astype(BF16)
    mid = x[...] + part(mod, 2, patches) * att
    middle[...] = mid.astype(BF16)
    standard, _ = standardise(mid)
    hidden_in = (standard * (1.0 + part(mod, 4, patches)) + part(mod, 3, patches)).astype(BF16)
    chunks = [slice(at, at + BLOCK) for at in range(0, w_up_t.shape[0], BLOCK)]

    def up(place):
        wide_rows = slice(place * BLOCK, (place + 2) * BLOCK)
        both = nn(w_up_t[wide_rows, :], hidden_in)
        return [both[:BLOCK], both[BLOCK:]]

    down = None
    waiting = None
    acts = up(0)
    for place, rows in enumerate(chunks):
        act = acts[place]
        if place % 2 == 0 and place + 2 < len(chunks):
            acts += up(place + 2)
        if place > 0:
            term = nn(w_down_t[:, chunks[place - 1]], waiting)
            down = term if down is None else down + term
        act = act.astype(BF16)
        inner = GELU_A + (GELU_A * GELU_B) * (act * act)
        half = 0.5 + 0.5 * jnp.tanh(act * inner)
        waiting = gelu = act * half
        hidden[rows, :] = waiting
        slope[rows, :] = (half + (gelu - gelu * half) * (6.0 * inner - 4.0 * GELU_A))
    down = down + nn(w_down_t[:, chunks[-1]], waiting)
    branch[...] = down.astype(BF16)
    out = mid + part(mod, 5, patches) * down
    if last:
        own = final.shape[0]
        final[...] = jnp.where(active[0] > 0.0, out[:, :own], x_step[:, :own]).T
    else:
        x_next[...] = out
        xb_next[...] = out.astype(BF16)
        project(out, mod_next, w_q_t, w_v_t, w_k, next_outs)


def put_grads(left_ref, right, where, count, at, mine, other, before):
    rows = [left_ref[pl.ds(pl.multiple_of(where[place] * count, 16), count), :] for place in range(2)]
    product = nt(jnp.concatenate(rows, axis=0), right)
    for column in range(0, product.shape[1], LANES):
        low = product[:count, column : column + LANES]
        high = product[count:, column : column + LANES]
        if before is not None:
            low = low + before[0][at : at + count, :]
            high = high + before[1][at : at + count, :]
        mine[at : at + count, :] = low.astype(mine.dtype)
        other[at : at + count, :] = high.astype(other.dtype)
        at += count


def dense_back_kernel(has_close, has_open, has_before, start, layers, waits, *refs):
    refs = list(refs)

    def take(count):
        taken = refs[:count]
        del refs[:count]
        return taken

    take(waits)
    where, active = take(2)
    close_before = open_before = None
    if has_close:
        d_own, d_got, dq, d_mid_in, x_in, mod_in, w_qkv = take(7)
        w_qkv = w_qkv.at[layers[0]]
        if has_before[0]:
            close_before = take(3)
    if start == "first":
        cots = take(2)
    elif start == "cross":
        cots = take(1)
    if has_open:
        mixed, attended, middle, hidden, slope, branch, mod, w_out, w_up, w_down = take(10)
        w_out, w_up, w_down = (ref.at[layers[1]] for ref in (w_out, w_up, w_down))
        if has_before[1]:
            open_before = take(3)
    else:
        (lines,) = take(1)
    if has_close:
        close_mine, close_other, close_mods = take(3)
    if start == "first":
        (cot_out,) = take(1)
    if has_open:
        open_mine, open_other, open_mods, d_mid_out, do_out, cen_out = take(6)
    else:
        g_out, sums_out = take(2)
        sums_at = close_before[1].shape[0]
    if has_close:
        grads_scr, normed_scr = take(2)
    if has_open:
        pg_scr, hin_scr = take(2)

    patches = middle.shape[1] if has_open else x_in.shape[1]
    totals = {}

    def add_sums(name, values):
        totals[name] = totals[name] + folded(values) if name in totals else folded(values)

    def put_sums(out, before, names):
        for place, name in enumerate(names):
            rows = slice(place * D, (place + 1) * D)
            out[rows, :] = totals[name] + before[2][rows, :] if before else totals[name]

    if start == "first":
        for index, ref in enumerate(cots):
            rows = ref.shape[0]
            cot_out[:, index * rows : (index + 1) * rows] = turned(ref[...])

    def close(at):
        standard, scale = standardise(x_in[:, at].astype(F32))
        gain = 1.0 + part(mod_in, 1, patches)
        normed_scr[:, at] = (standard * gain + part(mod_in, 0, patches)).astype(BF16)
        for third in range(3):
            if third == 0:
                piece = dq[:, at]
            else:
                rows = slice((third - 1) * D, third * D)
                piece = (d_own[rows, at] + d_got[rows, at].astype(F32)).astype(BF16)
            grads_scr[third * D : (third + 1) * D, at] = piece
        back = nn(w_qkv[...], grads_scr[:, at])
        put_grads(normed_scr, grads_scr[...], where, D // 8, 0, close_mine, close_other, close_before)
        add_sums("shift_a", back)
        add_sums("scale_a", back * standard)
        g = d_mid_in[:, at] + pre_norm_back(standard, scale, back, gain)
        if start == "cross":
            g = g + (1.0 - active[0]) * cots[0][:, at].astype(F32)
        return g

    def dense(at, g):
        standard, scale = standardise(middle[:, at].astype(F32))
        gain = 1.0 + part(mod, 4, patches)
        hin_scr[:, at] = (standard * gain + part(mod, 3, patches)).astype(BF16)
        branch_grad = (part(mod, 5, patches) * g).astype(BF16)
        add_sums("gate_m", g * branch[:, at].astype(F32))
        chunks = [slice(start, start + BLOCK) for start in range(0, w_down.shape[0], BLOCK)]
        back = None
        waiting = None

        def down(place):
            wide_rows = slice(place * BLOCK, (place + 2) * BLOCK)
            both = nn(w_down[wide_rows, :], branch_grad)
            return [both[:BLOCK], both[BLOCK:]]

        hidden_grads = down(0)
        for place, rows in enumerate(chunks):
            hidden_grad = hidden_grads[place]
            if place % 2 == 0 and place + 2 < len(chunks):
                hidden_grads += down(place + 2)
            if place > 0:
                term = nn(w_up[:, chunks[place - 1]], waiting)
                back = term if back is None else back + term
            waiting = slope[rows, at] * hidden_grad.astype(BF16)
            pg_scr[rows, at] = waiting
        back = back + nn(w_up[:, chunks[-1]], waiting)
        count = w_down.shape[0] // 8
        start_at = count * (D // LANES)
        put_grads(hidden, branch_grad, where, count, 0, open_mine, open_other, open_before)
        put_grads(hin_scr, pg_scr[...], where, D // 8, start_at, open_mine, open_other, open_before)
        add_sums("shift_m", back)
        add_sums("scale_m", back * standard)
        d_mid = g + pre_norm_back(standard, scale, back, gain)
        d_mid_out[:, at] = d_mid
        att_grad = (part(mod, 2, patches) * d_mid).astype(BF16)
        mixed_grad = nn(w_out[...], att_grad).astype(BF16)
        do_out[:, at] = mixed_grad
        start_at += (w_up.shape[1] // LANES) * (D // 8)
        put_grads(mixed, att_grad, where, D // 8, start_at, open_mine, open_other, open_before)
        add_sums("gate_a", d_mid * attended[:, at].astype(F32))
        product = mixed_grad.astype(F32) * mixed[:, at].astype(F32)
        for head in range(HEADS):
            cen_out[head : head + 1, at] = jnp.sum(product[head_rows(head)], axis=0, keepdims=True)

    at = slice(0, patches)
    g = close(at) if has_close else cot_out[:, at].astype(F32) * active[0]
    if has_open:
        dense(at, g)
    else:
        g_out[...] = g[:, : g_out.shape[0]].T
    if has_close:
        put_sums(close_mods, close_before, ("shift_a", "scale_a"))
    if has_open:
        put_sums(open_mods, open_before, ("gate_a", "shift_m", "scale_m", "gate_m"))
    else:
        sums_out[...] = lines[...]
        put_lines(sums_out, 0, close_mods[...])
        close_other[sums_at:, :] = sums_out[...].astype(BF16)


def attend_back_kernel(has_before, waits, q, kn, vt, lse, d_out, centre, *refs):
    if has_before:
        before, *refs = refs
    d_kv, dq_out, kt_scr, vn_scr = refs[waits:]
    for column in range(0, D, LANES):
        kt_scr[column : column + LANES, :] = turned(kn[:, column : column + LANES])
    for column in range(0, vt.shape[1], BLOCK):
        vn_scr[column : column + BLOCK, :] = turned(vt[:, column : column + BLOCK])

    steps = [(head, slice(at, at + BLOCK)) for head in range(HEADS) for at in range(0, kn.shape[0], BLOCK)]

    def score(head, at):
        columns = pair_columns(head)
        rows = head_rows(head)
        return nn(kn[at, columns], padded(q[rows, :], head)), nn(vn_scr[at, columns], padded(d_out[rows, :], head))

    totals = {}

    def finish(head, at, probs, score_grads):
        rows = head_rows(head)
        d_kv[D + rows.start : D + rows.stop, at] = nt(d_out[rows, :], probs).astype(d_kv.dtype)
        d_kv[rows, at] = nt(q[rows, :], score_grads).astype(d_kv.dtype)
        term = nn(kt_scr[rows, at], score_grads)
        if head not in totals:
            totals[head] = before[rows, :] + term if has_before else term
            return
        term = totals[head] + term
        if has_before:
            term = term * HEAD_DIM ** (-0.5)
        dq_out[rows, :] = term.astype(dq_out.dtype)

    waiting = None
    following = score(*steps[0])
    for place, (head, at) in enumerate(steps):
        scores, prob_grads = following
        if place + 1 < len(steps):
            following = score(*steps[place + 1])
        if waiting is not None:
            finish(*waiting)
        probs = jnp.exp(scores - lse[head : head + 1, :])
        score_grads = (probs * (prob_grads - centre[head : head + 1, :])).astype(BF16)
        waiting = (head, at, probs.astype(BF16), score_grads)
    finish(*waiting)


def split_kernel(waits, where, *refs):
    *halves, keep, sent, total_scr = refs[waits:]
    rows_half = keep.shape[0]
    at = 0
    for mine, other in zip(halves[::2], halves[1::2]):
        rows = mine.shape[0]
        total_scr[at : at + rows, :] = mine[...] + other[...].astype(F32)
        at += rows
    if at < total_scr.shape[0]:
        total_scr[at:, :] = jnp.zeros((total_scr.shape[0] - at, LANES), F32)
    odd = where[3]
    keep[...] = total_scr[pl.ds(pl.multiple_of(odd * rows_half, 16), rows_half), :]
    sent[...] = total_scr[pl.ds(pl.multiple_of((1 - odd) * rows_half, 16), rows_half), :].astype(BF16)


def pair_sum_kernel(waits, *refs):
    refs = refs[waits:]
    count = len(refs) // 3
    for keep, got, out in zip(refs[:count], refs[count : 2 * count], refs[2 * count :]):
        out[...] = (keep[...].astype(F32) + got[...].astype(F32)).astype(BF16)


def put_lines(out, row, values):
    ones = jnp.ones((16, LANES), BF16)
    high = values.astype(BF16)
    low = (values - high.astype(F32)).astype(BF16)
    line = (nt(ones, high) + nt(ones, low))[0:1]
    for column in range(0, line.shape[1], LANES):
        out[row : row + 1, :] = line[:, column : column + LANES]
        row += 1
    return row


def lines_kernel(early, context, *refs):
    *sums, out = refs
    out[...] = jnp.zeros_like(out)
    row = 2 * D // LANES
    for ref in sums:
        row = put_lines(out, row, ref[...])
    for column in range(0, D, LANES):
        out[row : row + 1, :] = context[0:1, column : column + LANES].astype(F32)
        row += 1


def join_kernel(sum_count, early, mine, sums, got, out):
    rows = mine.shape[0]
    out[:rows, :] = (mine[...] + got[:rows, :].astype(F32)).astype(BF16)
    other = got[rows:, :].astype(F32)
    summed = lax.broadcasted_iota(jnp.int32, (SUM_ROWS, LANES), 0) < sum_count
    out[rows:, :] = (sums[...] + jnp.where(summed, other, 0.0)).astype(BF16)


def pair_kernel(rows, where, own, got, out):
    out[:rows, :] = (own[:rows, :].astype(F32) + got[:rows, :].astype(F32)).astype(BF16)
    odd = where[3]
    size = SUM_ROWS
    out[pl.ds(pl.multiple_of(rows + odd * size, 16), size), :] = own[rows:, :]
    out[pl.ds(pl.multiple_of(rows + (1 - odd) * size, 16), size), :] = got[rows:, :]


def gather_kernel(layer, where, own, got, *refs):
    outs, qkv_out, rows_scr, scratch, sems = refs[-9:-6], refs[-6], refs[-5], refs[-4:-1], refs[-1]
    if layer == 1:
        outs = refs[-8:-5]
    half = own.shape[0]
    rows_scr[pl.ds(pl.multiple_of(where[3] * half, 16), half), :] = own[...]
    rows_scr[pl.ds(pl.multiple_of((1 - where[3]) * half, 16), half), :] = got[...]
    at = 0
    copies = []
    for place, (out, held) in enumerate(zip(outs, scratch)):
        rows = held.shape[0]
        for column in range(0, held.shape[1], LANES):
            held[:, column : column + LANES] = rows_scr[at : at + rows, :].astype(F32)
            at += rows
        copies.append(pltpu.make_async_copy(held, out.at[layer], sems.at[place]))
        copies[-1].start()
    if layer == 0:
        rows = qkv_out.shape[0]
        for column in range(0, qkv_out.shape[1], LANES):
            qkv_out[:, column : column + LANES] = rows_scr[at : at + rows, :].astype(F32)
            at += rows
    for copy in copies:
        copy.wait()


def finish_kernel(item_count, where, own, got, qkv_1, qkv_out, ada_out, bias_out, shift_out, sum_scr, bias_scr, shift_scr):
    layers = 2
    device, high = where[0], where[4]
    slice_rows = qkv_out.shape[1]
    close_rows = slice_rows * (3 * D // LANES)
    for other in range(2):
        rows = slice(close_rows + other * SUM_ROWS, close_rows + (other + 1) * SUM_ROWS)
        sum_scr[2 * high + other] = own[rows, :].astype(F32)
        sum_scr[2 * (1 - high) + other] = got[rows, :].astype(F32)
    qkv_out[1] = qkv_1[...]
    for tile in range(3 * D // LANES):
        rows = slice(tile * slice_rows, (tile + 1) * slice_rows)
        total = own[rows, :].astype(F32) + got[rows, :].astype(F32)
        qkv_out[0, :, tile * LANES : (tile + 1) * LANES] = total
    tiles = 6 * D // LANES
    contexts = []
    for other in range(item_count):
        line = jnp.concatenate([sum_scr[other, layers * tiles + c : layers * tiles + c + 1, :] for c in range(3)], axis=1)
        contexts.append(line)
    square = jnp.concatenate(contexts + [jnp.zeros((8 - item_count, D), F32)], axis=0)
    spot = lax.broadcasted_iota(jnp.int32, (slice_rows, D), 1)
    want = lax.broadcasted_iota(jnp.int32, (slice_rows, D), 0) + device * slice_rows
    pick = jnp.where(spot == want, 1.0, 0.0).astype(BF16)
    columns = nt(pick, square.astype(BF16))
    bias_rows = bias_out.shape[1]
    for index in range(layers):
        flats = []
        for tile in range(tiles):
            row = index * tiles + tile
            total = None
            flat = None
            for other in range(item_count):
                line = sum_scr[other, row : row + 1, :]
                term = columns[:, other : other + 1] * line
                total = term if total is None else total + term
                flat = line if flat is None else flat + line
            ada_out[index, :, tile * LANES : (tile + 1) * LANES] = total
            flats.append(flat)
        flat = jnp.concatenate(flats, axis=1)
        for place in range(flat.shape[1] // bias_rows):
            bias_scr[place, index : index + 1, :] = flat[:, place * bias_rows : (place + 1) * bias_rows]
            at = 3 * D + place * slice_rows
            shift_scr[place, index : index + 1, :] = flat[:, at : at + slice_rows]
    bias_out[...] = bias_scr[device]
    shift_out[...] = shift_scr[device]


VMEM = pl.BlockSpec(memory_space=pltpu.VMEM)
SMEM = pl.BlockSpec(memory_space=pltpu.SMEM)
ANY = pl.BlockSpec(memory_space=pl.ANY)
HBM = pl.BlockSpec(memory_space=pltpu.HBM)


def layer_block(array, index):
    return pl.BlockSpec((None,) + array.shape[1:], lambda step: (index,) + (0,) * (array.ndim - 1))


def call(body, args, outs, scratch=(), flops=0, name=None, direct=0, aliases=None):
    arrays = [arg[0] if isinstance(arg, tuple) else arg for arg in args]
    specs = [arg[1] if isinstance(arg, tuple) else VMEM for arg in args]
    return pl.pallas_call(
        body,
        out_shape=[jax.ShapeDtypeStruct(shape, kind) for shape, kind in outs],
        in_specs=specs,
        out_specs=[ANY] * direct + [VMEM] * (len(outs) - direct),
        input_output_aliases=aliases or {},
        scratch_shapes=[one if not isinstance(one, tuple) else pltpu.VMEM(*one) for one in scratch],
        compiler_params=pltpu.CompilerParams(vmem_limit_bytes=VMEM_LIMIT),
        cost_estimate=pl.CostEstimate(flops=flops, bytes_accessed=0, transcendentals=0),
        name=name,
    )(*arrays)


VMEM_LIMIT = 14 * 1024 * 1024


def fast_shards(
    lat_count, lon_count, item_count,
    fields, lead_index, rollout, w_qkv, w_out, w_up, w_down, w_ada, b_ada, cotangent,
):
    _, rows_dev, cols_dev, width = fields.shape
    local = rows_dev * cols_dev
    layers = w_qkv.shape[0]
    ff = w_up.shape[2]
    patches = 4 * local
    device = lax.axis_index("lat") * lon_count + lax.axis_index("lon")
    item = lax.axis_index("item")
    where = jnp.stack([device, device ^ 1, item, item & 1, item >> 1]).astype(jnp.int32)
    active = (1 < rollout[0]).astype(F32)[None]

    def plane_flip(value, flip_lat, flip_y):
        pairs = [
            (a * lon_count + b, (a ^ flip_lat) * lon_count + (b ^ (2 * flip_y)))
            for a in range(lat_count)
            for b in range(lon_count)
        ]
        return lax.ppermute(value, ("lat", "lon"), pairs)

    def swap(value):
        return lax.ppermute(value, "lon", [(index, index ^ 1) for index in range(lon_count)])

    def with_item(value, flip):
        return lax.ppermute(value, "item", [(index, index ^ flip) for index in range(item_count)])

    def plane_parts(value):
        return [value, plane_flip(value, 1, 0), plane_flip(value, 0, 1), plane_flip(value, 1, 1)]

    field_parts = plane_parts(fields.reshape(local, width))

    context = jax.nn.silu(embedding(lead_index[0])).astype(BF16)
    context = jnp.broadcast_to(context[None, :], (16, width))
    square = (width, patches)
    natural = (patches, width)
    weights = (w_qkv, w_ada, b_ada, w_out, w_up, w_down)
    weights = [(pltpu.with_memory_space_constraint(value, pltpu.HBM), HBM) for value in weights]
    first_outs = [((6 * width, LANES), F32)] + [((width, width), BF16)] * 3
    rest_outs = [((width, width), BF16), ((ff, width), BF16), ((width, ff), BF16)]
    first_fetch = [((width, 3 * width), BF16), ((width, 6 * width), BF16)]
    rest_fetch = [((width, width), BF16), ((width, ff), BF16), ((ff, width), BF16)]
    prepared = call(
        prepare_kernel,
        [context, *weights, (where, SMEM), (active, SMEM)],
        first_outs * 2 + rest_outs,
        first_fetch + [(b_ada.shape, F32)] + rest_fetch + first_fetch + [pltpu.SemaphoreType.DMA((8,))],
        name="prepare",
    )
    first_parts = [prepared[0:4], prepared[4:8]]
    rest_parts = [prepared[8:11]]
    mods = [one[0] for one in first_parts]

    project_outs = [(square, F32), (square, BF16), (square, BF16), (natural, BF16), (square, BF16)]
    dense_flops = 2 * patches * (width * 3 * width + width * width + 2 * width * ff)
    score_flops = 2 * patches * 2 * patches * width * 4
    x, xb, *projected = call(
        first_kernel,
        [*field_parts, *first_parts[0]],
        project_outs,
        flops=2 * patches * width * 4 * width,
        name="first",
    )
    saved = []
    for step in range(STEPS):
        for index in range(layers):
            q, kn, vt = projected
            if len(rest_parts) == index:
                rest_parts.append(
                    call(
                        functools.partial(prepare_rest_kernel, index),
                        [(kn, ANY), w_out, w_up, w_down],
                        rest_outs,
                        name="prepare_rest",
                    )
                )
            kn_far, vt_far = swap(kn), swap(vt)
            early = [w_up] if len(rest_parts) == index + 1 < layers else []
            passing = []
            if step == STEPS - 1:
                passing = [cotangent.reshape(local, width)] if index == 0 else cot_parts
            passed = [((len(passing) * local, width), BF16)] if passing else []
            sums, tops, *passed = call(
                functools.partial(attend_own_kernel, len(early)),
                early + [q, kn, vt] + passing,
                [((HEADS, HEAD_DIM + ONES, patches), F32), ((16, LANES), F32)] + passed,
                flops=10 * score_flops,
                name="forward_own",
            )
            if passed:
                cot_parts = [passed[0], plane_flip(passed[0], 1 - index, index)]
            last = step == STEPS - 1 and index == layers - 1
            if index == 0 and step > 0:
                x_step = x
            following = list(first_parts[(index + 1) % layers])
            early = [w_down] if len(rest_parts) == index + 1 < layers else []
            lse, mixed, attended, middle, hidden, slope, branch, *results = call(
                functools.partial(forward_kernel, last, len(early)),
                early
                + ([(active, SMEM), x, x_step] if last else [x])
                + [q, kn, kn_far, vt, vt_far, sums, tops, mods[index], *rest_parts[index]]
                + ([] if last else following),
                [
                    ((HEADS, patches), F32),
                    (square, BF16),
                    (square, BF16),
                    (square, BF16),
                    ((ff, patches), BF16),
                    ((ff, patches), BF16),
                    (square, BF16),
                ]
                + ([((local, width), F32)] if last else project_outs),
                flops=dense_flops + 2 * score_flops,
                name="forward",
            )
            saved.append((xb, [mixed, attended, middle, hidden, slope, branch], (q, kn, kn_far, vt, vt_far, lse)))
            if last:
                final = results[0]
            else:
                x, xb, *projected = results

    slice_rows = width // 8
    open_rows = 2 * (ff // 8) * (width // LANES) + slice_rows * (width // LANES)
    close_rows = slice_rows * (3 * width // LANES)
    order = [(step, index) for step in reversed(range(STEPS)) for index in reversed(range(layers))]
    open_done = [None] * layers
    close_done = [None] * layers
    pending = None
    for place in range(len(order) + 1):
        has_close = pending is not None
        has_open = place < len(order)
        use = [order[place - 1][1], order[place][1] if has_open else 0]
        waits = []
        if has_close and close_done[use[0]]:
            waits = [pair_1] if has_open else [item_got_1]
        args = [(value, ANY) for value in waits] + [(where, SMEM), (active, SMEM)]
        outs = []
        scratch = []
        has_before = [False, False]
        start = ""
        if has_close:
            args += pending
            if close_done[use[0]] is not None:
                has_before[0] = True
                args += close_done[use[0]]
            outs += [((close_rows, LANES), F32)]
            sent_rows = close_rows + (0 if has_open else SUM_ROWS)
            outs += [((sent_rows, LANES), BF16 if has_before[0] else F32), ((2 * width, LANES), F32)]
            scratch += [((3 * width, patches), BF16), (square, BF16)]
        if place == 0:
            start = "first"
            args += cot_parts
            outs += [(square, BF16)]
        elif has_open and order[place][0] != order[place - 1][0]:
            start = "cross"
            args += [cot_t]
        if has_open:
            step, index = order[place]
            xb, kept, heads = saved[step * layers + index]
            args += kept + [mods[index], w_out, w_up, w_down]
            if open_done[index] is not None:
                has_before[1] = True
                args += open_done[index]
            outs += [
                ((open_rows, LANES), F32),
                ((open_rows, LANES), BF16 if has_before[1] else F32),
                ((4 * width, LANES), F32),
                (square, F32),
                (square, BF16),
                ((HEADS, patches), F32),
            ]
            scratch += [((ff, patches), BF16), (square, BF16)]
        else:
            args += [lines]
            outs += [((local, width), F32), ((SUM_ROWS, LANES), F32)]
        results = list(
            call(
                functools.partial(dense_back_kernel, has_close, has_open, has_before, start, use, len(waits)),
                args,
                outs,
                scratch,
                flops=2 * dense_flops if has_open else 0,
                name="dense_back" if has_open else "close_back",
            )
        )
        if has_close:
            close_done[use[0]] = results[:3]
            del results[:3]
        if start == "first":
            cot_t = results.pop(0)
        if not has_open:
            gradient, line = results
            break
        open_done[index] = results[:3]
        d_mid, d_out, centre = results[3:]
        q, kn, kn_far, vt, vt_far, lse = heads
        halves = [open_done[index][0], open_done[index][1]]
        if index == 0:
            halves += [close_done[1][0], close_done[1][1]]
        half_rows = -(-sum(half.shape[0] for half in halves[::2]) // 32) * 16

        def split(waits):
            pieces = [half if place % 2 == 0 else swap(half) for place, half in enumerate(halves)]
            return call(
                functools.partial(split_kernel, len(waits)),
                [(where, SMEM), *waits, *pieces],
                [((half_rows, LANES), F32), ((half_rows, LANES), BF16)],
                [((2 * half_rows, LANES), F32)],
                name="split",
            )

        def pair_sum(late, keeps, gots, others=()):
            outs = [(keep.shape, BF16) for keep in keeps]
            body = functools.partial(pair_sum_kernel, 1 + len(others))
            return call(body, [(late, ANY), *others, *keeps, *gots], outs, name="pair_sum")

        waits = []
        if has_before[1] and index == 0:
            pair_got_1 = with_item(pair_1, 2)
            lines = call(
                lines_kernel,
                [(pair_got_1, ANY), context, open_done[0][2], close_done[1][2], open_done[1][2]],
                [((SUM_ROWS, LANES), F32)],
                flops=10 * score_flops,
                name="lines",
            )[0]
            keep, sent = split([(lines, ANY)])
            got_0 = with_item(sent, 1)
            waits = [keep]
        d_far, dq = call(
            functools.partial(attend_back_kernel, False, len(waits)),
            [q, kn_far, vt_far, lse, d_out, centre] + [(value, ANY) for value in waits],
            [((2 * width, patches), BF16), (square, F32)],
            [(square, BF16), (natural, BF16)],
            flops=10 * score_flops,
            name="attend_far",
        )
        d_got = swap(d_far)
        waits = []
        if has_before[1]:
            if index == 1:
                keep, sent = split([(d_far, ANY)])
                got_1 = with_item(sent, 1)
                waits = [keep]
            else:
                (item_1,) = pair_sum(d_far, [pair_1], [pair_got_1])
                item_got_1 = with_item(item_1, 1)
                (pair_0,) = pair_sum(d_far, [keep], [got_0], [(item_1, ANY)])
                pair_got_0 = with_item(pair_0, 2)
                waits = [pair_0]
        d_own, dq = call(
            functools.partial(attend_back_kernel, True, len(waits)),
            [q, kn, vt, lse, d_out, centre, dq] + [(value, ANY) for value in waits],
            [((2 * width, patches), F32), (square, BF16)],
            [(square, BF16), (natural, BF16)],
            flops=10 * score_flops,
            name="attend_own",
        )
        if has_before[1] and index == 1:
            (pair_1,) = pair_sum(dq, [keep], [got_1])
        pending = [d_own, d_got, dq, d_mid, xb, mods[index], w_qkv]

    message = call(
        functools.partial(join_kernel, layers * 6 * width // LANES),
        [(pair_got_0, ANY), close_done[0][0], line, swap(close_done[0][1])],
        [((close_rows + SUM_ROWS, LANES), BF16)],
        name="join",
    )[0]
    message_got = with_item(message, 1)
    stacks = [
        ((layers, ff // 8, width), F32),
        ((layers, slice_rows, ff), F32),
        ((layers, slice_rows, width), F32),
    ]
    held = [(shape[1:], kind) for shape, kind in stacks]
    sems = [pltpu.SemaphoreType.DMA((3,))]
    stacked = call(
        functools.partial(gather_kernel, 1),
        [(where, SMEM), item_1, item_got_1],
        stacks,
        [((2 * pair_1.shape[0], LANES), BF16)] + held + sems,
        name="gather",
        direct=3,
    )
    early = (pltpu.with_memory_space_constraint(stacked[2], pltpu.HBM), HBM)
    (item_0,) = pair_sum(message_got, [pair_0], [pair_got_0], [early])
    message = call(
        functools.partial(pair_kernel, close_rows),
        [(where, SMEM), message, message_got],
        [((close_rows + 2 * SUM_ROWS, LANES), BF16)],
        name="pair",
    )[0]
    down_grad, up_grad, out_grad, qkv_1 = call(
        functools.partial(gather_kernel, 0),
        [(where, SMEM), item_0, with_item(item_0, 1)] + [(value, ANY) for value in stacked],
        stacks + [((slice_rows, 3 * width), F32)],
        [((2 * pair_0.shape[0], LANES), BF16)] + held + sems,
        name="gather",
        direct=3,
        aliases={3: 0, 4: 1, 5: 2},
    )
    bias_rows = 6 * width // 8
    qkv_grad, ada_grad, bias_grad, shift_grad = call(
        functools.partial(finish_kernel, item_count),
        [(where, SMEM), message, with_item(message, 2), qkv_1],
        [
            ((layers, slice_rows, 3 * width), F32),
            ((layers, slice_rows, 6 * width), F32),
            ((layers, bias_rows), F32),
            ((layers, slice_rows), F32),
        ],
        [
            ((item_count, SUM_ROWS, LANES), F32),
            ((8, layers, bias_rows), F32),
            ((8, layers, slice_rows), F32),
        ],
        name="finish",
    )
    field_shape = (1, rows_dev, cols_dev, width)
    return (
        final.reshape(field_shape),
        gradient.reshape(field_shape),
        qkv_grad,
        out_grad,
        up_grad,
        down_grad,
        ada_grad,
        bias_grad,
        shift_grad,
    )


def solution(mesh):
    lat_count, lon_count, item_count = mesh.shape["lat"], mesh.shape["lon"], mesh.shape["item"]
    if lat_count == 2 and lon_count == 4:
        body = functools.partial(fast_shards, lat_count, lon_count, item_count)
    else:
        body = shards
    return jax.shard_map(
        body,
        mesh=mesh,
        in_specs=(
            P("item", "lat", "lon", None),
            P("item"),
            P("item"),
            P(),
            P(),
            P(),
            P(),
            P(),
            P(),
            P("item", "lat", "lon", None),
        ),
        out_specs=(
            P("item", "lat", "lon", None),
            P("item", "lat", "lon", None),
            P(None, ("lat", "lon"), None),
            P(None, ("lat", "lon"), None),
            P(None, ("lat", "lon"), None),
            P(None, ("lat", "lon"), None),
            P(None, ("lat", "lon"), None),
            P(None, ("lat", "lon")),
            P(None, ("lat", "lon")),
        ),
        check_vma=False,
    )
```

```python
import functools
import math

import jax
import jax.numpy as jnp
from jax import lax
from jax.experimental import pallas as pl
from jax.experimental.pallas import tpu as pltpu
from jax.sharding import PartitionSpec as P

D = 384
HEADS = 6
HEAD_DIM = 64
STEPS = 2


def shortened(shard):
    return jax.tree.map(lambda a: a.astype(jnp.bfloat16) if a.dtype == jnp.float32 else a, shard)


def embedding(lead):
    half_width = D // 2
    lead_hours = 6.0 * (lead.astype(jnp.float32) + 1.0)
    frequencies = jnp.exp(
        -math.log(10000.0) * jnp.arange(half_width, dtype=jnp.float32) / half_width
    )
    angles = lead_hours * frequencies
    return jnp.concatenate([jnp.sin(angles), jnp.cos(angles)])


def pre_norm(values, shift_part, scale_part):
    centred = values - jnp.mean(values, axis=-1, keepdims=True)
    variance = jnp.mean(centred * centred, axis=-1, keepdims=True)
    return centred * lax.rsqrt(variance + 1e-06) * (1.0 + scale_part) + shift_part


def gather_keys(keys_values):
    band_rows = lax.all_gather(keys_values, "lon", axis=0, tiled=True)
    return lax.all_gather(band_rows, "lat", axis=0, tiled=True)


def spread_keys(key_value_grads):
    band_grads = lax.psum_scatter(
        key_value_grads.astype(jnp.bfloat16), "lat", scatter_dimension=0, tiled=True
    )
    return lax.psum_scatter(band_grads, "lon", scatter_dimension=0, tiled=True).astype(jnp.float32)


def forward_layer(current, modulation, weight_qkv, weight_out, weight_up, weight_down):
    local_rows, width = current.shape
    shift_attn, scale_attn, gate_attn, shift_mlp, scale_mlp, gate_mlp = modulation
    normed = pre_norm(current, shift_attn, scale_attn).astype(jnp.bfloat16)
    projected = jnp.dot(normed, weight_qkv, preferred_element_type=jnp.float32).astype(jnp.bfloat16)
    queries = projected[:, :width].reshape(local_rows, HEADS, HEAD_DIM)
    own_keys = projected[:, width:]
    gathered = gather_keys(own_keys)
    total_rows = gathered.shape[0]
    key_heads = gathered[:, :width].reshape(total_rows, HEADS, HEAD_DIM)
    value_heads = gathered[:, width:].reshape(total_rows, HEADS, HEAD_DIM)
    scores = jnp.einsum(
        "thd,nhd->htn", queries, key_heads, preferred_element_type=jnp.float32
    ) * HEAD_DIM ** (-0.5)
    log_total = jax.nn.logsumexp(scores, axis=-1, keepdims=True)
    probabilities = jnp.exp(scores - log_total).astype(jnp.bfloat16)
    mixed = jnp.einsum(
        "htn,nhd->thd", probabilities, value_heads, preferred_element_type=jnp.float32
    )
    mixed = mixed.reshape(local_rows, width).astype(jnp.bfloat16)
    attended = jnp.dot(mixed, weight_out, preferred_element_type=jnp.float32)
    middle = current + gate_attn * attended
    hidden_in = pre_norm(middle, shift_mlp, scale_mlp).astype(jnp.bfloat16)
    pre_act = jnp.dot(hidden_in, weight_up, preferred_element_type=jnp.float32)
    hidden = jax.nn.gelu(pre_act).astype(jnp.bfloat16)
    branch = jnp.dot(hidden, weight_down, preferred_element_type=jnp.float32)
    output = middle + gate_mlp * branch
    kept = (
        current,
        normed,
        queries,
        gathered,
        own_keys,
        log_total,
        mixed,
        attended,
        middle,
        hidden_in,
        pre_act,
        hidden,
        branch,
    )
    return (output, kept)


def backward_layer(grad_out, kept, modulation, weight_qkv, weight_out, weight_up, weight_down):
    (
        current,
        normed,
        queries,
        gathered,
        own_keys,
        log_total,
        mixed,
        attended,
        middle,
        hidden_in,
        pre_act,
        hidden,
        branch,
    ) = kept
    local_rows, width = current.shape
    total_rows = gathered.shape[0]
    shift_attn, scale_attn, gate_attn, shift_mlp, scale_mlp, gate_mlp = modulation
    factor = HEAD_DIM ** (-0.5)
    branch_grad = (gate_mlp * grad_out).astype(jnp.bfloat16)
    gate_mlp_grad = jnp.sum(grad_out * branch, axis=0)
    hidden_grad = jnp.dot(branch_grad, weight_down.T, preferred_element_type=jnp.float32)
    down_grad = jnp.dot(hidden.T, branch_grad, preferred_element_type=jnp.float32)
    _, gelu_back = jax.vjp(jax.nn.gelu, pre_act)
    pre_grad = gelu_back(hidden_grad)[0].astype(jnp.bfloat16)
    hidden_in_grad = jnp.dot(pre_grad, weight_up.T, preferred_element_type=jnp.float32)
    up_grad = jnp.dot(hidden_in.T, pre_grad, preferred_element_type=jnp.float32)
    _, second_back = jax.vjp(pre_norm, middle, shift_mlp, scale_mlp)
    middle_part, shift_mlp_grad, scale_mlp_grad = second_back(hidden_in_grad)
    middle_grad = grad_out + middle_part
    attended_grad = (gate_attn * middle_grad).astype(jnp.bfloat16)
    gate_attn_grad = jnp.sum(middle_grad * attended, axis=0)
    mixed_grad = jnp.dot(attended_grad, weight_out.T, preferred_element_type=jnp.float32).astype(
        jnp.bfloat16
    )
    out_grad = jnp.dot(mixed.T, attended_grad, preferred_element_type=jnp.float32)
    mixed_heads = mixed_grad.reshape(local_rows, HEADS, HEAD_DIM)
    key_heads = gathered[:, :width].reshape(total_rows, HEADS, HEAD_DIM)
    value_heads = gathered[:, width:].reshape(total_rows, HEADS, HEAD_DIM)
    scores = (
        jnp.einsum("thd,nhd->htn", queries, key_heads, preferred_element_type=jnp.float32) * factor
    )
    probabilities = jnp.exp(scores - log_total)
    prob_grads = jnp.einsum(
        "thd,nhd->htn", mixed_heads, value_heads, preferred_element_type=jnp.float32
    )
    centre = jnp.sum(prob_grads * probabilities, axis=-1, keepdims=True)
    score_grads = (probabilities * (prob_grads - centre)).astype(jnp.bfloat16)
    query_grads = (
        jnp.einsum("htn,nhd->thd", score_grads, key_heads, preferred_element_type=jnp.float32)
        * factor
    )
    value_grads = jnp.einsum(
        "htn,thd->nhd",
        probabilities.astype(jnp.bfloat16),
        mixed_heads,
        preferred_element_type=jnp.float32,
    )
    key_grads = (
        jnp.einsum("htn,thd->nhd", score_grads, queries, preferred_element_type=jnp.float32)
        * factor
    )
    key_value_grads = jnp.concatenate(
        [key_grads.reshape(total_rows, width), value_grads.reshape(total_rows, width)], axis=1
    )
    local_grads = spread_keys(key_value_grads)
    projected_grad = jnp.concatenate(
        [query_grads.reshape(local_rows, width), local_grads], axis=1
    ).astype(jnp.bfloat16)
    normed_grad = jnp.dot(projected_grad, weight_qkv.T, preferred_element_type=jnp.float32)
    qkv_grad = jnp.dot(normed.T, projected_grad, preferred_element_type=jnp.float32)
    _, first_back = jax.vjp(pre_norm, current, shift_attn, scale_attn)
    current_part, shift_attn_grad, scale_attn_grad = first_back(normed_grad)
    input_grad = middle_grad + current_part
    modulation_grad = jnp.concatenate(
        [
            shift_attn_grad,
            scale_attn_grad,
            gate_attn_grad,
            shift_mlp_grad,
            scale_mlp_grad,
            gate_mlp_grad,
        ]
    )
    return (input_grad, (qkv_grad, out_grad, up_grad, down_grad, modulation_grad))


def shards(fields, lead_index, rollout, w_qkv, w_out, w_up, w_down, w_ada, b_ada, cotangent):
    _, rows_dev, cols_dev, width = fields.shape
    local_rows = rows_dev * cols_dev
    layer_count = w_qkv.shape[0]
    context = jax.nn.silu(embedding(lead_index[0])).astype(jnp.bfloat16)
    context_wide = context.astype(jnp.float32)
    modulations = [
        (
            jnp.dot(context[None, :], w_ada[index], preferred_element_type=jnp.float32)[0]
            + b_ada[index]
        ).reshape(6, width)
        for index in range(layer_count)
    ]
    weight_sets = [
        (w_qkv[index], w_out[index], w_up[index], w_down[index]) for index in range(layer_count)
    ]
    count = rollout[0]
    current = fields.reshape(local_rows, width).astype(jnp.float32)
    saved = []
    for rollout_step in range(STEPS):
        updated = current
        kept_layers = []
        for index in range(layer_count):
            updated, kept = forward_layer(updated, modulations[index], *weight_sets[index])
            kept_layers.append(kept)
        current = jnp.where(rollout_step < count, updated, current)
        saved.append(kept_layers)
    gradient = cotangent.reshape(local_rows, width).astype(jnp.float32)
    summed = None
    shares = None
    for rollout_step in reversed(range(STEPS)):
        active = (rollout_step < count).astype(jnp.float32)
        inner = gradient * active
        layer_terms = [None] * layer_count
        for index in reversed(range(layer_count)):
            inner, layer_terms[index] = backward_layer(
                inner, saved[rollout_step][index], modulations[index], *weight_sets[index]
            )
        gradient = inner + (1.0 - active) * gradient
        modulation_grads = jnp.stack([terms[4] for terms in layer_terms])
        step_terms = (
            jnp.stack([terms[0] for terms in layer_terms]),
            jnp.stack([terms[1] for terms in layer_terms]),
            jnp.stack([terms[2] for terms in layer_terms]),
            jnp.stack([terms[3] for terms in layer_terms]),
            context_wide[None, :, None] * modulation_grads[:, None, :],
            modulation_grads,
            modulation_grads[:, 3 * width : 4 * width],
        )
        summed = step_terms if summed is None else jax.tree.map(jnp.add, summed, step_terms)
    shares = lax.psum_scatter(summed, ("lat", "lon"), scatter_dimension=1, tiled=True)
    totals = jax.tree.map(
        lambda part: part.astype(jnp.float32), lax.psum(shortened(shares), "item")
    )
    return (
        current.reshape(1, rows_dev, cols_dev, width),
        gradient.reshape(1, rows_dev, cols_dev, width),
        totals[0],
        totals[1],
        totals[2],
        totals[3],
        totals[4],
        totals[5],
        totals[6],
    )


F32 = jnp.float32
BF16 = jnp.bfloat16
GELU_A = math.sqrt(2.0 / math.pi)
GELU_B = 0.044715
LANES = 128
BLOCK = 256
PAIR = 2 * HEAD_DIM
SUM_ROWS = 48
ONES = 16
SAFE_SCORE = 60.0


def nn(left, right, precision=None):
    return lax.dot_general(
        left, right, (((1,), (0,)), ((), ())), preferred_element_type=F32, precision=precision
    )


def nt(left, right, precision=None):
    return lax.dot_general(
        left, right, (((1,), (1,)), ((), ())), preferred_element_type=F32, precision=precision
    )


def identity(size):
    rows = lax.broadcasted_iota(jnp.int32, (size, size), 0)
    columns = lax.broadcasted_iota(jnp.int32, (size, size), 1)
    return jnp.where(rows == columns, 1.0, 0.0).astype(BF16)


def turned(values):
    return nt(identity(values.shape[1]), values).astype(BF16)


def wide(column_tile, lanes):
    return jnp.concatenate([column_tile] * (lanes // LANES), axis=1)


def folded(values):
    pieces = [values[:, at : at + LANES] for at in range(0, values.shape[1], LANES)]
    return sum(pieces[1:], pieces[0])


def standardise(values):
    rows = values.shape[0]
    centred = values - jnp.sum(values, axis=0, keepdims=True) * (1.0 / rows)
    variance = jnp.sum(centred * centred, axis=0, keepdims=True) * (1.0 / rows)
    scale = lax.rsqrt(variance + 1e-06)
    return centred * scale, scale


def pre_norm_back(standard, scale, grad, gain):
    rows = standard.shape[0]
    inner = grad * gain
    first = jnp.sum(inner, axis=0, keepdims=True) * (1.0 / rows)
    second = jnp.sum(inner * standard, axis=0, keepdims=True) * (1.0 / rows)
    return scale * (inner - first - standard * second)


def part(mod_ref, index, lanes):
    return wide(mod_ref[index * D : (index + 1) * D, :], lanes)


def turn_into(source, out, at=0):
    for column in range(0, out.shape[0], BLOCK):
        width = min(BLOCK, out.shape[0] - column)
        out[column : column + width, :] = turned(source[:, at + column : at + column + width])


def prepare_first(mod, w_q_t, w_v_t, w_k, w_qkv, w_ada, b_ada, context):
    w_k[...] = w_qkv[:, D : 2 * D]
    turn_into(w_qkv, w_q_t)
    turn_into(w_qkv, w_v_t, 2 * D)
    values = nn(context[...], w_ada[...])[0:1] + b_ada
    for column in range(0, values.shape[1], LANES):
        tile = jnp.broadcast_to(values[:, column : column + LANES], (LANES, LANES))
        mod[column : column + LANES, :] = tile.T


def prepare_kernel(context, *refs):
    w_qkv, w_ada, b_ada, w_out, w_up, w_down = refs[:6]
    outs, scratch, sems = refs[8:19], refs[19:-1], refs[-1]
    sources = [w_qkv.at[0], w_ada.at[0], b_ada, w_out.at[0], w_up.at[0], w_down.at[0], w_qkv.at[1], w_ada.at[1]]
    copies = [
        pltpu.make_async_copy(source, target, sems.at[place])
        for place, (source, target) in enumerate(zip(sources, scratch))
    ]
    for copy in copies:
        copy.start()
    for copy in copies[:3]:
        copy.wait()
    prepare_first(*outs[0:4], scratch[0], scratch[1], scratch[2][0:1, :], context)
    for copy, source, out in zip(copies[3:6], scratch[3:6], outs[8:11]):
        copy.wait()
        turn_into(source, out)
    for copy in copies[6:]:
        copy.wait()
    prepare_first(*outs[4:8], scratch[6], scratch[7], scratch[2][1:2, :], context)


def prepare_rest_kernel(index, early, w_out, w_up, w_down, *outs):
    for weight, out in zip((w_out, w_up, w_down), outs):
        turn_into(weight.at[index], out)


def project(x, mod_ref, w_q_t, w_v_t, w_k, outs):
    q_out, kn_out, vt_out = outs
    lanes = x.shape[1]
    standard, _ = standardise(x)
    normed = (standard * (1.0 + part(mod_ref, 1, lanes)) + part(mod_ref, 0, lanes)).astype(BF16)
    vt_out[...] = nn(w_v_t[...], normed).astype(BF16)
    q_out[...] = (nn(w_q_t[...], normed) * HEAD_DIM ** (-0.5)).astype(BF16)
    for at in range(0, lanes, BLOCK):
        kn_out[at : at + BLOCK, :] = nn(turned(normed[:, at : at + BLOCK]), w_k[...]).astype(BF16)


def first_kernel(own, flip_x, flip_y, flip_xy, cot, cot_x, mod, w_q_t, w_v_t, w_k, cot_out, x_out, xb_out, *outs):
    rows = cot.shape[0]
    cot_out[:rows, :] = cot[...]
    cot_out[rows:, :] = cot_x[...]
    for index, ref in enumerate((own, flip_x, flip_y, flip_xy)):
        rows = ref.shape[0]
        flat = turned(ref[...])
        xb_out[:, index * rows : (index + 1) * rows] = flat
        x_out[:, index * rows : (index + 1) * rows] = flat.astype(F32)
    project(x_out[...], mod, w_q_t, w_v_t, w_k, outs)


def head_rows(head):
    return slice(head * HEAD_DIM, (head + 1) * HEAD_DIM)


def pair_columns(head):
    return slice(head // 2 * PAIR, (head // 2 + 1) * PAIR)


def padded(rows, head):
    zeros = jnp.zeros_like(rows)
    return jnp.concatenate([rows, zeros] if head % 2 == 0 else [zeros, rows], axis=0)


def query_top(q):
    square = q[...].astype(F32)
    square = square * square
    norms = [jnp.sum(square[head_rows(head)], axis=0, keepdims=True) for head in range(HEADS)]
    return jnp.max(functools.reduce(jnp.maximum, norms), axis=1, keepdims=True)


def key_top(kn):
    first = lax.broadcasted_iota(jnp.int32, (D, LANES), 1) * HEAD_DIM
    row = lax.broadcasted_iota(jnp.int32, (D, LANES), 0)
    pick = jnp.where((row >= first) & (row < first + HEAD_DIM), 1.0, 0.0).astype(BF16)
    square = kn[...].astype(F32)
    norms = nn((square * square).astype(BF16), pick)
    return jnp.max(jnp.max(norms, axis=0, keepdims=True), axis=1, keepdims=True) * 1.02


def value_rows(vt, rows, at):
    values = vt[rows, at]
    return jnp.concatenate([values, jnp.ones((ONES, values.shape[1]), BF16)], axis=0)


def attend_plain(q, kn, vt, put):
    chunks = [slice(at, at + BLOCK) for at in range(0, kn.shape[0], BLOCK)]

    def score(head):
        return nn(kn[:, pair_columns(head)], padded(q[head_rows(head), :], head))

    totals = {}

    def finish(head, at, probs):
        term = nn(value_rows(vt, head_rows(head), at), probs)
        totals[head] = totals[head] + term if head in totals else term
        if at == chunks[-1]:
            put(head, totals[head])

    waiting = None
    following = score(0)
    for head in range(HEADS):
        scores = following
        for at in chunks:
            if at == chunks[0] and head + 1 < HEADS:
                following = score(head + 1)
            if waiting is not None:
                finish(*waiting)
            waiting = (head, at, jnp.exp(scores[at]).astype(BF16))
    finish(*waiting)


def attend_own_kernel(early, *refs):
    q, kn, vt, *refs = refs[early:]
    passing = []
    if len(refs) > 2:
        *passing, sums, tops, passed = refs
    else:
        sums, tops = refs
    at = 0
    for source in passing:
        rows = source.shape[0]
        passed[at : at + rows, :] = source[...]
        at += rows

    def put(head, total):
        sums[head] = total

    query, key = query_top(q), key_top(kn)
    tops[0:8, :] = jnp.broadcast_to(query, (8, LANES))
    tops[8:16, :] = jnp.broadcast_to(key, (8, LANES))

    @pl.when(jnp.max(query * key) < SAFE_SCORE**2)
    def _():
        attend_plain(q, kn, vt, put)


def forward_kernel(last, early, *refs):
    refs = refs[early:]
    if last:
        active, x, x_step, *refs = refs
    else:
        x, *refs = refs
    q, kn_own, kn_far, vt_own, vt_far, sums, tops, mod, w_out_t, w_up_t, w_down_t, *refs = refs
    if not last:
        mod_next, w_q_t, w_v_t, w_k, *refs = refs
    lse, mixed, attended, middle, hidden, slope, branch, *refs = refs
    if last:
        (final,) = refs
    else:
        x_next, xb_next, *next_outs = refs
    patches = x.shape[1]
    bound = tops[0:1, 0:1] * jnp.maximum(tops[8:9, 0:1], key_top(kn_far))
    safe = jnp.max(bound) < SAFE_SCORE**2

    def put(head, total):
        total = sums[head] + total
        weight = total[HEAD_DIM : HEAD_DIM + 1]
        mixed[head_rows(head), :] = (total[:HEAD_DIM] * (1.0 / weight)).astype(BF16)
        lse[head : head + 1, :] = jnp.log(weight)

    @pl.when(safe)
    def _():
        attend_plain(q, kn_far, vt_far, put)

    @pl.when(jnp.logical_not(safe))
    def _():
        def pair_heads(pair, _):
            columns = pl.ds(pl.multiple_of(pair * PAIR, PAIR), PAIR)
            for head in range(2):
                rows = pl.ds(pl.multiple_of(pair * PAIR + head * HEAD_DIM, HEAD_DIM), HEAD_DIM)
                query = padded(q[rows, :], head)
                scores = [nn(kn[:, columns], query) for kn in (kn_own, kn_far)]
                tops = [jnp.max(score, axis=0, keepdims=True) for score in scores]
                top = jnp.maximum(*tops)
                total = None
                for score, vt in zip(scores, (vt_own, vt_far)):
                    term = nn(value_rows(vt, rows, slice(None)), jnp.exp(score - top).astype(BF16))
                    total = term if total is None else total + term
                weight = total[HEAD_DIM : HEAD_DIM + 1]
                mixed[rows, :] = (total[:HEAD_DIM] * (1.0 / weight)).astype(BF16)
                lse[pl.ds(pair * 2 + head, 1), :] = top + jnp.log(weight)
            return 0

        lax.fori_loop(0, HEADS // 2, pair_heads, 0)

    att = nn(w_out_t[...], mixed[...])
    attended[...] = att.astype(BF16)
    mid = x[...] + part(mod, 2, patches) * att
    middle[...] = mid.astype(BF16)
    standard, _ = standardise(mid)
    hidden_in = (standard * (1.0 + part(mod, 4, patches)) + part(mod, 3, patches)).astype(BF16)
    chunks = [slice(at, at + BLOCK) for at in range(0, w_up_t.shape[0], BLOCK)]

    def up(place):
        wide_rows = slice(place * BLOCK, (place + 2) * BLOCK)
        both = nn(w_up_t[wide_rows, :], hidden_in)
        return [both[:BLOCK], both[BLOCK:]]

    down = None
    waiting = None
    acts = up(0)
    for place, rows in enumerate(chunks):
        act = acts[place]
        if place % 2 == 0 and place + 2 < len(chunks):
            acts += up(place + 2)
        if place > 0:
            term = nn(w_down_t[:, chunks[place - 1]], waiting)
            down = term if down is None else down + term
        act = act.astype(BF16)
        inner = GELU_A + (GELU_A * GELU_B) * (act * act)
        half = 0.5 + 0.5 * jnp.tanh(act * inner)
        waiting = gelu = act * half
        hidden[rows, :] = waiting
        slope[rows, :] = (half + (gelu - gelu * half) * (6.0 * inner - 4.0 * GELU_A))
    down = down + nn(w_down_t[:, chunks[-1]], waiting)
    branch[...] = down.astype(BF16)
    out = mid + part(mod, 5, patches) * down
    if last:
        own = final.shape[0]
        final[...] = jnp.where(active[0] > 0.0, out[:, :own], x_step[:, :own]).T
    else:
        x_next[...] = out
        xb_next[...] = out.astype(BF16)
        project(out, mod_next, w_q_t, w_v_t, w_k, next_outs)


def put_grads(left_ref, right, where, count, at, mine, other, before):
    rows = [left_ref[pl.ds(pl.multiple_of(where[place] * count, 16), count), :] for place in range(2)]
    product = nt(jnp.concatenate(rows, axis=0), right)
    for column in range(0, product.shape[1], LANES):
        low = product[:count, column : column + LANES]
        high = product[count:, column : column + LANES]
        if before is not None:
            low = low + before[0][at : at + count, :]
            high = high + before[1][at : at + count, :]
        mine[at : at + count, :] = low.astype(mine.dtype)
        other[at : at + count, :] = high.astype(other.dtype)
        at += count


def dense_back_kernel(has_close, has_open, has_before, start, layers, waits, *refs):
    refs = list(refs)

    def take(count):
        taken = refs[:count]
        del refs[:count]
        return taken

    take(waits)
    where, active = take(2)
    close_before = open_before = None
    if has_close:
        d_own, d_got, dq, d_mid_in, x_in, mod_in, w_qkv = take(7)
        w_qkv = w_qkv.at[layers[0]]
        if has_before[0]:
            close_before = take(3)
    if start == "first":
        cots = take(2)
    elif start == "cross":
        cots = take(1)
    if has_open:
        mixed, attended, middle, hidden, slope, branch, mod, w_out, w_up, w_down = take(10)
        w_out, w_up, w_down = (ref.at[layers[1]] for ref in (w_out, w_up, w_down))
        if has_before[1]:
            open_before = take(3)
    else:
        (lines,) = take(1)
    if has_close:
        close_mine, close_other, close_mods = take(3)
    if start == "first":
        (cot_out,) = take(1)
    if has_open:
        open_mine, open_other, open_mods, d_mid_out, do_out, cen_out = take(6)
    else:
        g_out, sums_out = take(2)
        sums_at = close_before[1].shape[0]
    if has_close:
        grads_scr, normed_scr = take(2)
    if has_open:
        pg_scr, hin_scr = take(2)

    patches = middle.shape[1] if has_open else x_in.shape[1]
    totals = {}

    def add_sums(name, values):
        totals[name] = totals[name] + folded(values) if name in totals else folded(values)

    def put_sums(out, before, names):
        for place, name in enumerate(names):
            rows = slice(place * D, (place + 1) * D)
            out[rows, :] = totals[name] + before[2][rows, :] if before else totals[name]

    if start == "first":
        for index, ref in enumerate(cots):
            rows = ref.shape[0]
            cot_out[:, index * rows : (index + 1) * rows] = turned(ref[...])

    def close(at):
        standard, scale = standardise(x_in[:, at].astype(F32))
        gain = 1.0 + part(mod_in, 1, patches)
        normed_scr[:, at] = (standard * gain + part(mod_in, 0, patches)).astype(BF16)
        for third in range(3):
            if third == 0:
                piece = dq[:, at]
            else:
                rows = slice((third - 1) * D, third * D)
                piece = (d_own[rows, at] + d_got[rows, at].astype(F32)).astype(BF16)
            grads_scr[third * D : (third + 1) * D, at] = piece
        back = nn(w_qkv[...], grads_scr[:, at])
        put_grads(normed_scr, grads_scr[...], where, D // 8, 0, close_mine, close_other, close_before)
        add_sums("shift_a", back)
        add_sums("scale_a", back * standard)
        g = d_mid_in[:, at] + pre_norm_back(standard, scale, back, gain)
        if start == "cross":
            g = g + (1.0 - active[0]) * cots[0][:, at].astype(F32)
        return g

    def dense(at, g):
        standard, scale = standardise(middle[:, at].astype(F32))
        gain = 1.0 + part(mod, 4, patches)
        hin_scr[:, at] = (standard * gain + part(mod, 3, patches)).astype(BF16)
        branch_grad = (part(mod, 5, patches) * g).astype(BF16)
        add_sums("gate_m", g * branch[:, at].astype(F32))
        chunks = [slice(start, start + BLOCK) for start in range(0, w_down.shape[0], BLOCK)]
        back = None
        waiting = None

        def down(place):
            wide_rows = slice(place * BLOCK, (place + 2) * BLOCK)
            both = nn(w_down[wide_rows, :], branch_grad)
            return [both[:BLOCK], both[BLOCK:]]

        hidden_grads = down(0)
        for place, rows in enumerate(chunks):
            hidden_grad = hidden_grads[place]
            if place % 2 == 0 and place + 2 < len(chunks):
                hidden_grads += down(place + 2)
            if place > 0:
                term = nn(w_up[:, chunks[place - 1]], waiting)
                back = term if back is None else back + term
            waiting = slope[rows, at] * hidden_grad.astype(BF16)
            pg_scr[rows, at] = waiting
        back = back + nn(w_up[:, chunks[-1]], waiting)
        count = w_down.shape[0] // 8
        start_at = count * (D // LANES)
        put_grads(hidden, branch_grad, where, count, 0, open_mine, open_other, open_before)
        put_grads(hin_scr, pg_scr[...], where, D // 8, start_at, open_mine, open_other, open_before)
        add_sums("shift_m", back)
        add_sums("scale_m", back * standard)
        d_mid = g + pre_norm_back(standard, scale, back, gain)
        d_mid_out[:, at] = d_mid
        att_grad = (part(mod, 2, patches) * d_mid).astype(BF16)
        mixed_grad = nn(w_out[...], att_grad).astype(BF16)
        do_out[:, at] = mixed_grad
        start_at += (w_up.shape[1] // LANES) * (D // 8)
        put_grads(mixed, att_grad, where, D // 8, start_at, open_mine, open_other, open_before)
        add_sums("gate_a", d_mid * attended[:, at].astype(F32))
        product = mixed_grad.astype(F32) * mixed[:, at].astype(F32)
        for head in range(HEADS):
            cen_out[head : head + 1, at] = jnp.sum(product[head_rows(head)], axis=0, keepdims=True)

    at = slice(0, patches)
    g = close(at) if has_close else cot_out[:, at].astype(F32) * active[0]
    if has_open:
        dense(at, g)
    else:
        g_out[...] = g[:, : g_out.shape[0]].T
    if has_close:
        put_sums(close_mods, close_before, ("shift_a", "scale_a"))
    if has_open:
        put_sums(open_mods, open_before, ("gate_a", "shift_m", "scale_m", "gate_m"))
    else:
        sums_out[...] = lines[...]
        put_lines(sums_out, 0, close_mods[...])
        close_other[sums_at:, :] = sums_out[...].astype(BF16)


def attend_back_kernel(has_before, waits, q, kn, vt, lse, d_out, centre, *refs):
    if has_before:
        before, *refs = refs
    d_kv, dq_out, kt_scr, vn_scr = refs[waits:]
    for column in range(0, D, LANES):
        kt_scr[column : column + LANES, :] = turned(kn[:, column : column + LANES])
    for column in range(0, vt.shape[1], BLOCK):
        vn_scr[column : column + BLOCK, :] = turned(vt[:, column : column + BLOCK])

    steps = [(head, slice(at, at + BLOCK)) for head in range(HEADS) for at in range(0, kn.shape[0], BLOCK)]

    def score(head, at):
        columns = pair_columns(head)
        rows = head_rows(head)
        return nn(kn[at, columns], padded(q[rows, :], head)), nn(vn_scr[at, columns], padded(d_out[rows, :], head))

    totals = {}

    def finish(head, at, probs, score_grads):
        rows = head_rows(head)
        d_kv[D + rows.start : D + rows.stop, at] = nt(d_out[rows, :], probs).astype(d_kv.dtype)
        d_kv[rows, at] = nt(q[rows, :], score_grads).astype(d_kv.dtype)
        term = nn(kt_scr[rows, at], score_grads)
        if head not in totals:
            totals[head] = before[rows, :] + term if has_before else term
            return
        term = totals[head] + term
        if has_before:
            term = term * HEAD_DIM ** (-0.5)
        dq_out[rows, :] = term.astype(dq_out.dtype)

    waiting = None
    following = score(*steps[0])
    for place, (head, at) in enumerate(steps):
        scores, prob_grads = following
        if place + 1 < len(steps):
            following = score(*steps[place + 1])
        if waiting is not None:
            finish(*waiting)
        probs = jnp.exp(scores - lse[head : head + 1, :])
        score_grads = (probs * (prob_grads - centre[head : head + 1, :])).astype(BF16)
        waiting = (head, at, probs.astype(BF16), score_grads)
    finish(*waiting)


def split_kernel(waits, where, *refs):
    *halves, keep, sent, total_scr = refs[waits:]
    rows_half = keep.shape[0]
    at = 0
    for mine, other in zip(halves[::2], halves[1::2]):
        rows = mine.shape[0]
        total_scr[at : at + rows, :] = mine[...] + other[...].astype(F32)
        at += rows
    if at < total_scr.shape[0]:
        total_scr[at:, :] = jnp.zeros((total_scr.shape[0] - at, LANES), F32)
    odd = where[3]
    keep[...] = total_scr[pl.ds(pl.multiple_of(odd * rows_half, 16), rows_half), :]
    sent[...] = total_scr[pl.ds(pl.multiple_of((1 - odd) * rows_half, 16), rows_half), :].astype(BF16)


def pair_sum_kernel(waits, *refs):
    refs = refs[waits:]
    count = len(refs) // 3
    for keep, got, out in zip(refs[:count], refs[count : 2 * count], refs[2 * count :]):
        out[...] = (keep[...].astype(F32) + got[...].astype(F32)).astype(BF16)


def put_lines(out, row, values):
    ones = jnp.ones((16, LANES), BF16)
    high = values.astype(BF16)
    low = (values - high.astype(F32)).astype(BF16)
    line = (nt(ones, high) + nt(ones, low))[0:1]
    for column in range(0, line.shape[1], LANES):
        out[row : row + 1, :] = line[:, column : column + LANES]
        row += 1
    return row


def lines_kernel(early, context, *refs):
    *sums, out = refs
    out[...] = jnp.zeros_like(out)
    row = 2 * D // LANES
    for ref in sums:
        row = put_lines(out, row, ref[...])
    for column in range(0, D, LANES):
        out[row : row + 1, :] = context[0:1, column : column + LANES].astype(F32)
        row += 1


def join_kernel(sum_count, early, other_early, mine, sums, got, out):
    rows = mine.shape[0]
    out[:rows, :] = (mine[...] + got[:rows, :].astype(F32)).astype(BF16)
    other = got[rows:, :].astype(F32)
    summed = lax.broadcasted_iota(jnp.int32, (SUM_ROWS, LANES), 0) < sum_count
    out[rows:, :] = (sums[...] + jnp.where(summed, other, 0.0)).astype(BF16)


def pair_kernel(rows, where, own, got, out):
    out[:rows, :] = (own[:rows, :].astype(F32) + got[:rows, :].astype(F32)).astype(BF16)
    odd = where[3]
    size = SUM_ROWS
    out[pl.ds(pl.multiple_of(rows + odd * size, 16), size), :] = own[rows:, :]
    out[pl.ds(pl.multiple_of(rows + (1 - odd) * size, 16), size), :] = got[rows:, :]


def gather_kernel(layer, where, own, got, *refs):
    outs, qkv_out, rows_scr, scratch, sems = refs[-9:-6], refs[-6], refs[-5], refs[-4:-1], refs[-1]
    if layer == 1:
        outs = refs[-8:-5]
    half = own.shape[0]
    rows_scr[pl.ds(pl.multiple_of(where[3] * half, 16), half), :] = own[...]
    rows_scr[pl.ds(pl.multiple_of((1 - where[3]) * half, 16), half), :] = got[...]
    at = 0
    copies = []
    for place, (out, held) in enumerate(zip(outs, scratch)):
        rows = held.shape[0]
        for column in range(0, held.shape[1], LANES):
            held[:, column : column + LANES] = rows_scr[at : at + rows, :].astype(F32)
            at += rows
        copies.append(pltpu.make_async_copy(held, out.at[layer], sems.at[place]))
        copies[-1].start()
    if layer == 0:
        rows = qkv_out.shape[0]
        for column in range(0, qkv_out.shape[1], LANES):
            qkv_out[:, column : column + LANES] = rows_scr[at : at + rows, :].astype(F32)
            at += rows
    for copy in copies:
        copy.wait()


def finish_kernel(item_count, where, own, got, qkv_1, qkv_out, ada_out, bias_out, shift_out, sum_scr, bias_scr, shift_scr):
    layers = 2
    device, high = where[0], where[4]
    slice_rows = qkv_out.shape[1]
    close_rows = slice_rows * (3 * D // LANES)
    for other in range(2):
        rows = slice(close_rows + other * SUM_ROWS, close_rows + (other + 1) * SUM_ROWS)
        sum_scr[2 * high + other] = own[rows, :].astype(F32)
        sum_scr[2 * (1 - high) + other] = got[rows, :].astype(F32)
    qkv_out[1] = qkv_1[...]
    for tile in range(3 * D // LANES):
        rows = slice(tile * slice_rows, (tile + 1) * slice_rows)
        total = own[rows, :].astype(F32) + got[rows, :].astype(F32)
        qkv_out[0, :, tile * LANES : (tile + 1) * LANES] = total
    tiles = 6 * D // LANES
    contexts = []
    for other in range(item_count):
        line = jnp.concatenate([sum_scr[other, layers * tiles + c : layers * tiles + c + 1, :] for c in range(3)], axis=1)
        contexts.append(line)
    square = jnp.concatenate(contexts + [jnp.zeros((8 - item_count, D), F32)], axis=0)
    spot = lax.broadcasted_iota(jnp.int32, (slice_rows, D), 1)
    want = lax.broadcasted_iota(jnp.int32, (slice_rows, D), 0) + device * slice_rows
    pick = jnp.where(spot == want, 1.0, 0.0).astype(BF16)
    columns = nt(pick, square.astype(BF16))
    bias_rows = bias_out.shape[1]
    for index in range(layers):
        flats = []
        for tile in range(tiles):
            row = index * tiles + tile
            total = None
            flat = None
            for other in range(item_count):
                line = sum_scr[other, row : row + 1, :]
                term = columns[:, other : other + 1] * line
                total = term if total is None else total + term
                flat = line if flat is None else flat + line
            ada_out[index, :, tile * LANES : (tile + 1) * LANES] = total
            flats.append(flat)
        flat = jnp.concatenate(flats, axis=1)
        for place in range(flat.shape[1] // bias_rows):
            bias_scr[place, index : index + 1, :] = flat[:, place * bias_rows : (place + 1) * bias_rows]
            at = 3 * D + place * slice_rows
            shift_scr[place, index : index + 1, :] = flat[:, at : at + slice_rows]
    bias_out[...] = bias_scr[device]
    shift_out[...] = shift_scr[device]


VMEM = pl.BlockSpec(memory_space=pltpu.VMEM)
SMEM = pl.BlockSpec(memory_space=pltpu.SMEM)
ANY = pl.BlockSpec(memory_space=pl.ANY)
HBM = pl.BlockSpec(memory_space=pltpu.HBM)


def layer_block(array, index):
    return pl.BlockSpec((None,) + array.shape[1:], lambda step: (index,) + (0,) * (array.ndim - 1))


def call(body, args, outs, scratch=(), flops=0, name=None, direct=0, aliases=None):
    arrays = [arg[0] if isinstance(arg, tuple) else arg for arg in args]
    specs = [arg[1] if isinstance(arg, tuple) else VMEM for arg in args]
    return pl.pallas_call(
        body,
        out_shape=[jax.ShapeDtypeStruct(shape, kind) for shape, kind in outs],
        in_specs=specs,
        out_specs=[ANY] * direct + [VMEM] * (len(outs) - direct),
        input_output_aliases=aliases or {},
        scratch_shapes=[one if not isinstance(one, tuple) else pltpu.VMEM(*one) for one in scratch],
        compiler_params=pltpu.CompilerParams(vmem_limit_bytes=VMEM_LIMIT),
        cost_estimate=pl.CostEstimate(flops=flops, bytes_accessed=0, transcendentals=0),
        name=name,
    )(*arrays)


VMEM_LIMIT = 14 * 1024 * 1024


def fast_shards(
    lat_count, lon_count, item_count,
    fields, lead_index, rollout, w_qkv, w_out, w_up, w_down, w_ada, b_ada, cotangent,
):
    _, rows_dev, cols_dev, width = fields.shape
    local = rows_dev * cols_dev
    layers = w_qkv.shape[0]
    ff = w_up.shape[2]
    patches = 4 * local
    device = lax.axis_index("lat") * lon_count + lax.axis_index("lon")
    item = lax.axis_index("item")
    where = jnp.stack([device, device ^ 1, item, item & 1, item >> 1]).astype(jnp.int32)
    active = (1 < rollout[0]).astype(F32)[None]

    def plane_flip(value, flip_lat, flip_y):
        pairs = [
            (a * lon_count + b, (a ^ flip_lat) * lon_count + (b ^ (2 * flip_y)))
            for a in range(lat_count)
            for b in range(lon_count)
        ]
        return lax.ppermute(value, ("lat", "lon"), pairs)

    def swap(value):
        return lax.ppermute(value, "lon", [(index, index ^ 1) for index in range(lon_count)])

    def with_item(value, flip):
        return lax.ppermute(value, "item", [(index, index ^ flip) for index in range(item_count)])

    def plane_parts(value):
        return [value, plane_flip(value, 1, 0), plane_flip(value, 0, 1), plane_flip(value, 1, 1)]

    field_parts = plane_parts(fields.reshape(local, width))

    context = jax.nn.silu(embedding(lead_index[0])).astype(BF16)
    context = jnp.broadcast_to(context[None, :], (16, width))
    square = (width, patches)
    natural = (patches, width)
    weights = (w_qkv, w_ada, b_ada, w_out, w_up, w_down)
    weights = [(pltpu.with_memory_space_constraint(value, pltpu.HBM), HBM) for value in weights]
    first_outs = [((6 * width, LANES), F32)] + [((width, width), BF16)] * 3
    rest_outs = [((width, width), BF16), ((ff, width), BF16), ((width, ff), BF16)]
    first_fetch = [((width, 3 * width), BF16), ((width, 6 * width), BF16)]
    rest_fetch = [((width, width), BF16), ((width, ff), BF16), ((ff, width), BF16)]
    prepared = call(
        prepare_kernel,
        [context, *weights, (where, SMEM), (active, SMEM)],
        first_outs * 2 + rest_outs,
        first_fetch + [(b_ada.shape, F32)] + rest_fetch + first_fetch + [pltpu.SemaphoreType.DMA((8,))],
        name="prepare",
    )
    first_parts = [prepared[0:4], prepared[4:8]]
    rest_parts = [prepared[8:11]]
    mods = [one[0] for one in first_parts]

    project_outs = [(square, F32), (square, BF16), (square, BF16), (natural, BF16), (square, BF16)]
    dense_flops = 2 * patches * (width * 3 * width + width * width + 2 * width * ff)
    score_flops = 2 * patches * 2 * patches * width * 4
    cot = cotangent.reshape(local, width)
    cot, x, xb, *projected = call(
        first_kernel,
        [*field_parts, cot, plane_flip(cot, 1, 0), *first_parts[0]],
        [((2 * local, width), BF16)] + project_outs,
        flops=2 * patches * width * 4 * width,
        name="first",
    )
    saved = []
    for step in range(STEPS):
        for index in range(layers):
            q, kn, vt = projected
            if len(rest_parts) == index:
                rest_parts.append(
                    call(
                        functools.partial(prepare_rest_kernel, index),
                        [(kn, ANY), w_out, w_up, w_down],
                        rest_outs,
                        name="prepare_rest",
                    )
                )
            kn_far, vt_far = swap(kn), swap(vt)
            early = [w_up] if len(rest_parts) == index + 1 < layers else []
            passing = [cot] if step == STEPS - 1 and index == 0 else []
            passed = [((2 * local, width), BF16)] if passing else []
            sums, tops, *passed = call(
                functools.partial(attend_own_kernel, len(early)),
                early + [q, kn, vt] + passing,
                [((HEADS, HEAD_DIM + ONES, patches), F32), ((16, LANES), F32)] + passed,
                flops=10 * score_flops,
                name="forward_own",
            )
            if passed:
                cot_parts = [passed[0], plane_flip(passed[0], 0, 1)]
            last = step == STEPS - 1 and index == layers - 1
            if index == 0 and step > 0:
                x_step = x
            following = list(first_parts[(index + 1) % layers])
            early = [w_down] if len(rest_parts) == index + 1 < layers else []
            lse, mixed, attended, middle, hidden, slope, branch, *results = call(
                functools.partial(forward_kernel, last, len(early)),
                early
                + ([(active, SMEM), x, x_step] if last else [x])
                + [q, kn, kn_far, vt, vt_far, sums, tops, mods[index], *rest_parts[index]]
                + ([] if last else following),
                [
                    ((HEADS, patches), F32),
                    (square, BF16),
                    (square, BF16),
                    (square, BF16),
                    ((ff, patches), BF16),
                    ((ff, patches), BF16),
                    (square, BF16),
                ]
                + ([((local, width), F32)] if last else project_outs),
                flops=dense_flops + 2 * score_flops,
                name="forward",
            )
            saved.append((xb, [mixed, attended, middle, hidden, slope, branch], (q, kn, kn_far, vt, vt_far, lse)))
            if last:
                final = results[0]
            else:
                x, xb, *projected = results

    slice_rows = width // 8
    open_rows = 2 * (ff // 8) * (width // LANES) + slice_rows * (width // LANES)
    close_rows = slice_rows * (3 * width // LANES)
    order = [(step, index) for step in reversed(range(STEPS)) for index in reversed(range(layers))]
    open_done = [None] * layers
    close_done = [None] * layers
    pending = None
    for place in range(len(order) + 1):
        has_close = pending is not None
        has_open = place < len(order)
        use = [order[place - 1][1], order[place][1] if has_open else 0]
        waits = []
        if has_close and close_done[use[0]]:
            waits = [pair_1] if has_open else []
        args = [(value, ANY) for value in waits] + [(where, SMEM), (active, SMEM)]
        outs = []
        scratch = []
        has_before = [False, False]
        start = ""
        if has_close:
            args += pending
            if close_done[use[0]] is not None:
                has_before[0] = True
                args += close_done[use[0]]
            outs += [((close_rows, LANES), F32)]
            sent_rows = close_rows + (0 if has_open else SUM_ROWS)
            outs += [((sent_rows, LANES), BF16 if has_before[0] else F32), ((2 * width, LANES), F32)]
            scratch += [((3 * width, patches), BF16), (square, BF16)]
        if place == 0:
            start = "first"
            args += cot_parts
            outs += [(square, BF16)]
        elif has_open and order[place][0] != order[place - 1][0]:
            start = "cross"
            args += [cot_t]
        if has_open:
            step, index = order[place]
            xb, kept, heads = saved[step * layers + index]
            args += kept + [mods[index], w_out, w_up, w_down]
            if open_done[index] is not None:
                has_before[1] = True
                args += open_done[index]
            outs += [
                ((open_rows, LANES), F32),
                ((open_rows, LANES), BF16 if has_before[1] else F32),
                ((4 * width, LANES), F32),
                (square, F32),
                (square, BF16),
                ((HEADS, patches), F32),
            ]
            scratch += [((ff, patches), BF16), (square, BF16)]
        else:
            args += [lines]
            outs += [((local, width), F32), ((SUM_ROWS, LANES), F32)]
        results = list(
            call(
                functools.partial(dense_back_kernel, has_close, has_open, has_before, start, use, len(waits)),
                args,
                outs,
                scratch,
                flops=2 * dense_flops if has_open else 0,
                name="dense_back" if has_open else "close_back",
            )
        )
        if has_close:
            close_done[use[0]] = results[:3]
            del results[:3]
        if start == "first":
            cot_t = results.pop(0)
        if not has_open:
            gradient, line = results
            break
        open_done[index] = results[:3]
        d_mid, d_out, centre = results[3:]
        q, kn, kn_far, vt, vt_far, lse = heads
        halves = [open_done[index][0], open_done[index][1]]
        if index == 0:
            halves += [close_done[1][0], close_done[1][1]]
        half_rows = -(-sum(half.shape[0] for half in halves[::2]) // 32) * 16

        def split(waits):
            pieces = [half if place % 2 == 0 else swap(half) for place, half in enumerate(halves)]
            return call(
                functools.partial(split_kernel, len(waits)),
                [(where, SMEM), *waits, *pieces],
                [((half_rows, LANES), F32), ((half_rows, LANES), BF16)],
                [((2 * half_rows, LANES), F32)],
                name="split",
            )

        def pair_sum(late, keeps, gots, others=()):
            outs = [(keep.shape, BF16) for keep in keeps]
            body = functools.partial(pair_sum_kernel, 1 + len(others))
            return call(body, [(late, ANY), *others, *keeps, *gots], outs, name="pair_sum")

        waits = []
        if has_before[1] and index == 0:
            pair_got_1 = with_item(pair_1, 2)
            lines = call(
                lines_kernel,
                [(pair_got_1, ANY), context, open_done[0][2], close_done[1][2], open_done[1][2]],
                [((SUM_ROWS, LANES), F32)],
                flops=10 * score_flops,
                name="lines",
            )[0]
            keep, sent = split([(lines, ANY)])
            got_0 = with_item(sent, 1)
            waits = [keep]
        d_far, dq = call(
            functools.partial(attend_back_kernel, False, len(waits)),
            [q, kn_far, vt_far, lse, d_out, centre] + [(value, ANY) for value in waits],
            [((2 * width, patches), BF16), (square, F32)],
            [(square, BF16), (natural, BF16)],
            flops=10 * score_flops,
            name="attend_far",
        )
        d_got = swap(d_far)
        waits = []
        if has_before[1]:
            if index == 1:
                keep, sent = split([(d_far, ANY)])
                got_1 = with_item(sent, 1)
                waits = [keep]
            else:
                (item_1,) = pair_sum(d_far, [pair_1], [pair_got_1])
                item_got_1 = with_item(item_1, 1)
                (pair_0,) = pair_sum(d_far, [keep], [got_0], [(item_1, ANY)])
                pair_got_0 = with_item(pair_0, 2)
                waits = [pair_0]
        d_own, dq = call(
            functools.partial(attend_back_kernel, True, len(waits)),
            [q, kn, vt, lse, d_out, centre, dq] + [(value, ANY) for value in waits],
            [((2 * width, patches), F32), (square, BF16)],
            [(square, BF16), (natural, BF16)],
            flops=10 * score_flops,
            name="attend_own",
        )
        if has_before[1] and index == 1:
            (pair_1,) = pair_sum(dq, [keep], [got_1])
        pending = [d_own, d_got, dq, d_mid, xb, mods[index], w_qkv]

    message = call(
        functools.partial(join_kernel, layers * 6 * width // LANES),
        [(pair_got_0, ANY), (item_got_1, ANY), close_done[0][0], line, swap(close_done[0][1])],
        [((close_rows + SUM_ROWS, LANES), BF16)],
        name="join",
    )[0]
    message_got = with_item(message, 1)
    stacks = [
        ((layers, ff // 8, width), F32),
        ((layers, slice_rows, ff), F32),
        ((layers, slice_rows, width), F32),
    ]
    held = [(shape[1:], kind) for shape, kind in stacks]
    sems = [pltpu.SemaphoreType.DMA((3,))]
    stacked = call(
        functools.partial(gather_kernel, 1),
        [(where, SMEM), item_1, item_got_1],
        stacks,
        [((2 * pair_1.shape[0], LANES), BF16)] + held + sems,
        name="gather",
        direct=3,
    )
    early = (pltpu.with_memory_space_constraint(stacked[2], pltpu.HBM), HBM)
    (item_0,) = pair_sum(message_got, [pair_0], [pair_got_0], [early])
    message = call(
        functools.partial(pair_kernel, close_rows),
        [(where, SMEM), message, message_got],
        [((close_rows + 2 * SUM_ROWS, LANES), BF16)],
        name="pair",
    )[0]
    down_grad, up_grad, out_grad, qkv_1 = call(
        functools.partial(gather_kernel, 0),
        [(where, SMEM), item_0, with_item(item_0, 1)] + [(value, ANY) for value in stacked],
        stacks + [((slice_rows, 3 * width), F32)],
        [((2 * pair_0.shape[0], LANES), BF16)] + held + sems,
        name="gather",
        direct=3,
        aliases={3: 0, 4: 1, 5: 2},
    )
    bias_rows = 6 * width // 8
    qkv_grad, ada_grad, bias_grad, shift_grad = call(
        functools.partial(finish_kernel, item_count),
        [(where, SMEM), message, with_item(message, 2), qkv_1],
        [
            ((layers, slice_rows, 3 * width), F32),
            ((layers, slice_rows, 6 * width), F32),
            ((layers, bias_rows), F32),
            ((layers, slice_rows), F32),
        ],
        [
            ((item_count, SUM_ROWS, LANES), F32),
            ((8, layers, bias_rows), F32),
            ((8, layers, slice_rows), F32),
        ],
        name="finish",
    )
    field_shape = (1, rows_dev, cols_dev, width)
    return (
        final.reshape(field_shape),
        gradient.reshape(field_shape),
        qkv_grad,
        out_grad,
        up_grad,
        down_grad,
        ada_grad,
        bias_grad,
        shift_grad,
    )


def solution(mesh):
    lat_count, lon_count, item_count = mesh.shape["lat"], mesh.shape["lon"], mesh.shape["item"]
    if lat_count == 2 and lon_count == 4:
        body = functools.partial(fast_shards, lat_count, lon_count, item_count)
    else:
        body = shards
    return jax.shard_map(
        body,
        mesh=mesh,
        in_specs=(
            P("item", "lat", "lon", None),
            P("item"),
            P("item"),
            P(),
            P(),
            P(),
            P(),
            P(),
            P(),
            P("item", "lat", "lon", None),
        ),
        out_specs=(
            P("item", "lat", "lon", None),
            P("item", "lat", "lon", None),
            P(None, ("lat", "lon"), None),
            P(None, ("lat", "lon"), None),
            P(None, ("lat", "lon"), None),
            P(None, ("lat", "lon"), None),
            P(None, ("lat", "lon"), None),
            P(None, ("lat", "lon")),
            P(None, ("lat", "lon")),
        ),
        check_vma=False,
    )
```

```python
import functools
import math

import jax
import jax.numpy as jnp
from jax import lax
from jax.experimental import pallas as pl
from jax.experimental.pallas import tpu as pltpu
from jax.sharding import PartitionSpec as P

D = 384
HEADS = 6
HEAD_DIM = 64
STEPS = 2


def shortened(shard):
    return jax.tree.map(lambda a: a.astype(jnp.bfloat16) if a.dtype == jnp.float32 else a, shard)


def embedding(lead):
    half_width = D // 2
    lead_hours = 6.0 * (lead.astype(jnp.float32) + 1.0)
    frequencies = jnp.exp(
        -math.log(10000.0) * jnp.arange(half_width, dtype=jnp.float32) / half_width
    )
    angles = lead_hours * frequencies
    return jnp.concatenate([jnp.sin(angles), jnp.cos(angles)], axis=-1)


def pre_norm(values, shift_part, scale_part):
    centred = values - jnp.mean(values, axis=-1, keepdims=True)
    variance = jnp.mean(centred * centred, axis=-1, keepdims=True)
    return centred * lax.rsqrt(variance + 1e-06) * (1.0 + scale_part) + shift_part


def gather_keys(keys_values):
    band_rows = lax.all_gather(keys_values, "lon", axis=0, tiled=True)
    return lax.all_gather(band_rows, "lat", axis=0, tiled=True)


def spread_keys(key_value_grads):
    band_grads = lax.psum_scatter(
        key_value_grads.astype(jnp.bfloat16), "lat", scatter_dimension=0, tiled=True
    )
    return lax.psum_scatter(band_grads, "lon", scatter_dimension=0, tiled=True).astype(jnp.float32)


def forward_layer(current, modulation, weight_qkv, weight_out, weight_up, weight_down):
    local_rows, width = current.shape
    shift_attn, scale_attn, gate_attn, shift_mlp, scale_mlp, gate_mlp = modulation
    normed = pre_norm(current, shift_attn, scale_attn).astype(jnp.bfloat16)
    projected = jnp.dot(normed, weight_qkv, preferred_element_type=jnp.float32).astype(jnp.bfloat16)
    queries = projected[:, :width].reshape(local_rows, HEADS, HEAD_DIM)
    own_keys = projected[:, width:]
    gathered = gather_keys(own_keys)
    total_rows = gathered.shape[0]
    key_heads = gathered[:, :width].reshape(total_rows, HEADS, HEAD_DIM)
    value_heads = gathered[:, width:].reshape(total_rows, HEADS, HEAD_DIM)
    scores = jnp.einsum(
        "thd,nhd->htn", queries, key_heads, preferred_element_type=jnp.float32
    ) * HEAD_DIM ** (-0.5)
    log_total = jax.nn.logsumexp(scores, axis=-1, keepdims=True)
    probabilities = jnp.exp(scores - log_total).astype(jnp.bfloat16)
    mixed = jnp.einsum(
        "htn,nhd->thd", probabilities, value_heads, preferred_element_type=jnp.float32
    )
    mixed = mixed.reshape(local_rows, width).astype(jnp.bfloat16)
    attended = jnp.dot(mixed, weight_out, preferred_element_type=jnp.float32)
    middle = current + gate_attn * attended
    hidden_in = pre_norm(middle, shift_mlp, scale_mlp).astype(jnp.bfloat16)
    pre_act = jnp.dot(hidden_in, weight_up, preferred_element_type=jnp.float32)
    hidden = jax.nn.gelu(pre_act).astype(jnp.bfloat16)
    branch = jnp.dot(hidden, weight_down, preferred_element_type=jnp.float32)
    output = middle + gate_mlp * branch
    kept = (
        current,
        normed,
        queries,
        gathered,
        own_keys,
        log_total,
        mixed,
        attended,
        middle,
        hidden_in,
        pre_act,
        hidden,
        branch,
    )
    return (output, kept)


def backward_layer(grad_out, kept, modulation, weight_qkv, weight_out, weight_up, weight_down):
    (
        current,
        normed,
        queries,
        gathered,
        own_keys,
        log_total,
        mixed,
        attended,
        middle,
        hidden_in,
        pre_act,
        hidden,
        branch,
    ) = kept
    local_rows, width = current.shape
    total_rows = gathered.shape[0]
    shift_attn, scale_attn, gate_attn, shift_mlp, scale_mlp, gate_mlp = modulation
    factor = HEAD_DIM ** (-0.5)
    branch_grad = (gate_mlp * grad_out).astype(jnp.bfloat16)
    gate_mlp_grad = jnp.sum(grad_out * branch, axis=0)
    hidden_grad = jnp.dot(branch_grad, weight_down.T, preferred_element_type=jnp.float32)
    down_grad = jnp.dot(hidden.T, branch_grad, preferred_element_type=jnp.float32)
    _, gelu_back = jax.vjp(jax.nn.gelu, pre_act)
    pre_grad = gelu_back(hidden_grad)[0].astype(jnp.bfloat16)
    hidden_in_grad = jnp.dot(pre_grad, weight_up.T, preferred_element_type=jnp.float32)
    up_grad = jnp.dot(hidden_in.T, pre_grad, preferred_element_type=jnp.float32)
    _, second_back = jax.vjp(pre_norm, middle, shift_mlp, scale_mlp)
    middle_part, shift_mlp_grad, scale_mlp_grad = second_back(hidden_in_grad)
    middle_grad = grad_out + middle_part
    attended_grad = (gate_attn * middle_grad).astype(jnp.bfloat16)
    gate_attn_grad = jnp.sum(middle_grad * attended, axis=0)
    mixed_grad = jnp.dot(attended_grad, weight_out.T, preferred_element_type=jnp.float32).astype(
        jnp.bfloat16
    )
    out_grad = jnp.dot(mixed.T, attended_grad, preferred_element_type=jnp.float32)
    mixed_heads = mixed_grad.reshape(local_rows, HEADS, HEAD_DIM)
    key_heads = gathered[:, :width].reshape(total_rows, HEADS, HEAD_DIM)
    value_heads = gathered[:, width:].reshape(total_rows, HEADS, HEAD_DIM)
    scores = (
        jnp.einsum("thd,nhd->htn", queries, key_heads, preferred_element_type=jnp.float32) * factor
    )
    probabilities = jnp.exp(scores - log_total)
    prob_grads = jnp.einsum(
        "thd,nhd->htn", mixed_heads, value_heads, preferred_element_type=jnp.float32
    )
    centre = jnp.sum(prob_grads * probabilities, axis=-1, keepdims=True)
    score_grads = (probabilities * (prob_grads - centre)).astype(jnp.bfloat16)
    query_grads = (
        jnp.einsum("htn,nhd->thd", score_grads, key_heads, preferred_element_type=jnp.float32)
        * factor
    )
    value_grads = jnp.einsum(
        "htn,thd->nhd",
        probabilities.astype(jnp.bfloat16),
        mixed_heads,
        preferred_element_type=jnp.float32,
    )
    key_grads = (
        jnp.einsum("htn,thd->nhd", score_grads, queries, preferred_element_type=jnp.float32)
        * factor
    )
    key_value_grads = jnp.concatenate(
        [key_grads.reshape(total_rows, width), value_grads.reshape(total_rows, width)], axis=1
    )
    local_grads = spread_keys(key_value_grads)
    projected_grad = jnp.concatenate(
        [query_grads.reshape(local_rows, width), local_grads], axis=1
    ).astype(jnp.bfloat16)
    normed_grad = jnp.dot(projected_grad, weight_qkv.T, preferred_element_type=jnp.float32)
    qkv_grad = jnp.dot(normed.T, projected_grad, preferred_element_type=jnp.float32)
    _, first_back = jax.vjp(pre_norm, current, shift_attn, scale_attn)
    current_part, shift_attn_grad, scale_attn_grad = first_back(normed_grad)
    input_grad = middle_grad + current_part
    modulation_grad = jnp.concatenate(
        [
            shift_attn_grad,
            scale_attn_grad,
            gate_attn_grad,
            shift_mlp_grad,
            scale_mlp_grad,
            gate_mlp_grad,
        ]
    )
    return (input_grad, (qkv_grad, out_grad, up_grad, down_grad, modulation_grad))


def shards(fields, lead_index, rollout, w_qkv, w_out, w_up, w_down, w_ada, b_ada, cotangent):
    _, rows_dev, cols_dev, width = fields.shape
    local_rows = rows_dev * cols_dev
    layer_count = w_qkv.shape[0]
    context = jax.nn.silu(embedding(lead_index[0])).astype(jnp.bfloat16)
    context_wide = context.astype(jnp.float32)
    modulations = [
        (
            jnp.dot(context[None, :], w_ada[index], preferred_element_type=jnp.float32)[0]
            + b_ada[index]
        ).reshape(6, width)
        for index in range(layer_count)
    ]
    weight_sets = [
        (w_qkv[index], w_out[index], w_up[index], w_down[index]) for index in range(layer_count)
    ]
    count = rollout[0]
    current = fields.reshape(local_rows, width).astype(jnp.float32)
    saved = []
    for rollout_step in range(STEPS):
        updated = current
        kept_layers = []
        for index in range(layer_count):
            updated, kept = forward_layer(updated, modulations[index], *weight_sets[index])
            kept_layers.append(kept)
        current = jnp.where(rollout_step < count, updated, current)
        saved.append(kept_layers)
    gradient = cotangent.reshape(local_rows, width).astype(jnp.float32)
    summed = None
    shares = None
    for rollout_step in reversed(range(STEPS)):
        active = (rollout_step < count).astype(jnp.float32)
        inner = gradient * active
        layer_terms = [None] * layer_count
        for index in reversed(range(layer_count)):
            inner, layer_terms[index] = backward_layer(
                inner, saved[rollout_step][index], modulations[index], *weight_sets[index]
            )
        gradient = inner + (1.0 - active) * gradient
        modulation_grads = jnp.stack([terms[4] for terms in layer_terms])
        step_terms = (
            jnp.stack([terms[0] for terms in layer_terms]),
            jnp.stack([terms[1] for terms in layer_terms]),
            jnp.stack([terms[2] for terms in layer_terms]),
            jnp.stack([terms[3] for terms in layer_terms]),
            context_wide[None, :, None] * modulation_grads[:, None, :],
            modulation_grads,
            modulation_grads[:, 3 * width : 4 * width],
        )
        summed = step_terms if summed is None else jax.tree.map(jnp.add, summed, step_terms)
    shares = lax.psum_scatter(summed, ("lat", "lon"), scatter_dimension=1, tiled=True)
    totals = jax.tree.map(
        lambda part: part.astype(jnp.float32), lax.psum(shortened(shares), "item")
    )
    return (
        current.reshape(1, rows_dev, cols_dev, width),
        gradient.reshape(1, rows_dev, cols_dev, width),
        totals[0],
        totals[1],
        totals[2],
        totals[3],
        totals[4],
        totals[5],
        totals[6],
    )


F32 = jnp.float32
BF16 = jnp.bfloat16
GELU_A = math.sqrt(2.0 / math.pi)
GELU_B = 0.044715
LANES = 128
BLOCK = 256
PAIR = 2 * HEAD_DIM
SUM_ROWS = 48
ONES = 16
SAFE_SCORE = 60.0


def nn(left, right, precision=None):
    return lax.dot_general(
        left, right, (((1,), (0,)), ((), ())), preferred_element_type=F32, precision=precision
    )


def nt(left, right, precision=None):
    return lax.dot_general(
        left, right, (((1,), (1,)), ((), ())), preferred_element_type=F32, precision=precision
    )


def identity(size):
    rows = lax.broadcasted_iota(jnp.int32, (size, size), 0)
    columns = lax.broadcasted_iota(jnp.int32, (size, size), 1)
    return jnp.where(rows == columns, 1.0, 0.0).astype(BF16)


def turned(values):
    return nt(identity(values.shape[1]), values).astype(BF16)


def wide(column_tile, lanes):
    return jnp.concatenate([column_tile] * (lanes // LANES), axis=1)


def folded(values):
    pieces = [values[:, at : at + LANES] for at in range(0, values.shape[1], LANES)]
    return sum(pieces[1:], pieces[0])


def standardise(values):
    rows = values.shape[0]
    centred = values - jnp.sum(values, axis=0, keepdims=True) * (1.0 / rows)
    variance = jnp.sum(centred * centred, axis=0, keepdims=True) * (1.0 / rows)
    scale = lax.rsqrt(variance + 1e-06)
    return centred * scale, scale


def pre_norm_back(standard, scale, grad, gain):
    rows = standard.shape[0]
    inner = grad * gain
    first = jnp.sum(inner, axis=0, keepdims=True) * (1.0 / rows)
    second = jnp.sum(inner * standard, axis=0, keepdims=True) * (1.0 / rows)
    return scale * (inner - first - standard * second)


def part(mod_ref, index, lanes):
    return wide(mod_ref[index * D : (index + 1) * D, :], lanes)


def turn_into(source, out, at=0):
    for column in range(0, out.shape[0], BLOCK):
        width = min(BLOCK, out.shape[0] - column)
        out[column : column + width, :] = turned(source[:, at + column : at + column + width])


def prepare_first(mod, w_q_t, w_v_t, w_k, w_qkv, w_ada, b_ada, context):
    w_k[...] = w_qkv[:, D : 2 * D]
    turn_into(w_qkv, w_q_t)
    turn_into(w_qkv, w_v_t, 2 * D)
    values = nn(context[...], w_ada[...])[0:1] + b_ada
    for column in range(0, values.shape[1], LANES):
        tile = jnp.broadcast_to(values[:, column : column + LANES], (LANES, LANES))
        mod[column : column + LANES, :] = tile.T


def prepare_kernel(context, *refs):
    w_qkv, w_ada, b_ada, w_out, w_up, w_down = refs[:6]
    outs, scratch, sems = refs[8:19], refs[19:-1], refs[-1]
    sources = [w_qkv.at[0], w_ada.at[0], b_ada, w_out.at[0], w_up.at[0], w_down.at[0], w_qkv.at[1], w_ada.at[1]]
    copies = [
        pltpu.make_async_copy(source, target, sems.at[place])
        for place, (source, target) in enumerate(zip(sources, scratch))
    ]
    for copy in copies:
        copy.start()
    for copy in copies[:3]:
        copy.wait()
    prepare_first(*outs[0:4], scratch[0], scratch[1], scratch[2][0:1, :], context)
    for copy, source, out in zip(copies[3:6], scratch[3:6], outs[8:11]):
        copy.wait()
        turn_into(source, out)
    for copy in copies[6:]:
        copy.wait()
    prepare_first(*outs[4:8], scratch[6], scratch[7], scratch[2][1:2, :], context)


def prepare_rest_kernel(index, early, w_out, w_up, w_down, *outs):
    for weight, out in zip((w_out, w_up, w_down), outs):
        turn_into(weight.at[index], out)


def project(x, mod_ref, w_q_t, w_v_t, w_k, outs):
    q_out, kn_out, vt_out = outs
    lanes = x.shape[1]
    standard, _ = standardise(x)
    normed = (standard * (1.0 + part(mod_ref, 1, lanes)) + part(mod_ref, 0, lanes)).astype(BF16)
    vt_out[...] = nn(w_v_t[...], normed).astype(BF16)
    q_out[...] = (nn(w_q_t[...], normed) * HEAD_DIM ** (-0.5)).astype(BF16)
    for at in range(0, lanes, BLOCK):
        kn_out[at : at + BLOCK, :] = nn(turned(normed[:, at : at + BLOCK]), w_k[...]).astype(BF16)


def first_kernel(own, flip_x, flip_y, flip_xy, cot, cot_x, mod, w_q_t, w_v_t, w_k, cot_out, x_out, xb_out, *outs):
    rows = cot.shape[0]
    cot_out[:rows, :] = cot[...]
    cot_out[rows:, :] = cot_x[...]
    for index, ref in enumerate((own, flip_x, flip_y, flip_xy)):
        rows = ref.shape[0]
        flat = turned(ref[...])
        xb_out[:, index * rows : (index + 1) * rows] = flat
        x_out[:, index * rows : (index + 1) * rows] = flat.astype(F32)
    project(x_out[...], mod, w_q_t, w_v_t, w_k, outs)


def head_rows(head):
    return slice(head * HEAD_DIM, (head + 1) * HEAD_DIM)


def pair_columns(head):
    return slice(head // 2 * PAIR, (head // 2 + 1) * PAIR)


def padded(rows, head):
    zeros = jnp.zeros_like(rows)
    return jnp.concatenate([rows, zeros] if head % 2 == 0 else [zeros, rows], axis=0)


def query_top(q):
    square = q[...].astype(F32)
    square = square * square
    norms = [jnp.sum(square[head_rows(head)], axis=0, keepdims=True) for head in range(HEADS)]
    return jnp.max(functools.reduce(jnp.maximum, norms), axis=1, keepdims=True)


def key_top(kn):
    first = lax.broadcasted_iota(jnp.int32, (D, LANES), 1) * HEAD_DIM
    row = lax.broadcasted_iota(jnp.int32, (D, LANES), 0)
    pick = jnp.where((row >= first) & (row < first + HEAD_DIM), 1.0, 0.0).astype(BF16)
    square = kn[...].astype(F32)
    norms = nn((square * square).astype(BF16), pick)
    return jnp.max(jnp.max(norms, axis=0, keepdims=True), axis=1, keepdims=True) * 1.02


def value_rows(vt, rows, at):
    values = vt[rows, at]
    return jnp.concatenate([values, jnp.ones((ONES, values.shape[1]), BF16)], axis=0)


def attend_plain(q, kn, vt, put):
    chunks = [slice(at, at + BLOCK) for at in range(0, kn.shape[0], BLOCK)]

    def score(head):
        return nn(kn[:, pair_columns(head)], padded(q[head_rows(head), :], head))

    totals = {}

    def finish(head, at, probs):
        term = nn(value_rows(vt, head_rows(head), at), probs)
        totals[head] = totals[head] + term if head in totals else term
        if at == chunks[-1]:
            put(head, totals[head])

    waiting = None
    following = score(0)
    for head in range(HEADS):
        scores = following
        for at in chunks:
            if at == chunks[0] and head + 1 < HEADS:
                following = score(head + 1)
            if waiting is not None:
                finish(*waiting)
            waiting = (head, at, jnp.exp(scores[at]).astype(BF16))
    finish(*waiting)


def attend_own_kernel(early, *refs):
    q, kn, vt, *refs = refs[early:]
    passing = []
    if len(refs) > 2:
        *passing, sums, tops, passed = refs
    else:
        sums, tops = refs
    at = 0
    for source in passing:
        rows = source.shape[0]
        passed[at : at + rows, :] = source[...]
        at += rows

    def put(head, total):
        sums[head] = total

    query, key = query_top(q), key_top(kn)
    tops[0:8, :] = jnp.broadcast_to(query, (8, LANES))
    tops[8:16, :] = jnp.broadcast_to(key, (8, LANES))

    @pl.when(jnp.max(query * key) < SAFE_SCORE**2)
    def _():
        attend_plain(q, kn, vt, put)


def forward_kernel(last, early, *refs):
    refs = refs[early:]
    if last:
        rollout, x, x_step, *refs = refs
    else:
        x, *refs = refs
    q, kn_own, kn_far, vt_own, vt_far, sums, tops, mod, w_out_t, w_up_t, w_down_t, *refs = refs
    if not last:
        mod_next, w_q_t, w_v_t, w_k, *refs = refs
    lse, mixed, attended, middle, hidden, slope, branch, *refs = refs
    if last:
        (final,) = refs
    else:
        x_next, xb_next, *next_outs = refs
    patches = x.shape[1]
    bound = tops[0:1, 0:1] * jnp.maximum(tops[8:9, 0:1], key_top(kn_far))
    safe = jnp.max(bound) < SAFE_SCORE**2

    def put(head, total):
        total = sums[head] + total
        weight = total[HEAD_DIM : HEAD_DIM + 1]
        mixed[head_rows(head), :] = (total[:HEAD_DIM] * (1.0 / weight)).astype(BF16)
        lse[head : head + 1, :] = jnp.log(weight)

    @pl.when(safe)
    def _():
        attend_plain(q, kn_far, vt_far, put)

    @pl.when(jnp.logical_not(safe))
    def _():
        def pair_heads(pair, _):
            columns = pl.ds(pl.multiple_of(pair * PAIR, PAIR), PAIR)
            for head in range(2):
                rows = pl.ds(pl.multiple_of(pair * PAIR + head * HEAD_DIM, HEAD_DIM), HEAD_DIM)
                query = padded(q[rows, :], head)
                scores = [nn(kn[:, columns], query) for kn in (kn_own, kn_far)]
                tops = [jnp.max(score, axis=0, keepdims=True) for score in scores]
                top = jnp.maximum(*tops)
                total = None
                for score, vt in zip(scores, (vt_own, vt_far)):
                    term = nn(value_rows(vt, rows, slice(None)), jnp.exp(score - top).astype(BF16))
                    total = term if total is None else total + term
                weight = total[HEAD_DIM : HEAD_DIM + 1]
                mixed[rows, :] = (total[:HEAD_DIM] * (1.0 / weight)).astype(BF16)
                lse[pl.ds(pair * 2 + head, 1), :] = top + jnp.log(weight)
            return 0

        lax.fori_loop(0, HEADS // 2, pair_heads, 0)

    att = nn(w_out_t[...], mixed[...])
    attended[...] = att.astype(BF16)
    mid = x[...] + part(mod, 2, patches) * att
    middle[...] = mid.astype(BF16)
    standard, _ = standardise(mid)
    hidden_in = (standard * (1.0 + part(mod, 4, patches)) + part(mod, 3, patches)).astype(BF16)
    chunks = [slice(at, at + BLOCK) for at in range(0, w_up_t.shape[0], BLOCK)]

    def up(place):
        wide_rows = slice(place * BLOCK, (place + 2) * BLOCK)
        both = nn(w_up_t[wide_rows, :], hidden_in)
        return [both[:BLOCK], both[BLOCK:]]

    down = None
    waiting = None
    acts = up(0)
    for place, rows in enumerate(chunks):
        act = acts[place]
        if place % 2 == 0 and place + 2 < len(chunks):
            acts += up(place + 2)
        if place > 0:
            term = nn(w_down_t[:, chunks[place - 1]], waiting)
            down = term if down is None else down + term
        act = act.astype(BF16)
        inner = GELU_A + (GELU_A * GELU_B) * (act * act)
        half = 0.5 + 0.5 * jnp.tanh(act * inner)
        waiting = gelu = act * half
        hidden[rows, :] = waiting
        slope[rows, :] = (half + (gelu - gelu * half) * (6.0 * inner - 4.0 * GELU_A))
    down = down + nn(w_down_t[:, chunks[-1]], waiting)
    branch[...] = down.astype(BF16)
    out = mid + part(mod, 5, patches) * down
    if last:
        own = final.shape[0]
        final[...] = jnp.where(rollout[0] > 1, out[:, :own], x_step[:, :own]).T
    else:
        x_next[...] = out
        xb_next[...] = out.astype(BF16)
        project(out, mod_next, w_q_t, w_v_t, w_k, next_outs)


def put_grads(left_ref, right, where, count, at, mine, other, before):
    rows = [left_ref[pl.ds(pl.multiple_of(where[place] * count, 16), count), :] for place in range(2)]
    product = nt(jnp.concatenate(rows, axis=0), right)
    for column in range(0, product.shape[1], LANES):
        low = product[:count, column : column + LANES]
        high = product[count:, column : column + LANES]
        if before is not None:
            low = low + before[0][at : at + count, :]
            high = high + before[1][at : at + count, :]
        mine[at : at + count, :] = low.astype(mine.dtype)
        other[at : at + count, :] = high.astype(other.dtype)
        at += count


def dense_back_kernel(has_close, has_open, has_before, start, layers, waits, *refs):
    refs = list(refs)

    def take(count):
        taken = refs[:count]
        del refs[:count]
        return taken

    take(waits)
    where, rollout = take(2)
    active = jnp.where(rollout[0] > 1, 1.0, 0.0)
    close_before = open_before = None
    if has_close:
        d_own, d_got, dq, d_mid_in, x_in, mod_in, w_qkv = take(7)
        w_qkv = w_qkv.at[layers[0]]
        if has_before[0]:
            close_before = take(3)
    if start == "first":
        cots = take(2)
    elif start == "cross":
        cots = take(1)
    if has_open:
        mixed, attended, middle, hidden, slope, branch, mod, w_out, w_up, w_down = take(10)
        w_out, w_up, w_down = (ref.at[layers[1]] for ref in (w_out, w_up, w_down))
        if has_before[1]:
            open_before = take(3)
    else:
        (lines,) = take(1)
    if has_close:
        close_mine, close_other, close_mods = take(3)
    if start == "first":
        (cot_out,) = take(1)
    if has_open:
        open_mine, open_other, open_mods, d_mid_out, do_out, cen_out = take(6)
    else:
        g_out, sums_out = take(2)
        sums_at = close_before[1].shape[0]
    if has_close:
        grads_scr, normed_scr = take(2)
    if has_open:
        pg_scr, hin_scr = take(2)

    patches = middle.shape[1] if has_open else x_in.shape[1]
    totals = {}

    def add_sums(name, values):
        totals[name] = totals[name] + folded(values) if name in totals else folded(values)

    def put_sums(out, before, names):
        for place, name in enumerate(names):
            rows = slice(place * D, (place + 1) * D)
            out[rows, :] = totals[name] + before[2][rows, :] if before else totals[name]

    if start == "first":
        for index, ref in enumerate(cots):
            rows = ref.shape[0]
            cot_out[:, index * rows : (index + 1) * rows] = turned(ref[...])

    def close(at):
        standard, scale = standardise(x_in[:, at].astype(F32))
        gain = 1.0 + part(mod_in, 1, patches)
        normed_scr[:, at] = (standard * gain + part(mod_in, 0, patches)).astype(BF16)
        for third in range(3):
            if third == 0:
                piece = dq[:, at]
            else:
                rows = slice((third - 1) * D, third * D)
                piece = d_own[rows, at] + d_got[rows, at]
            grads_scr[third * D : (third + 1) * D, at] = piece
        back = nn(w_qkv[...], grads_scr[:, at])
        put_grads(normed_scr, grads_scr[...], where, D // 8, 0, close_mine, close_other, close_before)
        add_sums("shift_a", back)
        add_sums("scale_a", back * standard)
        g = d_mid_in[:, at] + pre_norm_back(standard, scale, back, gain)
        if start == "cross":
            g = g + (1.0 - active) * cots[0][:, at].astype(F32)
        return g

    def dense(at, g):
        standard, scale = standardise(middle[:, at].astype(F32))
        gain = 1.0 + part(mod, 4, patches)
        hin_scr[:, at] = (standard * gain + part(mod, 3, patches)).astype(BF16)
        branch_grad = (part(mod, 5, patches) * g).astype(BF16)
        add_sums("gate_m", g * branch[:, at].astype(F32))
        chunks = [slice(start, start + BLOCK) for start in range(0, w_down.shape[0], BLOCK)]
        back = None
        waiting = None

        def down(place):
            wide_rows = slice(place * BLOCK, (place + 2) * BLOCK)
            both = nn(w_down[wide_rows, :], branch_grad)
            return [both[:BLOCK], both[BLOCK:]]

        hidden_grads = down(0)
        for place, rows in enumerate(chunks):
            hidden_grad = hidden_grads[place]
            if place % 2 == 0 and place + 2 < len(chunks):
                hidden_grads += down(place + 2)
            if place > 0:
                term = nn(w_up[:, chunks[place - 1]], waiting)
                back = term if back is None else back + term
            waiting = slope[rows, at] * hidden_grad.astype(BF16)
            pg_scr[rows, at] = waiting
        back = back + nn(w_up[:, chunks[-1]], waiting)
        count = w_down.shape[0] // 8
        start_at = count * (D // LANES)
        put_grads(hidden, branch_grad, where, count, 0, open_mine, open_other, open_before)
        put_grads(hin_scr, pg_scr[...], where, D // 8, start_at, open_mine, open_other, open_before)
        add_sums("shift_m", back)
        add_sums("scale_m", back * standard)
        d_mid = g + pre_norm_back(standard, scale, back, gain)
        d_mid_out[:, at] = d_mid
        att_grad = (part(mod, 2, patches) * d_mid).astype(BF16)
        mixed_grad = nn(w_out[...], att_grad).astype(BF16)
        do_out[:, at] = mixed_grad
        start_at += (w_up.shape[1] // LANES) * (D // 8)
        put_grads(mixed, att_grad, where, D // 8, start_at, open_mine, open_other, open_before)
        add_sums("gate_a", d_mid * attended[:, at].astype(F32))
        product = mixed_grad.astype(F32) * mixed[:, at].astype(F32)
        for head in range(HEADS):
            cen_out[head : head + 1, at] = jnp.sum(product[head_rows(head)], axis=0, keepdims=True)

    at = slice(0, patches)
    g = close(at) if has_close else cot_out[:, at].astype(F32) * active
    if has_open:
        dense(at, g)
    else:
        g_out[...] = g[:, : g_out.shape[0]].T
    if has_close:
        put_sums(close_mods, close_before, ("shift_a", "scale_a"))
    if has_open:
        put_sums(open_mods, open_before, ("gate_a", "shift_m", "scale_m", "gate_m"))
    else:
        sums_out[...] = lines[...]
        put_lines(sums_out, 0, close_mods[...])
        close_other[sums_at:, :] = sums_out[...].astype(BF16)


def attend_back_kernel(has_before, waits, q, kn, vt, lse, d_out, centre, *refs):
    if has_before:
        before, *refs = refs
    d_kv, dq_out, kt_scr, vn_scr = refs[waits:]
    for column in range(0, D, LANES):
        kt_scr[column : column + LANES, :] = turned(kn[:, column : column + LANES])
    for column in range(0, vt.shape[1], BLOCK):
        vn_scr[column : column + BLOCK, :] = turned(vt[:, column : column + BLOCK])

    steps = [(head, slice(at, at + BLOCK)) for head in range(HEADS) for at in range(0, kn.shape[0], BLOCK)]

    def score(head, at):
        columns = pair_columns(head)
        rows = head_rows(head)
        return nn(kn[at, columns], padded(q[rows, :], head)), nn(vn_scr[at, columns], padded(d_out[rows, :], head))

    totals = {}

    def finish(head, at, probs, score_grads):
        rows = head_rows(head)
        d_kv[D + rows.start : D + rows.stop, at] = nt(d_out[rows, :], probs).astype(d_kv.dtype)
        d_kv[rows, at] = nt(q[rows, :], score_grads).astype(d_kv.dtype)
        term = nn(kt_scr[rows, at], score_grads)
        if head not in totals:
            totals[head] = before[rows, :] + term if has_before else term
            return
        term = totals[head] + term
        if has_before:
            term = term * HEAD_DIM ** (-0.5)
        dq_out[rows, :] = term.astype(dq_out.dtype)

    waiting = None
    following = score(*steps[0])
    for place, (head, at) in enumerate(steps):
        scores, prob_grads = following
        if place + 1 < len(steps):
            following = score(*steps[place + 1])
        if waiting is not None:
            finish(*waiting)
        probs = jnp.exp(scores - lse[head : head + 1, :])
        score_grads = (probs * (prob_grads - centre[head : head + 1, :])).astype(BF16)
        waiting = (head, at, probs.astype(BF16), score_grads)
    finish(*waiting)


def split_kernel(waits, where, *refs):
    *halves, keep, sent, total_scr = refs[waits:]
    rows_half = keep.shape[0]
    at = 0
    for mine, other in zip(halves[::2], halves[1::2]):
        rows = mine.shape[0]
        total_scr[at : at + rows, :] = mine[...] + other[...].astype(F32)
        at += rows
    if at < total_scr.shape[0]:
        total_scr[at:, :] = jnp.zeros((total_scr.shape[0] - at, LANES), F32)
    odd = where[3]
    keep[...] = total_scr[pl.ds(pl.multiple_of(odd * rows_half, 16), rows_half), :]
    sent[...] = total_scr[pl.ds(pl.multiple_of((1 - odd) * rows_half, 16), rows_half), :].astype(BF16)


def pair_sum_kernel(waits, *refs):
    refs = refs[waits:]
    count = len(refs) // 3
    for keep, got, out in zip(refs[:count], refs[count : 2 * count], refs[2 * count :]):
        out[...] = (keep[...].astype(F32) + got[...].astype(F32)).astype(BF16)


def put_lines(out, row, values):
    ones = jnp.ones((16, LANES), BF16)
    high = values.astype(BF16)
    low = (values - high.astype(F32)).astype(BF16)
    line = (nt(ones, high) + nt(ones, low))[0:1]
    for column in range(0, line.shape[1], LANES):
        out[row : row + 1, :] = line[:, column : column + LANES]
        row += 1
    return row


def lines_kernel(early, context, *refs):
    *sums, out = refs
    out[...] = jnp.zeros_like(out)
    row = 2 * D // LANES
    for ref in sums:
        row = put_lines(out, row, ref[...])
    for column in range(0, D, LANES):
        out[row : row + 1, :] = context[0:1, column : column + LANES].astype(F32)
        row += 1


def join_kernel(sum_count, early, other_early, mine, sums, got, out):
    rows = mine.shape[0]
    out[:rows, :] = (mine[...] + got[:rows, :].astype(F32)).astype(BF16)
    other = got[rows:, :].astype(F32)
    summed = lax.broadcasted_iota(jnp.int32, (SUM_ROWS, LANES), 0) < sum_count
    out[rows:, :] = (sums[...] + jnp.where(summed, other, 0.0)).astype(BF16)


def pair_kernel(rows, where, own, got, out):
    out[:rows, :] = (own[:rows, :].astype(F32) + got[:rows, :].astype(F32)).astype(BF16)
    odd = where[3]
    size = SUM_ROWS
    out[pl.ds(pl.multiple_of(rows + odd * size, 16), size), :] = own[rows:, :]
    out[pl.ds(pl.multiple_of(rows + (1 - odd) * size, 16), size), :] = got[rows:, :]


def gather_kernel(layer, where, own, got, *refs):
    outs, qkv_out, rows_scr, scratch, sems = refs[-9:-6], refs[-6], refs[-5], refs[-4:-1], refs[-1]
    if layer == 1:
        outs = refs[-8:-5]
    half = own.shape[0]
    rows_scr[pl.ds(pl.multiple_of(where[3] * half, 16), half), :] = own[...]
    rows_scr[pl.ds(pl.multiple_of((1 - where[3]) * half, 16), half), :] = got[...]
    at = 0
    copies = []
    for place, (out, held) in enumerate(zip(outs, scratch)):
        rows = held.shape[0]
        for column in range(0, held.shape[1], LANES):
            held[:, column : column + LANES] = rows_scr[at : at + rows, :].astype(F32)
            at += rows
        copies.append(pltpu.make_async_copy(held, out.at[layer], sems.at[place]))
        copies[-1].start()
    if layer == 0:
        rows = qkv_out.shape[0]
        for column in range(0, qkv_out.shape[1], LANES):
            qkv_out[:, column : column + LANES] = rows_scr[at : at + rows, :].astype(F32)
            at += rows
    for copy in copies:
        copy.wait()


def finish_kernel(item_count, where, own, got, qkv_1, qkv_out, ada_out, bias_out, shift_out, sum_scr, bias_scr, shift_scr):
    layers = 2
    device, high = where[0], where[4]
    slice_rows = qkv_out.shape[1]
    close_rows = slice_rows * (3 * D // LANES)
    for other in range(2):
        rows = slice(close_rows + other * SUM_ROWS, close_rows + (other + 1) * SUM_ROWS)
        sum_scr[2 * high + other] = own[rows, :].astype(F32)
        sum_scr[2 * (1 - high) + other] = got[rows, :].astype(F32)
    qkv_out[1] = qkv_1[...]
    for tile in range(3 * D // LANES):
        rows = slice(tile * slice_rows, (tile + 1) * slice_rows)
        total = own[rows, :].astype(F32) + got[rows, :].astype(F32)
        qkv_out[0, :, tile * LANES : (tile + 1) * LANES] = total
    tiles = 6 * D // LANES
    contexts = []
    for other in range(item_count):
        line = jnp.concatenate([sum_scr[other, layers * tiles + c : layers * tiles + c + 1, :] for c in range(3)], axis=1)
        contexts.append(line)
    square = jnp.concatenate(contexts + [jnp.zeros((8 - item_count, D), F32)], axis=0)
    spot = lax.broadcasted_iota(jnp.int32, (slice_rows, D), 1)
    want = lax.broadcasted_iota(jnp.int32, (slice_rows, D), 0) + device * slice_rows
    pick = jnp.where(spot == want, 1.0, 0.0).astype(BF16)
    columns = nt(pick, square.astype(BF16))
    bias_rows = bias_out.shape[1]
    for index in range(layers):
        flats = []
        for tile in range(tiles):
            row = index * tiles + tile
            total = None
            flat = None
            for other in range(item_count):
                line = sum_scr[other, row : row + 1, :]
                term = columns[:, other : other + 1] * line
                total = term if total is None else total + term
                flat = line if flat is None else flat + line
            ada_out[index, :, tile * LANES : (tile + 1) * LANES] = total
            flats.append(flat)
        flat = jnp.concatenate(flats, axis=1)
        for place in range(flat.shape[1] // bias_rows):
            bias_scr[place, index : index + 1, :] = flat[:, place * bias_rows : (place + 1) * bias_rows]
            at = 3 * D + place * slice_rows
            shift_scr[place, index : index + 1, :] = flat[:, at : at + slice_rows]
    bias_out[...] = bias_scr[device]
    shift_out[...] = shift_scr[device]


VMEM = pl.BlockSpec(memory_space=pltpu.VMEM)
SMEM = pl.BlockSpec(memory_space=pltpu.SMEM)
ANY = pl.BlockSpec(memory_space=pl.ANY)
HBM = pl.BlockSpec(memory_space=pltpu.HBM)


def layer_block(array, index):
    return pl.BlockSpec((None,) + array.shape[1:], lambda step: (index,) + (0,) * (array.ndim - 1))


def call(body, args, outs, scratch=(), flops=0, name=None, direct=0, aliases=None):
    arrays = [arg[0] if isinstance(arg, tuple) else arg for arg in args]
    specs = [arg[1] if isinstance(arg, tuple) else VMEM for arg in args]
    return pl.pallas_call(
        body,
        out_shape=[jax.ShapeDtypeStruct(shape, kind) for shape, kind in outs],
        in_specs=specs,
        out_specs=[ANY] * direct + [VMEM] * (len(outs) - direct),
        input_output_aliases=aliases or {},
        scratch_shapes=[one if not isinstance(one, tuple) else pltpu.VMEM(*one) for one in scratch],
        compiler_params=pltpu.CompilerParams(vmem_limit_bytes=VMEM_LIMIT),
        cost_estimate=pl.CostEstimate(flops=flops, bytes_accessed=0, transcendentals=0),
        name=name,
    )(*arrays)


VMEM_LIMIT = 14 * 1024 * 1024


def fast_shards(
    lat_count, lon_count, item_count,
    fields, lead_index, rollout, w_qkv, w_out, w_up, w_down, w_ada, b_ada, cotangent,
):
    _, rows_dev, cols_dev, width = fields.shape
    local = rows_dev * cols_dev
    layers = w_qkv.shape[0]
    ff = w_up.shape[2]
    patches = 4 * local
    device = lax.axis_index("lat") * lon_count + lax.axis_index("lon")
    item = lax.axis_index("item")
    where = jnp.stack([device, device ^ 1, item, item & 1, item >> 1]).astype(jnp.int32)

    def plane_flip(value, flip_lat, flip_y):
        pairs = [
            (a * lon_count + b, (a ^ flip_lat) * lon_count + (b ^ (2 * flip_y)))
            for a in range(lat_count)
            for b in range(lon_count)
        ]
        return lax.ppermute(value, ("lat", "lon"), pairs)

    def swap(value):
        return lax.ppermute(value, "lon", [(index, index ^ 1) for index in range(lon_count)])

    def with_item(value, flip):
        return lax.ppermute(value, "item", [(index, index ^ flip) for index in range(item_count)])

    def plane_parts(value):
        return [value, plane_flip(value, 1, 0), plane_flip(value, 0, 1), plane_flip(value, 1, 1)]

    field_parts = plane_parts(fields.reshape(local, width))

    lead = lax.optimization_barrier(jnp.broadcast_to(lead_index[:, None], (16, width // 2)))
    context = jax.nn.silu(embedding(lead)).astype(BF16)
    square = (width, patches)
    natural = (patches, width)
    weights = (w_qkv, w_ada, b_ada, w_out, w_up, w_down)
    weights = [(pltpu.with_memory_space_constraint(value, pltpu.HBM), HBM) for value in weights]
    first_outs = [((6 * width, LANES), F32)] + [((width, width), BF16)] * 3
    rest_outs = [((width, width), BF16), ((ff, width), BF16), ((width, ff), BF16)]
    first_fetch = [((width, 3 * width), BF16), ((width, 6 * width), BF16)]
    rest_fetch = [((width, width), BF16), ((width, ff), BF16), ((ff, width), BF16)]
    prepared = call(
        prepare_kernel,
        [context, *weights, (where, SMEM), (rollout, SMEM)],
        first_outs * 2 + rest_outs,
        first_fetch + [(b_ada.shape, F32)] + rest_fetch + first_fetch + [pltpu.SemaphoreType.DMA((8,))],
        name="prepare",
    )
    first_parts = [prepared[0:4], prepared[4:8]]
    rest_parts = [prepared[8:11]]
    mods = [one[0] for one in first_parts]

    project_outs = [(square, F32), (square, BF16), (square, BF16), (natural, BF16), (square, BF16)]
    dense_flops = 2 * patches * (width * 3 * width + width * width + 2 * width * ff)
    score_flops = 2 * patches * 2 * patches * width * 4
    cot = cotangent.reshape(local, width)
    cot, x, xb, *projected = call(
        first_kernel,
        [*field_parts, cot, plane_flip(cot, 1, 0), *first_parts[0]],
        [((2 * local, width), BF16)] + project_outs,
        flops=2 * patches * width * 4 * width,
        name="first",
    )
    saved = []
    for step in range(STEPS):
        for index in range(layers):
            q, kn, vt = projected
            if len(rest_parts) == index:
                rest_parts.append(
                    call(
                        functools.partial(prepare_rest_kernel, index),
                        [(kn, ANY), w_out, w_up, w_down],
                        rest_outs,
                        name="prepare_rest",
                    )
                )
            kn_far, vt_far = swap(kn), swap(vt)
            early = [w_up] if len(rest_parts) == index + 1 < layers else []
            passing = [cot] if step == STEPS - 1 and index == 0 else []
            passed = [((2 * local, width), BF16)] if passing else []
            sums, tops, *passed = call(
                functools.partial(attend_own_kernel, len(early)),
                early + [q, kn, vt] + passing,
                [((HEADS, HEAD_DIM + ONES, patches), F32), ((16, LANES), F32)] + passed,
                flops=10 * score_flops,
                name="forward_own",
            )
            if passed:
                cot_parts = [passed[0], plane_flip(passed[0], 0, 1)]
            last = step == STEPS - 1 and index == layers - 1
            if index == 0 and step > 0:
                x_step = x
            following = list(first_parts[(index + 1) % layers])
            early = [w_down] if len(rest_parts) == index + 1 < layers else []
            lse, mixed, attended, middle, hidden, slope, branch, *results = call(
                functools.partial(forward_kernel, last, len(early)),
                early
                + ([(rollout, SMEM), x, x_step] if last else [x])
                + [q, kn, kn_far, vt, vt_far, sums, tops, mods[index], *rest_parts[index]]
                + ([] if last else following),
                [
                    ((HEADS, patches), F32),
                    (square, BF16),
                    (square, BF16),
                    (square, BF16),
                    ((ff, patches), BF16),
                    ((ff, patches), BF16),
                    (square, BF16),
                ]
                + ([((local, width), F32)] if last else project_outs),
                flops=dense_flops + 2 * score_flops,
                name="forward",
            )
            saved.append((xb, [mixed, attended, middle, hidden, slope, branch], (q, kn, kn_far, vt, vt_far, lse)))
            if last:
                final = results[0]
            else:
                x, xb, *projected = results

    slice_rows = width // 8
    open_rows = 2 * (ff // 8) * (width // LANES) + slice_rows * (width // LANES)
    close_rows = slice_rows * (3 * width // LANES)
    order = [(step, index) for step in reversed(range(STEPS)) for index in reversed(range(layers))]
    open_done = [None] * layers
    close_done = [None] * layers
    pending = None
    for place in range(len(order) + 1):
        has_close = pending is not None
        has_open = place < len(order)
        use = [order[place - 1][1], order[place][1] if has_open else 0]
        waits = []
        if has_close and close_done[use[0]]:
            waits = [pair_1] if has_open else []
        args = [(value, ANY) for value in waits] + [(where, SMEM), (rollout, SMEM)]
        outs = []
        scratch = []
        has_before = [False, False]
        start = ""
        if has_close:
            args += pending
            if close_done[use[0]] is not None:
                has_before[0] = True
                args += close_done[use[0]]
            outs += [((close_rows, LANES), F32)]
            sent_rows = close_rows + (0 if has_open else SUM_ROWS)
            outs += [((sent_rows, LANES), BF16 if has_before[0] else F32), ((2 * width, LANES), F32)]
            scratch += [((3 * width, patches), BF16), (square, BF16)]
        if place == 0:
            start = "first"
            args += cot_parts
            outs += [(square, BF16)]
        elif has_open and order[place][0] != order[place - 1][0]:
            start = "cross"
            args += [cot_t]
        if has_open:
            step, index = order[place]
            xb, kept, heads = saved[step * layers + index]
            args += kept + [mods[index], w_out, w_up, w_down]
            if open_done[index] is not None:
                has_before[1] = True
                args += open_done[index]
            outs += [
                ((open_rows, LANES), F32),
                ((open_rows, LANES), BF16 if has_before[1] else F32),
                ((4 * width, LANES), F32),
                (square, F32),
                (square, BF16),
                ((HEADS, patches), F32),
            ]
            scratch += [((ff, patches), BF16), (square, BF16)]
        else:
            args += [lines]
            outs += [((local, width), F32), ((SUM_ROWS, LANES), F32)]
        results = list(
            call(
                functools.partial(dense_back_kernel, has_close, has_open, has_before, start, use, len(waits)),
                args,
                outs,
                scratch,
                flops=2 * dense_flops if has_open else 0,
                name="dense_back" if has_open else "close_back",
            )
        )
        if has_close:
            close_done[use[0]] = results[:3]
            del results[:3]
        if start == "first":
            cot_t = results.pop(0)
        if not has_open:
            gradient, line = results
            break
        open_done[index] = results[:3]
        d_mid, d_out, centre = results[3:]
        q, kn, kn_far, vt, vt_far, lse = heads
        halves = [open_done[index][0], open_done[index][1]]
        if index == 0:
            halves += [close_done[1][0], close_done[1][1]]
        half_rows = -(-sum(half.shape[0] for half in halves[::2]) // 32) * 16

        def split(waits):
            pieces = [half if place % 2 == 0 else swap(half) for place, half in enumerate(halves)]
            return call(
                functools.partial(split_kernel, len(waits)),
                [(where, SMEM), *waits, *pieces],
                [((half_rows, LANES), F32), ((half_rows, LANES), BF16)],
                [((2 * half_rows, LANES), F32)],
                name="split",
            )

        def pair_sum(late, keeps, gots, others=()):
            outs = [(keep.shape, BF16) for keep in keeps]
            body = functools.partial(pair_sum_kernel, 1 + len(others))
            return call(body, [(late, ANY), *others, *keeps, *gots], outs, name="pair_sum")

        waits = []
        if has_before[1] and index == 0:
            pair_got_1 = with_item(pair_1, 2)
            lines = call(
                lines_kernel,
                [(pair_got_1, ANY), context, open_done[0][2], close_done[1][2], open_done[1][2]],
                [((SUM_ROWS, LANES), F32)],
                flops=10 * score_flops,
                name="lines",
            )[0]
            keep, sent = split([(lines, ANY)])
            got_0 = with_item(sent, 1)
            waits = [keep]
        d_far, dq = call(
            functools.partial(attend_back_kernel, False, len(waits)),
            [q, kn_far, vt_far, lse, d_out, centre] + [(value, ANY) for value in waits],
            [((2 * width, patches), BF16), (square, F32)],
            [(square, BF16), (natural, BF16)],
            flops=10 * score_flops,
            name="attend_far",
        )
        d_got = swap(d_far)
        waits = []
        if has_before[1]:
            if index == 1:
                keep, sent = split([(d_far, ANY)])
                got_1 = with_item(sent, 1)
                waits = [keep]
            else:
                (item_1,) = pair_sum(d_far, [pair_1], [pair_got_1])
                item_got_1 = with_item(item_1, 1)
                (pair_0,) = pair_sum(d_far, [keep], [got_0], [(item_1, ANY)])
                pair_got_0 = with_item(pair_0, 2)
                waits = [pair_0]
        d_own, dq = call(
            functools.partial(attend_back_kernel, True, len(waits)),
            [q, kn, vt, lse, d_out, centre, dq] + [(value, ANY) for value in waits],
            [((2 * width, patches), BF16), (square, BF16)],
            [(square, BF16), (natural, BF16)],
            flops=10 * score_flops,
            name="attend_own",
        )
        if has_before[1] and index == 1:
            (pair_1,) = pair_sum(dq, [keep], [got_1])
        pending = [d_own, d_got, dq, d_mid, xb, mods[index], w_qkv]

    message = call(
        functools.partial(join_kernel, layers * 6 * width // LANES),
        [(pair_got_0, ANY), (item_got_1, ANY), close_done[0][0], line, swap(close_done[0][1])],
        [((close_rows + SUM_ROWS, LANES), BF16)],
        name="join",
    )[0]
    message_got = with_item(message, 1)
    stacks = [
        ((layers, ff // 8, width), F32),
        ((layers, slice_rows, ff), F32),
        ((layers, slice_rows, width), F32),
    ]
    held = [(shape[1:], kind) for shape, kind in stacks]
    sems = [pltpu.SemaphoreType.DMA((3,))]
    stacked = call(
        functools.partial(gather_kernel, 1),
        [(where, SMEM), item_1, item_got_1],
        stacks,
        [((2 * pair_1.shape[0], LANES), BF16)] + held + sems,
        name="gather",
        direct=3,
    )
    early = (pltpu.with_memory_space_constraint(stacked[2], pltpu.HBM), HBM)
    (item_0,) = pair_sum(message_got, [pair_0], [pair_got_0], [early])
    message = call(
        functools.partial(pair_kernel, close_rows),
        [(where, SMEM), message, message_got],
        [((close_rows + 2 * SUM_ROWS, LANES), BF16)],
        name="pair",
    )[0]
    down_grad, up_grad, out_grad, qkv_1 = call(
        functools.partial(gather_kernel, 0),
        [(where, SMEM), item_0, with_item(item_0, 1)] + [(value, ANY) for value in stacked],
        stacks + [((slice_rows, 3 * width), F32)],
        [((2 * pair_0.shape[0], LANES), BF16)] + held + sems,
        name="gather",
        direct=3,
        aliases={3: 0, 4: 1, 5: 2},
    )
    bias_rows = 6 * width // 8
    qkv_grad, ada_grad, bias_grad, shift_grad = call(
        functools.partial(finish_kernel, item_count),
        [(where, SMEM), message, with_item(message, 2), qkv_1],
        [
            ((layers, slice_rows, 3 * width), F32),
            ((layers, slice_rows, 6 * width), F32),
            ((layers, bias_rows), F32),
            ((layers, slice_rows), F32),
        ],
        [
            ((item_count, SUM_ROWS, LANES), F32),
            ((8, layers, bias_rows), F32),
            ((8, layers, slice_rows), F32),
        ],
        name="finish",
    )
    field_shape = (1, rows_dev, cols_dev, width)
    return (
        final.reshape(field_shape),
        gradient.reshape(field_shape),
        qkv_grad,
        out_grad,
        up_grad,
        down_grad,
        ada_grad,
        bias_grad,
        shift_grad,
    )


def solution(mesh):
    lat_count, lon_count, item_count = mesh.shape["lat"], mesh.shape["lon"], mesh.shape["item"]
    if lat_count == 2 and lon_count == 4:
        body = functools.partial(fast_shards, lat_count, lon_count, item_count)
    else:
        body = shards
    return jax.shard_map(
        body,
        mesh=mesh,
        in_specs=(
            P("item", "lat", "lon", None),
            P("item"),
            P("item"),
            P(),
            P(),
            P(),
            P(),
            P(),
            P(),
            P("item", "lat", "lon", None),
        ),
        out_specs=(
            P("item", "lat", "lon", None),
            P("item", "lat", "lon", None),
            P(None, ("lat", "lon"), None),
            P(None, ("lat", "lon"), None),
            P(None, ("lat", "lon"), None),
            P(None, ("lat", "lon"), None),
            P(None, ("lat", "lon"), None),
            P(None, ("lat", "lon")),
            P(None, ("lat", "lon")),
        ),
        check_vma=False,
    )
```

```python
import functools
import math

import jax
import jax.numpy as jnp
from jax import lax
from jax.experimental import pallas as pl
from jax.experimental.pallas import tpu as pltpu
from jax.sharding import PartitionSpec as P

D = 384
HEADS = 6
HEAD_DIM = 64
STEPS = 2


def shortened(shard):
    return jax.tree.map(lambda a: a.astype(jnp.bfloat16) if a.dtype == jnp.float32 else a, shard)


def embedding(lead):
    half_width = D // 2
    lead_hours = 6.0 * (lead.astype(jnp.float32) + 1.0)
    frequencies = jnp.exp(
        -math.log(10000.0) * jnp.arange(half_width, dtype=jnp.float32) / half_width
    )
    angles = lead_hours * frequencies
    return jnp.concatenate([jnp.sin(angles), jnp.cos(angles)], axis=-1)


def pre_norm(values, shift_part, scale_part):
    centred = values - jnp.mean(values, axis=-1, keepdims=True)
    variance = jnp.mean(centred * centred, axis=-1, keepdims=True)
    return centred * lax.rsqrt(variance + 1e-06) * (1.0 + scale_part) + shift_part


def gather_keys(keys_values):
    band_rows = lax.all_gather(keys_values, "lon", axis=0, tiled=True)
    return lax.all_gather(band_rows, "lat", axis=0, tiled=True)


def spread_keys(key_value_grads):
    band_grads = lax.psum_scatter(
        key_value_grads.astype(jnp.bfloat16), "lat", scatter_dimension=0, tiled=True
    )
    return lax.psum_scatter(band_grads, "lon", scatter_dimension=0, tiled=True).astype(jnp.float32)


def forward_layer(current, modulation, weight_qkv, weight_out, weight_up, weight_down):
    local_rows, width = current.shape
    shift_attn, scale_attn, gate_attn, shift_mlp, scale_mlp, gate_mlp = modulation
    normed = pre_norm(current, shift_attn, scale_attn).astype(jnp.bfloat16)
    projected = jnp.dot(normed, weight_qkv, preferred_element_type=jnp.float32).astype(jnp.bfloat16)
    queries = projected[:, :width].reshape(local_rows, HEADS, HEAD_DIM)
    own_keys = projected[:, width:]
    gathered = gather_keys(own_keys)
    total_rows = gathered.shape[0]
    key_heads = gathered[:, :width].reshape(total_rows, HEADS, HEAD_DIM)
    value_heads = gathered[:, width:].reshape(total_rows, HEADS, HEAD_DIM)
    scores = jnp.einsum(
        "thd,nhd->htn", queries, key_heads, preferred_element_type=jnp.float32
    ) * HEAD_DIM ** (-0.5)
    log_total = jax.nn.logsumexp(scores, axis=-1, keepdims=True)
    probabilities = jnp.exp(scores - log_total).astype(jnp.bfloat16)
    mixed = jnp.einsum(
        "htn,nhd->thd", probabilities, value_heads, preferred_element_type=jnp.float32
    )
    mixed = mixed.reshape(local_rows, width).astype(jnp.bfloat16)
    attended = jnp.dot(mixed, weight_out, preferred_element_type=jnp.float32)
    middle = current + gate_attn * attended
    hidden_in = pre_norm(middle, shift_mlp, scale_mlp).astype(jnp.bfloat16)
    pre_act = jnp.dot(hidden_in, weight_up, preferred_element_type=jnp.float32)
    hidden = jax.nn.gelu(pre_act).astype(jnp.bfloat16)
    branch = jnp.dot(hidden, weight_down, preferred_element_type=jnp.float32)
    output = middle + gate_mlp * branch
    kept = (
        current,
        normed,
        queries,
        gathered,
        own_keys,
        log_total,
        mixed,
        attended,
        middle,
        hidden_in,
        pre_act,
        hidden,
        branch,
    )
    return (output, kept)


def backward_layer(grad_out, kept, modulation, weight_qkv, weight_out, weight_up, weight_down):
    (
        current,
        normed,
        queries,
        gathered,
        own_keys,
        log_total,
        mixed,
        attended,
        middle,
        hidden_in,
        pre_act,
        hidden,
        branch,
    ) = kept
    local_rows, width = current.shape
    total_rows = gathered.shape[0]
    shift_attn, scale_attn, gate_attn, shift_mlp, scale_mlp, gate_mlp = modulation
    factor = HEAD_DIM ** (-0.5)
    branch_grad = (gate_mlp * grad_out).astype(jnp.bfloat16)
    gate_mlp_grad = jnp.sum(grad_out * branch, axis=0)
    hidden_grad = jnp.dot(branch_grad, weight_down.T, preferred_element_type=jnp.float32)
    down_grad = jnp.dot(hidden.T, branch_grad, preferred_element_type=jnp.float32)
    _, gelu_back = jax.vjp(jax.nn.gelu, pre_act)
    pre_grad = gelu_back(hidden_grad)[0].astype(jnp.bfloat16)
    hidden_in_grad = jnp.dot(pre_grad, weight_up.T, preferred_element_type=jnp.float32)
    up_grad = jnp.dot(hidden_in.T, pre_grad, preferred_element_type=jnp.float32)
    _, second_back = jax.vjp(pre_norm, middle, shift_mlp, scale_mlp)
    middle_part, shift_mlp_grad, scale_mlp_grad = second_back(hidden_in_grad)
    middle_grad = grad_out + middle_part
    attended_grad = (gate_attn * middle_grad).astype(jnp.bfloat16)
    gate_attn_grad = jnp.sum(middle_grad * attended, axis=0)
    mixed_grad = jnp.dot(attended_grad, weight_out.T, preferred_element_type=jnp.float32).astype(
        jnp.bfloat16
    )
    out_grad = jnp.dot(mixed.T, attended_grad, preferred_element_type=jnp.float32)
    mixed_heads = mixed_grad.reshape(local_rows, HEADS, HEAD_DIM)
    key_heads = gathered[:, :width].reshape(total_rows, HEADS, HEAD_DIM)
    value_heads = gathered[:, width:].reshape(total_rows, HEADS, HEAD_DIM)
    scores = (
        jnp.einsum("thd,nhd->htn", queries, key_heads, preferred_element_type=jnp.float32) * factor
    )
    probabilities = jnp.exp(scores - log_total)
    prob_grads = jnp.einsum(
        "thd,nhd->htn", mixed_heads, value_heads, preferred_element_type=jnp.float32
    )
    centre = jnp.sum(prob_grads * probabilities, axis=-1, keepdims=True)
    score_grads = (probabilities * (prob_grads - centre)).astype(jnp.bfloat16)
    query_grads = (
        jnp.einsum("htn,nhd->thd", score_grads, key_heads, preferred_element_type=jnp.float32)
        * factor
    )
    value_grads = jnp.einsum(
        "htn,thd->nhd",
        probabilities.astype(jnp.bfloat16),
        mixed_heads,
        preferred_element_type=jnp.float32,
    )
    key_grads = (
        jnp.einsum("htn,thd->nhd", score_grads, queries, preferred_element_type=jnp.float32)
        * factor
    )
    key_value_grads = jnp.concatenate(
        [key_grads.reshape(total_rows, width), value_grads.reshape(total_rows, width)], axis=1
    )
    local_grads = spread_keys(key_value_grads)
    projected_grad = jnp.concatenate(
        [query_grads.reshape(local_rows, width), local_grads], axis=1
    ).astype(jnp.bfloat16)
    normed_grad = jnp.dot(projected_grad, weight_qkv.T, preferred_element_type=jnp.float32)
    qkv_grad = jnp.dot(normed.T, projected_grad, preferred_element_type=jnp.float32)
    _, first_back = jax.vjp(pre_norm, current, shift_attn, scale_attn)
    current_part, shift_attn_grad, scale_attn_grad = first_back(normed_grad)
    input_grad = middle_grad + current_part
    modulation_grad = jnp.concatenate(
        [
            shift_attn_grad,
            scale_attn_grad,
            gate_attn_grad,
            shift_mlp_grad,
            scale_mlp_grad,
            gate_mlp_grad,
        ]
    )
    return (input_grad, (qkv_grad, out_grad, up_grad, down_grad, modulation_grad))


def shards(fields, lead_index, rollout, w_qkv, w_out, w_up, w_down, w_ada, b_ada, cotangent):
    _, rows_dev, cols_dev, width = fields.shape
    local_rows = rows_dev * cols_dev
    layer_count = w_qkv.shape[0]
    context = jax.nn.silu(embedding(lead_index[0])).astype(jnp.bfloat16)
    context_wide = context.astype(jnp.float32)
    modulations = [
        (
            jnp.dot(context[None, :], w_ada[index], preferred_element_type=jnp.float32)[0]
            + b_ada[index]
        ).reshape(6, width)
        for index in range(layer_count)
    ]
    weight_sets = [
        (w_qkv[index], w_out[index], w_up[index], w_down[index]) for index in range(layer_count)
    ]
    count = rollout[0]
    current = fields.reshape(local_rows, width).astype(jnp.float32)
    saved = []
    for rollout_step in range(STEPS):
        updated = current
        kept_layers = []
        for index in range(layer_count):
            updated, kept = forward_layer(updated, modulations[index], *weight_sets[index])
            kept_layers.append(kept)
        current = jnp.where(rollout_step < count, updated, current)
        saved.append(kept_layers)
    gradient = cotangent.reshape(local_rows, width).astype(jnp.float32)
    summed = None
    shares = None
    for rollout_step in reversed(range(STEPS)):
        active = (rollout_step < count).astype(jnp.float32)
        inner = gradient * active
        layer_terms = [None] * layer_count
        for index in reversed(range(layer_count)):
            inner, layer_terms[index] = backward_layer(
                inner, saved[rollout_step][index], modulations[index], *weight_sets[index]
            )
        gradient = inner + (1.0 - active) * gradient
        modulation_grads = jnp.stack([terms[4] for terms in layer_terms])
        step_terms = (
            jnp.stack([terms[0] for terms in layer_terms]),
            jnp.stack([terms[1] for terms in layer_terms]),
            jnp.stack([terms[2] for terms in layer_terms]),
            jnp.stack([terms[3] for terms in layer_terms]),
            context_wide[None, :, None] * modulation_grads[:, None, :],
            modulation_grads,
            modulation_grads[:, 3 * width : 4 * width],
        )
        summed = step_terms if summed is None else jax.tree.map(jnp.add, summed, step_terms)
    shares = lax.psum_scatter(summed, ("lat", "lon"), scatter_dimension=1, tiled=True)
    totals = jax.tree.map(
        lambda part: part.astype(jnp.float32), lax.psum(shortened(shares), "item")
    )
    return (
        current.reshape(1, rows_dev, cols_dev, width),
        gradient.reshape(1, rows_dev, cols_dev, width),
        totals[0],
        totals[1],
        totals[2],
        totals[3],
        totals[4],
        totals[5],
        totals[6],
    )


F32 = jnp.float32
BF16 = jnp.bfloat16
GELU_A = math.sqrt(2.0 / math.pi)
GELU_B = 0.044715
LANES = 128
BLOCK = 256
PAIR = 2 * HEAD_DIM
SUM_ROWS = 48
PIECES = 4
ONES = 16
SAFE_SCORE = 60.0


def nn(left, right, precision=None):
    return lax.dot_general(
        left, right, (((1,), (0,)), ((), ())), preferred_element_type=F32, precision=precision
    )


def nt(left, right, precision=None):
    return lax.dot_general(
        left, right, (((1,), (1,)), ((), ())), preferred_element_type=F32, precision=precision
    )


def identity(size):
    rows = lax.broadcasted_iota(jnp.int32, (size, size), 0)
    columns = lax.broadcasted_iota(jnp.int32, (size, size), 1)
    return jnp.where(rows == columns, 1.0, 0.0).astype(BF16)


def turned(values):
    return nt(identity(values.shape[1]), values).astype(BF16)


def wide(column_tile, lanes):
    return jnp.concatenate([column_tile] * (lanes // LANES), axis=1)


def folded(values):
    pieces = [values[:, at : at + LANES] for at in range(0, values.shape[1], LANES)]
    return sum(pieces[1:], pieces[0])


def standardise(values):
    rows = values.shape[0]
    centred = values - jnp.sum(values, axis=0, keepdims=True) * (1.0 / rows)
    variance = jnp.sum(centred * centred, axis=0, keepdims=True) * (1.0 / rows)
    scale = lax.rsqrt(variance + 1e-06)
    return centred * scale, scale


def pre_norm_back(standard, scale, grad, gain):
    rows = standard.shape[0]
    inner = grad * gain
    first = jnp.sum(inner, axis=0, keepdims=True) * (1.0 / rows)
    second = jnp.sum(inner * standard, axis=0, keepdims=True) * (1.0 / rows)
    return scale * (inner - first - standard * second)


def part(mod_ref, index, lanes):
    return wide(mod_ref[index * D : (index + 1) * D, :], lanes)


def turn_into(source, out, at=0):
    for column in range(0, out.shape[0], BLOCK):
        width = min(BLOCK, out.shape[0] - column)
        out[column : column + width, :] = turned(source[:, at + column : at + column + width])


def prepare_first(mod, w_q_t, w_v_t, w_k, w_qkv, w_ada, b_ada, context):
    w_k[...] = w_qkv[:, D : 2 * D]
    turn_into(w_qkv, w_q_t)
    turn_into(w_qkv, w_v_t, 2 * D)
    values = nn(context[...], w_ada[...])[0:1] + b_ada
    for column in range(0, values.shape[1], LANES):
        tile = jnp.broadcast_to(values[:, column : column + LANES], (LANES, LANES))
        mod[column : column + LANES, :] = tile.T


def prepare_kernel(context, *refs):
    w_qkv, w_ada, b_ada, w_out, w_up, w_down = refs[:6]
    outs, scratch, sems = refs[8:19], refs[19:-1], refs[-1]
    sources = [w_qkv.at[0], w_ada.at[0], b_ada, w_out.at[0], w_up.at[0], w_down.at[0], w_qkv.at[1], w_ada.at[1]]
    copies = []
    for place, (source, target) in enumerate(zip(sources, scratch)):
        pieces = PIECES if target.shape[0] % (16 * PIECES) == 0 else 1
        rows = target.shape[0] // pieces
        for piece in range(pieces):
            at = pl.ds(piece * rows, rows)
            copies.append((place, pltpu.make_async_copy(source.at[at], target.at[at], sems.at[place, piece])))
            copies[-1][1].start()

    def wait(*places):
        for place, copy in copies:
            if place in places:
                copy.wait()

    wait(0, 1, 2)
    prepare_first(*outs[0:4], scratch[0], scratch[1], scratch[2][0:1, :], context)
    for place, out in zip((3, 4, 5), outs[8:11]):
        wait(place)
        turn_into(scratch[place], out)
    wait(6, 7)
    prepare_first(*outs[4:8], scratch[6], scratch[7], scratch[2][1:2, :], context)


def prepare_rest_kernel(index, early, w_out, w_up, w_down, *outs):
    for weight, out in zip((w_out, w_up, w_down), outs):
        turn_into(weight.at[index], out)


def project(x, mod_ref, w_q_t, w_v_t, w_k, outs):
    q_out, kn_out, vt_out = outs
    lanes = x.shape[1]
    standard, _ = standardise(x)
    normed = (standard * (1.0 + part(mod_ref, 1, lanes)) + part(mod_ref, 0, lanes)).astype(BF16)
    vt_out[...] = nn(w_v_t[...], normed).astype(BF16)
    q_out[...] = (nn(w_q_t[...], normed) * HEAD_DIM ** (-0.5)).astype(BF16)
    for at in range(0, lanes, BLOCK):
        kn_out[at : at + BLOCK, :] = nn(turned(normed[:, at : at + BLOCK]), w_k[...]).astype(BF16)


def first_kernel(own, flip_x, flip_y, flip_xy, cot, cot_x, mod, w_q_t, w_v_t, w_k, cot_out, x_out, xb_out, *outs):
    rows = cot.shape[0]
    cot_out[:rows, :] = cot[...]
    cot_out[rows:, :] = cot_x[...]
    for index, ref in enumerate((own, flip_x, flip_y, flip_xy)):
        rows = ref.shape[0]
        flat = turned(ref[...])
        xb_out[:, index * rows : (index + 1) * rows] = flat
        x_out[:, index * rows : (index + 1) * rows] = flat.astype(F32)
    project(x_out[...], mod, w_q_t, w_v_t, w_k, outs)


def head_rows(head):
    return slice(head * HEAD_DIM, (head + 1) * HEAD_DIM)


def pair_columns(head):
    return slice(head // 2 * PAIR, (head // 2 + 1) * PAIR)


def padded(rows, head):
    zeros = jnp.zeros_like(rows)
    return jnp.concatenate([rows, zeros] if head % 2 == 0 else [zeros, rows], axis=0)


def query_top(q):
    square = q[...].astype(F32)
    square = square * square
    norms = [jnp.sum(square[head_rows(head)], axis=0, keepdims=True) for head in range(HEADS)]
    return jnp.max(functools.reduce(jnp.maximum, norms), axis=1, keepdims=True)


def key_top(kn):
    first = lax.broadcasted_iota(jnp.int32, (D, LANES), 1) * HEAD_DIM
    row = lax.broadcasted_iota(jnp.int32, (D, LANES), 0)
    pick = jnp.where((row >= first) & (row < first + HEAD_DIM), 1.0, 0.0).astype(BF16)
    square = kn[...].astype(F32)
    norms = nn((square * square).astype(BF16), pick)
    return jnp.max(jnp.max(norms, axis=0, keepdims=True), axis=1, keepdims=True) * 1.02


def value_rows(vt, rows, at):
    values = vt[rows, at]
    return jnp.concatenate([values, jnp.ones((ONES, values.shape[1]), BF16)], axis=0)


def attend_plain(q, kn, vt, put):
    chunks = [slice(at, at + BLOCK) for at in range(0, kn.shape[0], BLOCK)]

    def score(head):
        return nn(kn[:, pair_columns(head)], padded(q[head_rows(head), :], head))

    totals = {}

    def finish(head, at, probs):
        term = nn(value_rows(vt, head_rows(head), at), probs)
        totals[head] = totals[head] + term if head in totals else term
        if at == chunks[-1]:
            put(head, totals[head])

    waiting = None
    following = score(0)
    for head in range(HEADS):
        scores = following
        for at in chunks:
            if at == chunks[0] and head + 1 < HEADS:
                following = score(head + 1)
            if waiting is not None:
                finish(*waiting)
            waiting = (head, at, jnp.exp(scores[at]).astype(BF16))
    finish(*waiting)


def attend_own_kernel(early, *refs):
    q, kn, vt, *refs = refs[early:]
    passing = []
    if len(refs) > 2:
        *passing, sums, tops, passed = refs
    else:
        sums, tops = refs
    at = 0
    for source in passing:
        rows = source.shape[0]
        passed[at : at + rows, :] = source[...]
        at += rows

    def put(head, total):
        sums[head] = total

    query, key = query_top(q), key_top(kn)
    tops[0:8, :] = jnp.broadcast_to(query, (8, LANES))
    tops[8:16, :] = jnp.broadcast_to(key, (8, LANES))

    @pl.when(jnp.max(query * key) < SAFE_SCORE**2)
    def _():
        attend_plain(q, kn, vt, put)


def forward_kernel(last, early, *refs):
    refs = refs[early:]
    if last:
        rollout, x, x_step, *refs = refs
    else:
        x, *refs = refs
    q, kn_own, kn_far, vt_own, vt_far, sums, tops, mod, w_out_t, w_up_t, w_down_t, *refs = refs
    if not last:
        mod_next, w_q_t, w_v_t, w_k, *refs = refs
    lse, mixed, attended, middle, hidden, slope, branch, *refs = refs
    if last:
        (final,) = refs
    else:
        x_next, xb_next, *next_outs = refs
    patches = x.shape[1]
    bound = tops[0:1, 0:1] * jnp.maximum(tops[8:9, 0:1], key_top(kn_far))
    safe = jnp.max(bound) < SAFE_SCORE**2

    def put(head, total):
        total = sums[head] + total
        weight = total[HEAD_DIM : HEAD_DIM + 1]
        mixed[head_rows(head), :] = (total[:HEAD_DIM] * (1.0 / weight)).astype(BF16)
        lse[head : head + 1, :] = jnp.log(weight)

    @pl.when(safe)
    def _():
        attend_plain(q, kn_far, vt_far, put)

    @pl.when(jnp.logical_not(safe))
    def _():
        def pair_heads(pair, _):
            columns = pl.ds(pl.multiple_of(pair * PAIR, PAIR), PAIR)
            for head in range(2):
                rows = pl.ds(pl.multiple_of(pair * PAIR + head * HEAD_DIM, HEAD_DIM), HEAD_DIM)
                query = padded(q[rows, :], head)
                scores = [nn(kn[:, columns], query) for kn in (kn_own, kn_far)]
                tops = [jnp.max(score, axis=0, keepdims=True) for score in scores]
                top = jnp.maximum(*tops)
                total = None
                for score, vt in zip(scores, (vt_own, vt_far)):
                    term = nn(value_rows(vt, rows, slice(None)), jnp.exp(score - top).astype(BF16))
                    total = term if total is None else total + term
                weight = total[HEAD_DIM : HEAD_DIM + 1]
                mixed[rows, :] = (total[:HEAD_DIM] * (1.0 / weight)).astype(BF16)
                lse[pl.ds(pair * 2 + head, 1), :] = top + jnp.log(weight)
            return 0

        lax.fori_loop(0, HEADS // 2, pair_heads, 0)

    att = nn(w_out_t[...], mixed[...])
    attended[...] = att.astype(BF16)
    mid = x[...] + part(mod, 2, patches) * att
    middle[...] = mid.astype(BF16)
    standard, _ = standardise(mid)
    hidden_in = (standard * (1.0 + part(mod, 4, patches)) + part(mod, 3, patches)).astype(BF16)
    chunks = [slice(at, at + BLOCK) for at in range(0, w_up_t.shape[0], BLOCK)]

    def up(place):
        wide_rows = slice(place * BLOCK, (place + 2) * BLOCK)
        both = nn(w_up_t[wide_rows, :], hidden_in)
        return [both[:BLOCK], both[BLOCK:]]

    down = None
    waiting = None
    acts = up(0)
    for place, rows in enumerate(chunks):
        act = acts[place]
        if place % 2 == 0 and place + 2 < len(chunks):
            acts += up(place + 2)
        if place > 0:
            term = nn(w_down_t[:, chunks[place - 1]], waiting)
            down = term if down is None else down + term
        act = act.astype(BF16)
        inner = GELU_A + (GELU_A * GELU_B) * (act * act)
        half = 0.5 + 0.5 * jnp.tanh(act * inner)
        waiting = gelu = act * half
        hidden[rows, :] = waiting
        slope[rows, :] = (half + (gelu - gelu * half) * (6.0 * inner - 4.0 * GELU_A))
    down = down + nn(w_down_t[:, chunks[-1]], waiting)
    branch[...] = down.astype(BF16)
    out = mid + part(mod, 5, patches) * down
    if last:
        own = final.shape[0]
        final[...] = jnp.where(rollout[0] > 1, out[:, :own], x_step[:, :own]).T
    else:
        x_next[...] = out
        xb_next[...] = out.astype(BF16)
        project(out, mod_next, w_q_t, w_v_t, w_k, next_outs)


def put_grads(left_ref, right, where, count, at, mine, other, before):
    rows = [left_ref[pl.ds(pl.multiple_of(where[place] * count, 16), count), :] for place in range(2)]
    product = nt(jnp.concatenate(rows, axis=0), right)
    for column in range(0, product.shape[1], LANES):
        low = product[:count, column : column + LANES]
        high = product[count:, column : column + LANES]
        if before is not None:
            low = low + before[0][at : at + count, :]
            high = high + before[1][at : at + count, :]
        mine[at : at + count, :] = low.astype(mine.dtype)
        other[at : at + count, :] = high.astype(other.dtype)
        at += count


def dense_back_kernel(has_close, has_open, has_before, start, layers, waits, *refs):
    refs = list(refs)

    def take(count):
        taken = refs[:count]
        del refs[:count]
        return taken

    take(waits)
    where, rollout = take(2)
    active = jnp.where(rollout[0] > 1, 1.0, 0.0)
    close_before = open_before = None
    if has_close:
        d_own, d_got, dq, d_mid_in, x_in, mod_in, w_qkv = take(7)
        w_qkv = w_qkv.at[layers[0]]
        if has_before[0]:
            close_before = take(3)
    if start == "first":
        cots = take(2)
    elif start == "cross":
        cots = take(1)
    if has_open:
        mixed, attended, middle, hidden, slope, branch, mod, w_out, w_up, w_down = take(10)
        w_out, w_up, w_down = (ref.at[layers[1]] for ref in (w_out, w_up, w_down))
        if has_before[1]:
            open_before = take(3)
    else:
        (lines,) = take(1)
    if has_close:
        close_mine, close_other, close_mods = take(3)
    if start == "first":
        (cot_out,) = take(1)
    if has_open:
        open_mine, open_other, open_mods, d_mid_out, do_out, cen_out = take(6)
    else:
        g_out, sums_out = take(2)
        sums_at = close_before[1].shape[0]
    if has_close:
        grads_scr, normed_scr = take(2)
    if has_open:
        pg_scr, hin_scr = take(2)

    patches = middle.shape[1] if has_open else x_in.shape[1]
    totals = {}

    def add_sums(name, values):
        totals[name] = totals[name] + folded(values) if name in totals else folded(values)

    def put_sums(out, before, names):
        for place, name in enumerate(names):
            rows = slice(place * D, (place + 1) * D)
            out[rows, :] = totals[name] + before[2][rows, :] if before else totals[name]

    if start == "first":
        for index, ref in enumerate(cots):
            rows = ref.shape[0]
            cot_out[:, index * rows : (index + 1) * rows] = turned(ref[...])

    def close(at):
        standard, scale = standardise(x_in[:, at].astype(F32))
        gain = 1.0 + part(mod_in, 1, patches)
        normed_scr[:, at] = (standard * gain + part(mod_in, 0, patches)).astype(BF16)
        for third in range(3):
            if third == 0:
                piece = dq[:, at]
            else:
                rows = slice((third - 1) * D, third * D)
                piece = d_own[rows, at] + d_got[rows, at]
            grads_scr[third * D : (third + 1) * D, at] = piece
        back = nn(w_qkv[...], grads_scr[:, at])
        put_grads(normed_scr, grads_scr[...], where, D // 8, 0, close_mine, close_other, close_before)
        add_sums("shift_a", back)
        add_sums("scale_a", back * standard)
        g = d_mid_in[:, at] + pre_norm_back(standard, scale, back, gain)
        if start == "cross":
            g = g + (1.0 - active) * cots[0][:, at].astype(F32)
        return g

    def dense(at, g):
        standard, scale = standardise(middle[:, at].astype(F32))
        gain = 1.0 + part(mod, 4, patches)
        hin_scr[:, at] = (standard * gain + part(mod, 3, patches)).astype(BF16)
        branch_grad = (part(mod, 5, patches) * g).astype(BF16)
        add_sums("gate_m", g * branch[:, at].astype(F32))
        chunks = [slice(start, start + BLOCK) for start in range(0, w_down.shape[0], BLOCK)]
        back = None
        waiting = None

        def down(place):
            wide_rows = slice(place * BLOCK, (place + 2) * BLOCK)
            both = nn(w_down[wide_rows, :], branch_grad)
            return [both[:BLOCK], both[BLOCK:]]

        hidden_grads = down(0)
        for place, rows in enumerate(chunks):
            hidden_grad = hidden_grads[place]
            if place % 2 == 0 and place + 2 < len(chunks):
                hidden_grads += down(place + 2)
            if place > 0:
                term = nn(w_up[:, chunks[place - 1]], waiting)
                back = term if back is None else back + term
            waiting = slope[rows, at] * hidden_grad.astype(BF16)
            pg_scr[rows, at] = waiting
        back = back + nn(w_up[:, chunks[-1]], waiting)
        count = w_down.shape[0] // 8
        start_at = count * (D // LANES)
        put_grads(hidden, branch_grad, where, count, 0, open_mine, open_other, open_before)
        put_grads(hin_scr, pg_scr[...], where, D // 8, start_at, open_mine, open_other, open_before)
        add_sums("shift_m", back)
        add_sums("scale_m", back * standard)
        d_mid = g + pre_norm_back(standard, scale, back, gain)
        d_mid_out[:, at] = d_mid
        att_grad = (part(mod, 2, patches) * d_mid).astype(BF16)
        mixed_grad = nn(w_out[...], att_grad).astype(BF16)
        do_out[:, at] = mixed_grad
        start_at += (w_up.shape[1] // LANES) * (D // 8)
        put_grads(mixed, att_grad, where, D // 8, start_at, open_mine, open_other, open_before)
        add_sums("gate_a", d_mid * attended[:, at].astype(F32))
        product = mixed_grad.astype(F32) * mixed[:, at].astype(F32)
        for head in range(HEADS):
            cen_out[head : head + 1, at] = jnp.sum(product[head_rows(head)], axis=0, keepdims=True)

    at = slice(0, patches)
    g = close(at) if has_close else cot_out[:, at].astype(F32) * active
    if has_open:
        dense(at, g)
    else:
        g_out[...] = g[:, : g_out.shape[0]].T
    if has_close:
        put_sums(close_mods, close_before, ("shift_a", "scale_a"))
    if has_open:
        put_sums(open_mods, open_before, ("gate_a", "shift_m", "scale_m", "gate_m"))
    else:
        sums_out[...] = lines[...]
        put_lines(sums_out, 0, close_mods[...])
        close_other[sums_at:, :] = sums_out[...].astype(BF16)


def attend_back_kernel(has_before, waits, q, kn, vt, lse, d_out, centre, *refs):
    if has_before:
        before, *refs = refs
    d_kv, dq_out, kt_scr, vn_scr = refs[waits:]
    for column in range(0, D, LANES):
        kt_scr[column : column + LANES, :] = turned(kn[:, column : column + LANES])
    for column in range(0, vt.shape[1], BLOCK):
        vn_scr[column : column + BLOCK, :] = turned(vt[:, column : column + BLOCK])

    steps = [(head, slice(at, at + BLOCK)) for head in range(HEADS) for at in range(0, kn.shape[0], BLOCK)]

    def score(head, at):
        columns = pair_columns(head)
        rows = head_rows(head)
        return nn(kn[at, columns], padded(q[rows, :], head)), nn(vn_scr[at, columns], padded(d_out[rows, :], head))

    totals = {}

    def finish(head, at, probs, score_grads):
        rows = head_rows(head)
        d_kv[D + rows.start : D + rows.stop, at] = nt(d_out[rows, :], probs).astype(d_kv.dtype)
        d_kv[rows, at] = nt(q[rows, :], score_grads).astype(d_kv.dtype)
        term = nn(kt_scr[rows, at], score_grads)
        if head not in totals:
            totals[head] = before[rows, :] + term if has_before else term
            return
        term = totals[head] + term
        if has_before:
            term = term * HEAD_DIM ** (-0.5)
        dq_out[rows, :] = term.astype(dq_out.dtype)

    waiting = None
    following = score(*steps[0])
    for place, (head, at) in enumerate(steps):
        scores, prob_grads = following
        if place + 1 < len(steps):
            following = score(*steps[place + 1])
        if waiting is not None:
            finish(*waiting)
        probs = jnp.exp(scores - lse[head : head + 1, :])
        score_grads = (probs * (prob_grads - centre[head : head + 1, :])).astype(BF16)
        waiting = (head, at, probs.astype(BF16), score_grads)
    finish(*waiting)


def split_kernel(waits, where, *refs):
    *halves, keep, sent, total_scr = refs[waits:]
    rows_half = keep.shape[0]
    at = 0
    for mine, other in zip(halves[::2], halves[1::2]):
        rows = mine.shape[0]
        total_scr[at : at + rows, :] = mine[...] + other[...].astype(F32)
        at += rows
    if at < total_scr.shape[0]:
        total_scr[at:, :] = jnp.zeros((total_scr.shape[0] - at, LANES), F32)
    odd = where[3]
    keep[...] = total_scr[pl.ds(pl.multiple_of(odd * rows_half, 16), rows_half), :]
    sent[...] = total_scr[pl.ds(pl.multiple_of((1 - odd) * rows_half, 16), rows_half), :].astype(BF16)


def pair_sum_kernel(waits, *refs):
    refs = refs[waits:]
    count = len(refs) // 3
    for keep, got, out in zip(refs[:count], refs[count : 2 * count], refs[2 * count :]):
        out[...] = (keep[...].astype(F32) + got[...].astype(F32)).astype(BF16)


def put_lines(out, row, values):
    ones = jnp.ones((16, LANES), BF16)
    high = values.astype(BF16)
    low = (values - high.astype(F32)).astype(BF16)
    line = (nt(ones, high) + nt(ones, low))[0:1]
    for column in range(0, line.shape[1], LANES):
        out[row : row + 1, :] = line[:, column : column + LANES]
        row += 1
    return row


def lines_kernel(early, context, *refs):
    *sums, out = refs
    out[...] = jnp.zeros_like(out)
    row = 2 * D // LANES
    for ref in sums:
        row = put_lines(out, row, ref[...])
    for column in range(0, D, LANES):
        out[row : row + 1, :] = context[0:1, column : column + LANES].astype(F32)
        row += 1


def join_kernel(sum_count, early, other_early, mine, sums, got, out):
    rows = mine.shape[0]
    out[:rows, :] = (mine[...] + got[:rows, :].astype(F32)).astype(BF16)
    other = got[rows:, :].astype(F32)
    summed = lax.broadcasted_iota(jnp.int32, (SUM_ROWS, LANES), 0) < sum_count
    out[rows:, :] = (sums[...] + jnp.where(summed, other, 0.0)).astype(BF16)


def pair_kernel(rows, where, own, got, out):
    out[:rows, :] = (own[:rows, :].astype(F32) + got[:rows, :].astype(F32)).astype(BF16)
    odd = where[3]
    size = SUM_ROWS
    out[pl.ds(pl.multiple_of(rows + odd * size, 16), size), :] = own[rows:, :]
    out[pl.ds(pl.multiple_of(rows + (1 - odd) * size, 16), size), :] = got[rows:, :]


def gather_kernel(layer, where, own, got, *refs):
    outs, qkv_out, rows_scr, scratch, sems = refs[-9:-6], refs[-6], refs[-5], refs[-4:-1], refs[-1]
    if layer == 1:
        outs = refs[-8:-5]
    half = own.shape[0]
    rows_scr[pl.ds(pl.multiple_of(where[3] * half, 16), half), :] = own[...]
    rows_scr[pl.ds(pl.multiple_of((1 - where[3]) * half, 16), half), :] = got[...]
    at = 0
    copies = []
    for place, (out, held) in enumerate(zip(outs, scratch)):
        rows = held.shape[0]
        for column in range(0, held.shape[1], LANES):
            held[:, column : column + LANES] = rows_scr[at : at + rows, :].astype(F32)
            at += rows
        copies.append(pltpu.make_async_copy(held, out.at[layer], sems.at[place]))
        copies[-1].start()
    if layer == 0:
        rows = qkv_out.shape[0]
        for column in range(0, qkv_out.shape[1], LANES):
            qkv_out[:, column : column + LANES] = rows_scr[at : at + rows, :].astype(F32)
            at += rows
    for copy in copies:
        copy.wait()


def finish_kernel(item_count, where, own, got, qkv_1, qkv_out, ada_out, bias_out, shift_out, sum_scr, bias_scr, shift_scr):
    layers = 2
    device, high = where[0], where[4]
    slice_rows = qkv_out.shape[1]
    close_rows = slice_rows * (3 * D // LANES)
    for other in range(2):
        rows = slice(close_rows + other * SUM_ROWS, close_rows + (other + 1) * SUM_ROWS)
        sum_scr[2 * high + other] = own[rows, :].astype(F32)
        sum_scr[2 * (1 - high) + other] = got[rows, :].astype(F32)
    qkv_out[1] = qkv_1[...]
    for tile in range(3 * D // LANES):
        rows = slice(tile * slice_rows, (tile + 1) * slice_rows)
        total = own[rows, :].astype(F32) + got[rows, :].astype(F32)
        qkv_out[0, :, tile * LANES : (tile + 1) * LANES] = total
    tiles = 6 * D // LANES
    contexts = []
    for other in range(item_count):
        line = jnp.concatenate([sum_scr[other, layers * tiles + c : layers * tiles + c + 1, :] for c in range(3)], axis=1)
        contexts.append(line)
    square = jnp.concatenate(contexts + [jnp.zeros((8 - item_count, D), F32)], axis=0)
    spot = lax.broadcasted_iota(jnp.int32, (slice_rows, D), 1)
    want = lax.broadcasted_iota(jnp.int32, (slice_rows, D), 0) + device * slice_rows
    pick = jnp.where(spot == want, 1.0, 0.0).astype(BF16)
    columns = nt(pick, square.astype(BF16))
    bias_rows = bias_out.shape[1]
    for index in range(layers):
        flats = []
        for tile in range(tiles):
            row = index * tiles + tile
            total = None
            flat = None
            for other in range(item_count):
                line = sum_scr[other, row : row + 1, :]
                term = columns[:, other : other + 1] * line
                total = term if total is None else total + term
                flat = line if flat is None else flat + line
            ada_out[index, :, tile * LANES : (tile + 1) * LANES] = total
            flats.append(flat)
        flat = jnp.concatenate(flats, axis=1)
        for place in range(flat.shape[1] // bias_rows):
            bias_scr[place, index : index + 1, :] = flat[:, place * bias_rows : (place + 1) * bias_rows]
            at = 3 * D + place * slice_rows
            shift_scr[place, index : index + 1, :] = flat[:, at : at + slice_rows]
    bias_out[...] = bias_scr[device]
    shift_out[...] = shift_scr[device]


VMEM = pl.BlockSpec(memory_space=pltpu.VMEM)
SMEM = pl.BlockSpec(memory_space=pltpu.SMEM)
ANY = pl.BlockSpec(memory_space=pl.ANY)
HBM = pl.BlockSpec(memory_space=pltpu.HBM)


def layer_block(array, index):
    return pl.BlockSpec((None,) + array.shape[1:], lambda step: (index,) + (0,) * (array.ndim - 1))


def call(body, args, outs, scratch=(), flops=0, name=None, direct=0, aliases=None):
    arrays = [arg[0] if isinstance(arg, tuple) else arg for arg in args]
    specs = [arg[1] if isinstance(arg, tuple) else VMEM for arg in args]
    return pl.pallas_call(
        body,
        out_shape=[jax.ShapeDtypeStruct(shape, kind) for shape, kind in outs],
        in_specs=specs,
        out_specs=[ANY] * direct + [VMEM] * (len(outs) - direct),
        input_output_aliases=aliases or {},
        scratch_shapes=[one if not isinstance(one, tuple) else pltpu.VMEM(*one) for one in scratch],
        compiler_params=pltpu.CompilerParams(vmem_limit_bytes=VMEM_LIMIT),
        cost_estimate=pl.CostEstimate(flops=flops, bytes_accessed=0, transcendentals=0),
        name=name,
    )(*arrays)


VMEM_LIMIT = 14 * 1024 * 1024


def fast_shards(
    lat_count, lon_count, item_count,
    fields, lead_index, rollout, w_qkv, w_out, w_up, w_down, w_ada, b_ada, cotangent,
):
    _, rows_dev, cols_dev, width = fields.shape
    local = rows_dev * cols_dev
    layers = w_qkv.shape[0]
    ff = w_up.shape[2]
    patches = 4 * local
    device = lax.axis_index("lat") * lon_count + lax.axis_index("lon")
    item = lax.axis_index("item")
    where = jnp.stack([device, device ^ 1, item, item & 1, item >> 1]).astype(jnp.int32)

    def plane_flip(value, flip_lat, flip_y):
        pairs = [
            (a * lon_count + b, (a ^ flip_lat) * lon_count + (b ^ (2 * flip_y)))
            for a in range(lat_count)
            for b in range(lon_count)
        ]
        return lax.ppermute(value, ("lat", "lon"), pairs)

    def swap(value):
        return lax.ppermute(value, "lon", [(index, index ^ 1) for index in range(lon_count)])

    def with_item(value, flip):
        return lax.ppermute(value, "item", [(index, index ^ flip) for index in range(item_count)])

    def plane_parts(value):
        return [value, plane_flip(value, 1, 0), plane_flip(value, 0, 1), plane_flip(value, 1, 1)]

    field_parts = plane_parts(fields.reshape(local, width))

    lead = lax.optimization_barrier(jnp.broadcast_to(lead_index[:, None], (16, width // 2)))
    context = jax.nn.silu(embedding(lead)).astype(BF16)
    square = (width, patches)
    natural = (patches, width)
    weights = (w_qkv, w_ada, b_ada, w_out, w_up, w_down)
    weights = [(pltpu.with_memory_space_constraint(value, pltpu.HBM), HBM) for value in weights]
    first_outs = [((6 * width, LANES), F32)] + [((width, width), BF16)] * 3
    rest_outs = [((width, width), BF16), ((ff, width), BF16), ((width, ff), BF16)]
    first_fetch = [((width, 3 * width), BF16), ((width, 6 * width), BF16)]
    rest_fetch = [((width, width), BF16), ((width, ff), BF16), ((ff, width), BF16)]
    prepared = call(
        prepare_kernel,
        [context, *weights, (where, SMEM), (rollout, SMEM)],
        first_outs * 2 + rest_outs,
        first_fetch + [(b_ada.shape, F32)] + rest_fetch + first_fetch + [pltpu.SemaphoreType.DMA((8, PIECES))],
        name="prepare",
    )
    first_parts = [prepared[0:4], prepared[4:8]]
    rest_parts = [prepared[8:11]]
    mods = [one[0] for one in first_parts]

    project_outs = [(square, F32), (square, BF16), (square, BF16), (natural, BF16), (square, BF16)]
    dense_flops = 2 * patches * (width * 3 * width + width * width + 2 * width * ff)
    score_flops = 2 * patches * 2 * patches * width * 4
    cot = cotangent.reshape(local, width)
    cot, x, xb, *projected = call(
        first_kernel,
        [*field_parts, cot, plane_flip(cot, 1, 0), *first_parts[0]],
        [((2 * local, width), BF16)] + project_outs,
        flops=2 * patches * width * 4 * width,
        name="first",
    )
    saved = []
    for step in range(STEPS):
        for index in range(layers):
            q, kn, vt = projected
            if len(rest_parts) == index:
                rest_parts.append(
                    call(
                        functools.partial(prepare_rest_kernel, index),
                        [(kn, ANY), w_out, w_up, w_down],
                        rest_outs,
                        name="prepare_rest",
                    )
                )
            kn_far, vt_far = swap(kn), swap(vt)
            early = [w_up] if len(rest_parts) == index + 1 < layers else []
            passing = [cot] if step == STEPS - 1 and index == 0 else []
            passed = [((2 * local, width), BF16)] if passing else []
            sums, tops, *passed = call(
                functools.partial(attend_own_kernel, len(early)),
                early + [q, kn, vt] + passing,
                [((HEADS, HEAD_DIM + ONES, patches), F32), ((16, LANES), F32)] + passed,
                flops=10 * score_flops,
                name="forward_own",
            )
            if passed:
                cot_parts = [passed[0], plane_flip(passed[0], 0, 1)]
            last = step == STEPS - 1 and index == layers - 1
            if index == 0 and step > 0:
                x_step = x
            following = list(first_parts[(index + 1) % layers])
            early = [w_down] if len(rest_parts) == index + 1 < layers else []
            lse, mixed, attended, middle, hidden, slope, branch, *results = call(
                functools.partial(forward_kernel, last, len(early)),
                early
                + ([(rollout, SMEM), x, x_step] if last else [x])
                + [q, kn, kn_far, vt, vt_far, sums, tops, mods[index], *rest_parts[index]]
                + ([] if last else following),
                [
                    ((HEADS, patches), F32),
                    (square, BF16),
                    (square, BF16),
                    (square, BF16),
                    ((ff, patches), BF16),
                    ((ff, patches), BF16),
                    (square, BF16),
                ]
                + ([((local, width), F32)] if last else project_outs),
                flops=dense_flops + 2 * score_flops,
                name="forward",
            )
            saved.append((xb, [mixed, attended, middle, hidden, slope, branch], (q, kn, kn_far, vt, vt_far, lse)))
            if last:
                final = results[0]
            else:
                x, xb, *projected = results

    slice_rows = width // 8
    open_rows = 2 * (ff // 8) * (width // LANES) + slice_rows * (width // LANES)
    close_rows = slice_rows * (3 * width // LANES)
    order = [(step, index) for step in reversed(range(STEPS)) for index in reversed(range(layers))]
    open_done = [None] * layers
    close_done = [None] * layers
    pending = None
    for place in range(len(order) + 1):
        has_close = pending is not None
        has_open = place < len(order)
        use = [order[place - 1][1], order[place][1] if has_open else 0]
        waits = []
        if has_close and close_done[use[0]]:
            waits = [pair_1] if has_open else []
        args = [(value, ANY) for value in waits] + [(where, SMEM), (rollout, SMEM)]
        outs = []
        scratch = []
        has_before = [False, False]
        start = ""
        if has_close:
            args += pending
            if close_done[use[0]] is not None:
                has_before[0] = True
                args += close_done[use[0]]
            outs += [((close_rows, LANES), F32)]
            sent_rows = close_rows + (0 if has_open else SUM_ROWS)
            outs += [((sent_rows, LANES), BF16 if has_before[0] else F32), ((2 * width, LANES), F32)]
            scratch += [((3 * width, patches), BF16), (square, BF16)]
        if place == 0:
            start = "first"
            args += cot_parts
            outs += [(square, BF16)]
        elif has_open and order[place][0] != order[place - 1][0]:
            start = "cross"
            args += [cot_t]
        if has_open:
            step, index = order[place]
            xb, kept, heads = saved[step * layers + index]
            args += kept + [mods[index], w_out, w_up, w_down]
            if open_done[index] is not None:
                has_before[1] = True
                args += open_done[index]
            outs += [
                ((open_rows, LANES), F32),
                ((open_rows, LANES), BF16 if has_before[1] else F32),
                ((4 * width, LANES), F32),
                (square, F32),
                (square, BF16),
                ((HEADS, patches), F32),
            ]
            scratch += [((ff, patches), BF16), (square, BF16)]
        else:
            args += [lines]
            outs += [((local, width), F32), ((SUM_ROWS, LANES), F32)]
        results = list(
            call(
                functools.partial(dense_back_kernel, has_close, has_open, has_before, start, use, len(waits)),
                args,
                outs,
                scratch,
                flops=2 * dense_flops if has_open else 0,
                name="dense_back" if has_open else "close_back",
            )
        )
        if has_close:
            close_done[use[0]] = results[:3]
            del results[:3]
        if start == "first":
            cot_t = results.pop(0)
        if not has_open:
            gradient, line = results
            break
        open_done[index] = results[:3]
        d_mid, d_out, centre = results[3:]
        q, kn, kn_far, vt, vt_far, lse = heads
        halves = [open_done[index][0], open_done[index][1]]
        if index == 0:
            halves += [close_done[1][0], close_done[1][1]]
        half_rows = -(-sum(half.shape[0] for half in halves[::2]) // 32) * 16

        def split(waits):
            pieces = [half if place % 2 == 0 else swap(half) for place, half in enumerate(halves)]
            return call(
                functools.partial(split_kernel, len(waits)),
                [(where, SMEM), *waits, *pieces],
                [((half_rows, LANES), F32), ((half_rows, LANES), BF16)],
                [((2 * half_rows, LANES), F32)],
                name="split",
            )

        def pair_sum(late, keeps, gots, others=()):
            outs = [(keep.shape, BF16) for keep in keeps]
            body = functools.partial(pair_sum_kernel, 1 + len(others))
            return call(body, [(late, ANY), *others, *keeps, *gots], outs, name="pair_sum")

        waits = []
        if has_before[1] and index == 0:
            pair_got_1 = with_item(pair_1, 2)
            lines = call(
                lines_kernel,
                [(pair_got_1, ANY), context, open_done[0][2], close_done[1][2], open_done[1][2]],
                [((SUM_ROWS, LANES), F32)],
                flops=10 * score_flops,
                name="lines",
            )[0]
            keep, sent = split([(lines, ANY)])
            got_0 = with_item(sent, 1)
            waits = [keep]
        d_far, dq = call(
            functools.partial(attend_back_kernel, False, len(waits)),
            [q, kn_far, vt_far, lse, d_out, centre] + [(value, ANY) for value in waits],
            [((2 * width, patches), BF16), (square, F32)],
            [(square, BF16), (natural, BF16)],
            flops=10 * score_flops,
            name="attend_far",
        )
        d_got = swap(d_far)
        waits = []
        if has_before[1]:
            if index == 1:
                keep, sent = split([(d_far, ANY)])
                got_1 = with_item(sent, 1)
                waits = [keep]
            else:
                (item_1,) = pair_sum(d_far, [pair_1], [pair_got_1])
                item_got_1 = with_item(item_1, 1)
                (pair_0,) = pair_sum(d_far, [keep], [got_0], [(item_1, ANY)])
                pair_got_0 = with_item(pair_0, 2)
                waits = [pair_0]
        d_own, dq = call(
            functools.partial(attend_back_kernel, True, len(waits)),
            [q, kn, vt, lse, d_out, centre, dq] + [(value, ANY) for value in waits],
            [((2 * width, patches), BF16), (square, BF16)],
            [(square, BF16), (natural, BF16)],
            flops=10 * score_flops,
            name="attend_own",
        )
        if has_before[1] and index == 1:
            (pair_1,) = pair_sum(dq, [keep], [got_1])
        pending = [d_own, d_got, dq, d_mid, xb, mods[index], w_qkv]

    message = call(
        functools.partial(join_kernel, layers * 6 * width // LANES),
        [(pair_got_0, ANY), (item_got_1, ANY), close_done[0][0], line, swap(close_done[0][1])],
        [((close_rows + SUM_ROWS, LANES), BF16)],
        name="join",
    )[0]
    message_got = with_item(message, 1)
    stacks = [
        ((layers, ff // 8, width), F32),
        ((layers, slice_rows, ff), F32),
        ((layers, slice_rows, width), F32),
    ]
    held = [(shape[1:], kind) for shape, kind in stacks]
    sems = [pltpu.SemaphoreType.DMA((3,))]
    stacked = call(
        functools.partial(gather_kernel, 1),
        [(where, SMEM), item_1, item_got_1],
        stacks,
        [((2 * pair_1.shape[0], LANES), BF16)] + held + sems,
        name="gather",
        direct=3,
    )
    early = (pltpu.with_memory_space_constraint(stacked[2], pltpu.HBM), HBM)
    (item_0,) = pair_sum(message_got, [pair_0], [pair_got_0], [early])
    message = call(
        functools.partial(pair_kernel, close_rows),
        [(where, SMEM), message, message_got],
        [((close_rows + 2 * SUM_ROWS, LANES), BF16)],
        name="pair",
    )[0]
    down_grad, up_grad, out_grad, qkv_1 = call(
        functools.partial(gather_kernel, 0),
        [(where, SMEM), item_0, with_item(item_0, 1)] + [(value, ANY) for value in stacked],
        stacks + [((slice_rows, 3 * width), F32)],
        [((2 * pair_0.shape[0], LANES), BF16)] + held + sems,
        name="gather",
        direct=3,
        aliases={3: 0, 4: 1, 5: 2},
    )
    bias_rows = 6 * width // 8
    qkv_grad, ada_grad, bias_grad, shift_grad = call(
        functools.partial(finish_kernel, item_count),
        [(where, SMEM), message, with_item(message, 2), qkv_1],
        [
            ((layers, slice_rows, 3 * width), F32),
            ((layers, slice_rows, 6 * width), F32),
            ((layers, bias_rows), F32),
            ((layers, slice_rows), F32),
        ],
        [
            ((item_count, SUM_ROWS, LANES), F32),
            ((8, layers, bias_rows), F32),
            ((8, layers, slice_rows), F32),
        ],
        name="finish",
    )
    field_shape = (1, rows_dev, cols_dev, width)
    return (
        final.reshape(field_shape),
        gradient.reshape(field_shape),
        qkv_grad,
        out_grad,
        up_grad,
        down_grad,
        ada_grad,
        bias_grad,
        shift_grad,
    )


def solution(mesh):
    lat_count, lon_count, item_count = mesh.shape["lat"], mesh.shape["lon"], mesh.shape["item"]
    if lat_count == 2 and lon_count == 4:
        body = functools.partial(fast_shards, lat_count, lon_count, item_count)
    else:
        body = shards
    return jax.shard_map(
        body,
        mesh=mesh,
        in_specs=(
            P("item", "lat", "lon", None),
            P("item"),
            P("item"),
            P(),
            P(),
            P(),
            P(),
            P(),
            P(),
            P("item", "lat", "lon", None),
        ),
        out_specs=(
            P("item", "lat", "lon", None),
            P("item", "lat", "lon", None),
            P(None, ("lat", "lon"), None),
            P(None, ("lat", "lon"), None),
            P(None, ("lat", "lon"), None),
            P(None, ("lat", "lon"), None),
            P(None, ("lat", "lon"), None),
            P(None, ("lat", "lon")),
            P(None, ("lat", "lon")),
        ),
        check_vma=False,
    )
```

```python
import functools
import math

import jax
import jax.numpy as jnp
from jax import lax
from jax.experimental import pallas as pl
from jax.experimental.pallas import tpu as pltpu
from jax.sharding import PartitionSpec as P

D = 384
HEADS = 6
HEAD_DIM = 64
STEPS = 2


def shortened(shard):
    return jax.tree.map(lambda a: a.astype(jnp.bfloat16) if a.dtype == jnp.float32 else a, shard)


def embedding(lead):
    half_width = D // 2
    lead_hours = 6.0 * (lead.astype(jnp.float32) + 1.0)
    frequencies = jnp.exp(
        -math.log(10000.0) * jnp.arange(half_width, dtype=jnp.float32) / half_width
    )
    angles = lead_hours * frequencies
    return jnp.concatenate([jnp.sin(angles), jnp.cos(angles)])


def pre_norm(values, shift_part, scale_part):
    centred = values - jnp.mean(values, axis=-1, keepdims=True)
    variance = jnp.mean(centred * centred, axis=-1, keepdims=True)
    return centred * lax.rsqrt(variance + 1e-06) * (1.0 + scale_part) + shift_part


def gather_keys(keys_values):
    band_rows = lax.all_gather(keys_values, "lon", axis=0, tiled=True)
    return lax.all_gather(band_rows, "lat", axis=0, tiled=True)


def spread_keys(key_value_grads):
    band_grads = lax.psum_scatter(
        key_value_grads.astype(jnp.bfloat16), "lat", scatter_dimension=0, tiled=True
    )
    return lax.psum_scatter(band_grads, "lon", scatter_dimension=0, tiled=True).astype(jnp.float32)


def forward_layer(current, modulation, weight_qkv, weight_out, weight_up, weight_down):
    local_rows, width = current.shape
    shift_attn, scale_attn, gate_attn, shift_mlp, scale_mlp, gate_mlp = modulation
    normed = pre_norm(current, shift_attn, scale_attn).astype(jnp.bfloat16)
    projected = jnp.dot(normed, weight_qkv, preferred_element_type=jnp.float32).astype(jnp.bfloat16)
    queries = projected[:, :width].reshape(local_rows, HEADS, HEAD_DIM)
    own_keys = projected[:, width:]
    gathered = gather_keys(own_keys)
    total_rows = gathered.shape[0]
    key_heads = gathered[:, :width].reshape(total_rows, HEADS, HEAD_DIM)
    value_heads = gathered[:, width:].reshape(total_rows, HEADS, HEAD_DIM)
    scores = jnp.einsum(
        "thd,nhd->htn", queries, key_heads, preferred_element_type=jnp.float32
    ) * HEAD_DIM ** (-0.5)
    log_total = jax.nn.logsumexp(scores, axis=-1, keepdims=True)
    probabilities = jnp.exp(scores - log_total).astype(jnp.bfloat16)
    mixed = jnp.einsum(
        "htn,nhd->thd", probabilities, value_heads, preferred_element_type=jnp.float32
    )
    mixed = mixed.reshape(local_rows, width).astype(jnp.bfloat16)
    attended = jnp.dot(mixed, weight_out, preferred_element_type=jnp.float32)
    middle = current + gate_attn * attended
    hidden_in = pre_norm(middle, shift_mlp, scale_mlp).astype(jnp.bfloat16)
    pre_act = jnp.dot(hidden_in, weight_up, preferred_element_type=jnp.float32)
    hidden = jax.nn.gelu(pre_act).astype(jnp.bfloat16)
    branch = jnp.dot(hidden, weight_down, preferred_element_type=jnp.float32)
    output = middle + gate_mlp * branch
    kept = (
        current,
        normed,
        queries,
        gathered,
        own_keys,
        log_total,
        mixed,
        attended,
        middle,
        hidden_in,
        pre_act,
        hidden,
        branch,
    )
    return (output, kept)


def backward_layer(grad_out, kept, modulation, weight_qkv, weight_out, weight_up, weight_down):
    (
        current,
        normed,
        queries,
        gathered,
        own_keys,
        log_total,
        mixed,
        attended,
        middle,
        hidden_in,
        pre_act,
        hidden,
        branch,
    ) = kept
    local_rows, width = current.shape
    total_rows = gathered.shape[0]
    shift_attn, scale_attn, gate_attn, shift_mlp, scale_mlp, gate_mlp = modulation
    factor = HEAD_DIM ** (-0.5)
    branch_grad = (gate_mlp * grad_out).astype(jnp.bfloat16)
    gate_mlp_grad = jnp.sum(grad_out * branch, axis=0)
    hidden_grad = jnp.dot(branch_grad, weight_down.T, preferred_element_type=jnp.float32)
    down_grad = jnp.dot(hidden.T, branch_grad, preferred_element_type=jnp.float32)
    _, gelu_back = jax.vjp(jax.nn.gelu, pre_act)
    pre_grad = gelu_back(hidden_grad)[0].astype(jnp.bfloat16)
    hidden_in_grad = jnp.dot(pre_grad, weight_up.T, preferred_element_type=jnp.float32)
    up_grad = jnp.dot(hidden_in.T, pre_grad, preferred_element_type=jnp.float32)
    _, second_back = jax.vjp(pre_norm, middle, shift_mlp, scale_mlp)
    middle_part, shift_mlp_grad, scale_mlp_grad = second_back(hidden_in_grad)
    middle_grad = grad_out + middle_part
    attended_grad = (gate_attn * middle_grad).astype(jnp.bfloat16)
    gate_attn_grad = jnp.sum(middle_grad * attended, axis=0)
    mixed_grad = jnp.dot(attended_grad, weight_out.T, preferred_element_type=jnp.float32).astype(
        jnp.bfloat16
    )
    out_grad = jnp.dot(mixed.T, attended_grad, preferred_element_type=jnp.float32)
    mixed_heads = mixed_grad.reshape(local_rows, HEADS, HEAD_DIM)
    key_heads = gathered[:, :width].reshape(total_rows, HEADS, HEAD_DIM)
    value_heads = gathered[:, width:].reshape(total_rows, HEADS, HEAD_DIM)
    scores = (
        jnp.einsum("thd,nhd->htn", queries, key_heads, preferred_element_type=jnp.float32) * factor
    )
    probabilities = jnp.exp(scores - log_total)
    prob_grads = jnp.einsum(
        "thd,nhd->htn", mixed_heads, value_heads, preferred_element_type=jnp.float32
    )
    centre = jnp.sum(prob_grads * probabilities, axis=-1, keepdims=True)
    score_grads = (probabilities * (prob_grads - centre)).astype(jnp.bfloat16)
    query_grads = (
        jnp.einsum("htn,nhd->thd", score_grads, key_heads, preferred_element_type=jnp.float32)
        * factor
    )
    value_grads = jnp.einsum(
        "htn,thd->nhd",
        probabilities.astype(jnp.bfloat16),
        mixed_heads,
        preferred_element_type=jnp.float32,
    )
    key_grads = (
        jnp.einsum("htn,thd->nhd", score_grads, queries, preferred_element_type=jnp.float32)
        * factor
    )
    key_value_grads = jnp.concatenate(
        [key_grads.reshape(total_rows, width), value_grads.reshape(total_rows, width)], axis=1
    )
    local_grads = spread_keys(key_value_grads)
    projected_grad = jnp.concatenate(
        [query_grads.reshape(local_rows, width), local_grads], axis=1
    ).astype(jnp.bfloat16)
    normed_grad = jnp.dot(projected_grad, weight_qkv.T, preferred_element_type=jnp.float32)
    qkv_grad = jnp.dot(normed.T, projected_grad, preferred_element_type=jnp.float32)
    _, first_back = jax.vjp(pre_norm, current, shift_attn, scale_attn)
    current_part, shift_attn_grad, scale_attn_grad = first_back(normed_grad)
    input_grad = middle_grad + current_part
    modulation_grad = jnp.concatenate(
        [
            shift_attn_grad,
            scale_attn_grad,
            gate_attn_grad,
            shift_mlp_grad,
            scale_mlp_grad,
            gate_mlp_grad,
        ]
    )
    return (input_grad, (qkv_grad, out_grad, up_grad, down_grad, modulation_grad))


def shards(fields, lead_index, rollout, w_qkv, w_out, w_up, w_down, w_ada, b_ada, cotangent):
    _, rows_dev, cols_dev, width = fields.shape
    local_rows = rows_dev * cols_dev
    layer_count = w_qkv.shape[0]
    context = jax.nn.silu(embedding(lead_index[0])).astype(jnp.bfloat16)
    context_wide = context.astype(jnp.float32)
    modulations = [
        (
            jnp.dot(context[None, :], w_ada[index], preferred_element_type=jnp.float32)[0]
            + b_ada[index]
        ).reshape(6, width)
        for index in range(layer_count)
    ]
    weight_sets = [
        (w_qkv[index], w_out[index], w_up[index], w_down[index]) for index in range(layer_count)
    ]
    count = rollout[0]
    current = fields.reshape(local_rows, width).astype(jnp.float32)
    saved = []
    for rollout_step in range(STEPS):
        updated = current
        kept_layers = []
        for index in range(layer_count):
            updated, kept = forward_layer(updated, modulations[index], *weight_sets[index])
            kept_layers.append(kept)
        current = jnp.where(rollout_step < count, updated, current)
        saved.append(kept_layers)
    gradient = cotangent.reshape(local_rows, width).astype(jnp.float32)
    summed = None
    shares = None
    for rollout_step in reversed(range(STEPS)):
        active = (rollout_step < count).astype(jnp.float32)
        inner = gradient * active
        layer_terms = [None] * layer_count
        for index in reversed(range(layer_count)):
            inner, layer_terms[index] = backward_layer(
                inner, saved[rollout_step][index], modulations[index], *weight_sets[index]
            )
        gradient = inner + (1.0 - active) * gradient
        modulation_grads = jnp.stack([terms[4] for terms in layer_terms])
        step_terms = (
            jnp.stack([terms[0] for terms in layer_terms]),
            jnp.stack([terms[1] for terms in layer_terms]),
            jnp.stack([terms[2] for terms in layer_terms]),
            jnp.stack([terms[3] for terms in layer_terms]),
            context_wide[None, :, None] * modulation_grads[:, None, :],
            modulation_grads,
            modulation_grads[:, 3 * width : 4 * width],
        )
        summed = step_terms if summed is None else jax.tree.map(jnp.add, summed, step_terms)
    shares = lax.psum_scatter(summed, ("lat", "lon"), scatter_dimension=1, tiled=True)
    totals = jax.tree.map(
        lambda part: part.astype(jnp.float32), lax.psum(shortened(shares), "item")
    )
    return (
        current.reshape(1, rows_dev, cols_dev, width),
        gradient.reshape(1, rows_dev, cols_dev, width),
        totals[0],
        totals[1],
        totals[2],
        totals[3],
        totals[4],
        totals[5],
        totals[6],
    )


F32 = jnp.float32
BF16 = jnp.bfloat16
GELU_A = math.sqrt(2.0 / math.pi)
GELU_B = 0.044715
LANES = 128
BLOCK = 256
PAIR = 2 * HEAD_DIM
SUM_ROWS = 48
ONES = 16
SAFE_SCORE = 60.0


def nn(left, right, precision=None):
    return lax.dot_general(
        left, right, (((1,), (0,)), ((), ())), preferred_element_type=F32, precision=precision
    )


def nt(left, right, precision=None):
    return lax.dot_general(
        left, right, (((1,), (1,)), ((), ())), preferred_element_type=F32, precision=precision
    )


def identity(size):
    rows = lax.broadcasted_iota(jnp.int32, (size, size), 0)
    columns = lax.broadcasted_iota(jnp.int32, (size, size), 1)
    return jnp.where(rows == columns, 1.0, 0.0).astype(BF16)


def turned(values):
    return nt(identity(values.shape[1]), values).astype(BF16)


def wide(column_tile, lanes):
    return jnp.concatenate([column_tile] * (lanes // LANES), axis=1)


def folded(values):
    pieces = [values[:, at : at + LANES] for at in range(0, values.shape[1], LANES)]
    return sum(pieces[1:], pieces[0])


def standardise(values):
    rows = values.shape[0]
    centred = values - jnp.sum(values, axis=0, keepdims=True) * (1.0 / rows)
    variance = jnp.sum(centred * centred, axis=0, keepdims=True) * (1.0 / rows)
    scale = lax.rsqrt(variance + 1e-06)
    return centred * scale, scale


def pre_norm_back(standard, scale, grad, gain):
    rows = standard.shape[0]
    inner = grad * gain
    first = jnp.sum(inner, axis=0, keepdims=True) * (1.0 / rows)
    second = jnp.sum(inner * standard, axis=0, keepdims=True) * (1.0 / rows)
    return scale * (inner - first - standard * second)


def part(mod_ref, index, lanes):
    return wide(mod_ref[index * D : (index + 1) * D, :], lanes)


def turn_into(source, out, at=0):
    for column in range(0, out.shape[0], BLOCK):
        width = min(BLOCK, out.shape[0] - column)
        out[column : column + width, :] = turned(source[:, at + column : at + column + width])


def prepare_first(mod, w_q_t, w_v_t, w_k, w_qkv, w_ada, b_ada, context):
    w_k[...] = w_qkv[:, D : 2 * D]
    turn_into(w_qkv, w_q_t)
    turn_into(w_qkv, w_v_t, 2 * D)
    values = nn(context[...], w_ada[...])[0:1] + b_ada
    for column in range(0, values.shape[1], LANES):
        tile = jnp.broadcast_to(values[:, column : column + LANES], (LANES, LANES))
        mod[column : column + LANES, :] = tile.T


def prepare_kernel(context, *refs):
    w_qkv, w_ada, b_ada, w_out, w_up, w_down = refs[:6]
    outs, scratch, sems = refs[8:19], refs[19:-1], refs[-1]
    sources = [w_qkv.at[0], w_ada.at[0], b_ada, w_out.at[0], w_up.at[0], w_down.at[0], w_qkv.at[1], w_ada.at[1]]
    copies = [
        pltpu.make_async_copy(source, target, sems.at[place])
        for place, (source, target) in enumerate(zip(sources, scratch))
    ]
    for copy in copies:
        copy.start()
    for copy in copies[:3]:
        copy.wait()
    prepare_first(*outs[0:4], scratch[0], scratch[1], scratch[2][0:1, :], context)
    for copy, source, out in zip(copies[3:6], scratch[3:6], outs[8:11]):
        copy.wait()
        turn_into(source, out)
    for copy in copies[6:]:
        copy.wait()
    prepare_first(*outs[4:8], scratch[6], scratch[7], scratch[2][1:2, :], context)


def prepare_rest_kernel(index, early, w_out, w_up, w_down, *outs):
    for weight, out in zip((w_out, w_up, w_down), outs):
        turn_into(weight.at[index], out)


def project(x, mod_ref, w_q_t, w_v_t, w_k, outs):
    q_out, kn_out, vt_out = outs
    lanes = x.shape[1]
    standard, _ = standardise(x)
    normed = (standard * (1.0 + part(mod_ref, 1, lanes)) + part(mod_ref, 0, lanes)).astype(BF16)
    vt_out[...] = nn(w_v_t[...], normed).astype(BF16)
    q_out[...] = (nn(w_q_t[...], normed) * HEAD_DIM ** (-0.5)).astype(BF16)
    for at in range(0, lanes, BLOCK):
        kn_out[at : at + BLOCK, :] = nn(turned(normed[:, at : at + BLOCK]), w_k[...]).astype(BF16)


def first_kernel(own, flip_x, flip_y, flip_xy, cot, cot_x, mod, w_q_t, w_v_t, w_k, cot_out, x_out, xb_out, *outs):
    rows = cot.shape[0]
    cot_out[:rows, :] = cot[...]
    cot_out[rows:, :] = cot_x[...]
    for index, ref in enumerate((own, flip_x, flip_y, flip_xy)):
        rows = ref.shape[0]
        flat = turned(ref[...])
        xb_out[:, index * rows : (index + 1) * rows] = flat
        x_out[:, index * rows : (index + 1) * rows] = flat.astype(F32)
    project(x_out[...], mod, w_q_t, w_v_t, w_k, outs)


def head_rows(head):
    return slice(head * HEAD_DIM, (head + 1) * HEAD_DIM)


def pair_columns(head):
    return slice(head // 2 * PAIR, (head // 2 + 1) * PAIR)


def padded(rows, head):
    zeros = jnp.zeros_like(rows)
    return jnp.concatenate([rows, zeros] if head % 2 == 0 else [zeros, rows], axis=0)


def query_top(q):
    square = q[...].astype(F32)
    square = square * square
    norms = [jnp.sum(square[head_rows(head)], axis=0, keepdims=True) for head in range(HEADS)]
    return jnp.max(functools.reduce(jnp.maximum, norms), axis=1, keepdims=True)


def key_top(kn):
    first = lax.broadcasted_iota(jnp.int32, (D, LANES), 1) * HEAD_DIM
    row = lax.broadcasted_iota(jnp.int32, (D, LANES), 0)
    pick = jnp.where((row >= first) & (row < first + HEAD_DIM), 1.0, 0.0).astype(BF16)
    square = kn[...].astype(F32)
    norms = nn((square * square).astype(BF16), pick)
    return jnp.max(jnp.max(norms, axis=0, keepdims=True), axis=1, keepdims=True) * 1.02


def value_rows(vt, rows, at):
    values = vt[rows, at]
    return jnp.concatenate([values, jnp.ones((ONES, values.shape[1]), BF16)], axis=0)


def attend_plain(q, kn, vt, put):
    chunks = [slice(at, at + BLOCK) for at in range(0, kn.shape[0], BLOCK)]

    def score(head):
        return nn(kn[:, pair_columns(head)], padded(q[head_rows(head), :], head))

    totals = {}

    def finish(head, at, probs):
        term = nn(value_rows(vt, head_rows(head), at), probs)
        totals[head] = totals[head] + term if head in totals else term
        if at == chunks[-1]:
            put(head, totals[head])

    waiting = None
    following = score(0)
    for head in range(HEADS):
        scores = following
        for at in chunks:
            if at == chunks[0] and head + 1 < HEADS:
                following = score(head + 1)
            if waiting is not None:
                finish(*waiting)
            waiting = (head, at, jnp.exp(scores[at]).astype(BF16))
    finish(*waiting)


def attend_own_kernel(early, *refs):
    q, kn, vt, *refs = refs[early:]
    passing = []
    if len(refs) > 2:
        *passing, sums, tops, passed = refs
    else:
        sums, tops = refs
    at = 0
    for source in passing:
        rows = source.shape[0]
        passed[at : at + rows, :] = source[...]
        at += rows

    def put(head, total):
        sums[head] = total

    query, key = query_top(q), key_top(kn)
    tops[0:8, :] = jnp.broadcast_to(query, (8, LANES))
    tops[8:16, :] = jnp.broadcast_to(key, (8, LANES))

    @pl.when(jnp.max(query * key) < SAFE_SCORE**2)
    def _():
        attend_plain(q, kn, vt, put)


def forward_kernel(last, early, *refs):
    refs = refs[early:]
    if last:
        active, x, x_step, *refs = refs
    else:
        x, *refs = refs
    q, kn_own, kn_far, vt_own, vt_far, sums, tops, mod, w_out_t, w_up_t, w_down_t, *refs = refs
    if not last:
        mod_next, w_q_t, w_v_t, w_k, *refs = refs
    lse, mixed, attended, middle, hidden, slope, branch, *refs = refs
    if last:
        (final,) = refs
    else:
        x_next, xb_next, *next_outs = refs
    patches = x.shape[1]
    bound = tops[0:1, 0:1] * jnp.maximum(tops[8:9, 0:1], key_top(kn_far))
    safe = jnp.max(bound) < SAFE_SCORE**2

    def put(head, total):
        total = sums[head] + total
        weight = total[HEAD_DIM : HEAD_DIM + 1]
        mixed[head_rows(head), :] = (total[:HEAD_DIM] * (1.0 / weight)).astype(BF16)
        lse[head : head + 1, :] = jnp.log(weight)

    @pl.when(safe)
    def _():
        attend_plain(q, kn_far, vt_far, put)

    @pl.when(jnp.logical_not(safe))
    def _():
        def pair_heads(pair, _):
            columns = pl.ds(pl.multiple_of(pair * PAIR, PAIR), PAIR)
            for head in range(2):
                rows = pl.ds(pl.multiple_of(pair * PAIR + head * HEAD_DIM, HEAD_DIM), HEAD_DIM)
                query = padded(q[rows, :], head)
                scores = [nn(kn[:, columns], query) for kn in (kn_own, kn_far)]
                tops = [jnp.max(score, axis=0, keepdims=True) for score in scores]
                top = jnp.maximum(*tops)
                total = None
                for score, vt in zip(scores, (vt_own, vt_far)):
                    term = nn(value_rows(vt, rows, slice(None)), jnp.exp(score - top).astype(BF16))
                    total = term if total is None else total + term
                weight = total[HEAD_DIM : HEAD_DIM + 1]
                mixed[rows, :] = (total[:HEAD_DIM] * (1.0 / weight)).astype(BF16)
                lse[pl.ds(pair * 2 + head, 1), :] = top + jnp.log(weight)
            return 0

        lax.fori_loop(0, HEADS // 2, pair_heads, 0)

    att = nn(w_out_t[...], mixed[...])
    attended[...] = att.astype(BF16)
    mid = x[...] + part(mod, 2, patches) * att
    middle[...] = mid.astype(BF16)
    standard, _ = standardise(mid)
    hidden_in = (standard * (1.0 + part(mod, 4, patches)) + part(mod, 3, patches)).astype(BF16)
    chunks = [slice(at, at + BLOCK) for at in range(0, w_up_t.shape[0], BLOCK)]

    def up(place):
        wide_rows = slice(place * BLOCK, (place + 2) * BLOCK)
        both = nn(w_up_t[wide_rows, :], hidden_in)
        return [both[:BLOCK], both[BLOCK:]]

    down = None
    waiting = None
    acts = up(0)
    for place, rows in enumerate(chunks):
        act = acts[place]
        if place % 2 == 0 and place + 2 < len(chunks):
            acts += up(place + 2)
        if place > 0:
            term = nn(w_down_t[:, chunks[place - 1]], waiting)
            down = term if down is None else down + term
        act = act.astype(BF16)
        inner = GELU_A + (GELU_A * GELU_B) * (act * act)
        half = 0.5 + 0.5 * jnp.tanh(act * inner)
        waiting = gelu = act * half
        hidden[rows, :] = waiting
        slope[rows, :] = (half + (gelu - gelu * half) * (6.0 * inner - 4.0 * GELU_A))
    down = down + nn(w_down_t[:, chunks[-1]], waiting)
    branch[...] = down.astype(BF16)
    out = mid + part(mod, 5, patches) * down
    if last:
        own = final.shape[0]
        final[...] = jnp.where(active[0] > 0.0, out[:, :own], x_step[:, :own]).T
    else:
        x_next[...] = out
        xb_next[...] = out.astype(BF16)
        project(out, mod_next, w_q_t, w_v_t, w_k, next_outs)


def put_grads(left_ref, right, where, count, at, mine, other, before):
    rows = [left_ref[pl.ds(pl.multiple_of(where[place] * count, 16), count), :] for place in range(2)]
    product = nt(jnp.concatenate(rows, axis=0), right)
    for column in range(0, product.shape[1], LANES):
        low = product[:count, column : column + LANES]
        high = product[count:, column : column + LANES]
        if before is not None:
            low = low + before[0][at : at + count, :]
            high = high + before[1][at : at + count, :]
        mine[at : at + count, :] = low.astype(mine.dtype)
        other[at : at + count, :] = high.astype(other.dtype)
        at += count


def dense_back_kernel(has_close, has_open, has_before, start, layers, waits, *refs):
    refs = list(refs)

    def take(count):
        taken = refs[:count]
        del refs[:count]
        return taken

    take(waits)
    where, active = take(2)
    close_before = open_before = None
    if has_close:
        d_own, d_got, dq, d_mid_in, x_in, mod_in, w_qkv = take(7)
        w_qkv = w_qkv.at[layers[0]]
        if has_before[0]:
            close_before = take(3)
    if start == "first":
        cots = take(2)
    elif start == "cross":
        cots = take(1)
    if has_open:
        mixed, attended, middle, hidden, slope, branch, mod, w_out, w_up, w_down = take(10)
        w_out, w_up, w_down = (ref.at[layers[1]] for ref in (w_out, w_up, w_down))
        if has_before[1]:
            open_before = take(3)
    else:
        (lines,) = take(1)
    if has_close:
        close_mine, close_other, close_mods = take(3)
    if start == "first":
        (cot_out,) = take(1)
    if has_open:
        open_mine, open_other, open_mods, d_mid_out, do_out, cen_out = take(6)
    else:
        g_out, sums_out = take(2)
        sums_at = close_before[1].shape[0]
    if has_close:
        grads_scr, normed_scr = take(2)
    if has_open:
        pg_scr, hin_scr = take(2)

    patches = middle.shape[1] if has_open else x_in.shape[1]
    totals = {}

    def add_sums(name, values):
        totals[name] = totals[name] + folded(values) if name in totals else folded(values)

    def put_sums(out, before, names):
        for place, name in enumerate(names):
            rows = slice(place * D, (place + 1) * D)
            out[rows, :] = totals[name] + before[2][rows, :] if before else totals[name]

    if start == "first":
        for index, ref in enumerate(cots):
            rows = ref.shape[0]
            cot_out[:, index * rows : (index + 1) * rows] = turned(ref[...])

    def close(at):
        standard, scale = standardise(x_in[:, at].astype(F32))
        gain = 1.0 + part(mod_in, 1, patches)
        normed_scr[:, at] = (standard * gain + part(mod_in, 0, patches)).astype(BF16)
        for third in range(3):
            if third == 0:
                piece = dq[:, at]
            else:
                rows = slice((third - 1) * D, third * D)
                piece = (d_own[rows, at] + d_got[rows, at].astype(F32)).astype(BF16)
            grads_scr[third * D : (third + 1) * D, at] = piece
        back = nn(w_qkv[...], grads_scr[:, at])
        put_grads(normed_scr, grads_scr[...], where, D // 8, 0, close_mine, close_other, close_before)
        add_sums("shift_a", back)
        add_sums("scale_a", back * standard)
        g = d_mid_in[:, at] + pre_norm_back(standard, scale, back, gain)
        if start == "cross":
            g = g + (1.0 - active[0]) * cots[0][:, at].astype(F32)
        return g

    def dense(at, g):
        standard, scale = standardise(middle[:, at].astype(F32))
        gain = 1.0 + part(mod, 4, patches)
        hin_scr[:, at] = (standard * gain + part(mod, 3, patches)).astype(BF16)
        branch_grad = (part(mod, 5, patches) * g).astype(BF16)
        add_sums("gate_m", g * branch[:, at].astype(F32))
        chunks = [slice(start, start + BLOCK) for start in range(0, w_down.shape[0], BLOCK)]
        back = None
        waiting = None

        def down(place):
            wide_rows = slice(place * BLOCK, (place + 2) * BLOCK)
            both = nn(w_down[wide_rows, :], branch_grad)
            return [both[:BLOCK], both[BLOCK:]]

        hidden_grads = down(0)
        for place, rows in enumerate(chunks):
            hidden_grad = hidden_grads[place]
            if place % 2 == 0 and place + 2 < len(chunks):
                hidden_grads += down(place + 2)
            if place > 0:
                term = nn(w_up[:, chunks[place - 1]], waiting)
                back = term if back is None else back + term
            waiting = slope[rows, at] * hidden_grad.astype(BF16)
            pg_scr[rows, at] = waiting
        back = back + nn(w_up[:, chunks[-1]], waiting)
        count = w_down.shape[0] // 8
        start_at = count * (D // LANES)
        put_grads(hidden, branch_grad, where, count, 0, open_mine, open_other, open_before)
        put_grads(hin_scr, pg_scr[...], where, D // 8, start_at, open_mine, open_other, open_before)
        add_sums("shift_m", back)
        add_sums("scale_m", back * standard)
        d_mid = g + pre_norm_back(standard, scale, back, gain)
        d_mid_out[:, at] = d_mid
        att_grad = (part(mod, 2, patches) * d_mid).astype(BF16)
        mixed_grad = nn(w_out[...], att_grad).astype(BF16)
        do_out[:, at] = mixed_grad
        start_at += (w_up.shape[1] // LANES) * (D // 8)
        put_grads(mixed, att_grad, where, D // 8, start_at, open_mine, open_other, open_before)
        add_sums("gate_a", d_mid * attended[:, at].astype(F32))
        product = mixed_grad.astype(F32) * mixed[:, at].astype(F32)
        for head in range(HEADS):
            cen_out[head : head + 1, at] = jnp.sum(product[head_rows(head)], axis=0, keepdims=True)

    at = slice(0, patches)
    g = close(at) if has_close else cot_out[:, at].astype(F32) * active[0]
    if has_open:
        dense(at, g)
    else:
        g_out[...] = g[:, : g_out.shape[0]].T
    if has_close:
        put_sums(close_mods, close_before, ("shift_a", "scale_a"))
    if has_open:
        put_sums(open_mods, open_before, ("gate_a", "shift_m", "scale_m", "gate_m"))
    else:
        sums_out[...] = lines[...]
        put_lines(sums_out, 0, close_mods[...])
        close_other[sums_at:, :] = sums_out[...].astype(BF16)


def attend_back_kernel(has_before, waits, q, kn, vt, lse, d_out, centre, *refs):
    if has_before:
        before, *refs = refs
    d_kv, dq_out, kt_scr, vn_scr = refs[waits:]
    for column in range(0, D, LANES):
        kt_scr[column : column + LANES, :] = turned(kn[:, column : column + LANES])
    for column in range(0, vt.shape[1], BLOCK):
        vn_scr[column : column + BLOCK, :] = turned(vt[:, column : column + BLOCK])

    steps = [(head, slice(at, at + BLOCK)) for head in range(HEADS) for at in range(0, kn.shape[0], BLOCK)]

    def score(head, at):
        columns = pair_columns(head)
        rows = head_rows(head)
        return nn(kn[at, columns], padded(q[rows, :], head)), nn(vn_scr[at, columns], padded(d_out[rows, :], head))

    totals = {}

    def finish(head, at, probs, score_grads):
        rows = head_rows(head)
        d_kv[D + rows.start : D + rows.stop, at] = nt(d_out[rows, :], probs).astype(d_kv.dtype)
        d_kv[rows, at] = nt(q[rows, :], score_grads).astype(d_kv.dtype)
        term = nn(kt_scr[rows, at], score_grads)
        if head not in totals:
            totals[head] = before[rows, :] + term if has_before else term
            return
        term = totals[head] + term
        if has_before:
            term = term * HEAD_DIM ** (-0.5)
        dq_out[rows, :] = term.astype(dq_out.dtype)

    waiting = None
    following = score(*steps[0])
    for place, (head, at) in enumerate(steps):
        scores, prob_grads = following
        if place + 1 < len(steps):
            following = score(*steps[place + 1])
        if waiting is not None:
            finish(*waiting)
        probs = jnp.exp(scores - lse[head : head + 1, :])
        score_grads = (probs * (prob_grads - centre[head : head + 1, :])).astype(BF16)
        waiting = (head, at, probs.astype(BF16), score_grads)
    finish(*waiting)


def split_kernel(waits, where, *refs):
    *halves, keep, sent, total_scr = refs[waits:]
    rows_half = keep.shape[0]
    at = 0
    for mine, other in zip(halves[::2], halves[1::2]):
        rows = mine.shape[0]
        total_scr[at : at + rows, :] = mine[...] + other[...].astype(F32)
        at += rows
    if at < total_scr.shape[0]:
        total_scr[at:, :] = jnp.zeros((total_scr.shape[0] - at, LANES), F32)
    odd = where[3]
    keep[...] = total_scr[pl.ds(pl.multiple_of(odd * rows_half, 16), rows_half), :]
    sent[...] = total_scr[pl.ds(pl.multiple_of((1 - odd) * rows_half, 16), rows_half), :].astype(BF16)


def pair_sum_kernel(waits, *refs):
    refs = refs[waits:]
    count = len(refs) // 3
    for keep, got, out in zip(refs[:count], refs[count : 2 * count], refs[2 * count :]):
        out[...] = (keep[...].astype(F32) + got[...].astype(F32)).astype(BF16)


def put_lines(out, row, values):
    ones = jnp.ones((16, LANES), BF16)
    high = values.astype(BF16)
    low = (values - high.astype(F32)).astype(BF16)
    line = (nt(ones, high) + nt(ones, low))[0:1]
    for column in range(0, line.shape[1], LANES):
        out[row : row + 1, :] = line[:, column : column + LANES]
        row += 1
    return row


def lines_kernel(early, context, *refs):
    *sums, out = refs
    out[...] = jnp.zeros_like(out)
    row = 2 * D // LANES
    for ref in sums:
        row = put_lines(out, row, ref[...])
    for column in range(0, D, LANES):
        out[row : row + 1, :] = context[0:1, column : column + LANES].astype(F32)
        row += 1


def join_kernel(sum_count, early, other_early, mine, sums, got, out):
    rows = mine.shape[0]
    out[:rows, :] = (mine[...] + got[:rows, :].astype(F32)).astype(BF16)
    other = got[rows:, :].astype(F32)
    summed = lax.broadcasted_iota(jnp.int32, (SUM_ROWS, LANES), 0) < sum_count
    out[rows:, :] = (sums[...] + jnp.where(summed, other, 0.0)).astype(BF16)


def pair_kernel(rows, where, own, got, out):
    out[:rows, :] = (own[:rows, :].astype(F32) + got[:rows, :].astype(F32)).astype(BF16)
    odd = where[3]
    size = SUM_ROWS
    out[pl.ds(pl.multiple_of(rows + odd * size, 16), size), :] = own[rows:, :]
    out[pl.ds(pl.multiple_of(rows + (1 - odd) * size, 16), size), :] = got[rows:, :]


def gather_kernel(layer, where, own, got, *refs):
    outs, qkv_out, rows_scr, scratch, sems = refs[-9:-6], refs[-6], refs[-5], refs[-4:-1], refs[-1]
    if layer == 1:
        outs = refs[-8:-5]
    half = own.shape[0]
    rows_scr[pl.ds(pl.multiple_of(where[3] * half, 16), half), :] = own[...]
    rows_scr[pl.ds(pl.multiple_of((1 - where[3]) * half, 16), half), :] = got[...]
    at = 0
    copies = []
    for place, (out, held) in enumerate(zip(outs, scratch)):
        rows = held.shape[0]
        for column in range(0, held.shape[1], LANES):
            held[:, column : column + LANES] = rows_scr[at : at + rows, :].astype(F32)
            at += rows
        copies.append(pltpu.make_async_copy(held, out.at[layer], sems.at[place]))
        copies[-1].start()
    if layer == 0:
        rows = qkv_out.shape[0]
        for column in range(0, qkv_out.shape[1], LANES):
            qkv_out[:, column : column + LANES] = rows_scr[at : at + rows, :].astype(F32)
            at += rows
    for copy in copies:
        copy.wait()


def finish_kernel(item_count, where, own, got, qkv_1, qkv_out, ada_out, bias_out, shift_out, sum_scr, bias_scr, shift_scr):
    layers = 2
    device, high = where[0], where[4]
    slice_rows = qkv_out.shape[1]
    close_rows = slice_rows * (3 * D // LANES)
    for other in range(2):
        rows = slice(close_rows + other * SUM_ROWS, close_rows + (other + 1) * SUM_ROWS)
        sum_scr[2 * high + other] = own[rows, :].astype(F32)
        sum_scr[2 * (1 - high) + other] = got[rows, :].astype(F32)
    qkv_out[1] = qkv_1[...]
    for tile in range(3 * D // LANES):
        rows = slice(tile * slice_rows, (tile + 1) * slice_rows)
        total = own[rows, :].astype(F32) + got[rows, :].astype(F32)
        qkv_out[0, :, tile * LANES : (tile + 1) * LANES] = total
    tiles = 6 * D // LANES
    contexts = []
    for other in range(item_count):
        line = jnp.concatenate([sum_scr[other, layers * tiles + c : layers * tiles + c + 1, :] for c in range(3)], axis=1)
        contexts.append(line)
    square = jnp.concatenate(contexts + [jnp.zeros((8 - item_count, D), F32)], axis=0)
    spot = lax.broadcasted_iota(jnp.int32, (slice_rows, D), 1)
    want = lax.broadcasted_iota(jnp.int32, (slice_rows, D), 0) + device * slice_rows
    pick = jnp.where(spot == want, 1.0, 0.0).astype(BF16)
    columns = nt(pick, square.astype(BF16))
    bias_rows = bias_out.shape[1]
    for index in range(layers):
        flats = []
        for tile in range(tiles):
            row = index * tiles + tile
            total = None
            flat = None
            for other in range(item_count):
                line = sum_scr[other, row : row + 1, :]
                term = columns[:, other : other + 1] * line
                total = term if total is None else total + term
                flat = line if flat is None else flat + line
            ada_out[index, :, tile * LANES : (tile + 1) * LANES] = total
            flats.append(flat)
        flat = jnp.concatenate(flats, axis=1)
        for place in range(flat.shape[1] // bias_rows):
            bias_scr[place, index : index + 1, :] = flat[:, place * bias_rows : (place + 1) * bias_rows]
            at = 3 * D + place * slice_rows
            shift_scr[place, index : index + 1, :] = flat[:, at : at + slice_rows]
    bias_out[...] = bias_scr[device]
    shift_out[...] = shift_scr[device]


VMEM = pl.BlockSpec(memory_space=pltpu.VMEM)
SMEM = pl.BlockSpec(memory_space=pltpu.SMEM)
ANY = pl.BlockSpec(memory_space=pl.ANY)
HBM = pl.BlockSpec(memory_space=pltpu.HBM)


def layer_block(array, index):
    return pl.BlockSpec((None,) + array.shape[1:], lambda step: (index,) + (0,) * (array.ndim - 1))


def call(body, args, outs, scratch=(), flops=0, name=None, direct=0, aliases=None):
    arrays = [arg[0] if isinstance(arg, tuple) else arg for arg in args]
    specs = [arg[1] if isinstance(arg, tuple) else VMEM for arg in args]
    return pl.pallas_call(
        body,
        out_shape=[jax.ShapeDtypeStruct(shape, kind) for shape, kind in outs],
        in_specs=specs,
        out_specs=[ANY] * direct + [VMEM] * (len(outs) - direct),
        input_output_aliases=aliases or {},
        scratch_shapes=[one if not isinstance(one, tuple) else pltpu.VMEM(*one) for one in scratch],
        compiler_params=pltpu.CompilerParams(vmem_limit_bytes=VMEM_LIMIT),
        cost_estimate=pl.CostEstimate(flops=flops, bytes_accessed=0, transcendentals=0),
        name=name,
    )(*arrays)


VMEM_LIMIT = 14 * 1024 * 1024


def fast_shards(
    lat_count, lon_count, item_count,
    fields, lead_index, rollout, w_qkv, w_out, w_up, w_down, w_ada, b_ada, cotangent,
):
    _, rows_dev, cols_dev, width = fields.shape
    local = rows_dev * cols_dev
    layers = w_qkv.shape[0]
    ff = w_up.shape[2]
    patches = 4 * local
    device = lax.axis_index("lat") * lon_count + lax.axis_index("lon")
    item = lax.axis_index("item")
    where = jnp.stack([device, device ^ 1, item, item & 1, item >> 1]).astype(jnp.int32)
    active = (1 < rollout[0]).astype(F32)[None]

    def plane_flip(value, flip_lat, flip_y):
        pairs = [
            (a * lon_count + b, (a ^ flip_lat) * lon_count + (b ^ (2 * flip_y)))
            for a in range(lat_count)
            for b in range(lon_count)
        ]
        return lax.ppermute(value, ("lat", "lon"), pairs)

    def swap(value):
        return lax.ppermute(value, "lon", [(index, index ^ 1) for index in range(lon_count)])

    def with_item(value, flip):
        return lax.ppermute(value, "item", [(index, index ^ flip) for index in range(item_count)])

    def plane_parts(value):
        return [value, plane_flip(value, 1, 0), plane_flip(value, 0, 1), plane_flip(value, 1, 1)]

    field_parts = plane_parts(fields.reshape(local, width))

    context = jax.nn.silu(embedding(lead_index[0])).astype(BF16)
    context = jnp.broadcast_to(context[None, :], (16, width))
    square = (width, patches)
    natural = (patches, width)
    weights = (w_qkv, w_ada, b_ada, w_out, w_up, w_down)
    weights = [(pltpu.with_memory_space_constraint(value, pltpu.HBM), HBM) for value in weights]
    first_outs = [((6 * width, LANES), F32)] + [((width, width), BF16)] * 3
    rest_outs = [((width, width), BF16), ((ff, width), BF16), ((width, ff), BF16)]
    first_fetch = [((width, 3 * width), BF16), ((width, 6 * width), BF16)]
    rest_fetch = [((width, width), BF16), ((width, ff), BF16), ((ff, width), BF16)]
    prepared = call(
        prepare_kernel,
        [context, *weights, (where, SMEM), (active, SMEM)],
        first_outs * 2 + rest_outs,
        first_fetch + [(b_ada.shape, F32)] + rest_fetch + first_fetch + [pltpu.SemaphoreType.DMA((8,))],
        name="prepare",
    )
    first_parts = [prepared[0:4], prepared[4:8]]
    rest_parts = [prepared[8:11]]
    mods = [one[0] for one in first_parts]

    project_outs = [(square, F32), (square, BF16), (square, BF16), (natural, BF16), (square, BF16)]
    dense_flops = 2 * patches * (width * 3 * width + width * width + 2 * width * ff)
    score_flops = 2 * patches * 2 * patches * width * 4
    cot = cotangent.reshape(local, width)
    cot, x, xb, *projected = call(
        first_kernel,
        [*field_parts, cot, plane_flip(cot, 1, 0), *first_parts[0]],
        [((2 * local, width), BF16)] + project_outs,
        flops=2 * patches * width * 4 * width,
        name="first",
    )
    saved = []
    for step in range(STEPS):
        for index in range(layers):
            q, kn, vt = projected
            if len(rest_parts) == index:
                rest_parts.append(
                    call(
                        functools.partial(prepare_rest_kernel, index),
                        [(kn, ANY), w_out, w_up, w_down],
                        rest_outs,
                        name="prepare_rest",
                    )
                )
            kn_far, vt_far = swap(kn), swap(vt)
            early = [w_up] if len(rest_parts) == index + 1 < layers else []
            passing = [cot] if step == STEPS - 1 and index == 0 else []
            passed = [((2 * local, width), BF16)] if passing else []
            sums, tops, *passed = call(
                functools.partial(attend_own_kernel, len(early)),
                early + [q, kn, vt] + passing,
                [((HEADS, HEAD_DIM + ONES, patches), F32), ((16, LANES), F32)] + passed,
                flops=10 * score_flops,
                name="forward_own",
            )
            if passed:
                cot_parts = [passed[0], plane_flip(passed[0], 0, 1)]
            last = step == STEPS - 1 and index == layers - 1
            if index == 0 and step > 0:
                x_step = x
            following = list(first_parts[(index + 1) % layers])
            early = [w_down] if len(rest_parts) == index + 1 < layers else []
            lse, mixed, attended, middle, hidden, slope, branch, *results = call(
                functools.partial(forward_kernel, last, len(early)),
                early
                + ([(active, SMEM), x, x_step] if last else [x])
                + [q, kn, kn_far, vt, vt_far, sums, tops, mods[index], *rest_parts[index]]
                + ([] if last else following),
                [
                    ((HEADS, patches), F32),
                    (square, BF16),
                    (square, BF16),
                    (square, BF16),
                    ((ff, patches), BF16),
                    ((ff, patches), BF16),
                    (square, BF16),
                ]
                + ([((local, width), F32)] if last else project_outs),
                flops=dense_flops + 2 * score_flops,
                name="forward",
            )
            saved.append((xb, [mixed, attended, middle, hidden, slope, branch], (q, kn, kn_far, vt, vt_far, lse)))
            if last:
                final = results[0]
            else:
                x, xb, *projected = results

    slice_rows = width // 8
    open_rows = 2 * (ff // 8) * (width // LANES) + slice_rows * (width // LANES)
    close_rows = slice_rows * (3 * width // LANES)
    order = [(step, index) for step in reversed(range(STEPS)) for index in reversed(range(layers))]
    open_done = [None] * layers
    close_done = [None] * layers
    pending = None
    for place in range(len(order) + 1):
        has_close = pending is not None
        has_open = place < len(order)
        use = [order[place - 1][1], order[place][1] if has_open else 0]
        waits = []
        if has_close and close_done[use[0]]:
            waits = [pair_1] if has_open else []
        args = [(value, ANY) for value in waits] + [(where, SMEM), (active, SMEM)]
        outs = []
        scratch = []
        has_before = [False, False]
        start = ""
        if has_close:
            args += pending
            if close_done[use[0]] is not None:
                has_before[0] = True
                args += close_done[use[0]]
            outs += [((close_rows, LANES), F32)]
            sent_rows = close_rows + (0 if has_open else SUM_ROWS)
            outs += [((sent_rows, LANES), BF16 if has_before[0] else F32), ((2 * width, LANES), F32)]
            scratch += [((3 * width, patches), BF16), (square, BF16)]
        if place == 0:
            start = "first"
            args += cot_parts
            outs += [(square, BF16)]
        elif has_open and order[place][0] != order[place - 1][0]:
            start = "cross"
            args += [cot_t]
        if has_open:
            step, index = order[place]
            xb, kept, heads = saved[step * layers + index]
            args += kept + [mods[index], w_out, w_up, w_down]
            if open_done[index] is not None:
                has_before[1] = True
                args += open_done[index]
            outs += [
                ((open_rows, LANES), F32),
                ((open_rows, LANES), BF16 if has_before[1] else F32),
                ((4 * width, LANES), F32),
                (square, F32),
                (square, BF16),
                ((HEADS, patches), F32),
            ]
            scratch += [((ff, patches), BF16), (square, BF16)]
        else:
            args += [lines]
            outs += [((local, width), F32), ((SUM_ROWS, LANES), F32)]
        results = list(
            call(
                functools.partial(dense_back_kernel, has_close, has_open, has_before, start, use, len(waits)),
                args,
                outs,
                scratch,
                flops=2 * dense_flops if has_open else 0,
                name="dense_back" if has_open else "close_back",
            )
        )
        if has_close:
            close_done[use[0]] = results[:3]
            del results[:3]
        if start == "first":
            cot_t = results.pop(0)
        if not has_open:
            gradient, line = results
            break
        open_done[index] = results[:3]
        d_mid, d_out, centre = results[3:]
        q, kn, kn_far, vt, vt_far, lse = heads
        halves = [open_done[index][0], open_done[index][1]]
        if index == 0:
            halves += [close_done[1][0], close_done[1][1]]
        half_rows = -(-sum(half.shape[0] for half in halves[::2]) // 32) * 16

        def split(waits):
            pieces = [half if place % 2 == 0 else swap(half) for place, half in enumerate(halves)]
            return call(
                functools.partial(split_kernel, len(waits)),
                [(where, SMEM), *waits, *pieces],
                [((half_rows, LANES), F32), ((half_rows, LANES), BF16)],
                [((2 * half_rows, LANES), F32)],
                name="split",
            )

        def pair_sum(late, keeps, gots, others=()):
            outs = [(keep.shape, BF16) for keep in keeps]
            body = functools.partial(pair_sum_kernel, 1 + len(others))
            return call(body, [(late, ANY), *others, *keeps, *gots], outs, name="pair_sum")

        waits = []
        if has_before[1] and index == 0:
            pair_got_1 = with_item(pair_1, 2)
            lines = call(
                lines_kernel,
                [(pair_got_1, ANY), context, open_done[0][2], close_done[1][2], open_done[1][2]],
                [((SUM_ROWS, LANES), F32)],
                flops=10 * score_flops,
                name="lines",
            )[0]
            keep, sent = split([(lines, ANY)])
            got_0 = with_item(sent, 1)
            waits = [keep]
        d_far, dq = call(
            functools.partial(attend_back_kernel, False, len(waits)),
            [q, kn_far, vt_far, lse, d_out, centre] + [(value, ANY) for value in waits],
            [((2 * width, patches), BF16), (square, F32)],
            [(square, BF16), (natural, BF16)],
            flops=10 * score_flops,
            name="attend_far",
        )
        d_got = swap(d_far)
        waits = []
        if has_before[1]:
            if index == 1:
                keep, sent = split([(d_far, ANY)])
                got_1 = with_item(sent, 1)
                waits = [keep]
            else:
                (item_1,) = pair_sum(d_far, [pair_1], [pair_got_1])
                item_got_1 = with_item(item_1, 1)
                (pair_0,) = pair_sum(d_far, [keep], [got_0], [(item_1, ANY)])
                pair_got_0 = with_item(pair_0, 2)
                waits = [pair_0]
        d_own, dq = call(
            functools.partial(attend_back_kernel, True, len(waits)),
            [q, kn, vt, lse, d_out, centre, dq] + [(value, ANY) for value in waits],
            [((2 * width, patches), F32), (square, BF16)],
            [(square, BF16), (natural, BF16)],
            flops=10 * score_flops,
            name="attend_own",
        )
        if has_before[1] and index == 1:
            (pair_1,) = pair_sum(dq, [keep], [got_1])
        pending = [d_own, d_got, dq, d_mid, xb, mods[index], w_qkv]

    message = call(
        functools.partial(join_kernel, layers * 6 * width // LANES),
        [(pair_got_0, ANY), (item_got_1, ANY), close_done[0][0], line, swap(close_done[0][1])],
        [((close_rows + SUM_ROWS, LANES), BF16)],
        name="join",
    )[0]
    message_got = with_item(message, 1)
    stacks = [
        ((layers, ff // 8, width), F32),
        ((layers, slice_rows, ff), F32),
        ((layers, slice_rows, width), F32),
    ]
    held = [(shape[1:], kind) for shape, kind in stacks]
    sems = [pltpu.SemaphoreType.DMA((3,))]
    stacked = call(
        functools.partial(gather_kernel, 1),
        [(where, SMEM), item_1, item_got_1, (message, ANY)],
        stacks,
        [((2 * pair_1.shape[0], LANES), BF16)] + held + sems,
        name="gather",
        direct=3,
    )
    early = (pltpu.with_memory_space_constraint(stacked[2], pltpu.HBM), HBM)
    (item_0,) = pair_sum(message, [pair_0], [pair_got_0], [early])
    message = call(
        functools.partial(pair_kernel, close_rows),
        [(where, SMEM), message, message_got],
        [((close_rows + 2 * SUM_ROWS, LANES), BF16)],
        name="pair",
    )[0]
    down_grad, up_grad, out_grad, qkv_1 = call(
        functools.partial(gather_kernel, 0),
        [(where, SMEM), item_0, with_item(item_0, 1)] + [(value, ANY) for value in stacked],
        stacks + [((slice_rows, 3 * width), F32)],
        [((2 * pair_0.shape[0], LANES), BF16)] + held + sems,
        name="gather",
        direct=3,
        aliases={3: 0, 4: 1, 5: 2},
    )
    bias_rows = 6 * width // 8
    qkv_grad, ada_grad, bias_grad, shift_grad = call(
        functools.partial(finish_kernel, item_count),
        [(where, SMEM), message, with_item(message, 2), qkv_1],
        [
            ((layers, slice_rows, 3 * width), F32),
            ((layers, slice_rows, 6 * width), F32),
            ((layers, bias_rows), F32),
            ((layers, slice_rows), F32),
        ],
        [
            ((item_count, SUM_ROWS, LANES), F32),
            ((8, layers, bias_rows), F32),
            ((8, layers, slice_rows), F32),
        ],
        name="finish",
    )
    field_shape = (1, rows_dev, cols_dev, width)
    return (
        final.reshape(field_shape),
        gradient.reshape(field_shape),
        qkv_grad,
        out_grad,
        up_grad,
        down_grad,
        ada_grad,
        bias_grad,
        shift_grad,
    )


def solution(mesh):
    lat_count, lon_count, item_count = mesh.shape["lat"], mesh.shape["lon"], mesh.shape["item"]
    if lat_count == 2 and lon_count == 4:
        body = functools.partial(fast_shards, lat_count, lon_count, item_count)
    else:
        body = shards
    return jax.shard_map(
        body,
        mesh=mesh,
        in_specs=(
            P("item", "lat", "lon", None),
            P("item"),
            P("item"),
            P(),
            P(),
            P(),
            P(),
            P(),
            P(),
            P("item", "lat", "lon", None),
        ),
        out_specs=(
            P("item", "lat", "lon", None),
            P("item", "lat", "lon", None),
            P(None, ("lat", "lon"), None),
            P(None, ("lat", "lon"), None),
            P(None, ("lat", "lon"), None),
            P(None, ("lat", "lon"), None),
            P(None, ("lat", "lon"), None),
            P(None, ("lat", "lon")),
            P(None, ("lat", "lon")),
        ),
        check_vma=False,
    )
```
